32 devices in a mesh: hop: 4 (over y, x), rows: 8 (over z, core).
Axes of the slice: x: 2, y: 2, z: 4, core: 2. Of those that a mesh axis runs over, the one named last changes fastest.
Arguments:
- features: bfloat16 [4, 65536, 100], P('hop', 'rows'), may hold values from -6 to 6
- branch_weight: bfloat16 [4, 100, 512], P('hop'), may hold values from -0.625 to 0.625
- branch_gain: float32 [4, 512], P('hop'), may hold values from 0.25 to 1.75
- branch_bias: float32 [4, 512], P('hop'), may hold values from -3 to 3
- mix_weight: bfloat16 [2048, 512], P('hop'), may hold values from -0.25 to 0.25
- mixing_norm_gain: float32 [512], replicated, may hold values from 0.25 to 1.75
- mixing_norm_bias: float32 [512], replicated, may hold values from -3 to 3
- class_weight: bfloat16 [512, 47], replicated, may hold values from -0.79296875 to 0.79296875
- class_bias: float32 [47], replicated, may hold values from -3 to 3
- labels: int32 [65536], P('rows'), may hold values from 0 to 46
- hop_mask: int32 [512, 2], P('rows'), may hold values 0 or 1
Outputs:
- log_probs: float32 [65536, 47], P('rows')
- loss: float32 [], replicated
- grad_features: float32 [4, 65536, 100], P('hop', 'rows')
- grad_branch_weight: float32 [4, 100, 512], P('hop')
- grad_branch_gain: float32 [4, 512], P('hop')
- grad_branch_bias: float32 [4, 512], P('hop')
- grad_mix_weight: float32 [2048, 512], P('hop')
- grad_head_gain: float32 [512], replicated
- grad_head_bias: float32 [512], replicated
- grad_class_weight: float32 [512, 47], replicated
- grad_class_bias: float32 [47], replicated
The draws below stay inside these ranges and needn't reach their ends.
All inputs are finite; a program needn't handle non-finite values. No bound on the sum of `hop_mask` on one device may be relied on, other than what follows from the above.
Results may differ from the reference program's by a relative error of at most 0.017.
Values may be sent and summed in bfloat16 or wider, within the bound.
A program may use at most 512 MiB of HBM per device.

```python
import jax
import jax.numpy as jnp
from jax import lax

HOPS = 4
FEAT = 100
HIDDEN_SIZE = 512
CLASSES = 47
MASK_BLOCK = 128
NODES = 65536
BLOCKS = 512


def touch_ends(array, rng, least, largest):
    place = [jax.random.randint(jax.random.fold_in(rng, axis), (), 0, length) for axis, length in enumerate(array.shape)]
    main_axis = array.shape.index(max(array.shape))
    neighbour = place[:main_axis] + [(place[main_axis] + 1) % array.shape[main_axis]] + place[main_axis + 1:]
    return array.at[tuple(place)].set(least).at[tuple(neighbour)].set(largest)


def block_scale(key, extent, split, low, high):
    factor_of, own = 1.0, jax.random.fold_in(key, 6)
    for dim, shards_of in split:
        heights = jnp.exp(jax.random.uniform(jax.random.fold_in(own, dim), (shards_of,), jnp.float32, low / len(split), high / len(split)))
        factor_of = factor_of * jnp.repeat(heights, extent[dim] // shards_of).reshape([-1 if axis == dim else 1 for axis in range(len(extent))])
    return factor_of


def gaussian(key, extent, width, most, shards=(), kind=jnp.bfloat16):
    entries = width * jax.random.normal(key, extent, jnp.float32)
    if shards:
        entries = entries * block_scale(key, extent, shards, -0.22, 0.18)
    return jnp.clip(entries, -most, most).astype(kind)


def setup_inputs(seed: int = 0) -> dict:
    keys = jax.random.split(jax.random.key(seed), 12)
    return {
        "features": gaussian(keys[0], (HOPS, NODES, FEAT), 1.0, 6.0, ((0, 4), (1, 8))),
        "branch_weight": gaussian(keys[1], (HOPS, FEAT, HIDDEN_SIZE), FEAT ** -0.5, 0.625, ((0, 4),)),
        "branch_gain": jnp.clip(1.0 + 0.15 * jax.random.normal(keys[2], (HOPS, HIDDEN_SIZE), jnp.float32), 0.25, 1.75),
        "branch_bias": gaussian(keys[3], (HOPS, HIDDEN_SIZE), 0.5, 3.0, ((0, 4),), jnp.float32),
        "mix_weight": gaussian(keys[4], (HOPS * HIDDEN_SIZE, HIDDEN_SIZE), HIDDEN_SIZE ** -0.5, 0.25, ((0, 4),)),
        "mixing_norm_gain": jnp.clip(1.0 + 0.15 * jax.random.normal(keys[5], (HIDDEN_SIZE,), jnp.float32), 0.25, 1.75),
        "mixing_norm_bias": gaussian(keys[6], (HIDDEN_SIZE,), 0.5, 3.0, (), jnp.float32),
        "class_weight": gaussian(keys[7], (HIDDEN_SIZE, CLASSES), (3.0 / HIDDEN_SIZE ** 0.5), 0.79296875),
        "class_bias": gaussian(keys[8], (CLASSES,), 0.5, 3.0, (), jnp.float32),
        "labels": touch_ends(jax.random.randint(keys[9], (NODES,), 0, CLASSES), jax.random.fold_in(keys[9], 1), 0, CLASSES - 1).astype(jnp.int32),
        "hop_mask": touch_ends((jax.random.randint(keys[10], (BLOCKS, 2), 0, 2) < 1).astype(jnp.int32), jax.random.fold_in(keys[10], 1), 0, 1),
    }


@jax.custom_vjp
def lower_precision(v):
    return lax.optimization_barrier(v.astype(jnp.bfloat16)).astype(jnp.float32)

@jax.custom_vjp
def low_back(v):
    return v

def low_keep(v):
    return (lower_precision(v), None)

def low_pass(kept, grad):
    return (grad,)

def back_keep(v):
    return (v, None)

def back_low(kept, grad):
    return (lower_precision(grad),)
lower_precision.defvjp(low_keep, low_pass)
low_back.defvjp(back_keep, back_low)
EPS = 1e-05
HIGH = lax.Precision.HIGHEST

def layer_normalize(values, axis):
    mean = lax.optimization_barrier(jnp.mean(values, axis=axis, keepdims=True))
    var = lax.optimization_barrier(jnp.mean(values * values, axis=axis, keepdims=True)) - mean * mean
    return (values - mean) * lax.rsqrt(var + EPS)

def reference(features, branch_weight, branch_gain, branch_bias, mix_weight, mixing_norm_gain, mixing_norm_bias, class_weight, class_bias, labels, hop_mask):
    keep_late = jnp.repeat(hop_mask.astype(jnp.float32), MASK_BLOCK, axis=0)
    keep_mask = jnp.concatenate([jnp.ones((NODES, 2), jnp.float32), keep_late], axis=1).T[:, :, None]
    onehot = (labels[:, None] == jnp.arange(CLASSES, dtype=jnp.int32)[None, :]).astype(jnp.float32)

    def forward(feat, w_one, first_gain, first_bias, w_two, g_two, b_two, w_cls, b_cls):
        pre_activation = low_back(jnp.einsum('hnf,hfk->hnk', feat, w_one, precision=HIGH))
        normalized_input = layer_normalize(pre_activation, 1)
        branch_index = lower_precision(jax.nn.gelu(normalized_input * first_gain[:, None, :] + first_bias[:, None, :]) * keep_mask)
        mixed_in = lower_precision(jax.nn.gelu(branch_index))
        mixed_output = low_back(jnp.einsum('hnk,hkj->nj', mixed_in, w_two.reshape(HOPS, HIDDEN_SIZE, HIDDEN_SIZE), precision=HIGH))
        head = lower_precision(jax.nn.gelu(layer_normalize(mixed_output, 0) * g_two + b_two))
        logits = low_back(jnp.dot(head, w_cls, precision=HIGH) + b_cls)
        log_probs = jax.nn.log_softmax(logits, axis=-1)
        loss = -jnp.mean(lax.optimization_barrier(jnp.sum(onehot * log_probs, axis=1)))
        return (loss, log_probs)
    params = (features.astype(jnp.float32), branch_weight.astype(jnp.float32), branch_gain, branch_bias, mix_weight.astype(jnp.float32), mixing_norm_gain, mixing_norm_bias, class_weight.astype(jnp.float32), class_bias)
    loss, vjp_fn, log_probs = jax.vjp(forward, *params, has_aux=True)
    grads = vjp_fn(jnp.float32(1.0))
    return (log_probs, loss, grads[0], grads[1], grads[2], grads[3], grads[4], grads[5], grads[6], grads[7], grads[8])
```

```python
import functools
import math

import jax
import jax.numpy as jnp
from jax import lax
from jax.experimental import pallas as pl
from jax.experimental.layout import Layout, with_layout_constraint
from jax.experimental.pallas import tpu as pltpu
from jax.sharding import PartitionSpec as P

MESH = pl.DeviceIdType.MESH
EPS = 1e-05
HOPS = 4
ONES = 100
FP = 112
TILE = 256
C0 = math.sqrt(2.0 / math.pi)
C1 = C0 * 0.044715
F32 = jnp.float32
BF16 = jnp.bfloat16


def dot(a, b):
    return lax.dot_general(a, b, (((1,), (0,)), ((), ())), preferred_element_type=F32)


def dot_nt(a, b):
    return lax.dot_general(a, b, (((1,), (1,)), ((), ())), preferred_element_type=F32)


def split2(x):
    hi = x.astype(BF16)
    return hi, (x - hi.astype(F32)).astype(BF16)


def split3(x):
    hi = x.astype(BF16)
    rest = x - hi.astype(F32)
    mid = rest.astype(BF16)
    return hi, mid, (rest - mid.astype(F32)).astype(BF16)


def gelu_slope(z):
    u = z * z
    t = jnp.tanh(z * (C0 + C1 * u))
    s = 0.5 * t + 0.5
    g = z * s
    return g, s + (g - g * s) * (2.0 * C0 + 6.0 * C1 * u)


def fold(x):
    total = x[:, :128]
    for i in range(1, x.shape[1] // 128):
        total = total + x[:, i * 128 : (i + 1) * 128]
    return total


def spread(c, n):
    return jnp.concatenate([c] * (n // 128), axis=1)


def row_of(acc):
    return jnp.sum(acc.T, axis=0, keepdims=True)


def col_of(row):
    return jnp.broadcast_to(row, (128, row.shape[1])).T


def each(lo, hi, body):
    if hi - lo <= 16:
        for i in range(lo, hi):
            body(i)
    else:
        pl.loop(lo, hi)(body)


class Alloc:
    def __init__(self):
        self.n = 0

    def __call__(self, count):
        base = self.n
        self.n += count
        return base


def sem_plan(R):
    Z = R // 2
    a = Alloc()
    names = {}
    for name, count in (
        ("feat", 4), ("w", 4), ("ws", 4), ("zf", Z), ("dd", 1), ("s1", R), ("ab", 4), ("gr", R),
        ("s2h", 4), ("s2r", R), ("lp", 4), ("s3h", 4), ("s3r", R), ("cwh", 4), ("cwr", R), ("cwg", 4),
        ("pair", 1), ("hop", 4), ("zr", Z), ("zg", Z), ("ddm", 1), ("d", 4), ("p", 4), ("q", 4),
        ("qr", R), ("pp", 1), ("pz", Z), ("pd", 1),
    ):
        names[name] = a(count)
    return names, a.n


def chunk(base, i, rows, pieces, cols):
    if rows // pieces >= 16:
        take = rows // pieces
        return pl.ds(pl.multiple_of(base + i * take, 16), take), pl.ds(0, cols)
    m = 16 * pieces // rows
    wide = cols // m
    return (
        pl.ds(pl.multiple_of(base + (i // m) * 16, 16), 16),
        pl.ds(pl.multiple_of((i % m) * wide, 128), wide),
    )


def main_kernel(
    R,
    nodes,
    ft, wb, bgain, bbias, wm, gain2, bias2, wc, cb, lab, msk,
    o_lp, o_d, o_m, o_mix, o_gw, o_small, o_cw,
    fs, fx, wx, wl, aw, wmx, wmT, keep, mi, gp, mixed, dn2, dmx,
    gbuf, s1, ab, s2h, s2r, s3h, s3r, cwp, cwh, cwr, cwg, lps,
    wcs, cbs, acc0, acc1, accl, accw, cols,
    dmp, pr, hr, zr, fin, dsend, pT, ps, prv, qs, qv, qr, ph, pz, pfin,
    ss, rs,
):
    names, _ = sem_plan(R)
    Z = R // 2
    h = lax.axis_index("hop")
    r = lax.axis_index("rows")
    c = lax.rem(r, 2)
    zi = lax.div(r, 2)
    sib = r + 1 - 2 * c
    local = ft.shape[1]
    sub = local // HOPS
    hid = wm.shape[0]
    half = hid // 2
    T = sub // TILE
    inv_n = 1.0 / nodes
    peers = [h, h + 1 - 2 * lax.rem(h, 2), h + 2 - 4 * lax.div(h, 2), 3 - h]

    def rc(src, dst, name, i, hh, rr):
        return pltpu.make_async_remote_copy(
            src_ref=src, dst_ref=dst, send_sem=ss.at[names[name] + i], recv_sem=rs.at[names[name] + i],
            device_id=(hh, rr), device_id_type=MESH,
        )

    barrier = pltpu.get_barrier_semaphore()

    def greet(hh, rr):
        pl.semaphore_signal(barrier, inc=1, device_id=(hh, rr), device_id_type=MESH)

    for d in range(1, HOPS):
        greet(peers[d], r)

    @functools.partial(each, 1, R)
    def _(e):
        greet(h, lax.rem(r + e, R))

    def rows_start(buf, name):
        @functools.partial(each, 1, R)
        def _(e):
            rc(buf.at[r], buf.at[r], name, e, h, lax.rem(r + e, R)).start()

    def rows_wait(buf, name):
        @functools.partial(each, 1, R)
        def _(e):
            src = lax.rem(r + R - e, R)
            cp = rc(buf.at[src], buf.at[src], name, e, h, lax.rem(r + e, R))
            cp.wait_send()
            cp.wait_recv()

    def hops_start(buf, name):
        for d in range(1, HOPS):
            rc(buf.at[h], buf.at[h], name, d, peers[d], r).start()

    def hops_wait(buf, name):
        for d in range(1, HOPS):
            cp = rc(buf.at[peers[d]], buf.at[peers[d]], name, d, peers[d], r)
            cp.wait_send()
            cp.wait_recv()

    def total(buf, n):
        t = buf[0]
        for i in range(1, n):
            t = t + buf[i]
        return t

    for i in range(4):
        lanes = pl.ds(i * sub, sub)
        fs[pl.ds(0, 96), lanes] = ft[pl.ds(0, 96), lanes]
        row = lax.broadcasted_iota(jnp.int32, (32, sub), 0)
        fs[pl.ds(96, 32), lanes] = jnp.where(row == ONES - 96, 1.0, 0.0).astype(BF16)
        fs[pl.ds(96, 4), lanes] = ft[pl.ds(96, 4), lanes]
    wx[0, pl.ds(96, 32), :] = jnp.zeros((32, hid), BF16)
    wx[0, pl.ds(0, 100), :] = wb[...]
    for d in range(1, HOPS):
        fx[d, pl.ds(FP, 128 - FP), :] = jnp.zeros((128 - FP, sub), BF16)
        wx[d, pl.ds(FP, 128 - FP), :] = jnp.zeros((128 - FP, hid), BF16)
    own_lanes = pl.ds(pl.multiple_of(h * sub, sub), sub)
    fx[0] = fs[:, own_lanes]
    wmx[0] = wm[...]

    pl.semaphore_wait(barrier, HOPS - 1 + R - 1)

    wslice = chunk(c * half, zi, half, Z, hid)

    def feat_copy(d):
        lanes = pl.ds(pl.multiple_of(peers[d] * sub, sub), sub)
        return rc(fs.at[pl.ds(0, FP), lanes], fx.at[d, pl.ds(0, FP), :], "feat", d, peers[d], r)

    def w_copy(d):
        return rc(wx.at[0, pl.ds(0, FP), :], wx.at[d, pl.ds(0, FP), :], "w", d, peers[d], r)

    def ws_copy(d):
        rows, lanes = wslice
        return rc(wmx.at[0, rows, lanes], wmx.at[d, rows, lanes], "ws", d, peers[d], r)

    for d in range(1, HOPS):
        w_copy(d).start()
    for d in range(1, HOPS):
        ws_copy(d).start()
    for d in range(1, HOPS):
        feat_copy(d).start()

    def gram(i, g):
        f = fs[:, pl.ds(pl.multiple_of(i * sub, sub), sub)]
        return g + dot_nt(f, f)

    g = lax.fori_loop(0, HOPS, gram, jnp.zeros((128, 128), F32))
    wown = wx[0]
    wown32 = wown.astype(F32)
    g1, g2, g3 = split3(g)
    gw = dot(g1, wown) + dot(g2, wown) + dot(g3, wown)
    s1[r, :, pl.ds(0, hid)] = gw[ONES : ONES + 1, :]
    s1[r, :, pl.ds(hid, hid)] = jnp.sum(gw * wown32, axis=0, keepdims=True)
    rows_start(s1, "s1")
    gbuf[r] = g[:FP]

    for d in range(HOPS):
        for b in range(sub // 128):
            where_b = h * (sub // 128) + b
            late = peers[d] - 2
            col = jnp.maximum(late, 0)
            m = jnp.where(late >= 0, msk[col, where_b], 1)
            keep[d, :, pl.ds(b * 128, 128)] = jnp.full((1, 128), m.astype(F32))
    wcs[...] = jnp.zeros(wcs.shape, F32)
    wcs[pl.ds(0, wc.shape[0]), :] = wc[...].astype(F32)
    cbs[...] = jnp.zeros(cbs.shape, F32)
    cbs[pl.ds(0, 1), pl.ds(0, cb.shape[1])] = cb[...]
    ncls = wc.shape[0]
    wmT[0] = wmx[0].astype(F32).T.astype(BF16)

    rows_wait(s1, "s1")
    st = total(s1, R)
    mean = st[:, :hid] * inv_n
    var = st[:, hid:] * inv_n - mean * mean
    inv = lax.rsqrt(var + EPS)
    scale = inv * bgain[...]
    ab[0, :, pl.ds(0, hid)] = scale
    ab[0, :, pl.ds(hid, hid)] = bbias[...] - mean * scale

    def ab_copy(d):
        return rc(ab.at[0], ab.at[d], "ab", d, peers[d], r)

    for d in range(1, HOPS):
        ab_copy(d).start()

    rows_start(gbuf, "gr")
    for d in range(1, HOPS):
        cp = ws_copy(d)
        cp.wait_send()
        cp.wait_recv()

    def zf_copy(e, which):
        rows, lanes = chunk(c * half, which, half, Z, hid)
        ref = wmx.at[pl.ds(1, HOPS - 1), rows, lanes]
        return rc(ref, ref, "zf", e, h, lax.rem(zi + e, Z) * 2 + c)

    @functools.partial(each, 1, Z)
    def _(e):
        zf_copy(e, zi).start()

    def prepare(d):
        a = ab[d, :, pl.ds(0, hid)]
        b = ab[d, :, pl.ds(hid, hid)]
        ws = wx[d].astype(F32) * a
        aw[d] = ws[:FP].astype(BF16)
        row = lax.broadcasted_iota(jnp.int32, (128, hid), 0)
        wt = jnp.where(row == ONES, b, ws).T
        hi, lo = split2(wt)
        wl[d, :, pl.ds(0, 128)] = hi
        wl[d, :, pl.ds(128, 128)] = lo

    def forward(d):
        @pl.loop(0, T)
        def _(t):
            n = pl.ds(pl.multiple_of(t * TILE, TILE), TILE)
            f = fx[d, :, n]
            z = dot(wl[d], jnp.concatenate([f, f], axis=0))
            k = keep[d, :, n]
            parts = []
            for i in range(0, hid, 64):
                gv, dg = gelu_slope(z[i : i + 64])
                bv = (gv * k).astype(BF16).astype(F32)
                g2v, dg2 = gelu_slope(bv)
                m = g2v.astype(BF16)
                mi[d, pl.ds(i, 64), n] = m
                gp[d, pl.ds(i, 64), n] = (dg * dg2 * k).astype(BF16)
                parts.append(m)
            add = dot(wmT[d], jnp.concatenate(parts, axis=0))
            if d == 0:
                mixed[:, n] = add
            else:
                mixed[:, n] = mixed[:, n] + add

    prepare(0)
    forward(0)

    @functools.partial(each, 1, Z)
    def _(e):
        src = lax.rem(zi + Z - e, Z)
        zf_copy(e, zi).wait_send()
        zf_copy(e, src).wait_recv()

    def dd_copy(core):
        ref = wmx.at[pl.ds(1, HOPS - 1), pl.ds(pl.multiple_of(core * half, half), half), :]
        return rc(ref, ref, "dd", 0, h, sib)

    dd_copy(c).start()
    for d in range(1, HOPS):
        cp = w_copy(d)
        cp.wait_send()
        cp.wait_recv()
        cp = ab_copy(d)
        cp.wait_send()
        cp.wait_recv()
        prepare(d)
    dd_copy(c).wait_send()
    dd_copy(1 - c).wait_recv()
    for d in range(1, HOPS):
        wmT[d] = wmx[d].astype(F32).T.astype(BF16)
        cp = feat_copy(d)
        cp.wait_send()
        cp.wait_recv()
        forward(d)

    acc0[...] = jnp.zeros(acc0.shape, F32)
    acc1[...] = jnp.zeros(acc1.shape, F32)

    @pl.loop(0, T)
    def _(t):
        n = pl.ds(pl.multiple_of(t * TILE, TILE), TILE)
        x = mixed[:, n]
        acc0[...] += fold(x)
        acc1[...] += fold(x * x)

    s2h[h, :, pl.ds(0, hid)] = row_of(acc0[...])
    s2h[h, :, pl.ds(hid, hid)] = row_of(acc1[...])
    hops_start(s2h, "s2h")
    hops_wait(s2h, "s2h")
    s2r[r] = total(s2h, HOPS)
    rows_start(s2r, "s2r")
    wc48 = wcs[pl.ds(0, 48), :].astype(BF16)
    wcN = wcs[...].T.astype(BF16)
    crow = lax.broadcasted_iota(jnp.int32, (128, 128), 0)
    cbc = jnp.where(crow < ncls, jnp.broadcast_to(cbs[pl.ds(0, 1), :], (128, 128)).T, -1e30)[:48]
    rows_wait(s2r, "s2r")
    st2 = total(s2r, R)
    mean2 = st2[:, :hid] * inv_n
    inv2 = lax.rsqrt(st2[:, hid:] * inv_n - mean2 * mean2 + EPS)
    scale2 = inv2 * gain2[...]
    cols[0] = col_of(scale2)
    cols[1] = col_of(bias2[...] - mean2 * scale2)
    acc0[...] = jnp.zeros(acc0.shape, F32)
    acc1[...] = jnp.zeros(acc1.shape, F32)
    accl[...] = jnp.zeros(accl.shape, F32)
    accw[...] = jnp.zeros(accw.shape, F32)

    @pl.loop(0, T)
    def _(t):
        n = pl.ds(pl.multiple_of(t * TILE, TILE), TILE)
        heads, slopes = [], []
        for i in range(0, hid, 64):
            rows = pl.ds(i, 64)
            z2 = mixed[rows, n] * spread(cols[0, rows, :], TILE) + spread(cols[1, rows, :], TILE)
            gv, dg = gelu_slope(z2)
            heads.append(gv.astype(BF16))
            slopes.append(dg)
        hb = jnp.concatenate(heads, axis=0)
        lg = dot(wc48, hb) + spread(cbc, TILE)
        lg = lg - jnp.max(lg, axis=0, keepdims=True)
        ex = jnp.exp(lg)
        se = jnp.sum(ex, axis=0, keepdims=True)
        lp = lg - jnp.log(se)
        lps[:, n] = jnp.maximum(lp, -1e30).astype(BF16)
        own = pl.ds(pl.multiple_of(h * sub + t * TILE, TILE), TILE)
        hit = lax.broadcasted_iota(jnp.int32, (48, TILE), 0) == lab[:, own]
        accl[pl.ds(48, 48), :] += fold(jnp.where(hit, lp, 0.0))
        dl = ((ex / se - jnp.where(hit, 1.0, 0.0)) * inv_n).astype(BF16)
        accl[pl.ds(0, 48), :] += fold(dl.astype(F32))
        accw[...] += dot_nt(dl, hb)
        dh = dot(wcN, jnp.concatenate([dl, jnp.zeros((80, TILE), BF16)], axis=0))
        for j, i in enumerate(range(0, hid, 64)):
            rows = pl.ds(i, 64)
            dn = dh[i : i + 64] * slopes[j]
            dn2[rows, n] = dn
            acc0[rows, :] += fold(dn * mixed[rows, n])
            acc1[rows, :] += fold(dn)

    s3h[h, :, pl.ds(0, hid)] = row_of(acc0[...])
    s3h[h, :, pl.ds(hid, hid)] = row_of(acc1[...])
    zpad = jnp.zeros((80, 128), F32)
    s3h[h, :, pl.ds(2 * hid, 128)] = row_of(jnp.concatenate([accl[pl.ds(0, 48), :], zpad], axis=0))
    s3h[h, :, pl.ds(2 * hid + 128, 128)] = row_of(jnp.concatenate([accl[pl.ds(48, 48), :], zpad], axis=0))
    hops_start(s3h, "s3h")

    o_own = pl.ds(pl.multiple_of(h * sub, sub), sub)

    def lp_copy(d):
        return rc(lps, o_lp.at[:, o_own], "lp", d, peers[d], r)

    def cwh_copy(d):
        return rc(cwp.at[d], cwh.at[d], "cwh", d, peers[d], r)

    q = hid // HOPS
    for d in range(HOPS):
        cwp[d] = accw[:, pl.ds(pl.multiple_of(peers[d] * q, q), q)]
    hops_wait(s3h, "s3h")
    s3r[r] = total(s3h, HOPS)
    rows_start(s3r, "s3r")
    for d in range(1, HOPS):
        cwh_copy(d).start()
    for d in range(1, HOPS):
        lp_copy(d).start()
    rows_wait(s3r, "s3r")
    st3 = total(s3r, R)
    db2 = st3[:, hid : 2 * hid]
    dg2t = inv2 * (st3[:, :hid] - mean2 * db2)
    o_small[pl.ds(0, 1), :] = dg2t
    o_small[pl.ds(1, 1), :] = db2
    o_small[pl.ds(4, 1), pl.ds(0, 256)] = st3[:, 2 * hid : 2 * hid + 256]
    o_small[pl.ds(4, 1), pl.ds(256, hid - 256)] = jnp.zeros((1, hid - 256), F32)
    t2 = scale2 * inv2 * dg2t * inv_n
    cols[1] = col_of(-t2)
    cols[2] = col_of(t2 * mean2 - scale2 * db2 * inv_n)

    @pl.loop(0, T)
    def _(t):
        n = pl.ds(pl.multiple_of(t * TILE, TILE), TILE)
        for i in range(0, hid, 64):
            rows = pl.ds(i, 64)
            v = dn2[rows, n] * spread(cols[0, rows, :], TILE)
            v = v + mixed[rows, n] * spread(cols[1, rows, :], TILE) + spread(cols[2, rows, :], TILE)
            dmx[rows, n] = v.astype(BF16)

    @pl.loop(0, 2 * HOPS)
    def _(i):
        d = lax.div(i, 2)
        rows = pl.ds(pl.multiple_of(lax.rem(i, 2) * half, half), half)
        dmp[d, rows, :] = dot_nt(mi[d, rows, :], dmx[...]).astype(BF16)

    mine = pl.ds(pl.multiple_of(c * half, half), half)
    theirs = pl.ds(pl.multiple_of((1 - c) * half, half), half)
    pair = rc(dmp.at[:, theirs, :], pr, "pair", 0, h, sib)
    pair.start()

    for d in range(1, HOPS):
        cp = cwh_copy(d)
        cp.wait_send()
        cp.wait_recv()
    cwr[r] = cwp[0] + (cwh[1] + cwh[2] + cwh[3])
    rows_start(cwr, "cwr")

    def d_copy(d):
        return rc(dsend.at[d], o_d.at[h], "d", d, peers[d], r)

    def p_copy(d):
        return rc(ps.at[d], prv.at[d], "p", d, peers[d], r)

    def q_copy(d):
        return rc(qs.at[d], qv.at[d], "q", d, peers[d], r)

    def backward(d):
        pT[...] = jnp.zeros(pT.shape, F32)

        @pl.loop(0, T)
        def _(t):
            n = pl.ds(pl.multiple_of(t * TILE, TILE), TILE)
            dc = dot(wmx[d], dmx[:, n])
            parts = []
            for i in range(0, hid, 64):
                parts.append((dc[i : i + 64] * gp[d, pl.ds(i, 64), n].astype(F32)).astype(BF16))
            dn = jnp.concatenate(parts, axis=0)
            pT[...] += dot_nt(dn, fx[d, :, n])
            dsend[d, :, n] = dot(aw[d], dn).astype(BF16)

        pw = pT[...].T
        qs[d, :, pl.ds(0, hid)] = jnp.sum(pw * wx[d].astype(F32), axis=0, keepdims=True)
        qs[d, :, pl.ds(hid, hid)] = pw[ONES : ONES + 1, :]
        if d == 0:
            return pw[:FP]
        ps[d] = pw[:FP].astype(BF16)
        q_copy(d).start()
        p_copy(d).start()
        d_copy(d).start()

    backward(1)

    pair.wait_send()
    pair.wait_recv()

    @pl.loop(0, HOPS)
    def _(d):
        dmp[d, mine, :] = (dmp[d, mine, :].astype(F32) + pr[d].astype(F32)).astype(BF16)

    def hop_copy(d):
        return rc(dmp.at[d, mine, :], hr.at[d], "hop", d, peers[d], r)

    for d in range(1, HOPS):
        hop_copy(d).start()
    rows_wait(cwr, "cwr")
    cwg[h] = total(cwr, R)
    hops_start(cwg, "cwg")

    backward(2)

    for d in range(1, HOPS):
        cp = hop_copy(d)
        cp.wait_send()
        cp.wait_recv()
    hsum = dmp[0, mine, :].astype(F32) + hr[1].astype(F32) + hr[2].astype(F32) + hr[3].astype(F32)
    hr[0] = hsum.astype(BF16)

    def zr_copy(e, which):
        rows, lanes = chunk(0, which, half, Z, hid)
        return rc(hr.at[0, rows, lanes], zr.at[e], "zr", e, h, lax.rem(zi + e, Z) * 2 + c)

    @functools.partial(each, 1, Z)
    def _(e):
        zr_copy(e, lax.rem(zi + e, Z)).start()

    hops_wait(cwg, "cwg")
    for j in range(HOPS):
        o_cw[:, pl.ds(j * q, q)] = cwg[j]

    backward(3)

    @functools.partial(each, 1, Z)
    def _(e):
        cp = zr_copy(e, lax.rem(zi + e, Z))
        cp.wait_send()
        cp.wait_recv()

    rows, lanes = chunk(0, zi, half, Z, hid)
    zt = hr[0, rows, lanes].astype(F32)
    for e in range(1, Z):
        zt = zt + zr[e].astype(F32)
    frows, flanes = chunk(c * half, zi, half, Z, hid)
    fin[frows, flanes] = zt.astype(BF16)

    def zg_copy(e, which):
        rows, lanes = chunk(c * half, which, half, Z, hid)
        ref = fin.at[rows, lanes]
        return rc(ref, ref, "zg", e, h, lax.rem(zi + e, Z) * 2 + c)

    @functools.partial(each, 1, Z)
    def _(e):
        zg_copy(e, zi).start()

    pw0 = backward(0)
    for d in range(1, HOPS):
        cp = q_copy(d)
        cp.wait_send()
        cp.wait_recv()
    qr[r] = qs[0] + (qv[1] + qv[2] + qv[3])
    rows_start(qr, "qr")
    own_d = pltpu.make_async_copy(dsend.at[0], o_d.at[h], ss.at[names["d"]])
    own_d.start()
    own_lp = pltpu.make_async_copy(lps, o_lp.at[:, o_own], ss.at[names["lp"]])
    own_lp.start()

    for d in range(1, HOPS):
        cp = p_copy(d)
        cp.wait_send()
        cp.wait_recv()
    pw0 = pw0 + prv[1].astype(F32) + prv[2].astype(F32) + prv[3].astype(F32)
    ps[0] = pw0.astype(BF16)
    pmine = pl.ds(pl.multiple_of(c * half, half), half)
    ptheirs = pl.ds(pl.multiple_of((1 - c) * half, half), half)
    pp = rc(ps.at[0, :, ptheirs], ph, "pp", 0, h, sib)
    pp.start()

    @functools.partial(each, 1, Z)
    def _(e):
        zg_copy(e, zi).wait_send()
        zg_copy(e, lax.rem(zi + Z - e, Z)).wait_recv()

    def ddm_copy(core):
        ref = fin.at[pl.ds(pl.multiple_of(core * half, half), half), :]
        return rc(ref, ref, "ddm", 0, h, sib)

    ddm_copy(c).start()
    pp.wait_send()
    pp.wait_recv()
    pz[zi] = (ps[0, :, pmine].astype(F32) + ph[...].astype(F32)).astype(BF16)

    def pz_copy(e, which):
        return rc(pz.at[which], pz.at[which], "pz", e, h, lax.rem(zi + e, Z) * 2 + c)

    @functools.partial(each, 1, Z)
    def _(e):
        pz_copy(e, zi).start()

    rows_wait(qr, "qr")
    qt = total(qr, R)
    db = qt[:, hid:]
    dgn = inv * (qt[:, :hid] - mean * db)
    o_small[pl.ds(2, 1), :] = dgn
    o_small[pl.ds(3, 1), :] = db
    c1 = scale * db * inv_n
    c2 = inv * scale * dgn * inv_n
    shift = c1 - mean * c2
    row = lax.broadcasted_iota(jnp.int32, (128, hid), 0)
    q1, q2 = split2(jnp.where(row == ONES, shift, wown32 * c2))
    o_m[...] = (dot_nt(wown, q1) + dot_nt(wown, q2))[:FP]
    rows_wait(gbuf, "gr")
    g1, g2, g3 = split3(total(gbuf, R))
    gq = dot(g1, q1) + dot(g2, q1) + dot(g3, q1) + dot(g1, q2) + dot(g2, q2)

    @functools.partial(each, 1, Z)
    def _(e):
        pz_copy(e, zi).wait_send()
        pz_copy(e, lax.rem(zi + Z - e, Z)).wait_recv()

    pt = pz[0].astype(F32)
    for j in range(1, Z):
        pt = pt + pz[j].astype(F32)
    pfin[c] = pt.astype(BF16)

    def pd_copy(core):
        return rc(pfin.at[core], pfin.at[core], "pd", 0, h, sib)

    pd_copy(c).start()
    ddm_copy(c).wait_send()
    ddm_copy(1 - c).wait_recv()
    o_mix[...] = fin[...]
    pd_copy(c).wait_send()
    pd_copy(1 - c).wait_recv()
    ptot = jnp.concatenate([pfin[0], pfin[1]], axis=1).astype(F32)
    o_gw[...] = ptot * scale - gq
    own_d.wait()
    own_lp.wait()
    for d in range(1, HOPS):
        cp = d_copy(d)
        cp.wait_send()
        cp.wait_recv()
        cp = lp_copy(d)
        cp.wait_send()
        cp.wait_recv()


def last_kernel(
    nodes,
    ft, d, lp, m, mix, gw, small, cw,
    o_lp, o_gf, o_mix, o_gw, o_gg, o_gb, o_hg, o_hb, o_cw, o_cb, o_loss,
):
    feat, n = ft.shape
    ncls = o_lp.shape[0]
    o_lp[...] = lp[...].astype(F32)[:ncls]
    mm = m[...]
    hi, lo = split2(mm[:feat, :feat])
    f = ft[...]
    gf = d[0].astype(F32)[:feat] - dot(hi, f) - dot(lo, f) - mm[:feat, ONES : ONES + 1]
    for i in range(n // 128):
        o_gf[:, i, :] = gf[:, i * 128 : (i + 1) * 128]

    @pl.when(pl.program_id(0) == 0)
    def _():
        hid = mix.shape[1]
        o_mix[...] = mix[...].astype(F32)
        for i in range(hid // 128):
            o_gw[:, i, :] = gw[pl.ds(0, feat), pl.ds(i * 128, 128)]
        o_hg[...] = small[pl.ds(0, 1), :]
        o_hb[...] = small[pl.ds(1, 1), :]
        o_gg[...] = small[pl.ds(2, 1), :]
        o_gb[...] = small[pl.ds(3, 1), :]
        o_cw[...] = cw[pl.ds(0, ncls), :]
        o_cb[...] = small[pl.ds(4, 1), pl.ds(0, ncls)]
        o_loss[...] = jnp.sum(small[pl.ds(4, 1), pl.ds(128, 128)], axis=1, keepdims=True) * (-1.0 / nodes)


def shards(
    R, features, branch_weight, branch_gain, branch_bias, mix_weight, mixing_norm_gain, mixing_norm_bias,
    class_weight, class_bias, labels, hop_mask,
):
    local, feat = features.shape[1:]
    hid = mix_weight.shape[0]
    ncls = class_weight.shape[1]
    nodes = local * R
    sub = local // HOPS
    Z = R // 2
    half = hid // 2
    zrows, zcols = chunk(0, 0, half, Z, hid)
    assert feat == ONES and ncls == 47 and local // hop_mask.shape[0] == 128
    ft = features[0].T
    sd = jax.ShapeDtypeStruct
    vm = pl.BlockSpec(memory_space=pltpu.VMEM)
    hbm = pl.BlockSpec(memory_space=pl.ANY)
    _, nsem = sem_plan(R)
    V = pltpu.VMEM
    outs = pl.pallas_call(
        functools.partial(main_kernel, R, nodes),
        out_shape=(
            sd((48, local), BF16),
            sd((HOPS, FP, sub), BF16),
            sd((FP, 128), F32),
            sd((hid, hid), BF16),
            sd((FP, hid), F32),
            sd((8, hid), F32),
            sd((48, hid), F32),
        ),
        in_specs=[vm] * 10 + [pl.BlockSpec(memory_space=pltpu.SMEM)],
        out_specs=(hbm, hbm, vm, vm, vm, vm, vm),
        scratch_shapes=[
            V((128, local), BF16),
            V((HOPS, 128, sub), BF16),
            V((HOPS, 128, hid), BF16),
            V((HOPS, hid, 256), BF16),
            V((HOPS, FP, hid), BF16),
            V((HOPS, hid, hid), BF16),
            V((HOPS, hid, hid), BF16),
            V((HOPS, 1, sub), F32),
            V((HOPS, hid, sub), BF16),
            V((HOPS, hid, sub), BF16),
            V((hid, sub), F32),
            V((hid, sub), F32),
            V((hid, sub), BF16),
            V((R, FP, 128), F32),
            V((R, 1, 2 * hid), F32),
            V((HOPS, 1, 2 * hid), F32),
            V((HOPS, 1, 2 * hid), F32),
            V((R, 1, 2 * hid), F32),
            V((HOPS, 1, 2 * hid + 256), F32),
            V((R, 1, 2 * hid + 256), F32),
            V((HOPS, 48, hid // HOPS), F32),
            V((HOPS, 48, hid // HOPS), F32),
            V((R, 48, hid // HOPS), F32),
            V((HOPS, 48, hid // HOPS), F32),
            V((48, sub), BF16),
            V((128, hid), F32),
            V((8, 128), F32),
            V((hid, 128), F32),
            V((hid, 128), F32),
            V((96, 128), F32),
            V((48, hid), F32),
            V((3, hid, 128), F32),
            V((HOPS, hid, hid), BF16),
            V((HOPS, half, hid), BF16),
            V((HOPS, half, hid), BF16),
            V((max(Z, 2), zrows.size, zcols.size), BF16),
            V((hid, hid), BF16),
            V((HOPS, FP, sub), BF16),
            V((hid, 128), F32),
            V((HOPS, FP, hid), BF16),
            V((HOPS, FP, hid), BF16),
            V((HOPS, 1, 2 * hid), F32),
            V((HOPS, 1, 2 * hid), F32),
            V((R, 1, 2 * hid), F32),
            V((FP, half), BF16),
            V((Z, FP, half), BF16),
            V((2, FP, half), BF16),
            pltpu.SemaphoreType.DMA((nsem,)),
            pltpu.SemaphoreType.DMA((nsem,)),
        ],
        compiler_params=pltpu.CompilerParams(
            collective_id=0, has_side_effects=True, vmem_limit_bytes=63 * 1024 * 1024
        ),
        cost_estimate=pl.CostEstimate(flops=2 * 8 * 10**9, bytes_accessed=10**7, transcendentals=10**7),
        name="main",
    )(
        ft, branch_weight[0], branch_gain, branch_bias, mix_weight, mixing_norm_gain[None], mixing_norm_bias[None],
        class_weight.T, class_bias[None], labels[None], hop_mask.T,
    )
    lp, dd, m, mix, gw, small, cw = outs
    nb = min(1024, sub)
    per = sub // nb
    whole = lambda shape: pl.BlockSpec(shape, lambda i: (0,) * len(shape))
    lp, gf, mix, gw, gg, gb, hg, hb, cw, cb, loss = pl.pallas_call(
        functools.partial(last_kernel, nodes),
        grid=(local // nb,),
        out_shape=(
            sd((ncls, local), F32),
            sd((feat, local // 128, 128), F32),
            sd((hid, hid), F32),
            sd((feat, hid // 128, 128), F32),
            sd((1, hid), F32),
            sd((1, hid), F32),
            sd((1, hid), F32),
            sd((1, hid), F32),
            sd((ncls, hid), F32),
            sd((1, ncls), F32),
            sd((1, 1), F32),
        ),
        in_specs=[
            pl.BlockSpec((feat, nb), lambda i: (0, i)),
            pl.BlockSpec((1, FP, nb), lambda i: (i // per, 0, i % per)),
            pl.BlockSpec((48, nb), lambda i: (0, i)),
            whole((FP, 128)),
            whole((hid, hid)),
            whole((FP, hid)),
            whole((8, hid)),
            whole((48, hid)),
        ],
        out_specs=(
            pl.BlockSpec((ncls, nb), lambda i: (0, i)),
            pl.BlockSpec((feat, nb // 128, 128), lambda i: (0, i, 0)),
            whole((hid, hid)),
            whole((feat, hid // 128, 128)),
            whole((1, hid)),
            whole((1, hid)),
            whole((1, hid)),
            whole((1, hid)),
            whole((ncls, hid)),
            whole((1, ncls)),
            whole((1, 1)),
        ),
        compiler_params=pltpu.CompilerParams(vmem_limit_bytes=60 * 1024 * 1024),
        name="last",
    )(ft, dd, lp, m, mix, gw, small, cw)
    return (
        lp.T,
        loss[0, 0],
        with_layout_constraint(gf.reshape(feat, 1, local), Layout((0, 1, 2))).transpose(1, 2, 0),
        gw.reshape(1, feat, hid),
        gg,
        gb,
        mix,
        hg[0],
        hb[0],
        cw.T,
        cb[0],
    )


def solution(mesh):
    placed = (
        P("hop", "rows", None), P("hop", None, None), P("hop", None), P("hop", None), P("hop", None),
        P(), P(), P(), P(), P("rows"), P("rows", None),
    )
    assert mesh.shape["hop"] == HOPS
    return jax.shard_map(
        functools.partial(shards, mesh.shape["rows"]),
        mesh=mesh,
        in_specs=placed,
        out_specs=(
            P("rows", None), P(), P("hop", "rows", None), P("hop", None, None), P("hop", None), P("hop", None),
            P("hop", None), P(), P(), P(), P(),
        ),
        check_vma=False,
    )
```

```python
import functools
import math

import jax
import jax.numpy as jnp
from jax import lax
from jax.experimental import pallas as pl
from jax.experimental.layout import Layout, with_layout_constraint
from jax.experimental.pallas import tpu as pltpu
from jax.sharding import PartitionSpec as P

MESH = pl.DeviceIdType.MESH
EPS = 1e-05
HOPS = 4
ONES = 100
FP = 112
TILE = 256
C0 = math.sqrt(2.0 / math.pi)
C1 = C0 * 0.044715
KAPPA = C1 ** (1.0 / 3.0)
ALPHA = C0 / KAPPA
F32 = jnp.float32
BF16 = jnp.bfloat16


def dot(a, b):
    return lax.dot_general(a, b, (((1,), (0,)), ((), ())), preferred_element_type=F32)


def dot_nt(a, b):
    return lax.dot_general(a, b, (((1,), (1,)), ((), ())), preferred_element_type=F32)


def split2(x):
    hi = x.astype(BF16)
    return hi, (x - hi.astype(F32)).astype(BF16)


def split3(x):
    hi = x.astype(BF16)
    rest = x - hi.astype(F32)
    mid = rest.astype(BF16)
    return hi, mid, (rest - mid.astype(F32)).astype(BF16)


def gelu_slope(z):
    u = z * z
    t = jnp.tanh(z * (C0 + C1 * u))
    s = 0.5 * t + 0.5
    g = z * s
    return g, s + (g - g * s) * (2.0 * C0 + 6.0 * C1 * u)


def scaled_gelu_slope(y):
    u = y * y
    t = jnp.tanh(y * (u + ALPHA))
    up = t + 1.0
    g = y * up
    return g, up + (g * (1.0 - t)) * (3.0 * u + ALPHA)


def fold(x):
    total = x[:, :128]
    for i in range(1, x.shape[1] // 128):
        total = total + x[:, i * 128 : (i + 1) * 128]
    return total


def spread(c, n):
    return jnp.concatenate([c] * (n // 128), axis=1)


def row_of(acc):
    return jnp.sum(acc.T, axis=0, keepdims=True)


def col_of(row):
    return jnp.broadcast_to(row, (128, row.shape[1])).T


def each(lo, hi, body):
    if hi - lo <= 16:
        for i in range(lo, hi):
            body(i)
    else:
        pl.loop(lo, hi)(body)


class Alloc:
    def __init__(self):
        self.n = 0

    def __call__(self, count):
        base = self.n
        self.n += count
        return base


def sem_plan(R):
    Z = R // 2
    a = Alloc()
    names = {}
    for name, count in (
        ("feat", 4), ("ws", 4), ("zf", 4), ("dd", 4), ("s1", R), ("ab", 4), ("gr", R),
        ("s2h", 4), ("s2r", R), ("lp", 4), ("s3h", 4), ("s3r", R), ("cwh", 4), ("cwr", R), ("cwg", 4),
        ("pair", 1), ("hop", 4), ("zr", Z), ("zg", Z), ("ddm", 1), ("d", 4), ("p", 4), ("q", 4),
        ("qr", R), ("pp", 4), ("pz", Z), ("pd", 1),
    ):
        names[name] = a(count)
    return names, a.n


def chunk(base, i, rows, pieces, cols):
    if rows // pieces >= 16:
        take = rows // pieces
        return pl.ds(pl.multiple_of(base + i * take, 16), take), pl.ds(0, cols)
    m = 16 * pieces // rows
    wide = cols // m
    return (
        pl.ds(pl.multiple_of(base + (i // m) * 16, 16), 16),
        pl.ds(pl.multiple_of((i % m) * wide, 128), wide),
    )


def main_kernel(
    R,
    nodes,
    ft, wb, bgain, bbias, wm, gain2, bias2, wc, cb, lab, msk,
    o_lp, o_d, o_m, o_mix, o_gw, o_small, o_cw,
    fs, fx, wall, wl, aw, wmx, keep, mi, gp, mixed, dn2, dmx,
    gbuf, s1, ab, s2h, s2r, s3h, s3r, cwp, cwh, cwr, cwg, lps,
    wcs, cbs, acc0, acc1, accl, accw, cols,
    dmp, pr, hr, zr, fin, dsend, pT, ps, ph, phalf, prv, qs, qv, qr, pz, pfin,
    ss, rs,
):
    names, _ = sem_plan(R)
    Z = R // 2
    h = lax.axis_index("hop")
    r = lax.axis_index("rows")
    c = lax.rem(r, 2)
    zi = lax.div(r, 2)
    sib = r + 1 - 2 * c
    local = ft.shape[1]
    sub = local // HOPS
    hid = wm.shape[0]
    half = hid // 2
    big = min(2 * TILE, sub)
    UN = big // TILE
    NT = sub // big
    inv_n = 1.0 / nodes

    def peer(d):
        x = lax.rem(h + d, 2)
        y = lax.rem(lax.div(h, 2) + lax.div(d, 2), 2)
        return 2 * y + x

    def rc(src, dst, name, i, hh, rr):
        return pltpu.make_async_remote_copy(
            src_ref=src, dst_ref=dst, send_sem=ss.at[names[name] + i], recv_sem=rs.at[names[name] + i],
            device_id=(hh, rr), device_id_type=MESH,
        )

    def done(cp):
        cp.wait_send()
        cp.wait_recv()

    def lanes_at(i, n):
        return pl.ds(pl.multiple_of(i * n, n), n)

    barrier = pltpu.get_barrier_semaphore()

    def greet(hh, rr):
        pl.semaphore_signal(barrier, inc=1, device_id=(hh, rr), device_id_type=MESH)

    for d in range(1, HOPS):
        greet(peer(d), r)

    @functools.partial(each, 1, R)
    def _(e):
        greet(h, lax.rem(r + e, R))

    def rows_start(buf, name):
        @functools.partial(each, 1, R)
        def _(e):
            rc(buf.at[r], buf.at[r], name, e, h, lax.rem(r + e, R)).start()

    def rows_wait(buf, name):
        @functools.partial(each, 1, R)
        def _(e):
            src = lax.rem(r + R - e, R)
            done(rc(buf.at[src], buf.at[src], name, e, h, lax.rem(r + e, R)))

    def hops_start(buf, name):
        for d in range(1, HOPS):
            rc(buf.at[h], buf.at[h], name, d, peer(d), r).start()

    def hops_wait(buf, name):
        for d in range(1, HOPS):
            done(rc(buf.at[peer(d)], buf.at[peer(d)], name, d, peer(d), r))

    def total(buf, n):
        t = buf[0]
        for i in range(1, n):
            t = t + buf[i]
        return t

    wrow = pl.ds(hid, 128)
    for i in range(HOPS):
        lanes = pl.ds(i * sub, sub)
        fs[pl.ds(0, 96), lanes] = ft[pl.ds(0, 96), lanes]
        row = lax.broadcasted_iota(jnp.int32, (32, sub), 0)
        fs[pl.ds(96, 32), lanes] = jnp.where(row == ONES - 96, 1.0, 0.0).astype(BF16)
        fs[pl.ds(96, 4), lanes] = ft[pl.ds(96, 4), lanes]
    wall[0, pl.ds(hid + 96, 32), :] = jnp.zeros((32, hid), BF16)
    wall[0, pl.ds(hid, 100), :] = wb[...]
    wall[0, pl.ds(0, hid), :] = wm[...].astype(F32).T.astype(BF16)
    for d in range(1, HOPS):
        fx[d, pl.ds(FP, 128 - FP), :] = jnp.zeros((128 - FP, sub), BF16)
    fx[0] = fs[:, lanes_at(h, sub)]

    pl.semaphore_wait(barrier, HOPS - 1 + R - 1)

    S = min(Z, 2)
    part = (hid + 128) // (2 * S)
    zpar = lax.rem(zi, S)
    zmate = zi + (S - 1) - 2 * (S - 1) * zpar

    def part_rows(core, par):
        return pl.ds(pl.multiple_of((core * S + par) * part, 16), part)

    def feat_copy(d):
        return rc(fs.at[pl.ds(0, FP), lanes_at(peer(d), sub)], fx.at[d, pl.ds(0, FP), :], "feat", d, peer(d), r)

    def ws_copy(d):
        rows = part_rows(c, zpar)
        return rc(wall.at[0, rows, :], wall.at[d, rows, :], "ws", d, peer(d), r)

    def zf_copy(d, par):
        ref = wall.at[d, part_rows(c, par), :]
        return rc(ref, ref, "zf", d, h, 2 * zmate + c)

    def dd_copy(d, core):
        ref = wall.at[d, pl.ds(pl.multiple_of(core * S * part, 16), S * part), :]
        return rc(ref, ref, "dd", d, h, sib)

    for d in range(1, HOPS):
        ws_copy(d).start()
    for d in range(1, HOPS - 1):
        feat_copy(d).start()

    def gram(i, g):
        f = fs[:, lanes_at(i, sub)]
        return g + dot_nt(f, f)

    g = lax.fori_loop(0, HOPS, gram, jnp.zeros((128, 128), F32))
    wown = wall[0, wrow, :]
    wown32 = wown.astype(F32)
    g1, g2, g3 = split3(g)
    gw = dot(g1, wown) + dot(g2, wown) + dot(g3, wown)
    s1[r, :, pl.ds(0, hid)] = gw[ONES : ONES + 1, :]
    s1[r, :, pl.ds(hid, hid)] = jnp.sum(gw * wown32, axis=0, keepdims=True)
    rows_start(s1, "s1")
    gbuf[r] = g[:FP]

    for d in range(HOPS):
        late = peer(d) - 2
        col = jnp.maximum(late, 0)
        for b in range(sub // 128):
            m = jnp.where(late >= 0, msk[col, h * (sub // 128) + b], 1)
            keep[d, :, pl.ds(b * 128, 128)] = jnp.full((16, 128), 0.5 * m.astype(F32)).astype(BF16)
    wcs[...] = jnp.zeros(wcs.shape, F32)
    wcs[pl.ds(0, wc.shape[0]), :] = wc[...].astype(F32)
    cbs[...] = jnp.zeros(cbs.shape, F32)
    cbs[pl.ds(0, 1), pl.ds(0, cb.shape[1])] = cb[...]
    ncls = wc.shape[0]

    @pl.loop(0, sub // TILE)
    def _(t):
        mixed[:, lanes_at(t, TILE)] = jnp.zeros((hid, TILE), F32)

    mi[0, :, pl.ds(0, big)] = jnp.zeros((hid, big), BF16)

    if S > 1:
        for d in range(1, HOPS):
            done(ws_copy(d))
            zf_copy(d, zpar).start()

    rows_wait(s1, "s1")
    st = total(s1, R)
    mean = st[:, :hid] * inv_n
    var = st[:, hid:] * inv_n - mean * mean
    inv = lax.rsqrt(var + EPS)
    scale = inv * bgain[...]
    ab[0, :, pl.ds(0, hid)] = scale
    ab[0, :, pl.ds(hid, hid)] = bbias[...] - mean * scale

    def ab_copy(d):
        return rc(ab.at[0], ab.at[d], "ab", d, peer(d), r)

    for d in range(1, HOPS):
        ab_copy(d).start()

    def prepare(d):
        a = ab[d, :, pl.ds(0, hid)]
        b = ab[d, :, pl.ds(hid, hid)]
        ws = wall[d, wrow, :].astype(F32) * (a * KAPPA)
        aw[d] = ws[:FP].astype(BF16)
        row = lax.broadcasted_iota(jnp.int32, (128, hid), 0)
        wt = jnp.where(row == ONES, b * KAPPA, ws).T
        hi, lo = split2(wt)
        wl[d, :, pl.ds(0, 128)] = hi
        wl[d, :, pl.ds(128, 128)] = lo

    prepare(0)

    @pl.loop(0, HOPS * NT)
    def _(it):
        d = lax.div(it, NT)
        t = lax.rem(it, NT)

        @pl.when(jnp.logical_and(t == 0, d > 0))
        def _():
            done(feat_copy(d))
            dd_copy(d, c).wait_send()
            dd_copy(d, 1 - c).wait_recv()
            done(ab_copy(d))
            prepare(d)

        @pl.when(jnp.logical_and(t == NT - 1, d < HOPS - 1))
        def _():
            if S > 1:
                zf_copy(d + 1, zpar).wait_send()
                zf_copy(d + 1, 1 - zpar).wait_recv()
            else:
                done(ws_copy(d + 1))
            dd_copy(d + 1, c).start()

        @pl.when(it == min(1, NT - 1))
        def _():
            feat_copy(HOPS - 1).start()

        @pl.when(it == 2 * NT)
        def _():
            rows_start(gbuf, "gr")

        pit = jnp.maximum(it - 1, 0)
        pd = lax.div(pit, NT)
        pt = lax.rem(pit, NT)
        adds = []
        for u in range(UN):
            adds.append(dot(wall[pd, pl.ds(0, hid), :], mi[pd, :, lanes_at(pt * UN + u, TILE)]))
        for u in range(UN):
            n = lanes_at(t * UN + u, TILE)
            f = fx[d, :, n]
            z = dot(wl[d], jnp.concatenate([f, f], axis=0))
            k = keep[d, :, n]
            k = jnp.concatenate([k] * 4, axis=0)
            for i in range(0, hid, 64):
                g1, d1 = scaled_gelu_slope(z[i : i + 64].astype(BF16))
                g2, d2 = scaled_gelu_slope(g1 * k)
                mi[d, pl.ds(i, 64), n] = g2
                gp[d, pl.ds(i, 64), n] = d1 * d2 * k
        for u in range(UN):
            n = lanes_at(pt * UN + u, TILE)
            mixed[:, n] = mixed[:, n] + adds[u]

    acc0[...] = jnp.zeros(acc0.shape, F32)
    acc1[...] = jnp.zeros(acc1.shape, F32)
    for u in range(UN):
        n = pl.ds((NT - 1) * big + u * TILE, TILE)
        mixed[:, n] = mixed[:, n] + dot(wall[HOPS - 1, pl.ds(0, hid), :], mi[HOPS - 1, :, n])

    @pl.loop(0, sub // TILE)
    def _(t):
        x = mixed[:, lanes_at(t, TILE)]
        acc0[...] += fold(x)
        acc1[...] += fold(x * x)

    s2h[h, :, pl.ds(0, hid)] = row_of(acc0[...])
    s2h[h, :, pl.ds(hid, hid)] = row_of(acc1[...])
    hops_start(s2h, "s2h")
    for d in range(2):
        wmx[d] = wall[d, pl.ds(0, hid), :].astype(F32).T.astype(BF16)
    hops_wait(s2h, "s2h")
    s2r[r] = total(s2h, HOPS)
    rows_start(s2r, "s2r")
    for d in range(2, HOPS):
        wmx[d] = wall[d, pl.ds(0, hid), :].astype(F32).T.astype(BF16)
    wc48 = wcs[pl.ds(0, 48), :].astype(BF16)
    wcN = wcs[...].T.astype(BF16)
    crow = lax.broadcasted_iota(jnp.int32, (128, 128), 0)
    cbc = jnp.where(crow < ncls, jnp.broadcast_to(cbs[pl.ds(0, 1), :], (128, 128)).T, -1e30)[:48]
    rows_wait(s2r, "s2r")
    st2 = total(s2r, R)
    mean2 = st2[:, :hid] * inv_n
    inv2 = lax.rsqrt(st2[:, hid:] * inv_n - mean2 * mean2 + EPS * 4.0 * KAPPA * KAPPA)
    scale2 = inv2 * gain2[...]
    cols[0] = col_of(scale2)
    cols[1] = col_of(bias2[...] - mean2 * scale2)
    acc0[...] = jnp.zeros(acc0.shape, F32)
    acc1[...] = jnp.zeros(acc1.shape, F32)
    accl[...] = jnp.zeros(accl.shape, F32)
    accw[...] = jnp.zeros(accw.shape, F32)

    @pl.loop(0, NT)
    def _(t):
        hbs, slopes, dhs = [], [], []
        ns = [lanes_at(t * UN + u, TILE) for u in range(UN)]
        for n in ns:
            heads, sl = [], []
            for i in range(0, hid, 64):
                rows = pl.ds(i, 64)
                z2 = mixed[rows, n] * spread(cols[0, rows, :], TILE) + spread(cols[1, rows, :], TILE)
                gv, dg = gelu_slope(z2)
                heads.append(gv.astype(BF16))
                sl.append(dg)
            hbs.append(jnp.concatenate(heads, axis=0))
            slopes.append(sl)
        for u, n in enumerate(ns):
            lg = dot(wc48, hbs[u]) + spread(cbc, TILE)
            lg = lg - jnp.max(lg, axis=0, keepdims=True)
            ex = jnp.exp(lg)
            se = jnp.sum(ex, axis=0, keepdims=True)
            lp = lg - jnp.log(se)
            lps[:, n] = lp.astype(BF16)
            own = pl.ds(pl.multiple_of(h * sub + (t * UN + u) * TILE, TILE), TILE)
            hit = lax.broadcasted_iota(jnp.int32, (48, TILE), 0) == lab[:, own]
            accl[pl.ds(48, 48), :] += fold(jnp.where(hit, lp, 0.0))
            dl = ((ex / se - jnp.where(hit, 1.0, 0.0)) * inv_n).astype(BF16)
            accl[pl.ds(0, 48), :] += fold(dl.astype(F32))
            accw[...] += dot_nt(dl, hbs[u])
            dhs.append(dot(wcN, jnp.concatenate([dl, jnp.zeros((80, TILE), BF16)], axis=0)))
        for u, n in enumerate(ns):
            for j, i in enumerate(range(0, hid, 64)):
                rows = pl.ds(i, 64)
                dn = dhs[u][i : i + 64] * slopes[u][j]
                dn2[rows, n] = dn
                acc0[rows, :] += fold(dn * mixed[rows, n])
                acc1[rows, :] += fold(dn)

    s3h[h, :, pl.ds(0, hid)] = row_of(acc0[...])
    s3h[h, :, pl.ds(hid, hid)] = row_of(acc1[...])
    zpad = jnp.zeros((80, 128), F32)
    s3h[h, :, pl.ds(2 * hid, 128)] = row_of(jnp.concatenate([accl[pl.ds(0, 48), :], zpad], axis=0))
    s3h[h, :, pl.ds(2 * hid + 128, 128)] = row_of(jnp.concatenate([accl[pl.ds(48, 48), :], zpad], axis=0))
    hops_start(s3h, "s3h")

    o_own = lanes_at(h, sub)

    def lp_copy(d):
        return rc(lps, o_lp.at[:, o_own], "lp", d, peer(d), r)

    def cwh_copy(d):
        return rc(cwp.at[d], cwh.at[d], "cwh", d, peer(d), r)

    q = hid // HOPS
    for d in range(HOPS):
        cwp[d] = accw[:, lanes_at(peer(d), q)]
    hops_wait(s3h, "s3h")
    s3r[r] = total(s3h, HOPS)
    rows_start(s3r, "s3r")
    for d in range(1, HOPS):
        cwh_copy(d).start()
    for d in range(1, HOPS):
        lp_copy(d).start()
    rows_wait(s3r, "s3r")
    st3 = total(s3r, R)
    db2 = st3[:, hid : 2 * hid]
    dg2t = inv2 * (st3[:, :hid] - mean2 * db2)
    o_small[pl.ds(0, 1), :] = dg2t
    o_small[pl.ds(1, 1), :] = db2
    o_small[pl.ds(4, 1), pl.ds(0, 256)] = st3[:, 2 * hid : 2 * hid + 256]
    o_small[pl.ds(4, 1), pl.ds(256, hid - 256)] = jnp.zeros((1, hid - 256), F32)
    t2 = scale2 * inv2 * dg2t * inv_n
    cols[1] = col_of(-t2)
    cols[2] = col_of(t2 * mean2 - scale2 * db2 * inv_n)

    @pl.loop(0, sub // TILE)
    def _(t):
        n = lanes_at(t, TILE)
        for i in range(0, hid, 64):
            rows = pl.ds(i, 64)
            v = dn2[rows, n] * spread(cols[0, rows, :], TILE)
            v = v + mixed[rows, n] * spread(cols[1, rows, :], TILE) + spread(cols[2, rows, :], TILE)
            dmx[rows, n] = v.astype(BF16)

    @pl.loop(0, 2 * HOPS)
    def _(i):
        d = lax.div(i, 2)
        rows = lanes_at(lax.rem(i, 2), half)
        dmp[d, rows, :] = dot_nt(mi[d, rows, :], dmx[...]).astype(BF16)

    mine = lanes_at(c, half)
    theirs = lanes_at(1 - c, half)
    pair = rc(dmp.at[:, theirs, :], pr, "pair", 0, h, sib)
    pair.start()

    def hop_copy(d):
        return rc(dmp.at[d, mine, :], hr.at[d], "hop", d, peer(d), r)

    def zr_copy(e, which):
        rows, lanes = chunk(0, which, half, Z, hid)
        return rc(hr.at[0, rows, lanes], zr.at[e], "zr", e, h, lax.rem(zi + e, Z) * 2 + c)

    def zg_copy(e, which):
        rows, lanes = chunk(c * half, which, half, Z, hid)
        ref = fin.at[rows, lanes]
        return rc(ref, ref, "zg", e, h, lax.rem(zi + e, Z) * 2 + c)

    def ddm_copy(core):
        ref = fin.at[lanes_at(core, half), :]
        return rc(ref, ref, "ddm", 0, h, sib)

    def d_copy(d):
        return rc(dsend.at[d], o_d.at[h], "d", d, peer(d), r)

    def pp_copy(d):
        return rc(ps.at[d, :, theirs], ph.at[d], "pp", d, h, sib)

    def p_copy(d):
        return rc(phalf.at[d], prv.at[d], "p", d, peer(d), r)

    def q_copy(d):
        return rc(qs.at[d], qv.at[d], "q", d, peer(d), r)

    def p_half(d):
        done(pp_copy(d))
        phalf[d] = (ps[d, :, mine].astype(F32) + ph[d].astype(F32)).astype(BF16)

    @pl.loop(0, HOPS * NT)
    def _(it):
        dd = lax.div(it, NT)
        t = lax.rem(it, NT)
        d = lax.rem(dd + 1, HOPS)

        @pl.when(t == 0)
        def _():
            pT[...] = jnp.zeros(pT.shape, F32)

        @pl.when(it == 3 * NT + NT // 2)
        def _():
            p_half(3)
            p_copy(3).start()

        ns = [lanes_at(t * UN + u, TILE) for u in range(UN)]
        dcs = [dot(wmx[d], dmx[:, n]) for n in ns]
        for u, n in enumerate(ns):
            dn = jnp.concatenate(
                [dcs[u][i : i + 64].astype(BF16) * gp[d, pl.ds(i, 64), n] for i in range(0, hid, 64)], axis=0
            )
            pT[...] += dot_nt(dn, fx[d, :, n])
            dsend[d, :, n] = dot(aw[d], dn).astype(BF16)

        @pl.when(t == NT - 1)
        def _():
            pw = pT[...].T * KAPPA
            qs[d, :, pl.ds(0, hid)] = jnp.sum(pw * wall[d, wrow, :].astype(F32), axis=0, keepdims=True)
            qs[d, :, pl.ds(hid, hid)] = pw[ONES : ONES + 1, :]
            ps[d] = pw[:FP].astype(BF16)
            pp_copy(d).start()

            @pl.when(dd < HOPS - 1)
            def _():
                q_copy(d).start()
                d_copy(d).start()

        @pl.when(it == NT - 1)
        def _():
            done(pair)
            for j in range(HOPS):
                dmp[j, mine, :] = (dmp[j, mine, :].astype(F32) + pr[j].astype(F32)).astype(BF16)
            for j in range(1, HOPS):
                hop_copy(j).start()
            for j in range(1, HOPS):
                done(cwh_copy(j))
            cwr[r] = cwp[0] + (cwh[1] + cwh[2] + cwh[3])
            rows_start(cwr, "cwr")

        @pl.when(it == 2 * NT - 1)
        def _():
            p_half(1)
            p_copy(1).start()
            for j in range(1, HOPS):
                done(hop_copy(j))
            hsum = dmp[0, mine, :].astype(F32) + hr[1].astype(F32) + hr[2].astype(F32) + hr[3].astype(F32)
            hr[0] = hsum.astype(BF16)

            @functools.partial(each, 1, Z)
            def _(e):
                zr_copy(e, lax.rem(zi + e, Z)).start()

            rows_wait(cwr, "cwr")
            cwg[h] = total(cwr, R)
            hops_start(cwg, "cwg")

        @pl.when(it == 3 * NT - 1)
        def _():
            p_half(2)
            p_copy(2).start()

            @functools.partial(each, 1, Z)
            def _(e):
                done(zr_copy(e, lax.rem(zi + e, Z)))

            rows, lanes = chunk(0, zi, half, Z, hid)
            zt = hr[0, rows, lanes].astype(F32)
            for e in range(1, Z):
                zt = zt + zr[e].astype(F32)
            frows, flanes = chunk(c * half, zi, half, Z, hid)
            fin[frows, flanes] = zt.astype(BF16)

            @functools.partial(each, 1, Z)
            def _(e):
                zg_copy(e, zi).start()

            hops_wait(cwg, "cwg")
            for j in range(HOPS):
                o_cw[:, pl.ds(j * q, q)] = cwg[j]

    for d in range(1, HOPS):
        done(q_copy(d))
    qr[r] = qs[0] + (qv[1] + qv[2] + qv[3])
    rows_start(qr, "qr")
    own_d = pltpu.make_async_copy(dsend.at[0], o_d.at[h], ss.at[names["d"]])
    own_d.start()
    own_lp = pltpu.make_async_copy(lps, o_lp.at[:, o_own], ss.at[names["lp"]])
    own_lp.start()

    p_half(0)
    for d in range(1, HOPS):
        done(p_copy(d))
    psum = phalf[0].astype(F32) + (prv[1].astype(F32) + prv[2].astype(F32) + prv[3].astype(F32))
    pz[zi] = psum.astype(BF16)

    def pz_copy(e, which):
        return rc(pz.at[which], pz.at[which], "pz", e, h, lax.rem(zi + e, Z) * 2 + c)

    @functools.partial(each, 1, Z)
    def _(e):
        pz_copy(e, zi).start()

    @functools.partial(each, 1, Z)
    def _(e):
        zg_copy(e, zi).wait_send()
        zg_copy(e, lax.rem(zi + Z - e, Z)).wait_recv()

    ddm_copy(c).start()

    rows_wait(qr, "qr")
    qt = total(qr, R)
    db = qt[:, hid:]
    dgn = inv * (qt[:, :hid] - mean * db)
    o_small[pl.ds(2, 1), :] = dgn
    o_small[pl.ds(3, 1), :] = db
    c1 = scale * db * inv_n
    c2 = inv * scale * dgn * inv_n
    shift = c1 - mean * c2
    row = lax.broadcasted_iota(jnp.int32, (128, hid), 0)
    q1, q2 = split2(jnp.where(row == ONES, shift, wown32 * c2))
    o_m[...] = (dot_nt(wown, q1) + dot_nt(wown, q2))[:FP]
    rows_wait(gbuf, "gr")
    g1, g2, g3 = split3(total(gbuf, R))
    gq = dot(g1, q1) + dot(g2, q1) + dot(g3, q1) + dot(g1, q2) + dot(g2, q2)

    @functools.partial(each, 1, Z)
    def _(e):
        pz_copy(e, zi).wait_send()
        pz_copy(e, lax.rem(zi + Z - e, Z)).wait_recv()

    pt = pz[0].astype(F32)
    for j in range(1, Z):
        pt = pt + pz[j].astype(F32)
    pfin[c] = pt.astype(BF16)

    def pd_copy(core):
        return rc(pfin.at[core], pfin.at[core], "pd", 0, h, sib)

    pd_copy(c).start()
    ddm_copy(c).wait_send()
    ddm_copy(1 - c).wait_recv()
    o_mix[...] = fin[...]
    pd_copy(c).wait_send()
    pd_copy(1 - c).wait_recv()
    ptot = jnp.concatenate([pfin[0], pfin[1]], axis=1).astype(F32)
    o_gw[...] = ptot * scale - gq
    own_d.wait()
    own_lp.wait()
    for d in range(1, HOPS):
        done(d_copy(d))
        done(lp_copy(d))


def last_kernel(
    nodes,
    ft, d, lp, m, mix, gw, small, cw,
    o_lp, o_gf, o_mix, o_gw, o_gg, o_gb, o_hg, o_hb, o_cw, o_cb, o_loss,
):
    feat, n = ft.shape
    ncls = o_lp.shape[0]
    o_lp[...] = lp[...].astype(F32)[:ncls]
    mm = m[...]
    f = ft[...]
    gf = d[0].astype(F32)[:feat] - dot(mm[:feat, :feat].astype(BF16), f) - mm[:feat, ONES : ONES + 1]
    for i in range(n // 128):
        o_gf[:, i, :] = gf[:, i * 128 : (i + 1) * 128]

    @pl.when(pl.program_id(0) == 0)
    def _():
        hid = mix.shape[1]
        o_mix[...] = mix[...].astype(F32)
        for i in range(hid // 128):
            o_gw[:, i, :] = gw[pl.ds(0, feat), pl.ds(i * 128, 128)]
        o_hg[...] = small[pl.ds(0, 1), :]
        o_hb[...] = small[pl.ds(1, 1), :]
        o_gg[...] = small[pl.ds(2, 1), :]
        o_gb[...] = small[pl.ds(3, 1), :]
        o_cw[...] = cw[pl.ds(0, ncls), :]
        o_cb[...] = small[pl.ds(4, 1), pl.ds(0, ncls)]
        o_loss[...] = jnp.sum(small[pl.ds(4, 1), pl.ds(128, 128)], axis=1, keepdims=True) * (-1.0 / nodes)


def shards(
    R, features, branch_weight, branch_gain, branch_bias, mix_weight, mixing_norm_gain, mixing_norm_bias,
    class_weight, class_bias, labels, hop_mask,
):
    local, feat = features.shape[1:]
    hid = mix_weight.shape[0]
    ncls = class_weight.shape[1]
    nodes = local * R
    sub = local // HOPS
    Z = R // 2
    half = hid // 2
    zrows, zcols = chunk(0, 0, half, Z, hid)
    assert feat == ONES and ncls == 47 and local // hop_mask.shape[0] == 128
    ft = features[0].T
    sd = jax.ShapeDtypeStruct
    vm = pl.BlockSpec(memory_space=pltpu.VMEM)
    hbm = pl.BlockSpec(memory_space=pl.ANY)
    _, nsem = sem_plan(R)
    V = pltpu.VMEM
    outs = pl.pallas_call(
        functools.partial(main_kernel, R, nodes),
        out_shape=(
            sd((48, local), BF16),
            sd((HOPS, FP, sub), BF16),
            sd((FP, 128), F32),
            sd((hid, hid), BF16),
            sd((FP, hid), F32),
            sd((8, hid), F32),
            sd((48, hid), F32),
        ),
        in_specs=[vm] * 10 + [pl.BlockSpec(memory_space=pltpu.SMEM)],
        out_specs=(hbm, hbm, vm, vm, vm, vm, vm),
        scratch_shapes=[
            V((128, local), BF16),
            V((HOPS, 128, sub), BF16),
            V((HOPS, hid + 128, hid), BF16),
            V((HOPS, hid, 256), BF16),
            V((HOPS, FP, hid), BF16),
            V((HOPS, hid, hid), BF16),
            V((HOPS, 16, sub), BF16),
            V((HOPS, hid, sub), BF16),
            V((HOPS, hid, sub), BF16),
            V((hid, sub), F32),
            V((hid, sub), F32),
            V((hid, sub), BF16),
            V((R, FP, 128), F32),
            V((R, 1, 2 * hid), F32),
            V((HOPS, 1, 2 * hid), F32),
            V((HOPS, 1, 2 * hid), F32),
            V((R, 1, 2 * hid), F32),
            V((HOPS, 1, 2 * hid + 256), F32),
            V((R, 1, 2 * hid + 256), F32),
            V((HOPS, 48, hid // HOPS), F32),
            V((HOPS, 48, hid // HOPS), F32),
            V((R, 48, hid // HOPS), F32),
            V((HOPS, 48, hid // HOPS), F32),
            V((48, sub), BF16),
            V((128, hid), F32),
            V((8, 128), F32),
            V((hid, 128), F32),
            V((hid, 128), F32),
            V((96, 128), F32),
            V((48, hid), F32),
            V((3, hid, 128), F32),
            V((HOPS, hid, hid), BF16),
            V((HOPS, half, hid), BF16),
            V((HOPS, half, hid), BF16),
            V((max(Z, 2), zrows.size, zcols.size), BF16),
            V((hid, hid), BF16),
            V((HOPS, FP, sub), BF16),
            V((hid, 128), F32),
            V((HOPS, FP, hid), BF16),
            V((HOPS, FP, half), BF16),
            V((HOPS, FP, half), BF16),
            V((HOPS, FP, half), BF16),
            V((HOPS, 1, 2 * hid), F32),
            V((HOPS, 1, 2 * hid), F32),
            V((R, 1, 2 * hid), F32),
            V((Z, FP, half), BF16),
            V((2, FP, half), BF16),
            pltpu.SemaphoreType.DMA((nsem,)),
            pltpu.SemaphoreType.DMA((nsem,)),
        ],
        compiler_params=pltpu.CompilerParams(
            collective_id=0, has_side_effects=True, vmem_limit_bytes=63 * 1024 * 1024
        ),
        cost_estimate=pl.CostEstimate(flops=2 * 8 * 10**9, bytes_accessed=10**7, transcendentals=10**7),
        name="main",
    )(
        ft, branch_weight[0], branch_gain, branch_bias, mix_weight, mixing_norm_gain[None], mixing_norm_bias[None],
        class_weight.T, class_bias[None], labels[None], hop_mask.T,
    )
    lp, dd, m, mix, gw, small, cw = outs
    nb = sub
    per = sub // nb
    whole = lambda shape: pl.BlockSpec(shape, lambda i: (0,) * len(shape))
    lp, gf, mix, gw, gg, gb, hg, hb, cw, cb, loss = pl.pallas_call(
        functools.partial(last_kernel, nodes),
        grid=(local // nb,),
        out_shape=(
            sd((ncls, local), F32),
            sd((feat, local // 128, 128), F32),
            sd((hid, hid), F32),
            sd((feat, hid // 128, 128), F32),
            sd((1, hid), F32),
            sd((1, hid), F32),
            sd((1, hid), F32),
            sd((1, hid), F32),
            sd((ncls, hid), F32),
            sd((1, ncls), F32),
            sd((1, 1), F32),
        ),
        in_specs=[
            pl.BlockSpec((feat, nb), lambda i: (0, i)),
            pl.BlockSpec((1, FP, nb), lambda i: (i // per, 0, i % per)),
            pl.BlockSpec((48, nb), lambda i: (0, i)),
            whole((FP, 128)),
            whole((hid, hid)),
            whole((FP, hid)),
            whole((8, hid)),
            whole((48, hid)),
        ],
        out_specs=(
            pl.BlockSpec((ncls, nb), lambda i: (0, i)),
            pl.BlockSpec((feat, nb // 128, 128), lambda i: (0, i, 0)),
            whole((hid, hid)),
            whole((feat, hid // 128, 128)),
            whole((1, hid)),
            whole((1, hid)),
            whole((1, hid)),
            whole((1, hid)),
            whole((ncls, hid)),
            whole((1, ncls)),
            whole((1, 1)),
        ),
        compiler_params=pltpu.CompilerParams(vmem_limit_bytes=60 * 1024 * 1024),
        name="last",
    )(ft, dd, lp, m, mix, gw, small, cw)
    return (
        lp.T,
        loss[0, 0],
        with_layout_constraint(gf.reshape(feat, 1, local), Layout((0, 1, 2))).transpose(1, 2, 0),
        gw.reshape(1, feat, hid),
        gg,
        gb,
        mix,
        hg[0],
        hb[0],
        cw.T,
        cb[0],
    )


def solution(mesh):
    placed = (
        P("hop", "rows", None), P("hop", None, None), P("hop", None), P("hop", None), P("hop", None),
        P(), P(), P(), P(), P("rows"), P("rows", None),
    )
    assert mesh.shape["hop"] == HOPS
    return jax.shard_map(
        functools.partial(shards, mesh.shape["rows"]),
        mesh=mesh,
        in_specs=placed,
        out_specs=(
            P("rows", None), P(), P("hop", "rows", None), P("hop", None, None), P("hop", None), P("hop", None),
            P("hop", None), P(), P(), P(), P(),
        ),
        check_vma=False,
    )
```

```python
import functools
import math

import jax
import jax.numpy as jnp
from jax import lax
from jax.experimental import pallas as pl
from jax.experimental.layout import Layout, with_layout_constraint
from jax.experimental.pallas import tpu as pltpu
from jax.sharding import PartitionSpec as P

MESH = pl.DeviceIdType.MESH
EPS = 1e-05
HOPS = 4
ONES = 100
FP = 112
TILE = 256
STRIDED = True
C0 = math.sqrt(2.0 / math.pi)
C1 = C0 * 0.044715
KAPPA = C1 ** (1.0 / 3.0)
ALPHA = C0 / KAPPA
F32 = jnp.float32
BF16 = jnp.bfloat16


def dot(a, b):
    return lax.dot_general(a, b, (((1,), (0,)), ((), ())), preferred_element_type=F32)


def dot_nt(a, b):
    return lax.dot_general(a, b, (((1,), (1,)), ((), ())), preferred_element_type=F32)


def split2(x):
    hi = x.astype(BF16)
    return hi, (x - hi.astype(F32)).astype(BF16)


def split3(x):
    hi = x.astype(BF16)
    rest = x - hi.astype(F32)
    mid = rest.astype(BF16)
    return hi, mid, (rest - mid.astype(F32)).astype(BF16)


def gelu_slope(z):
    u = z * z
    t = jnp.tanh(z * (C0 + C1 * u))
    s = 0.5 * t + 0.5
    g = z * s
    return g, s + (g - g * s) * (2.0 * C0 + 6.0 * C1 * u)


def scaled_gelu_slope(y):
    u = y * y
    t = jnp.tanh(y * (u + ALPHA))
    up = t + 1.0
    g = y * up
    return g, up + (g * (1.0 - t)) * (3.0 * u + ALPHA)


def fold(x):
    total = x[:, :128]
    for i in range(1, x.shape[1] // 128):
        total = total + x[:, i * 128 : (i + 1) * 128]
    return total


def spread(c, n):
    return jnp.concatenate([c] * (n // 128), axis=1)


def row_of(acc):
    return jnp.sum(acc.T, axis=0, keepdims=True)


def col_of(row):
    return jnp.broadcast_to(row, (128, row.shape[1])).T


def each(lo, hi, body):
    if hi - lo <= 16:
        for i in range(lo, hi):
            body(i)
    else:
        pl.loop(lo, hi)(body)


class Alloc:
    def __init__(self):
        self.n = 0

    def __call__(self, count):
        base = self.n
        self.n += count
        return base


def sem_plan(R):
    Z = R // 2
    a = Alloc()
    names = {}
    for name, count in (
        ("feat", 4), ("ws", 4), ("zf", 4), ("dd", 4), ("s1", R), ("ab", 4), ("gr", R),
        ("s2h", 4), ("s2r", R), ("lp", 8), ("s3h", 4), ("s3r", R), ("cwh", 4), ("cwr", R), ("cwg", 4),
        ("pair", 4), ("hop", 4), ("zr", Z), ("zg", Z), ("ddm", 1), ("d", 4), ("p", 4), ("q", 4),
        ("qr", R), ("pp", 4), ("pz", Z), ("pd", 1),
    ):
        names[name] = a(count)
    return names, a.n


def chunk(base, i, rows, pieces, cols):
    if rows // pieces >= 16:
        take = rows // pieces
        return pl.ds(pl.multiple_of(base + i * take, 16), take), pl.ds(0, cols)
    m = 16 * pieces // rows
    wide = cols // m
    return (
        pl.ds(pl.multiple_of(base + (i // m) * 16, 16), 16),
        pl.ds(pl.multiple_of((i % m) * wide, 128), wide),
    )


def main_kernel(
    R,
    nodes,
    ft, wb, bgain, bbias, wm, gain2, bias2, wc, cb, lab, msk,
    o_lp, o_d, o_m, o_mix, o_gw, o_small, o_cw,
    fs, fx, wall, wl, aw, wmx, keep, mi, gp, mixed, dn2, dmx,
    gbuf, s1, ab, s2h, s2r, s3h, s3r, cwp, cwh, cwr, cwg, lps,
    wcs, cbs, acc0, acc1, accl, accw, cols,
    dmp, pr, hr, zr, fin, dsend, pT, ps, ph, phalf, prv, qs, qv, qr, pz, pfin,
    ss, rs,
):
    names, _ = sem_plan(R)
    Z = R // 2
    h = lax.axis_index("hop")
    r = lax.axis_index("rows")
    c = lax.rem(r, 2)
    zi = lax.div(r, 2)
    sib = r + 1 - 2 * c
    local = ft.shape[1]
    sub = local // HOPS
    hid = wm.shape[0]
    half = hid // 2
    big = min(2 * TILE, sub)
    UN = big // TILE
    NT = sub // big
    inv_n = 1.0 / nodes

    def peer(d):
        x = lax.rem(h + d, 2)
        y = lax.rem(lax.div(h, 2) + lax.div(d, 2), 2)
        return 2 * y + x

    def rc(src, dst, name, i, hh, rr):
        return pltpu.make_async_remote_copy(
            src_ref=src, dst_ref=dst, send_sem=ss.at[names[name] + i], recv_sem=rs.at[names[name] + i],
            device_id=(hh, rr), device_id_type=MESH,
        )

    def done(cp):
        cp.wait_send()
        cp.wait_recv()

    def lanes_at(i, n):
        return pl.ds(pl.multiple_of(i * n, n), n)

    barrier = pltpu.get_barrier_semaphore()

    def greet(hh, rr):
        pl.semaphore_signal(barrier, inc=1, device_id=(hh, rr), device_id_type=MESH)

    for d in range(1, HOPS):
        greet(peer(d), r)

    @functools.partial(each, 1, R)
    def _(e):
        greet(h, lax.rem(r + e, R))

    def rows_start(buf, name):
        @functools.partial(each, 1, R)
        def _(e):
            rc(buf.at[r], buf.at[r], name, e, h, lax.rem(r + e, R)).start()

    def rows_wait(buf, name):
        @functools.partial(each, 1, R)
        def _(e):
            src = lax.rem(r + R - e, R)
            done(rc(buf.at[src], buf.at[src], name, e, h, lax.rem(r + e, R)))

    def hops_start(buf, name):
        for d in range(1, HOPS):
            rc(buf.at[h], buf.at[h], name, d, peer(d), r).start()

    def hops_wait(buf, name):
        for d in range(1, HOPS):
            done(rc(buf.at[peer(d)], buf.at[peer(d)], name, d, peer(d), r))

    def total(buf, n):
        t = buf[0]
        for i in range(1, n):
            t = t + buf[i]
        return t

    wrow = pl.ds(hid, 128)
    for i in range(HOPS):
        lanes = pl.ds(i * sub, sub)
        fs[pl.ds(0, 96), lanes] = ft[pl.ds(0, 96), lanes]
        row = lax.broadcasted_iota(jnp.int32, (32, sub), 0)
        fs[pl.ds(96, 32), lanes] = jnp.where(row == ONES - 96, 1.0, 0.0).astype(BF16)
        fs[pl.ds(96, 4), lanes] = ft[pl.ds(96, 4), lanes]
    wall[0, pl.ds(hid + 96, 32), :] = jnp.zeros((32, hid), BF16)
    wall[0, pl.ds(hid, 100), :] = wb[...]
    wall[0, pl.ds(0, hid), :] = wm[...].astype(F32).T.astype(BF16)
    for d in range(1, HOPS):
        fx[d, pl.ds(FP, 128 - FP), :] = jnp.zeros((128 - FP, sub), BF16)
    fx[0] = fs[:, lanes_at(h, sub)]

    pl.semaphore_wait(barrier, HOPS - 1 + R - 1)

    S = min(Z, 2)
    part = (hid + 128) // (2 * S)
    zpar = lax.rem(zi, S)
    zmate = zi + (S - 1) - 2 * (S - 1) * zpar

    def part_rows(core, par):
        return pl.ds(pl.multiple_of((core * S + par) * part, 16), part)

    def feat_copy(d):
        return rc(fs.at[pl.ds(0, FP), lanes_at(peer(d), sub)], fx.at[d, pl.ds(0, FP), :], "feat", d, peer(d), r)

    def ws_copy(d):
        rows = part_rows(c, zpar)
        return rc(wall.at[0, rows, :], wall.at[d, rows, :], "ws", d, peer(d), r)

    def zf_copy(d, par):
        ref = wall.at[d, part_rows(c, par), :]
        return rc(ref, ref, "zf", d, h, 2 * zmate + c)

    def dd_copy(d, core):
        ref = wall.at[d, pl.ds(pl.multiple_of(core * S * part, 16), S * part), :]
        return rc(ref, ref, "dd", d, h, sib)

    for d in range(1, HOPS):
        ws_copy(d).start()

    def gram(i, g):
        f = fs[:, lanes_at(i, sub)]
        return g + dot_nt(f, f)

    g = lax.fori_loop(0, HOPS, gram, jnp.zeros((128, 128), F32))
    wown = wall[0, wrow, :]
    wown32 = wown.astype(F32)
    g1, g2, g3 = split3(g)
    gw = dot(g1, wown) + dot(g2, wown) + dot(g3, wown)
    s1[r, :, pl.ds(0, hid)] = gw[ONES : ONES + 1, :]
    s1[r, :, pl.ds(hid, hid)] = jnp.sum(gw * wown32, axis=0, keepdims=True)
    rows_start(s1, "s1")
    for d in range(1, HOPS - 1):
        feat_copy(d).start()
    gbuf[r] = g[:FP]

    for d in range(HOPS):
        late = peer(d) - 2
        col = jnp.maximum(late, 0)
        for b in range(sub // 128):
            m = jnp.where(late >= 0, msk[col, h * (sub // 128) + b], 1)
            keep[d, :, pl.ds(b * 128, 128)] = jnp.full((16, 128), 0.5 * m.astype(F32)).astype(BF16)
    wcs[...] = jnp.zeros(wcs.shape, F32)
    wcs[pl.ds(0, wc.shape[0]), :] = wc[...].astype(F32)
    cbs[...] = jnp.zeros(cbs.shape, F32)
    cbs[pl.ds(0, 1), pl.ds(0, cb.shape[1])] = cb[...]
    ncls = wc.shape[0]

    @pl.loop(0, sub // TILE)
    def _(t):
        mixed[:, lanes_at(t, TILE)] = jnp.zeros((hid, TILE), F32)

    mi[0, :, pl.ds(0, big)] = jnp.zeros((hid, big), BF16)

    rows_wait(s1, "s1")
    st = total(s1, R)
    mean = st[:, :hid] * inv_n
    var = st[:, hid:] * inv_n - mean * mean
    inv = lax.rsqrt(var + EPS)
    scale = inv * bgain[...]
    ab[0, :, pl.ds(0, hid)] = scale
    ab[0, :, pl.ds(hid, hid)] = bbias[...] - mean * scale

    def ab_copy(d):
        return rc(ab.at[0], ab.at[d], "ab", d, peer(d), r)

    for d in range(1, HOPS):
        ab_copy(d).start()

    def prepare(d):
        a = ab[d, :, pl.ds(0, hid)]
        b = ab[d, :, pl.ds(hid, hid)]
        ws = wall[d, wrow, :].astype(F32) * (a * KAPPA)
        aw[d] = ws[:FP].astype(BF16)
        row = lax.broadcasted_iota(jnp.int32, (128, hid), 0)
        wt = jnp.where(row == ONES, b * KAPPA, ws).T
        hi, lo = split2(wt)
        wl[d, :, pl.ds(0, 128)] = hi
        wl[d, :, pl.ds(128, 128)] = lo

    prepare(0)

    @pl.loop(0, HOPS * NT)
    def _(it):
        d = lax.div(it, NT)
        t = lax.rem(it, NT)

        @pl.when(jnp.logical_and(t == 0, d > 0))
        def _():
            done(feat_copy(d))
            dd_copy(d, c).wait_send()
            dd_copy(d, 1 - c).wait_recv()
            done(ab_copy(d))
            prepare(d)

        if S > 1:

            @pl.when(it == min(1, NT - 1))
            def _():
                for j in range(1, HOPS):
                    done(ws_copy(j))
                    zf_copy(j, zpar).start()

        @pl.when(it == min(2, NT - 1))
        def _():
            feat_copy(HOPS - 1).start()

        @pl.when(jnp.logical_and(t == NT - 1, d < HOPS - 1))
        def _():
            if S > 1:
                zf_copy(d + 1, zpar).wait_send()
                zf_copy(d + 1, 1 - zpar).wait_recv()
            else:
                done(ws_copy(d + 1))
            dd_copy(d + 1, c).start()

        @pl.when(it == 2 * NT)
        def _():
            rows_start(gbuf, "gr")

        pit = jnp.maximum(it - 1, 0)
        pd = lax.div(pit, NT)
        pt = lax.rem(pit, NT)
        adds = []
        for u in range(UN):
            adds.append(dot(wall[pd, pl.ds(0, hid), :], mi[pd, :, lanes_at(pt * UN + u, TILE)]))
        for u in range(UN):
            n = lanes_at(t * UN + u, TILE)
            f = fx[d, :, n]
            z = dot(wl[d], jnp.concatenate([f, f], axis=0))
            k = keep[d, :, n]
            k = jnp.concatenate([k] * 4, axis=0)
            for i in range(0, hid, 64):
                g1, d1 = scaled_gelu_slope(z[i : i + 64].astype(BF16))
                g2, d2 = scaled_gelu_slope(g1 * k)
                mi[d, pl.ds(i, 64), n] = g2
                gp[d, pl.ds(i, 64), n] = d1 * d2 * k
        for u in range(UN):
            n = lanes_at(pt * UN + u, TILE)
            mixed[:, n] = mixed[:, n] + adds[u]

    acc0[...] = jnp.zeros(acc0.shape, F32)
    acc1[...] = jnp.zeros(acc1.shape, F32)
    for u in range(UN):
        n = pl.ds((NT - 1) * big + u * TILE, TILE)
        mixed[:, n] = mixed[:, n] + dot(wall[HOPS - 1, pl.ds(0, hid), :], mi[HOPS - 1, :, n])

    @pl.loop(0, sub // TILE)
    def _(t):
        x = mixed[:, lanes_at(t, TILE)]
        acc0[...] += fold(x)
        acc1[...] += fold(x * x)

    s2h[h, :, pl.ds(0, hid)] = row_of(acc0[...])
    s2h[h, :, pl.ds(hid, hid)] = row_of(acc1[...])
    hops_start(s2h, "s2h")
    for d in range(2):
        wmx[d] = wall[d, pl.ds(0, hid), :].astype(F32).T.astype(BF16)
    hops_wait(s2h, "s2h")
    s2r[r] = total(s2h, HOPS)
    rows_start(s2r, "s2r")
    for d in range(2, HOPS):
        wmx[d] = wall[d, pl.ds(0, hid), :].astype(F32).T.astype(BF16)
    wc48 = wcs[pl.ds(0, 48), :].astype(BF16)
    wcN = wcs[...].T.astype(BF16)
    crow = lax.broadcasted_iota(jnp.int32, (128, 128), 0)
    cbc = jnp.where(crow < ncls, jnp.broadcast_to(cbs[pl.ds(0, 1), :], (128, 128)).T, -1e30)[:48]
    rows_wait(s2r, "s2r")
    st2 = total(s2r, R)
    mean2 = st2[:, :hid] * inv_n
    inv2 = lax.rsqrt(st2[:, hid:] * inv_n - mean2 * mean2 + EPS * 4.0 * KAPPA * KAPPA)
    scale2 = inv2 * gain2[...]
    cols[0] = col_of(scale2)
    cols[1] = col_of(bias2[...] - mean2 * scale2)
    acc0[...] = jnp.zeros(acc0.shape, F32)
    acc1[...] = jnp.zeros(acc1.shape, F32)
    accl[...] = jnp.zeros(accl.shape, F32)
    accw[...] = jnp.zeros(accw.shape, F32)

    o_own = lanes_at(h, sub)

    def lp_copy(d, part):
        n = sub // 2
        return rc(
            lps.at[:, pl.ds(part * n, n)], o_lp.at[:, lanes_at(2 * h + part, n)], "lp", 4 * part + d, peer(d), r
        )

    @pl.loop(0, NT)
    def _(t):
        if NT > 1:

            @pl.when(t == NT // 2)
            def _():
                for d in range(1, HOPS):
                    lp_copy(d, 0).start()

        hbs, slopes, dhs = [], [], []
        ns = [lanes_at(t * UN + u, TILE) for u in range(UN)]
        for n in ns:
            heads, sl = [], []
            for i in range(0, hid, 64):
                rows = pl.ds(i, 64)
                z2 = mixed[rows, n] * spread(cols[0, rows, :], TILE) + spread(cols[1, rows, :], TILE)
                gv, dg = gelu_slope(z2)
                heads.append(gv.astype(BF16))
                sl.append(dg)
            hbs.append(jnp.concatenate(heads, axis=0))
            slopes.append(sl)
        for u, n in enumerate(ns):
            lg = dot(wc48, hbs[u]) + spread(cbc, TILE)
            lg = lg - jnp.max(lg, axis=0, keepdims=True)
            ex = jnp.exp(lg)
            se = jnp.sum(ex, axis=0, keepdims=True)
            lp = lg - jnp.log(se)
            lps[:, n] = lp.astype(BF16)
            own = pl.ds(pl.multiple_of(h * sub + (t * UN + u) * TILE, TILE), TILE)
            hit = lax.broadcasted_iota(jnp.int32, (48, TILE), 0) == lab[:, own]
            accl[pl.ds(48, 48), :] += fold(jnp.where(hit, lp, 0.0))
            dl = ((ex / se - jnp.where(hit, 1.0, 0.0)) * inv_n).astype(BF16)
            accl[pl.ds(0, 48), :] += fold(dl.astype(F32))
            accw[...] += dot_nt(dl, hbs[u])
            dhs.append(dot(wcN, jnp.concatenate([dl, jnp.zeros((80, TILE), BF16)], axis=0)))
        for u, n in enumerate(ns):
            for j, i in enumerate(range(0, hid, 64)):
                rows = pl.ds(i, 64)
                dn = dhs[u][i : i + 64] * slopes[u][j]
                dn2[rows, n] = dn
                acc0[rows, :] += fold(dn * mixed[rows, n])
                acc1[rows, :] += fold(dn)

    for d in range(1, HOPS):
        if NT == 1:
            lp_copy(d, 0).start()
        lp_copy(d, 1).start()
    own_lp = pltpu.make_async_copy(lps, o_lp.at[:, o_own], ss.at[names["lp"]])
    own_lp.start()
    s3h[h, :, pl.ds(0, hid)] = row_of(acc0[...])
    s3h[h, :, pl.ds(hid, hid)] = row_of(acc1[...])
    zpad = jnp.zeros((80, 128), F32)
    s3h[h, :, pl.ds(2 * hid, 128)] = row_of(jnp.concatenate([accl[pl.ds(0, 48), :], zpad], axis=0))
    s3h[h, :, pl.ds(2 * hid + 128, 128)] = row_of(jnp.concatenate([accl[pl.ds(48, 48), :], zpad], axis=0))
    hops_start(s3h, "s3h")

    def cwh_copy(d):
        return rc(cwp.at[d], cwh.at[d], "cwh", d, peer(d), r)

    q = hid // HOPS
    for d in range(HOPS):
        cwp[d] = accw[:, lanes_at(peer(d), q)]
    hops_wait(s3h, "s3h")
    s3r[r] = total(s3h, HOPS)
    rows_start(s3r, "s3r")
    for d in range(1, HOPS):
        cwh_copy(d).start()
    rows_wait(s3r, "s3r")
    st3 = total(s3r, R)
    db2 = st3[:, hid : 2 * hid]
    dg2t = inv2 * (st3[:, :hid] - mean2 * db2)
    o_small[pl.ds(0, 1), :] = dg2t
    o_small[pl.ds(1, 1), :] = db2
    o_small[pl.ds(4, 1), pl.ds(0, 256)] = st3[:, 2 * hid : 2 * hid + 256]
    o_small[pl.ds(4, 1), pl.ds(256, hid - 256)] = jnp.zeros((1, hid - 256), F32)
    t2 = scale2 * inv2 * dg2t * inv_n
    cols[1] = col_of(-t2)
    cols[2] = col_of(t2 * mean2 - scale2 * db2 * inv_n)

    @pl.loop(0, sub // TILE)
    def _(t):
        n = lanes_at(t, TILE)
        for i in range(0, hid, 64):
            rows = pl.ds(i, 64)
            v = dn2[rows, n] * spread(cols[0, rows, :], TILE)
            v = v + mixed[rows, n] * spread(cols[1, rows, :], TILE) + spread(cols[2, rows, :], TILE)
            dmx[rows, n] = v.astype(BF16)

    mine = lanes_at(c, half)
    theirs = lanes_at(1 - c, half)

    def pair_copy(d):
        return rc(dmp.at[d, theirs, :], pr.at[d], "pair", d, h, sib)

    def hop_copy(d):
        return rc(dmp.at[d, mine, :], hr.at[d], "hop", d, peer(d), r)

    def pair_sum(d):
        done(pair_copy(d))
        dmp[d, mine, :] = (dmp[d, mine, :].astype(F32) + pr[d].astype(F32)).astype(BF16)

    @pl.loop(0, HOPS)
    def _(i):
        d = HOPS - 1 - i

        @pl.loop(0, 2)
        def _(j):
            rows = lanes_at(j, half)
            dmp[d, rows, :] = dot_nt(mi[d, rows, :], dmx[...]).astype(BF16)

        pair_copy(d).start()

        @pl.when(i > 0)
        def _():
            pair_sum(d + 1)
            hop_copy(d + 1).start()

    def zr_copy(e, which):
        rows, lanes = chunk(0, which, half, Z, hid)
        return rc(hr.at[0, rows, lanes], zr.at[e], "zr", e, h, lax.rem(zi + e, Z) * 2 + c)

    def zg_copy(e, which):
        rows, lanes = chunk(c * half, which, half, Z, hid)
        ref = fin.at[rows, lanes]
        return rc(ref, ref, "zg", e, h, lax.rem(zi + e, Z) * 2 + c)

    def ddm_copy(core):
        ref = fin.at[lanes_at(core, half), :]
        return rc(ref, ref, "ddm", 0, h, sib)

    def d_copy(d):
        return rc(dsend.at[d], o_d.at[h], "d", d, peer(d), r)

    def pp_copy(d):
        return rc(ps.at[d, :, theirs], ph.at[d], "pp", d, h, sib)

    def p_copy(d):
        return rc(phalf.at[d], prv.at[d], "p", d, peer(d), r)

    def q_copy(d):
        return rc(qs.at[d], qv.at[d], "q", d, peer(d), r)

    def p_half(d):
        done(pp_copy(d))
        phalf[d] = (ps[d, :, mine].astype(F32) + ph[d].astype(F32)).astype(BF16)

    @pl.loop(0, HOPS * NT)
    def _(it):
        dd = lax.div(it, NT)
        t = lax.rem(it, NT)
        d = HOPS - 1 - dd

        @pl.when(t == 0)
        def _():
            pT[...] = jnp.zeros(pT.shape, F32)

        @pl.when(jnp.logical_and(t == NT // 2, dd > 0))
        def _():
            p_half(d + 1)
            p_copy(d + 1).start()

        @pl.when(it == NT // 2)
        def _():
            pair_sum(0)

        @pl.when(it == NT + NT // 2)
        def _():
            for j in range(1, HOPS):
                done(cwh_copy(j))
            cwr[r] = cwp[0] + (cwh[1] + cwh[2] + cwh[3])
            rows_start(cwr, "cwr")

        @pl.when(it == 2 * NT + NT // 2)
        def _():
            for j in range(1, HOPS):
                done(hop_copy(j))
            hsum = dmp[0, mine, :].astype(F32) + hr[1].astype(F32) + hr[2].astype(F32) + hr[3].astype(F32)
            hr[0] = hsum.astype(BF16)

            @functools.partial(each, 1, Z)
            def _(e):
                zr_copy(e, lax.rem(zi + e, Z)).start()

            rows_wait(cwr, "cwr")
            cwg[h] = total(cwr, R)
            hops_start(cwg, "cwg")

        @pl.when(it == 3 * NT + NT // 2)
        def _():
            @functools.partial(each, 1, Z)
            def _(e):
                done(zr_copy(e, lax.rem(zi + e, Z)))

            rows, lanes = chunk(0, zi, half, Z, hid)
            zt = hr[0, rows, lanes].astype(F32)
            for e in range(1, Z):
                zt = zt + zr[e].astype(F32)
            frows, flanes = chunk(c * half, zi, half, Z, hid)
            fin[frows, flanes] = zt.astype(BF16)

            @functools.partial(each, 1, Z)
            def _(e):
                zg_copy(e, zi).start()

            hops_wait(cwg, "cwg")
            for j in range(HOPS):
                o_cw[:, pl.ds(j * q, q)] = cwg[j]

        ns = [lanes_at(t * UN + u, TILE) for u in range(UN)]
        dcs = [dot(wmx[d], dmx[:, n]) for n in ns]
        for u, n in enumerate(ns):
            dn = jnp.concatenate(
                [dcs[u][i : i + 64].astype(BF16) * gp[d, pl.ds(i, 64), n] for i in range(0, hid, 64)], axis=0
            )
            pT[...] += dot_nt(dn, fx[d, :, n])
            dsend[d, :, n] = dot(aw[d], dn).astype(BF16)

        @pl.when(t == NT - 1)
        def _():
            pw = pT[...].T * KAPPA
            qs[d, :, pl.ds(0, hid)] = jnp.sum(pw * wall[d, wrow, :].astype(F32), axis=0, keepdims=True)
            qs[d, :, pl.ds(hid, hid)] = pw[ONES : ONES + 1, :]
            ps[d] = pw[:FP].astype(BF16)
            pp_copy(d).start()

            @pl.when(dd < HOPS - 1)
            def _():
                q_copy(d).start()
                d_copy(d).start()

    for d in range(1, HOPS):
        done(q_copy(d))
    qr[r] = qs[0] + (qv[1] + qv[2] + qv[3])
    rows_start(qr, "qr")
    own_d = pltpu.make_async_copy(dsend.at[0], o_d.at[h], ss.at[names["d"]])
    own_d.start()

    p_half(0)
    for d in range(1, HOPS):
        done(p_copy(d))
    psum = phalf[0].astype(F32) + (prv[1].astype(F32) + prv[2].astype(F32) + prv[3].astype(F32))
    pz[zi] = psum.astype(BF16)

    def pz_copy(e, which):
        return rc(pz.at[which], pz.at[which], "pz", e, h, lax.rem(zi + e, Z) * 2 + c)

    @functools.partial(each, 1, Z)
    def _(e):
        pz_copy(e, zi).start()

    @functools.partial(each, 1, Z)
    def _(e):
        zg_copy(e, zi).wait_send()
        zg_copy(e, lax.rem(zi + Z - e, Z)).wait_recv()

    ddm_copy(c).start()

    rows_wait(qr, "qr")
    qt = total(qr, R)
    db = qt[:, hid:]
    dgn = inv * (qt[:, :hid] - mean * db)
    o_small[pl.ds(2, 1), :] = dgn
    o_small[pl.ds(3, 1), :] = db
    c1 = scale * db * inv_n
    c2 = inv * scale * dgn * inv_n
    shift = c1 - mean * c2
    row = lax.broadcasted_iota(jnp.int32, (128, hid), 0)
    q1, q2 = split2(jnp.where(row == ONES, shift, wown32 * c2))
    o_m[...] = (dot_nt(wown, q1) + dot_nt(wown, q2))[:FP]
    rows_wait(gbuf, "gr")
    g1, g2, g3 = split3(total(gbuf, R))
    gq = dot(g1, q1) + dot(g2, q1) + dot(g3, q1) + dot(g1, q2) + dot(g2, q2)

    @functools.partial(each, 1, Z)
    def _(e):
        pz_copy(e, zi).wait_send()
        pz_copy(e, lax.rem(zi + Z - e, Z)).wait_recv()

    pt = pz[0].astype(F32)
    for j in range(1, Z):
        pt = pt + pz[j].astype(F32)
    pfin[c] = pt.astype(BF16)

    def pd_copy(core):
        return rc(pfin.at[core], pfin.at[core], "pd", 0, h, sib)

    pd_copy(c).start()
    ddm_copy(c).wait_send()
    ddm_copy(1 - c).wait_recv()
    o_mix[...] = fin[...]
    pd_copy(c).wait_send()
    pd_copy(1 - c).wait_recv()
    ptot = jnp.concatenate([pfin[0], pfin[1]], axis=1).astype(F32)
    o_gw[...] = ptot * scale - gq
    own_d.wait()
    own_lp.wait()
    for d in range(1, HOPS):
        done(d_copy(d))
        done(lp_copy(d, 0))
        done(lp_copy(d, 1))


def last_kernel(
    nodes,
    ft, d, lp, m, mix, gw, small, cw,
    o_lp, o_gf, o_mix, o_gw, o_gg, o_gb, o_hg, o_hb, o_cw, o_cb, o_loss,
):
    feat, n = ft.shape
    ncls = o_lp.shape[0]
    o_lp[...] = lp[...].astype(F32)[:ncls]
    mm = m[...]
    f = ft[...]
    gf = d[0].astype(F32)[:feat] - dot(mm[:feat, :feat].astype(BF16), f) - mm[:feat, ONES : ONES + 1]
    if STRIDED:
        flat = o_gf.reshape(feat * (n // 128), 128)
        for i in range(n // 128):
            flat[pl.ds(i, feat, stride=n // 128), :] = gf[:, i * 128 : (i + 1) * 128]
    else:
        for i in range(n // 128):
            o_gf[:, i, :] = gf[:, i * 128 : (i + 1) * 128]

    @pl.when(pl.program_id(0) == 0)
    def _():
        hid = mix.shape[1]
        o_mix[...] = mix[...].astype(F32)
        for i in range(hid // 128):
            o_gw[:, i, :] = gw[pl.ds(0, feat), pl.ds(i * 128, 128)]
        o_hg[...] = small[pl.ds(0, 1), :]
        o_hb[...] = small[pl.ds(1, 1), :]
        o_gg[...] = small[pl.ds(2, 1), :]
        o_gb[...] = small[pl.ds(3, 1), :]
        o_cw[...] = cw[pl.ds(0, ncls), :]
        o_cb[...] = small[pl.ds(4, 1), pl.ds(0, ncls)]
        o_loss[...] = jnp.sum(small[pl.ds(4, 1), pl.ds(128, 128)], axis=1, keepdims=True) * (-1.0 / nodes)


def shards(
    R, features, branch_weight, branch_gain, branch_bias, mix_weight, mixing_norm_gain, mixing_norm_bias,
    class_weight, class_bias, labels, hop_mask,
):
    local, feat = features.shape[1:]
    hid = mix_weight.shape[0]
    ncls = class_weight.shape[1]
    nodes = local * R
    sub = local // HOPS
    Z = R // 2
    half = hid // 2
    zrows, zcols = chunk(0, 0, half, Z, hid)
    assert feat == ONES and ncls == 47 and local // hop_mask.shape[0] == 128
    ft = features[0].T
    sd = jax.ShapeDtypeStruct
    vm = pl.BlockSpec(memory_space=pltpu.VMEM)
    hbm = pl.BlockSpec(memory_space=pl.ANY)
    _, nsem = sem_plan(R)
    V = pltpu.VMEM
    outs = pl.pallas_call(
        functools.partial(main_kernel, R, nodes),
        out_shape=(
            sd((48, local), BF16),
            sd((HOPS, FP, sub), BF16),
            sd((FP, 128), F32),
            sd((hid, hid), BF16),
            sd((FP, hid), F32),
            sd((8, hid), F32),
            sd((48, hid), F32),
        ),
        in_specs=[vm] * 10 + [pl.BlockSpec(memory_space=pltpu.SMEM)],
        out_specs=(hbm, hbm, vm, vm, vm, vm, vm),
        scratch_shapes=[
            V((128, local), BF16),
            V((HOPS, 128, sub), BF16),
            V((HOPS, hid + 128, hid), BF16),
            V((HOPS, hid, 256), BF16),
            V((HOPS, FP, hid), BF16),
            V((HOPS, hid, hid), BF16),
            V((HOPS, 16, sub), BF16),
            V((HOPS, hid, sub), BF16),
            V((HOPS, hid, sub), BF16),
            V((hid, sub), F32),
            V((hid, sub), F32),
            V((hid, sub), BF16),
            V((R, FP, 128), F32),
            V((R, 1, 2 * hid), F32),
            V((HOPS, 1, 2 * hid), F32),
            V((HOPS, 1, 2 * hid), F32),
            V((R, 1, 2 * hid), F32),
            V((HOPS, 1, 2 * hid + 256), F32),
            V((R, 1, 2 * hid + 256), F32),
            V((HOPS, 48, hid // HOPS), F32),
            V((HOPS, 48, hid // HOPS), F32),
            V((R, 48, hid // HOPS), F32),
            V((HOPS, 48, hid // HOPS), F32),
            V((48, sub), BF16),
            V((128, hid), F32),
            V((8, 128), F32),
            V((hid, 128), F32),
            V((hid, 128), F32),
            V((96, 128), F32),
            V((48, hid), F32),
            V((3, hid, 128), F32),
            V((HOPS, hid, hid), BF16),
            V((HOPS, half, hid), BF16),
            V((HOPS, half, hid), BF16),
            V((max(Z, 2), zrows.size, zcols.size), BF16),
            V((hid, hid), BF16),
            V((HOPS, FP, sub), BF16),
            V((hid, 128), F32),
            V((HOPS, FP, hid), BF16),
            V((HOPS, FP, half), BF16),
            V((HOPS, FP, half), BF16),
            V((HOPS, FP, half), BF16),
            V((HOPS, 1, 2 * hid), F32),
            V((HOPS, 1, 2 * hid), F32),
            V((R, 1, 2 * hid), F32),
            V((Z, FP, half), BF16),
            V((2, FP, half), BF16),
            pltpu.SemaphoreType.DMA((nsem,)),
            pltpu.SemaphoreType.DMA((nsem,)),
        ],
        compiler_params=pltpu.CompilerParams(
            collective_id=0, has_side_effects=True, vmem_limit_bytes=63 * 1024 * 1024
        ),
        cost_estimate=pl.CostEstimate(flops=2 * 8 * 10**9, bytes_accessed=10**7, transcendentals=10**7),
        name="main",
    )(
        ft, branch_weight[0], branch_gain, branch_bias, mix_weight, mixing_norm_gain[None], mixing_norm_bias[None],
        class_weight.T, class_bias[None], labels[None], hop_mask.T,
    )
    lp, dd, m, mix, gw, small, cw = outs
    nb = sub
    per = sub // nb
    whole = lambda shape: pl.BlockSpec(shape, lambda i: (0,) * len(shape))
    lp, gf, mix, gw, gg, gb, hg, hb, cw, cb, loss = pl.pallas_call(
        functools.partial(last_kernel, nodes),
        grid=(local // nb,),
        out_shape=(
            sd((ncls, local), F32),
            sd((feat, local // 128, 128), F32),
            sd((hid, hid), F32),
            sd((feat, hid // 128, 128), F32),
            sd((1, hid), F32),
            sd((1, hid), F32),
            sd((1, hid), F32),
            sd((1, hid), F32),
            sd((ncls, hid), F32),
            sd((1, ncls), F32),
            sd((1, 1), F32),
        ),
        in_specs=[
            pl.BlockSpec((feat, nb), lambda i: (0, i)),
            pl.BlockSpec((1, FP, nb), lambda i: (i // per, 0, i % per)),
            pl.BlockSpec((48, nb), lambda i: (0, i)),
            whole((FP, 128)),
            whole((hid, hid)),
            whole((FP, hid)),
            whole((8, hid)),
            whole((48, hid)),
        ],
        out_specs=(
            pl.BlockSpec((ncls, nb), lambda i: (0, i)),
            pl.BlockSpec((feat, nb // 128, 128), lambda i: (0, i, 0)),
            whole((hid, hid)),
            whole((feat, hid // 128, 128)),
            whole((1, hid)),
            whole((1, hid)),
            whole((1, hid)),
            whole((1, hid)),
            whole((ncls, hid)),
            whole((1, ncls)),
            whole((1, 1)),
        ),
        compiler_params=pltpu.CompilerParams(vmem_limit_bytes=60 * 1024 * 1024),
        name="last",
    )(ft, dd, lp, m, mix, gw, small, cw)
    return (
        lp.T,
        loss[0, 0],
        with_layout_constraint(gf.reshape(feat, 1, local), Layout((0, 1, 2))).transpose(1, 2, 0),
        gw.reshape(1, feat, hid),
        gg,
        gb,
        mix,
        hg[0],
        hb[0],
        cw.T,
        cb[0],
    )


def solution(mesh):
    placed = (
        P("hop", "rows", None), P("hop", None, None), P("hop", None), P("hop", None), P("hop", None),
        P(), P(), P(), P(), P("rows"), P("rows", None),
    )
    assert mesh.shape["hop"] == HOPS
    return jax.shard_map(
        functools.partial(shards, mesh.shape["rows"]),
        mesh=mesh,
        in_specs=placed,
        out_specs=(
            P("rows", None), P(), P("hop", "rows", None), P("hop", None, None), P("hop", None), P("hop", None),
            P("hop", None), P(), P(), P(), P(),
        ),
        check_vma=False,
    )
```

```python
import functools
import math

import jax
import jax.numpy as jnp
from jax import lax
from jax.experimental import pallas as pl
from jax.experimental.layout import Layout, with_layout_constraint
from jax.experimental.pallas import tpu as pltpu
from jax.sharding import PartitionSpec as P

MESH = pl.DeviceIdType.MESH
EPS = 1e-05
HOPS = 4
ONES = 100
FP = 112
MAIN = 96
TILE = 256
STRIDED = True
C0 = math.sqrt(2.0 / math.pi)
C1 = C0 * 0.044715
KAPPA = C1 ** (1.0 / 3.0)
ALPHA = C0 / KAPPA
F32 = jnp.float32
BF16 = jnp.bfloat16


def dot(a, b):
    return lax.dot_general(a, b, (((1,), (0,)), ((), ())), preferred_element_type=F32)


def dot_nt(a, b):
    return lax.dot_general(a, b, (((1,), (1,)), ((), ())), preferred_element_type=F32)


def split2(x):
    hi = x.astype(BF16)
    return hi, (x - hi.astype(F32)).astype(BF16)


def split3(x):
    hi = x.astype(BF16)
    rest = x - hi.astype(F32)
    mid = rest.astype(BF16)
    return hi, mid, (rest - mid.astype(F32)).astype(BF16)


def gelu_slope(z):
    u = z * z
    t = jnp.tanh(z * (C0 + C1 * u))
    s = 0.5 * t + 0.5
    g = z * s
    return g, s + (g - g * s) * (2.0 * C0 + 6.0 * C1 * u)


def scaled_gelu_slope(y):
    u = y * y
    t = jnp.tanh(y * (u + ALPHA))
    up = t + 1.0
    g = y * up
    return g, up + (g * (1.0 - t)) * (3.0 * u + ALPHA)


def fold(x):
    total = x[:, :128]
    for i in range(1, x.shape[1] // 128):
        total = total + x[:, i * 128 : (i + 1) * 128]
    return total


def spread(c, n):
    return jnp.concatenate([c] * (n // 128), axis=1)


def row_of(acc):
    return jnp.sum(acc.T, axis=0, keepdims=True)


def col_of(row):
    return jnp.broadcast_to(row, (128, row.shape[1])).T


def each(lo, hi, body):
    if hi - lo <= 16:
        for i in range(lo, hi):
            body(i)
    else:
        pl.loop(lo, hi)(body)


class Alloc:
    def __init__(self):
        self.n = 0

    def __call__(self, count):
        base = self.n
        self.n += count
        return base


def sem_plan(R):
    Z = R // 2
    a = Alloc()
    names = {}
    for name, count in (
        ("feat", 4), ("ft", 4), ("loc", 1), ("ws", 4), ("zf", 4), ("dd", 4), ("s1", R), ("ab", 4), ("gr", R),
        ("s2h", 4), ("s2r", R), ("lp", 8), ("s3h", 4), ("s3r", R), ("cwh", 4), ("cwr", R), ("cwg", 4),
        ("pair", 4), ("z1", 4), ("hop", 4), ("zr", Z), ("zg", Z), ("ddm", 1), ("d", 4), ("dt", 4), ("p", 4), ("q", 4),
        ("qr", R), ("pp", 4), ("pz", Z), ("pd", 1),
    ):
        names[name] = a(count)
    return names, a.n


def chunk(base, i, rows, pieces, cols):
    if rows // pieces >= 16:
        take = rows // pieces
        return pl.ds(pl.multiple_of(base + i * take, 16), take), pl.ds(0, cols)
    m = 16 * pieces // rows
    wide = cols // m
    return (
        pl.ds(pl.multiple_of(base + (i // m) * 16, 16), 16),
        pl.ds(pl.multiple_of((i % m) * wide, 128), wide),
    )


def main_kernel(
    R,
    nodes,
    ft, ft4, wb, bgain, bbias, wm, gain2, bias2, wc, cb, lab, msk,
    o_lp, o_d, o_dt, o_m, o_mix, o_gw, o_small, o_cw,
    fs, fx, ftail, frt, st4, wall, wl, aw, wmx, keep, mi, gp, mixed, dn2, dmx,
    gbuf, s1, ab, s2h, s2r, s3h, s3r, cwp, cwh, cwr, cwg, lps,
    wcs, cbs, acc0, acc1, accl, accw, cols,
    dmp, pr, z1r, hr, zr, fin, dsend, d4, dtail, pT, ps, ph, phalf, prv, qs, qv, qr, pz, pfin,
    ss, rs,
):
    names, _ = sem_plan(R)
    Z = R // 2
    h = lax.axis_index("hop")
    r = lax.axis_index("rows")
    c = lax.rem(r, 2)
    zi = lax.div(r, 2)
    sib = r + 1 - 2 * c
    local = ft.shape[1]
    sub = local // HOPS
    hid = wm.shape[0]
    half = hid // 2
    big = min(2 * TILE, sub)
    UN = big // TILE
    NT = sub // big
    inv_n = 1.0 / nodes

    def peer(d):
        x = lax.rem(h + d, 2)
        y = lax.rem(lax.div(h, 2) + lax.div(d, 2), 2)
        return 2 * y + x

    def rc(src, dst, name, i, hh, rr):
        return pltpu.make_async_remote_copy(
            src_ref=src, dst_ref=dst, send_sem=ss.at[names[name] + i], recv_sem=rs.at[names[name] + i],
            device_id=(hh, rr), device_id_type=MESH,
        )

    def done(cp):
        cp.wait_send()
        cp.wait_recv()

    def lanes_at(i, n):
        return pl.ds(pl.multiple_of(i * n, n), n)

    barrier = pltpu.get_barrier_semaphore()

    def greet(hh, rr):
        pl.semaphore_signal(barrier, inc=1, device_id=(hh, rr), device_id_type=MESH)

    for d in range(1, HOPS):
        greet(peer(d), r)

    @functools.partial(each, 1, R)
    def _(e):
        greet(h, lax.rem(r + e, R))

    def rows_start(buf, name):
        @functools.partial(each, 1, R)
        def _(e):
            rc(buf.at[r], buf.at[r], name, e, h, lax.rem(r + e, R)).start()

    def rows_wait(buf, name):
        @functools.partial(each, 1, R)
        def _(e):
            src = lax.rem(r + R - e, R)
            done(rc(buf.at[src], buf.at[src], name, e, h, lax.rem(r + e, R)))

    def hops_start(buf, name):
        for d in range(1, HOPS):
            rc(buf.at[h], buf.at[h], name, d, peer(d), r).start()

    def hops_wait(buf, name):
        for d in range(1, HOPS):
            done(rc(buf.at[peer(d)], buf.at[peer(d)], name, d, peer(d), r))

    def total(buf, n):
        t = buf[0]
        for i in range(1, n):
            t = t + buf[i]
        return t

    loc = pltpu.make_async_copy(ft.at[pl.ds(0, MAIN), :], fs.at[pl.ds(0, MAIN), :], ss.at[names["loc"]])
    loc.start()

    def pack4(src, dst):
        n = st4.shape[1]
        for b in range(4):
            st4[pl.ds(4 * b, 4), :] = src[pl.ds(0, 4), pl.ds(b * n, n)].astype(F32)
        dst[...] = st4[pl.ds(0, 16), :].astype(BF16)

    def unpack4(src, dst):
        n = st4.shape[1]
        row = lax.broadcasted_iota(jnp.int32, (32, n), 0)
        st4[pl.ds(0, 16), :] = src[...].astype(F32)
        st4[pl.ds(16, 32), :] = jnp.where(row == ONES - MAIN, 1.0, 0.0)
        for b in range(4):
            st4[pl.ds(16, 4), :] = st4[pl.ds(4 * b, 4), :]
            dst[pl.ds(MAIN, 32), pl.ds(b * n, n)] = st4[pl.ds(16, 32), :].astype(BF16)

    wrow = pl.ds(hid, 128)
    wall[0, pl.ds(hid + 96, 32), :] = jnp.zeros((32, hid), BF16)
    wall[0, pl.ds(hid, 100), :] = wb[...]
    wall[0, pl.ds(0, hid), :] = wm[...].astype(F32).T.astype(BF16)

    def feat_copy(d):
        rows = pl.ds(0, MAIN)
        return rc(ft.at[rows, lanes_at(peer(d), sub)], fx.at[d, rows, :], "feat", d, peer(d), r)

    def ft_copy(d):
        return rc(ftail.at[peer(d)], frt.at[d], "ft", d, peer(d), r)

    pl.semaphore_wait(barrier, HOPS - 1 + R - 1)

    S = min(Z, 2)
    part = (hid + 128) // (2 * S)
    zpar = lax.rem(zi, S)
    zmate = zi + (S - 1) - 2 * (S - 1) * zpar

    def part_rows(core, par):
        return pl.ds(pl.multiple_of((core * S + par) * part, 16), part)

    def ws_copy(d):
        rows = part_rows(c, zpar)
        return rc(wall.at[0, rows, :], wall.at[d, rows, :], "ws", d, peer(d), r)

    def zf_copy(d, par):
        ref = wall.at[d, part_rows(c, par), :]
        return rc(ref, ref, "zf", d, h, 2 * zmate + c)

    def dd_copy(d, core):
        ref = wall.at[d, pl.ds(pl.multiple_of(core * S * part, 16), S * part), :]
        return rc(ref, ref, "dd", d, h, sib)

    for d in range(1, HOPS):
        ws_copy(d).start()
    for d in range(1, HOPS - 1):
        feat_copy(d).start()
    for j in range(HOPS):
        lanes = pl.ds(j * sub, sub)
        pack4(ft4.at[:, lanes], ftail.at[j])
        unpack4(ftail.at[j], fs.at[:, lanes])
    for d in range(1, HOPS):
        ft_copy(d).start()
    loc.wait()
    fx[0] = fs[:, lanes_at(h, sub)]

    def gram(i, g):
        f = fs[:, lanes_at(i, sub)]
        return g + dot_nt(f, f)

    g = lax.fori_loop(0, HOPS, gram, jnp.zeros((128, 128), F32))
    wown = wall[0, wrow, :]
    wown32 = wown.astype(F32)
    g1, g2, g3 = split3(g)
    gw = dot(g1, wown) + dot(g2, wown) + dot(g3, wown)
    s1[r, :, pl.ds(0, hid)] = gw[ONES : ONES + 1, :]
    s1[r, :, pl.ds(hid, hid)] = jnp.sum(gw * wown32, axis=0, keepdims=True)
    rows_start(s1, "s1")
    gbuf[r] = g[:FP]

    for d in range(HOPS):
        late = peer(d) - 2
        col = jnp.maximum(late, 0)
        for b in range(sub // 128):
            m = jnp.where(late >= 0, msk[col, h * (sub // 128) + b], 1)
            keep[d, :, pl.ds(b * 128, 128)] = jnp.full((16, 128), 0.5 * m.astype(F32)).astype(BF16)
    wcs[...] = jnp.zeros(wcs.shape, F32)
    wcs[pl.ds(0, wc.shape[0]), :] = wc[...].astype(F32)
    cbs[...] = jnp.zeros(cbs.shape, F32)
    cbs[pl.ds(0, 1), pl.ds(0, cb.shape[1])] = cb[...]
    ncls = wc.shape[0]

    @pl.loop(0, sub // TILE)
    def _(t):
        mixed[:, lanes_at(t, TILE)] = jnp.zeros((hid, TILE), F32)

    mi[0, :, pl.ds(0, big)] = jnp.zeros((hid, big), BF16)

    rows_wait(s1, "s1")
    st = total(s1, R)
    mean = st[:, :hid] * inv_n
    var = st[:, hid:] * inv_n - mean * mean
    inv = lax.rsqrt(var + EPS)
    scale = inv * bgain[...]
    ab[0, :, pl.ds(0, hid)] = scale
    ab[0, :, pl.ds(hid, hid)] = bbias[...] - mean * scale

    def ab_copy(d):
        return rc(ab.at[0], ab.at[d], "ab", d, peer(d), r)

    for d in range(1, HOPS):
        ab_copy(d).start()

    def prepare(d):
        a = ab[d, :, pl.ds(0, hid)]
        b = ab[d, :, pl.ds(hid, hid)]
        ws = wall[d, wrow, :].astype(F32) * (a * KAPPA)
        aw[d] = ws[:FP].astype(BF16)
        row = lax.broadcasted_iota(jnp.int32, (128, hid), 0)
        wt = jnp.where(row == ONES, b * KAPPA, ws).T
        hi, lo = split2(wt)
        wl[d, :, pl.ds(0, 128)] = hi
        wl[d, :, pl.ds(128, 128)] = lo

    prepare(0)

    @pl.loop(0, HOPS * NT)
    def _(it):
        d = lax.div(it, NT)
        t = lax.rem(it, NT)

        @pl.when(jnp.logical_and(t == 0, d > 0))
        def _():
            done(feat_copy(d))
            done(ft_copy(d))
            unpack4(frt.at[d], fx.at[d])
            dd_copy(d, c).wait_send()
            dd_copy(d, 1 - c).wait_recv()
            done(ab_copy(d))
            prepare(d)

        if S > 1:

            @pl.when(it == min(1, NT - 1))
            def _():
                for j in range(1, HOPS):
                    done(ws_copy(j))
                    zf_copy(j, zpar).start()

        @pl.when(it == min(2, NT - 1))
        def _():
            feat_copy(HOPS - 1).start()

        @pl.when(jnp.logical_and(t == NT - 1, d < HOPS - 1))
        def _():
            if S > 1:
                zf_copy(d + 1, zpar).wait_send()
                zf_copy(d + 1, 1 - zpar).wait_recv()
            else:
                done(ws_copy(d + 1))
            dd_copy(d + 1, c).start()

        @pl.when(it == 2 * NT)
        def _():
            rows_start(gbuf, "gr")

        pit = jnp.maximum(it - 1, 0)
        pd = lax.div(pit, NT)
        pt = lax.rem(pit, NT)
        adds = []
        for u in range(UN):
            adds.append(dot(wall[pd, pl.ds(0, hid), :], mi[pd, :, lanes_at(pt * UN + u, TILE)]))
        for u in range(UN):
            n = lanes_at(t * UN + u, TILE)
            f = fx[d, :, n]
            z = dot(wl[d], jnp.concatenate([f, f], axis=0))
            k = keep[d, :, n]
            k = jnp.concatenate([k] * 4, axis=0)
            for i in range(0, hid, 64):
                g1, d1 = scaled_gelu_slope(z[i : i + 64].astype(BF16))
                g2, d2 = scaled_gelu_slope(g1 * k)
                mi[d, pl.ds(i, 64), n] = g2
                gp[d, pl.ds(i, 64), n] = d1 * d2 * k
        for u in range(UN):
            n = lanes_at(pt * UN + u, TILE)
            mixed[:, n] = mixed[:, n] + adds[u]

    acc0[...] = jnp.zeros(acc0.shape, F32)
    acc1[...] = jnp.zeros(acc1.shape, F32)
    for u in range(UN):
        n = pl.ds((NT - 1) * big + u * TILE, TILE)
        mixed[:, n] = mixed[:, n] + dot(wall[HOPS - 1, pl.ds(0, hid), :], mi[HOPS - 1, :, n])

    @pl.loop(0, sub // TILE)
    def _(t):
        x = mixed[:, lanes_at(t, TILE)]
        acc0[...] += fold(x)
        acc1[...] += fold(x * x)

    s2h[h, :, pl.ds(0, hid)] = row_of(acc0[...])
    s2h[h, :, pl.ds(hid, hid)] = row_of(acc1[...])
    hops_start(s2h, "s2h")
    for d in range(2):
        wmx[d] = wall[d, pl.ds(0, hid), :].astype(F32).T.astype(BF16)
    hops_wait(s2h, "s2h")
    s2r[r] = total(s2h, HOPS)
    rows_start(s2r, "s2r")
    for d in range(2, HOPS):
        wmx[d] = wall[d, pl.ds(0, hid), :].astype(F32).T.astype(BF16)
    wc48 = wcs[pl.ds(0, 48), :].astype(BF16)
    wcN = wcs[...].T.astype(BF16)
    crow = lax.broadcasted_iota(jnp.int32, (128, 128), 0)
    cbc = jnp.where(crow < ncls, jnp.broadcast_to(cbs[pl.ds(0, 1), :], (128, 128)).T, -1e30)[:48]
    rows_wait(s2r, "s2r")
    st2 = total(s2r, R)
    mean2 = st2[:, :hid] * inv_n
    inv2 = lax.rsqrt(st2[:, hid:] * inv_n - mean2 * mean2 + EPS * 4.0 * KAPPA * KAPPA)
    scale2 = inv2 * gain2[...]
    cols[0] = col_of(scale2)
    cols[1] = col_of(bias2[...] - mean2 * scale2)
    acc0[...] = jnp.zeros(acc0.shape, F32)
    acc1[...] = jnp.zeros(acc1.shape, F32)
    accl[...] = jnp.zeros(accl.shape, F32)
    accw[...] = jnp.zeros(accw.shape, F32)

    o_own = lanes_at(h, sub)

    def lp_copy(d, part):
        n = sub // 2
        return rc(
            lps.at[:, pl.ds(part * n, n)], o_lp.at[:, lanes_at(2 * h + part, n)], "lp", 4 * part + d, peer(d), r
        )

    @pl.loop(0, NT)
    def _(t):
        if NT > 1:

            @pl.when(t == NT // 2)
            def _():
                for d in range(1, HOPS):
                    lp_copy(d, 0).start()

        hbs, slopes, dhs = [], [], []
        ns = [lanes_at(t * UN + u, TILE) for u in range(UN)]
        for n in ns:
            heads, sl = [], []
            for i in range(0, hid, 64):
                rows = pl.ds(i, 64)
                z2 = mixed[rows, n] * spread(cols[0, rows, :], TILE) + spread(cols[1, rows, :], TILE)
                gv, dg = gelu_slope(z2)
                heads.append(gv.astype(BF16))
                sl.append(dg)
            hbs.append(jnp.concatenate(heads, axis=0))
            slopes.append(sl)
        for u, n in enumerate(ns):
            lg = dot(wc48, hbs[u]) + spread(cbc, TILE)
            lg = lg - jnp.max(lg, axis=0, keepdims=True)
            ex = jnp.exp(lg)
            se = jnp.sum(ex, axis=0, keepdims=True)
            lp = lg - jnp.log(se)
            lps[:, n] = lp.astype(BF16)
            own = pl.ds(pl.multiple_of(h * sub + (t * UN + u) * TILE, TILE), TILE)
            hit = lax.broadcasted_iota(jnp.int32, (48, TILE), 0) == lab[:, own]
            accl[pl.ds(48, 48), :] += fold(jnp.where(hit, lp, 0.0))
            dl = ((ex / se - jnp.where(hit, 1.0, 0.0)) * inv_n).astype(BF16)
            accl[pl.ds(0, 48), :] += fold(dl.astype(F32))
            accw[...] += dot_nt(dl, hbs[u])
            dhs.append(dot(wcN, jnp.concatenate([dl, jnp.zeros((80, TILE), BF16)], axis=0)))
        for u, n in enumerate(ns):
            for j, i in enumerate(range(0, hid, 64)):
                rows = pl.ds(i, 64)
                dn = dhs[u][i : i + 64] * slopes[u][j]
                dn2[rows, n] = dn
                acc0[rows, :] += fold(dn * mixed[rows, n])
                acc1[rows, :] += fold(dn)

    for d in range(1, HOPS):
        if NT == 1:
            lp_copy(d, 0).start()
        lp_copy(d, 1).start()
    own_lp = pltpu.make_async_copy(lps, o_lp.at[:, o_own], ss.at[names["lp"]])
    own_lp.start()
    s3h[h, :, pl.ds(0, hid)] = row_of(acc0[...])
    s3h[h, :, pl.ds(hid, hid)] = row_of(acc1[...])
    zpad = jnp.zeros((80, 128), F32)
    s3h[h, :, pl.ds(2 * hid, 128)] = row_of(jnp.concatenate([accl[pl.ds(0, 48), :], zpad], axis=0))
    s3h[h, :, pl.ds(2 * hid + 128, 128)] = row_of(jnp.concatenate([accl[pl.ds(48, 48), :], zpad], axis=0))
    hops_start(s3h, "s3h")

    def cwh_copy(d):
        return rc(cwp.at[d], cwh.at[d], "cwh", d, peer(d), r)

    q = hid // HOPS
    for d in range(HOPS):
        cwp[d] = accw[:, lanes_at(peer(d), q)]
    hops_wait(s3h, "s3h")
    s3r[r] = total(s3h, HOPS)
    rows_start(s3r, "s3r")
    for d in range(1, HOPS):
        cwh_copy(d).start()
    rows_wait(s3r, "s3r")
    st3 = total(s3r, R)
    db2 = st3[:, hid : 2 * hid]
    dg2t = inv2 * (st3[:, :hid] - mean2 * db2)
    o_small[pl.ds(0, 1), :] = dg2t
    o_small[pl.ds(1, 1), :] = db2
    o_small[pl.ds(4, 1), pl.ds(0, 256)] = st3[:, 2 * hid : 2 * hid + 256]
    o_small[pl.ds(4, 1), pl.ds(256, hid - 256)] = jnp.zeros((1, hid - 256), F32)
    t2 = scale2 * inv2 * dg2t * inv_n
    cols[1] = col_of(-t2)
    cols[2] = col_of(t2 * mean2 - scale2 * db2 * inv_n)

    @pl.loop(0, sub // TILE)
    def _(t):
        n = lanes_at(t, TILE)
        for i in range(0, hid, 64):
            rows = pl.ds(i, 64)
            v = dn2[rows, n] * spread(cols[0, rows, :], TILE)
            v = v + mixed[rows, n] * spread(cols[1, rows, :], TILE) + spread(cols[2, rows, :], TILE)
            dmx[rows, n] = v.astype(BF16)

    mine = lanes_at(c, half)
    theirs = lanes_at(1 - c, half)

    def pair_copy(d):
        return rc(dmp.at[d, theirs, :], pr.at[d], "pair", d, h, sib)

    qrows = half // S
    zown = pl.ds(pl.multiple_of(c * half + zpar * qrows, 16), qrows)
    zother = pl.ds(pl.multiple_of(c * half + (1 - zpar) * qrows, 16), qrows)

    def z1_copy(d):
        return rc(dmp.at[d, zother, :], z1r.at[d], "z1", d, h, 2 * zmate + c)

    def z1_start(d):
        if S > 1:
            z1_copy(d).start()

    def z1_sum(d):
        if S > 1:
            done(z1_copy(d))
            dmp[d, zown, :] = (dmp[d, zown, :].astype(F32) + z1r[d].astype(F32)).astype(BF16)

    def hop_copy(d):
        return rc(dmp.at[d, zown, :], hr.at[d], "hop", d, peer(d), r)

    def pair_sum(d):
        done(pair_copy(d))
        dmp[d, mine, :] = (dmp[d, mine, :].astype(F32) + pr[d].astype(F32)).astype(BF16)

    @pl.loop(0, HOPS)
    def _(i):
        d = HOPS - 1 - i

        @pl.loop(0, 2)
        def _(j):
            rows = lanes_at(j, half)
            dmp[d, rows, :] = dot_nt(mi[d, rows, :], dmx[...]).astype(BF16)

        pair_copy(d).start()

        @pl.when(i > 0)
        def _():
            pair_sum(d + 1)
            z1_start(d + 1)

        @pl.when(i > 1)
        def _():
            z1_sum(d + 2)
            hop_copy(d + 2).start()

    G2 = Z // S
    zq = lax.div(zi, S)

    def zr_copy(e, which):
        rows, lanes = chunk(0, which, qrows, G2, hid)
        return rc(hr.at[0, rows, lanes], zr.at[e], "zr", e, h, (lax.rem(zq + e, G2) * S + zpar) * 2 + c)

    def final_chunk(z):
        return chunk(c * half + lax.rem(z, S) * qrows, lax.div(z, S), qrows, G2, hid)

    def zg_copy(e, which):
        rows, lanes = final_chunk(which)
        ref = fin.at[rows, lanes]
        return rc(ref, ref, "zg", e, h, lax.rem(zi + e, Z) * 2 + c)

    def ddm_copy(core):
        ref = fin.at[lanes_at(core, half), :]
        return rc(ref, ref, "ddm", 0, h, sib)

    def d_copy(d):
        return rc(dsend.at[d], o_d.at[h], "d", d, peer(d), r)

    def dt_copy(d):
        return rc(dtail.at[d], o_dt.at[h], "dt", d, peer(d), r)

    def pp_copy(d):
        return rc(ps.at[d, :, theirs], ph.at[d], "pp", d, h, sib)

    def p_copy(d):
        return rc(phalf.at[d], prv.at[d], "p", d, peer(d), r)

    def q_copy(d):
        return rc(qs.at[d], qv.at[d], "q", d, peer(d), r)

    def p_half(d):
        done(pp_copy(d))
        phalf[d] = (ps[d, :, mine].astype(F32) + ph[d].astype(F32)).astype(BF16)

    @pl.loop(0, HOPS * NT)
    def _(it):
        dd = lax.div(it, NT)
        t = lax.rem(it, NT)
        d = HOPS - 1 - dd

        @pl.when(t == 0)
        def _():
            pT[...] = jnp.zeros(pT.shape, F32)

        @pl.when(jnp.logical_and(t == NT // 2, dd > 0))
        def _():
            p_half(d + 1)
            p_copy(d + 1).start()

        @pl.when(it == NT // 2)
        def _():
            pair_sum(0)
            z1_start(0)
            z1_sum(1)
            hop_copy(1).start()

        @pl.when(it == NT + NT // 2)
        def _():
            for j in range(1, HOPS):
                done(cwh_copy(j))
            cwr[r] = cwp[0] + (cwh[1] + cwh[2] + cwh[3])
            rows_start(cwr, "cwr")
            z1_sum(0)

        @pl.when(it == 2 * NT + NT // 2)
        def _():
            for j in range(1, HOPS):
                done(hop_copy(j))
            hsum = dmp[0, zown, :].astype(F32) + hr[1].astype(F32) + hr[2].astype(F32) + hr[3].astype(F32)
            hr[0] = hsum.astype(BF16)

            @functools.partial(each, 1, G2)
            def _(e):
                zr_copy(e, lax.rem(zq + e, G2)).start()

            rows_wait(cwr, "cwr")
            cwg[h] = total(cwr, R)
            hops_start(cwg, "cwg")

        @pl.when(it == 3 * NT + NT // 2)
        def _():
            @functools.partial(each, 1, G2)
            def _(e):
                done(zr_copy(e, lax.rem(zq + e, G2)))

            rows, lanes = chunk(0, zq, qrows, G2, hid)
            zt = hr[0, rows, lanes].astype(F32)
            for e in range(1, G2):
                zt = zt + zr[e].astype(F32)
            frows, flanes = final_chunk(zi)
            fin[frows, flanes] = zt.astype(BF16)

            @functools.partial(each, 1, Z)
            def _(e):
                zg_copy(e, zi).start()

            hops_wait(cwg, "cwg")
            for j in range(HOPS):
                o_cw[:, pl.ds(j * q, q)] = cwg[j]

        ns = [lanes_at(t * UN + u, TILE) for u in range(UN)]
        dcs = [dot(wmx[d], dmx[:, n]) for n in ns]
        for u, n in enumerate(ns):
            dn = jnp.concatenate(
                [dcs[u][i : i + 64].astype(BF16) * gp[d, pl.ds(i, 64), n] for i in range(0, hid, 64)], axis=0
            )
            pT[...] += dot_nt(dn, fx[d, :, n])
            grad = dot(aw[d], dn)
            dsend[d, :, n] = grad[:MAIN].astype(BF16)
            d4[:, n] = grad[MAIN : MAIN + 8]

        @pl.when(t == NT - 1)
        def _():
            pw = pT[...].T * KAPPA
            qs[d, :, pl.ds(0, hid)] = jnp.sum(pw * wall[d, wrow, :].astype(F32), axis=0, keepdims=True)
            qs[d, :, pl.ds(hid, hid)] = pw[ONES : ONES + 1, :]
            ps[d] = pw[:FP].astype(BF16)
            pp_copy(d).start()
            pack4(d4, dtail.at[d])

            @pl.when(dd < HOPS - 1)
            def _():
                q_copy(d).start()
                d_copy(d).start()
                dt_copy(d).start()

    for d in range(1, HOPS):
        done(q_copy(d))
    qr[r] = qs[0] + (qv[1] + qv[2] + qv[3])
    rows_start(qr, "qr")
    own_d = pltpu.make_async_copy(dsend.at[0], o_d.at[h], ss.at[names["d"]])
    own_d.start()
    own_dt = pltpu.make_async_copy(dtail.at[0], o_dt.at[h], ss.at[names["dt"]])
    own_dt.start()

    p_half(0)
    for d in range(1, HOPS):
        done(p_copy(d))
    psum = phalf[0].astype(F32) + (prv[1].astype(F32) + prv[2].astype(F32) + prv[3].astype(F32))
    pz[zi] = psum.astype(BF16)

    def pz_copy(e, which):
        return rc(pz.at[which], pz.at[which], "pz", e, h, lax.rem(zi + e, Z) * 2 + c)

    @functools.partial(each, 1, Z)
    def _(e):
        pz_copy(e, zi).start()

    @functools.partial(each, 1, Z)
    def _(e):
        zg_copy(e, zi).wait_send()
        zg_copy(e, lax.rem(zi + Z - e, Z)).wait_recv()

    ddm_copy(c).start()

    rows_wait(qr, "qr")
    qt = total(qr, R)
    db = qt[:, hid:]
    dgn = inv * (qt[:, :hid] - mean * db)
    o_small[pl.ds(2, 1), :] = dgn
    o_small[pl.ds(3, 1), :] = db
    c1 = scale * db * inv_n
    c2 = inv * scale * dgn * inv_n
    shift = c1 - mean * c2
    row = lax.broadcasted_iota(jnp.int32, (128, hid), 0)
    q1, q2 = split2(jnp.where(row == ONES, shift, wown32 * c2))
    o_m[...] = (dot_nt(wown, q1) + dot_nt(wown, q2))[:FP]
    rows_wait(gbuf, "gr")
    g1, g2, g3 = split3(total(gbuf, R))
    gq = dot(g1, q1) + dot(g2, q1) + dot(g3, q1) + dot(g1, q2) + dot(g2, q2)

    @functools.partial(each, 1, Z)
    def _(e):
        pz_copy(e, zi).wait_send()
        pz_copy(e, lax.rem(zi + Z - e, Z)).wait_recv()

    pt = pz[0].astype(F32)
    for j in range(1, Z):
        pt = pt + pz[j].astype(F32)
    pfin[c] = pt.astype(BF16)

    def pd_copy(core):
        return rc(pfin.at[core], pfin.at[core], "pd", 0, h, sib)

    pd_copy(c).start()
    ddm_copy(c).wait_send()
    ddm_copy(1 - c).wait_recv()
    o_mix[...] = fin[...]
    pd_copy(c).wait_send()
    pd_copy(1 - c).wait_recv()
    ptot = jnp.concatenate([pfin[0], pfin[1]], axis=1).astype(F32)
    o_gw[...] = ptot * scale - gq
    own_d.wait()
    own_dt.wait()
    own_lp.wait()
    for d in range(1, HOPS):
        done(d_copy(d))
        done(dt_copy(d))
        done(lp_copy(d, 0))
        done(lp_copy(d, 1))


def last_kernel(
    nodes,
    ft, d, dt, lp, m, mix, gw, small, cw,
    o_lp, o_gf, o_mix, o_gw, o_gg, o_gb, o_hg, o_hb, o_cw, o_cb, o_loss, low,
):
    feat, n = ft.shape
    ncls = o_lp.shape[0]
    o_lp[...] = lp[...].astype(F32)[:ncls]
    mm = m[...]
    f = ft[...]
    fix = dot(mm[:, :feat].astype(BF16), f) + mm[:, ONES : ONES + 1]
    tail = dt[0].astype(F32)
    for b in range(4):
        low[pl.ds(0, 4), pl.ds(b * (n // 4), n // 4)] = tail[4 * b : 4 * b + 4]
    gf = jnp.concatenate([d[0].astype(F32), low[...]], axis=0)[:feat] - fix[:feat]
    if STRIDED:
        flat = o_gf.reshape(feat * (n // 128), 128)
        for i in range(n // 128):
            flat[pl.ds(i, feat, stride=n // 128), :] = gf[:, i * 128 : (i + 1) * 128]
    else:
        for i in range(n // 128):
            o_gf[:, i, :] = gf[:, i * 128 : (i + 1) * 128]

    @pl.when(pl.program_id(0) == 0)
    def _():
        hid = mix.shape[1]
        o_mix[...] = mix[...].astype(F32)
        for i in range(hid // 128):
            o_gw[:, i, :] = gw[pl.ds(0, feat), pl.ds(i * 128, 128)]
        o_hg[...] = small[pl.ds(0, 1), :]
        o_hb[...] = small[pl.ds(1, 1), :]
        o_gg[...] = small[pl.ds(2, 1), :]
        o_gb[...] = small[pl.ds(3, 1), :]
        o_cw[...] = cw[pl.ds(0, ncls), :]
        o_cb[...] = small[pl.ds(4, 1), pl.ds(0, ncls)]
        o_loss[...] = jnp.sum(small[pl.ds(4, 1), pl.ds(128, 128)], axis=1, keepdims=True) * (-1.0 / nodes)


def shards(
    R, features, branch_weight, branch_gain, branch_bias, mix_weight, mixing_norm_gain, mixing_norm_bias,
    class_weight, class_bias, labels, hop_mask,
):
    local, feat = features.shape[1:]
    hid = mix_weight.shape[0]
    ncls = class_weight.shape[1]
    nodes = local * R
    sub = local // HOPS
    Z = R // 2
    half = hid // 2
    S = min(Z, 2)
    G2, qrows = Z // S, half // S
    zrows, zcols = chunk(0, 0, qrows, G2, hid)
    assert feat == ONES and ncls == 47 and local // hop_mask.shape[0] == 128
    ft = features[0].T
    sd = jax.ShapeDtypeStruct
    vm = pl.BlockSpec(memory_space=pltpu.VMEM)
    hbm = pl.BlockSpec(memory_space=pl.ANY)
    _, nsem = sem_plan(R)
    V = pltpu.VMEM
    outs = pl.pallas_call(
        functools.partial(main_kernel, R, nodes),
        grid=(1,),
        out_shape=(
            sd((48, local), BF16),
            sd((HOPS, MAIN, sub), BF16),
            sd((HOPS, 16, sub // 4), BF16),
            sd((FP, 128), F32),
            sd((hid, hid), BF16),
            sd((FP, hid), F32),
            sd((8, hid), F32),
            sd((48, hid), F32),
        ),
        in_specs=[hbm, pl.BlockSpec((16, local), lambda i: (MAIN // 16, 0))]
        + [vm] * 9
        + [pl.BlockSpec(memory_space=pltpu.SMEM)],
        out_specs=(hbm, hbm, hbm, vm, vm, vm, vm, vm),
        scratch_shapes=[
            V((128, local), BF16),
            V((HOPS, 128, sub), BF16),
            V((HOPS, 16, sub // 4), BF16),
            V((HOPS, 16, sub // 4), BF16),
            V((48, sub // 4), F32),
            V((HOPS, hid + 128, hid), BF16),
            V((HOPS, hid, 256), BF16),
            V((HOPS, FP, hid), BF16),
            V((HOPS, hid, hid), BF16),
            V((HOPS, 16, sub), BF16),
            V((HOPS, hid, sub), BF16),
            V((HOPS, hid, sub), BF16),
            V((hid, sub), F32),
            V((hid, sub), F32),
            V((hid, sub), BF16),
            V((R, FP, 128), F32),
            V((R, 1, 2 * hid), F32),
            V((HOPS, 1, 2 * hid), F32),
            V((HOPS, 1, 2 * hid), F32),
            V((R, 1, 2 * hid), F32),
            V((HOPS, 1, 2 * hid + 256), F32),
            V((R, 1, 2 * hid + 256), F32),
            V((HOPS, 48, hid // HOPS), F32),
            V((HOPS, 48, hid // HOPS), F32),
            V((R, 48, hid // HOPS), F32),
            V((HOPS, 48, hid // HOPS), F32),
            V((48, sub), BF16),
            V((128, hid), F32),
            V((8, 128), F32),
            V((hid, 128), F32),
            V((hid, 128), F32),
            V((96, 128), F32),
            V((48, hid), F32),
            V((3, hid, 128), F32),
            V((HOPS, hid, hid), BF16),
            V((HOPS, half, hid), BF16),
            V((HOPS, qrows, hid), BF16),
            V((HOPS, qrows, hid), BF16),
            V((max(G2, 2), zrows.size, zcols.size), BF16),
            V((hid, hid), BF16),
            V((HOPS, MAIN, sub), BF16),
            V((8, sub), F32),
            V((HOPS, 16, sub // 4), BF16),
            V((hid, 128), F32),
            V((HOPS, FP, hid), BF16),
            V((HOPS, FP, half), BF16),
            V((HOPS, FP, half), BF16),
            V((HOPS, FP, half), BF16),
            V((HOPS, 1, 2 * hid), F32),
            V((HOPS, 1, 2 * hid), F32),
            V((R, 1, 2 * hid), F32),
            V((Z, FP, half), BF16),
            V((2, FP, half), BF16),
            pltpu.SemaphoreType.DMA((nsem,)),
            pltpu.SemaphoreType.DMA((nsem,)),
        ],
        compiler_params=pltpu.CompilerParams(
            collective_id=0, has_side_effects=True, vmem_limit_bytes=63 * 1024 * 1024
        ),
        cost_estimate=pl.CostEstimate(flops=2 * 8 * 10**9, bytes_accessed=10**7, transcendentals=10**7),
        name="main",
    )(
        ft, ft, branch_weight[0], branch_gain, branch_bias, mix_weight, mixing_norm_gain[None], mixing_norm_bias[None],
        class_weight.T, class_bias[None], labels[None], hop_mask.T,
    )
    lp, dd, dt, m, mix, gw, small, cw = outs
    nb = sub
    whole = lambda shape: pl.BlockSpec(shape, lambda i: (0,) * len(shape))
    lp, gf, mix, gw, gg, gb, hg, hb, cw, cb, loss = pl.pallas_call(
        functools.partial(last_kernel, nodes),
        grid=(local // nb,),
        out_shape=(
            sd((ncls, local), F32),
            sd((feat, local // 128, 128), F32),
            sd((hid, hid), F32),
            sd((feat, hid // 128, 128), F32),
            sd((1, hid), F32),
            sd((1, hid), F32),
            sd((1, hid), F32),
            sd((1, hid), F32),
            sd((ncls, hid), F32),
            sd((1, ncls), F32),
            sd((1, 1), F32),
        ),
        in_specs=[
            pl.BlockSpec((feat, nb), lambda i: (0, i)),
            pl.BlockSpec((1, MAIN, nb), lambda i: (i, 0, 0)),
            pl.BlockSpec((1, 16, nb // 4), lambda i: (i, 0, 0)),
            pl.BlockSpec((48, nb), lambda i: (0, i)),
            whole((FP, 128)),
            whole((hid, hid)),
            whole((FP, hid)),
            whole((8, hid)),
            whole((48, hid)),
        ],
        out_specs=(
            pl.BlockSpec((ncls, nb), lambda i: (0, i)),
            pl.BlockSpec((feat, nb // 128, 128), lambda i: (0, i, 0)),
            whole((hid, hid)),
            whole((feat, hid // 128, 128)),
            whole((1, hid)),
            whole((1, hid)),
            whole((1, hid)),
            whole((1, hid)),
            whole((ncls, hid)),
            whole((1, ncls)),
            whole((1, 1)),
        ),
        scratch_shapes=[V((8, nb), F32)],
        compiler_params=pltpu.CompilerParams(vmem_limit_bytes=60 * 1024 * 1024),
        name="last",
    )(ft, dd, dt, lp, m, mix, gw, small, cw)
    return (
        lp.T,
        loss[0, 0],
        with_layout_constraint(gf.reshape(feat, 1, local), Layout((0, 1, 2))).transpose(1, 2, 0),
        gw.reshape(1, feat, hid),
        gg,
        gb,
        mix,
        hg[0],
        hb[0],
        cw.T,
        cb[0],
    )


def solution(mesh):
    placed = (
        P("hop", "rows", None), P("hop", None, None), P("hop", None), P("hop", None), P("hop", None),
        P(), P(), P(), P(), P("rows"), P("rows", None),
    )
    assert mesh.shape["hop"] == HOPS
    return jax.shard_map(
        functools.partial(shards, mesh.shape["rows"]),
        mesh=mesh,
        in_specs=placed,
        out_specs=(
            P("rows", None), P(), P("hop", "rows", None), P("hop", None, None), P("hop", None), P("hop", None),
            P("hop", None), P(), P(), P(), P(),
        ),
        check_vma=False,
    )
```

```python
import functools
import math

import jax
import jax.numpy as jnp
from jax import lax
from jax.experimental import pallas as pl
from jax.experimental.layout import Layout, with_layout_constraint
from jax.experimental.pallas import tpu as pltpu
from jax.sharding import PartitionSpec as P

MESH = pl.DeviceIdType.MESH
EPS = 1e-05
HOPS = 4
ONES = 100
FP = 112
MAIN = 96
TILE = 256
STRIDED = True
C0 = math.sqrt(2.0 / math.pi)
C1 = C0 * 0.044715
KAPPA = C1 ** (1.0 / 3.0)
ALPHA = C0 / KAPPA
F32 = jnp.float32
BF16 = jnp.bfloat16


def dot(a, b):
    return lax.dot_general(a, b, (((1,), (0,)), ((), ())), preferred_element_type=F32)


def dot_nt(a, b):
    return lax.dot_general(a, b, (((1,), (1,)), ((), ())), preferred_element_type=F32)


def split2(x):
    hi = x.astype(BF16)
    return hi, (x - hi.astype(F32)).astype(BF16)


def split3(x):
    hi = x.astype(BF16)
    rest = x - hi.astype(F32)
    mid = rest.astype(BF16)
    return hi, mid, (rest - mid.astype(F32)).astype(BF16)


def gelu_slope(z):
    u = z * z
    t = jnp.tanh(z * (C0 + C1 * u))
    s = 0.5 * t + 0.5
    g = z * s
    return g, s + (g - g * s) * (2.0 * C0 + 6.0 * C1 * u)


def scaled_gelu_slope(y):
    u = y * y
    t = jnp.tanh(y * (u + ALPHA))
    up = t + 1.0
    g = y * up
    return g, up + (g * (1.0 - t)) * (3.0 * u + ALPHA)


def fold(x):
    total = x[:, :128]
    for i in range(1, x.shape[1] // 128):
        total = total + x[:, i * 128 : (i + 1) * 128]
    return total


def spread(c, n):
    return jnp.concatenate([c] * (n // 128), axis=1)


def row_of(acc):
    return jnp.sum(acc.T, axis=0, keepdims=True)


def col_of(row):
    return jnp.broadcast_to(row, (128, row.shape[1])).T


def each(lo, hi, body):
    if hi - lo <= 16:
        for i in range(lo, hi):
            body(i)
    else:
        pl.loop(lo, hi)(body)


class Alloc:
    def __init__(self):
        self.n = 0

    def __call__(self, count):
        base = self.n
        self.n += count
        return base


def sem_plan(R):
    Z = R // 2
    a = Alloc()
    names = {}
    for name, count in (
        ("feat", 4), ("ft", 4), ("loc", 1), ("ws", 4), ("zf", 4), ("dd", 4), ("s1", R), ("ab", 4), ("gr", R),
        ("s2", HOPS * R), ("s3", HOPS * R), ("lp", 8), ("cwh", 4), ("cwr", R), ("cwg", 4),
        ("pair", 4), ("z1", 4), ("hop", 4), ("zr", Z), ("zg", Z), ("ddm", 1), ("d", 4), ("dt", 4), ("p", 4), ("q", 4),
        ("qr", R), ("prs", R), ("pag", R),
    ):
        names[name] = a(count)
    return names, a.n


def chunk(base, i, rows, pieces, cols):
    if rows // pieces >= 16:
        take = rows // pieces
        return pl.ds(pl.multiple_of(base + i * take, 16), take), pl.ds(0, cols)
    m = 16 * pieces // rows
    wide = cols // m
    return (
        pl.ds(pl.multiple_of(base + (i // m) * 16, 16), 16),
        pl.ds(pl.multiple_of((i % m) * wide, 128), wide),
    )


def main_kernel(
    R,
    nodes,
    ft, ft4, wb, bgain, bbias, wm, gain2, bias2, wc, cb, lab, msk,
    o_lp, o_d, o_dt, o_m, o_mix, o_gw, o_small, o_cw,
    fs, fx, ftail, frt, st4, wall, wl, aw, wmx, keep, mi, gp, mixed, dn2, dmx,
    gbuf, s1, ab, s2, s3, cwp, cwh, cwr, cwg, lps,
    wcs, cbs, acc0, acc1, accl, accw, cols,
    dmp, pr, z1r, hr, zr, fin, dsend, d4, dtail, pT, ps, prv, qs, qv, qr, prs, psum, pfin,
    ss, rs,
):
    names, _ = sem_plan(R)
    Z = R // 2
    h = lax.axis_index("hop")
    r = lax.axis_index("rows")
    c = lax.rem(r, 2)
    zi = lax.div(r, 2)
    sib = r + 1 - 2 * c
    local = ft.shape[1]
    sub = local // HOPS
    hid = wm.shape[0]
    half = hid // 2
    big = min(2 * TILE, sub)
    UN = big // TILE
    NT = sub // big
    inv_n = 1.0 / nodes

    def peer(d):
        x = lax.rem(h + d, 2)
        y = lax.rem(lax.div(h, 2) + lax.div(d, 2), 2)
        return 2 * y + x

    def rc(src, dst, name, i, hh, rr):
        return pltpu.make_async_remote_copy(
            src_ref=src, dst_ref=dst, send_sem=ss.at[names[name] + i], recv_sem=rs.at[names[name] + i],
            device_id=(hh, rr), device_id_type=MESH,
        )

    def done(cp):
        cp.wait_send()
        cp.wait_recv()

    def lanes_at(i, n):
        return pl.ds(pl.multiple_of(i * n, n), n)

    barrier = pltpu.get_barrier_semaphore()

    def greet(hh, rr):
        pl.semaphore_signal(barrier, inc=1, device_id=(hh, rr), device_id_type=MESH)

    D = HOPS * R
    me = h * R + r

    @functools.partial(each, 1, D)
    def _(e):
        other = lax.rem(me + e, D)
        greet(lax.div(other, R), lax.rem(other, R))

    def all_start(buf, name):
        @functools.partial(each, 1, D)
        def _(e):
            other = lax.rem(me + e, D)
            rc(buf.at[me], buf.at[me], name, e, lax.div(other, R), lax.rem(other, R)).start()

    def all_wait(buf, name):
        @functools.partial(each, 1, D)
        def _(e):
            other = lax.rem(me + D - e, D)
            done(rc(buf.at[other], buf.at[other], name, e, lax.div(other, R), lax.rem(other, R)))

    def rows_start(buf, name):
        @functools.partial(each, 1, R)
        def _(e):
            rc(buf.at[r], buf.at[r], name, e, h, lax.rem(r + e, R)).start()

    def rows_wait(buf, name):
        @functools.partial(each, 1, R)
        def _(e):
            src = lax.rem(r + R - e, R)
            done(rc(buf.at[src], buf.at[src], name, e, h, lax.rem(r + e, R)))

    def hops_start(buf, name):
        for d in range(1, HOPS):
            rc(buf.at[h], buf.at[h], name, d, peer(d), r).start()

    def hops_wait(buf, name):
        for d in range(1, HOPS):
            done(rc(buf.at[peer(d)], buf.at[peer(d)], name, d, peer(d), r))

    def total(buf, n):
        t = buf[0]
        for i in range(1, n):
            t = t + buf[i]
        return t

    loc = pltpu.make_async_copy(ft.at[pl.ds(0, MAIN), :], fs.at[pl.ds(0, MAIN), :], ss.at[names["loc"]])
    loc.start()

    def pack4(src, dst):
        n = st4.shape[1]
        for b in range(4):
            st4[pl.ds(4 * b, 4), :] = src[pl.ds(0, 4), pl.ds(b * n, n)].astype(F32)
        dst[...] = st4[pl.ds(0, 16), :].astype(BF16)

    def unpack4(src, dst):
        n = st4.shape[1]
        row = lax.broadcasted_iota(jnp.int32, (32, n), 0)
        st4[pl.ds(0, 16), :] = src[...].astype(F32)
        st4[pl.ds(16, 32), :] = jnp.where(row == ONES - MAIN, 1.0, 0.0)
        for b in range(4):
            st4[pl.ds(16, 4), :] = st4[pl.ds(4 * b, 4), :]
            dst[pl.ds(MAIN, 32), pl.ds(b * n, n)] = st4[pl.ds(16, 32), :].astype(BF16)

    wrow = pl.ds(hid, 128)
    wall[0, pl.ds(hid + 96, 32), :] = jnp.zeros((32, hid), BF16)
    wall[0, pl.ds(hid, 100), :] = wb[...]
    wall[0, pl.ds(0, hid), :] = wm[...].astype(F32).T.astype(BF16)

    def feat_copy(d):
        rows = pl.ds(0, MAIN)
        return rc(ft.at[rows, lanes_at(peer(d), sub)], fx.at[d, rows, :], "feat", d, peer(d), r)

    def ft_copy(d):
        return rc(ftail.at[peer(d)], frt.at[d], "ft", d, peer(d), r)

    pl.semaphore_wait(barrier, D - 1)

    S = min(Z, 2)
    part = (hid + 128) // (2 * S)
    zpar = lax.rem(zi, S)
    zmate = zi + (S - 1) - 2 * (S - 1) * zpar

    def part_rows(core, par):
        return pl.ds(pl.multiple_of((core * S + par) * part, 16), part)

    def ws_copy(d):
        rows = part_rows(c, zpar)
        return rc(wall.at[0, rows, :], wall.at[d, rows, :], "ws", d, peer(d), r)

    def zf_copy(d, par):
        ref = wall.at[d, part_rows(c, par), :]
        return rc(ref, ref, "zf", d, h, 2 * zmate + c)

    def dd_copy(d, core):
        ref = wall.at[d, pl.ds(pl.multiple_of(core * S * part, 16), S * part), :]
        return rc(ref, ref, "dd", d, h, sib)

    for d in range(1, HOPS):
        ws_copy(d).start()
    for d in range(1, HOPS - 1):
        feat_copy(d).start()
    for j in range(HOPS):
        lanes = pl.ds(j * sub, sub)
        pack4(ft4.at[:, lanes], ftail.at[j])
        unpack4(ftail.at[j], fs.at[:, lanes])
    for d in range(1, HOPS):
        ft_copy(d).start()
    loc.wait()
    fx[0] = fs[:, lanes_at(h, sub)]

    def gram(i, g):
        f = fs[:, lanes_at(i, sub)]
        return g + dot_nt(f, f)

    g = lax.fori_loop(0, HOPS, gram, jnp.zeros((128, 128), F32))
    wown = wall[0, wrow, :]
    wown32 = wown.astype(F32)
    g1, g2, g3 = split3(g)
    gw = dot(g1, wown) + dot(g2, wown) + dot(g3, wown)
    s1[r, :, pl.ds(0, hid)] = gw[ONES : ONES + 1, :]
    s1[r, :, pl.ds(hid, hid)] = jnp.sum(gw * wown32, axis=0, keepdims=True)
    rows_start(s1, "s1")
    gbuf[r] = g[:FP]

    for d in range(HOPS):
        late = peer(d) - 2
        col = jnp.maximum(late, 0)
        for b in range(sub // 128):
            m = jnp.where(late >= 0, msk[col, h * (sub // 128) + b], 1)
            keep[d, :, pl.ds(b * 128, 128)] = jnp.full((16, 128), 0.5 * m.astype(F32)).astype(BF16)
    wcs[...] = jnp.zeros(wcs.shape, F32)
    wcs[pl.ds(0, wc.shape[0]), :] = wc[...].astype(F32)
    cbs[...] = jnp.zeros(cbs.shape, F32)
    cbs[pl.ds(0, 1), pl.ds(0, cb.shape[1])] = cb[...]
    ncls = wc.shape[0]

    @pl.loop(0, sub // TILE)
    def _(t):
        mixed[:, lanes_at(t, TILE)] = jnp.zeros((hid, TILE), F32)

    mi[0, :, pl.ds(0, big)] = jnp.zeros((hid, big), BF16)

    rows_wait(s1, "s1")
    st = total(s1, R)
    mean = st[:, :hid] * inv_n
    var = st[:, hid:] * inv_n - mean * mean
    inv = lax.rsqrt(var + EPS)
    scale = inv * bgain[...]
    ab[0, :, pl.ds(0, hid)] = scale
    ab[0, :, pl.ds(hid, hid)] = bbias[...] - mean * scale

    def ab_copy(d):
        return rc(ab.at[0], ab.at[d], "ab", d, peer(d), r)

    for d in range(1, HOPS):
        ab_copy(d).start()

    def prepare(d):
        a = ab[d, :, pl.ds(0, hid)]
        b = ab[d, :, pl.ds(hid, hid)]
        ws = wall[d, wrow, :].astype(F32) * (a * KAPPA)
        aw[d] = ws[:FP].astype(BF16)
        row = lax.broadcasted_iota(jnp.int32, (128, hid), 0)
        wt = jnp.where(row == ONES, b * KAPPA, ws).T
        hi, lo = split2(wt)
        wl[d, :, pl.ds(0, 128)] = hi
        wl[d, :, pl.ds(128, 128)] = lo

    prepare(0)

    @pl.loop(0, HOPS * NT)
    def _(it):
        d = lax.div(it, NT)
        t = lax.rem(it, NT)

        @pl.when(jnp.logical_and(t == 0, d > 0))
        def _():
            done(feat_copy(d))
            done(ft_copy(d))
            unpack4(frt.at[d], fx.at[d])
            dd_copy(d, c).wait_send()
            dd_copy(d, 1 - c).wait_recv()
            done(ab_copy(d))
            prepare(d)

        if S > 1:

            @pl.when(it == min(1, NT - 1))
            def _():
                for j in range(1, HOPS):
                    done(ws_copy(j))
                    zf_copy(j, zpar).start()

        @pl.when(it == min(2, NT - 1))
        def _():
            feat_copy(HOPS - 1).start()

        @pl.when(jnp.logical_and(t == NT - 1, d < HOPS - 1))
        def _():
            if S > 1:
                zf_copy(d + 1, zpar).wait_send()
                zf_copy(d + 1, 1 - zpar).wait_recv()
            else:
                done(ws_copy(d + 1))
            dd_copy(d + 1, c).start()

        @pl.when(it == 2 * NT)
        def _():
            rows_start(gbuf, "gr")

        pit = jnp.maximum(it - 1, 0)
        pd = lax.div(pit, NT)
        pt = lax.rem(pit, NT)
        adds = []
        for u in range(UN):
            adds.append(dot(wall[pd, pl.ds(0, hid), :], mi[pd, :, lanes_at(pt * UN + u, TILE)]))
        for u in range(UN):
            n = lanes_at(t * UN + u, TILE)
            f = fx[d, :, n]
            z = dot(wl[d], jnp.concatenate([f, f], axis=0))
            k = keep[d, :, n]
            k = jnp.concatenate([k] * 4, axis=0)
            for i in range(0, hid, 64):
                g1, d1 = scaled_gelu_slope(z[i : i + 64].astype(BF16))
                g2, d2 = scaled_gelu_slope(g1 * k)
                mi[d, pl.ds(i, 64), n] = g2
                gp[d, pl.ds(i, 64), n] = d1 * d2 * k
        for u in range(UN):
            n = lanes_at(pt * UN + u, TILE)
            mixed[:, n] = mixed[:, n] + adds[u]

    acc0[...] = jnp.zeros(acc0.shape, F32)
    acc1[...] = jnp.zeros(acc1.shape, F32)
    for u in range(UN):
        n = pl.ds((NT - 1) * big + u * TILE, TILE)
        mixed[:, n] = mixed[:, n] + dot(wall[HOPS - 1, pl.ds(0, hid), :], mi[HOPS - 1, :, n])

    @pl.loop(0, sub // TILE)
    def _(t):
        x = mixed[:, lanes_at(t, TILE)]
        acc0[...] += fold(x)
        acc1[...] += fold(x * x)

    s2[me, :, pl.ds(0, hid)] = row_of(acc0[...])
    s2[me, :, pl.ds(hid, hid)] = row_of(acc1[...])
    all_start(s2, "s2")
    for d in range(HOPS):
        wmx[d] = wall[d, pl.ds(0, hid), :].astype(F32).T.astype(BF16)
    wc48 = wcs[pl.ds(0, 48), :].astype(BF16)
    wcN = wcs[...].T.astype(BF16)
    crow = lax.broadcasted_iota(jnp.int32, (128, 128), 0)
    cbc = jnp.where(crow < ncls, jnp.broadcast_to(cbs[pl.ds(0, 1), :], (128, 128)).T, -1e30)[:48]
    all_wait(s2, "s2")
    st2 = total(s2, D)
    mean2 = st2[:, :hid] * inv_n
    inv2 = lax.rsqrt(st2[:, hid:] * inv_n - mean2 * mean2 + EPS * 4.0 * KAPPA * KAPPA)
    scale2 = inv2 * gain2[...]
    cols[0] = col_of(scale2)
    cols[1] = col_of(bias2[...] - mean2 * scale2)
    acc0[...] = jnp.zeros(acc0.shape, F32)
    acc1[...] = jnp.zeros(acc1.shape, F32)
    accl[...] = jnp.zeros(accl.shape, F32)
    accw[...] = jnp.zeros(accw.shape, F32)

    o_own = lanes_at(h, sub)

    def lp_copy(d, part):
        n = sub // 2
        return rc(
            lps.at[:, pl.ds(part * n, n)], o_lp.at[:, lanes_at(2 * h + part, n)], "lp", 4 * part + d, peer(d), r
        )

    @pl.loop(0, NT)
    def _(t):
        if NT > 1:

            @pl.when(t == NT // 2)
            def _():
                for d in range(1, HOPS):
                    lp_copy(d, 0).start()

        hbs, slopes, dhs = [], [], []
        ns = [lanes_at(t * UN + u, TILE) for u in range(UN)]
        for n in ns:
            heads, sl = [], []
            for i in range(0, hid, 64):
                rows = pl.ds(i, 64)
                z2 = mixed[rows, n] * spread(cols[0, rows, :], TILE) + spread(cols[1, rows, :], TILE)
                gv, dg = gelu_slope(z2)
                heads.append(gv.astype(BF16))
                sl.append(dg)
            hbs.append(jnp.concatenate(heads, axis=0))
            slopes.append(sl)
        for u, n in enumerate(ns):
            lg = dot(wc48, hbs[u]) + spread(cbc, TILE)
            lg = lg - jnp.max(lg, axis=0, keepdims=True)
            ex = jnp.exp(lg)
            se = jnp.sum(ex, axis=0, keepdims=True)
            lp = lg - jnp.log(se)
            lps[:, n] = lp.astype(BF16)
            own = pl.ds(pl.multiple_of(h * sub + (t * UN + u) * TILE, TILE), TILE)
            hit = lax.broadcasted_iota(jnp.int32, (48, TILE), 0) == lab[:, own]
            accl[pl.ds(48, 48), :] += fold(jnp.where(hit, lp, 0.0))
            dl = ((ex / se - jnp.where(hit, 1.0, 0.0)) * inv_n).astype(BF16)
            accl[pl.ds(0, 48), :] += fold(dl.astype(F32))
            accw[...] += dot_nt(dl, hbs[u])
            dhs.append(dot(wcN, jnp.concatenate([dl, jnp.zeros((80, TILE), BF16)], axis=0)))
        for u, n in enumerate(ns):
            for j, i in enumerate(range(0, hid, 64)):
                rows = pl.ds(i, 64)
                dn = dhs[u][i : i + 64] * slopes[u][j]
                dn2[rows, n] = dn
                acc0[rows, :] += fold(dn * mixed[rows, n])
                acc1[rows, :] += fold(dn)

    for d in range(1, HOPS):
        if NT == 1:
            lp_copy(d, 0).start()
        lp_copy(d, 1).start()
    own_lp = pltpu.make_async_copy(lps, o_lp.at[:, o_own], ss.at[names["lp"]])
    own_lp.start()
    s3[me, :, pl.ds(0, hid)] = row_of(acc0[...])
    s3[me, :, pl.ds(hid, hid)] = row_of(acc1[...])
    zpad = jnp.zeros((80, 128), F32)
    s3[me, :, pl.ds(2 * hid, 128)] = row_of(jnp.concatenate([accl[pl.ds(0, 48), :], zpad], axis=0))
    s3[me, :, pl.ds(2 * hid + 128, 128)] = row_of(jnp.concatenate([accl[pl.ds(48, 48), :], zpad], axis=0))
    all_start(s3, "s3")

    def cwh_copy(d):
        return rc(cwp.at[d], cwh.at[d], "cwh", d, peer(d), r)

    q = hid // HOPS
    for d in range(HOPS):
        cwp[d] = accw[:, lanes_at(peer(d), q)]
    for d in range(1, HOPS):
        cwh_copy(d).start()
    all_wait(s3, "s3")
    st3 = total(s3, D)
    db2 = st3[:, hid : 2 * hid]
    dg2t = inv2 * (st3[:, :hid] - mean2 * db2)
    o_small[pl.ds(0, 1), :] = dg2t
    o_small[pl.ds(1, 1), :] = db2
    o_small[pl.ds(4, 1), pl.ds(0, 256)] = st3[:, 2 * hid : 2 * hid + 256]
    o_small[pl.ds(4, 1), pl.ds(256, hid - 256)] = jnp.zeros((1, hid - 256), F32)
    t2 = scale2 * inv2 * dg2t * inv_n
    cols[1] = col_of(-t2)
    cols[2] = col_of(t2 * mean2 - scale2 * db2 * inv_n)

    @pl.loop(0, sub // TILE)
    def _(t):
        n = lanes_at(t, TILE)
        for i in range(0, hid, 64):
            rows = pl.ds(i, 64)
            v = dn2[rows, n] * spread(cols[0, rows, :], TILE)
            v = v + mixed[rows, n] * spread(cols[1, rows, :], TILE) + spread(cols[2, rows, :], TILE)
            dmx[rows, n] = v.astype(BF16)

    mine = lanes_at(c, half)
    theirs = lanes_at(1 - c, half)

    def pair_copy(d):
        return rc(dmp.at[d, theirs, :], pr.at[d], "pair", d, h, sib)

    qrows = half // S
    zown = pl.ds(pl.multiple_of(c * half + zpar * qrows, 16), qrows)
    zother = pl.ds(pl.multiple_of(c * half + (1 - zpar) * qrows, 16), qrows)

    def z1_copy(d):
        return rc(dmp.at[d, zother, :], z1r.at[d], "z1", d, h, 2 * zmate + c)

    def z1_start(d):
        if S > 1:
            z1_copy(d).start()

    def z1_sum(d):
        if S > 1:
            done(z1_copy(d))
            dmp[d, zown, :] = (dmp[d, zown, :].astype(F32) + z1r[d].astype(F32)).astype(BF16)

    def hop_copy(d):
        return rc(dmp.at[d, zown, :], hr.at[d], "hop", d, peer(d), r)

    def pair_sum(d):
        done(pair_copy(d))
        dmp[d, mine, :] = (dmp[d, mine, :].astype(F32) + pr[d].astype(F32)).astype(BF16)

    @pl.loop(0, HOPS)
    def _(i):
        d = HOPS - 1 - i

        @pl.loop(0, 2)
        def _(j):
            rows = lanes_at(j, half)
            dmp[d, rows, :] = dot_nt(mi[d, rows, :], dmx[...]).astype(BF16)

        pair_copy(d).start()

        @pl.when(i > 0)
        def _():
            pair_sum(d + 1)
            z1_start(d + 1)

        @pl.when(i > 1)
        def _():
            z1_sum(d + 2)
            hop_copy(d + 2).start()

    G2 = Z // S
    zq = lax.div(zi, S)

    def zr_copy(e, which):
        rows, lanes = chunk(0, which, qrows, G2, hid)
        return rc(hr.at[0, rows, lanes], zr.at[e], "zr", e, h, (lax.rem(zq + e, G2) * S + zpar) * 2 + c)

    def final_chunk(z):
        return chunk(c * half + lax.rem(z, S) * qrows, lax.div(z, S), qrows, G2, hid)

    def zg_copy(e, which):
        rows, lanes = final_chunk(which)
        ref = fin.at[rows, lanes]
        return rc(ref, ref, "zg", e, h, lax.rem(zi + e, Z) * 2 + c)

    def ddm_copy(core):
        ref = fin.at[lanes_at(core, half), :]
        return rc(ref, ref, "ddm", 0, h, sib)

    def d_copy(d):
        return rc(dsend.at[d], o_d.at[h], "d", d, peer(d), r)

    def dt_copy(d):
        return rc(dtail.at[d], o_dt.at[h], "dt", d, peer(d), r)

    def p_copy(d):
        return rc(ps.at[d], prv.at[d], "p", d, peer(d), r)

    def q_copy(d):
        return rc(qs.at[d], qv.at[d], "q", d, peer(d), r)

    @pl.loop(0, HOPS * NT)
    def _(it):
        dd = lax.div(it, NT)
        t = lax.rem(it, NT)
        d = HOPS - 1 - dd

        @pl.when(t == 0)
        def _():
            pT[...] = jnp.zeros(pT.shape, F32)

        @pl.when(it == NT // 2)
        def _():
            pair_sum(0)
            z1_start(0)
            z1_sum(1)
            hop_copy(1).start()

        @pl.when(it == NT + NT // 2)
        def _():
            for j in range(1, HOPS):
                done(cwh_copy(j))
            cwr[r] = cwp[0] + (cwh[1] + cwh[2] + cwh[3])
            rows_start(cwr, "cwr")
            z1_sum(0)

        @pl.when(it == 2 * NT + NT // 2)
        def _():
            for j in range(1, HOPS):
                done(hop_copy(j))
            hsum = dmp[0, zown, :].astype(F32) + hr[1].astype(F32) + hr[2].astype(F32) + hr[3].astype(F32)
            hr[0] = hsum.astype(BF16)

            @functools.partial(each, 1, G2)
            def _(e):
                zr_copy(e, lax.rem(zq + e, G2)).start()

            rows_wait(cwr, "cwr")
            cwg[h] = total(cwr, R)
            hops_start(cwg, "cwg")

        @pl.when(it == 3 * NT + NT // 2)
        def _():
            @functools.partial(each, 1, G2)
            def _(e):
                done(zr_copy(e, lax.rem(zq + e, G2)))

            rows, lanes = chunk(0, zq, qrows, G2, hid)
            zt = hr[0, rows, lanes].astype(F32)
            for e in range(1, G2):
                zt = zt + zr[e].astype(F32)
            frows, flanes = final_chunk(zi)
            fin[frows, flanes] = zt.astype(BF16)

            @functools.partial(each, 1, Z)
            def _(e):
                zg_copy(e, zi).start()

            hops_wait(cwg, "cwg")
            for j in range(HOPS):
                o_cw[:, pl.ds(j * q, q)] = cwg[j]

        ns = [lanes_at(t * UN + u, TILE) for u in range(UN)]
        dcs = [dot(wmx[d], dmx[:, n]) for n in ns]
        for u, n in enumerate(ns):
            dn = jnp.concatenate(
                [dcs[u][i : i + 64].astype(BF16) * gp[d, pl.ds(i, 64), n] for i in range(0, hid, 64)], axis=0
            )
            pT[...] += dot_nt(dn, fx[d, :, n])
            grad = dot(aw[d], dn)
            dsend[d, :, n] = grad[:MAIN].astype(BF16)
            d4[:, n] = grad[MAIN : MAIN + 8]

        @pl.when(t == NT - 1)
        def _():
            pw = pT[...].T * KAPPA
            qs[d, :, pl.ds(0, hid)] = jnp.sum(pw * wall[d, wrow, :].astype(F32), axis=0, keepdims=True)
            qs[d, :, pl.ds(hid, hid)] = pw[ONES : ONES + 1, :]
            ps[d] = pw.astype(BF16)
            pack4(d4, dtail.at[d])

            @pl.when(dd < HOPS - 1)
            def _():
                q_copy(d).start()
                p_copy(d).start()
                d_copy(d).start()
                dt_copy(d).start()

    for d in range(1, HOPS):
        done(q_copy(d))
    qr[r] = qs[0] + (qv[1] + qv[2] + qv[3])
    rows_start(qr, "qr")
    own_d = pltpu.make_async_copy(dsend.at[0], o_d.at[h], ss.at[names["d"]])
    own_d.start()
    own_dt = pltpu.make_async_copy(dtail.at[0], o_dt.at[h], ss.at[names["dt"]])
    own_dt.start()

    for d in range(1, HOPS):
        done(p_copy(d))
    psum[...] = (
        ps[0].astype(F32) + (prv[1].astype(F32) + prv[2].astype(F32) + prv[3].astype(F32))
    ).astype(BF16)
    owners = min(R, 32)

    def if_owner(who, body):
        if owners == R:
            body()
        else:
            pl.when(who < owners)(body)

    def prs_copy(e, to, slot):
        rows, lanes = chunk(0, to, 128, owners, hid)
        return rc(psum.at[rows, lanes], prs.at[slot], "prs", e, h, lax.rem(r + e, R))

    def pag_copy(e, who):
        rows, lanes = chunk(0, who, 128, owners, hid)
        return rc(pfin.at[rows, lanes], pfin.at[rows, lanes], "pag", e, h, lax.rem(r + e, R))

    @functools.partial(each, 1, R)
    def _(e):
        to = lax.rem(r + e, R)
        if_owner(to, lambda: prs_copy(e, to, r).start())

    @functools.partial(each, 1, Z)
    def _(e):
        zg_copy(e, zi).wait_send()
        zg_copy(e, lax.rem(zi + Z - e, Z)).wait_recv()

    ddm_copy(c).start()

    rows_wait(qr, "qr")
    qt = total(qr, R)
    db = qt[:, hid:]
    dgn = inv * (qt[:, :hid] - mean * db)
    o_small[pl.ds(2, 1), :] = dgn
    o_small[pl.ds(3, 1), :] = db
    c1 = scale * db * inv_n
    c2 = inv * scale * dgn * inv_n
    shift = c1 - mean * c2
    row = lax.broadcasted_iota(jnp.int32, (128, hid), 0)
    q1, q2 = split2(jnp.where(row == ONES, shift, wown32 * c2))
    o_m[...] = (dot_nt(wown, q1) + dot_nt(wown, q2))[:FP]
    rows_wait(gbuf, "gr")
    g1, g2, g3 = split3(total(gbuf, R))
    gq = dot(g1, q1) + dot(g2, q1) + dot(g3, q1) + dot(g1, q2) + dot(g2, q2)

    @functools.partial(each, 1, R)
    def _(e):
        to = lax.rem(r + e, R)
        src = lax.rem(r + R - e, R)
        if_owner(to, lambda: prs_copy(e, to, r).wait_send())
        if_owner(r, lambda: prs_copy(e, r, src).wait_recv())

    def gather():
        rows, lanes = chunk(0, r, 128, owners, hid)
        prs[r] = psum[rows, lanes]
        pt = prs[0].astype(F32)
        for j in range(1, R):
            pt = pt + prs[j].astype(F32)
        pfin[rows, lanes] = pt.astype(BF16)

        @functools.partial(each, 1, R)
        def _(e):
            pag_copy(e, r).start()

    if_owner(r, gather)
    ddm_copy(c).wait_send()
    ddm_copy(1 - c).wait_recv()
    o_mix[...] = fin[...]

    @functools.partial(each, 1, R)
    def _(e):
        src = lax.rem(r + R - e, R)
        if_owner(r, lambda: pag_copy(e, r).wait_send())
        if_owner(src, lambda: pag_copy(e, src).wait_recv())

    o_gw[...] = pfin[pl.ds(0, FP), :].astype(F32) * scale - gq
    own_d.wait()
    own_dt.wait()
    own_lp.wait()
    for d in range(1, HOPS):
        done(d_copy(d))
        done(dt_copy(d))
        done(lp_copy(d, 0))
        done(lp_copy(d, 1))


def last_kernel(
    nodes,
    ft, d, dt, lp, m, mix, gw, small, cw,
    o_lp, o_gf, o_mix, o_gw, o_gg, o_gb, o_hg, o_hb, o_cw, o_cb, o_loss, low,
):
    feat, n = ft.shape
    ncls = o_lp.shape[0]
    o_lp[...] = lp[...].astype(F32)[:ncls]
    mm = m[...]
    f = ft[...]
    fix = dot(mm[:, :feat].astype(BF16), f) + mm[:, ONES : ONES + 1]
    tail = dt[0].astype(F32)
    for b in range(4):
        low[pl.ds(0, 4), pl.ds(b * (n // 4), n // 4)] = tail[4 * b : 4 * b + 4]
    gf = jnp.concatenate([d[0].astype(F32), low[...]], axis=0)[:feat] - fix[:feat]
    if STRIDED:
        flat = o_gf.reshape(feat * (n // 128), 128)
        for i in range(n // 128):
            flat[pl.ds(i, feat, stride=n // 128), :] = gf[:, i * 128 : (i + 1) * 128]
    else:
        for i in range(n // 128):
            o_gf[:, i, :] = gf[:, i * 128 : (i + 1) * 128]

    @pl.when(pl.program_id(0) == 0)
    def _():
        hid = mix.shape[1]
        o_mix[...] = mix[...].astype(F32)
        for i in range(hid // 128):
            o_gw[:, i, :] = gw[pl.ds(0, feat), pl.ds(i * 128, 128)]
        o_hg[...] = small[pl.ds(0, 1), :]
        o_hb[...] = small[pl.ds(1, 1), :]
        o_gg[...] = small[pl.ds(2, 1), :]
        o_gb[...] = small[pl.ds(3, 1), :]
        o_cw[...] = cw[pl.ds(0, ncls), :]
        o_cb[...] = small[pl.ds(4, 1), pl.ds(0, ncls)]
        o_loss[...] = jnp.sum(small[pl.ds(4, 1), pl.ds(128, 128)], axis=1, keepdims=True) * (-1.0 / nodes)


def shards(
    R, features, branch_weight, branch_gain, branch_bias, mix_weight, mixing_norm_gain, mixing_norm_bias,
    class_weight, class_bias, labels, hop_mask,
):
    local, feat = features.shape[1:]
    hid = mix_weight.shape[0]
    ncls = class_weight.shape[1]
    nodes = local * R
    sub = local // HOPS
    Z = R // 2
    half = hid // 2
    S = min(Z, 2)
    G2, qrows = Z // S, half // S
    zrows, zcols = chunk(0, 0, qrows, G2, hid)
    prows, pcols = chunk(0, 0, 128, min(R, 32), hid)
    assert feat == ONES and ncls == 47 and local // hop_mask.shape[0] == 128
    ft = features[0].T
    sd = jax.ShapeDtypeStruct
    vm = pl.BlockSpec(memory_space=pltpu.VMEM)
    hbm = pl.BlockSpec(memory_space=pl.ANY)
    _, nsem = sem_plan(R)
    V = pltpu.VMEM
    outs = pl.pallas_call(
        functools.partial(main_kernel, R, nodes),
        grid=(1,),
        out_shape=(
            sd((48, local), BF16),
            sd((HOPS, MAIN, sub), BF16),
            sd((HOPS, 16, sub // 4), BF16),
            sd((FP, 128), F32),
            sd((hid, hid), BF16),
            sd((FP, hid), F32),
            sd((8, hid), F32),
            sd((48, hid), F32),
        ),
        in_specs=[hbm, pl.BlockSpec((16, local), lambda i: (MAIN // 16, 0))]
        + [vm] * 9
        + [pl.BlockSpec(memory_space=pltpu.SMEM)],
        out_specs=(hbm, hbm, hbm, vm, vm, vm, vm, vm),
        scratch_shapes=[
            V((128, local), BF16),
            V((HOPS, 128, sub), BF16),
            V((HOPS, 16, sub // 4), BF16),
            V((HOPS, 16, sub // 4), BF16),
            V((48, sub // 4), F32),
            V((HOPS, hid + 128, hid), BF16),
            V((HOPS, hid, 256), BF16),
            V((HOPS, FP, hid), BF16),
            V((HOPS, hid, hid), BF16),
            V((HOPS, 16, sub), BF16),
            V((HOPS, hid, sub), BF16),
            V((HOPS, hid, sub), BF16),
            V((hid, sub), F32),
            V((hid, sub), F32),
            V((hid, sub), BF16),
            V((R, FP, 128), F32),
            V((R, 1, 2 * hid), F32),
            V((HOPS, 1, 2 * hid), F32),
            V((HOPS * R, 1, 2 * hid), F32),
            V((HOPS * R, 1, 2 * hid + 256), F32),
            V((HOPS, 48, hid // HOPS), F32),
            V((HOPS, 48, hid // HOPS), F32),
            V((R, 48, hid // HOPS), F32),
            V((HOPS, 48, hid // HOPS), F32),
            V((48, sub), BF16),
            V((128, hid), F32),
            V((8, 128), F32),
            V((hid, 128), F32),
            V((hid, 128), F32),
            V((96, 128), F32),
            V((48, hid), F32),
            V((3, hid, 128), F32),
            V((HOPS, hid, hid), BF16),
            V((HOPS, half, hid), BF16),
            V((HOPS, qrows, hid), BF16),
            V((HOPS, qrows, hid), BF16),
            V((max(G2, 2), zrows.size, zcols.size), BF16),
            V((hid, hid), BF16),
            V((HOPS, MAIN, sub), BF16),
            V((8, sub), F32),
            V((HOPS, 16, sub // 4), BF16),
            V((hid, 128), F32),
            V((HOPS, 128, hid), BF16),
            V((HOPS, 128, hid), BF16),
            V((HOPS, 1, 2 * hid), F32),
            V((HOPS, 1, 2 * hid), F32),
            V((R, 1, 2 * hid), F32),
            V((R, prows.size, pcols.size), BF16),
            V((128, hid), BF16),
            V((128, hid), BF16),
            pltpu.SemaphoreType.DMA((nsem,)),
            pltpu.SemaphoreType.DMA((nsem,)),
        ],
        compiler_params=pltpu.CompilerParams(
            collective_id=0, has_side_effects=True, vmem_limit_bytes=63 * 1024 * 1024
        ),
        cost_estimate=pl.CostEstimate(flops=2 * 8 * 10**9, bytes_accessed=10**7, transcendentals=10**7),
        name="main",
    )(
        ft, ft, branch_weight[0], branch_gain, branch_bias, mix_weight, mixing_norm_gain[None], mixing_norm_bias[None],
        class_weight.T, class_bias[None], labels[None], hop_mask.T,
    )
    lp, dd, dt, m, mix, gw, small, cw = outs
    nb = sub
    whole = lambda shape: pl.BlockSpec(shape, lambda i: (0,) * len(shape))
    lp, gf, mix, gw, gg, gb, hg, hb, cw, cb, loss = pl.pallas_call(
        functools.partial(last_kernel, nodes),
        grid=(local // nb,),
        out_shape=(
            sd((ncls, local), F32),
            sd((feat, local // 128, 128), F32),
            sd((hid, hid), F32),
            sd((feat, hid // 128, 128), F32),
            sd((1, hid), F32),
            sd((1, hid), F32),
            sd((1, hid), F32),
            sd((1, hid), F32),
            sd((ncls, hid), F32),
            sd((1, ncls), F32),
            sd((1, 1), F32),
        ),
        in_specs=[
            pl.BlockSpec((feat, nb), lambda i: (0, i)),
            pl.BlockSpec((1, MAIN, nb), lambda i: (i, 0, 0)),
            pl.BlockSpec((1, 16, nb // 4), lambda i: (i, 0, 0)),
            pl.BlockSpec((48, nb), lambda i: (0, i)),
            whole((FP, 128)),
            whole((hid, hid)),
            whole((FP, hid)),
            whole((8, hid)),
            whole((48, hid)),
        ],
        out_specs=(
            pl.BlockSpec((ncls, nb), lambda i: (0, i)),
            pl.BlockSpec((feat, nb // 128, 128), lambda i: (0, i, 0)),
            whole((hid, hid)),
            whole((feat, hid // 128, 128)),
            whole((1, hid)),
            whole((1, hid)),
            whole((1, hid)),
            whole((1, hid)),
            whole((ncls, hid)),
            whole((1, ncls)),
            whole((1, 1)),
        ),
        scratch_shapes=[V((8, nb), F32)],
        compiler_params=pltpu.CompilerParams(vmem_limit_bytes=60 * 1024 * 1024),
        name="last",
    )(ft, dd, dt, lp, m, mix, gw, small, cw)
    return (
        lp.T,
        loss[0, 0],
        with_layout_constraint(gf.reshape(feat, 1, local), Layout((0, 1, 2))).transpose(1, 2, 0),
        gw.reshape(1, feat, hid),
        gg,
        gb,
        mix,
        hg[0],
        hb[0],
        cw.T,
        cb[0],
    )


def solution(mesh):
    placed = (
        P("hop", "rows", None), P("hop", None, None), P("hop", None), P("hop", None), P("hop", None),
        P(), P(), P(), P(), P("rows"), P("rows", None),
    )
    assert mesh.shape["hop"] == HOPS
    return jax.shard_map(
        functools.partial(shards, mesh.shape["rows"]),
        mesh=mesh,
        in_specs=placed,
        out_specs=(
            P("rows", None), P(), P("hop", "rows", None), P("hop", None, None), P("hop", None), P("hop", None),
            P("hop", None), P(), P(), P(), P(),
        ),
        check_vma=False,
    )
```

```python
import functools
import math

import jax
import jax.numpy as jnp
from jax import lax
from jax.experimental import pallas as pl
from jax.experimental.layout import Layout, with_layout_constraint
from jax.experimental.pallas import tpu as pltpu
from jax.sharding import PartitionSpec as P

MESH = pl.DeviceIdType.MESH
EPS = 1e-05
HOPS = 4
ONES = 100
FP = 112
MAIN = 96
TILE = 256
STRIDED = True
C0 = math.sqrt(2.0 / math.pi)
C1 = C0 * 0.044715
KAPPA = C1 ** (1.0 / 3.0)
ALPHA = C0 / KAPPA
F32 = jnp.float32
BF16 = jnp.bfloat16


def dot(a, b):
    return lax.dot_general(a, b, (((1,), (0,)), ((), ())), preferred_element_type=F32)


def dot_nt(a, b):
    return lax.dot_general(a, b, (((1,), (1,)), ((), ())), preferred_element_type=F32)


def split2(x):
    hi = x.astype(BF16)
    return hi, (x - hi.astype(F32)).astype(BF16)


def split3(x):
    hi = x.astype(BF16)
    rest = x - hi.astype(F32)
    mid = rest.astype(BF16)
    return hi, mid, (rest - mid.astype(F32)).astype(BF16)


def gelu_slope(z):
    u = z * z
    t = jnp.tanh(z * (C0 + C1 * u))
    s = 0.5 * t + 0.5
    g = z * s
    return g, s + (g - g * s) * (2.0 * C0 + 6.0 * C1 * u)


def scaled_gelu_slope(y):
    u = y * y
    t = jnp.tanh(y * (u + ALPHA))
    up = t + 1.0
    g = y * up
    return g, up + (g * (1.0 - t)) * (3.0 * u + ALPHA)


def fold(x):
    total = x[:, :128]
    for i in range(1, x.shape[1] // 128):
        total = total + x[:, i * 128 : (i + 1) * 128]
    return total


def spread(c, n):
    return jnp.concatenate([c] * (n // 128), axis=1)


def row_of(acc):
    return jnp.sum(acc.T, axis=0, keepdims=True)


def col_of(row):
    return jnp.broadcast_to(row, (128, row.shape[1])).T


def each(lo, hi, body):
    if hi - lo == 1:
        body(lo)
    elif hi > lo:
        pl.loop(lo, hi)(body)


class Alloc:
    def __init__(self):
        self.n = 0

    def __call__(self, count):
        base = self.n
        self.n += count
        return base


def sem_plan(R):
    Z = R // 2
    a = Alloc()
    names = {}
    for name, count in (
        ("feat", 4), ("ft", 4), ("loc", 1), ("ws", 4), ("zf", 4), ("dd", 4), ("s1", R), ("ab", 4), ("gr", R),
        ("s2", HOPS * R), ("s3", HOPS * R), ("lp", 8), ("cwh", 4), ("cwr", R), ("cwg", 4),
        ("pair", 4), ("z1", 4), ("hop", 4), ("zr", Z), ("zg", Z), ("ddm", 1), ("d", 4), ("dt", 4), ("p", 4), ("q", 4),
        ("qr", R), ("prs", R), ("pag", R),
    ):
        names[name] = a(count)
    return names, a.n


def chunk(base, i, rows, pieces, cols):
    if rows // pieces >= 16:
        take = rows // pieces
        return pl.ds(pl.multiple_of(base + i * take, 16), take), pl.ds(0, cols)
    m = 16 * pieces // rows
    wide = cols // m
    return (
        pl.ds(pl.multiple_of(base + (i // m) * 16, 16), 16),
        pl.ds(pl.multiple_of((i % m) * wide, 128), wide),
    )


def main_kernel(
    R,
    nodes,
    ft, ft4, wb, bgain, bbias, wm, gain2, bias2, wc, cb, lab, msk,
    o_lp, o_d, o_dt, o_m, o_mix, o_gw, o_small, o_cw,
    fs, fx, ftail, frt, st4, wall, wl, aw, wmx, keep, mi, gp, mixed, dn2, dmx,
    gbuf, s1, ab, s2, s3, cwp, cwh, cwr, cwg, lps,
    wcs, wcNs, cbs, hb, dlp, acc0, acc1, accl, accw, cols,
    dmp, pr, z1r, hr, zr, fin, dsend, d4, dtail, pT, ps, prv, qs, qv, qr, prs, psum, pfin,
    ss, rs,
):
    names, _ = sem_plan(R)
    Z = R // 2
    h = lax.axis_index("hop")
    r = lax.axis_index("rows")
    c = lax.rem(r, 2)
    zi = lax.div(r, 2)
    sib = r + 1 - 2 * c
    local = ft.shape[1]
    sub = local // HOPS
    hid = wm.shape[0]
    half = hid // 2
    big = min(2 * TILE, sub)
    UN = big // TILE
    NT = sub // big
    inv_n = 1.0 / nodes

    def peer(d):
        x = lax.rem(h + d, 2)
        y = lax.rem(lax.div(h, 2) + lax.div(d, 2), 2)
        return 2 * y + x

    def rc(src, dst, name, i, hh, rr):
        return pltpu.make_async_remote_copy(
            src_ref=src, dst_ref=dst, send_sem=ss.at[names[name] + i], recv_sem=rs.at[names[name] + i],
            device_id=(hh, rr), device_id_type=MESH,
        )

    def done(cp):
        cp.wait_send()
        cp.wait_recv()

    def lanes_at(i, n):
        return pl.ds(pl.multiple_of(i * n, n), n)

    barrier = pltpu.get_barrier_semaphore()

    def greet(hh, rr):
        pl.semaphore_signal(barrier, inc=1, device_id=(hh, rr), device_id_type=MESH)

    D = HOPS * R
    me = h * R + r

    @functools.partial(each, 1, D)
    def _(e):
        other = lax.rem(me + e, D)
        greet(lax.div(other, R), lax.rem(other, R))

    def all_start(buf, name):
        @functools.partial(each, 1, D)
        def _(e):
            other = lax.rem(me + e, D)
            rc(buf.at[me], buf.at[me], name, e, lax.div(other, R), lax.rem(other, R)).start()

    def all_wait(buf, name):
        @functools.partial(each, 1, D)
        def _(e):
            other = lax.rem(me + D - e, D)
            done(rc(buf.at[other], buf.at[other], name, e, lax.div(other, R), lax.rem(other, R)))

    def rows_start(buf, name):
        @functools.partial(each, 1, R)
        def _(e):
            rc(buf.at[r], buf.at[r], name, e, h, lax.rem(r + e, R)).start()

    def rows_wait(buf, name):
        @functools.partial(each, 1, R)
        def _(e):
            src = lax.rem(r + R - e, R)
            done(rc(buf.at[src], buf.at[src], name, e, h, lax.rem(r + e, R)))

    def hops_start(buf, name):
        @pl.loop(1, HOPS)
        def _(d):
            rc(buf.at[h], buf.at[h], name, d, peer(d), r).start()

    def hops_wait(buf, name):
        @pl.loop(1, HOPS)
        def _(d):
            done(rc(buf.at[peer(d)], buf.at[peer(d)], name, d, peer(d), r))

    def total(buf, n):
        return lax.fori_loop(1, n, lambda i, t: t + buf[i], buf[0])

    loc = pltpu.make_async_copy(ft.at[pl.ds(0, MAIN), :], fs.at[pl.ds(0, MAIN), :], ss.at[names["loc"]])
    loc.start()

    def pack4(src, dst):
        n = st4.shape[1]
        for b in range(4):
            st4[pl.ds(4 * b, 4), :] = src[pl.ds(0, 4), pl.ds(b * n, n)].astype(F32)
        dst[...] = st4[pl.ds(0, 16), :].astype(BF16)

    def unpack4(src, dst):
        n = st4.shape[1]
        row = lax.broadcasted_iota(jnp.int32, (32, n), 0)
        st4[pl.ds(0, 16), :] = src[...].astype(F32)
        st4[pl.ds(16, 32), :] = jnp.where(row == ONES - MAIN, 1.0, 0.0)
        for b in range(4):
            st4[pl.ds(16, 4), :] = st4[pl.ds(4 * b, 4), :]
            dst[pl.ds(MAIN, 32), pl.ds(b * n, n)] = st4[pl.ds(16, 32), :].astype(BF16)

    wrow = pl.ds(hid, 128)
    wall[0, pl.ds(hid + 96, 32), :] = jnp.zeros((32, hid), BF16)
    wall[0, pl.ds(hid, 100), :] = wb[...]

    @pl.loop(0, hid // 128)
    def _(i):
        k = lanes_at(i, 128)
        wall[0, pl.ds(0, hid), k] = wm[k, :].astype(F32).T.astype(BF16)

    def feat_copy(d):
        rows = pl.ds(0, MAIN)
        return rc(ft.at[rows, lanes_at(peer(d), sub)], fx.at[d, rows, :], "feat", d, peer(d), r)

    def ft_copy(d):
        return rc(ftail.at[peer(d)], frt.at[d], "ft", d, peer(d), r)

    pl.semaphore_wait(barrier, D - 1)

    S = min(Z, 2)
    part = (hid + 128) // (2 * S)
    zpar = lax.rem(zi, S)
    zmate = zi + (S - 1) - 2 * (S - 1) * zpar

    def part_rows(core, par):
        return pl.ds(pl.multiple_of((core * S + par) * part, 16), part)

    def ws_copy(d):
        rows = part_rows(c, zpar)
        return rc(wall.at[0, rows, :], wall.at[d, rows, :], "ws", d, peer(d), r)

    def zf_copy(d, par):
        ref = wall.at[d, part_rows(c, par), :]
        return rc(ref, ref, "zf", d, h, 2 * zmate + c)

    def dd_copy(d, core):
        ref = wall.at[d, pl.ds(pl.multiple_of(core * S * part, 16), S * part), :]
        return rc(ref, ref, "dd", d, h, sib)

    @pl.loop(1, HOPS)
    def _(d):
        ws_copy(d).start()

    @pl.loop(1, HOPS - 1)
    def _(d):
        feat_copy(d).start()

    @pl.loop(0, HOPS)
    def _(j):
        lanes = lanes_at(j, sub)
        pack4(ft4.at[:, lanes], ftail.at[j])
        unpack4(ftail.at[j], fs.at[:, lanes])

    @pl.loop(1, HOPS)
    def _(d):
        ft_copy(d).start()

    loc.wait()
    fx0 = pltpu.make_async_copy(fs.at[:, lanes_at(h, sub)], fx.at[0], ss.at[names["loc"]])
    fx0.start()

    def gram(i, g):
        f = fs[:, lanes_at(i, sub)]
        return g + dot_nt(f, f)

    g = lax.fori_loop(0, HOPS, gram, jnp.zeros((128, 128), F32))
    wown = wall[0, wrow, :]
    wown32 = wown.astype(F32)
    g1, g2, g3 = split3(g)
    gw = dot(g1, wown) + dot(g2, wown) + dot(g3, wown)
    s1[r, :, pl.ds(0, hid)] = gw[ONES : ONES + 1, :]
    s1[r, :, pl.ds(hid, hid)] = jnp.sum(gw * wown32, axis=0, keepdims=True)
    rows_start(s1, "s1")
    gbuf[r] = g[:FP]

    @pl.loop(0, HOPS * (sub // 128))
    def _(i):
        d = lax.div(i, sub // 128)
        b = lax.rem(i, sub // 128)
        late = peer(d) - 2
        m = jnp.where(late >= 0, msk[jnp.maximum(late, 0), h * (sub // 128) + b], 1)
        keep[d, :, lanes_at(b, 128)] = jnp.full((16, 128), 0.5 * m.astype(F32)).astype(BF16)

    wcs[...] = jnp.zeros(wcs.shape, F32)
    wcs[pl.ds(0, wc.shape[0]), :] = wc[...].astype(F32)
    cbs[...] = jnp.zeros(cbs.shape, F32)
    cbs[pl.ds(0, 1), pl.ds(0, cb.shape[1])] = cb[...]
    ncls = wc.shape[0]

    @pl.loop(0, hid // 16)
    def _(i):
        rows = lanes_at(i, 16)
        mixed[rows, :] = jnp.zeros((16, sub), F32)
        mi[0, rows, pl.ds(0, big)] = jnp.zeros((16, big), BF16)

    fx0.wait()

    rows_wait(s1, "s1")
    st = total(s1, R)
    mean = st[:, :hid] * inv_n
    var = st[:, hid:] * inv_n - mean * mean
    inv = lax.rsqrt(var + EPS)
    scale = inv * bgain[...]
    ab[0, :, pl.ds(0, hid)] = scale
    ab[0, :, pl.ds(hid, hid)] = bbias[...] - mean * scale

    def ab_copy(d):
        return rc(ab.at[0], ab.at[d], "ab", d, peer(d), r)

    @pl.loop(1, HOPS)
    def _(d):
        ab_copy(d).start()

    def prepare(d):
        a = ab[d, :, pl.ds(0, hid)]
        b = ab[d, :, pl.ds(hid, hid)]
        ws = wall[d, wrow, :].astype(F32) * (a * KAPPA)
        aw[d] = ws[:FP].astype(BF16)
        row = lax.broadcasted_iota(jnp.int32, (128, hid), 0)
        wt = jnp.where(row == ONES, b * KAPPA, ws).T
        hi, lo = split2(wt)
        wl[d, :, pl.ds(0, 128)] = hi
        wl[d, :, pl.ds(128, 128)] = lo

    @pl.loop(0, HOPS * NT)
    def _(it):
        d = lax.div(it, NT)
        t = lax.rem(it, NT)

        @pl.when(t == 0)
        def _():
            @pl.when(d > 0)
            def _():
                done(feat_copy(d))
                done(ft_copy(d))
                unpack4(frt.at[d], fx.at[d])
                dd_copy(d, c).wait_send()
                dd_copy(d, 1 - c).wait_recv()
                done(ab_copy(d))

            prepare(d)

        if S > 1:

            @pl.when(it == min(1, NT - 1))
            def _():
                @pl.loop(1, HOPS)
                def _(j):
                    done(ws_copy(j))
                    zf_copy(j, zpar).start()

        @pl.when(it == min(2, NT - 1))
        def _():
            feat_copy(HOPS - 1).start()

        @pl.when(jnp.logical_and(t == NT - 1, d < HOPS - 1))
        def _():
            if S > 1:
                zf_copy(d + 1, zpar).wait_send()
                zf_copy(d + 1, 1 - zpar).wait_recv()
            else:
                done(ws_copy(d + 1))
            dd_copy(d + 1, c).start()

        @pl.when(it == 2 * NT)
        def _():
            rows_start(gbuf, "gr")

        pit = jnp.maximum(it - 1, 0)
        pd = lax.div(pit, NT)
        pt = lax.rem(pit, NT)
        adds = []
        for u in range(UN):
            adds.append(dot(wall[pd, pl.ds(0, hid), :], mi[pd, :, lanes_at(pt * UN + u, TILE)]))
        for u in range(UN):
            n = lanes_at(t * UN + u, TILE)
            f = fx[d, :, n]
            z = dot(wl[d], jnp.concatenate([f, f], axis=0))
            k = keep[d, :, n]
            k = jnp.concatenate([k] * 4, axis=0)
            for i in range(0, hid, 64):
                g1, d1 = scaled_gelu_slope(z[i : i + 64].astype(BF16))
                g2, d2 = scaled_gelu_slope(g1 * k)
                mi[d, pl.ds(i, 64), n] = g2
                gp[d, pl.ds(i, 64), n] = d1 * d2 * k
        for u in range(UN):
            n = lanes_at(pt * UN + u, TILE)
            mixed[:, n] = mixed[:, n] + adds[u]

    acc0[...] = jnp.zeros(acc0.shape, F32)
    acc1[...] = jnp.zeros(acc1.shape, F32)

    @pl.loop(0, UN)
    def _(u):
        n = lanes_at((NT - 1) * UN + u, TILE)
        mixed[:, n] = mixed[:, n] + dot(wall[HOPS - 1, pl.ds(0, hid), :], mi[HOPS - 1, :, n])

    @pl.loop(0, hid // 32)
    def _(i):
        rows = lanes_at(i, 32)
        x = mixed[rows, :]
        acc0[rows, :] = fold(x)
        acc1[rows, :] = fold(x * x)

    s2[me, :, pl.ds(0, hid)] = row_of(acc0[...])
    s2[me, :, pl.ds(hid, hid)] = row_of(acc1[...])
    all_start(s2, "s2")

    @pl.loop(0, HOPS * (hid // 128))
    def _(i):
        d = lax.div(i, hid // 128)
        k = lanes_at(lax.rem(i, hid // 128), 128)
        wmx[d, k, :] = wall[d, pl.ds(0, hid), k].astype(F32).T.astype(BF16)

    wc48 = wcs[pl.ds(0, 48), :].astype(BF16)
    wcNs[...] = wcs[...].T.astype(BF16)
    crow = lax.broadcasted_iota(jnp.int32, (128, 128), 0)
    cbc = jnp.where(crow < ncls, jnp.broadcast_to(cbs[pl.ds(0, 1), :], (128, 128)).T, -1e30)[:48]
    all_wait(s2, "s2")
    st2 = total(s2, D)
    mean2 = st2[:, :hid] * inv_n
    inv2 = lax.rsqrt(st2[:, hid:] * inv_n - mean2 * mean2 + EPS * 4.0 * KAPPA * KAPPA)
    scale2 = inv2 * gain2[...]
    cols[0] = col_of(scale2)
    cols[1] = col_of(bias2[...] - mean2 * scale2)
    acc0[...] = jnp.zeros(acc0.shape, F32)
    acc1[...] = jnp.zeros(acc1.shape, F32)
    accl[...] = jnp.zeros(accl.shape, F32)
    accw[...] = jnp.zeros(accw.shape, F32)

    o_own = lanes_at(h, sub)

    def lp_copy(d, part):
        n = sub // 2
        return rc(
            lps.at[:, pl.ds(part * n, n)], o_lp.at[:, lanes_at(2 * h + part, n)], "lp", 4 * part + d, peer(d), r
        )

    dlp[...] = jnp.zeros(dlp.shape, BF16)
    HR = 128

    @pl.loop(0, NT)
    def _(t):
        n = lanes_at(t, big)

        if NT > 1:

            @pl.when(t == NT // 2)
            def _():
                @pl.loop(1, HOPS)
                def _(d):
                    lp_copy(d, 0).start()

        @pl.loop(0, hid // HR)
        def _(i):
            rows = lanes_at(i, HR)
            z2 = mixed[rows, n] * spread(cols[0, rows, :], big) + spread(cols[1, rows, :], big)
            gv, dg = gelu_slope(z2)
            hb[rows, :] = gv.astype(BF16)
            dn2[rows, n] = dg

        lg = dot(wc48, hb[...]) + spread(cbc, big)
        lg = lg - jnp.max(lg, axis=0, keepdims=True)
        ex = jnp.exp(lg)
        se = jnp.sum(ex, axis=0, keepdims=True)
        lp = lg - jnp.log(se)
        lps[:, n] = lp.astype(BF16)
        own = lanes_at(h * NT + t, big)
        hit = lax.broadcasted_iota(jnp.int32, (48, big), 0) == lab[:, own]
        accl[pl.ds(48, 48), :] += fold(jnp.where(hit, lp, 0.0))
        dl = ((ex / se - jnp.where(hit, 1.0, 0.0)) * inv_n).astype(BF16)
        accl[pl.ds(0, 48), :] += fold(dl.astype(F32))
        accw[...] += dot_nt(dl, hb[...])
        dlp[pl.ds(0, 48), :] = dl

        @pl.loop(0, hid // HR)
        def _(i):
            rows = lanes_at(i, HR)
            dn = dot(wcNs[rows, :], dlp[...]) * dn2[rows, n]
            dn2[rows, n] = dn
            acc0[rows, :] += fold(dn * mixed[rows, n])
            acc1[rows, :] += fold(dn)

    @pl.loop(1, HOPS)
    def _(d):
        if NT == 1:
            lp_copy(d, 0).start()
        lp_copy(d, 1).start()

    own_lp = pltpu.make_async_copy(lps, o_lp.at[:, o_own], ss.at[names["lp"]])
    own_lp.start()
    s3[me, :, pl.ds(0, hid)] = row_of(acc0[...])
    s3[me, :, pl.ds(hid, hid)] = row_of(acc1[...])
    zpad = jnp.zeros((80, 128), F32)
    s3[me, :, pl.ds(2 * hid, 128)] = row_of(jnp.concatenate([accl[pl.ds(0, 48), :], zpad], axis=0))
    s3[me, :, pl.ds(2 * hid + 128, 128)] = row_of(jnp.concatenate([accl[pl.ds(48, 48), :], zpad], axis=0))
    all_start(s3, "s3")

    def cwh_copy(d):
        return rc(cwp.at[d], cwh.at[d], "cwh", d, peer(d), r)

    q = hid // HOPS

    @pl.loop(0, HOPS)
    def _(d):
        cwp[d] = accw[:, lanes_at(peer(d), q)]


    @pl.loop(1, HOPS)
    def _(d):
        cwh_copy(d).start()

    all_wait(s3, "s3")
    st3 = total(s3, D)
    db2 = st3[:, hid : 2 * hid]
    dg2t = inv2 * (st3[:, :hid] - mean2 * db2)
    o_small[pl.ds(0, 1), :] = dg2t
    o_small[pl.ds(1, 1), :] = db2
    o_small[pl.ds(4, 1), pl.ds(0, 256)] = st3[:, 2 * hid : 2 * hid + 256]
    o_small[pl.ds(4, 1), pl.ds(256, hid - 256)] = jnp.zeros((1, hid - 256), F32)
    t2 = scale2 * inv2 * dg2t * inv_n
    cols[1] = col_of(-t2)
    cols[2] = col_of(t2 * mean2 - scale2 * db2 * inv_n)

    @pl.loop(0, hid // 16)
    def _(i):
        rows = lanes_at(i, 16)
        v = dn2[rows, :] * spread(cols[0, rows, :], sub)
        v = v + mixed[rows, :] * spread(cols[1, rows, :], sub) + spread(cols[2, rows, :], sub)
        dmx[rows, :] = v.astype(BF16)

    mine = lanes_at(c, half)
    theirs = lanes_at(1 - c, half)

    def pair_copy(d):
        return rc(dmp.at[d, theirs, :], pr.at[d], "pair", d, h, sib)

    qrows = half // S
    zown = pl.ds(pl.multiple_of(c * half + zpar * qrows, 16), qrows)
    zother = pl.ds(pl.multiple_of(c * half + (1 - zpar) * qrows, 16), qrows)

    def z1_copy(d):
        return rc(dmp.at[d, zother, :], z1r.at[d], "z1", d, h, 2 * zmate + c)

    def z1_start(d):
        if S > 1:
            z1_copy(d).start()

    def z1_sum(d):
        if S > 1:
            done(z1_copy(d))

            @pl.loop(0, qrows // 32)
            def _(i):
                rows = pl.ds(pl.multiple_of(c * half + zpar * qrows + i * 32, 32), 32)
                dmp[d, rows, :] = (dmp[d, rows, :].astype(F32) + z1r[d, lanes_at(i, 32), :].astype(F32)).astype(BF16)

    def hop_copy(d):
        return rc(dmp.at[d, zown, :], hr.at[d], "hop", d, peer(d), r)

    def pair_sum(d):
        done(pair_copy(d))

        @pl.loop(0, half // 32)
        def _(i):
            rows = pl.ds(pl.multiple_of(c * half + i * 32, 32), 32)
            dmp[d, rows, :] = (dmp[d, rows, :].astype(F32) + pr[d, lanes_at(i, 32), :].astype(F32)).astype(BF16)

    @pl.loop(0, HOPS)
    def _(i):
        d = HOPS - 1 - i

        @pl.loop(0, 2)
        def _(j):
            rows = lanes_at(j, half)
            dmp[d, rows, :] = dot_nt(mi[d, rows, :], dmx[...]).astype(BF16)

        pair_copy(d).start()

        @pl.when(i > 0)
        def _():
            pair_sum(d + 1)
            z1_start(d + 1)

        @pl.when(i > 1)
        def _():
            z1_sum(d + 2)
            hop_copy(d + 2).start()

    G2 = Z // S
    zq = lax.div(zi, S)

    def zr_copy(e, which):
        rows, lanes = chunk(0, which, qrows, G2, hid)
        return rc(hr.at[0, rows, lanes], zr.at[e], "zr", e, h, (lax.rem(zq + e, G2) * S + zpar) * 2 + c)

    def final_chunk(z):
        return chunk(c * half + lax.rem(z, S) * qrows, lax.div(z, S), qrows, G2, hid)

    def zg_copy(e, which):
        rows, lanes = final_chunk(which)
        ref = fin.at[rows, lanes]
        return rc(ref, ref, "zg", e, h, lax.rem(zi + e, Z) * 2 + c)

    def ddm_copy(core):
        ref = fin.at[lanes_at(core, half), :]
        return rc(ref, ref, "ddm", 0, h, sib)

    def d_copy(d):
        return rc(dsend.at[d], o_d.at[h], "d", d, peer(d), r)

    def dt_copy(d):
        return rc(dtail.at[d], o_dt.at[h], "dt", d, peer(d), r)

    def p_copy(d):
        return rc(ps.at[d], prv.at[d], "p", d, peer(d), r)

    def q_copy(d):
        return rc(qs.at[d], qv.at[d], "q", d, peer(d), r)

    @pl.loop(0, HOPS * NT)
    def _(it):
        dd = lax.div(it, NT)
        t = lax.rem(it, NT)
        d = HOPS - 1 - dd

        @pl.when(t == 0)
        def _():
            pT[...] = jnp.zeros(pT.shape, F32)

        @pl.when(it == NT // 2)
        def _():
            pair_sum(0)
            z1_start(0)
            z1_sum(1)
            hop_copy(1).start()

        @pl.when(it == NT + NT // 2)
        def _():
            @pl.loop(1, HOPS)
            def _(j):
                done(cwh_copy(j))

            cwr[r] = cwp[0] + (cwh[1] + cwh[2] + cwh[3])
            rows_start(cwr, "cwr")
            z1_sum(0)

        @pl.when(it == 2 * NT + NT // 2)
        def _():
            @pl.loop(1, HOPS)
            def _(j):
                done(hop_copy(j))

            @pl.loop(0, qrows // 32)
            def _(i):
                rows = lanes_at(i, 32)
                own = pl.ds(pl.multiple_of(c * half + zpar * qrows + i * 32, 32), 32)
                hsum = dmp[0, own, :].astype(F32)
                for j in range(1, HOPS):
                    hsum = hsum + hr[j, rows, :].astype(F32)
                hr[0, rows, :] = hsum.astype(BF16)

            @functools.partial(each, 1, G2)
            def _(e):
                zr_copy(e, lax.rem(zq + e, G2)).start()

            rows_wait(cwr, "cwr")
            cwg[h] = total(cwr, R)
            hops_start(cwg, "cwg")

        @pl.when(it == 3 * NT + NT // 2)
        def _():
            @functools.partial(each, 1, G2)
            def _(e):
                done(zr_copy(e, lax.rem(zq + e, G2)))

            rows, lanes = chunk(0, zq, qrows, G2, hid)
            zt = lax.fori_loop(1, G2, lambda e, v: v + zr[e].astype(F32), hr[0, rows, lanes].astype(F32))
            frows, flanes = final_chunk(zi)
            fin[frows, flanes] = zt.astype(BF16)

            @functools.partial(each, 1, Z)
            def _(e):
                zg_copy(e, zi).start()

            hops_wait(cwg, "cwg")
            for j in range(HOPS):
                o_cw[:, pl.ds(j * q, q)] = cwg[j]

        n = lanes_at(t, big)
        dn = dot(wmx[d], dmx[:, n]).astype(BF16) * gp[d, :, n]
        pT[...] += dot_nt(dn, fx[d, :, n])
        grad = dot(aw[d], dn)
        dsend[d, :, n] = grad[:MAIN].astype(BF16)
        d4[:, n] = grad[MAIN : MAIN + 8]

        @pl.when(t == NT - 1)
        def _():
            pw = pT[...].T * KAPPA
            qs[d, :, pl.ds(0, hid)] = jnp.sum(pw * wall[d, wrow, :].astype(F32), axis=0, keepdims=True)
            qs[d, :, pl.ds(hid, hid)] = pw[ONES : ONES + 1, :]
            ps[d] = pw.astype(BF16)
            pack4(d4, dtail.at[d])

            @pl.when(dd < HOPS - 1)
            def _():
                q_copy(d).start()
                p_copy(d).start()
                d_copy(d).start()
                dt_copy(d).start()

    @pl.loop(1, HOPS)
    def _(d):
        done(q_copy(d))

    qr[r] = qs[0] + (qv[1] + qv[2] + qv[3])
    rows_start(qr, "qr")
    own_d = pltpu.make_async_copy(dsend.at[0], o_d.at[h], ss.at[names["d"]])
    own_d.start()
    own_dt = pltpu.make_async_copy(dtail.at[0], o_dt.at[h], ss.at[names["dt"]])
    own_dt.start()

    @pl.loop(1, HOPS)
    def _(d):
        done(p_copy(d))

    @pl.loop(0, 4)
    def _(i):
        rows = lanes_at(i, 32)
        v = ps[0, rows, :].astype(F32)
        for j in range(1, HOPS):
            v = v + prv[j, rows, :].astype(F32)
        psum[rows, :] = v.astype(BF16)

    owners = min(R, 32)

    def if_owner(who, body):
        if owners == R:
            body()
        else:
            pl.when(who < owners)(body)

    def prs_copy(e, to, slot):
        rows, lanes = chunk(0, to, 128, owners, hid)
        return rc(psum.at[rows, lanes], prs.at[slot], "prs", e, h, lax.rem(r + e, R))

    def pag_copy(e, who):
        rows, lanes = chunk(0, who, 128, owners, hid)
        return rc(pfin.at[rows, lanes], pfin.at[rows, lanes], "pag", e, h, lax.rem(r + e, R))

    @functools.partial(each, 1, R)
    def _(e):
        to = lax.rem(r + e, R)
        if_owner(to, lambda: prs_copy(e, to, r).start())

    @functools.partial(each, 1, Z)
    def _(e):
        zg_copy(e, zi).wait_send()
        zg_copy(e, lax.rem(zi + Z - e, Z)).wait_recv()

    ddm_copy(c).start()

    rows_wait(qr, "qr")
    qt = total(qr, R)
    db = qt[:, hid:]
    dgn = inv * (qt[:, :hid] - mean * db)
    o_small[pl.ds(2, 1), :] = dgn
    o_small[pl.ds(3, 1), :] = db
    c1 = scale * db * inv_n
    c2 = inv * scale * dgn * inv_n
    shift = c1 - mean * c2
    row = lax.broadcasted_iota(jnp.int32, (128, hid), 0)
    q1, q2 = split2(jnp.where(row == ONES, shift, wown32 * c2))
    o_m[...] = (dot_nt(wown, q1) + dot_nt(wown, q2))[:FP]
    rows_wait(gbuf, "gr")
    g1, g2, g3 = split3(total(gbuf, R))
    gq = dot(g1, q1) + dot(g2, q1) + dot(g3, q1) + dot(g1, q2) + dot(g2, q2)

    @functools.partial(each, 1, R)
    def _(e):
        to = lax.rem(r + e, R)
        src = lax.rem(r + R - e, R)
        if_owner(to, lambda: prs_copy(e, to, r).wait_send())
        if_owner(r, lambda: prs_copy(e, r, src).wait_recv())

    def gather():
        rows, lanes = chunk(0, r, 128, owners, hid)
        prs[r] = psum[rows, lanes]
        pt = lax.fori_loop(1, R, lambda j, v: v + prs[j].astype(F32), prs[0].astype(F32))
        pfin[rows, lanes] = pt.astype(BF16)

        @functools.partial(each, 1, R)
        def _(e):
            pag_copy(e, r).start()

    if_owner(r, gather)
    ddm_copy(c).wait_send()
    ddm_copy(1 - c).wait_recv()
    o_mix[...] = fin[...]

    @functools.partial(each, 1, R)
    def _(e):
        src = lax.rem(r + R - e, R)
        if_owner(r, lambda: pag_copy(e, r).wait_send())
        if_owner(src, lambda: pag_copy(e, src).wait_recv())

    o_gw[...] = pfin[pl.ds(0, FP), :].astype(F32) * scale - gq
    own_d.wait()
    own_dt.wait()
    own_lp.wait()

    @pl.loop(1, HOPS)
    def _(d):
        done(d_copy(d))
        done(dt_copy(d))
        done(lp_copy(d, 0))
        done(lp_copy(d, 1))


def last_kernel(
    nodes,
    ft, d, dt, lp, m, mix, gw, small, cw,
    o_lp, o_gf, o_mix, o_gw, o_gg, o_gb, o_hg, o_hb, o_cw, o_cb, o_loss, low,
):
    feat, n = ft.shape
    ncls = o_lp.shape[0]
    o_lp[...] = lp[...].astype(F32)[:ncls]
    mm = m[...]
    f = ft[...]
    fix = dot(mm[:, :feat].astype(BF16), f) + mm[:, ONES : ONES + 1]
    tail = dt[0].astype(F32)
    for b in range(4):
        low[pl.ds(0, 4), pl.ds(b * (n // 4), n // 4)] = tail[4 * b : 4 * b + 4]
    gf = jnp.concatenate([d[0].astype(F32), low[...]], axis=0)[:feat] - fix[:feat]
    if STRIDED:
        flat = o_gf.reshape(feat * (n // 128), 128)
        for i in range(n // 128):
            flat[pl.ds(i, feat, stride=n // 128), :] = gf[:, i * 128 : (i + 1) * 128]
    else:
        for i in range(n // 128):
            o_gf[:, i, :] = gf[:, i * 128 : (i + 1) * 128]

    @pl.when(pl.program_id(0) == 0)
    def _():
        hid = mix.shape[1]
        o_mix[...] = mix[...].astype(F32)
        for i in range(hid // 128):
            o_gw[:, i, :] = gw[pl.ds(0, feat), pl.ds(i * 128, 128)]
        o_hg[...] = small[pl.ds(0, 1), :]
        o_hb[...] = small[pl.ds(1, 1), :]
        o_gg[...] = small[pl.ds(2, 1), :]
        o_gb[...] = small[pl.ds(3, 1), :]
        o_cw[...] = cw[pl.ds(0, ncls), :]
        o_cb[...] = small[pl.ds(4, 1), pl.ds(0, ncls)]
        o_loss[...] = jnp.sum(small[pl.ds(4, 1), pl.ds(128, 128)], axis=1, keepdims=True) * (-1.0 / nodes)


def shards(
    R, features, branch_weight, branch_gain, branch_bias, mix_weight, mixing_norm_gain, mixing_norm_bias,
    class_weight, class_bias, labels, hop_mask,
):
    local, feat = features.shape[1:]
    hid = mix_weight.shape[0]
    ncls = class_weight.shape[1]
    nodes = local * R
    sub = local // HOPS
    Z = R // 2
    half = hid // 2
    S = min(Z, 2)
    G2, qrows = Z // S, half // S
    zrows, zcols = chunk(0, 0, qrows, G2, hid)
    prows, pcols = chunk(0, 0, 128, min(R, 32), hid)
    assert feat == ONES and ncls == 47 and local // hop_mask.shape[0] == 128
    ft = features[0].T
    sd = jax.ShapeDtypeStruct
    vm = pl.BlockSpec(memory_space=pltpu.VMEM)
    hbm = pl.BlockSpec(memory_space=pl.ANY)
    _, nsem = sem_plan(R)
    V = pltpu.VMEM
    outs = pl.pallas_call(
        functools.partial(main_kernel, R, nodes),
        grid=(1,),
        out_shape=(
            sd((48, local), BF16),
            sd((HOPS, MAIN, sub), BF16),
            sd((HOPS, 16, sub // 4), BF16),
            sd((FP, 128), F32),
            sd((hid, hid), BF16),
            sd((FP, hid), F32),
            sd((8, hid), F32),
            sd((48, hid), F32),
        ),
        in_specs=[hbm, pl.BlockSpec((16, local), lambda i: (MAIN // 16, 0))]
        + [vm] * 9
        + [pl.BlockSpec(memory_space=pltpu.SMEM)],
        out_specs=(hbm, hbm, hbm, vm, vm, vm, vm, vm),
        scratch_shapes=[
            V((128, local), BF16),
            V((HOPS, 128, sub), BF16),
            V((HOPS, 16, sub // 4), BF16),
            V((HOPS, 16, sub // 4), BF16),
            V((48, sub // 4), F32),
            V((HOPS, hid + 128, hid), BF16),
            V((HOPS, hid, 256), BF16),
            V((HOPS, FP, hid), BF16),
            V((HOPS, hid, hid), BF16),
            V((HOPS, 16, sub), BF16),
            V((HOPS, hid, sub), BF16),
            V((HOPS, hid, sub), BF16),
            V((hid, sub), F32),
            V((hid, sub), F32),
            V((hid, sub), BF16),
            V((R, FP, 128), F32),
            V((R, 1, 2 * hid), F32),
            V((HOPS, 1, 2 * hid), F32),
            V((HOPS * R, 1, 2 * hid), F32),
            V((HOPS * R, 1, 2 * hid + 256), F32),
            V((HOPS, 48, hid // HOPS), F32),
            V((HOPS, 48, hid // HOPS), F32),
            V((R, 48, hid // HOPS), F32),
            V((HOPS, 48, hid // HOPS), F32),
            V((48, sub), BF16),
            V((128, hid), F32),
            V((hid, 128), BF16),
            V((8, 128), F32),
            V((hid, min(2 * TILE, sub)), BF16),
            V((128, min(2 * TILE, sub)), BF16),
            V((hid, 128), F32),
            V((hid, 128), F32),
            V((96, 128), F32),
            V((48, hid), F32),
            V((3, hid, 128), F32),
            V((HOPS, hid, hid), BF16),
            V((HOPS, half, hid), BF16),
            V((HOPS, qrows, hid), BF16),
            V((HOPS, qrows, hid), BF16),
            V((max(G2, 2), zrows.size, zcols.size), BF16),
            V((hid, hid), BF16),
            V((HOPS, MAIN, sub), BF16),
            V((8, sub), F32),
            V((HOPS, 16, sub // 4), BF16),
            V((hid, 128), F32),
            V((HOPS, 128, hid), BF16),
            V((HOPS, 128, hid), BF16),
            V((HOPS, 1, 2 * hid), F32),
            V((HOPS, 1, 2 * hid), F32),
            V((R, 1, 2 * hid), F32),
            V((R, prows.size, pcols.size), BF16),
            V((128, hid), BF16),
            V((128, hid), BF16),
            pltpu.SemaphoreType.DMA((nsem,)),
            pltpu.SemaphoreType.DMA((nsem,)),
        ],
        compiler_params=pltpu.CompilerParams(
            collective_id=0, has_side_effects=True, vmem_limit_bytes=63 * 1024 * 1024
        ),
        cost_estimate=pl.CostEstimate(flops=2 * 8 * 10**9, bytes_accessed=10**7, transcendentals=10**7),
        name="main",
    )(
        ft, ft, branch_weight[0], branch_gain, branch_bias, mix_weight, mixing_norm_gain[None], mixing_norm_bias[None],
        class_weight.T, class_bias[None], labels[None], hop_mask.T,
    )
    lp, dd, dt, m, mix, gw, small, cw = outs
    nb = sub
    whole = lambda shape: pl.BlockSpec(shape, lambda i: (0,) * len(shape))
    lp, gf, mix, gw, gg, gb, hg, hb, cw, cb, loss = pl.pallas_call(
        functools.partial(last_kernel, nodes),
        grid=(local // nb,),
        out_shape=(
            sd((ncls, local), F32),
            sd((feat, local // 128, 128), F32),
            sd((hid, hid), F32),
            sd((feat, hid // 128, 128), F32),
            sd((1, hid), F32),
            sd((1, hid), F32),
            sd((1, hid), F32),
            sd((1, hid), F32),
            sd((ncls, hid), F32),
            sd((1, ncls), F32),
            sd((1, 1), F32),
        ),
        in_specs=[
            pl.BlockSpec((feat, nb), lambda i: (0, i)),
            pl.BlockSpec((1, MAIN, nb), lambda i: (i, 0, 0)),
            pl.BlockSpec((1, 16, nb // 4), lambda i: (i, 0, 0)),
            pl.BlockSpec((48, nb), lambda i: (0, i)),
            whole((FP, 128)),
            whole((hid, hid)),
            whole((FP, hid)),
            whole((8, hid)),
            whole((48, hid)),
        ],
        out_specs=(
            pl.BlockSpec((ncls, nb), lambda i: (0, i)),
            pl.BlockSpec((feat, nb // 128, 128), lambda i: (0, i, 0)),
            whole((hid, hid)),
            whole((feat, hid // 128, 128)),
            whole((1, hid)),
            whole((1, hid)),
            whole((1, hid)),
            whole((1, hid)),
            whole((ncls, hid)),
            whole((1, ncls)),
            whole((1, 1)),
        ),
        scratch_shapes=[V((8, nb), F32)],
        compiler_params=pltpu.CompilerParams(vmem_limit_bytes=60 * 1024 * 1024),
        name="last",
    )(ft, dd, dt, lp, m, mix, gw, small, cw)
    return (
        lp.T,
        loss[0, 0],
        with_layout_constraint(gf.reshape(feat, 1, local), Layout((0, 1, 2))).transpose(1, 2, 0),
        gw.reshape(1, feat, hid),
        gg,
        gb,
        mix,
        hg[0],
        hb[0],
        cw.T,
        cb[0],
    )


def solution(mesh):
    placed = (
        P("hop", "rows", None), P("hop", None, None), P("hop", None), P("hop", None), P("hop", None),
        P(), P(), P(), P(), P("rows"), P("rows", None),
    )
    assert mesh.shape["hop"] == HOPS
    return jax.shard_map(
        functools.partial(shards, mesh.shape["rows"]),
        mesh=mesh,
        in_specs=placed,
        out_specs=(
            P("rows", None), P(), P("hop", "rows", None), P("hop", None, None), P("hop", None), P("hop", None),
            P("hop", None), P(), P(), P(), P(),
        ),
        check_vma=False,
    )
```

```python
import functools
import math

import jax
import jax.numpy as jnp
from jax import lax
from jax.experimental import pallas as pl
from jax.experimental.layout import Layout, with_layout_constraint
from jax.experimental.pallas import tpu as pltpu
from jax.sharding import PartitionSpec as P

MESH = pl.DeviceIdType.MESH
EPS = 1e-05
HOPS = 4
ONES = 100
FP = 112
MAIN = 96
TILE = 256
STRIDED = True
C0 = math.sqrt(2.0 / math.pi)
C1 = C0 * 0.044715
KAPPA = C1 ** (1.0 / 3.0)
ALPHA = C0 / KAPPA
F32 = jnp.float32
BF16 = jnp.bfloat16


def dot(a, b):
    return lax.dot_general(a, b, (((1,), (0,)), ((), ())), preferred_element_type=F32)


def dot_nt(a, b):
    return lax.dot_general(a, b, (((1,), (1,)), ((), ())), preferred_element_type=F32)


def split2(x):
    hi = x.astype(BF16)
    return hi, (x - hi.astype(F32)).astype(BF16)


def split3(x):
    hi = x.astype(BF16)
    rest = x - hi.astype(F32)
    mid = rest.astype(BF16)
    return hi, mid, (rest - mid.astype(F32)).astype(BF16)


def gelu_slope(z):
    u = z * z
    t = jnp.tanh(z * (C0 + C1 * u))
    s = 0.5 * t + 0.5
    g = z * s
    return g, s + (g - g * s) * (2.0 * C0 + 6.0 * C1 * u)


def scaled_gelu_slope(y):
    u = y * y
    t = jnp.tanh(y * (u + ALPHA))
    up = t + 1.0
    g = y * up
    return g, up + (g * (1.0 - t)) * (3.0 * u + ALPHA)


def fold(x):
    total = x[:, :128]
    for i in range(1, x.shape[1] // 128):
        total = total + x[:, i * 128 : (i + 1) * 128]
    return total


def spread(c, n):
    return jnp.concatenate([c] * (n // 128), axis=1)


def row_of(acc):
    return jnp.sum(acc.T, axis=0, keepdims=True)


def col_of(row):
    return jnp.broadcast_to(row, (128, row.shape[1])).T


def each(lo, hi, body):
    if hi - lo == 1:
        body(lo)
    elif hi > lo:
        pl.loop(lo, hi)(body)


class Alloc:
    def __init__(self):
        self.n = 0

    def __call__(self, count):
        base = self.n
        self.n += count
        return base


def sem_plan(R):
    Z = R // 2
    a = Alloc()
    names = {}
    for name, count in (
        ("feat", 4), ("ft", 4), ("loc", 1), ("ws", 4), ("zf", 4), ("dd", 4), ("s1", R), ("ab", 4), ("gp", 1), ("gz", Z), ("gd", 1),
        ("s2h", 4), ("s2r", R), ("s3h", 4), ("s3r", R), ("lp", 8), ("cwh", 4), ("cwr", R), ("cwg", 4),
        ("pair", 4), ("z1", 4), ("hop", 4), ("zr", Z), ("zg", Z), ("ddm", 1), ("d", 4), ("dt", 4), ("p", 4), ("q", 4),
        ("qr", R), ("pp", 4), ("pz", Z), ("pd", 1),
    ):
        names[name] = a(count)
    return names, a.n


def chunk(base, i, rows, pieces, cols):
    if rows // pieces >= 16:
        take = rows // pieces
        return pl.ds(pl.multiple_of(base + i * take, 16), take), pl.ds(0, cols)
    m = 16 * pieces // rows
    wide = cols // m
    return (
        pl.ds(pl.multiple_of(base + (i // m) * 16, 16), 16),
        pl.ds(pl.multiple_of((i % m) * wide, 128), wide),
    )


def main_kernel(
    R,
    nodes,
    ft, ft4, wb, bgain, bbias, wm, gain2, bias2, wc, cb, lab, msk,
    o_lp, o_d, o_dt, o_m, o_mix, o_gw, o_small, o_cw,
    fs, fx, ftail, frt, st4, wall, wl, aw, wmx, keep, mi, gp, mixed, dn2, dmx,
    gown, gpr, gz, gfin, s1, ab, s2h, s2r, s3h, s3r, cwp, cwh, cwr, cwg, lps,
    wcs, wcNs, cbs, hb, dlp, acc0, acc1, accl, accw, cols,
    dmp, pr, z1r, hr, zr, fin, dsend, d4, dtail, pT, ps, ph, phalf, prv, qs, qv, qr, pz, pfin,
    ss, rs,
):
    names, _ = sem_plan(R)
    Z = R // 2
    h = lax.axis_index("hop")
    r = lax.axis_index("rows")
    c = lax.rem(r, 2)
    zi = lax.div(r, 2)
    sib = r + 1 - 2 * c
    local = ft.shape[1]
    sub = local // HOPS
    hid = wm.shape[0]
    half = hid // 2
    big = min(2 * TILE, sub)
    UN = big // TILE
    NT = sub // big
    inv_n = 1.0 / nodes

    def peer(d):
        x = lax.rem(h + d, 2)
        y = lax.rem(lax.div(h, 2) + lax.div(d, 2), 2)
        return 2 * y + x

    def rc(src, dst, name, i, hh, rr):
        return pltpu.make_async_remote_copy(
            src_ref=src, dst_ref=dst, send_sem=ss.at[names[name] + i], recv_sem=rs.at[names[name] + i],
            device_id=(hh, rr), device_id_type=MESH,
        )

    def done(cp):
        cp.wait_send()
        cp.wait_recv()

    def lanes_at(i, n):
        return pl.ds(pl.multiple_of(i * n, n), n)

    barrier = pltpu.get_barrier_semaphore()

    def greet(hh, rr):
        pl.semaphore_signal(barrier, inc=1, device_id=(hh, rr), device_id_type=MESH)

    @pl.loop(1, HOPS)
    def _(d):
        greet(peer(d), r)

    @functools.partial(each, 1, R)
    def _(e):
        greet(h, lax.rem(r + e, R))

    def rows_start(buf, name):
        @functools.partial(each, 1, R)
        def _(e):
            rc(buf.at[r], buf.at[r], name, e, h, lax.rem(r + e, R)).start()

    def rows_wait(buf, name):
        @functools.partial(each, 1, R)
        def _(e):
            src = lax.rem(r + R - e, R)
            done(rc(buf.at[src], buf.at[src], name, e, h, lax.rem(r + e, R)))

    def hops_start(buf, name):
        @pl.loop(1, HOPS)
        def _(d):
            rc(buf.at[h], buf.at[h], name, d, peer(d), r).start()

    def hops_wait(buf, name):
        @pl.loop(1, HOPS)
        def _(d):
            done(rc(buf.at[peer(d)], buf.at[peer(d)], name, d, peer(d), r))

    def total(buf, n, dtype=F32):
        return lax.fori_loop(1, n, lambda i, t: t + buf[i].astype(dtype), buf[0].astype(dtype))

    loc = pltpu.make_async_copy(ft.at[pl.ds(0, MAIN), :], fs.at[pl.ds(0, MAIN), :], ss.at[names["loc"]])
    loc.start()

    def pack4(src, dst):
        n = st4.shape[1]
        for b in range(4):
            st4[pl.ds(4 * b, 4), :] = src[pl.ds(0, 4), pl.ds(b * n, n)].astype(F32)
        dst[...] = st4[pl.ds(0, 16), :].astype(BF16)

    def unpack4(src, dst):
        n = st4.shape[1]
        row = lax.broadcasted_iota(jnp.int32, (32, n), 0)
        st4[pl.ds(0, 16), :] = src[...].astype(F32)
        st4[pl.ds(16, 32), :] = jnp.where(row == ONES - MAIN, 1.0, 0.0)
        for b in range(4):
            st4[pl.ds(16, 4), :] = st4[pl.ds(4 * b, 4), :]
            dst[pl.ds(MAIN, 32), pl.ds(b * n, n)] = st4[pl.ds(16, 32), :].astype(BF16)

    wrow = pl.ds(hid, 128)
    wall[0, pl.ds(hid + 96, 32), :] = jnp.zeros((32, hid), BF16)
    wall[0, pl.ds(hid, 100), :] = wb[...]

    @pl.loop(0, hid // 128)
    def _(i):
        k = lanes_at(i, 128)
        wall[0, pl.ds(0, hid), k] = wm[k, :].astype(F32).T.astype(BF16)

    def feat_copy(d):
        rows = pl.ds(0, MAIN)
        return rc(ft.at[rows, lanes_at(peer(d), sub)], fx.at[d, rows, :], "feat", d, peer(d), r)

    def ft_copy(d):
        return rc(ftail.at[peer(d)], frt.at[d], "ft", d, peer(d), r)

    pl.semaphore_wait(barrier, HOPS - 1 + R - 1)

    S = min(Z, 2)
    part = (hid + 128) // (2 * S)
    zpar = lax.rem(zi, S)
    zmate = zi + (S - 1) - 2 * (S - 1) * zpar

    def part_rows(core, par):
        return pl.ds(pl.multiple_of((core * S + par) * part, 16), part)

    def ws_copy(d):
        rows = part_rows(c, zpar)
        return rc(wall.at[0, rows, :], wall.at[d, rows, :], "ws", d, peer(d), r)

    def zf_copy(d, par):
        ref = wall.at[d, part_rows(c, par), :]
        return rc(ref, ref, "zf", d, h, 2 * zmate + c)

    def dd_copy(d, core):
        ref = wall.at[d, pl.ds(pl.multiple_of(core * S * part, 16), S * part), :]
        return rc(ref, ref, "dd", d, h, sib)

    @pl.loop(1, HOPS)
    def _(d):
        ws_copy(d).start()

    @pl.loop(1, HOPS - 1)
    def _(d):
        feat_copy(d).start()

    @pl.loop(0, HOPS)
    def _(j):
        lanes = lanes_at(j, sub)
        pack4(ft4.at[:, lanes], ftail.at[j])
        unpack4(ftail.at[j], fs.at[:, lanes])

    @pl.loop(1, HOPS)
    def _(d):
        ft_copy(d).start()

    loc.wait()
    fx0 = pltpu.make_async_copy(fs.at[:, lanes_at(h, sub)], fx.at[0], ss.at[names["loc"]])
    fx0.start()

    def gram(i, g):
        f = fs[:, lanes_at(i, sub)]
        return g + dot_nt(f, f)

    g = lax.fori_loop(0, HOPS, gram, jnp.zeros((128, 128), F32))
    wown = wall[0, wrow, :]
    wown32 = wown.astype(F32)
    g1, g2, g3 = split3(g)
    gw = dot(g1, wown) + dot(g2, wown) + dot(g3, wown)
    s1[r, :, pl.ds(0, hid)] = gw[ONES : ONES + 1, :]
    s1[r, :, pl.ds(hid, hid)] = jnp.sum(gw * wown32, axis=0, keepdims=True)
    rows_start(s1, "s1")
    gown[...] = g

    @pl.loop(0, HOPS * (sub // 128))
    def _(i):
        d = lax.div(i, sub // 128)
        b = lax.rem(i, sub // 128)
        late = peer(d) - 2
        m = jnp.where(late >= 0, msk[jnp.maximum(late, 0), h * (sub // 128) + b], 1)
        keep[d, :, lanes_at(b, 128)] = jnp.full((16, 128), 0.5 * m.astype(F32)).astype(BF16)

    wcs[...] = jnp.zeros(wcs.shape, F32)
    wcs[pl.ds(0, wc.shape[0]), :] = wc[...].astype(F32)
    cbs[...] = jnp.zeros(cbs.shape, F32)
    cbs[pl.ds(0, 1), pl.ds(0, cb.shape[1])] = cb[...]
    ncls = wc.shape[0]

    @pl.loop(0, hid // 16)
    def _(i):
        rows = lanes_at(i, 16)
        mixed[rows, :] = jnp.zeros((16, sub), F32)
        mi[0, rows, pl.ds(0, big)] = jnp.zeros((16, big), BF16)

    fx0.wait()

    rows_wait(s1, "s1")
    st = total(s1, R)
    mean = st[:, :hid] * inv_n
    var = st[:, hid:] * inv_n - mean * mean
    inv = lax.rsqrt(var + EPS)
    scale = inv * bgain[...]
    ab[0, :, pl.ds(0, hid)] = scale
    ab[0, :, pl.ds(hid, hid)] = bbias[...] - mean * scale

    def ab_copy(d):
        return rc(ab.at[0], ab.at[d], "ab", d, peer(d), r)

    @pl.loop(1, HOPS)
    def _(d):
        ab_copy(d).start()

    def prepare(d):
        a = ab[d, :, pl.ds(0, hid)]
        b = ab[d, :, pl.ds(hid, hid)]
        ws = wall[d, wrow, :].astype(F32) * (a * KAPPA)
        aw[d] = ws[:FP].astype(BF16)
        row = lax.broadcasted_iota(jnp.int32, (128, hid), 0)
        wt = jnp.where(row == ONES, b * KAPPA, ws).T
        hi, lo = split2(wt)
        wl[d, :, pl.ds(0, 128)] = hi
        wl[d, :, pl.ds(128, 128)] = lo

    g_pair = rc(gown.at[lanes_at(1 - c, 64), :], gpr, "gp", 0, h, sib)

    def gz_copy(e, which):
        return rc(gz.at[which], gz.at[which], "gz", e, h, lax.rem(zi + e, Z) * 2 + c)

    def gd_copy(core):
        return rc(gfin.at[core], gfin.at[core], "gd", 0, h, sib)

    @pl.loop(0, HOPS * NT)
    def _(it):
        d = lax.div(it, NT)
        t = lax.rem(it, NT)

        @pl.when(t == 0)
        def _():
            @pl.when(d > 0)
            def _():
                done(feat_copy(d))
                done(ft_copy(d))
                unpack4(frt.at[d], fx.at[d])
                dd_copy(d, c).wait_send()
                dd_copy(d, 1 - c).wait_recv()
                done(ab_copy(d))

            prepare(d)

        if S > 1:

            @pl.when(it == min(1, NT - 1))
            def _():
                @pl.loop(1, HOPS)
                def _(j):
                    done(ws_copy(j))
                    zf_copy(j, zpar).start()

        @pl.when(it == min(2, NT - 1))
        def _():
            feat_copy(HOPS - 1).start()

        @pl.when(jnp.logical_and(t == NT - 1, d < HOPS - 1))
        def _():
            if S > 1:
                zf_copy(d + 1, zpar).wait_send()
                zf_copy(d + 1, 1 - zpar).wait_recv()
            else:
                done(ws_copy(d + 1))
            dd_copy(d + 1, c).start()

        @pl.when(it == 2 * NT)
        def _():
            g_pair.start()

        @pl.when(it == 3 * NT)
        def _():
            done(g_pair)
            gz[zi] = gown[lanes_at(c, 64), :] + gpr[...]

            @functools.partial(each, 1, Z)
            def _(e):
                gz_copy(e, zi).start()

        pit = jnp.maximum(it - 1, 0)
        pd = lax.div(pit, NT)
        pt = lax.rem(pit, NT)
        adds = []
        for u in range(UN):
            adds.append(dot(wall[pd, pl.ds(0, hid), :], mi[pd, :, lanes_at(pt * UN + u, TILE)]))
        for u in range(UN):
            n = lanes_at(t * UN + u, TILE)
            f = fx[d, :, n]
            z = dot(wl[d], jnp.concatenate([f, f], axis=0))
            k = keep[d, :, n]
            k = jnp.concatenate([k] * 4, axis=0)
            for i in range(0, hid, 64):
                g1, d1 = scaled_gelu_slope(z[i : i + 64].astype(BF16))
                g2, d2 = scaled_gelu_slope(g1 * k)
                mi[d, pl.ds(i, 64), n] = g2
                gp[d, pl.ds(i, 64), n] = d1 * d2 * k
        for u in range(UN):
            n = lanes_at(pt * UN + u, TILE)
            mixed[:, n] = mixed[:, n] + adds[u]

    acc0[...] = jnp.zeros(acc0.shape, F32)
    acc1[...] = jnp.zeros(acc1.shape, F32)

    @pl.loop(0, UN)
    def _(u):
        n = lanes_at((NT - 1) * UN + u, TILE)
        mixed[:, n] = mixed[:, n] + dot(wall[HOPS - 1, pl.ds(0, hid), :], mi[HOPS - 1, :, n])

    @pl.loop(0, hid // 32)
    def _(i):
        rows = lanes_at(i, 32)
        x = mixed[rows, :]
        acc0[rows, :] = fold(x)
        acc1[rows, :] = fold(x * x)

    def natural(lo, hi):
        @pl.loop(lo * (hid // 128), hi * (hid // 128))
        def _(i):
            d = lax.div(i, hid // 128)
            k = lanes_at(lax.rem(i, hid // 128), 128)
            wmx[d, k, :] = wall[d, pl.ds(0, hid), k].astype(F32).T.astype(BF16)

    s2h[h, :, pl.ds(0, hid)] = row_of(acc0[...])
    s2h[h, :, pl.ds(hid, hid)] = row_of(acc1[...])
    hops_start(s2h, "s2h")
    natural(0, 2)
    hops_wait(s2h, "s2h")
    s2r[r] = total(s2h, HOPS)
    rows_start(s2r, "s2r")
    natural(2, HOPS)
    wc48 = wcs[pl.ds(0, 48), :].astype(BF16)
    wcNs[...] = wcs[...].T.astype(BF16)
    crow = lax.broadcasted_iota(jnp.int32, (128, 128), 0)
    cbc = jnp.where(crow < ncls, jnp.broadcast_to(cbs[pl.ds(0, 1), :], (128, 128)).T, -1e30)[:48]
    rows_wait(s2r, "s2r")
    st2 = total(s2r, R)
    mean2 = st2[:, :hid] * inv_n
    inv2 = lax.rsqrt(st2[:, hid:] * inv_n - mean2 * mean2 + EPS * 4.0 * KAPPA * KAPPA)
    scale2 = inv2 * gain2[...]
    cols[0] = col_of(scale2)
    cols[1] = col_of(bias2[...] - mean2 * scale2)
    acc0[...] = jnp.zeros(acc0.shape, F32)
    acc1[...] = jnp.zeros(acc1.shape, F32)
    accl[...] = jnp.zeros(accl.shape, F32)
    accw[...] = jnp.zeros(accw.shape, F32)

    o_own = lanes_at(h, sub)

    def lp_copy(d, part):
        n = sub // 2
        return rc(
            lps.at[:, pl.ds(part * n, n)], o_lp.at[:, lanes_at(2 * h + part, n)], "lp", 4 * part + d, peer(d), r
        )

    dlp[...] = jnp.zeros(dlp.shape, BF16)
    HR = 128

    @pl.loop(0, NT)
    def _(t):
        n = lanes_at(t, big)

        if NT > 1:

            @pl.when(t == NT // 2)
            def _():
                @pl.loop(1, HOPS)
                def _(d):
                    lp_copy(d, 0).start()

        @pl.loop(0, hid // HR)
        def _(i):
            rows = lanes_at(i, HR)
            z2 = mixed[rows, n] * spread(cols[0, rows, :], big) + spread(cols[1, rows, :], big)
            gv, dg = gelu_slope(z2)
            hb[rows, :] = gv.astype(BF16)
            dn2[rows, n] = dg

        lg = dot(wc48, hb[...]) + spread(cbc, big)
        lg = lg - jnp.max(lg, axis=0, keepdims=True)
        ex = jnp.exp(lg)
        se = jnp.sum(ex, axis=0, keepdims=True)
        lp = lg - jnp.log(se)
        lps[:, n] = lp.astype(BF16)
        own = lanes_at(h * NT + t, big)
        hit = lax.broadcasted_iota(jnp.int32, (48, big), 0) == lab[:, own]
        accl[pl.ds(48, 48), :] += fold(jnp.where(hit, lp, 0.0))
        dl = ((ex / se - jnp.where(hit, 1.0, 0.0)) * inv_n).astype(BF16)
        accl[pl.ds(0, 48), :] += fold(dl.astype(F32))
        accw[...] += dot_nt(dl, hb[...])
        dlp[pl.ds(0, 48), :] = dl

        @pl.loop(0, hid // HR)
        def _(i):
            rows = lanes_at(i, HR)
            dn = dot(wcNs[rows, :], dlp[...]) * dn2[rows, n]
            dn2[rows, n] = dn
            acc0[rows, :] += fold(dn * mixed[rows, n])
            acc1[rows, :] += fold(dn)

    @pl.loop(1, HOPS)
    def _(d):
        if NT == 1:
            lp_copy(d, 0).start()
        lp_copy(d, 1).start()

    own_lp = pltpu.make_async_copy(lps, o_lp.at[:, o_own], ss.at[names["lp"]])
    own_lp.start()
    s3h[h, :, pl.ds(0, hid)] = row_of(acc0[...])
    s3h[h, :, pl.ds(hid, hid)] = row_of(acc1[...])
    zpad = jnp.zeros((80, 128), F32)
    s3h[h, :, pl.ds(2 * hid, 128)] = row_of(jnp.concatenate([accl[pl.ds(0, 48), :], zpad], axis=0))
    s3h[h, :, pl.ds(2 * hid + 128, 128)] = row_of(jnp.concatenate([accl[pl.ds(48, 48), :], zpad], axis=0))
    hops_start(s3h, "s3h")

    def cwh_copy(d):
        return rc(cwp.at[d], cwh.at[d], "cwh", d, peer(d), r)

    q = hid // HOPS

    @pl.loop(0, HOPS)
    def _(d):
        cwp[d] = accw[:, lanes_at(peer(d), q)].astype(BF16)

    hops_wait(s3h, "s3h")
    s3r[r] = total(s3h, HOPS)
    rows_start(s3r, "s3r")

    @pl.loop(1, HOPS)
    def _(d):
        cwh_copy(d).start()

    rows_wait(s3r, "s3r")
    st3 = total(s3r, R)
    db2 = st3[:, hid : 2 * hid]
    dg2t = inv2 * (st3[:, :hid] - mean2 * db2)
    o_small[pl.ds(0, 1), :] = dg2t
    o_small[pl.ds(1, 1), :] = db2
    o_small[pl.ds(4, 1), pl.ds(0, 256)] = st3[:, 2 * hid : 2 * hid + 256]
    o_small[pl.ds(4, 1), pl.ds(256, hid - 256)] = jnp.zeros((1, hid - 256), F32)
    t2 = scale2 * inv2 * dg2t * inv_n
    cols[1] = col_of(-t2)
    cols[2] = col_of(t2 * mean2 - scale2 * db2 * inv_n)

    @pl.loop(0, hid // 16)
    def _(i):
        rows = lanes_at(i, 16)
        v = dn2[rows, :] * spread(cols[0, rows, :], sub)
        v = v + mixed[rows, :] * spread(cols[1, rows, :], sub) + spread(cols[2, rows, :], sub)
        dmx[rows, :] = v.astype(BF16)

    @functools.partial(each, 1, Z)
    def _(e):
        gz_copy(e, zi).wait_send()
        gz_copy(e, lax.rem(zi + Z - e, Z)).wait_recv()

    gfin[c] = total(gz, Z)
    gd_copy(c).start()

    mine = lanes_at(c, half)
    theirs = lanes_at(1 - c, half)

    def pair_copy(d):
        return rc(dmp.at[d, theirs, :], pr.at[d], "pair", d, h, sib)

    qrows = half // S
    zown = pl.ds(pl.multiple_of(c * half + zpar * qrows, 16), qrows)
    zother = pl.ds(pl.multiple_of(c * half + (1 - zpar) * qrows, 16), qrows)

    def z1_copy(d):
        return rc(dmp.at[d, zother, :], z1r.at[d], "z1", d, h, 2 * zmate + c)

    def z1_start(d):
        if S > 1:
            z1_copy(d).start()

    def z1_sum(d):
        if S > 1:
            done(z1_copy(d))

            @pl.loop(0, qrows // 32)
            def _(i):
                rows = pl.ds(pl.multiple_of(c * half + zpar * qrows + i * 32, 32), 32)
                dmp[d, rows, :] = (dmp[d, rows, :].astype(F32) + z1r[d, lanes_at(i, 32), :].astype(F32)).astype(BF16)

    def hop_copy(d):
        return rc(dmp.at[d, zown, :], hr.at[d], "hop", d, peer(d), r)

    def pair_sum(d):
        done(pair_copy(d))

        @pl.loop(0, half // 32)
        def _(i):
            rows = pl.ds(pl.multiple_of(c * half + i * 32, 32), 32)
            dmp[d, rows, :] = (dmp[d, rows, :].astype(F32) + pr[d, lanes_at(i, 32), :].astype(F32)).astype(BF16)

    @pl.loop(0, HOPS)
    def _(i):
        d = HOPS - 1 - i

        @pl.loop(0, 2)
        def _(j):
            rows = lanes_at(j, half)
            dmp[d, rows, :] = dot_nt(mi[d, rows, :], dmx[...]).astype(BF16)

        pair_copy(d).start()

        @pl.when(i > 0)
        def _():
            pair_sum(d + 1)
            z1_start(d + 1)

        @pl.when(i > 1)
        def _():
            z1_sum(d + 2)
            hop_copy(d + 2).start()

    G2 = Z // S
    zq = lax.div(zi, S)

    def zr_copy(e, which):
        rows, lanes = chunk(0, which, qrows, G2, hid)
        return rc(hr.at[0, rows, lanes], zr.at[e], "zr", e, h, (lax.rem(zq + e, G2) * S + zpar) * 2 + c)

    def final_chunk(z):
        return chunk(c * half + lax.rem(z, S) * qrows, lax.div(z, S), qrows, G2, hid)

    def zg_copy(e, which):
        rows, lanes = final_chunk(which)
        ref = fin.at[rows, lanes]
        return rc(ref, ref, "zg", e, h, lax.rem(zi + e, Z) * 2 + c)

    def ddm_copy(core):
        ref = fin.at[lanes_at(core, half), :]
        return rc(ref, ref, "ddm", 0, h, sib)

    def d_copy(d):
        return rc(dsend.at[d], o_d.at[h], "d", d, peer(d), r)

    def dt_copy(d):
        return rc(dtail.at[d], o_dt.at[h], "dt", d, peer(d), r)

    def pp_copy(d):
        return rc(ps.at[d, :, theirs], ph.at[d], "pp", d, h, sib)

    def p_copy(d):
        return rc(phalf.at[d], prv.at[d], "p", d, peer(d), r)

    def p_half(d):
        done(pp_copy(d))
        phalf[d] = (ps[d, :, mine].astype(F32) + ph[d].astype(F32)).astype(BF16)

    def q_copy(d):
        return rc(qs.at[d], qv.at[d], "q", d, peer(d), r)

    @pl.loop(0, HOPS * NT)
    def _(it):
        dd = lax.div(it, NT)
        t = lax.rem(it, NT)
        d = HOPS - 1 - dd

        @pl.when(t == 0)
        def _():
            pT[...] = jnp.zeros(pT.shape, F32)

        @pl.when(jnp.logical_and(t == NT // 2, dd > 0))
        def _():
            p_half(d + 1)
            p_copy(d + 1).start()

        @pl.when(it == NT // 2)
        def _():
            pair_sum(0)
            z1_start(0)
            z1_sum(1)
            hop_copy(1).start()

        @pl.when(it == NT + NT // 2)
        def _():
            @pl.loop(1, HOPS)
            def _(j):
                done(cwh_copy(j))

            cw = cwp[0].astype(F32)
            for j in range(1, HOPS):
                cw = cw + cwh[j].astype(F32)
            cwr[r] = cw.astype(BF16)
            rows_start(cwr, "cwr")
            z1_sum(0)

        @pl.when(it == 2 * NT + NT // 2)
        def _():
            @pl.loop(1, HOPS)
            def _(j):
                done(hop_copy(j))

            @pl.loop(0, qrows // 32)
            def _(i):
                rows = lanes_at(i, 32)
                own = pl.ds(pl.multiple_of(c * half + zpar * qrows + i * 32, 32), 32)
                hsum = dmp[0, own, :].astype(F32)
                for j in range(1, HOPS):
                    hsum = hsum + hr[j, rows, :].astype(F32)
                hr[0, rows, :] = hsum.astype(BF16)

            @functools.partial(each, 1, G2)
            def _(e):
                zr_copy(e, lax.rem(zq + e, G2)).start()

            rows_wait(cwr, "cwr")
            cwg[h] = total(cwr, R, F32).astype(BF16)
            hops_start(cwg, "cwg")

        @pl.when(it == 3 * NT + NT // 2)
        def _():
            @functools.partial(each, 1, G2)
            def _(e):
                done(zr_copy(e, lax.rem(zq + e, G2)))

            rows, lanes = chunk(0, zq, qrows, G2, hid)
            zt = lax.fori_loop(1, G2, lambda e, v: v + zr[e].astype(F32), hr[0, rows, lanes].astype(F32))
            frows, flanes = final_chunk(zi)
            fin[frows, flanes] = zt.astype(BF16)

            @functools.partial(each, 1, Z)
            def _(e):
                zg_copy(e, zi).start()

            hops_wait(cwg, "cwg")
            for j in range(HOPS):
                o_cw[:, pl.ds(j * q, q)] = cwg[j].astype(F32)

        n = lanes_at(t, big)
        dn = dot(wmx[d], dmx[:, n]).astype(BF16) * gp[d, :, n]
        pT[...] += dot_nt(dn, fx[d, :, n])
        grad = dot(aw[d], dn)
        dsend[d, :, n] = grad[:MAIN].astype(BF16)
        d4[:, n] = grad[MAIN : MAIN + 8]

        @pl.when(t == NT - 1)
        def _():
            pw = pT[...].T * KAPPA
            qs[d, :, pl.ds(0, hid)] = jnp.sum(pw * wall[d, wrow, :].astype(F32), axis=0, keepdims=True)
            qs[d, :, pl.ds(hid, hid)] = pw[ONES : ONES + 1, :]
            ps[d] = pw[:FP].astype(BF16)
            pp_copy(d).start()
            pack4(d4, dtail.at[d])

            @pl.when(dd < HOPS - 1)
            def _():
                q_copy(d).start()
                d_copy(d).start()
                dt_copy(d).start()

    @pl.loop(1, HOPS)
    def _(d):
        done(q_copy(d))

    qr[r] = qs[0] + (qv[1] + qv[2] + qv[3])
    rows_start(qr, "qr")
    own_d = pltpu.make_async_copy(dsend.at[0], o_d.at[h], ss.at[names["d"]])
    own_d.start()
    own_dt = pltpu.make_async_copy(dtail.at[0], o_dt.at[h], ss.at[names["dt"]])
    own_dt.start()

    p_half(0)

    @pl.loop(1, HOPS)
    def _(d):
        done(p_copy(d))

    psum = phalf[0].astype(F32) + (prv[1].astype(F32) + prv[2].astype(F32) + prv[3].astype(F32))
    pz[zi] = psum.astype(BF16)

    def pz_copy(e, which):
        return rc(pz.at[which], pz.at[which], "pz", e, h, lax.rem(zi + e, Z) * 2 + c)

    @functools.partial(each, 1, Z)
    def _(e):
        pz_copy(e, zi).start()

    @functools.partial(each, 1, Z)
    def _(e):
        zg_copy(e, zi).wait_send()
        zg_copy(e, lax.rem(zi + Z - e, Z)).wait_recv()

    ddm_copy(c).start()

    rows_wait(qr, "qr")
    qt = total(qr, R)
    db = qt[:, hid:]
    dgn = inv * (qt[:, :hid] - mean * db)
    o_small[pl.ds(2, 1), :] = dgn
    o_small[pl.ds(3, 1), :] = db
    c1 = scale * db * inv_n
    c2 = inv * scale * dgn * inv_n
    shift = c1 - mean * c2
    row = lax.broadcasted_iota(jnp.int32, (128, hid), 0)
    q1, q2 = split2(jnp.where(row == ONES, shift, wown32 * c2))
    o_m[...] = (dot_nt(wown, q1) + dot_nt(wown, q2))[:FP]
    gd_copy(c).wait_send()
    gd_copy(1 - c).wait_recv()
    g1, g2, g3 = split3(jnp.concatenate([gfin[0], gfin[1]], axis=0))
    gq = dot(g1, q1) + dot(g2, q1) + dot(g3, q1) + dot(g1, q2) + dot(g2, q2)

    @functools.partial(each, 1, Z)
    def _(e):
        pz_copy(e, zi).wait_send()
        pz_copy(e, lax.rem(zi + Z - e, Z)).wait_recv()

    pfin[c] = total(pz, Z).astype(BF16)

    def pd_copy(core):
        return rc(pfin.at[core], pfin.at[core], "pd", 0, h, sib)

    pd_copy(c).start()
    ddm_copy(c).wait_send()
    ddm_copy(1 - c).wait_recv()
    o_mix[...] = fin[...]

    pd_copy(c).wait_send()
    pd_copy(1 - c).wait_recv()
    ptot = jnp.concatenate([pfin[0], pfin[1]], axis=1).astype(F32)
    o_gw[...] = ptot * scale - gq[:FP]
    own_d.wait()
    own_dt.wait()
    own_lp.wait()

    @pl.loop(1, HOPS)
    def _(d):
        done(d_copy(d))
        done(dt_copy(d))
        done(lp_copy(d, 0))
        done(lp_copy(d, 1))


def last_kernel(
    nodes,
    ft, d, dt, lp, m, mix, gw, small, cw,
    o_lp, o_gf, o_mix, o_gw, o_gg, o_gb, o_hg, o_hb, o_cw, o_cb, o_loss, low,
):
    feat, n = ft.shape
    ncls = o_lp.shape[0]
    o_lp[...] = lp[...].astype(F32)[:ncls]
    mm = m[...]
    f = ft[...]
    fix = dot(mm[:, :feat].astype(BF16), f) + mm[:, ONES : ONES + 1]
    tail = dt[0].astype(F32)
    for b in range(4):
        low[pl.ds(0, 4), pl.ds(b * (n // 4), n // 4)] = tail[4 * b : 4 * b + 4]
    gf = jnp.concatenate([d[0].astype(F32), low[...]], axis=0)[:feat] - fix[:feat]
    if STRIDED:
        flat = o_gf.reshape(feat * (n // 128), 128)
        for i in range(n // 128):
            flat[pl.ds(i, feat, stride=n // 128), :] = gf[:, i * 128 : (i + 1) * 128]
    else:
        for i in range(n // 128):
            o_gf[:, i, :] = gf[:, i * 128 : (i + 1) * 128]

    @pl.when(pl.program_id(0) == 0)
    def _():
        hid = mix.shape[1]
        o_mix[...] = mix[...].astype(F32)
        for i in range(hid // 128):
            o_gw[:, i, :] = gw[pl.ds(0, feat), pl.ds(i * 128, 128)]
        o_hg[...] = small[pl.ds(0, 1), :]
        o_hb[...] = small[pl.ds(1, 1), :]
        o_gg[...] = small[pl.ds(2, 1), :]
        o_gb[...] = small[pl.ds(3, 1), :]
        o_cw[...] = cw[pl.ds(0, ncls), :]
        o_cb[...] = small[pl.ds(4, 1), pl.ds(0, ncls)]
        o_loss[...] = jnp.sum(small[pl.ds(4, 1), pl.ds(128, 128)], axis=1, keepdims=True) * (-1.0 / nodes)


def shards(
    R, features, branch_weight, branch_gain, branch_bias, mix_weight, mixing_norm_gain, mixing_norm_bias,
    class_weight, class_bias, labels, hop_mask,
):
    local, feat = features.shape[1:]
    hid = mix_weight.shape[0]
    ncls = class_weight.shape[1]
    nodes = local * R
    sub = local // HOPS
    Z = R // 2
    half = hid // 2
    S = min(Z, 2)
    G2, qrows = Z // S, half // S
    zrows, zcols = chunk(0, 0, qrows, G2, hid)
    assert feat == ONES and ncls == 47 and local // hop_mask.shape[0] == 128
    ft = features[0].T
    sd = jax.ShapeDtypeStruct
    vm = pl.BlockSpec(memory_space=pltpu.VMEM)
    hbm = pl.BlockSpec(memory_space=pl.ANY)
    _, nsem = sem_plan(R)
    V = pltpu.VMEM
    outs = pl.pallas_call(
        functools.partial(main_kernel, R, nodes),
        grid=(1,),
        out_shape=(
            sd((48, local), BF16),
            sd((HOPS, MAIN, sub), BF16),
            sd((HOPS, 16, sub // 4), BF16),
            sd((FP, 128), F32),
            sd((hid, hid), BF16),
            sd((FP, hid), F32),
            sd((8, hid), F32),
            sd((48, hid), F32),
        ),
        in_specs=[hbm, pl.BlockSpec((16, local), lambda i: (MAIN // 16, 0))]
        + [vm] * 9
        + [pl.BlockSpec(memory_space=pltpu.SMEM)],
        out_specs=(hbm, hbm, hbm, vm, vm, vm, vm, vm),
        scratch_shapes=[
            V((128, local), BF16),
            V((HOPS, 128, sub), BF16),
            V((HOPS, 16, sub // 4), BF16),
            V((HOPS, 16, sub // 4), BF16),
            V((48, sub // 4), F32),
            V((HOPS, hid + 128, hid), BF16),
            V((HOPS, hid, 256), BF16),
            V((HOPS, FP, hid), BF16),
            V((HOPS, hid, hid), BF16),
            V((HOPS, 16, sub), BF16),
            V((HOPS, hid, sub), BF16),
            V((HOPS, hid, sub), BF16),
            V((hid, sub), F32),
            V((hid, sub), F32),
            V((hid, sub), BF16),
            V((128, 128), F32),
            V((64, 128), F32),
            V((Z, 64, 128), F32),
            V((2, 64, 128), F32),
            V((R, 1, 2 * hid), F32),
            V((HOPS, 1, 2 * hid), F32),
            V((HOPS, 1, 2 * hid), F32),
            V((R, 1, 2 * hid), F32),
            V((HOPS, 1, 2 * hid + 256), F32),
            V((R, 1, 2 * hid + 256), F32),
            V((HOPS, 48, hid // HOPS), BF16),
            V((HOPS, 48, hid // HOPS), BF16),
            V((R, 48, hid // HOPS), BF16),
            V((HOPS, 48, hid // HOPS), BF16),
            V((48, sub), BF16),
            V((128, hid), F32),
            V((hid, 128), BF16),
            V((8, 128), F32),
            V((hid, min(2 * TILE, sub)), BF16),
            V((128, min(2 * TILE, sub)), BF16),
            V((hid, 128), F32),
            V((hid, 128), F32),
            V((96, 128), F32),
            V((48, hid), F32),
            V((3, hid, 128), F32),
            V((HOPS, hid, hid), BF16),
            V((HOPS, half, hid), BF16),
            V((HOPS, qrows, hid), BF16),
            V((HOPS, qrows, hid), BF16),
            V((max(G2, 2), zrows.size, zcols.size), BF16),
            V((hid, hid), BF16),
            V((HOPS, MAIN, sub), BF16),
            V((8, sub), F32),
            V((HOPS, 16, sub // 4), BF16),
            V((hid, 128), F32),
            V((HOPS, FP, hid), BF16),
            V((HOPS, FP, half), BF16),
            V((HOPS, FP, half), BF16),
            V((HOPS, FP, half), BF16),
            V((HOPS, 1, 2 * hid), F32),
            V((HOPS, 1, 2 * hid), F32),
            V((R, 1, 2 * hid), F32),
            V((Z, FP, half), BF16),
            V((2, FP, half), BF16),
            pltpu.SemaphoreType.DMA((nsem,)),
            pltpu.SemaphoreType.DMA((nsem,)),
        ],
        compiler_params=pltpu.CompilerParams(
            collective_id=0, has_side_effects=True, vmem_limit_bytes=63 * 1024 * 1024
        ),
        cost_estimate=pl.CostEstimate(flops=2 * 8 * 10**9, bytes_accessed=10**7, transcendentals=10**7),
        name="main",
    )(
        ft, ft, branch_weight[0], branch_gain, branch_bias, mix_weight, mixing_norm_gain[None], mixing_norm_bias[None],
        class_weight.T, class_bias[None], labels[None], hop_mask.T,
    )
    lp, dd, dt, m, mix, gw, small, cw = outs
    nb = sub
    whole = lambda shape: pl.BlockSpec(shape, lambda i: (0,) * len(shape))
    lp, gf, mix, gw, gg, gb, hg, hb, cw, cb, loss = pl.pallas_call(
        functools.partial(last_kernel, nodes),
        grid=(local // nb,),
        out_shape=(
            sd((ncls, local), F32),
            sd((feat, local // 128, 128), F32),
            sd((hid, hid), F32),
            sd((feat, hid // 128, 128), F32),
            sd((1, hid), F32),
            sd((1, hid), F32),
            sd((1, hid), F32),
            sd((1, hid), F32),
            sd((ncls, hid), F32),
            sd((1, ncls), F32),
            sd((1, 1), F32),
        ),
        in_specs=[
            pl.BlockSpec((feat, nb), lambda i: (0, i)),
            pl.BlockSpec((1, MAIN, nb), lambda i: (i, 0, 0)),
            pl.BlockSpec((1, 16, nb // 4), lambda i: (i, 0, 0)),
            pl.BlockSpec((48, nb), lambda i: (0, i)),
            whole((FP, 128)),
            whole((hid, hid)),
            whole((FP, hid)),
            whole((8, hid)),
            whole((48, hid)),
        ],
        out_specs=(
            pl.BlockSpec((ncls, nb), lambda i: (0, i)),
            pl.BlockSpec((feat, nb // 128, 128), lambda i: (0, i, 0)),
            whole((hid, hid)),
            whole((feat, hid // 128, 128)),
            whole((1, hid)),
            whole((1, hid)),
            whole((1, hid)),
            whole((1, hid)),
            whole((ncls, hid)),
            whole((1, ncls)),
            whole((1, 1)),
        ),
        scratch_shapes=[V((8, nb), F32)],
        compiler_params=pltpu.CompilerParams(vmem_limit_bytes=60 * 1024 * 1024),
        name="last",
    )(ft, dd, dt, lp, m, mix, gw, small, cw)
    return (
        lp.T,
        loss[0, 0],
        with_layout_constraint(gf.reshape(feat, 1, local), Layout((0, 1, 2))).transpose(1, 2, 0),
        gw.reshape(1, feat, hid),
        gg,
        gb,
        mix,
        hg[0],
        hb[0],
        cw.T,
        cb[0],
    )


def solution(mesh):
    placed = (
        P("hop", "rows", None), P("hop", None, None), P("hop", None), P("hop", None), P("hop", None),
        P(), P(), P(), P(), P("rows"), P("rows", None),
    )
    assert mesh.shape["hop"] == HOPS
    return jax.shard_map(
        functools.partial(shards, mesh.shape["rows"]),
        mesh=mesh,
        in_specs=placed,
        out_specs=(
            P("rows", None), P(), P("hop", "rows", None), P("hop", None, None), P("hop", None), P("hop", None),
            P("hop", None), P(), P(), P(), P(),
        ),
        check_vma=False,
    )
```

```python
import functools
import math

import jax
import jax.numpy as jnp
from jax import lax
from jax.experimental import pallas as pl
from jax.experimental.layout import Layout, with_layout_constraint
from jax.experimental.pallas import tpu as pltpu
from jax.sharding import PartitionSpec as P

MESH = pl.DeviceIdType.MESH
EPS = 1e-05
HOPS = 4
ONES = 100
FP = 112
MAIN = 96
TILE = 256
STRIDED = True
C0 = math.sqrt(2.0 / math.pi)
C1 = C0 * 0.044715
KAPPA = C1 ** (1.0 / 3.0)
ALPHA = C0 / KAPPA
F32 = jnp.float32
BF16 = jnp.bfloat16


def dot(a, b):
    return lax.dot_general(a, b, (((1,), (0,)), ((), ())), preferred_element_type=F32)


def dot_nt(a, b):
    return lax.dot_general(a, b, (((1,), (1,)), ((), ())), preferred_element_type=F32)


def split2(x):
    hi = x.astype(BF16)
    return hi, (x - hi.astype(F32)).astype(BF16)


def split3(x):
    hi = x.astype(BF16)
    rest = x - hi.astype(F32)
    mid = rest.astype(BF16)
    return hi, mid, (rest - mid.astype(F32)).astype(BF16)


def gelu_slope(z):
    u = z * z
    t = jnp.tanh(z * (C0 + C1 * u))
    s = 0.5 * t + 0.5
    g = z * s
    return g, s + (g - g * s) * (2.0 * C0 + 6.0 * C1 * u)


def scaled_gelu_slope(y):
    u = y * y
    t = jnp.tanh(y * (u + ALPHA))
    up = t + 1.0
    g = y * up
    return g, up + (g * (1.0 - t)) * (3.0 * u + ALPHA)


def fold(x):
    total = x[:, :128]
    for i in range(1, x.shape[1] // 128):
        total = total + x[:, i * 128 : (i + 1) * 128]
    return total


def spread(c, n):
    return jnp.concatenate([c] * (n // 128), axis=1)


def row_of(acc):
    return jnp.sum(acc.T, axis=0, keepdims=True)


def col_of(row):
    return jnp.broadcast_to(row, (128, row.shape[1])).T


def each(lo, hi, body):
    if hi - lo == 1:
        body(lo)
    elif hi > lo:
        pl.loop(lo, hi)(body)


class Alloc:
    def __init__(self):
        self.n = 0

    def __call__(self, count):
        base = self.n
        self.n += count
        return base


def sem_plan(R):
    Z = R // 2
    a = Alloc()
    names = {}
    for name, count in (
        ("feat", 4), ("ft", 4), ("loc", 1), ("ws", 4), ("zf", 4), ("dd", 4), ("s1", R), ("ab", 4), ("gp", 1), ("gz", Z), ("gd", 1),
        ("s2h", 4), ("s2r", R), ("s3h", 4), ("s3r", R), ("lp", 8), ("cwh", 4), ("cwr", R), ("cwg", 4),
        ("pair", 4), ("z1", 4), ("hop", 4), ("zr", Z), ("zg", Z), ("ddm", 1), ("d", 4), ("dt", 4), ("p", 4), ("q", 4),
        ("qr", R), ("pp", 4), ("pz", Z), ("pd", 1),
    ):
        names[name] = a(count)
    return names, a.n


def chunk(base, i, rows, pieces, cols):
    if rows // pieces >= 16:
        take = rows // pieces
        return pl.ds(pl.multiple_of(base + i * take, 16), take), pl.ds(0, cols)
    m = 16 * pieces // rows
    wide = cols // m
    return (
        pl.ds(pl.multiple_of(base + (i // m) * 16, 16), 16),
        pl.ds(pl.multiple_of((i % m) * wide, 128), wide),
    )


def main_kernel(
    R,
    nodes,
    ft, ft4, wb, bgain, bbias, wm, gain2, bias2, wc, cb, lab, msk,
    o_lp, o_d, o_dt, o_m, o_mix, o_gw, o_small, o_cw,
    fs, fx, ftail, frt, st4, wall, wl, aw, wmx, keep, mi, gp, mixed, dn2, dmx,
    gown, gpr, gz, gfin, s1, ab, s2h, s2r, s3h, s3r, cwp, cwh, cwr, cwg, lps,
    wcs, wcNs, cbs, hb, dlp, acc0, acc1, accl, accw, cols,
    dmp, pr, z1r, hr, zr, fin, dsend, d4, dtail, pT, ps, ph, phalf, prv, qs, qv, qr, pz, pfin,
    ss, rs,
):
    names, _ = sem_plan(R)
    Z = R // 2
    h = lax.axis_index("hop")
    r = lax.axis_index("rows")
    c = lax.rem(r, 2)
    zi = lax.div(r, 2)
    sib = r + 1 - 2 * c
    local = ft.shape[1]
    sub = local // HOPS
    hid = wm.shape[0]
    half = hid // 2
    big = min(2 * TILE, sub)
    UN = big // TILE
    NT = sub // big
    inv_n = 1.0 / nodes

    def peer(d):
        x = lax.rem(h + d, 2)
        y = lax.rem(lax.div(h, 2) + lax.div(d, 2), 2)
        return 2 * y + x

    def rc(src, dst, name, i, hh, rr):
        return pltpu.make_async_remote_copy(
            src_ref=src, dst_ref=dst, send_sem=ss.at[names[name] + i], recv_sem=rs.at[names[name] + i],
            device_id=(hh, rr), device_id_type=MESH,
        )

    def done(cp):
        cp.wait_send()
        cp.wait_recv()

    def lanes_at(i, n):
        return pl.ds(pl.multiple_of(i * n, n), n)

    barrier = pltpu.get_barrier_semaphore()

    def greet(hh, rr):
        pl.semaphore_signal(barrier, inc=1, device_id=(hh, rr), device_id_type=MESH)

    @pl.loop(1, HOPS)
    def _(d):
        greet(peer(d), r)

    @functools.partial(each, 1, R)
    def _(e):
        greet(h, lax.rem(r + e, R))

    def rows_start(buf, name):
        @functools.partial(each, 1, R)
        def _(e):
            rc(buf.at[r], buf.at[r], name, e, h, lax.rem(r + e, R)).start()

    def rows_wait(buf, name):
        @functools.partial(each, 1, R)
        def _(e):
            src = lax.rem(r + R - e, R)
            done(rc(buf.at[src], buf.at[src], name, e, h, lax.rem(r + e, R)))

    def hops_start(buf, name):
        @pl.loop(1, HOPS)
        def _(d):
            rc(buf.at[h], buf.at[h], name, d, peer(d), r).start()

    def hops_wait(buf, name):
        @pl.loop(1, HOPS)
        def _(d):
            done(rc(buf.at[peer(d)], buf.at[peer(d)], name, d, peer(d), r))

    def total(buf, n, dtype=F32):
        return lax.fori_loop(1, n, lambda i, t: t + buf[i].astype(dtype), buf[0].astype(dtype))

    loc = pltpu.make_async_copy(ft.at[pl.ds(0, MAIN), :], fs.at[pl.ds(0, MAIN), :], ss.at[names["loc"]])
    loc.start()

    def pack4(src, dst):
        n = st4.shape[1]
        for b in range(4):
            st4[pl.ds(4 * b, 4), :] = src[pl.ds(0, 4), pl.ds(b * n, n)].astype(F32)
        dst[...] = st4[pl.ds(0, 16), :].astype(BF16)

    def unpack4(src, dst):
        n = st4.shape[1]
        row = lax.broadcasted_iota(jnp.int32, (32, n), 0)
        st4[pl.ds(0, 16), :] = src[...].astype(F32)
        st4[pl.ds(16, 32), :] = jnp.where(row == ONES - MAIN, 1.0, 0.0)
        for b in range(4):
            st4[pl.ds(16, 4), :] = st4[pl.ds(4 * b, 4), :]
            dst[pl.ds(MAIN, 32), pl.ds(b * n, n)] = st4[pl.ds(16, 32), :].astype(BF16)

    wrow = pl.ds(hid, 128)
    wall[0, pl.ds(hid + 96, 32), :] = jnp.zeros((32, hid), BF16)
    wall[0, pl.ds(hid, 100), :] = wb[...]

    @pl.loop(0, hid // 128)
    def _(i):
        k = lanes_at(i, 128)
        wall[0, pl.ds(0, hid), k] = wm[k, :].astype(F32).T.astype(BF16)

    def feat_copy(d):
        rows = pl.ds(0, MAIN)
        return rc(ft.at[rows, lanes_at(peer(d), sub)], fx.at[d, rows, :], "feat", d, peer(d), r)

    def ft_copy(d):
        return rc(ftail.at[peer(d)], frt.at[d], "ft", d, peer(d), r)

    pl.semaphore_wait(barrier, HOPS - 1 + R - 1)

    S = min(Z, 2)
    part = (hid + 128) // (2 * S)
    zpar = lax.rem(zi, S)
    zmate = zi + (S - 1) - 2 * (S - 1) * zpar

    def part_rows(core, par):
        return pl.ds(pl.multiple_of((core * S + par) * part, 16), part)

    def ws_copy(d):
        rows = part_rows(c, zpar)
        return rc(wall.at[0, rows, :], wall.at[d, rows, :], "ws", d, peer(d), r)

    def zf_copy(d, par):
        ref = wall.at[d, part_rows(c, par), :]
        return rc(ref, ref, "zf", d, h, 2 * zmate + c)

    def dd_copy(d, core):
        ref = wall.at[d, pl.ds(pl.multiple_of(core * S * part, 16), S * part), :]
        return rc(ref, ref, "dd", d, h, sib)

    @pl.loop(1, HOPS)
    def _(d):
        ws_copy(d).start()

    @pl.loop(0, HOPS)
    def _(j):
        lanes = lanes_at(j, sub)
        pack4(ft4.at[:, lanes], ftail.at[j])
        unpack4(ftail.at[j], fs.at[:, lanes])

    loc.wait()
    fx0 = pltpu.make_async_copy(fs.at[:, lanes_at(h, sub)], fx.at[0], ss.at[names["loc"]])
    fx0.start()

    def gram(i, g):
        f = fs[:, lanes_at(i, sub)]
        return g + dot_nt(f, f)

    g = lax.fori_loop(0, HOPS, gram, jnp.zeros((128, 128), F32))
    wown = wall[0, wrow, :]
    wown32 = wown.astype(F32)
    g1, g2, g3 = split3(g)
    gw = dot(g1, wown) + dot(g2, wown) + dot(g3, wown)
    s1[r, :, pl.ds(0, hid)] = gw[ONES : ONES + 1, :]
    s1[r, :, pl.ds(hid, hid)] = jnp.sum(gw * wown32, axis=0, keepdims=True)
    rows_start(s1, "s1")

    @pl.loop(1, HOPS - 1)
    def _(d):
        feat_copy(d).start()

    @pl.loop(1, HOPS)
    def _(d):
        ft_copy(d).start()

    gown[...] = g

    @pl.loop(0, HOPS * (sub // 128))
    def _(i):
        d = lax.div(i, sub // 128)
        b = lax.rem(i, sub // 128)
        late = peer(d) - 2
        m = jnp.where(late >= 0, msk[jnp.maximum(late, 0), h * (sub // 128) + b], 1)
        keep[d, :, lanes_at(b, 128)] = jnp.full((16, 128), 0.5 * m.astype(F32)).astype(BF16)

    wcs[...] = jnp.zeros(wcs.shape, F32)
    wcs[pl.ds(0, wc.shape[0]), :] = wc[...].astype(F32)
    cbs[...] = jnp.zeros(cbs.shape, F32)
    cbs[pl.ds(0, 1), pl.ds(0, cb.shape[1])] = cb[...]
    ncls = wc.shape[0]

    @pl.loop(0, hid // 16)
    def _(i):
        rows = lanes_at(i, 16)
        mixed[rows, :] = jnp.zeros((16, sub), F32)
        mi[0, rows, pl.ds(0, big)] = jnp.zeros((16, big), BF16)

    fx0.wait()

    rows_wait(s1, "s1")
    st = total(s1, R)
    mean = st[:, :hid] * inv_n
    var = st[:, hid:] * inv_n - mean * mean
    inv = lax.rsqrt(var + EPS)
    scale = inv * bgain[...]
    ab[0, :, pl.ds(0, hid)] = scale
    ab[0, :, pl.ds(hid, hid)] = bbias[...] - mean * scale

    def ab_copy(d):
        return rc(ab.at[0], ab.at[d], "ab", d, peer(d), r)

    @pl.loop(1, HOPS)
    def _(d):
        ab_copy(d).start()

    def prepare(d):
        a = ab[d, :, pl.ds(0, hid)]
        b = ab[d, :, pl.ds(hid, hid)]
        ws = wall[d, wrow, :].astype(F32) * (a * KAPPA)
        aw[d] = ws[:FP].astype(BF16)
        row = lax.broadcasted_iota(jnp.int32, (128, hid), 0)
        wt = jnp.where(row == ONES, b * KAPPA, ws).T
        hi, lo = split2(wt)
        wl[d, :, pl.ds(0, 128)] = hi
        wl[d, :, pl.ds(128, 128)] = lo

    g_pair = rc(gown.at[lanes_at(1 - c, 64), :], gpr, "gp", 0, h, sib)

    def gz_copy(e, which):
        return rc(gz.at[which], gz.at[which], "gz", e, h, lax.rem(zi + e, Z) * 2 + c)

    def gd_copy(core):
        return rc(gfin.at[core], gfin.at[core], "gd", 0, h, sib)

    @pl.loop(0, HOPS * NT)
    def _(it):
        d = lax.div(it, NT)
        t = lax.rem(it, NT)

        @pl.when(t == 0)
        def _():
            @pl.when(d > 0)
            def _():
                done(feat_copy(d))
                done(ft_copy(d))
                unpack4(frt.at[d], fx.at[d])
                dd_copy(d, c).wait_send()
                dd_copy(d, 1 - c).wait_recv()
                done(ab_copy(d))

            prepare(d)

        if S > 1:

            @pl.when(it == min(1, NT - 1))
            def _():
                @pl.loop(1, HOPS)
                def _(j):
                    done(ws_copy(j))

                zf_copy(1, zpar).start()

        @pl.when(it == min(2, NT - 1))
        def _():
            feat_copy(HOPS - 1).start()

        @pl.when(jnp.logical_and(t == NT - 1, d < HOPS - 1))
        def _():
            if S > 1:
                zf_copy(d + 1, zpar).wait_send()
                zf_copy(d + 1, 1 - zpar).wait_recv()

                @pl.when(d < HOPS - 2)
                def _():
                    zf_copy(d + 2, zpar).start()

            else:
                done(ws_copy(d + 1))
            dd_copy(d + 1, c).start()

        @pl.when(it == 2 * NT)
        def _():
            g_pair.start()

        @pl.when(it == 3 * NT)
        def _():
            done(g_pair)
            gz[zi] = gown[lanes_at(c, 64), :] + gpr[...]

            @functools.partial(each, 1, Z)
            def _(e):
                gz_copy(e, zi).start()

        pit = jnp.maximum(it - 1, 0)
        pd = lax.div(pit, NT)
        pt = lax.rem(pit, NT)
        adds = []
        for u in range(UN):
            adds.append(dot(wall[pd, pl.ds(0, hid), :], mi[pd, :, lanes_at(pt * UN + u, TILE)]))
        for u in range(UN):
            n = lanes_at(t * UN + u, TILE)
            f = fx[d, :, n]
            z = dot(wl[d], jnp.concatenate([f, f], axis=0))
            k = keep[d, :, n]
            k = jnp.concatenate([k] * 4, axis=0)
            for i in range(0, hid, 64):
                g1, d1 = scaled_gelu_slope(z[i : i + 64].astype(BF16))
                g2, d2 = scaled_gelu_slope(g1 * k)
                mi[d, pl.ds(i, 64), n] = g2
                gp[d, pl.ds(i, 64), n] = d1 * d2 * k
        for u in range(UN):
            n = lanes_at(pt * UN + u, TILE)
            mixed[:, n] = mixed[:, n] + adds[u]

    acc0[...] = jnp.zeros(acc0.shape, F32)
    acc1[...] = jnp.zeros(acc1.shape, F32)

    @pl.loop(0, UN)
    def _(u):
        n = lanes_at((NT - 1) * UN + u, TILE)
        mixed[:, n] = mixed[:, n] + dot(wall[HOPS - 1, pl.ds(0, hid), :], mi[HOPS - 1, :, n])

    @pl.loop(0, hid // 32)
    def _(i):
        rows = lanes_at(i, 32)
        x = mixed[rows, :]
        acc0[rows, :] = fold(x)
        acc1[rows, :] = fold(x * x)

    def natural(lo, hi):
        @pl.loop(lo * (hid // 128), hi * (hid // 128))
        def _(i):
            d = lax.div(i, hid // 128)
            k = lanes_at(lax.rem(i, hid // 128), 128)
            wmx[d, k, :] = wall[d, pl.ds(0, hid), k].astype(F32).T.astype(BF16)

    s2h[h, :, pl.ds(0, hid)] = row_of(acc0[...])
    s2h[h, :, pl.ds(hid, hid)] = row_of(acc1[...])
    hops_start(s2h, "s2h")
    natural(0, 2)
    hops_wait(s2h, "s2h")
    s2r[r] = total(s2h, HOPS)
    rows_start(s2r, "s2r")
    natural(2, HOPS)
    wc48 = wcs[pl.ds(0, 48), :].astype(BF16)
    wcNs[...] = wcs[...].T.astype(BF16)
    crow = lax.broadcasted_iota(jnp.int32, (128, 128), 0)
    cbc = jnp.where(crow < ncls, jnp.broadcast_to(cbs[pl.ds(0, 1), :], (128, 128)).T, -1e30)[:48]
    rows_wait(s2r, "s2r")
    st2 = total(s2r, R)
    mean2 = st2[:, :hid] * inv_n
    inv2 = lax.rsqrt(st2[:, hid:] * inv_n - mean2 * mean2 + EPS * 4.0 * KAPPA * KAPPA)
    scale2 = inv2 * gain2[...]
    cols[0] = col_of(scale2)
    cols[1] = col_of(bias2[...] - mean2 * scale2)
    acc0[...] = jnp.zeros(acc0.shape, F32)
    acc1[...] = jnp.zeros(acc1.shape, F32)
    accl[...] = jnp.zeros(accl.shape, F32)
    accw[...] = jnp.zeros(accw.shape, F32)

    o_own = lanes_at(h, sub)

    def lp_copy(d, part):
        n = sub // 2
        return rc(
            lps.at[:, pl.ds(part * n, n)], o_lp.at[:, lanes_at(2 * h + part, n)], "lp", 4 * part + d, peer(d), r
        )

    dlp[...] = jnp.zeros(dlp.shape, BF16)
    HR = 128

    @pl.loop(0, NT)
    def _(t):
        n = lanes_at(t, big)

        if NT > 1:

            @pl.when(t == NT // 2)
            def _():
                @pl.loop(1, HOPS)
                def _(d):
                    lp_copy(d, 0).start()

        @pl.loop(0, hid // HR)
        def _(i):
            rows = lanes_at(i, HR)
            z2 = mixed[rows, n] * spread(cols[0, rows, :], big) + spread(cols[1, rows, :], big)
            gv, dg = gelu_slope(z2)
            hb[rows, :] = gv.astype(BF16)
            dn2[rows, n] = dg

        lg = dot(wc48, hb[...]) + spread(cbc, big)
        lg = lg - jnp.max(lg, axis=0, keepdims=True)
        ex = jnp.exp(lg)
        se = jnp.sum(ex, axis=0, keepdims=True)
        lp = lg - jnp.log(se)
        lps[:, n] = lp.astype(BF16)
        own = lanes_at(h * NT + t, big)
        hit = lax.broadcasted_iota(jnp.int32, (48, big), 0) == lab[:, own]
        accl[pl.ds(48, 48), :] += fold(jnp.where(hit, lp, 0.0))
        dl = ((ex / se - jnp.where(hit, 1.0, 0.0)) * inv_n).astype(BF16)
        accl[pl.ds(0, 48), :] += fold(dl.astype(F32))
        accw[...] += dot_nt(dl, hb[...])
        dlp[pl.ds(0, 48), :] = dl

        @pl.loop(0, hid // HR)
        def _(i):
            rows = lanes_at(i, HR)
            dn = dot(wcNs[rows, :], dlp[...]) * dn2[rows, n]
            dn2[rows, n] = dn
            acc0[rows, :] += fold(dn * mixed[rows, n])
            acc1[rows, :] += fold(dn)

    @pl.loop(1, HOPS)
    def _(d):
        if NT == 1:
            lp_copy(d, 0).start()
        lp_copy(d, 1).start()

    own_lp = pltpu.make_async_copy(lps, o_lp.at[:, o_own], ss.at[names["lp"]])
    own_lp.start()
    s3h[h, :, pl.ds(0, hid)] = row_of(acc0[...])
    s3h[h, :, pl.ds(hid, hid)] = row_of(acc1[...])
    zpad = jnp.zeros((80, 128), F32)
    s3h[h, :, pl.ds(2 * hid, 128)] = row_of(jnp.concatenate([accl[pl.ds(0, 48), :], zpad], axis=0))
    s3h[h, :, pl.ds(2 * hid + 128, 128)] = row_of(jnp.concatenate([accl[pl.ds(48, 48), :], zpad], axis=0))
    hops_start(s3h, "s3h")

    def cwh_copy(d):
        return rc(cwp.at[d], cwh.at[d], "cwh", d, peer(d), r)

    q = hid // HOPS

    @pl.loop(0, HOPS)
    def _(d):
        cwp[d] = accw[:, lanes_at(peer(d), q)].astype(BF16)

    hops_wait(s3h, "s3h")
    s3r[r] = total(s3h, HOPS)
    rows_start(s3r, "s3r")

    @pl.loop(1, HOPS)
    def _(d):
        cwh_copy(d).start()

    rows_wait(s3r, "s3r")
    st3 = total(s3r, R)
    db2 = st3[:, hid : 2 * hid]
    dg2t = inv2 * (st3[:, :hid] - mean2 * db2)
    o_small[pl.ds(0, 1), :] = dg2t
    o_small[pl.ds(1, 1), :] = db2
    o_small[pl.ds(4, 1), pl.ds(0, 256)] = st3[:, 2 * hid : 2 * hid + 256]
    o_small[pl.ds(4, 1), pl.ds(256, hid - 256)] = jnp.zeros((1, hid - 256), F32)
    t2 = scale2 * inv2 * dg2t * inv_n
    cols[1] = col_of(-t2)
    cols[2] = col_of(t2 * mean2 - scale2 * db2 * inv_n)

    @pl.loop(0, hid // 16)
    def _(i):
        rows = lanes_at(i, 16)
        v = dn2[rows, :] * spread(cols[0, rows, :], sub)
        v = v + mixed[rows, :] * spread(cols[1, rows, :], sub) + spread(cols[2, rows, :], sub)
        dmx[rows, :] = v.astype(BF16)

    @functools.partial(each, 1, Z)
    def _(e):
        gz_copy(e, zi).wait_send()
        gz_copy(e, lax.rem(zi + Z - e, Z)).wait_recv()

    gfin[c] = total(gz, Z)
    gd_copy(c).start()

    mine = lanes_at(c, half)
    theirs = lanes_at(1 - c, half)

    def pair_copy(d):
        return rc(dmp.at[d, theirs, :], pr.at[d], "pair", d, h, sib)

    qrows = half // S
    zown = pl.ds(pl.multiple_of(c * half + zpar * qrows, 16), qrows)
    zother = pl.ds(pl.multiple_of(c * half + (1 - zpar) * qrows, 16), qrows)

    def z1_copy(d):
        return rc(dmp.at[d, zother, :], z1r.at[d], "z1", d, h, 2 * zmate + c)

    def z1_start(d):
        if S > 1:
            z1_copy(d).start()

    def z1_sum(d):
        if S > 1:
            done(z1_copy(d))

            @pl.loop(0, qrows // 32)
            def _(i):
                rows = pl.ds(pl.multiple_of(c * half + zpar * qrows + i * 32, 32), 32)
                dmp[d, rows, :] = (dmp[d, rows, :].astype(F32) + z1r[d, lanes_at(i, 32), :].astype(F32)).astype(BF16)

    def hop_copy(d):
        return rc(dmp.at[d, zown, :], hr.at[d], "hop", d, peer(d), r)

    def pair_sum(d):
        done(pair_copy(d))

        @pl.loop(0, half // 32)
        def _(i):
            rows = pl.ds(pl.multiple_of(c * half + i * 32, 32), 32)
            dmp[d, rows, :] = (dmp[d, rows, :].astype(F32) + pr[d, lanes_at(i, 32), :].astype(F32)).astype(BF16)

    @pl.loop(0, HOPS)
    def _(i):
        d = HOPS - 1 - i

        dmp[d] = dot_nt(mi[d], dmx[...]).astype(BF16)
        pair_copy(d).start()

        @pl.when(i > 0)
        def _():
            pair_sum(d + 1)
            z1_start(d + 1)

        @pl.when(i > 1)
        def _():
            z1_sum(d + 2)
            hop_copy(d + 2).start()

    G2 = Z // S
    zq = lax.div(zi, S)

    def zr_copy(e, which):
        rows, lanes = chunk(0, which, qrows, G2, hid)
        return rc(hr.at[0, rows, lanes], zr.at[e], "zr", e, h, (lax.rem(zq + e, G2) * S + zpar) * 2 + c)

    def final_chunk(z):
        return chunk(c * half + lax.rem(z, S) * qrows, lax.div(z, S), qrows, G2, hid)

    def zg_copy(e, which):
        rows, lanes = final_chunk(which)
        ref = fin.at[rows, lanes]
        return rc(ref, ref, "zg", e, h, lax.rem(zi + e, Z) * 2 + c)

    def ddm_copy(core):
        ref = fin.at[lanes_at(core, half), :]
        return rc(ref, ref, "ddm", 0, h, sib)

    def d_copy(d):
        return rc(dsend.at[d], o_d.at[h], "d", d, peer(d), r)

    def dt_copy(d):
        return rc(dtail.at[d], o_dt.at[h], "dt", d, peer(d), r)

    def pp_copy(d):
        return rc(ps.at[d, :, theirs], ph.at[d], "pp", d, h, sib)

    def p_copy(d):
        return rc(phalf.at[d], prv.at[d], "p", d, peer(d), r)

    def p_half(d):
        done(pp_copy(d))
        phalf[d] = (ps[d, :, mine].astype(F32) + ph[d].astype(F32)).astype(BF16)

    def q_copy(d):
        return rc(qs.at[d], qv.at[d], "q", d, peer(d), r)

    @pl.loop(0, HOPS * NT)
    def _(it):
        dd = lax.div(it, NT)
        t = lax.rem(it, NT)
        d = HOPS - 1 - dd

        @pl.when(t == 0)
        def _():
            pT[...] = jnp.zeros(pT.shape, F32)

        @pl.when(jnp.logical_and(t == NT // 2, dd > 0))
        def _():
            p_half(d + 1)
            p_copy(d + 1).start()

        @pl.when(it == NT // 2)
        def _():
            pair_sum(0)
            z1_start(0)
            z1_sum(1)
            hop_copy(1).start()

        @pl.when(it == NT + NT // 2)
        def _():
            @pl.loop(1, HOPS)
            def _(j):
                done(cwh_copy(j))

            cw = cwp[0].astype(F32)
            for j in range(1, HOPS):
                cw = cw + cwh[j].astype(F32)
            cwr[r] = cw.astype(BF16)
            rows_start(cwr, "cwr")
            z1_sum(0)

        @pl.when(it == 2 * NT + NT // 2)
        def _():
            @pl.loop(1, HOPS)
            def _(j):
                done(hop_copy(j))

            @pl.loop(0, qrows // 32)
            def _(i):
                rows = lanes_at(i, 32)
                own = pl.ds(pl.multiple_of(c * half + zpar * qrows + i * 32, 32), 32)
                hsum = dmp[0, own, :].astype(F32)
                for j in range(1, HOPS):
                    hsum = hsum + hr[j, rows, :].astype(F32)
                hr[0, rows, :] = hsum.astype(BF16)

            @functools.partial(each, 1, G2)
            def _(e):
                zr_copy(e, lax.rem(zq + e, G2)).start()

            rows_wait(cwr, "cwr")
            cwg[h] = total(cwr, R, F32).astype(BF16)
            hops_start(cwg, "cwg")

        @pl.when(it == 3 * NT + NT // 2)
        def _():
            @functools.partial(each, 1, G2)
            def _(e):
                done(zr_copy(e, lax.rem(zq + e, G2)))

            rows, lanes = chunk(0, zq, qrows, G2, hid)
            zt = lax.fori_loop(1, G2, lambda e, v: v + zr[e].astype(F32), hr[0, rows, lanes].astype(F32))
            frows, flanes = final_chunk(zi)
            fin[frows, flanes] = zt.astype(BF16)

            @functools.partial(each, 1, Z)
            def _(e):
                zg_copy(e, zi).start()

            hops_wait(cwg, "cwg")
            for j in range(HOPS):
                o_cw[:, pl.ds(j * q, q)] = cwg[j].astype(F32)

        n = lanes_at(t, big)
        dn = dot(wmx[d], dmx[:, n]).astype(BF16) * gp[d, :, n]
        pT[...] += dot_nt(dn, fx[d, :, n])
        grad = dot(aw[d], dn)
        dsend[d, :, n] = grad[:MAIN].astype(BF16)
        d4[:, n] = grad[MAIN : MAIN + 8]

        @pl.when(t == NT - 1)
        def _():
            pw = pT[...].T * KAPPA
            qs[d, :, pl.ds(0, hid)] = jnp.sum(pw * wall[d, wrow, :].astype(F32), axis=0, keepdims=True)
            qs[d, :, pl.ds(hid, hid)] = pw[ONES : ONES + 1, :]
            ps[d] = pw[:FP].astype(BF16)
            pp_copy(d).start()
            pack4(d4, dtail.at[d])

            @pl.when(dd < HOPS - 1)
            def _():
                q_copy(d).start()
                d_copy(d).start()
                dt_copy(d).start()

    @pl.loop(1, HOPS)
    def _(d):
        done(q_copy(d))

    qr[r] = qs[0] + (qv[1] + qv[2] + qv[3])
    rows_start(qr, "qr")
    own_d = pltpu.make_async_copy(dsend.at[0], o_d.at[h], ss.at[names["d"]])
    own_d.start()
    own_dt = pltpu.make_async_copy(dtail.at[0], o_dt.at[h], ss.at[names["dt"]])
    own_dt.start()

    p_half(0)

    @pl.loop(1, HOPS)
    def _(d):
        done(p_copy(d))

    psum = phalf[0].astype(F32) + (prv[1].astype(F32) + prv[2].astype(F32) + prv[3].astype(F32))
    pz[zi] = psum.astype(BF16)

    def pz_copy(e, which):
        return rc(pz.at[which], pz.at[which], "pz", e, h, lax.rem(zi + e, Z) * 2 + c)

    @functools.partial(each, 1, Z)
    def _(e):
        pz_copy(e, zi).start()

    @functools.partial(each, 1, Z)
    def _(e):
        zg_copy(e, zi).wait_send()
        zg_copy(e, lax.rem(zi + Z - e, Z)).wait_recv()

    ddm_copy(c).start()

    rows_wait(qr, "qr")
    qt = total(qr, R)
    db = qt[:, hid:]
    dgn = inv * (qt[:, :hid] - mean * db)
    o_small[pl.ds(2, 1), :] = dgn
    o_small[pl.ds(3, 1), :] = db
    c1 = scale * db * inv_n
    c2 = inv * scale * dgn * inv_n
    shift = c1 - mean * c2
    row = lax.broadcasted_iota(jnp.int32, (128, hid), 0)
    q1, q2 = split2(jnp.where(row == ONES, shift, wown32 * c2))
    o_m[...] = (dot_nt(wown, q1) + dot_nt(wown, q2))[:FP]
    gd_copy(c).wait_send()
    gd_copy(1 - c).wait_recv()
    g1, g2, g3 = split3(jnp.concatenate([gfin[0], gfin[1]], axis=0))
    gq = dot(g1, q1) + dot(g2, q1) + dot(g3, q1) + dot(g1, q2) + dot(g2, q2)

    @functools.partial(each, 1, Z)
    def _(e):
        pz_copy(e, zi).wait_send()
        pz_copy(e, lax.rem(zi + Z - e, Z)).wait_recv()

    pfin[c] = total(pz, Z).astype(BF16)

    def pd_copy(core):
        return rc(pfin.at[core], pfin.at[core], "pd", 0, h, sib)

    pd_copy(c).start()
    ddm_copy(c).wait_send()
    ddm_copy(1 - c).wait_recv()
    o_mix[...] = fin[...]

    pd_copy(c).wait_send()
    pd_copy(1 - c).wait_recv()
    ptot = jnp.concatenate([pfin[0], pfin[1]], axis=1).astype(F32)
    o_gw[...] = ptot * scale - gq[:FP]
    own_d.wait()
    own_dt.wait()
    own_lp.wait()

    @pl.loop(1, HOPS)
    def _(d):
        done(d_copy(d))
        done(dt_copy(d))
        done(lp_copy(d, 0))
        done(lp_copy(d, 1))


def last_kernel(
    nodes,
    ft, d, dt, lp, m, mix, gw, small, cw,
    o_lp, o_gf, o_mix, o_gw, o_gg, o_gb, o_hg, o_hb, o_cw, o_cb, o_loss, low,
):
    feat, n = ft.shape
    ncls = o_lp.shape[0]
    o_lp[...] = lp[...].astype(F32)[:ncls]
    mm = m[...]
    f = ft[...]
    fix = dot(mm[:, :feat].astype(BF16), f) + mm[:, ONES : ONES + 1]
    tail = dt[0].astype(F32)
    for b in range(4):
        low[pl.ds(0, 4), pl.ds(b * (n // 4), n // 4)] = tail[4 * b : 4 * b + 4]
    gf = jnp.concatenate([d[0].astype(F32), low[...]], axis=0)[:feat] - fix[:feat]
    if STRIDED:
        flat = o_gf.reshape(feat * (n // 128), 128)
        for i in range(n // 128):
            flat[pl.ds(i, feat, stride=n // 128), :] = gf[:, i * 128 : (i + 1) * 128]
    else:
        for i in range(n // 128):
            o_gf[:, i, :] = gf[:, i * 128 : (i + 1) * 128]

    @pl.when(pl.program_id(0) == 0)
    def _():
        hid = mix.shape[1]
        o_mix[...] = mix[...].astype(F32)
        for i in range(hid // 128):
            o_gw[:, i, :] = gw[pl.ds(0, feat), pl.ds(i * 128, 128)]
        o_hg[...] = small[pl.ds(0, 1), :]
        o_hb[...] = small[pl.ds(1, 1), :]
        o_gg[...] = small[pl.ds(2, 1), :]
        o_gb[...] = small[pl.ds(3, 1), :]
        o_cw[...] = cw[pl.ds(0, ncls), :]
        o_cb[...] = small[pl.ds(4, 1), pl.ds(0, ncls)]
        o_loss[...] = jnp.sum(small[pl.ds(4, 1), pl.ds(128, 128)], axis=1, keepdims=True) * (-1.0 / nodes)


def shards(
    R, features, branch_weight, branch_gain, branch_bias, mix_weight, mixing_norm_gain, mixing_norm_bias,
    class_weight, class_bias, labels, hop_mask,
):
    local, feat = features.shape[1:]
    hid = mix_weight.shape[0]
    ncls = class_weight.shape[1]
    nodes = local * R
    sub = local // HOPS
    Z = R // 2
    half = hid // 2
    S = min(Z, 2)
    G2, qrows = Z // S, half // S
    zrows, zcols = chunk(0, 0, qrows, G2, hid)
    assert feat == ONES and ncls == 47 and local // hop_mask.shape[0] == 128
    ft = features[0].T
    sd = jax.ShapeDtypeStruct
    vm = pl.BlockSpec(memory_space=pltpu.VMEM)
    hbm = pl.BlockSpec(memory_space=pl.ANY)
    _, nsem = sem_plan(R)
    V = pltpu.VMEM
    outs = pl.pallas_call(
        functools.partial(main_kernel, R, nodes),
        grid=(1,),
        out_shape=(
            sd((48, local), BF16),
            sd((HOPS, MAIN, sub), BF16),
            sd((HOPS, 16, sub // 4), BF16),
            sd((FP, 128), F32),
            sd((hid, hid), BF16),
            sd((FP, hid), F32),
            sd((8, hid), F32),
            sd((48, hid), F32),
        ),
        in_specs=[hbm, pl.BlockSpec((16, local), lambda i: (MAIN // 16, 0))]
        + [vm] * 9
        + [pl.BlockSpec(memory_space=pltpu.SMEM)],
        out_specs=(hbm, hbm, hbm, vm, vm, vm, vm, vm),
        scratch_shapes=[
            V((128, local), BF16),
            V((HOPS, 128, sub), BF16),
            V((HOPS, 16, sub // 4), BF16),
            V((HOPS, 16, sub // 4), BF16),
            V((48, sub // 4), F32),
            V((HOPS, hid + 128, hid), BF16),
            V((HOPS, hid, 256), BF16),
            V((HOPS, FP, hid), BF16),
            V((HOPS, hid, hid), BF16),
            V((HOPS, 16, sub), BF16),
            V((HOPS, hid, sub), BF16),
            V((HOPS, hid, sub), BF16),
            V((hid, sub), F32),
            V((hid, sub), F32),
            V((hid, sub), BF16),
            V((128, 128), F32),
            V((64, 128), F32),
            V((Z, 64, 128), F32),
            V((2, 64, 128), F32),
            V((R, 1, 2 * hid), F32),
            V((HOPS, 1, 2 * hid), F32),
            V((HOPS, 1, 2 * hid), F32),
            V((R, 1, 2 * hid), F32),
            V((HOPS, 1, 2 * hid + 256), F32),
            V((R, 1, 2 * hid + 256), F32),
            V((HOPS, 48, hid // HOPS), BF16),
            V((HOPS, 48, hid // HOPS), BF16),
            V((R, 48, hid // HOPS), BF16),
            V((HOPS, 48, hid // HOPS), BF16),
            V((48, sub), BF16),
            V((128, hid), F32),
            V((hid, 128), BF16),
            V((8, 128), F32),
            V((hid, min(2 * TILE, sub)), BF16),
            V((128, min(2 * TILE, sub)), BF16),
            V((hid, 128), F32),
            V((hid, 128), F32),
            V((96, 128), F32),
            V((48, hid), F32),
            V((3, hid, 128), F32),
            V((HOPS, hid, hid), BF16),
            V((HOPS, half, hid), BF16),
            V((HOPS, qrows, hid), BF16),
            V((HOPS, qrows, hid), BF16),
            V((max(G2, 2), zrows.size, zcols.size), BF16),
            V((hid, hid), BF16),
            V((HOPS, MAIN, sub), BF16),
            V((8, sub), F32),
            V((HOPS, 16, sub // 4), BF16),
            V((hid, 128), F32),
            V((HOPS, FP, hid), BF16),
            V((HOPS, FP, half), BF16),
            V((HOPS, FP, half), BF16),
            V((HOPS, FP, half), BF16),
            V((HOPS, 1, 2 * hid), F32),
            V((HOPS, 1, 2 * hid), F32),
            V((R, 1, 2 * hid), F32),
            V((Z, FP, half), BF16),
            V((2, FP, half), BF16),
            pltpu.SemaphoreType.DMA((nsem,)),
            pltpu.SemaphoreType.DMA((nsem,)),
        ],
        compiler_params=pltpu.CompilerParams(
            collective_id=0, has_side_effects=True, vmem_limit_bytes=63 * 1024 * 1024
        ),
        cost_estimate=pl.CostEstimate(flops=2 * 8 * 10**9, bytes_accessed=10**7, transcendentals=10**7),
        name="main",
    )(
        ft, ft, branch_weight[0], branch_gain, branch_bias, mix_weight, mixing_norm_gain[None], mixing_norm_bias[None],
        class_weight.T, class_bias[None], labels[None], hop_mask.T,
    )
    lp, dd, dt, m, mix, gw, small, cw = outs
    nb = sub
    whole = lambda shape: pl.BlockSpec(shape, lambda i: (0,) * len(shape))
    lp, gf, mix, gw, gg, gb, hg, hb, cw, cb, loss = pl.pallas_call(
        functools.partial(last_kernel, nodes),
        grid=(local // nb,),
        out_shape=(
            sd((ncls, local), F32),
            sd((feat, local // 128, 128), F32),
            sd((hid, hid), F32),
            sd((feat, hid // 128, 128), F32),
            sd((1, hid), F32),
            sd((1, hid), F32),
            sd((1, hid), F32),
            sd((1, hid), F32),
            sd((ncls, hid), F32),
            sd((1, ncls), F32),
            sd((1, 1), F32),
        ),
        in_specs=[
            pl.BlockSpec((feat, nb), lambda i: (0, i)),
            pl.BlockSpec((1, MAIN, nb), lambda i: (i, 0, 0)),
            pl.BlockSpec((1, 16, nb // 4), lambda i: (i, 0, 0)),
            pl.BlockSpec((48, nb), lambda i: (0, i)),
            whole((FP, 128)),
            whole((hid, hid)),
            whole((FP, hid)),
            whole((8, hid)),
            whole((48, hid)),
        ],
        out_specs=(
            pl.BlockSpec((ncls, nb), lambda i: (0, i)),
            pl.BlockSpec((feat, nb // 128, 128), lambda i: (0, i, 0)),
            whole((hid, hid)),
            whole((feat, hid // 128, 128)),
            whole((1, hid)),
            whole((1, hid)),
            whole((1, hid)),
            whole((1, hid)),
            whole((ncls, hid)),
            whole((1, ncls)),
            whole((1, 1)),
        ),
        scratch_shapes=[V((8, nb), F32)],
        compiler_params=pltpu.CompilerParams(vmem_limit_bytes=60 * 1024 * 1024),
        name="last",
    )(ft, dd, dt, lp, m, mix, gw, small, cw)
    return (
        lp.T,
        loss[0, 0],
        with_layout_constraint(gf.reshape(feat, 1, local), Layout((0, 1, 2))).transpose(1, 2, 0),
        gw.reshape(1, feat, hid),
        gg,
        gb,
        mix,
        hg[0],
        hb[0],
        cw.T,
        cb[0],
    )


def solution(mesh):
    placed = (
        P("hop", "rows", None), P("hop", None, None), P("hop", None), P("hop", None), P("hop", None),
        P(), P(), P(), P(), P("rows"), P("rows", None),
    )
    assert mesh.shape["hop"] == HOPS
    return jax.shard_map(
        functools.partial(shards, mesh.shape["rows"]),
        mesh=mesh,
        in_specs=placed,
        out_specs=(
            P("rows", None), P(), P("hop", "rows", None), P("hop", None, None), P("hop", None), P("hop", None),
            P("hop", None), P(), P(), P(), P(),
        ),
        check_vma=False,
    )
```

```python
import functools
import math

import jax
import jax.numpy as jnp
from jax import lax
from jax.experimental import pallas as pl
from jax.experimental.layout import Layout, with_layout_constraint
from jax.experimental.pallas import tpu as pltpu
from jax.sharding import PartitionSpec as P

MESH = pl.DeviceIdType.MESH
EPS = 1e-05
HOPS = 4
ONES = 100
FP = 112
MAIN = 96
TILE = 256
STRIDED = True
C0 = math.sqrt(2.0 / math.pi)
C1 = C0 * 0.044715
KAPPA = C1 ** (1.0 / 3.0)
ALPHA = C0 / KAPPA
F32 = jnp.float32
BF16 = jnp.bfloat16


def dot(a, b):
    return lax.dot_general(a, b, (((1,), (0,)), ((), ())), preferred_element_type=F32)


def dot_nt(a, b):
    return lax.dot_general(a, b, (((1,), (1,)), ((), ())), preferred_element_type=F32)


def split2(x):
    hi = x.astype(BF16)
    return hi, (x - hi.astype(F32)).astype(BF16)


def split3(x):
    hi = x.astype(BF16)
    rest = x - hi.astype(F32)
    mid = rest.astype(BF16)
    return hi, mid, (rest - mid.astype(F32)).astype(BF16)


def gelu_slope(z):
    u = z * z
    t = jnp.tanh(z * (C0 + C1 * u))
    s = 0.5 * t + 0.5
    g = z * s
    return g, s + (g - g * s) * (2.0 * C0 + 6.0 * C1 * u)


def scaled_gelu_slope(y):
    u = y * y
    t = jnp.tanh(y * (u + ALPHA))
    up = t + 1.0
    g = y * up
    return g, up + (g * (1.0 - t)) * (3.0 * u + ALPHA)


def fold(x):
    total = x[:, :128]
    for i in range(1, x.shape[1] // 128):
        total = total + x[:, i * 128 : (i + 1) * 128]
    return total


def spread(c, n):
    return jnp.concatenate([c] * (n // 128), axis=1)


def row_of(acc):
    return jnp.sum(acc.T, axis=0, keepdims=True)


def col_of(row):
    return jnp.broadcast_to(row, (128, row.shape[1])).T


def each(lo, hi, body):
    if hi - lo == 1:
        body(lo)
    elif hi > lo:
        pl.loop(lo, hi)(body)


class Alloc:
    def __init__(self):
        self.n = 0

    def __call__(self, count):
        base = self.n
        self.n += count
        return base


def sem_plan(R):
    Z = R // 2
    a = Alloc()
    names = {}
    for name, count in (
        ("feat", 4), ("ft", 4), ("loc", 1), ("ws", 4), ("zf", 4), ("dd", 4), ("s1", R), ("ab", 4), ("gp", 1), ("gz", Z), ("gd", 1),
        ("s2h", 4), ("s2r", R), ("s3h", 4), ("s3r", R), ("lp", 8), ("cwh", 4), ("cwr", R), ("cwg", 4),
        ("pair", 4), ("z1", 4), ("hop", 4), ("zr", Z), ("zg", Z), ("ddm", 1), ("d", 4), ("dt", 4), ("p", 4), ("q", 4),
        ("qr", R), ("pp", 4), ("pz", Z), ("pd", 1),
    ):
        names[name] = a(count)
    return names, a.n


def chunk(base, i, rows, pieces, cols):
    if rows // pieces >= 16:
        take = rows // pieces
        return pl.ds(pl.multiple_of(base + i * take, 16), take), pl.ds(0, cols)
    m = 16 * pieces // rows
    wide = cols // m
    return (
        pl.ds(pl.multiple_of(base + (i // m) * 16, 16), 16),
        pl.ds(pl.multiple_of((i % m) * wide, 128), wide),
    )


def main_kernel(
    R,
    nodes,
    ft, ft4, wb, bgain, bbias, wm, gain2, bias2, wc, cb, lab, msk,
    o_lp, o_d, o_dt, o_m, o_mix, o_gw, o_small, o_cw,
    fs, fx, ftail, frt, st4, wall, wl, aw, wmx, keep, mi, gp, mixed, dn2, dmx,
    gown, gpr, gz, gfin, s1, ab, s2h, s2r, s3h, s3r, cwp, cwh, cwr, cwg, lps,
    wcs, wcNs, cbs, hb, dlp, acc0, acc1, accl, accw, cols,
    dmp, pr, z1r, hr, zr, fin, dsend, d4, dtail, pT, ps, ph, phalf, prv, qs, qv, qr, pz, pfin,
    ss, rs,
):
    names, _ = sem_plan(R)
    Z = R // 2
    h = lax.axis_index("hop")
    r = lax.axis_index("rows")
    c = lax.rem(r, 2)
    zi = lax.div(r, 2)
    sib = r + 1 - 2 * c
    local = ft.shape[1]
    sub = local // HOPS
    hid = wm.shape[0]
    half = hid // 2
    big = min(2 * TILE, sub)
    UN = big // TILE
    NT = sub // big
    inv_n = 1.0 / nodes

    def peer(d):
        x = lax.rem(h + d, 2)
        y = lax.rem(lax.div(h, 2) + lax.div(d, 2), 2)
        return 2 * y + x

    def rc(src, dst, name, i, hh, rr):
        return pltpu.make_async_remote_copy(
            src_ref=src, dst_ref=dst, send_sem=ss.at[names[name] + i], recv_sem=rs.at[names[name] + i],
            device_id=(hh, rr), device_id_type=MESH,
        )

    def done(cp):
        cp.wait_send()
        cp.wait_recv()

    def lanes_at(i, n):
        return pl.ds(pl.multiple_of(i * n, n), n)

    barrier = pltpu.get_barrier_semaphore()

    def greet(hh, rr):
        pl.semaphore_signal(barrier, inc=1, device_id=(hh, rr), device_id_type=MESH)

    @pl.loop(1, HOPS)
    def _(d):
        greet(peer(d), r)

    @functools.partial(each, 1, R)
    def _(e):
        greet(h, lax.rem(r + e, R))

    def rows_start(buf, name):
        @functools.partial(each, 1, R)
        def _(e):
            rc(buf.at[r], buf.at[r], name, e, h, lax.rem(r + e, R)).start()

    def rows_wait(buf, name):
        @functools.partial(each, 1, R)
        def _(e):
            src = lax.rem(r + R - e, R)
            done(rc(buf.at[src], buf.at[src], name, e, h, lax.rem(r + e, R)))

    def hops_start(buf, name):
        @pl.loop(1, HOPS)
        def _(d):
            rc(buf.at[h], buf.at[h], name, d, peer(d), r).start()

    def hops_wait(buf, name):
        @pl.loop(1, HOPS)
        def _(d):
            done(rc(buf.at[peer(d)], buf.at[peer(d)], name, d, peer(d), r))

    def total(buf, n, dtype=F32):
        return lax.fori_loop(1, n, lambda i, t: t + buf[i].astype(dtype), buf[0].astype(dtype))

    loc = pltpu.make_async_copy(ft.at[pl.ds(0, MAIN), :], fs.at[pl.ds(0, MAIN), :], ss.at[names["loc"]])
    loc.start()

    def pack4(src, dst):
        n = st4.shape[1]
        for b in range(4):
            st4[pl.ds(4 * b, 4), :] = src[pl.ds(0, 4), pl.ds(b * n, n)].astype(F32)
        dst[...] = st4[pl.ds(0, 16), :].astype(BF16)

    def unpack4(src, dst):
        n = st4.shape[1]
        row = lax.broadcasted_iota(jnp.int32, (32, n), 0)
        st4[pl.ds(0, 16), :] = src[...].astype(F32)
        st4[pl.ds(16, 32), :] = jnp.where(row == ONES - MAIN, 1.0, 0.0)
        for b in range(4):
            st4[pl.ds(16, 4), :] = st4[pl.ds(4 * b, 4), :]
            dst[pl.ds(MAIN, 32), pl.ds(b * n, n)] = st4[pl.ds(16, 32), :].astype(BF16)

    def feat_copy(d):
        rows = pl.ds(0, MAIN)
        return rc(ft.at[rows, lanes_at(peer(d), sub)], fx.at[d, rows, :], "feat", d, peer(d), r)

    def ft_copy(d):
        return rc(ftail.at[peer(d)], frt.at[d], "ft", d, peer(d), r)

    pl.semaphore_wait(barrier, HOPS - 1 + R - 1)

    @pl.loop(1, HOPS)
    def _(d):
        feat_copy(d).start()

    wrow = pl.ds(hid, 128)
    wall[0, pl.ds(hid + 96, 32), :] = jnp.zeros((32, hid), BF16)
    wall[0, pl.ds(hid, 100), :] = wb[...]

    @pl.loop(0, hid // 128)
    def _(i):
        k = lanes_at(i, 128)
        wall[0, pl.ds(0, hid), k] = wm[k, :].astype(F32).T.astype(BF16)

    S = min(Z, 2)
    part = (hid + 128) // (2 * S)
    zpar = lax.rem(zi, S)
    zmate = zi + (S - 1) - 2 * (S - 1) * zpar

    def part_rows(core, par):
        return pl.ds(pl.multiple_of((core * S + par) * part, 16), part)

    def ws_copy(d):
        rows = part_rows(c, zpar)
        return rc(wall.at[0, rows, :], wall.at[d, rows, :], "ws", d, peer(d), r)

    def zf_copy(d, par):
        ref = wall.at[d, part_rows(c, par), :]
        return rc(ref, ref, "zf", d, h, 2 * zmate + c)

    def dd_copy(d, core):
        ref = wall.at[d, pl.ds(pl.multiple_of(core * S * part, 16), S * part), :]
        return rc(ref, ref, "dd", d, h, sib)

    @pl.loop(1, HOPS)
    def _(d):
        ws_copy(d).start()

    @pl.loop(0, HOPS)
    def _(j):
        lanes = lanes_at(j, sub)
        pack4(ft4.at[:, lanes], ftail.at[j])
        unpack4(ftail.at[j], fs.at[:, lanes])

    @pl.loop(1, HOPS)
    def _(d):
        ft_copy(d).start()

    loc.wait()
    fx0 = pltpu.make_async_copy(fs.at[:, lanes_at(h, sub)], fx.at[0], ss.at[names["loc"]])
    fx0.start()

    def gram(i, g):
        f = fs[:, lanes_at(i, sub)]
        return g + dot_nt(f, f)

    g = lax.fori_loop(0, HOPS, gram, jnp.zeros((128, 128), F32))
    wown = wall[0, wrow, :]
    wown32 = wown.astype(F32)
    g1, g2, g3 = split3(g)
    gw = dot(g1, wown) + dot(g2, wown) + dot(g3, wown)
    s1[r, :, pl.ds(0, hid)] = gw[ONES : ONES + 1, :]
    s1[r, :, pl.ds(hid, hid)] = jnp.sum(gw * wown32, axis=0, keepdims=True)
    rows_start(s1, "s1")
    gown[...] = g

    @pl.loop(0, HOPS * (sub // 128))
    def _(i):
        d = lax.div(i, sub // 128)
        b = lax.rem(i, sub // 128)
        late = peer(d) - 2
        m = jnp.where(late >= 0, msk[jnp.maximum(late, 0), h * (sub // 128) + b], 1)
        keep[d, :, lanes_at(b, 128)] = jnp.full((16, 128), 0.5 * m.astype(F32)).astype(BF16)

    wcs[...] = jnp.zeros(wcs.shape, F32)
    wcs[pl.ds(0, wc.shape[0]), :] = wc[...].astype(F32)
    cbs[...] = jnp.zeros(cbs.shape, F32)
    cbs[pl.ds(0, 1), pl.ds(0, cb.shape[1])] = cb[...]
    ncls = wc.shape[0]

    @pl.loop(0, hid // 16)
    def _(i):
        rows = lanes_at(i, 16)
        mixed[rows, :] = jnp.zeros((16, sub), F32)
        mi[0, rows, pl.ds(0, big)] = jnp.zeros((16, big), BF16)

    fx0.wait()

    rows_wait(s1, "s1")
    st = total(s1, R)
    mean = st[:, :hid] * inv_n
    var = st[:, hid:] * inv_n - mean * mean
    inv = lax.rsqrt(var + EPS)
    scale = inv * bgain[...]
    ab[0, :, pl.ds(0, hid)] = scale
    ab[0, :, pl.ds(hid, hid)] = bbias[...] - mean * scale

    def ab_copy(d):
        return rc(ab.at[0], ab.at[d], "ab", d, peer(d), r)

    @pl.loop(1, HOPS)
    def _(d):
        ab_copy(d).start()

    def prepare(d):
        a = ab[d, :, pl.ds(0, hid)]
        b = ab[d, :, pl.ds(hid, hid)]
        ws = wall[d, wrow, :].astype(F32) * (a * KAPPA)
        aw[d] = ws[:FP].astype(BF16)
        row = lax.broadcasted_iota(jnp.int32, (128, hid), 0)
        wt = jnp.where(row == ONES, b * KAPPA, ws).T
        hi, lo = split2(wt)
        wl[d, :, pl.ds(0, 128)] = hi
        wl[d, :, pl.ds(128, 128)] = lo

    g_pair = rc(gown.at[lanes_at(1 - c, 64), :], gpr, "gp", 0, h, sib)

    def gz_copy(e, which):
        return rc(gz.at[which], gz.at[which], "gz", e, h, lax.rem(zi + e, Z) * 2 + c)

    def gd_copy(core):
        return rc(gfin.at[core], gfin.at[core], "gd", 0, h, sib)

    @pl.loop(0, HOPS * NT)
    def _(it):
        d = lax.div(it, NT)
        t = lax.rem(it, NT)

        @pl.when(t == 0)
        def _():
            @pl.when(d > 0)
            def _():
                done(feat_copy(d))
                done(ft_copy(d))
                unpack4(frt.at[d], fx.at[d])
                dd_copy(d, c).wait_send()
                dd_copy(d, 1 - c).wait_recv()
                done(ab_copy(d))

            prepare(d)

        if S > 1:

            @pl.when(it == min(1, NT - 1))
            def _():
                @pl.loop(1, HOPS)
                def _(j):
                    done(ws_copy(j))

                zf_copy(1, zpar).start()

        @pl.when(jnp.logical_and(t == NT - 1, d < HOPS - 1))
        def _():
            if S > 1:
                zf_copy(d + 1, zpar).wait_send()
                zf_copy(d + 1, 1 - zpar).wait_recv()

                @pl.when(d < HOPS - 2)
                def _():
                    zf_copy(d + 2, zpar).start()

            else:
                done(ws_copy(d + 1))
            dd_copy(d + 1, c).start()

        @pl.when(it == 2 * NT)
        def _():
            g_pair.start()

        @pl.when(it == 3 * NT)
        def _():
            done(g_pair)
            gz[zi] = gown[lanes_at(c, 64), :] + gpr[...]

            @functools.partial(each, 1, Z)
            def _(e):
                gz_copy(e, zi).start()

        pit = jnp.maximum(it - 1, 0)
        pd = lax.div(pit, NT)
        pt = lax.rem(pit, NT)
        adds = []
        for u in range(UN):
            adds.append(dot(wall[pd, pl.ds(0, hid), :], mi[pd, :, lanes_at(pt * UN + u, TILE)]))
        for u in range(UN):
            n = lanes_at(t * UN + u, TILE)
            f = fx[d, :, n]
            z = dot(wl[d], jnp.concatenate([f, f], axis=0))
            k = keep[d, :, n]
            k = jnp.concatenate([k] * 4, axis=0)
            for i in range(0, hid, 64):
                g1, d1 = scaled_gelu_slope(z[i : i + 64].astype(BF16))
                g2, d2 = scaled_gelu_slope(g1 * k)
                mi[d, pl.ds(i, 64), n] = g2
                gp[d, pl.ds(i, 64), n] = d1 * d2 * k
        for u in range(UN):
            n = lanes_at(pt * UN + u, TILE)
            mixed[:, n] = mixed[:, n] + adds[u]

    acc0[...] = jnp.zeros(acc0.shape, F32)
    acc1[...] = jnp.zeros(acc1.shape, F32)

    @pl.loop(0, UN)
    def _(u):
        n = lanes_at((NT - 1) * UN + u, TILE)
        mixed[:, n] = mixed[:, n] + dot(wall[HOPS - 1, pl.ds(0, hid), :], mi[HOPS - 1, :, n])

    @pl.loop(0, hid // 32)
    def _(i):
        rows = lanes_at(i, 32)
        x = mixed[rows, :]
        acc0[rows, :] = fold(x)
        acc1[rows, :] = fold(x * x)

    def natural(lo, hi):
        @pl.loop(lo * (hid // 128), hi * (hid // 128))
        def _(i):
            d = lax.div(i, hid // 128)
            k = lanes_at(lax.rem(i, hid // 128), 128)
            wmx[d, k, :] = wall[d, pl.ds(0, hid), k].astype(F32).T.astype(BF16)

    s2h[h, :, pl.ds(0, hid)] = row_of(acc0[...])
    s2h[h, :, pl.ds(hid, hid)] = row_of(acc1[...])
    hops_start(s2h, "s2h")
    natural(0, 2)
    hops_wait(s2h, "s2h")
    s2r[r] = total(s2h, HOPS)
    rows_start(s2r, "s2r")
    natural(2, HOPS)
    wc48 = wcs[pl.ds(0, 48), :].astype(BF16)
    wcNs[...] = wcs[...].T.astype(BF16)
    crow = lax.broadcasted_iota(jnp.int32, (128, 128), 0)
    cbc = jnp.where(crow < ncls, jnp.broadcast_to(cbs[pl.ds(0, 1), :], (128, 128)).T, -1e30)[:48]
    rows_wait(s2r, "s2r")
    st2 = total(s2r, R)
    mean2 = st2[:, :hid] * inv_n
    inv2 = lax.rsqrt(st2[:, hid:] * inv_n - mean2 * mean2 + EPS * 4.0 * KAPPA * KAPPA)
    scale2 = inv2 * gain2[...]
    cols[0] = col_of(scale2)
    cols[1] = col_of(bias2[...] - mean2 * scale2)
    acc0[...] = jnp.zeros(acc0.shape, F32)
    acc1[...] = jnp.zeros(acc1.shape, F32)
    accl[...] = jnp.zeros(accl.shape, F32)
    accw[...] = jnp.zeros(accw.shape, F32)

    o_own = lanes_at(h, sub)

    def lp_copy(d, part):
        n = sub // 2
        return rc(
            lps.at[:, pl.ds(part * n, n)], o_lp.at[:, lanes_at(2 * h + part, n)], "lp", 4 * part + d, peer(d), r
        )

    dlp[...] = jnp.zeros(dlp.shape, BF16)
    HR = 128

    @pl.loop(0, NT)
    def _(t):
        n = lanes_at(t, big)

        if NT > 1:

            @pl.when(t == NT // 2)
            def _():
                @pl.loop(1, HOPS)
                def _(d):
                    lp_copy(d, 0).start()

        @pl.loop(0, hid // HR)
        def _(i):
            rows = lanes_at(i, HR)
            z2 = mixed[rows, n] * spread(cols[0, rows, :], big) + spread(cols[1, rows, :], big)
            gv, dg = gelu_slope(z2)
            hb[rows, :] = gv.astype(BF16)
            dn2[rows, n] = dg

        lg = dot(wc48, hb[...]) + spread(cbc, big)
        lg = lg - jnp.max(lg, axis=0, keepdims=True)
        ex = jnp.exp(lg)
        se = jnp.sum(ex, axis=0, keepdims=True)
        lp = lg - jnp.log(se)
        lps[:, n] = lp.astype(BF16)
        own = lanes_at(h * NT + t, big)
        hit = lax.broadcasted_iota(jnp.int32, (48, big), 0) == lab[:, own]
        accl[pl.ds(48, 48), :] += fold(jnp.where(hit, lp, 0.0))
        dl = ((ex / se - jnp.where(hit, 1.0, 0.0)) * inv_n).astype(BF16)
        accl[pl.ds(0, 48), :] += fold(dl.astype(F32))
        accw[...] += dot_nt(dl, hb[...])
        dlp[pl.ds(0, 48), :] = dl

        @pl.loop(0, hid // HR)
        def _(i):
            rows = lanes_at(i, HR)
            dn = dot(wcNs[rows, :], dlp[...]) * dn2[rows, n]
            dn2[rows, n] = dn
            acc0[rows, :] += fold(dn * mixed[rows, n])
            acc1[rows, :] += fold(dn)

    @pl.loop(1, HOPS)
    def _(d):
        if NT == 1:
            lp_copy(d, 0).start()
        lp_copy(d, 1).start()

    own_lp = pltpu.make_async_copy(lps, o_lp.at[:, o_own], ss.at[names["lp"]])
    own_lp.start()
    s3h[h, :, pl.ds(0, hid)] = row_of(acc0[...])
    s3h[h, :, pl.ds(hid, hid)] = row_of(acc1[...])
    zpad = jnp.zeros((80, 128), F32)
    s3h[h, :, pl.ds(2 * hid, 128)] = row_of(jnp.concatenate([accl[pl.ds(0, 48), :], zpad], axis=0))
    s3h[h, :, pl.ds(2 * hid + 128, 128)] = row_of(jnp.concatenate([accl[pl.ds(48, 48), :], zpad], axis=0))
    hops_start(s3h, "s3h")

    def cwh_copy(d):
        return rc(cwp.at[d], cwh.at[d], "cwh", d, peer(d), r)

    q = hid // HOPS

    @pl.loop(0, HOPS)
    def _(d):
        cwp[d] = accw[:, lanes_at(peer(d), q)].astype(BF16)

    hops_wait(s3h, "s3h")
    s3r[r] = total(s3h, HOPS)
    rows_start(s3r, "s3r")

    @pl.loop(1, HOPS)
    def _(d):
        cwh_copy(d).start()

    rows_wait(s3r, "s3r")
    st3 = total(s3r, R)
    db2 = st3[:, hid : 2 * hid]
    dg2t = inv2 * (st3[:, :hid] - mean2 * db2)
    o_small[pl.ds(0, 1), :] = dg2t
    o_small[pl.ds(1, 1), :] = db2
    o_small[pl.ds(4, 1), pl.ds(0, 256)] = st3[:, 2 * hid : 2 * hid + 256]
    o_small[pl.ds(4, 1), pl.ds(256, hid - 256)] = jnp.zeros((1, hid - 256), F32)
    t2 = scale2 * inv2 * dg2t * inv_n
    cols[1] = col_of(-t2)
    cols[2] = col_of(t2 * mean2 - scale2 * db2 * inv_n)

    @pl.loop(0, hid // 16)
    def _(i):
        rows = lanes_at(i, 16)
        v = dn2[rows, :] * spread(cols[0, rows, :], sub)
        v = v + mixed[rows, :] * spread(cols[1, rows, :], sub) + spread(cols[2, rows, :], sub)
        dmx[rows, :] = v.astype(BF16)

    @functools.partial(each, 1, Z)
    def _(e):
        gz_copy(e, zi).wait_send()
        gz_copy(e, lax.rem(zi + Z - e, Z)).wait_recv()

    gfin[c] = total(gz, Z)
    gd_copy(c).start()

    mine = lanes_at(c, half)
    theirs = lanes_at(1 - c, half)

    def pair_copy(d):
        return rc(dmp.at[d, theirs, :], pr.at[d], "pair", d, h, sib)

    qrows = half // S
    zown = pl.ds(pl.multiple_of(c * half + zpar * qrows, 16), qrows)
    zother = pl.ds(pl.multiple_of(c * half + (1 - zpar) * qrows, 16), qrows)

    def z1_copy(d):
        return rc(dmp.at[d, zother, :], z1r.at[d], "z1", d, h, 2 * zmate + c)

    def z1_start(d):
        if S > 1:
            z1_copy(d).start()

    def z1_sum(d):
        if S > 1:
            done(z1_copy(d))

            @pl.loop(0, qrows // 32)
            def _(i):
                rows = pl.ds(pl.multiple_of(c * half + zpar * qrows + i * 32, 32), 32)
                dmp[d, rows, :] = (dmp[d, rows, :].astype(F32) + z1r[d, lanes_at(i, 32), :].astype(F32)).astype(BF16)

    def hop_copy(d):
        return rc(dmp.at[d, zown, :], hr.at[d], "hop", d, peer(d), r)

    def pair_sum(d):
        done(pair_copy(d))

        @pl.loop(0, half // 32)
        def _(i):
            rows = pl.ds(pl.multiple_of(c * half + i * 32, 32), 32)
            dmp[d, rows, :] = (dmp[d, rows, :].astype(F32) + pr[d, lanes_at(i, 32), :].astype(F32)).astype(BF16)

    @pl.loop(0, HOPS)
    def _(i):
        d = HOPS - 1 - i

        dmp[d] = dot_nt(mi[d], dmx[...]).astype(BF16)
        pair_copy(d).start()

        @pl.when(i > 0)
        def _():
            pair_sum(d + 1)
            z1_start(d + 1)

        @pl.when(i > 1)
        def _():
            z1_sum(d + 2)
            hop_copy(d + 2).start()

    G2 = Z // S
    zq = lax.div(zi, S)

    def zr_copy(e, which):
        rows, lanes = chunk(0, which, qrows, G2, hid)
        return rc(hr.at[0, rows, lanes], zr.at[e], "zr", e, h, (lax.rem(zq + e, G2) * S + zpar) * 2 + c)

    def final_chunk(z):
        return chunk(c * half + lax.rem(z, S) * qrows, lax.div(z, S), qrows, G2, hid)

    def zg_copy(e, which):
        rows, lanes = final_chunk(which)
        ref = fin.at[rows, lanes]
        return rc(ref, ref, "zg", e, h, lax.rem(zi + e, Z) * 2 + c)

    def ddm_copy(core):
        ref = fin.at[lanes_at(core, half), :]
        return rc(ref, ref, "ddm", 0, h, sib)

    def d_copy(d):
        return rc(dsend.at[d], o_d.at[h], "d", d, peer(d), r)

    def dt_copy(d):
        return rc(dtail.at[d], o_dt.at[h], "dt", d, peer(d), r)

    def pp_copy(d):
        return rc(ps.at[d, :, theirs], ph.at[d], "pp", d, h, sib)

    def p_copy(d):
        return rc(phalf.at[d], prv.at[d], "p", d, peer(d), r)

    def p_half(d):
        done(pp_copy(d))
        phalf[d] = (ps[d, :, mine].astype(F32) + ph[d].astype(F32)).astype(BF16)

    def q_copy(d):
        return rc(qs.at[d], qv.at[d], "q", d, peer(d), r)

    @pl.loop(0, HOPS * NT)
    def _(it):
        dd = lax.div(it, NT)
        t = lax.rem(it, NT)
        d = HOPS - 1 - dd

        @pl.when(t == 0)
        def _():
            pT[...] = jnp.zeros(pT.shape, F32)

        @pl.when(jnp.logical_and(t == NT // 2, dd > 0))
        def _():
            p_half(d + 1)
            p_copy(d + 1).start()

        @pl.when(it == NT // 2)
        def _():
            pair_sum(0)
            z1_start(0)
            z1_sum(1)
            hop_copy(1).start()

        @pl.when(it == NT + NT // 2)
        def _():
            @pl.loop(1, HOPS)
            def _(j):
                done(cwh_copy(j))

            cw = cwp[0].astype(F32)
            for j in range(1, HOPS):
                cw = cw + cwh[j].astype(F32)
            cwr[r] = cw.astype(BF16)
            rows_start(cwr, "cwr")
            z1_sum(0)

        @pl.when(it == 2 * NT + NT // 2)
        def _():
            @pl.loop(1, HOPS)
            def _(j):
                done(hop_copy(j))

            @pl.loop(0, qrows // 32)
            def _(i):
                rows = lanes_at(i, 32)
                own = pl.ds(pl.multiple_of(c * half + zpar * qrows + i * 32, 32), 32)
                hsum = dmp[0, own, :].astype(F32)
                for j in range(1, HOPS):
                    hsum = hsum + hr[j, rows, :].astype(F32)
                hr[0, rows, :] = hsum.astype(BF16)

            @functools.partial(each, 1, G2)
            def _(e):
                zr_copy(e, lax.rem(zq + e, G2)).start()

            rows_wait(cwr, "cwr")
            cwg[h] = total(cwr, R, F32).astype(BF16)
            hops_start(cwg, "cwg")

        @pl.when(it == 3 * NT + NT // 2)
        def _():
            @functools.partial(each, 1, G2)
            def _(e):
                done(zr_copy(e, lax.rem(zq + e, G2)))

            rows, lanes = chunk(0, zq, qrows, G2, hid)
            zt = lax.fori_loop(1, G2, lambda e, v: v + zr[e].astype(F32), hr[0, rows, lanes].astype(F32))
            frows, flanes = final_chunk(zi)
            fin[frows, flanes] = zt.astype(BF16)

            @functools.partial(each, 1, Z)
            def _(e):
                zg_copy(e, zi).start()

            hops_wait(cwg, "cwg")
            for j in range(HOPS):
                o_cw[:, pl.ds(j * q, q)] = cwg[j].astype(F32)

        n = lanes_at(t, big)
        dn = dot(wmx[d], dmx[:, n]).astype(BF16) * gp[d, :, n]
        pT[...] += dot_nt(dn, fx[d, :, n])
        grad = dot(aw[d], dn)
        dsend[d, :, n] = grad[:MAIN].astype(BF16)
        d4[:, n] = grad[MAIN : MAIN + 8]

        @pl.when(t == NT - 1)
        def _():
            pw = pT[...].T * KAPPA
            qs[d, :, pl.ds(0, hid)] = jnp.sum(pw * wall[d, wrow, :].astype(F32), axis=0, keepdims=True)
            qs[d, :, pl.ds(hid, hid)] = pw[ONES : ONES + 1, :]
            ps[d] = pw[:FP].astype(BF16)
            pp_copy(d).start()
            pack4(d4, dtail.at[d])

            @pl.when(dd < HOPS - 1)
            def _():
                q_copy(d).start()
                d_copy(d).start()
                dt_copy(d).start()

    @pl.loop(1, HOPS)
    def _(d):
        done(q_copy(d))

    qr[r] = qs[0] + (qv[1] + qv[2] + qv[3])
    rows_start(qr, "qr")
    own_d = pltpu.make_async_copy(dsend.at[0], o_d.at[h], ss.at[names["d"]])
    own_d.start()
    own_dt = pltpu.make_async_copy(dtail.at[0], o_dt.at[h], ss.at[names["dt"]])
    own_dt.start()

    p_half(0)

    @pl.loop(1, HOPS)
    def _(d):
        done(p_copy(d))

    psum = phalf[0].astype(F32) + (prv[1].astype(F32) + prv[2].astype(F32) + prv[3].astype(F32))
    pz[zi] = psum.astype(BF16)

    def pz_copy(e, which):
        return rc(pz.at[which], pz.at[which], "pz", e, h, lax.rem(zi + e, Z) * 2 + c)

    @functools.partial(each, 1, Z)
    def _(e):
        pz_copy(e, zi).start()

    @functools.partial(each, 1, Z)
    def _(e):
        zg_copy(e, zi).wait_send()
        zg_copy(e, lax.rem(zi + Z - e, Z)).wait_recv()

    ddm_copy(c).start()

    rows_wait(qr, "qr")
    qt = total(qr, R)
    db = qt[:, hid:]
    dgn = inv * (qt[:, :hid] - mean * db)
    o_small[pl.ds(2, 1), :] = dgn
    o_small[pl.ds(3, 1), :] = db
    c1 = scale * db * inv_n
    c2 = inv * scale * dgn * inv_n
    shift = c1 - mean * c2
    row = lax.broadcasted_iota(jnp.int32, (128, hid), 0)
    q1, q2 = split2(jnp.where(row == ONES, shift, wown32 * c2))
    o_m[...] = (dot_nt(wown, q1) + dot_nt(wown, q2))[:FP]
    gd_copy(c).wait_send()
    gd_copy(1 - c).wait_recv()
    g1, g2, g3 = split3(jnp.concatenate([gfin[0], gfin[1]], axis=0))
    gq = dot(g1, q1) + dot(g2, q1) + dot(g3, q1) + dot(g1, q2) + dot(g2, q2)

    @functools.partial(each, 1, Z)
    def _(e):
        pz_copy(e, zi).wait_send()
        pz_copy(e, lax.rem(zi + Z - e, Z)).wait_recv()

    pfin[c] = total(pz, Z).astype(BF16)

    def pd_copy(core):
        return rc(pfin.at[core], pfin.at[core], "pd", 0, h, sib)

    pd_copy(c).start()
    ddm_copy(c).wait_send()
    ddm_copy(1 - c).wait_recv()
    o_mix[...] = fin[...]

    pd_copy(c).wait_send()
    pd_copy(1 - c).wait_recv()
    ptot = jnp.concatenate([pfin[0], pfin[1]], axis=1).astype(F32)
    o_gw[...] = ptot * scale - gq[:FP]
    own_d.wait()
    own_dt.wait()
    own_lp.wait()

    @pl.loop(1, HOPS)
    def _(d):
        done(d_copy(d))
        done(dt_copy(d))
        done(lp_copy(d, 0))
        done(lp_copy(d, 1))


def last_kernel(
    nodes,
    ft, d, dt, lp, m, mix, gw, small, cw,
    o_lp, o_gf, o_mix, o_gw, o_gg, o_gb, o_hg, o_hb, o_cw, o_cb, o_loss, low,
):
    feat, n = ft.shape
    ncls = o_lp.shape[0]
    o_lp[...] = lp[...].astype(F32)[:ncls]
    mm = m[...]
    f = ft[...]
    fix = dot(mm[:, :feat].astype(BF16), f) + mm[:, ONES : ONES + 1]
    tail = dt[0].astype(F32)
    for b in range(4):
        low[pl.ds(0, 4), pl.ds(b * (n // 4), n // 4)] = tail[4 * b : 4 * b + 4]
    gf = jnp.concatenate([d[0].astype(F32), low[...]], axis=0)[:feat] - fix[:feat]
    if STRIDED:
        flat = o_gf.reshape(feat * (n // 128), 128)
        for i in range(n // 128):
            flat[pl.ds(i, feat, stride=n // 128), :] = gf[:, i * 128 : (i + 1) * 128]
    else:
        for i in range(n // 128):
            o_gf[:, i, :] = gf[:, i * 128 : (i + 1) * 128]

    @pl.when(pl.program_id(0) == 0)
    def _():
        hid = mix.shape[1]
        o_mix[...] = mix[...].astype(F32)
        for i in range(hid // 128):
            o_gw[:, i, :] = gw[pl.ds(0, feat), pl.ds(i * 128, 128)]
        o_hg[...] = small[pl.ds(0, 1), :]
        o_hb[...] = small[pl.ds(1, 1), :]
        o_gg[...] = small[pl.ds(2, 1), :]
        o_gb[...] = small[pl.ds(3, 1), :]
        o_cw[...] = cw[pl.ds(0, ncls), :]
        o_cb[...] = small[pl.ds(4, 1), pl.ds(0, ncls)]
        o_loss[...] = jnp.sum(small[pl.ds(4, 1), pl.ds(128, 128)], axis=1, keepdims=True) * (-1.0 / nodes)


def shards(
    R, features, branch_weight, branch_gain, branch_bias, mix_weight, mixing_norm_gain, mixing_norm_bias,
    class_weight, class_bias, labels, hop_mask,
):
    local, feat = features.shape[1:]
    hid = mix_weight.shape[0]
    ncls = class_weight.shape[1]
    nodes = local * R
    sub = local // HOPS
    Z = R // 2
    half = hid // 2
    S = min(Z, 2)
    G2, qrows = Z // S, half // S
    zrows, zcols = chunk(0, 0, qrows, G2, hid)
    assert feat == ONES and ncls == 47 and local // hop_mask.shape[0] == 128
    ft = features[0].T
    sd = jax.ShapeDtypeStruct
    vm = pl.BlockSpec(memory_space=pltpu.VMEM)
    hbm = pl.BlockSpec(memory_space=pl.ANY)
    _, nsem = sem_plan(R)
    V = pltpu.VMEM
    outs = pl.pallas_call(
        functools.partial(main_kernel, R, nodes),
        grid=(1,),
        out_shape=(
            sd((48, local), BF16),
            sd((HOPS, MAIN, sub), BF16),
            sd((HOPS, 16, sub // 4), BF16),
            sd((FP, 128), F32),
            sd((hid, hid), BF16),
            sd((FP, hid), F32),
            sd((8, hid), F32),
            sd((48, hid), F32),
        ),
        in_specs=[hbm, pl.BlockSpec((16, local), lambda i: (MAIN // 16, 0))]
        + [vm] * 9
        + [pl.BlockSpec(memory_space=pltpu.SMEM)],
        out_specs=(hbm, hbm, hbm, vm, vm, vm, vm, vm),
        scratch_shapes=[
            V((128, local), BF16),
            V((HOPS, 128, sub), BF16),
            V((HOPS, 16, sub // 4), BF16),
            V((HOPS, 16, sub // 4), BF16),
            V((48, sub // 4), F32),
            V((HOPS, hid + 128, hid), BF16),
            V((HOPS, hid, 256), BF16),
            V((HOPS, FP, hid), BF16),
            V((HOPS, hid, hid), BF16),
            V((HOPS, 16, sub), BF16),
            V((HOPS, hid, sub), BF16),
            V((HOPS, hid, sub), BF16),
            V((hid, sub), F32),
            V((hid, sub), F32),
            V((hid, sub), BF16),
            V((128, 128), F32),
            V((64, 128), F32),
            V((Z, 64, 128), F32),
            V((2, 64, 128), F32),
            V((R, 1, 2 * hid), F32),
            V((HOPS, 1, 2 * hid), F32),
            V((HOPS, 1, 2 * hid), F32),
            V((R, 1, 2 * hid), F32),
            V((HOPS, 1, 2 * hid + 256), F32),
            V((R, 1, 2 * hid + 256), F32),
            V((HOPS, 48, hid // HOPS), BF16),
            V((HOPS, 48, hid // HOPS), BF16),
            V((R, 48, hid // HOPS), BF16),
            V((HOPS, 48, hid // HOPS), BF16),
            V((48, sub), BF16),
            V((128, hid), F32),
            V((hid, 128), BF16),
            V((8, 128), F32),
            V((hid, min(2 * TILE, sub)), BF16),
            V((128, min(2 * TILE, sub)), BF16),
            V((hid, 128), F32),
            V((hid, 128), F32),
            V((96, 128), F32),
            V((48, hid), F32),
            V((3, hid, 128), F32),
            V((HOPS, hid, hid), BF16),
            V((HOPS, half, hid), BF16),
            V((HOPS, qrows, hid), BF16),
            V((HOPS, qrows, hid), BF16),
            V((max(G2, 2), zrows.size, zcols.size), BF16),
            V((hid, hid), BF16),
            V((HOPS, MAIN, sub), BF16),
            V((8, sub), F32),
            V((HOPS, 16, sub // 4), BF16),
            V((hid, 128), F32),
            V((HOPS, FP, hid), BF16),
            V((HOPS, FP, half), BF16),
            V((HOPS, FP, half), BF16),
            V((HOPS, FP, half), BF16),
            V((HOPS, 1, 2 * hid), F32),
            V((HOPS, 1, 2 * hid), F32),
            V((R, 1, 2 * hid), F32),
            V((Z, FP, half), BF16),
            V((2, FP, half), BF16),
            pltpu.SemaphoreType.DMA((nsem,)),
            pltpu.SemaphoreType.DMA((nsem,)),
        ],
        compiler_params=pltpu.CompilerParams(
            collective_id=0, has_side_effects=True, vmem_limit_bytes=63 * 1024 * 1024
        ),
        cost_estimate=pl.CostEstimate(flops=2 * 8 * 10**9, bytes_accessed=10**7, transcendentals=10**7),
        name="main",
    )(
        ft, ft, branch_weight[0], branch_gain, branch_bias, mix_weight, mixing_norm_gain[None], mixing_norm_bias[None],
        class_weight.T, class_bias[None], labels[None], hop_mask.T,
    )
    lp, dd, dt, m, mix, gw, small, cw = outs
    nb = sub
    whole = lambda shape: pl.BlockSpec(shape, lambda i: (0,) * len(shape))
    lp, gf, mix, gw, gg, gb, hg, hb, cw, cb, loss = pl.pallas_call(
        functools.partial(last_kernel, nodes),
        grid=(local // nb,),
        out_shape=(
            sd((ncls, local), F32),
            sd((feat, local // 128, 128), F32),
            sd((hid, hid), F32),
            sd((feat, hid // 128, 128), F32),
            sd((1, hid), F32),
            sd((1, hid), F32),
            sd((1, hid), F32),
            sd((1, hid), F32),
            sd((ncls, hid), F32),
            sd((1, ncls), F32),
            sd((1, 1), F32),
        ),
        in_specs=[
            pl.BlockSpec((feat, nb), lambda i: (0, i)),
            pl.BlockSpec((1, MAIN, nb), lambda i: (i, 0, 0)),
            pl.BlockSpec((1, 16, nb // 4), lambda i: (i, 0, 0)),
            pl.BlockSpec((48, nb), lambda i: (0, i)),
            whole((FP, 128)),
            whole((hid, hid)),
            whole((FP, hid)),
            whole((8, hid)),
            whole((48, hid)),
        ],
        out_specs=(
            pl.BlockSpec((ncls, nb), lambda i: (0, i)),
            pl.BlockSpec((feat, nb // 128, 128), lambda i: (0, i, 0)),
            whole((hid, hid)),
            whole((feat, hid // 128, 128)),
            whole((1, hid)),
            whole((1, hid)),
            whole((1, hid)),
            whole((1, hid)),
            whole((ncls, hid)),
            whole((1, ncls)),
            whole((1, 1)),
        ),
        scratch_shapes=[V((8, nb), F32)],
        compiler_params=pltpu.CompilerParams(vmem_limit_bytes=60 * 1024 * 1024),
        name="last",
    )(ft, dd, dt, lp, m, mix, gw, small, cw)
    return (
        lp.T,
        loss[0, 0],
        with_layout_constraint(gf.reshape(feat, 1, local), Layout((0, 1, 2))).transpose(1, 2, 0),
        gw.reshape(1, feat, hid),
        gg,
        gb,
        mix,
        hg[0],
        hb[0],
        cw.T,
        cb[0],
    )


def solution(mesh):
    placed = (
        P("hop", "rows", None), P("hop", None, None), P("hop", None), P("hop", None), P("hop", None),
        P(), P(), P(), P(), P("rows"), P("rows", None),
    )
    assert mesh.shape["hop"] == HOPS
    return jax.shard_map(
        functools.partial(shards, mesh.shape["rows"]),
        mesh=mesh,
        in_specs=placed,
        out_specs=(
            P("rows", None), P(), P("hop", "rows", None), P("hop", None, None), P("hop", None), P("hop", None),
            P("hop", None), P(), P(), P(), P(),
        ),
        check_vma=False,
    )
```

```python
import functools
import math

import jax
import jax.numpy as jnp
from jax import lax
from jax.experimental import pallas as pl
from jax.experimental.layout import Layout, with_layout_constraint
from jax.experimental.pallas import tpu as pltpu
from jax.sharding import PartitionSpec as P

MESH = pl.DeviceIdType.MESH
EPS = 1e-05
HOPS = 4
ONES = 100
FP = 112
MAIN = 96
TILE = 256
STRIDED = True
C0 = math.sqrt(2.0 / math.pi)
C1 = C0 * 0.044715
KAPPA = C1 ** (1.0 / 3.0)
ALPHA = C0 / KAPPA
F32 = jnp.float32
BF16 = jnp.bfloat16


def dot(a, b):
    return lax.dot_general(a, b, (((1,), (0,)), ((), ())), preferred_element_type=F32)


def dot_nt(a, b):
    return lax.dot_general(a, b, (((1,), (1,)), ((), ())), preferred_element_type=F32)


def split2(x):
    hi = x.astype(BF16)
    return hi, (x - hi.astype(F32)).astype(BF16)


def split3(x):
    hi = x.astype(BF16)
    rest = x - hi.astype(F32)
    mid = rest.astype(BF16)
    return hi, mid, (rest - mid.astype(F32)).astype(BF16)


def gelu_slope(z):
    u = z * z
    t = jnp.tanh(z * (C0 + C1 * u))
    s = 0.5 * t + 0.5
    g = z * s
    return g, s + (g - g * s) * (2.0 * C0 + 6.0 * C1 * u)


def scaled_gelu_slope(y):
    u = y * y
    t = jnp.tanh(y * (u + ALPHA))
    up = t + 1.0
    g = y * up
    return g, up + (g * (1.0 - t)) * (3.0 * u + ALPHA)


def fold(x):
    total = x[:, :128]
    for i in range(1, x.shape[1] // 128):
        total = total + x[:, i * 128 : (i + 1) * 128]
    return total


def spread(c, n):
    return jnp.concatenate([c] * (n // 128), axis=1)


def row_of(acc):
    return jnp.sum(acc.T, axis=0, keepdims=True)


def col_of(row):
    return jnp.broadcast_to(row, (128, row.shape[1])).T


def each(lo, hi, body):
    if hi - lo == 1:
        body(lo)
    elif hi > lo:
        pl.loop(lo, hi)(body)


class Alloc:
    def __init__(self):
        self.n = 0

    def __call__(self, count):
        base = self.n
        self.n += count
        return base


def sem_plan(R):
    Z = R // 2
    a = Alloc()
    names = {}
    for name, count in (
        ("feat", 4), ("ft", 4), ("loc", 1), ("ws", 4), ("dd", 4), ("s1", R), ("ab", 4), ("gp", 1), ("gz", Z), ("gd", 1),
        ("s2h", 4), ("s2r", R), ("s3h", 4), ("s3r", R), ("lp", 8), ("cwh", 4), ("cwr", R), ("cwg", 4),
        ("pair", 4), ("z1", 4), ("hop", 4), ("zr", Z), ("zg", Z), ("ddm", 1), ("d", 4), ("dt", 4), ("p", 4), ("q", 4),
        ("qr", R), ("pp", 4), ("pz", Z), ("pd", 1),
    ):
        names[name] = a(count)
    return names, a.n


def chunk(base, i, rows, pieces, cols):
    if rows // pieces >= 16:
        take = rows // pieces
        return pl.ds(pl.multiple_of(base + i * take, 16), take), pl.ds(0, cols)
    m = 16 * pieces // rows
    wide = cols // m
    return (
        pl.ds(pl.multiple_of(base + (i // m) * 16, 16), 16),
        pl.ds(pl.multiple_of((i % m) * wide, 128), wide),
    )


def main_kernel(
    R,
    nodes,
    ft, ft4, wb, bgain, bbias, wm, gain2, bias2, wc, cb, lab, msk,
    o_lp, o_d, o_dt, o_m, o_mix, o_gw, o_small, o_cw,
    fs, fx, ftail, frt, st4, wall, wl, aw, wmx, keep, mi, gp, mixed, dn2, dmx,
    gown, gpr, gz, gfin, s1, ab, s2h, s2r, s3h, s3r, cwp, cwh, cwr, cwg, lps,
    wcs, wcNs, cbs, hb, dlp, acc0, acc1, accl, accw, cols,
    dmp, pr, z1r, hr, zr, fin, dsend, d4, dtail, pT, ps, ph, phalf, prv, qs, qv, qr, pz, pfin,
    ss, rs,
):
    names, _ = sem_plan(R)
    Z = R // 2
    h = lax.axis_index("hop")
    r = lax.axis_index("rows")
    c = lax.rem(r, 2)
    zi = lax.div(r, 2)
    sib = r + 1 - 2 * c
    local = ft.shape[1]
    sub = local // HOPS
    hid = wm.shape[0]
    half = hid // 2
    big = min(2 * TILE, sub)
    UN = big // TILE
    NT = sub // big
    inv_n = 1.0 / nodes

    def peer(d):
        x = lax.rem(h + d, 2)
        y = lax.rem(lax.div(h, 2) + lax.div(d, 2), 2)
        return 2 * y + x

    def rc(src, dst, name, i, hh, rr):
        return pltpu.make_async_remote_copy(
            src_ref=src, dst_ref=dst, send_sem=ss.at[names[name] + i], recv_sem=rs.at[names[name] + i],
            device_id=(hh, rr), device_id_type=MESH,
        )

    def done(cp):
        cp.wait_send()
        cp.wait_recv()

    def lanes_at(i, n):
        return pl.ds(pl.multiple_of(i * n, n), n)

    barrier = pltpu.get_barrier_semaphore()

    def greet(hh, rr):
        pl.semaphore_signal(barrier, inc=1, device_id=(hh, rr), device_id_type=MESH)

    @pl.loop(1, HOPS)
    def _(d):
        greet(peer(d), r)

    @functools.partial(each, 1, R)
    def _(e):
        greet(h, lax.rem(r + e, R))

    def rows_start(buf, name):
        @functools.partial(each, 1, R)
        def _(e):
            rc(buf.at[r], buf.at[r], name, e, h, lax.rem(r + e, R)).start()

    def rows_wait(buf, name):
        @functools.partial(each, 1, R)
        def _(e):
            src = lax.rem(r + R - e, R)
            done(rc(buf.at[src], buf.at[src], name, e, h, lax.rem(r + e, R)))

    def hops_start(buf, name):
        @pl.loop(1, HOPS)
        def _(d):
            rc(buf.at[h], buf.at[h], name, d, peer(d), r).start()

    def hops_wait(buf, name):
        @pl.loop(1, HOPS)
        def _(d):
            done(rc(buf.at[peer(d)], buf.at[peer(d)], name, d, peer(d), r))

    def total(buf, n, dtype=F32):
        return lax.fori_loop(1, n, lambda i, t: t + buf[i].astype(dtype), buf[0].astype(dtype))

    loc = pltpu.make_async_copy(ft.at[pl.ds(0, MAIN), :], fs.at[pl.ds(0, MAIN), :], ss.at[names["loc"]])
    loc.start()

    def pack4(src, dst):
        n = st4.shape[1]
        for b in range(4):
            st4[pl.ds(4 * b, 4), :] = src[pl.ds(0, 4), pl.ds(b * n, n)].astype(F32)
        dst[...] = st4[pl.ds(0, 16), :].astype(BF16)

    def unpack4(src, dst):
        n = st4.shape[1]
        row = lax.broadcasted_iota(jnp.int32, (32, n), 0)
        st4[pl.ds(0, 16), :] = src[...].astype(F32)
        st4[pl.ds(16, 32), :] = jnp.where(row == ONES - MAIN, 1.0, 0.0)
        for b in range(4):
            st4[pl.ds(16, 4), :] = st4[pl.ds(4 * b, 4), :]
            dst[pl.ds(MAIN, 32), pl.ds(b * n, n)] = st4[pl.ds(16, 32), :].astype(BF16)

    wrow = pl.ds(hid, 128)
    wall[0, pl.ds(hid + 96, 32), :] = jnp.zeros((32, hid), BF16)
    wall[0, pl.ds(hid, 100), :] = wb[...]

    @pl.loop(0, hid // 128)
    def _(i):
        k = lanes_at(i, 128)
        wall[0, pl.ds(0, hid), k] = wm[k, :].astype(F32).T.astype(BF16)

    def feat_copy(d):
        rows = pl.ds(0, MAIN)
        return rc(ft.at[rows, lanes_at(peer(d), sub)], fx.at[d, rows, :], "feat", d, peer(d), r)

    def ft_copy(d):
        return rc(ftail.at[peer(d)], frt.at[d], "ft", d, peer(d), r)

    pl.semaphore_wait(barrier, HOPS - 1 + R - 1)

    part = (hid + 128) // 2
    first, second = 1 + c, 2 - c

    def part_of(d, core):
        return wall.at[d, pl.ds(pl.multiple_of(core * part, 16), part), :]

    def ws_copy(d):
        return rc(part_of(0, c), part_of(d, c), "ws", d, peer(d), r)

    def dd_copy(d, core):
        return rc(part_of(d, core), part_of(d, core), "dd", d, h, sib)

    ws_copy(first).start()
    ws_copy(second).start()

    @pl.loop(0, HOPS)
    def _(j):
        lanes = lanes_at(j, sub)
        pack4(ft4.at[:, lanes], ftail.at[j])
        unpack4(ftail.at[j], fs.at[:, lanes])

    loc.wait()
    fx0 = pltpu.make_async_copy(fs.at[:, lanes_at(h, sub)], fx.at[0], ss.at[names["loc"]])
    fx0.start()

    def gram(i, g):
        f = fs[:, lanes_at(i, sub)]
        return g + dot_nt(f, f)

    g = lax.fori_loop(0, HOPS, gram, jnp.zeros((128, 128), F32))
    wown = wall[0, wrow, :]
    wown32 = wown.astype(F32)
    g1, g2, g3 = split3(g)
    gw = dot(g1, wown) + dot(g2, wown) + dot(g3, wown)
    s1[r, :, pl.ds(0, hid)] = gw[ONES : ONES + 1, :]
    s1[r, :, pl.ds(hid, hid)] = jnp.sum(gw * wown32, axis=0, keepdims=True)
    rows_start(s1, "s1")

    gown[...] = g

    @pl.loop(1, HOPS - 1)
    def _(d):
        done(ws_copy(d))
        dd_copy(d, c).start()

    feat_copy(first).start()
    feat_copy(second).start()

    @pl.loop(1, HOPS)
    def _(d):
        ft_copy(d).start()

    ws_copy(HOPS - 1).start()
    feat_copy(HOPS - 1).start()

    @pl.loop(0, HOPS * (sub // 128))
    def _(i):
        d = lax.div(i, sub // 128)
        b = lax.rem(i, sub // 128)
        late = peer(d) - 2
        m = jnp.where(late >= 0, msk[jnp.maximum(late, 0), h * (sub // 128) + b], 1)
        keep[d, :, lanes_at(b, 128)] = jnp.full((16, 128), 0.5 * m.astype(F32)).astype(BF16)

    wcs[...] = jnp.zeros(wcs.shape, F32)
    wcs[pl.ds(0, wc.shape[0]), :] = wc[...].astype(F32)
    cbs[...] = jnp.zeros(cbs.shape, F32)
    cbs[pl.ds(0, 1), pl.ds(0, cb.shape[1])] = cb[...]
    ncls = wc.shape[0]

    @pl.loop(0, hid // 16)
    def _(i):
        rows = lanes_at(i, 16)
        mixed[rows, :] = jnp.zeros((16, sub), F32)
        mi[0, rows, pl.ds(0, big)] = jnp.zeros((16, big), BF16)

    fx0.wait()

    rows_wait(s1, "s1")
    st = total(s1, R)
    mean = st[:, :hid] * inv_n
    var = st[:, hid:] * inv_n - mean * mean
    inv = lax.rsqrt(var + EPS)
    scale = inv * bgain[...]
    ab[0, :, pl.ds(0, hid)] = scale
    ab[0, :, pl.ds(hid, hid)] = bbias[...] - mean * scale

    def ab_copy(d):
        return rc(ab.at[0], ab.at[d], "ab", d, peer(d), r)

    @pl.loop(1, HOPS)
    def _(d):
        ab_copy(d).start()

    def prepare(d):
        a = ab[d, :, pl.ds(0, hid)]
        b = ab[d, :, pl.ds(hid, hid)]
        ws = wall[d, wrow, :].astype(F32) * (a * KAPPA)
        aw[d] = ws[:FP].astype(BF16)
        row = lax.broadcasted_iota(jnp.int32, (128, hid), 0)
        wt = jnp.where(row == ONES, b * KAPPA, ws).T
        hi, lo = split2(wt)
        wl[d, :, pl.ds(0, 128)] = hi
        wl[d, :, pl.ds(128, 128)] = lo

    g_pair = rc(gown.at[lanes_at(1 - c, 64), :], gpr, "gp", 0, h, sib)

    def gz_copy(e, which):
        return rc(gz.at[which], gz.at[which], "gz", e, h, lax.rem(zi + e, Z) * 2 + c)

    def gd_copy(core):
        return rc(gfin.at[core], gfin.at[core], "gd", 0, h, sib)

    @pl.loop(0, HOPS * NT)
    def _(it):
        d = lax.div(it, NT)
        t = lax.rem(it, NT)

        @pl.when(t == 0)
        def _():
            @pl.when(d > 0)
            def _():
                done(feat_copy(d))
                done(ft_copy(d))
                unpack4(frt.at[d], fx.at[d])
                dd_copy(d, c).wait_send()
                dd_copy(d, 1 - c).wait_recv()
                done(ab_copy(d))

            prepare(d)

        @pl.when(it == NT + NT // 2)
        def _():
            done(ws_copy(HOPS - 1))
            dd_copy(HOPS - 1, c).start()

        @pl.when(it == 2 * NT)
        def _():
            g_pair.start()

        @pl.when(it == 3 * NT)
        def _():
            done(g_pair)
            gz[zi] = gown[lanes_at(c, 64), :] + gpr[...]

            @functools.partial(each, 1, Z)
            def _(e):
                gz_copy(e, zi).start()

        pit = jnp.maximum(it - 1, 0)
        pd = lax.div(pit, NT)
        pt = lax.rem(pit, NT)
        adds = []
        for u in range(UN):
            adds.append(dot(wall[pd, pl.ds(0, hid), :], mi[pd, :, lanes_at(pt * UN + u, TILE)]))
        for u in range(UN):
            n = lanes_at(t * UN + u, TILE)
            f = fx[d, :, n]
            z = dot(wl[d], jnp.concatenate([f, f], axis=0))
            k = keep[d, :, n]
            k = jnp.concatenate([k] * 4, axis=0)
            for i in range(0, hid, 64):
                g1, d1 = scaled_gelu_slope(z[i : i + 64].astype(BF16))
                g2, d2 = scaled_gelu_slope(g1 * k)
                mi[d, pl.ds(i, 64), n] = g2
                gp[d, pl.ds(i, 64), n] = d1 * d2 * k
        for u in range(UN):
            n = lanes_at(pt * UN + u, TILE)
            mixed[:, n] = mixed[:, n] + adds[u]

    acc0[...] = jnp.zeros(acc0.shape, F32)
    acc1[...] = jnp.zeros(acc1.shape, F32)

    @pl.loop(0, UN)
    def _(u):
        n = lanes_at((NT - 1) * UN + u, TILE)
        mixed[:, n] = mixed[:, n] + dot(wall[HOPS - 1, pl.ds(0, hid), :], mi[HOPS - 1, :, n])

    @pl.loop(0, hid // 32)
    def _(i):
        rows = lanes_at(i, 32)
        x = mixed[rows, :]
        acc0[rows, :] = fold(x)
        acc1[rows, :] = fold(x * x)

    def natural(lo, hi):
        @pl.loop(lo * (hid // 128), hi * (hid // 128))
        def _(i):
            d = lax.div(i, hid // 128)
            k = lanes_at(lax.rem(i, hid // 128), 128)
            wmx[d, k, :] = wall[d, pl.ds(0, hid), k].astype(F32).T.astype(BF16)

    s2h[h, :, pl.ds(0, hid)] = row_of(acc0[...])
    s2h[h, :, pl.ds(hid, hid)] = row_of(acc1[...])
    hops_start(s2h, "s2h")
    natural(0, 2)
    hops_wait(s2h, "s2h")
    s2r[r] = total(s2h, HOPS)
    rows_start(s2r, "s2r")
    natural(2, HOPS)
    wc48 = wcs[pl.ds(0, 48), :].astype(BF16)
    wcNs[...] = wcs[...].T.astype(BF16)
    crow = lax.broadcasted_iota(jnp.int32, (128, 128), 0)
    cbc = jnp.where(crow < ncls, jnp.broadcast_to(cbs[pl.ds(0, 1), :], (128, 128)).T, -1e30)[:48]
    rows_wait(s2r, "s2r")
    st2 = total(s2r, R)
    mean2 = st2[:, :hid] * inv_n
    inv2 = lax.rsqrt(st2[:, hid:] * inv_n - mean2 * mean2 + EPS * 4.0 * KAPPA * KAPPA)
    scale2 = inv2 * gain2[...]
    cols[0] = col_of(scale2)
    cols[1] = col_of(bias2[...] - mean2 * scale2)
    acc0[...] = jnp.zeros(acc0.shape, F32)
    acc1[...] = jnp.zeros(acc1.shape, F32)
    accl[...] = jnp.zeros(accl.shape, F32)
    accw[...] = jnp.zeros(accw.shape, F32)

    o_own = lanes_at(h, sub)

    def lp_copy(d, part):
        n = sub // 2
        return rc(
            lps.at[:, pl.ds(part * n, n)], o_lp.at[:, lanes_at(2 * h + part, n)], "lp", 4 * part + d, peer(d), r
        )

    dlp[...] = jnp.zeros(dlp.shape, BF16)
    HR = 128

    @pl.loop(0, NT)
    def _(t):
        n = lanes_at(t, big)

        if NT > 1:

            @pl.when(t == NT // 2)
            def _():
                @pl.loop(1, HOPS)
                def _(d):
                    lp_copy(d, 0).start()

        @pl.loop(0, hid // HR)
        def _(i):
            rows = lanes_at(i, HR)
            z2 = mixed[rows, n] * spread(cols[0, rows, :], big) + spread(cols[1, rows, :], big)
            gv, dg = gelu_slope(z2)
            hb[rows, :] = gv.astype(BF16)
            dn2[rows, n] = dg

        lg = dot(wc48, hb[...]) + spread(cbc, big)
        lg = lg - jnp.max(lg, axis=0, keepdims=True)
        ex = jnp.exp(lg)
        se = jnp.sum(ex, axis=0, keepdims=True)
        lp = lg - jnp.log(se)
        lps[:, n] = lp.astype(BF16)
        own = lanes_at(h * NT + t, big)
        hit = lax.broadcasted_iota(jnp.int32, (48, big), 0) == lab[:, own]
        accl[pl.ds(48, 48), :] += fold(jnp.where(hit, lp, 0.0))
        dl = ((ex / se - jnp.where(hit, 1.0, 0.0)) * inv_n).astype(BF16)
        accl[pl.ds(0, 48), :] += fold(dl.astype(F32))
        accw[...] += dot_nt(dl, hb[...])
        dlp[pl.ds(0, 48), :] = dl

        @pl.loop(0, hid // HR)
        def _(i):
            rows = lanes_at(i, HR)
            dn = dot(wcNs[rows, :], dlp[...]) * dn2[rows, n]
            dn2[rows, n] = dn
            acc0[rows, :] += fold(dn * mixed[rows, n])
            acc1[rows, :] += fold(dn)

    own_lp = pltpu.make_async_copy(lps, o_lp.at[:, o_own], ss.at[names["lp"]])
    own_lp.start()
    s3h[h, :, pl.ds(0, hid)] = row_of(acc0[...])
    s3h[h, :, pl.ds(hid, hid)] = row_of(acc1[...])
    zpad = jnp.zeros((80, 128), F32)
    s3h[h, :, pl.ds(2 * hid, 128)] = row_of(jnp.concatenate([accl[pl.ds(0, 48), :], zpad], axis=0))
    s3h[h, :, pl.ds(2 * hid + 128, 128)] = row_of(jnp.concatenate([accl[pl.ds(48, 48), :], zpad], axis=0))
    hops_start(s3h, "s3h")

    def cwh_copy(d):
        return rc(cwp.at[d], cwh.at[d], "cwh", d, peer(d), r)

    q = hid // HOPS

    @pl.loop(0, HOPS)
    def _(d):
        cwp[d] = accw[:, lanes_at(peer(d), q)].astype(BF16)

    hops_wait(s3h, "s3h")
    s3r[r] = total(s3h, HOPS)
    rows_start(s3r, "s3r")

    @pl.loop(1, HOPS)
    def _(d):
        cwh_copy(d).start()
        if NT == 1:
            lp_copy(d, 0).start()
        lp_copy(d, 1).start()

    rows_wait(s3r, "s3r")
    st3 = total(s3r, R)
    db2 = st3[:, hid : 2 * hid]
    dg2t = inv2 * (st3[:, :hid] - mean2 * db2)
    o_small[pl.ds(0, 1), :] = dg2t
    o_small[pl.ds(1, 1), :] = db2
    o_small[pl.ds(4, 1), pl.ds(0, 256)] = st3[:, 2 * hid : 2 * hid + 256]
    o_small[pl.ds(4, 1), pl.ds(256, hid - 256)] = jnp.zeros((1, hid - 256), F32)
    t2 = scale2 * inv2 * dg2t * inv_n
    cols[1] = col_of(-t2)
    cols[2] = col_of(t2 * mean2 - scale2 * db2 * inv_n)

    @pl.loop(0, hid // 16)
    def _(i):
        rows = lanes_at(i, 16)
        v = dn2[rows, :] * spread(cols[0, rows, :], sub)
        v = v + mixed[rows, :] * spread(cols[1, rows, :], sub) + spread(cols[2, rows, :], sub)
        dmx[rows, :] = v.astype(BF16)

    @functools.partial(each, 1, Z)
    def _(e):
        gz_copy(e, zi).wait_send()
        gz_copy(e, lax.rem(zi + Z - e, Z)).wait_recv()

    gfin[c] = total(gz, Z)
    gd_copy(c).start()

    mine = lanes_at(c, half)
    theirs = lanes_at(1 - c, half)

    def pair_copy(d):
        return rc(dmp.at[d, theirs, :], pr.at[d], "pair", d, h, sib)

    S = min(Z, 2)
    zpar = lax.rem(zi, S)
    zmate = zi + (S - 1) - 2 * (S - 1) * zpar
    qrows = half // S
    zown = pl.ds(pl.multiple_of(c * half + zpar * qrows, 16), qrows)
    zother = pl.ds(pl.multiple_of(c * half + (1 - zpar) * qrows, 16), qrows)

    def z1_copy(d):
        return rc(dmp.at[d, zother, :], z1r.at[d], "z1", d, h, 2 * zmate + c)

    def z1_start(d):
        if S > 1:
            z1_copy(d).start()

    def z1_sum(d):
        if S > 1:
            done(z1_copy(d))

            @pl.loop(0, qrows // 32)
            def _(i):
                rows = pl.ds(pl.multiple_of(c * half + zpar * qrows + i * 32, 32), 32)
                dmp[d, rows, :] = (dmp[d, rows, :].astype(F32) + z1r[d, lanes_at(i, 32), :].astype(F32)).astype(BF16)

    def hop_copy(d):
        return rc(dmp.at[d, zown, :], hr.at[d], "hop", d, peer(d), r)

    def pair_sum(d):
        done(pair_copy(d))

        @pl.loop(0, half // 32)
        def _(i):
            rows = pl.ds(pl.multiple_of(c * half + i * 32, 32), 32)
            dmp[d, rows, :] = (dmp[d, rows, :].astype(F32) + pr[d, lanes_at(i, 32), :].astype(F32)).astype(BF16)

    @pl.loop(0, HOPS)
    def _(i):
        d = HOPS - 1 - i

        dmp[d] = dot_nt(mi[d], dmx[...]).astype(BF16)
        pair_copy(d).start()

        @pl.when(i > 0)
        def _():
            pair_sum(d + 1)
            z1_start(d + 1)

        @pl.when(i > 1)
        def _():
            z1_sum(d + 2)
            hop_copy(d + 2).start()

    G2 = Z // S
    zq = lax.div(zi, S)

    def zr_copy(e, which):
        rows, lanes = chunk(0, which, qrows, G2, hid)
        return rc(hr.at[0, rows, lanes], zr.at[e], "zr", e, h, (lax.rem(zq + e, G2) * S + zpar) * 2 + c)

    def final_chunk(z):
        return chunk(c * half + lax.rem(z, S) * qrows, lax.div(z, S), qrows, G2, hid)

    def zg_copy(e, which):
        rows, lanes = final_chunk(which)
        ref = fin.at[rows, lanes]
        return rc(ref, ref, "zg", e, h, lax.rem(zi + e, Z) * 2 + c)

    def ddm_copy(core):
        ref = fin.at[lanes_at(core, half), :]
        return rc(ref, ref, "ddm", 0, h, sib)

    def d_copy(d):
        return rc(dsend.at[d], o_d.at[h], "d", d, peer(d), r)

    def dt_copy(d):
        return rc(dtail.at[d], o_dt.at[h], "dt", d, peer(d), r)

    def pp_copy(d):
        return rc(ps.at[d, :, theirs], ph.at[d], "pp", d, h, sib)

    def p_copy(d):
        return rc(phalf.at[d], prv.at[d], "p", d, peer(d), r)

    def p_half(d):
        done(pp_copy(d))
        phalf[d] = (ps[d, :, mine].astype(F32) + ph[d].astype(F32)).astype(BF16)

    def q_copy(d):
        return rc(qs.at[d], qv.at[d], "q", d, peer(d), r)

    @pl.loop(0, HOPS * NT)
    def _(it):
        dd = lax.div(it, NT)
        t = lax.rem(it, NT)
        d = HOPS - 1 - dd

        @pl.when(t == 0)
        def _():
            pT[...] = jnp.zeros(pT.shape, F32)

        @pl.when(jnp.logical_and(t == NT // 2, dd > 0))
        def _():
            p_half(d + 1)
            p_copy(d + 1).start()

        @pl.when(it == NT // 2)
        def _():
            pair_sum(0)
            z1_start(0)
            z1_sum(1)
            hop_copy(1).start()

        @pl.when(it == NT + NT // 2)
        def _():
            @pl.loop(1, HOPS)
            def _(j):
                done(cwh_copy(j))

            cw = cwp[0].astype(F32)
            for j in range(1, HOPS):
                cw = cw + cwh[j].astype(F32)
            cwr[r] = cw.astype(BF16)
            rows_start(cwr, "cwr")
            z1_sum(0)

        @pl.when(it == 2 * NT + NT // 2)
        def _():
            @pl.loop(1, HOPS)
            def _(j):
                done(hop_copy(j))

            @pl.loop(0, qrows // 32)
            def _(i):
                rows = lanes_at(i, 32)
                own = pl.ds(pl.multiple_of(c * half + zpar * qrows + i * 32, 32), 32)
                hsum = dmp[0, own, :].astype(F32)
                for j in range(1, HOPS):
                    hsum = hsum + hr[j, rows, :].astype(F32)
                hr[0, rows, :] = hsum.astype(BF16)

            @functools.partial(each, 1, G2)
            def _(e):
                zr_copy(e, lax.rem(zq + e, G2)).start()

            rows_wait(cwr, "cwr")
            cwg[h] = total(cwr, R, F32).astype(BF16)
            hops_start(cwg, "cwg")

        @pl.when(it == 3 * NT + NT // 2)
        def _():
            @functools.partial(each, 1, G2)
            def _(e):
                done(zr_copy(e, lax.rem(zq + e, G2)))

            rows, lanes = chunk(0, zq, qrows, G2, hid)
            zt = lax.fori_loop(1, G2, lambda e, v: v + zr[e].astype(F32), hr[0, rows, lanes].astype(F32))
            frows, flanes = final_chunk(zi)
            fin[frows, flanes] = zt.astype(BF16)

            @functools.partial(each, 1, Z)
            def _(e):
                zg_copy(e, zi).start()

            hops_wait(cwg, "cwg")
            for j in range(HOPS):
                o_cw[:, pl.ds(j * q, q)] = cwg[j].astype(F32)

        n = lanes_at(t, big)
        dn = dot(wmx[d], dmx[:, n]).astype(BF16) * gp[d, :, n]
        pT[...] += dot_nt(dn, fx[d, :, n])
        grad = dot(aw[d], dn)
        dsend[d, :, n] = grad[:MAIN].astype(BF16)
        d4[:, n] = grad[MAIN : MAIN + 8]

        @pl.when(t == NT - 1)
        def _():
            pw = pT[...].T * KAPPA
            qs[d, :, pl.ds(0, hid)] = jnp.sum(pw * wall[d, wrow, :].astype(F32), axis=0, keepdims=True)
            qs[d, :, pl.ds(hid, hid)] = pw[ONES : ONES + 1, :]
            ps[d] = pw[:FP].astype(BF16)
            pp_copy(d).start()
            pack4(d4, dtail.at[d])

            @pl.when(dd < HOPS - 1)
            def _():
                q_copy(d).start()
                d_copy(d).start()
                dt_copy(d).start()

    @pl.loop(1, HOPS)
    def _(d):
        done(q_copy(d))

    qr[r] = qs[0] + (qv[1] + qv[2] + qv[3])
    rows_start(qr, "qr")
    own_d = pltpu.make_async_copy(dsend.at[0], o_d.at[h], ss.at[names["d"]])
    own_d.start()
    own_dt = pltpu.make_async_copy(dtail.at[0], o_dt.at[h], ss.at[names["dt"]])
    own_dt.start()

    p_half(0)

    @pl.loop(1, HOPS)
    def _(d):
        done(p_copy(d))

    psum = phalf[0].astype(F32) + (prv[1].astype(F32) + prv[2].astype(F32) + prv[3].astype(F32))
    pz[zi] = psum.astype(BF16)

    def pz_copy(e, which):
        return rc(pz.at[which], pz.at[which], "pz", e, h, lax.rem(zi + e, Z) * 2 + c)

    @functools.partial(each, 1, Z)
    def _(e):
        pz_copy(e, zi).start()

    @functools.partial(each, 1, Z)
    def _(e):
        zg_copy(e, zi).wait_send()
        zg_copy(e, lax.rem(zi + Z - e, Z)).wait_recv()

    ddm_copy(c).start()

    rows_wait(qr, "qr")
    qt = total(qr, R)
    db = qt[:, hid:]
    dgn = inv * (qt[:, :hid] - mean * db)
    o_small[pl.ds(2, 1), :] = dgn
    o_small[pl.ds(3, 1), :] = db
    c1 = scale * db * inv_n
    c2 = inv * scale * dgn * inv_n
    shift = c1 - mean * c2
    row = lax.broadcasted_iota(jnp.int32, (128, hid), 0)
    q1, q2 = split2(jnp.where(row == ONES, shift, wown32 * c2))
    o_m[...] = (dot_nt(wown, q1) + dot_nt(wown, q2))[:FP]
    gd_copy(c).wait_send()
    gd_copy(1 - c).wait_recv()
    g1, g2, g3 = split3(jnp.concatenate([gfin[0], gfin[1]], axis=0))
    gq = dot(g1, q1) + dot(g2, q1) + dot(g3, q1) + dot(g1, q2) + dot(g2, q2)

    @functools.partial(each, 1, Z)
    def _(e):
        pz_copy(e, zi).wait_send()
        pz_copy(e, lax.rem(zi + Z - e, Z)).wait_recv()

    pfin[c] = total(pz, Z).astype(BF16)

    def pd_copy(core):
        return rc(pfin.at[core], pfin.at[core], "pd", 0, h, sib)

    pd_copy(c).start()
    ddm_copy(c).wait_send()
    ddm_copy(1 - c).wait_recv()
    o_mix[...] = fin[...]

    pd_copy(c).wait_send()
    pd_copy(1 - c).wait_recv()
    ptot = jnp.concatenate([pfin[0], pfin[1]], axis=1).astype(F32)
    o_gw[...] = ptot * scale - gq[:FP]
    own_d.wait()
    own_dt.wait()
    own_lp.wait()

    @pl.loop(1, HOPS)
    def _(d):
        done(d_copy(d))
        done(dt_copy(d))
        done(lp_copy(d, 0))
        done(lp_copy(d, 1))


def last_kernel(
    nodes,
    ft, d, dt, lp, m, mix, gw, small, cw,
    o_lp, o_gf, o_mix, o_gw, o_gg, o_gb, o_hg, o_hb, o_cw, o_cb, o_loss, low,
):
    feat, n = ft.shape
    ncls = o_lp.shape[0]
    o_lp[...] = lp[...].astype(F32)[:ncls]
    mm = m[...]
    f = ft[...]
    fix = dot(mm[:, :feat].astype(BF16), f) + mm[:, ONES : ONES + 1]
    tail = dt[0].astype(F32)
    for b in range(4):
        low[pl.ds(0, 4), pl.ds(b * (n // 4), n // 4)] = tail[4 * b : 4 * b + 4]
    gf = jnp.concatenate([d[0].astype(F32), low[...]], axis=0)[:feat] - fix[:feat]
    if STRIDED:
        flat = o_gf.reshape(feat * (n // 128), 128)
        for i in range(n // 128):
            flat[pl.ds(i, feat, stride=n // 128), :] = gf[:, i * 128 : (i + 1) * 128]
    else:
        for i in range(n // 128):
            o_gf[:, i, :] = gf[:, i * 128 : (i + 1) * 128]

    @pl.when(pl.program_id(0) == 0)
    def _():
        hid = mix.shape[1]
        o_mix[...] = mix[...].astype(F32)
        for i in range(hid // 128):
            o_gw[:, i, :] = gw[pl.ds(0, feat), pl.ds(i * 128, 128)]
        o_hg[...] = small[pl.ds(0, 1), :]
        o_hb[...] = small[pl.ds(1, 1), :]
        o_gg[...] = small[pl.ds(2, 1), :]
        o_gb[...] = small[pl.ds(3, 1), :]
        o_cw[...] = cw[pl.ds(0, ncls), :]
        o_cb[...] = small[pl.ds(4, 1), pl.ds(0, ncls)]
        o_loss[...] = jnp.sum(small[pl.ds(4, 1), pl.ds(128, 128)], axis=1, keepdims=True) * (-1.0 / nodes)


def shards(
    R, features, branch_weight, branch_gain, branch_bias, mix_weight, mixing_norm_gain, mixing_norm_bias,
    class_weight, class_bias, labels, hop_mask,
):
    local, feat = features.shape[1:]
    hid = mix_weight.shape[0]
    ncls = class_weight.shape[1]
    nodes = local * R
    sub = local // HOPS
    Z = R // 2
    half = hid // 2
    S = min(Z, 2)
    G2, qrows = Z // S, half // S
    zrows, zcols = chunk(0, 0, qrows, G2, hid)
    assert feat == ONES and ncls == 47 and local // hop_mask.shape[0] == 128
    ft = features[0].T
    sd = jax.ShapeDtypeStruct
    vm = pl.BlockSpec(memory_space=pltpu.VMEM)
    hbm = pl.BlockSpec(memory_space=pl.ANY)
    _, nsem = sem_plan(R)
    V = pltpu.VMEM
    outs = pl.pallas_call(
        functools.partial(main_kernel, R, nodes),
        grid=(1,),
        out_shape=(
            sd((48, local), BF16),
            sd((HOPS, MAIN, sub), BF16),
            sd((HOPS, 16, sub // 4), BF16),
            sd((FP, 128), F32),
            sd((hid, hid), BF16),
            sd((FP, hid), F32),
            sd((8, hid), F32),
            sd((48, hid), F32),
        ),
        in_specs=[hbm, pl.BlockSpec((16, local), lambda i: (MAIN // 16, 0))]
        + [vm] * 9
        + [pl.BlockSpec(memory_space=pltpu.SMEM)],
        out_specs=(hbm, hbm, hbm, vm, vm, vm, vm, vm),
        scratch_shapes=[
            V((128, local), BF16),
            V((HOPS, 128, sub), BF16),
            V((HOPS, 16, sub // 4), BF16),
            V((HOPS, 16, sub // 4), BF16),
            V((48, sub // 4), F32),
            V((HOPS, hid + 128, hid), BF16),
            V((HOPS, hid, 256), BF16),
            V((HOPS, FP, hid), BF16),
            V((HOPS, hid, hid), BF16),
            V((HOPS, 16, sub), BF16),
            V((HOPS, hid, sub), BF16),
            V((HOPS, hid, sub), BF16),
            V((hid, sub), F32),
            V((hid, sub), F32),
            V((hid, sub), BF16),
            V((128, 128), F32),
            V((64, 128), F32),
            V((Z, 64, 128), F32),
            V((2, 64, 128), F32),
            V((R, 1, 2 * hid), F32),
            V((HOPS, 1, 2 * hid), F32),
            V((HOPS, 1, 2 * hid), F32),
            V((R, 1, 2 * hid), F32),
            V((HOPS, 1, 2 * hid + 256), F32),
            V((R, 1, 2 * hid + 256), F32),
            V((HOPS, 48, hid // HOPS), BF16),
            V((HOPS, 48, hid // HOPS), BF16),
            V((R, 48, hid // HOPS), BF16),
            V((HOPS, 48, hid // HOPS), BF16),
            V((48, sub), BF16),
            V((128, hid), F32),
            V((hid, 128), BF16),
            V((8, 128), F32),
            V((hid, min(2 * TILE, sub)), BF16),
            V((128, min(2 * TILE, sub)), BF16),
            V((hid, 128), F32),
            V((hid, 128), F32),
            V((96, 128), F32),
            V((48, hid), F32),
            V((3, hid, 128), F32),
            V((HOPS, hid, hid), BF16),
            V((HOPS, half, hid), BF16),
            V((HOPS, qrows, hid), BF16),
            V((HOPS, qrows, hid), BF16),
            V((max(G2, 2), zrows.size, zcols.size), BF16),
            V((hid, hid), BF16),
            V((HOPS, MAIN, sub), BF16),
            V((8, sub), F32),
            V((HOPS, 16, sub // 4), BF16),
            V((hid, 128), F32),
            V((HOPS, FP, hid), BF16),
            V((HOPS, FP, half), BF16),
            V((HOPS, FP, half), BF16),
            V((HOPS, FP, half), BF16),
            V((HOPS, 1, 2 * hid), F32),
            V((HOPS, 1, 2 * hid), F32),
            V((R, 1, 2 * hid), F32),
            V((Z, FP, half), BF16),
            V((2, FP, half), BF16),
            pltpu.SemaphoreType.DMA((nsem,)),
            pltpu.SemaphoreType.DMA((nsem,)),
        ],
        compiler_params=pltpu.CompilerParams(
            collective_id=0, has_side_effects=True, vmem_limit_bytes=63 * 1024 * 1024
        ),
        cost_estimate=pl.CostEstimate(flops=2 * 8 * 10**9, bytes_accessed=10**7, transcendentals=10**7),
        name="main",
    )(
        ft, ft, branch_weight[0], branch_gain, branch_bias, mix_weight, mixing_norm_gain[None], mixing_norm_bias[None],
        class_weight.T, class_bias[None], labels[None], hop_mask.T,
    )
    lp, dd, dt, m, mix, gw, small, cw = outs
    nb = sub
    whole = lambda shape: pl.BlockSpec(shape, lambda i: (0,) * len(shape))
    lp, gf, mix, gw, gg, gb, hg, hb, cw, cb, loss = pl.pallas_call(
        functools.partial(last_kernel, nodes),
        grid=(local // nb,),
        out_shape=(
            sd((ncls, local), F32),
            sd((feat, local // 128, 128), F32),
            sd((hid, hid), F32),
            sd((feat, hid // 128, 128), F32),
            sd((1, hid), F32),
            sd((1, hid), F32),
            sd((1, hid), F32),
            sd((1, hid), F32),
            sd((ncls, hid), F32),
            sd((1, ncls), F32),
            sd((1, 1), F32),
        ),
        in_specs=[
            pl.BlockSpec((feat, nb), lambda i: (0, i)),
            pl.BlockSpec((1, MAIN, nb), lambda i: (i, 0, 0)),
            pl.BlockSpec((1, 16, nb // 4), lambda i: (i, 0, 0)),
            pl.BlockSpec((48, nb), lambda i: (0, i)),
            whole((FP, 128)),
            whole((hid, hid)),
            whole((FP, hid)),
            whole((8, hid)),
            whole((48, hid)),
        ],
        out_specs=(
            pl.BlockSpec((ncls, nb), lambda i: (0, i)),
            pl.BlockSpec((feat, nb // 128, 128), lambda i: (0, i, 0)),
            whole((hid, hid)),
            whole((feat, hid // 128, 128)),
            whole((1, hid)),
            whole((1, hid)),
            whole((1, hid)),
            whole((1, hid)),
            whole((ncls, hid)),
            whole((1, ncls)),
            whole((1, 1)),
        ),
        scratch_shapes=[V((8, nb), F32)],
        compiler_params=pltpu.CompilerParams(vmem_limit_bytes=60 * 1024 * 1024),
        name="last",
    )(ft, dd, dt, lp, m, mix, gw, small, cw)
    return (
        lp.T,
        loss[0, 0],
        with_layout_constraint(gf.reshape(feat, 1, local), Layout((0, 1, 2))).transpose(1, 2, 0),
        gw.reshape(1, feat, hid),
        gg,
        gb,
        mix,
        hg[0],
        hb[0],
        cw.T,
        cb[0],
    )


def solution(mesh):
    placed = (
        P("hop", "rows", None), P("hop", None, None), P("hop", None), P("hop", None), P("hop", None),
        P(), P(), P(), P(), P("rows"), P("rows", None),
    )
    assert mesh.shape["hop"] == HOPS
    return jax.shard_map(
        functools.partial(shards, mesh.shape["rows"]),
        mesh=mesh,
        in_specs=placed,
        out_specs=(
            P("rows", None), P(), P("hop", "rows", None), P("hop", None, None), P("hop", None), P("hop", None),
            P("hop", None), P(), P(), P(), P(),
        ),
        check_vma=False,
    )
```

```python
import functools
import math

import jax
import jax.numpy as jnp
from jax import lax
from jax.experimental import pallas as pl
from jax.experimental.layout import Layout, with_layout_constraint
from jax.experimental.pallas import tpu as pltpu
from jax.sharding import PartitionSpec as P

MESH = pl.DeviceIdType.MESH
EPS = 1e-05
HOPS = 4
ONES = 100
FP = 112
MAIN = 96
TILE = 256
STRIDED = True
C0 = math.sqrt(2.0 / math.pi)
C1 = C0 * 0.044715
KAPPA = C1 ** (1.0 / 3.0)
ALPHA = C0 / KAPPA
F32 = jnp.float32
BF16 = jnp.bfloat16


def dot(a, b):
    return lax.dot_general(a, b, (((1,), (0,)), ((), ())), preferred_element_type=F32)


def dot_nt(a, b):
    return lax.dot_general(a, b, (((1,), (1,)), ((), ())), preferred_element_type=F32)


def split2(x):
    hi = x.astype(BF16)
    return hi, (x - hi.astype(F32)).astype(BF16)


def split3(x):
    hi = x.astype(BF16)
    rest = x - hi.astype(F32)
    mid = rest.astype(BF16)
    return hi, mid, (rest - mid.astype(F32)).astype(BF16)


def gelu_slope(z):
    u = z * z
    t = jnp.tanh(z * (C0 + C1 * u))
    s = 0.5 * t + 0.5
    g = z * s
    return g, s + (g - g * s) * (2.0 * C0 + 6.0 * C1 * u)


def scaled_gelu_slope(y):
    u = y * y
    t = jnp.tanh(y * (u + ALPHA))
    up = t + 1.0
    g = y * up
    return g, up + (g * (1.0 - t)) * (3.0 * u + ALPHA)


def fold(x):
    total = x[:, :128]
    for i in range(1, x.shape[1] // 128):
        total = total + x[:, i * 128 : (i + 1) * 128]
    return total


def spread(c, n):
    return jnp.concatenate([c] * (n // 128), axis=1)


def row_of(acc):
    return jnp.sum(acc.T, axis=0, keepdims=True)


def col_of(row):
    return jnp.broadcast_to(row, (128, row.shape[1])).T


def each(lo, hi, body):
    if hi - lo == 1:
        body(lo)
    elif hi > lo:
        pl.loop(lo, hi)(body)


class Alloc:
    def __init__(self):
        self.n = 0

    def __call__(self, count):
        base = self.n
        self.n += count
        return base


def sem_plan(R):
    Z = R // 2
    a = Alloc()
    names = {}
    for name, count in (
        ("feat", 4), ("ft", 4), ("loc", 1), ("ws", 4), ("zf", 4), ("dd", 4), ("s1", R), ("ab", 4), ("gp", 1), ("gz", Z), ("gd", 1),
        ("s2h", 4), ("s2r", R), ("s3h", 4), ("s3r", R), ("lp", 8), ("cwh", 4), ("cwr", R), ("cwg", 4),
        ("pair", 4), ("z1", 4), ("hop", 4), ("zr", Z), ("zg", Z), ("ddm", 1), ("d", 4), ("dt", 4), ("p", 4), ("q", 4),
        ("qr", R), ("pp", 4), ("pz", Z), ("pd", 1),
    ):
        names[name] = a(count)
    return names, a.n


def chunk(base, i, rows, pieces, cols):
    if rows // pieces >= 16:
        take = rows // pieces
        return pl.ds(pl.multiple_of(base + i * take, 16), take), pl.ds(0, cols)
    m = 16 * pieces // rows
    wide = cols // m
    return (
        pl.ds(pl.multiple_of(base + (i // m) * 16, 16), 16),
        pl.ds(pl.multiple_of((i % m) * wide, 128), wide),
    )


def main_kernel(
    R,
    nodes,
    ft, ft4, wb, bgain, bbias, wm, gain2, bias2, wc, cb, lab, msk,
    o_lp, o_d, o_dt, o_m, o_mix, o_gw, o_small, o_cw,
    fs, fx, ftail, frt, st4, wall, wl, aw, wmx, keep, mi, gp, mixed, dn2, dmx,
    gown, gpr, gz, gfin, s1, ab, s2h, s2r, s3h, s3r, cwp, cwh, cwr, cwg, lps,
    wcs, wcNs, cbs, hb, dlp, acc0, acc1, accl, accw, cols,
    dmp, pr, z1r, hr, zr, fin, dsend, d4, dtail, pT, ps, ph, phalf, prv, qs, qv, qr, pz, pfin,
    ss, rs,
):
    names, _ = sem_plan(R)
    Z = R // 2
    h = lax.axis_index("hop")
    r = lax.axis_index("rows")
    c = lax.rem(r, 2)
    zi = lax.div(r, 2)
    sib = r + 1 - 2 * c
    local = ft.shape[1]
    sub = local // HOPS
    hid = wm.shape[0]
    half = hid // 2
    big = min(2 * TILE, sub)
    UN = big // TILE
    NT = sub // big
    inv_n = 1.0 / nodes

    def peer(d):
        x = lax.rem(h + d, 2)
        y = lax.rem(lax.div(h, 2) + lax.div(d, 2), 2)
        return 2 * y + x

    def rc(src, dst, name, i, hh, rr):
        return pltpu.make_async_remote_copy(
            src_ref=src, dst_ref=dst, send_sem=ss.at[names[name] + i], recv_sem=rs.at[names[name] + i],
            device_id=(hh, rr), device_id_type=MESH,
        )

    def done(cp):
        cp.wait_send()
        cp.wait_recv()

    def lanes_at(i, n):
        return pl.ds(pl.multiple_of(i * n, n), n)

    barrier = pltpu.get_barrier_semaphore()

    def greet(hh, rr):
        pl.semaphore_signal(barrier, inc=1, device_id=(hh, rr), device_id_type=MESH)

    @pl.loop(1, HOPS)
    def _(d):
        greet(peer(d), r)

    @functools.partial(each, 1, R)
    def _(e):
        greet(h, lax.rem(r + e, R))

    def rows_start(buf, name):
        @functools.partial(each, 1, R)
        def _(e):
            rc(buf.at[r], buf.at[r], name, e, h, lax.rem(r + e, R)).start()

    def rows_wait(buf, name):
        @functools.partial(each, 1, R)
        def _(e):
            src = lax.rem(r + R - e, R)
            done(rc(buf.at[src], buf.at[src], name, e, h, lax.rem(r + e, R)))

    def hops_start(buf, name):
        @pl.loop(1, HOPS)
        def _(d):
            rc(buf.at[h], buf.at[h], name, d, peer(d), r).start()

    def hops_wait(buf, name):
        @pl.loop(1, HOPS)
        def _(d):
            done(rc(buf.at[peer(d)], buf.at[peer(d)], name, d, peer(d), r))

    def total(buf, n, dtype=F32):
        return lax.fori_loop(1, n, lambda i, t: t + buf[i].astype(dtype), buf[0].astype(dtype))

    loc = pltpu.make_async_copy(ft.at[pl.ds(0, MAIN), :], fs.at[pl.ds(0, MAIN), :], ss.at[names["loc"]])
    loc.start()

    def pack4(src, dst):
        n = st4.shape[1]
        for b in range(4):
            st4[pl.ds(4 * b, 4), :] = src[pl.ds(0, 4), pl.ds(b * n, n)].astype(F32)
        dst[...] = st4[pl.ds(0, 16), :].astype(BF16)

    def unpack4(src, dst):
        n = st4.shape[1]
        row = lax.broadcasted_iota(jnp.int32, (32, n), 0)
        st4[pl.ds(0, 16), :] = src[...].astype(F32)
        st4[pl.ds(16, 32), :] = jnp.where(row == ONES - MAIN, 1.0, 0.0)
        for b in range(4):
            st4[pl.ds(16, 4), :] = st4[pl.ds(4 * b, 4), :]
            dst[pl.ds(MAIN, 32), pl.ds(b * n, n)] = st4[pl.ds(16, 32), :].astype(BF16)

    wrow = pl.ds(hid, 128)
    wall[0, pl.ds(hid + 96, 32), :] = jnp.zeros((32, hid), BF16)
    wall[0, pl.ds(hid, 100), :] = wb[...]

    @pl.loop(0, hid // 128)
    def _(i):
        k = lanes_at(i, 128)
        wall[0, pl.ds(0, hid), k] = wm[k, :].astype(F32).T.astype(BF16)

    def feat_copy(d):
        rows = pl.ds(0, MAIN)
        return rc(fs.at[rows, lanes_at(peer(d), sub)], fx.at[d, rows, :], "feat", d, peer(d), r)

    def ft_copy(d):
        return rc(ftail.at[peer(d)], frt.at[d], "ft", d, peer(d), r)

    pl.semaphore_wait(barrier, HOPS - 1 + R - 1)

    S = min(Z, 2)
    part = (hid + 128) // (2 * S)
    zpar = lax.rem(zi, S)
    zmate = zi + (S - 1) - 2 * (S - 1) * zpar

    def part_rows(core, par):
        return pl.ds(pl.multiple_of((core * S + par) * part, 16), part)

    def ws_copy(d):
        rows = part_rows(c, zpar)
        return rc(wall.at[0, rows, :], wall.at[d, rows, :], "ws", d, peer(d), r)

    def zf_copy(d, par):
        ref = wall.at[d, part_rows(c, par), :]
        return rc(ref, ref, "zf", d, h, 2 * zmate + c)

    def dd_copy(d, core):
        ref = wall.at[d, pl.ds(pl.multiple_of(core * S * part, 16), S * part), :]
        return rc(ref, ref, "dd", d, h, sib)

    first, second = 1 + c, 2 - c
    ws_copy(first).start()
    ws_copy(second).start()
    ws_copy(HOPS - 1).start()
    loc.wait()
    feat_copy(first).start()
    feat_copy(second).start()

    @pl.loop(0, HOPS)
    def _(j):
        lanes = lanes_at(j, sub)
        pack4(ft4.at[:, lanes], ftail.at[j])
        unpack4(ftail.at[j], fs.at[:, lanes])


    @pl.loop(1, HOPS)
    def _(d):
        ft_copy(d).start()

    fx0 = pltpu.make_async_copy(fs.at[:, lanes_at(h, sub)], fx.at[0], ss.at[names["loc"]])
    fx0.start()

    def gram(i, g):
        f = fs[:, lanes_at(i, sub)]
        return g + dot_nt(f, f)

    g = lax.fori_loop(0, HOPS, gram, jnp.zeros((128, 128), F32))
    wown = wall[0, wrow, :]
    wown32 = wown.astype(F32)
    g1, g2, g3 = split3(g)
    gw = dot(g1, wown) + dot(g2, wown) + dot(g3, wown)
    s1[r, :, pl.ds(0, hid)] = gw[ONES : ONES + 1, :]
    s1[r, :, pl.ds(hid, hid)] = jnp.sum(gw * wown32, axis=0, keepdims=True)
    rows_start(s1, "s1")
    gown[...] = g

    @pl.loop(0, HOPS * (sub // 128))
    def _(i):
        d = lax.div(i, sub // 128)
        b = lax.rem(i, sub // 128)
        late = peer(d) - 2
        m = jnp.where(late >= 0, msk[jnp.maximum(late, 0), h * (sub // 128) + b], 1)
        keep[d, :, lanes_at(b, 128)] = jnp.full((16, 128), 0.5 * m.astype(F32)).astype(BF16)

    wcs[...] = jnp.zeros(wcs.shape, F32)
    wcs[pl.ds(0, wc.shape[0]), :] = wc[...].astype(F32)
    cbs[...] = jnp.zeros(cbs.shape, F32)
    cbs[pl.ds(0, 1), pl.ds(0, cb.shape[1])] = cb[...]
    ncls = wc.shape[0]

    @pl.loop(0, hid // 16)
    def _(i):
        rows = lanes_at(i, 16)
        mixed[rows, :] = jnp.zeros((16, sub), F32)
        mi[0, rows, pl.ds(0, big)] = jnp.zeros((16, big), BF16)

    fx0.wait()

    rows_wait(s1, "s1")
    st = total(s1, R)
    mean = st[:, :hid] * inv_n
    var = st[:, hid:] * inv_n - mean * mean
    inv = lax.rsqrt(var + EPS)
    scale = inv * bgain[...]
    ab[0, :, pl.ds(0, hid)] = scale
    ab[0, :, pl.ds(hid, hid)] = bbias[...] - mean * scale

    def ab_copy(d):
        return rc(ab.at[0], ab.at[d], "ab", d, peer(d), r)

    @pl.loop(1, HOPS)
    def _(d):
        ab_copy(d).start()

    def prepare(d):
        a = ab[d, :, pl.ds(0, hid)]
        b = ab[d, :, pl.ds(hid, hid)]
        ws = wall[d, wrow, :].astype(F32) * (a * KAPPA)
        aw[d] = ws[:FP].astype(BF16)
        row = lax.broadcasted_iota(jnp.int32, (128, hid), 0)
        wt = jnp.where(row == ONES, b * KAPPA, ws).T
        hi, lo = split2(wt)
        wl[d, :, pl.ds(0, 128)] = hi
        wl[d, :, pl.ds(128, 128)] = lo

    g_pair = rc(gown.at[lanes_at(1 - c, 64), :], gpr, "gp", 0, h, sib)

    def gz_copy(e, which):
        return rc(gz.at[which], gz.at[which], "gz", e, h, lax.rem(zi + e, Z) * 2 + c)

    def gd_copy(core):
        return rc(gfin.at[core], gfin.at[core], "gd", 0, h, sib)

    @pl.loop(0, HOPS * NT)
    def _(it):
        d = lax.div(it, NT)
        t = lax.rem(it, NT)

        @pl.when(t == 0)
        def _():
            @pl.when(d > 0)
            def _():
                done(feat_copy(d))
                done(ft_copy(d))
                unpack4(frt.at[d], fx.at[d])
                dd_copy(d, c).wait_send()
                dd_copy(d, 1 - c).wait_recv()
                done(ab_copy(d))

            prepare(d)

        if S > 1:

            @pl.when(it == min(1, NT - 1))
            def _():
                @pl.loop(1, HOPS)
                def _(j):
                    done(ws_copy(j))

                zf_copy(1, zpar).start()

        @pl.when(it == min(2, NT - 1))
        def _():
            feat_copy(HOPS - 1).start()

        @pl.when(jnp.logical_and(t == NT - 1, d < HOPS - 1))
        def _():
            if S > 1:
                zf_copy(d + 1, zpar).wait_send()
                zf_copy(d + 1, 1 - zpar).wait_recv()

                @pl.when(d < HOPS - 2)
                def _():
                    zf_copy(d + 2, zpar).start()

            else:
                done(ws_copy(d + 1))
            dd_copy(d + 1, c).start()

        @pl.when(it == 2 * NT)
        def _():
            g_pair.start()

        @pl.when(it == 3 * NT)
        def _():
            done(g_pair)
            gz[zi] = gown[lanes_at(c, 64), :] + gpr[...]

            @functools.partial(each, 1, Z)
            def _(e):
                gz_copy(e, zi).start()

        pit = jnp.maximum(it - 1, 0)
        pd = lax.div(pit, NT)
        pt = lax.rem(pit, NT)
        adds = []
        for u in range(UN):
            adds.append(dot(wall[pd, pl.ds(0, hid), :], mi[pd, :, lanes_at(pt * UN + u, TILE)]))
        for u in range(UN):
            n = lanes_at(t * UN + u, TILE)
            f = fx[d, :, n]
            z = dot(wl[d], jnp.concatenate([f, f], axis=0))
            k = keep[d, :, n]
            k = jnp.concatenate([k] * 4, axis=0)
            for i in range(0, hid, 64):
                g1, d1 = scaled_gelu_slope(z[i : i + 64].astype(BF16))
                g2, d2 = scaled_gelu_slope(g1 * k)
                mi[d, pl.ds(i, 64), n] = g2
                gp[d, pl.ds(i, 64), n] = d1 * d2 * k
        for u in range(UN):
            n = lanes_at(pt * UN + u, TILE)
            mixed[:, n] = mixed[:, n] + adds[u]

    acc0[...] = jnp.zeros(acc0.shape, F32)
    acc1[...] = jnp.zeros(acc1.shape, F32)

    @pl.loop(0, UN)
    def _(u):
        n = lanes_at((NT - 1) * UN + u, TILE)
        mixed[:, n] = mixed[:, n] + dot(wall[HOPS - 1, pl.ds(0, hid), :], mi[HOPS - 1, :, n])

    @pl.loop(0, hid // 32)
    def _(i):
        rows = lanes_at(i, 32)
        x = mixed[rows, :]
        acc0[rows, :] = fold(x)
        acc1[rows, :] = fold(x * x)

    def natural(lo, hi):
        @pl.loop(lo * (hid // 128), hi * (hid // 128))
        def _(i):
            d = lax.div(i, hid // 128)
            k = lanes_at(lax.rem(i, hid // 128), 128)
            wmx[d, k, :] = wall[d, pl.ds(0, hid), k].astype(F32).T.astype(BF16)

    s2h[h, :, pl.ds(0, hid)] = row_of(acc0[...])
    s2h[h, :, pl.ds(hid, hid)] = row_of(acc1[...])
    hops_start(s2h, "s2h")
    natural(0, 2)
    hops_wait(s2h, "s2h")
    s2r[r] = total(s2h, HOPS)
    rows_start(s2r, "s2r")
    natural(2, HOPS)
    wc48 = wcs[pl.ds(0, 48), :].astype(BF16)
    wcNs[...] = wcs[...].T.astype(BF16)
    crow = lax.broadcasted_iota(jnp.int32, (128, 128), 0)
    cbc = jnp.where(crow < ncls, jnp.broadcast_to(cbs[pl.ds(0, 1), :], (128, 128)).T, -1e30)[:48]
    rows_wait(s2r, "s2r")
    st2 = total(s2r, R)
    mean2 = st2[:, :hid] * inv_n
    inv2 = lax.rsqrt(st2[:, hid:] * inv_n - mean2 * mean2 + EPS * 4.0 * KAPPA * KAPPA)
    scale2 = inv2 * gain2[...]
    cols[0] = col_of(scale2)
    cols[1] = col_of(bias2[...] - mean2 * scale2)
    acc0[...] = jnp.zeros(acc0.shape, F32)
    acc1[...] = jnp.zeros(acc1.shape, F32)
    accl[...] = jnp.zeros(accl.shape, F32)
    accw[...] = jnp.zeros(accw.shape, F32)

    o_own = lanes_at(h, sub)

    def lp_copy(d, part):
        n = sub // 2
        return rc(
            lps.at[:, pl.ds(part * n, n)], o_lp.at[:, lanes_at(2 * h + part, n)], "lp", 4 * part + d, peer(d), r
        )

    dlp[...] = jnp.zeros(dlp.shape, BF16)
    HR = 128

    @pl.loop(0, NT)
    def _(t):
        n = lanes_at(t, big)

        if NT > 1:

            @pl.when(t == NT // 2)
            def _():
                @pl.loop(1, HOPS)
                def _(d):
                    lp_copy(d, 0).start()

        @pl.loop(0, hid // HR)
        def _(i):
            rows = lanes_at(i, HR)
            z2 = mixed[rows, n] * spread(cols[0, rows, :], big) + spread(cols[1, rows, :], big)
            gv, dg = gelu_slope(z2)
            hb[rows, :] = gv.astype(BF16)
            dn2[rows, n] = dg

        lg = dot(wc48, hb[...]) + spread(cbc, big)
        lg = lg - jnp.max(lg, axis=0, keepdims=True)
        ex = jnp.exp(lg)
        se = jnp.sum(ex, axis=0, keepdims=True)
        lp = lg - jnp.log(se)
        lps[:, n] = lp.astype(BF16)
        own = lanes_at(h * NT + t, big)
        hit = lax.broadcasted_iota(jnp.int32, (48, big), 0) == lab[:, own]
        accl[pl.ds(48, 48), :] += fold(jnp.where(hit, lp, 0.0))
        dl = ((ex / se - jnp.where(hit, 1.0, 0.0)) * inv_n).astype(BF16)
        accl[pl.ds(0, 48), :] += fold(dl.astype(F32))
        accw[...] += dot_nt(dl, hb[...])
        dlp[pl.ds(0, 48), :] = dl

        @pl.loop(0, hid // HR)
        def _(i):
            rows = lanes_at(i, HR)
            dn = dot(wcNs[rows, :], dlp[...]) * dn2[rows, n]
            dn2[rows, n] = dn
            acc0[rows, :] += fold(dn * mixed[rows, n])
            acc1[rows, :] += fold(dn)

    @pl.loop(1, HOPS)
    def _(d):
        if NT == 1:
            lp_copy(d, 0).start()
        lp_copy(d, 1).start()

    own_lp = pltpu.make_async_copy(lps, o_lp.at[:, o_own], ss.at[names["lp"]])
    own_lp.start()
    s3h[h, :, pl.ds(0, hid)] = row_of(acc0[...])
    s3h[h, :, pl.ds(hid, hid)] = row_of(acc1[...])
    zpad = jnp.zeros((80, 128), F32)
    s3h[h, :, pl.ds(2 * hid, 128)] = row_of(jnp.concatenate([accl[pl.ds(0, 48), :], zpad], axis=0))
    s3h[h, :, pl.ds(2 * hid + 128, 128)] = row_of(jnp.concatenate([accl[pl.ds(48, 48), :], zpad], axis=0))
    hops_start(s3h, "s3h")

    def cwh_copy(d):
        return rc(cwp.at[d], cwh.at[d], "cwh", d, peer(d), r)

    q = hid // HOPS

    @pl.loop(0, HOPS)
    def _(d):
        cwp[d] = accw[:, lanes_at(peer(d), q)].astype(BF16)

    hops_wait(s3h, "s3h")
    s3r[r] = total(s3h, HOPS)
    rows_start(s3r, "s3r")

    @pl.loop(1, HOPS)
    def _(d):
        cwh_copy(d).start()

    rows_wait(s3r, "s3r")
    st3 = total(s3r, R)
    db2 = st3[:, hid : 2 * hid]
    dg2t = inv2 * (st3[:, :hid] - mean2 * db2)
    o_small[pl.ds(0, 1), :] = dg2t
    o_small[pl.ds(1, 1), :] = db2
    o_small[pl.ds(4, 1), pl.ds(0, 256)] = st3[:, 2 * hid : 2 * hid + 256]
    o_small[pl.ds(4, 1), pl.ds(256, hid - 256)] = jnp.zeros((1, hid - 256), F32)
    t2 = scale2 * inv2 * dg2t * inv_n
    cols[1] = col_of(-t2)
    cols[2] = col_of(t2 * mean2 - scale2 * db2 * inv_n)

    @pl.loop(0, hid // 16)
    def _(i):
        rows = lanes_at(i, 16)
        v = dn2[rows, :] * spread(cols[0, rows, :], sub)
        v = v + mixed[rows, :] * spread(cols[1, rows, :], sub) + spread(cols[2, rows, :], sub)
        dmx[rows, :] = v.astype(BF16)

    @functools.partial(each, 1, Z)
    def _(e):
        gz_copy(e, zi).wait_send()
        gz_copy(e, lax.rem(zi + Z - e, Z)).wait_recv()

    gfin[c] = total(gz, Z)
    gd_copy(c).start()

    mine = lanes_at(c, half)
    theirs = lanes_at(1 - c, half)

    def pair_copy(d):
        return rc(dmp.at[d, theirs, :], pr.at[d], "pair", d, h, sib)

    qrows = half // S
    zown = pl.ds(pl.multiple_of(c * half + zpar * qrows, 16), qrows)
    zother = pl.ds(pl.multiple_of(c * half + (1 - zpar) * qrows, 16), qrows)

    def z1_copy(d):
        return rc(dmp.at[d, zother, :], z1r.at[d], "z1", d, h, 2 * zmate + c)

    def z1_start(d):
        if S > 1:
            z1_copy(d).start()

    def z1_sum(d):
        if S > 1:
            done(z1_copy(d))

            @pl.loop(0, qrows // 32)
            def _(i):
                rows = pl.ds(pl.multiple_of(c * half + zpar * qrows + i * 32, 32), 32)
                dmp[d, rows, :] = (dmp[d, rows, :].astype(F32) + z1r[d, lanes_at(i, 32), :].astype(F32)).astype(BF16)

    def hop_copy(d):
        return rc(dmp.at[d, zown, :], hr.at[d], "hop", d, peer(d), r)

    def pair_sum(d):
        done(pair_copy(d))

        @pl.loop(0, half // 32)
        def _(i):
            rows = pl.ds(pl.multiple_of(c * half + i * 32, 32), 32)
            dmp[d, rows, :] = (dmp[d, rows, :].astype(F32) + pr[d, lanes_at(i, 32), :].astype(F32)).astype(BF16)

    @pl.loop(0, HOPS)
    def _(i):
        d = HOPS - 1 - i

        dmp[d] = dot_nt(mi[d], dmx[...]).astype(BF16)
        pair_copy(d).start()

        @pl.when(i > 0)
        def _():
            pair_sum(d + 1)
            z1_start(d + 1)

        @pl.when(i > 1)
        def _():
            z1_sum(d + 2)
            hop_copy(d + 2).start()

    G2 = Z // S
    zq = lax.div(zi, S)

    def zr_copy(e, which):
        rows, lanes = chunk(0, which, qrows, G2, hid)
        return rc(hr.at[0, rows, lanes], zr.at[e], "zr", e, h, (lax.rem(zq + e, G2) * S + zpar) * 2 + c)

    def final_chunk(z):
        return chunk(c * half + lax.rem(z, S) * qrows, lax.div(z, S), qrows, G2, hid)

    def zg_copy(e, which):
        rows, lanes = final_chunk(which)
        ref = fin.at[rows, lanes]
        return rc(ref, ref, "zg", e, h, lax.rem(zi + e, Z) * 2 + c)

    def ddm_copy(core):
        ref = fin.at[lanes_at(core, half), :]
        return rc(ref, ref, "ddm", 0, h, sib)

    def d_copy(d):
        return rc(dsend.at[d], o_d.at[h], "d", d, peer(d), r)

    def dt_copy(d):
        return rc(dtail.at[d], o_dt.at[h], "dt", d, peer(d), r)

    def pp_copy(d):
        return rc(ps.at[d, :, theirs], ph.at[d], "pp", d, h, sib)

    def p_copy(d):
        return rc(phalf.at[d], prv.at[d], "p", d, peer(d), r)

    def p_half(d):
        done(pp_copy(d))
        phalf[d] = (ps[d, :, mine].astype(F32) + ph[d].astype(F32)).astype(BF16)

    def q_copy(d):
        return rc(qs.at[d], qv.at[d], "q", d, peer(d), r)

    @pl.loop(0, HOPS * NT)
    def _(it):
        dd = lax.div(it, NT)
        t = lax.rem(it, NT)
        d = HOPS - 1 - dd

        @pl.when(t == 0)
        def _():
            pT[...] = jnp.zeros(pT.shape, F32)

        @pl.when(jnp.logical_and(t == NT // 2, dd > 0))
        def _():
            p_half(d + 1)
            p_copy(d + 1).start()

        @pl.when(it == NT // 2)
        def _():
            pair_sum(0)
            z1_start(0)
            z1_sum(1)
            hop_copy(1).start()

        @pl.when(it == NT + NT // 2)
        def _():
            @pl.loop(1, HOPS)
            def _(j):
                done(cwh_copy(j))

            cw = cwp[0].astype(F32)
            for j in range(1, HOPS):
                cw = cw + cwh[j].astype(F32)
            cwr[r] = cw.astype(BF16)
            rows_start(cwr, "cwr")
            z1_sum(0)

        @pl.when(it == 2 * NT + NT // 2)
        def _():
            @pl.loop(1, HOPS)
            def _(j):
                done(hop_copy(j))

            @pl.loop(0, qrows // 32)
            def _(i):
                rows = lanes_at(i, 32)
                own = pl.ds(pl.multiple_of(c * half + zpar * qrows + i * 32, 32), 32)
                hsum = dmp[0, own, :].astype(F32)
                for j in range(1, HOPS):
                    hsum = hsum + hr[j, rows, :].astype(F32)
                hr[0, rows, :] = hsum.astype(BF16)

            @functools.partial(each, 1, G2)
            def _(e):
                zr_copy(e, lax.rem(zq + e, G2)).start()

            rows_wait(cwr, "cwr")
            cwg[h] = total(cwr, R, F32).astype(BF16)
            hops_start(cwg, "cwg")

        @pl.when(it == 3 * NT + NT // 2)
        def _():
            @functools.partial(each, 1, G2)
            def _(e):
                done(zr_copy(e, lax.rem(zq + e, G2)))

            rows, lanes = chunk(0, zq, qrows, G2, hid)
            zt = lax.fori_loop(1, G2, lambda e, v: v + zr[e].astype(F32), hr[0, rows, lanes].astype(F32))
            frows, flanes = final_chunk(zi)
            fin[frows, flanes] = zt.astype(BF16)

            @functools.partial(each, 1, Z)
            def _(e):
                zg_copy(e, zi).start()

            hops_wait(cwg, "cwg")
            for j in range(HOPS):
                o_cw[:, pl.ds(j * q, q)] = cwg[j].astype(F32)

        n = lanes_at(t, big)
        dn = dot(wmx[d], dmx[:, n]).astype(BF16) * gp[d, :, n]
        pT[...] += dot_nt(dn, fx[d, :, n])
        grad = dot(aw[d], dn)
        dsend[d, :, n] = grad[:MAIN].astype(BF16)
        d4[:, n] = grad[MAIN : MAIN + 8]

        @pl.when(t == NT - 1)
        def _():
            pw = pT[...].T * KAPPA
            qs[d, :, pl.ds(0, hid)] = jnp.sum(pw * wall[d, wrow, :].astype(F32), axis=0, keepdims=True)
            qs[d, :, pl.ds(hid, hid)] = pw[ONES : ONES + 1, :]
            ps[d] = pw[:FP].astype(BF16)
            pp_copy(d).start()
            pack4(d4, dtail.at[d])

            @pl.when(dd < HOPS - 1)
            def _():
                q_copy(d).start()
                d_copy(d).start()
                dt_copy(d).start()

    @pl.loop(1, HOPS)
    def _(d):
        done(q_copy(d))

    qr[r] = qs[0] + (qv[1] + qv[2] + qv[3])
    rows_start(qr, "qr")
    own_d = pltpu.make_async_copy(dsend.at[0], o_d.at[h], ss.at[names["d"]])
    own_d.start()
    own_dt = pltpu.make_async_copy(dtail.at[0], o_dt.at[h], ss.at[names["dt"]])
    own_dt.start()

    p_half(0)

    @pl.loop(1, HOPS)
    def _(d):
        done(p_copy(d))

    psum = phalf[0].astype(F32) + (prv[1].astype(F32) + prv[2].astype(F32) + prv[3].astype(F32))
    pz[zi] = psum.astype(BF16)

    def pz_copy(e, which):
        return rc(pz.at[which], pz.at[which], "pz", e, h, lax.rem(zi + e, Z) * 2 + c)

    @functools.partial(each, 1, Z)
    def _(e):
        pz_copy(e, zi).start()

    @functools.partial(each, 1, Z)
    def _(e):
        zg_copy(e, zi).wait_send()
        zg_copy(e, lax.rem(zi + Z - e, Z)).wait_recv()

    ddm_copy(c).start()

    rows_wait(qr, "qr")
    qt = total(qr, R)
    db = qt[:, hid:]
    dgn = inv * (qt[:, :hid] - mean * db)
    o_small[pl.ds(2, 1), :] = dgn
    o_small[pl.ds(3, 1), :] = db
    c1 = scale * db * inv_n
    c2 = inv * scale * dgn * inv_n
    shift = c1 - mean * c2
    row = lax.broadcasted_iota(jnp.int32, (128, hid), 0)
    q1, q2 = split2(jnp.where(row == ONES, shift, wown32 * c2))
    o_m[...] = (dot_nt(wown, q1) + dot_nt(wown, q2))[:FP]
    gd_copy(c).wait_send()
    gd_copy(1 - c).wait_recv()
    g1, g2, g3 = split3(jnp.concatenate([gfin[0], gfin[1]], axis=0))
    gq = dot(g1, q1) + dot(g2, q1) + dot(g3, q1) + dot(g1, q2) + dot(g2, q2)

    @functools.partial(each, 1, Z)
    def _(e):
        pz_copy(e, zi).wait_send()
        pz_copy(e, lax.rem(zi + Z - e, Z)).wait_recv()

    pfin[c] = total(pz, Z).astype(BF16)

    def pd_copy(core):
        return rc(pfin.at[core], pfin.at[core], "pd", 0, h, sib)

    pd_copy(c).start()
    ddm_copy(c).wait_send()
    ddm_copy(1 - c).wait_recv()
    o_mix[...] = fin[...]

    pd_copy(c).wait_send()
    pd_copy(1 - c).wait_recv()
    ptot = jnp.concatenate([pfin[0], pfin[1]], axis=1).astype(F32)
    o_gw[...] = ptot * scale - gq[:FP]
    own_d.wait()
    own_dt.wait()
    own_lp.wait()

    @pl.loop(1, HOPS)
    def _(d):
        done(d_copy(d))
        done(dt_copy(d))
        done(lp_copy(d, 0))
        done(lp_copy(d, 1))


def last_kernel(
    nodes,
    ft, d, dt, lp, m, mix, gw, small, cw,
    o_lp, o_gf, o_mix, o_gw, o_gg, o_gb, o_hg, o_hb, o_cw, o_cb, o_loss, low,
):
    feat, n = ft.shape
    ncls = o_lp.shape[0]
    o_lp[...] = lp[...].astype(F32)[:ncls]
    mm = m[...]
    f = ft[...]
    fix = dot(mm[:, :feat].astype(BF16), f) + mm[:, ONES : ONES + 1]
    tail = dt[0].astype(F32)
    for b in range(4):
        low[pl.ds(0, 4), pl.ds(b * (n // 4), n // 4)] = tail[4 * b : 4 * b + 4]
    gf = jnp.concatenate([d[0].astype(F32), low[...]], axis=0)[:feat] - fix[:feat]
    if STRIDED:
        flat = o_gf.reshape(feat * (n // 128), 128)
        for i in range(n // 128):
            flat[pl.ds(i, feat, stride=n // 128), :] = gf[:, i * 128 : (i + 1) * 128]
    else:
        for i in range(n // 128):
            o_gf[:, i, :] = gf[:, i * 128 : (i + 1) * 128]

    @pl.when(pl.program_id(0) == 0)
    def _():
        hid = mix.shape[1]
        o_mix[...] = mix[...].astype(F32)
        for i in range(hid // 128):
            o_gw[:, i, :] = gw[pl.ds(0, feat), pl.ds(i * 128, 128)]
        o_hg[...] = small[pl.ds(0, 1), :]
        o_hb[...] = small[pl.ds(1, 1), :]
        o_gg[...] = small[pl.ds(2, 1), :]
        o_gb[...] = small[pl.ds(3, 1), :]
        o_cw[...] = cw[pl.ds(0, ncls), :]
        o_cb[...] = small[pl.ds(4, 1), pl.ds(0, ncls)]
        o_loss[...] = jnp.sum(small[pl.ds(4, 1), pl.ds(128, 128)], axis=1, keepdims=True) * (-1.0 / nodes)


def shards(
    R, features, branch_weight, branch_gain, branch_bias, mix_weight, mixing_norm_gain, mixing_norm_bias,
    class_weight, class_bias, labels, hop_mask,
):
    local, feat = features.shape[1:]
    hid = mix_weight.shape[0]
    ncls = class_weight.shape[1]
    nodes = local * R
    sub = local // HOPS
    Z = R // 2
    half = hid // 2
    S = min(Z, 2)
    G2, qrows = Z // S, half // S
    zrows, zcols = chunk(0, 0, qrows, G2, hid)
    assert feat == ONES and ncls == 47 and local // hop_mask.shape[0] == 128
    ft = features[0].T
    sd = jax.ShapeDtypeStruct
    vm = pl.BlockSpec(memory_space=pltpu.VMEM)
    hbm = pl.BlockSpec(memory_space=pl.ANY)
    _, nsem = sem_plan(R)
    V = pltpu.VMEM
    outs = pl.pallas_call(
        functools.partial(main_kernel, R, nodes),
        grid=(1,),
        out_shape=(
            sd((48, local), BF16),
            sd((HOPS, MAIN, sub), BF16),
            sd((HOPS, 16, sub // 4), BF16),
            sd((FP, 128), F32),
            sd((hid, hid), BF16),
            sd((FP, hid), F32),
            sd((8, hid), F32),
            sd((48, hid), F32),
        ),
        in_specs=[hbm, pl.BlockSpec((16, local), lambda i: (MAIN // 16, 0))]
        + [vm] * 9
        + [pl.BlockSpec(memory_space=pltpu.SMEM)],
        out_specs=(hbm, hbm, hbm, vm, vm, vm, vm, vm),
        scratch_shapes=[
            V((128, local), BF16),
            V((HOPS, 128, sub), BF16),
            V((HOPS, 16, sub // 4), BF16),
            V((HOPS, 16, sub // 4), BF16),
            V((48, sub // 4), F32),
            V((HOPS, hid + 128, hid), BF16),
            V((HOPS, hid, 256), BF16),
            V((HOPS, FP, hid), BF16),
            V((HOPS, hid, hid), BF16),
            V((HOPS, 16, sub), BF16),
            V((HOPS, hid, sub), BF16),
            V((HOPS, hid, sub), BF16),
            V((hid, sub), F32),
            V((hid, sub), F32),
            V((hid, sub), BF16),
            V((128, 128), F32),
            V((64, 128), F32),
            V((Z, 64, 128), F32),
            V((2, 64, 128), F32),
            V((R, 1, 2 * hid), F32),
            V((HOPS, 1, 2 * hid), F32),
            V((HOPS, 1, 2 * hid), F32),
            V((R, 1, 2 * hid), F32),
            V((HOPS, 1, 2 * hid + 256), F32),
            V((R, 1, 2 * hid + 256), F32),
            V((HOPS, 48, hid // HOPS), BF16),
            V((HOPS, 48, hid // HOPS), BF16),
            V((R, 48, hid // HOPS), BF16),
            V((HOPS, 48, hid // HOPS), BF16),
            V((48, sub), BF16),
            V((128, hid), F32),
            V((hid, 128), BF16),
            V((8, 128), F32),
            V((hid, min(2 * TILE, sub)), BF16),
            V((128, min(2 * TILE, sub)), BF16),
            V((hid, 128), F32),
            V((hid, 128), F32),
            V((96, 128), F32),
            V((48, hid), F32),
            V((3, hid, 128), F32),
            V((HOPS, hid, hid), BF16),
            V((HOPS, half, hid), BF16),
            V((HOPS, qrows, hid), BF16),
            V((HOPS, qrows, hid), BF16),
            V((max(G2, 2), zrows.size, zcols.size), BF16),
            V((hid, hid), BF16),
            V((HOPS, MAIN, sub), BF16),
            V((8, sub), F32),
            V((HOPS, 16, sub // 4), BF16),
            V((hid, 128), F32),
            V((HOPS, FP, hid), BF16),
            V((HOPS, FP, half), BF16),
            V((HOPS, FP, half), BF16),
            V((HOPS, FP, half), BF16),
            V((HOPS, 1, 2 * hid), F32),
            V((HOPS, 1, 2 * hid), F32),
            V((R, 1, 2 * hid), F32),
            V((Z, FP, half), BF16),
            V((2, FP, half), BF16),
            pltpu.SemaphoreType.DMA((nsem,)),
            pltpu.SemaphoreType.DMA((nsem,)),
        ],
        compiler_params=pltpu.CompilerParams(
            collective_id=0, has_side_effects=True, vmem_limit_bytes=63 * 1024 * 1024
        ),
        cost_estimate=pl.CostEstimate(flops=2 * 8 * 10**9, bytes_accessed=10**7, transcendentals=10**7),
        name="main",
    )(
        ft, ft, branch_weight[0], branch_gain, branch_bias, mix_weight, mixing_norm_gain[None], mixing_norm_bias[None],
        class_weight.T, class_bias[None], labels[None], hop_mask.T,
    )
    lp, dd, dt, m, mix, gw, small, cw = outs
    nb = sub
    whole = lambda shape: pl.BlockSpec(shape, lambda i: (0,) * len(shape))
    lp, gf, mix, gw, gg, gb, hg, hb, cw, cb, loss = pl.pallas_call(
        functools.partial(last_kernel, nodes),
        grid=(local // nb,),
        out_shape=(
            sd((ncls, local), F32),
            sd((feat, local // 128, 128), F32),
            sd((hid, hid), F32),
            sd((feat, hid // 128, 128), F32),
            sd((1, hid), F32),
            sd((1, hid), F32),
            sd((1, hid), F32),
            sd((1, hid), F32),
            sd((ncls, hid), F32),
            sd((1, ncls), F32),
            sd((1, 1), F32),
        ),
        in_specs=[
            pl.BlockSpec((feat, nb), lambda i: (0, i)),
            pl.BlockSpec((1, MAIN, nb), lambda i: (i, 0, 0)),
            pl.BlockSpec((1, 16, nb // 4), lambda i: (i, 0, 0)),
            pl.BlockSpec((48, nb), lambda i: (0, i)),
            whole((FP, 128)),
            whole((hid, hid)),
            whole((FP, hid)),
            whole((8, hid)),
            whole((48, hid)),
        ],
        out_specs=(
            pl.BlockSpec((ncls, nb), lambda i: (0, i)),
            pl.BlockSpec((feat, nb // 128, 128), lambda i: (0, i, 0)),
            whole((hid, hid)),
            whole((feat, hid // 128, 128)),
            whole((1, hid)),
            whole((1, hid)),
            whole((1, hid)),
            whole((1, hid)),
            whole((ncls, hid)),
            whole((1, ncls)),
            whole((1, 1)),
        ),
        scratch_shapes=[V((8, nb), F32)],
        compiler_params=pltpu.CompilerParams(vmem_limit_bytes=60 * 1024 * 1024),
        name="last",
    )(ft, dd, dt, lp, m, mix, gw, small, cw)
    return (
        lp.T,
        loss[0, 0],
        with_layout_constraint(gf.reshape(feat, 1, local), Layout((0, 1, 2))).transpose(1, 2, 0),
        gw.reshape(1, feat, hid),
        gg,
        gb,
        mix,
        hg[0],
        hb[0],
        cw.T,
        cb[0],
    )


def solution(mesh):
    placed = (
        P("hop", "rows", None), P("hop", None, None), P("hop", None), P("hop", None), P("hop", None),
        P(), P(), P(), P(), P("rows"), P("rows", None),
    )
    assert mesh.shape["hop"] == HOPS
    return jax.shard_map(
        functools.partial(shards, mesh.shape["rows"]),
        mesh=mesh,
        in_specs=placed,
        out_specs=(
            P("rows", None), P(), P("hop", "rows", None), P("hop", None, None), P("hop", None), P("hop", None),
            P("hop", None), P(), P(), P(), P(),
        ),
        check_vma=False,
    )
```

```python
import functools
import math

import jax
import jax.numpy as jnp
from jax import lax
from jax.experimental import pallas as pl
from jax.experimental.layout import Layout, with_layout_constraint
from jax.experimental.pallas import tpu as pltpu
from jax.sharding import PartitionSpec as P

MESH = pl.DeviceIdType.MESH
EPS = 1e-05
HOPS = 4
ONES = 100
FP = 112
MAIN = 96
TILE = 256
STRIDED = True
C0 = math.sqrt(2.0 / math.pi)
C1 = C0 * 0.044715
KAPPA = C1 ** (1.0 / 3.0)
ALPHA = C0 / KAPPA
F32 = jnp.float32
BF16 = jnp.bfloat16


def dot(a, b):
    return lax.dot_general(a, b, (((1,), (0,)), ((), ())), preferred_element_type=F32)


def dot_nt(a, b):
    return lax.dot_general(a, b, (((1,), (1,)), ((), ())), preferred_element_type=F32)


def split2(x):
    hi = x.astype(BF16)
    return hi, (x - hi.astype(F32)).astype(BF16)


def split3(x):
    hi = x.astype(BF16)
    rest = x - hi.astype(F32)
    mid = rest.astype(BF16)
    return hi, mid, (rest - mid.astype(F32)).astype(BF16)


def gelu_slope(z):
    u = z * z
    t = jnp.tanh(z * (C0 + C1 * u))
    s = 0.5 * t + 0.5
    g = z * s
    return g, s + (g - g * s) * (2.0 * C0 + 6.0 * C1 * u)


def scaled_gelu_slope(y):
    u = y * y
    t = jnp.tanh(y * (u + ALPHA))
    up = t + 1.0
    g = y * up
    return g, up + (g * (1.0 - t)) * (3.0 * u + ALPHA)


def fold(x):
    total = x[:, :128]
    for i in range(1, x.shape[1] // 128):
        total = total + x[:, i * 128 : (i + 1) * 128]
    return total


def spread(c, n):
    return jnp.concatenate([c] * (n // 128), axis=1)


def row_of(acc):
    return jnp.sum(acc.T, axis=0, keepdims=True)


def col_of(row):
    return jnp.broadcast_to(row, (128, row.shape[1])).T


def each(lo, hi, body):
    if hi - lo == 1:
        body(lo)
    elif hi > lo:
        pl.loop(lo, hi)(body)


class Alloc:
    def __init__(self):
        self.n = 0

    def __call__(self, count):
        base = self.n
        self.n += count
        return base


def sem_plan(R):
    Z = R // 2
    a = Alloc()
    names = {}
    for name, count in (
        ("feat", 4), ("ft", 4), ("loc", 1), ("ws", 4), ("zf", 4), ("dd", 4), ("s1", R), ("ab", 4), ("gp", 1), ("gz", Z), ("gd", 1),
        ("s2h", 4), ("s2r", R), ("s3h", 4), ("s3r", R), ("lp", 4), ("cwh", 4), ("cwr", R), ("cwg", 4),
        ("pair", 4), ("z1", 4), ("hop", 4), ("zr", Z), ("zg", Z), ("ddm", 1), ("d", 4), ("dt", 4), ("p", 4), ("q", 4),
        ("qr", R), ("pp", 4), ("pz", Z), ("pd", 1),
    ):
        names[name] = a(count)
    return names, a.n


def chunk(base, i, rows, pieces, cols):
    if rows // pieces >= 16:
        take = rows // pieces
        return pl.ds(pl.multiple_of(base + i * take, 16), take), pl.ds(0, cols)
    m = 16 * pieces // rows
    wide = cols // m
    return (
        pl.ds(pl.multiple_of(base + (i // m) * 16, 16), 16),
        pl.ds(pl.multiple_of((i % m) * wide, 128), wide),
    )


def main_kernel(
    R,
    nodes,
    ft, ft4, wb, bgain, bbias, wm, gain2, bias2, wc, cb, lab, msk,
    o_lp, o_d, o_dt, o_m, o_mix, o_gw, o_small, o_cw,
    fs, fx, ftail, frt, st4, wall, wl, aw, wmx, keep, mi, gp, mixed, dn2, dmx,
    gown, gpr, gz, gfin, s1, ab, s2h, s2r, s3h, s3r, cwp, cwh, cwr, cwg, lps,
    wcs, wcNs, cbs, hb, dlp, acc0, acc1, accl, accw, cols,
    dmp, pr, z1r, hr, zr, fin, dsend, d4, dtail, pT, ps, ph, phalf, prv, qs, qv, qr, pz, pfin,
    ss, rs,
):
    names, _ = sem_plan(R)
    Z = R // 2
    h = lax.axis_index("hop")
    r = lax.axis_index("rows")
    c = lax.rem(r, 2)
    zi = lax.div(r, 2)
    sib = r + 1 - 2 * c
    local = ft.shape[1]
    sub = local // HOPS
    hid = wm.shape[0]
    half = hid // 2
    big = min(2 * TILE, sub)
    UN = big // TILE
    NT = sub // big
    inv_n = 1.0 / nodes

    def peer(d):
        x = lax.rem(h + d, 2)
        y = lax.rem(lax.div(h, 2) + lax.div(d, 2), 2)
        return 2 * y + x

    def rc(src, dst, name, i, hh, rr):
        return pltpu.make_async_remote_copy(
            src_ref=src, dst_ref=dst, send_sem=ss.at[names[name] + i], recv_sem=rs.at[names[name] + i],
            device_id=(hh, rr), device_id_type=MESH,
        )

    def done(cp):
        cp.wait_send()
        cp.wait_recv()

    def lanes_at(i, n):
        return pl.ds(pl.multiple_of(i * n, n), n)

    barrier = pltpu.get_barrier_semaphore()

    def greet(hh, rr):
        pl.semaphore_signal(barrier, inc=1, device_id=(hh, rr), device_id_type=MESH)

    @pl.loop(1, HOPS)
    def _(d):
        greet(peer(d), r)

    @functools.partial(each, 1, R)
    def _(e):
        greet(h, lax.rem(r + e, R))

    def rows_start(buf, name):
        @functools.partial(each, 1, R)
        def _(e):
            rc(buf.at[r], buf.at[r], name, e, h, lax.rem(r + e, R)).start()

    def rows_wait(buf, name):
        @functools.partial(each, 1, R)
        def _(e):
            src = lax.rem(r + R - e, R)
            done(rc(buf.at[src], buf.at[src], name, e, h, lax.rem(r + e, R)))

    def hops_start(buf, name):
        @pl.loop(1, HOPS)
        def _(d):
            rc(buf.at[h], buf.at[h], name, d, peer(d), r).start()

    def hops_wait(buf, name):
        @pl.loop(1, HOPS)
        def _(d):
            done(rc(buf.at[peer(d)], buf.at[peer(d)], name, d, peer(d), r))

    def total(buf, n, dtype=F32):
        return lax.fori_loop(1, n, lambda i, t: t + buf[i].astype(dtype), buf[0].astype(dtype))

    loc = pltpu.make_async_copy(ft.at[pl.ds(0, MAIN), :], fs.at[pl.ds(0, MAIN), :], ss.at[names["loc"]])
    loc.start()

    def pack4(src, dst):
        n = st4.shape[1]
        for b in range(4):
            st4[pl.ds(4 * b, 4), :] = src[pl.ds(0, 4), pl.ds(b * n, n)].astype(F32)
        dst[...] = st4[pl.ds(0, 16), :].astype(BF16)

    def unpack4(src, dst):
        n = st4.shape[1]
        row = lax.broadcasted_iota(jnp.int32, (32, n), 0)
        st4[pl.ds(0, 16), :] = src[...].astype(F32)
        st4[pl.ds(16, 32), :] = jnp.where(row == ONES - MAIN, 1.0, 0.0)
        for b in range(4):
            st4[pl.ds(16, 4), :] = st4[pl.ds(4 * b, 4), :]
            dst[pl.ds(MAIN, 32), pl.ds(b * n, n)] = st4[pl.ds(16, 32), :].astype(BF16)

    wrow = pl.ds(hid, 128)
    wall[0, pl.ds(hid + 96, 32), :] = jnp.zeros((32, hid), BF16)
    wall[0, pl.ds(hid, 100), :] = wb[...]

    @pl.loop(0, hid // 128)
    def _(i):
        k = lanes_at(i, 128)
        wall[0, pl.ds(0, hid), k] = wm[k, :].astype(F32).T.astype(BF16)

    def feat_copy(d):
        rows = pl.ds(0, MAIN)
        return rc(fs.at[rows, lanes_at(peer(d), sub)], fx.at[d, rows, :], "feat", d, peer(d), r)

    def ft_copy(d):
        return rc(ftail.at[peer(d)], frt.at[d], "ft", d, peer(d), r)

    pl.semaphore_wait(barrier, HOPS - 1 + R - 1)

    S = min(Z, 2)
    part = (hid + 128) // (2 * S)
    zpar = lax.rem(zi, S)
    zmate = zi + (S - 1) - 2 * (S - 1) * zpar

    def part_rows(core, par):
        return pl.ds(pl.multiple_of((core * S + par) * part, 16), part)

    def ws_copy(d):
        rows = part_rows(c, zpar)
        return rc(wall.at[0, rows, :], wall.at[d, rows, :], "ws", d, peer(d), r)

    def zf_copy(d, par):
        ref = wall.at[d, part_rows(c, par), :]
        return rc(ref, ref, "zf", d, h, 2 * zmate + c)

    def dd_copy(d, core):
        ref = wall.at[d, pl.ds(pl.multiple_of(core * S * part, 16), S * part), :]
        return rc(ref, ref, "dd", d, h, sib)

    first, second = 1 + c, 2 - c
    ws_copy(first).start()
    ws_copy(second).start()
    ws_copy(HOPS - 1).start()
    loc.wait()
    feat_copy(first).start()
    feat_copy(second).start()

    @pl.loop(0, HOPS)
    def _(j):
        lanes = lanes_at(j, sub)
        pack4(ft4.at[:, lanes], ftail.at[j])
        unpack4(ftail.at[j], fs.at[:, lanes])


    @pl.loop(1, HOPS)
    def _(d):
        ft_copy(d).start()

    fx0 = pltpu.make_async_copy(fs.at[:, lanes_at(h, sub)], fx.at[0], ss.at[names["loc"]])
    fx0.start()

    def gram(i, g):
        f = fs[:, lanes_at(i, sub)]
        return g + dot_nt(f, f)

    g = lax.fori_loop(0, HOPS, gram, jnp.zeros((128, 128), F32))
    wown = wall[0, wrow, :]
    wown32 = wown.astype(F32)
    g1, g2, g3 = split3(g)
    gw = dot(g1, wown) + dot(g2, wown) + dot(g3, wown)
    s1[r, :, pl.ds(0, hid)] = gw[ONES : ONES + 1, :]
    s1[r, :, pl.ds(hid, hid)] = jnp.sum(gw * wown32, axis=0, keepdims=True)
    rows_start(s1, "s1")
    gown[...] = g

    @pl.loop(0, HOPS * (sub // 128))
    def _(i):
        d = lax.div(i, sub // 128)
        b = lax.rem(i, sub // 128)
        late = peer(d) - 2
        m = jnp.where(late >= 0, msk[jnp.maximum(late, 0), h * (sub // 128) + b], 1)
        keep[d, :, lanes_at(b, 128)] = jnp.full((16, 128), 0.5 * m.astype(F32)).astype(BF16)

    wcs[...] = jnp.zeros(wcs.shape, F32)
    wcs[pl.ds(0, wc.shape[0]), :] = wc[...].astype(F32)
    cbs[...] = jnp.zeros(cbs.shape, F32)
    cbs[pl.ds(0, 1), pl.ds(0, cb.shape[1])] = cb[...]
    ncls = wc.shape[0]

    @pl.loop(0, hid // 16)
    def _(i):
        rows = lanes_at(i, 16)
        mixed[rows, :] = jnp.zeros((16, sub), F32)
        mi[0, rows, pl.ds(0, big)] = jnp.zeros((16, big), BF16)

    fx0.wait()

    rows_wait(s1, "s1")
    st = total(s1, R)
    mean = st[:, :hid] * inv_n
    var = st[:, hid:] * inv_n - mean * mean
    inv = lax.rsqrt(var + EPS)
    scale = inv * bgain[...]
    ab[0, :, pl.ds(0, hid)] = scale
    ab[0, :, pl.ds(hid, hid)] = bbias[...] - mean * scale

    def ab_copy(d):
        return rc(ab.at[0], ab.at[d], "ab", d, peer(d), r)

    @pl.loop(1, HOPS)
    def _(d):
        ab_copy(d).start()

    def prepare(d):
        a = ab[d, :, pl.ds(0, hid)]
        b = ab[d, :, pl.ds(hid, hid)]
        ws = wall[d, wrow, :].astype(F32) * (a * KAPPA)
        aw[d] = ws[:FP].astype(BF16)
        row = lax.broadcasted_iota(jnp.int32, (128, hid), 0)
        wt = jnp.where(row == ONES, b * KAPPA, ws).T
        hi, lo = split2(wt)
        wl[d, :, pl.ds(0, 128)] = hi
        wl[d, :, pl.ds(128, 128)] = lo

    g_pair = rc(gown.at[lanes_at(1 - c, 64), :], gpr, "gp", 0, h, sib)

    def gz_copy(e, which):
        return rc(gz.at[which], gz.at[which], "gz", e, h, lax.rem(zi + e, Z) * 2 + c)

    def gd_copy(core):
        return rc(gfin.at[core], gfin.at[core], "gd", 0, h, sib)

    @pl.loop(0, HOPS * NT)
    def _(it):
        d = lax.div(it, NT)
        t = lax.rem(it, NT)

        @pl.when(t == 0)
        def _():
            @pl.when(d > 0)
            def _():
                done(feat_copy(d))
                done(ft_copy(d))
                unpack4(frt.at[d], fx.at[d])
                dd_copy(d, c).wait_send()
                dd_copy(d, 1 - c).wait_recv()
                done(ab_copy(d))

            prepare(d)

        if S > 1:

            @pl.when(it == min(1, NT - 1))
            def _():
                @pl.loop(1, HOPS)
                def _(j):
                    done(ws_copy(j))

                zf_copy(1, zpar).start()

        @pl.when(it == min(2, NT - 1))
        def _():
            feat_copy(HOPS - 1).start()

        @pl.when(jnp.logical_and(t == NT - 1, d < HOPS - 1))
        def _():
            if S > 1:
                zf_copy(d + 1, zpar).wait_send()
                zf_copy(d + 1, 1 - zpar).wait_recv()

                @pl.when(d < HOPS - 2)
                def _():
                    zf_copy(d + 2, zpar).start()

            else:
                done(ws_copy(d + 1))
            dd_copy(d + 1, c).start()

        @pl.when(it == 2 * NT)
        def _():
            g_pair.start()

        @pl.when(it == 3 * NT)
        def _():
            done(g_pair)
            gz[zi] = gown[lanes_at(c, 64), :] + gpr[...]

            @functools.partial(each, 1, Z)
            def _(e):
                gz_copy(e, zi).start()

        pit = jnp.maximum(it - 1, 0)
        pd = lax.div(pit, NT)
        pt = lax.rem(pit, NT)
        adds = []
        for u in range(UN):
            adds.append(dot(wall[pd, pl.ds(0, hid), :], mi[pd, :, lanes_at(pt * UN + u, TILE)]))
        for u in range(UN):
            n = lanes_at(t * UN + u, TILE)
            f = fx[d, :, n]
            z = dot(wl[d], jnp.concatenate([f, f], axis=0))
            k = keep[d, :, n]
            k = jnp.concatenate([k] * 4, axis=0)
            for i in range(0, hid, 64):
                g1, d1 = scaled_gelu_slope(z[i : i + 64].astype(BF16))
                g2, d2 = scaled_gelu_slope(g1 * k)
                mi[d, pl.ds(i, 64), n] = g2
                gp[d, pl.ds(i, 64), n] = d1 * d2 * k
        for u in range(UN):
            n = lanes_at(pt * UN + u, TILE)
            mixed[:, n] = mixed[:, n] + adds[u]

    acc0[...] = jnp.zeros(acc0.shape, F32)
    acc1[...] = jnp.zeros(acc1.shape, F32)

    @pl.loop(0, UN)
    def _(u):
        n = lanes_at((NT - 1) * UN + u, TILE)
        mixed[:, n] = mixed[:, n] + dot(wall[HOPS - 1, pl.ds(0, hid), :], mi[HOPS - 1, :, n])

    @pl.loop(0, hid // 32)
    def _(i):
        rows = lanes_at(i, 32)
        x = mixed[rows, :]
        acc0[rows, :] = fold(x)
        acc1[rows, :] = fold(x * x)

    def natural(lo, hi):
        @pl.loop(lo * (hid // 128), hi * (hid // 128))
        def _(i):
            d = lax.div(i, hid // 128)
            k = lanes_at(lax.rem(i, hid // 128), 128)
            wmx[d, k, :] = wall[d, pl.ds(0, hid), k].astype(F32).T.astype(BF16)

    s2h[h, :, pl.ds(0, hid)] = row_of(acc0[...])
    s2h[h, :, pl.ds(hid, hid)] = row_of(acc1[...])
    hops_start(s2h, "s2h")
    natural(0, 2)
    hops_wait(s2h, "s2h")
    s2r[r] = total(s2h, HOPS)
    rows_start(s2r, "s2r")
    natural(2, HOPS)
    wc48 = wcs[pl.ds(0, 48), :].astype(BF16)
    wcNs[...] = wcs[...].T.astype(BF16)
    crow = lax.broadcasted_iota(jnp.int32, (128, 128), 0)
    cbc = jnp.where(crow < ncls, jnp.broadcast_to(cbs[pl.ds(0, 1), :], (128, 128)).T, -1e30)[:48]
    rows_wait(s2r, "s2r")
    st2 = total(s2r, R)
    mean2 = st2[:, :hid] * inv_n
    inv2 = lax.rsqrt(st2[:, hid:] * inv_n - mean2 * mean2 + EPS * 4.0 * KAPPA * KAPPA)
    scale2 = inv2 * gain2[...]
    cols[0] = col_of(scale2)
    cols[1] = col_of(bias2[...] - mean2 * scale2)
    acc0[...] = jnp.zeros(acc0.shape, F32)
    acc1[...] = jnp.zeros(acc1.shape, F32)
    accl[...] = jnp.zeros(accl.shape, F32)
    accw[...] = jnp.zeros(accw.shape, F32)

    o_own = lanes_at(h, sub)

    def lp_copy(d):
        return rc(lps, o_lp.at[:, o_own], "lp", d, peer(d), r)

    dlp[...] = jnp.zeros(dlp.shape, BF16)
    HR = 128

    @pl.loop(0, NT)
    def _(t):
        n = lanes_at(t, big)

        @pl.loop(0, hid // HR)
        def _(i):
            rows = lanes_at(i, HR)
            z2 = mixed[rows, n] * spread(cols[0, rows, :], big) + spread(cols[1, rows, :], big)
            gv, dg = gelu_slope(z2)
            hb[rows, :] = gv.astype(BF16)
            dn2[rows, n] = dg

        lg = dot(wc48, hb[...]) + spread(cbc, big)
        lg = lg - jnp.max(lg, axis=0, keepdims=True)
        ex = jnp.exp(lg)
        se = jnp.sum(ex, axis=0, keepdims=True)
        lp = lg - jnp.log(se)
        lps[:, n] = lp.astype(BF16)
        own = lanes_at(h * NT + t, big)
        hit = lax.broadcasted_iota(jnp.int32, (48, big), 0) == lab[:, own]
        accl[pl.ds(48, 48), :] += fold(jnp.where(hit, lp, 0.0))
        dl = ((ex / se - jnp.where(hit, 1.0, 0.0)) * inv_n).astype(BF16)
        accl[pl.ds(0, 48), :] += fold(dl.astype(F32))
        accw[...] += dot_nt(dl, hb[...])
        dlp[pl.ds(0, 48), :] = dl

        @pl.loop(0, hid // HR)
        def _(i):
            rows = lanes_at(i, HR)
            dn = dot(wcNs[rows, :], dlp[...]) * dn2[rows, n]
            dn2[rows, n] = dn
            acc0[rows, :] += fold(dn * mixed[rows, n])
            acc1[rows, :] += fold(dn)

    own_lp = pltpu.make_async_copy(lps, o_lp.at[:, o_own], ss.at[names["lp"]])
    own_lp.start()
    s3h[h, :, pl.ds(0, hid)] = row_of(acc0[...])
    s3h[h, :, pl.ds(hid, hid)] = row_of(acc1[...])
    zpad = jnp.zeros((80, 128), F32)
    s3h[h, :, pl.ds(2 * hid, 128)] = row_of(jnp.concatenate([accl[pl.ds(0, 48), :], zpad], axis=0))
    s3h[h, :, pl.ds(2 * hid + 128, 128)] = row_of(jnp.concatenate([accl[pl.ds(48, 48), :], zpad], axis=0))
    hops_start(s3h, "s3h")

    def cwh_copy(d):
        return rc(cwp.at[d], cwh.at[d], "cwh", d, peer(d), r)

    q = hid // HOPS

    @pl.loop(0, HOPS)
    def _(d):
        cwp[d] = accw[:, lanes_at(peer(d), q)].astype(BF16)

    hops_wait(s3h, "s3h")
    s3r[r] = total(s3h, HOPS)
    rows_start(s3r, "s3r")

    @pl.loop(1, HOPS)
    def _(d):
        cwh_copy(d).start()

    lp_copy(first).start()
    lp_copy(second).start()
    lp_copy(HOPS - 1).start()
    rows_wait(s3r, "s3r")
    st3 = total(s3r, R)
    db2 = st3[:, hid : 2 * hid]
    dg2t = inv2 * (st3[:, :hid] - mean2 * db2)
    o_small[pl.ds(0, 1), :] = dg2t
    o_small[pl.ds(1, 1), :] = db2
    o_small[pl.ds(4, 1), pl.ds(0, 256)] = st3[:, 2 * hid : 2 * hid + 256]
    o_small[pl.ds(4, 1), pl.ds(256, hid - 256)] = jnp.zeros((1, hid - 256), F32)
    t2 = scale2 * inv2 * dg2t * inv_n
    cols[1] = col_of(-t2)
    cols[2] = col_of(t2 * mean2 - scale2 * db2 * inv_n)

    @pl.loop(0, hid // 16)
    def _(i):
        rows = lanes_at(i, 16)
        v = dn2[rows, :] * spread(cols[0, rows, :], sub)
        v = v + mixed[rows, :] * spread(cols[1, rows, :], sub) + spread(cols[2, rows, :], sub)
        dmx[rows, :] = v.astype(BF16)

    @functools.partial(each, 1, Z)
    def _(e):
        gz_copy(e, zi).wait_send()
        gz_copy(e, lax.rem(zi + Z - e, Z)).wait_recv()

    gfin[c] = total(gz, Z)
    gd_copy(c).start()

    mine = lanes_at(c, half)
    theirs = lanes_at(1 - c, half)

    def pair_copy(d):
        return rc(dmp.at[d, theirs, :], pr.at[d], "pair", d, h, sib)

    qrows = half // S
    zown = pl.ds(pl.multiple_of(c * half + zpar * qrows, 16), qrows)
    zother = pl.ds(pl.multiple_of(c * half + (1 - zpar) * qrows, 16), qrows)

    def z1_copy(d):
        return rc(dmp.at[d, zother, :], z1r.at[d], "z1", d, h, 2 * zmate + c)

    def z1_start(d):
        if S > 1:
            z1_copy(d).start()

    def z1_sum(d):
        if S > 1:
            done(z1_copy(d))

            @pl.loop(0, qrows // 32)
            def _(i):
                rows = pl.ds(pl.multiple_of(c * half + zpar * qrows + i * 32, 32), 32)
                dmp[d, rows, :] = (dmp[d, rows, :].astype(F32) + z1r[d, lanes_at(i, 32), :].astype(F32)).astype(BF16)

    def hop_copy(d):
        return rc(dmp.at[d, zown, :], hr.at[d], "hop", d, peer(d), r)

    def pair_sum(d):
        done(pair_copy(d))

        @pl.loop(0, half // 32)
        def _(i):
            rows = pl.ds(pl.multiple_of(c * half + i * 32, 32), 32)
            dmp[d, rows, :] = (dmp[d, rows, :].astype(F32) + pr[d, lanes_at(i, 32), :].astype(F32)).astype(BF16)

    @pl.loop(0, HOPS)
    def _(i):
        d = HOPS - 1 - i

        dmp[d] = dot_nt(mi[d], dmx[...]).astype(BF16)
        pair_copy(d).start()

        @pl.when(i > 0)
        def _():
            pair_sum(d + 1)
            z1_start(d + 1)

        @pl.when(i > 1)
        def _():
            z1_sum(d + 2)
            hop_copy(d + 2).start()

    G2 = Z // S
    zq = lax.div(zi, S)

    def zr_copy(e, which):
        rows, lanes = chunk(0, which, qrows, G2, hid)
        return rc(hr.at[0, rows, lanes], zr.at[e], "zr", e, h, (lax.rem(zq + e, G2) * S + zpar) * 2 + c)

    def final_chunk(z):
        return chunk(c * half + lax.rem(z, S) * qrows, lax.div(z, S), qrows, G2, hid)

    def zg_copy(e, which):
        rows, lanes = final_chunk(which)
        ref = fin.at[rows, lanes]
        return rc(ref, ref, "zg", e, h, lax.rem(zi + e, Z) * 2 + c)

    def ddm_copy(core):
        ref = fin.at[lanes_at(core, half), :]
        return rc(ref, ref, "ddm", 0, h, sib)

    def d_copy(d):
        return rc(dsend.at[d], o_d.at[h], "d", d, peer(d), r)

    def dt_copy(d):
        return rc(dtail.at[d], o_dt.at[h], "dt", d, peer(d), r)

    def pp_copy(d):
        return rc(ps.at[d, :, theirs], ph.at[d], "pp", d, h, sib)

    def p_copy(d):
        return rc(phalf.at[d], prv.at[d], "p", d, peer(d), r)

    def p_half(d):
        done(pp_copy(d))
        phalf[d] = (ps[d, :, mine].astype(F32) + ph[d].astype(F32)).astype(BF16)

    def q_copy(d):
        return rc(qs.at[d], qv.at[d], "q", d, peer(d), r)

    @pl.loop(0, HOPS * NT)
    def _(it):
        dd = lax.div(it, NT)
        t = lax.rem(it, NT)
        d = HOPS - 1 - dd

        @pl.when(t == 0)
        def _():
            pT[...] = jnp.zeros(pT.shape, F32)

        @pl.when(jnp.logical_and(t == NT // 2, dd > 0))
        def _():
            p_half(d + 1)
            p_copy(d + 1).start()
            dt_copy(d + 1).start()
            d_copy(d + 1).start()

        @pl.when(it == NT // 2)
        def _():
            pair_sum(0)
            z1_start(0)
            z1_sum(1)
            hop_copy(1).start()

        @pl.when(it == NT + NT // 2)
        def _():
            @pl.loop(1, HOPS)
            def _(j):
                done(cwh_copy(j))

            cw = cwp[0].astype(F32)
            for j in range(1, HOPS):
                cw = cw + cwh[j].astype(F32)
            cwr[r] = cw.astype(BF16)
            rows_start(cwr, "cwr")
            z1_sum(0)

        @pl.when(it == 2 * NT + NT // 2)
        def _():
            @pl.loop(1, HOPS)
            def _(j):
                done(hop_copy(j))

            @pl.loop(0, qrows // 32)
            def _(i):
                rows = lanes_at(i, 32)
                own = pl.ds(pl.multiple_of(c * half + zpar * qrows + i * 32, 32), 32)
                hsum = dmp[0, own, :].astype(F32)
                for j in range(1, HOPS):
                    hsum = hsum + hr[j, rows, :].astype(F32)
                hr[0, rows, :] = hsum.astype(BF16)

            @functools.partial(each, 1, G2)
            def _(e):
                zr_copy(e, lax.rem(zq + e, G2)).start()

            rows_wait(cwr, "cwr")
            cwg[h] = total(cwr, R, F32).astype(BF16)
            hops_start(cwg, "cwg")

        @pl.when(it == 3 * NT + NT // 2)
        def _():
            @functools.partial(each, 1, G2)
            def _(e):
                done(zr_copy(e, lax.rem(zq + e, G2)))

            rows, lanes = chunk(0, zq, qrows, G2, hid)
            zt = lax.fori_loop(1, G2, lambda e, v: v + zr[e].astype(F32), hr[0, rows, lanes].astype(F32))
            frows, flanes = final_chunk(zi)
            fin[frows, flanes] = zt.astype(BF16)

            @functools.partial(each, 1, Z)
            def _(e):
                zg_copy(e, zi).start()

            hops_wait(cwg, "cwg")
            for j in range(HOPS):
                o_cw[:, pl.ds(j * q, q)] = cwg[j].astype(F32)

        n = lanes_at(t, big)
        dn = dot(wmx[d], dmx[:, n]).astype(BF16) * gp[d, :, n]
        pT[...] += dot_nt(dn, fx[d, :, n])
        grad = dot(aw[d], dn)
        dsend[d, :, n] = grad[:MAIN].astype(BF16)
        d4[:, n] = grad[MAIN : MAIN + 8]

        @pl.when(t == NT - 1)
        def _():
            pw = pT[...].T * KAPPA
            qs[d, :, pl.ds(0, hid)] = jnp.sum(pw * wall[d, wrow, :].astype(F32), axis=0, keepdims=True)
            qs[d, :, pl.ds(hid, hid)] = pw[ONES : ONES + 1, :]
            ps[d] = pw[:FP].astype(BF16)
            pp_copy(d).start()
            pack4(d4, dtail.at[d])

            @pl.when(dd < HOPS - 1)
            def _():
                q_copy(d).start()

    @pl.loop(1, HOPS)
    def _(d):
        done(q_copy(d))

    qr[r] = qs[0] + (qv[1] + qv[2] + qv[3])
    rows_start(qr, "qr")
    own_d = pltpu.make_async_copy(dsend.at[0], o_d.at[h], ss.at[names["d"]])
    own_d.start()
    own_dt = pltpu.make_async_copy(dtail.at[0], o_dt.at[h], ss.at[names["dt"]])
    own_dt.start()

    p_half(0)

    @pl.loop(1, HOPS)
    def _(d):
        done(p_copy(d))

    psum = phalf[0].astype(F32) + (prv[1].astype(F32) + prv[2].astype(F32) + prv[3].astype(F32))
    pz[zi] = psum.astype(BF16)

    def pz_copy(e, which):
        return rc(pz.at[which], pz.at[which], "pz", e, h, lax.rem(zi + e, Z) * 2 + c)

    @functools.partial(each, 1, Z)
    def _(e):
        pz_copy(e, zi).start()

    @functools.partial(each, 1, Z)
    def _(e):
        zg_copy(e, zi).wait_send()
        zg_copy(e, lax.rem(zi + Z - e, Z)).wait_recv()

    ddm_copy(c).start()

    rows_wait(qr, "qr")
    qt = total(qr, R)
    db = qt[:, hid:]
    dgn = inv * (qt[:, :hid] - mean * db)
    o_small[pl.ds(2, 1), :] = dgn
    o_small[pl.ds(3, 1), :] = db
    c1 = scale * db * inv_n
    c2 = inv * scale * dgn * inv_n
    shift = c1 - mean * c2
    row = lax.broadcasted_iota(jnp.int32, (128, hid), 0)
    q1, q2 = split2(jnp.where(row == ONES, shift, wown32 * c2))
    o_m[...] = (dot_nt(wown, q1) + dot_nt(wown, q2))[:FP]
    gd_copy(c).wait_send()
    gd_copy(1 - c).wait_recv()
    g1, g2, g3 = split3(jnp.concatenate([gfin[0], gfin[1]], axis=0))
    gq = dot(g1, q1) + dot(g2, q1) + dot(g3, q1) + dot(g1, q2) + dot(g2, q2)

    @functools.partial(each, 1, Z)
    def _(e):
        pz_copy(e, zi).wait_send()
        pz_copy(e, lax.rem(zi + Z - e, Z)).wait_recv()

    pfin[c] = total(pz, Z).astype(BF16)

    def pd_copy(core):
        return rc(pfin.at[core], pfin.at[core], "pd", 0, h, sib)

    pd_copy(c).start()
    ddm_copy(c).wait_send()
    ddm_copy(1 - c).wait_recv()
    o_mix[...] = fin[...]

    pd_copy(c).wait_send()
    pd_copy(1 - c).wait_recv()
    ptot = jnp.concatenate([pfin[0], pfin[1]], axis=1).astype(F32)
    o_gw[...] = ptot * scale - gq[:FP]
    own_d.wait()
    own_dt.wait()
    own_lp.wait()

    @pl.loop(1, HOPS)
    def _(d):
        done(d_copy(d))
        done(dt_copy(d))
        done(lp_copy(d))


def last_kernel(
    nodes,
    ft, d, dt, lp, m, mix, gw, small, cw,
    o_lp, o_gf, o_mix, o_gw, o_gg, o_gb, o_hg, o_hb, o_cw, o_cb, o_loss, low,
):
    feat, n = ft.shape
    ncls = o_lp.shape[0]
    o_lp[...] = lp[...].astype(F32)[:ncls]
    mm = m[...]
    f = ft[...]
    fix = dot(mm[:, :feat].astype(BF16), f) + mm[:, ONES : ONES + 1]
    tail = dt[0].astype(F32)
    for b in range(4):
        low[pl.ds(0, 4), pl.ds(b * (n // 4), n // 4)] = tail[4 * b : 4 * b + 4]
    gf = jnp.concatenate([d[0].astype(F32), low[...]], axis=0)[:feat] - fix[:feat]
    if STRIDED:
        flat = o_gf.reshape(feat * (n // 128), 128)
        for i in range(n // 128):
            flat[pl.ds(i, feat, stride=n // 128), :] = gf[:, i * 128 : (i + 1) * 128]
    else:
        for i in range(n // 128):
            o_gf[:, i, :] = gf[:, i * 128 : (i + 1) * 128]

    @pl.when(pl.program_id(0) == 0)
    def _():
        hid = mix.shape[1]
        o_mix[...] = mix[...].astype(F32)
        for i in range(hid // 128):
            o_gw[:, i, :] = gw[pl.ds(0, feat), pl.ds(i * 128, 128)]
        o_hg[...] = small[pl.ds(0, 1), :]
        o_hb[...] = small[pl.ds(1, 1), :]
        o_gg[...] = small[pl.ds(2, 1), :]
        o_gb[...] = small[pl.ds(3, 1), :]
        o_cw[...] = cw[pl.ds(0, ncls), :]
        o_cb[...] = small[pl.ds(4, 1), pl.ds(0, ncls)]
        o_loss[...] = jnp.sum(small[pl.ds(4, 1), pl.ds(128, 128)], axis=1, keepdims=True) * (-1.0 / nodes)


def shards(
    R, features, branch_weight, branch_gain, branch_bias, mix_weight, mixing_norm_gain, mixing_norm_bias,
    class_weight, class_bias, labels, hop_mask,
):
    local, feat = features.shape[1:]
    hid = mix_weight.shape[0]
    ncls = class_weight.shape[1]
    nodes = local * R
    sub = local // HOPS
    Z = R // 2
    half = hid // 2
    S = min(Z, 2)
    G2, qrows = Z // S, half // S
    zrows, zcols = chunk(0, 0, qrows, G2, hid)
    assert feat == ONES and ncls == 47 and local // hop_mask.shape[0] == 128
    ft = features[0].T
    sd = jax.ShapeDtypeStruct
    vm = pl.BlockSpec(memory_space=pltpu.VMEM)
    hbm = pl.BlockSpec(memory_space=pl.ANY)
    _, nsem = sem_plan(R)
    V = pltpu.VMEM
    outs = pl.pallas_call(
        functools.partial(main_kernel, R, nodes),
        grid=(1,),
        out_shape=(
            sd((48, local), BF16),
            sd((HOPS, MAIN, sub), BF16),
            sd((HOPS, 16, sub // 4), BF16),
            sd((FP, 128), F32),
            sd((hid, hid), BF16),
            sd((FP, hid), F32),
            sd((8, hid), F32),
            sd((48, hid), F32),
        ),
        in_specs=[hbm, pl.BlockSpec((16, local), lambda i: (MAIN // 16, 0))]
        + [vm] * 9
        + [pl.BlockSpec(memory_space=pltpu.SMEM)],
        out_specs=(hbm, hbm, hbm, vm, vm, vm, vm, vm),
        scratch_shapes=[
            V((128, local), BF16),
            V((HOPS, 128, sub), BF16),
            V((HOPS, 16, sub // 4), BF16),
            V((HOPS, 16, sub // 4), BF16),
            V((48, sub // 4), F32),
            V((HOPS, hid + 128, hid), BF16),
            V((HOPS, hid, 256), BF16),
            V((HOPS, FP, hid), BF16),
            V((HOPS, hid, hid), BF16),
            V((HOPS, 16, sub), BF16),
            V((HOPS, hid, sub), BF16),
            V((HOPS, hid, sub), BF16),
            V((hid, sub), F32),
            V((hid, sub), F32),
            V((hid, sub), BF16),
            V((128, 128), F32),
            V((64, 128), F32),
            V((Z, 64, 128), F32),
            V((2, 64, 128), F32),
            V((R, 1, 2 * hid), F32),
            V((HOPS, 1, 2 * hid), F32),
            V((HOPS, 1, 2 * hid), F32),
            V((R, 1, 2 * hid), F32),
            V((HOPS, 1, 2 * hid + 256), F32),
            V((R, 1, 2 * hid + 256), F32),
            V((HOPS, 48, hid // HOPS), BF16),
            V((HOPS, 48, hid // HOPS), BF16),
            V((R, 48, hid // HOPS), BF16),
            V((HOPS, 48, hid // HOPS), BF16),
            V((48, sub), BF16),
            V((128, hid), F32),
            V((hid, 128), BF16),
            V((8, 128), F32),
            V((hid, min(2 * TILE, sub)), BF16),
            V((128, min(2 * TILE, sub)), BF16),
            V((hid, 128), F32),
            V((hid, 128), F32),
            V((96, 128), F32),
            V((48, hid), F32),
            V((3, hid, 128), F32),
            V((HOPS, hid, hid), BF16),
            V((HOPS, half, hid), BF16),
            V((HOPS, qrows, hid), BF16),
            V((HOPS, qrows, hid), BF16),
            V((max(G2, 2), zrows.size, zcols.size), BF16),
            V((hid, hid), BF16),
            V((HOPS, MAIN, sub), BF16),
            V((8, sub), F32),
            V((HOPS, 16, sub // 4), BF16),
            V((hid, 128), F32),
            V((HOPS, FP, hid), BF16),
            V((HOPS, FP, half), BF16),
            V((HOPS, FP, half), BF16),
            V((HOPS, FP, half), BF16),
            V((HOPS, 1, 2 * hid), F32),
            V((HOPS, 1, 2 * hid), F32),
            V((R, 1, 2 * hid), F32),
            V((Z, FP, half), BF16),
            V((2, FP, half), BF16),
            pltpu.SemaphoreType.DMA((nsem,)),
            pltpu.SemaphoreType.DMA((nsem,)),
        ],
        compiler_params=pltpu.CompilerParams(
            collective_id=0, has_side_effects=True, vmem_limit_bytes=63 * 1024 * 1024
        ),
        cost_estimate=pl.CostEstimate(flops=2 * 8 * 10**9, bytes_accessed=10**7, transcendentals=10**7),
        name="main",
    )(
        ft, ft, branch_weight[0], branch_gain, branch_bias, mix_weight, mixing_norm_gain[None], mixing_norm_bias[None],
        class_weight.T, class_bias[None], labels[None], hop_mask.T,
    )
    lp, dd, dt, m, mix, gw, small, cw = outs
    nb = sub
    whole = lambda shape: pl.BlockSpec(shape, lambda i: (0,) * len(shape))
    lp, gf, mix, gw, gg, gb, hg, hb, cw, cb, loss = pl.pallas_call(
        functools.partial(last_kernel, nodes),
        grid=(local // nb,),
        out_shape=(
            sd((ncls, local), F32),
            sd((feat, local // 128, 128), F32),
            sd((hid, hid), F32),
            sd((feat, hid // 128, 128), F32),
            sd((1, hid), F32),
            sd((1, hid), F32),
            sd((1, hid), F32),
            sd((1, hid), F32),
            sd((ncls, hid), F32),
            sd((1, ncls), F32),
            sd((1, 1), F32),
        ),
        in_specs=[
            pl.BlockSpec((feat, nb), lambda i: (0, i)),
            pl.BlockSpec((1, MAIN, nb), lambda i: (i, 0, 0)),
            pl.BlockSpec((1, 16, nb // 4), lambda i: (i, 0, 0)),
            pl.BlockSpec((48, nb), lambda i: (0, i)),
            whole((FP, 128)),
            whole((hid, hid)),
            whole((FP, hid)),
            whole((8, hid)),
            whole((48, hid)),
        ],
        out_specs=(
            pl.BlockSpec((ncls, nb), lambda i: (0, i)),
            pl.BlockSpec((feat, nb // 128, 128), lambda i: (0, i, 0)),
            whole((hid, hid)),
            whole((feat, hid // 128, 128)),
            whole((1, hid)),
            whole((1, hid)),
            whole((1, hid)),
            whole((1, hid)),
            whole((ncls, hid)),
            whole((1, ncls)),
            whole((1, 1)),
        ),
        scratch_shapes=[V((8, nb), F32)],
        compiler_params=pltpu.CompilerParams(vmem_limit_bytes=60 * 1024 * 1024),
        name="last",
    )(ft, dd, dt, lp, m, mix, gw, small, cw)
    return (
        lp.T,
        loss[0, 0],
        with_layout_constraint(gf.reshape(feat, 1, local), Layout((0, 1, 2))).transpose(1, 2, 0),
        gw.reshape(1, feat, hid),
        gg,
        gb,
        mix,
        hg[0],
        hb[0],
        cw.T,
        cb[0],
    )


def solution(mesh):
    placed = (
        P("hop", "rows", None), P("hop", None, None), P("hop", None), P("hop", None), P("hop", None),
        P(), P(), P(), P(), P("rows"), P("rows", None),
    )
    assert mesh.shape["hop"] == HOPS
    return jax.shard_map(
        functools.partial(shards, mesh.shape["rows"]),
        mesh=mesh,
        in_specs=placed,
        out_specs=(
            P("rows", None), P(), P("hop", "rows", None), P("hop", None, None), P("hop", None), P("hop", None),
            P("hop", None), P(), P(), P(), P(),
        ),
        check_vma=False,
    )
```

```python
import functools
import math

import jax
import jax.numpy as jnp
from jax import lax
from jax.experimental import pallas as pl
from jax.experimental.layout import Layout, with_layout_constraint
from jax.experimental.pallas import tpu as pltpu
from jax.sharding import PartitionSpec as P

MESH = pl.DeviceIdType.MESH
EPS = 1e-05
HOPS = 4
ONES = 100
FP = 112
MAIN = 96
TILE = 256
STRIDED = True
C0 = math.sqrt(2.0 / math.pi)
C1 = C0 * 0.044715
KAPPA = C1 ** (1.0 / 3.0)
ALPHA = C0 / KAPPA
F32 = jnp.float32
BF16 = jnp.bfloat16


def dot(a, b):
    return lax.dot_general(a, b, (((1,), (0,)), ((), ())), preferred_element_type=F32)


def dot_nt(a, b):
    return lax.dot_general(a, b, (((1,), (1,)), ((), ())), preferred_element_type=F32)


def split2(x):
    hi = x.astype(BF16)
    return hi, (x - hi.astype(F32)).astype(BF16)


def split3(x):
    hi = x.astype(BF16)
    rest = x - hi.astype(F32)
    mid = rest.astype(BF16)
    return hi, mid, (rest - mid.astype(F32)).astype(BF16)


def gelu_slope(z):
    u = z * z
    t = jnp.tanh(z * (C0 + C1 * u))
    s = 0.5 * t + 0.5
    g = z * s
    return g, s + (g - g * s) * (2.0 * C0 + 6.0 * C1 * u)


def scaled_gelu_slope(y):
    u = y * y
    t = jnp.tanh(y * (u + ALPHA))
    up = t + 1.0
    g = y * up
    return g, up + (g * (1.0 - t)) * (3.0 * u + ALPHA)


def fold(x):
    total = x[:, :128]
    for i in range(1, x.shape[1] // 128):
        total = total + x[:, i * 128 : (i + 1) * 128]
    return total


def spread(c, n):
    return jnp.concatenate([c] * (n // 128), axis=1)


def row_of(acc):
    return jnp.sum(acc.T, axis=0, keepdims=True)


def col_of(row):
    return jnp.broadcast_to(row, (128, row.shape[1])).T


def each(lo, hi, body):
    if hi - lo == 1:
        body(lo)
    elif hi > lo:
        pl.loop(lo, hi)(body)


class Alloc:
    def __init__(self):
        self.n = 0

    def __call__(self, count):
        base = self.n
        self.n += count
        return base


def sem_plan(R):
    Z = R // 2
    a = Alloc()
    names = {}
    for name, count in (
        ("feat", 5), ("ft", 4), ("loc", 1), ("ws", 4), ("zf", 4), ("dd", 4), ("s1", R), ("ab", 4), ("gp", 1), ("gz", Z), ("gd", 1),
        ("s2h", 4), ("s2r", R), ("s3h", 4), ("s3r", R), ("lp", 4), ("cwh", 4), ("cwr", R), ("cwg", 4),
        ("pair", 4), ("z1", 4), ("hop", 4), ("zr", Z), ("zg", Z), ("ddm", 1), ("d", 4), ("dt", 4), ("p", 4), ("q", 4),
        ("qr", R), ("pp", 4), ("pz", Z), ("pd", 1),
    ):
        names[name] = a(count)
    return names, a.n


def chunk(base, i, rows, pieces, cols):
    if rows // pieces >= 16:
        take = rows // pieces
        return pl.ds(pl.multiple_of(base + i * take, 16), take), pl.ds(0, cols)
    m = 16 * pieces // rows
    wide = cols // m
    return (
        pl.ds(pl.multiple_of(base + (i // m) * 16, 16), 16),
        pl.ds(pl.multiple_of((i % m) * wide, 128), wide),
    )


def main_kernel(
    R,
    nodes,
    ft, ft4, wb, bgain, bbias, wm, gain2, bias2, wc, cb, lab, msk,
    o_lp, o_d, o_dt, o_m, o_mix, o_gw, o_small, o_cw,
    fs, fx, ftail, frt, st4, wall, wl, aw, wmx, keep, mi, gp, mixed, dn2, dmx,
    gown, gpr, gz, gfin, s1, ab, s2h, s2r, s3h, s3r, cwp, cwh, cwr, cwg, lps,
    wcs, wcNs, cbs, hb, dlp, acc0, acc1, accl, accw, cols,
    dmp, pr, z1r, hr, zr, fin, dsend, d4, dtail, pT, ps, ph, phalf, prv, qs, qv, qr, pz, pfin,
    ss, rs,
):
    names, _ = sem_plan(R)
    Z = R // 2
    h = lax.axis_index("hop")
    r = lax.axis_index("rows")
    c = lax.rem(r, 2)
    zi = lax.div(r, 2)
    sib = r + 1 - 2 * c
    local = ft.shape[1]
    sub = local // HOPS
    hid = wm.shape[0]
    half = hid // 2
    big = min(2 * TILE, sub)
    UN = big // TILE
    NT = sub // big
    inv_n = 1.0 / nodes

    def peer(d):
        x = lax.rem(h + d, 2)
        y = lax.rem(lax.div(h, 2) + lax.div(d, 2), 2)
        return 2 * y + x

    def rc(src, dst, name, i, hh, rr):
        return pltpu.make_async_remote_copy(
            src_ref=src, dst_ref=dst, send_sem=ss.at[names[name] + i], recv_sem=rs.at[names[name] + i],
            device_id=(hh, rr), device_id_type=MESH,
        )

    def done(cp):
        cp.wait_send()
        cp.wait_recv()

    def lanes_at(i, n):
        return pl.ds(pl.multiple_of(i * n, n), n)

    barrier = pltpu.get_barrier_semaphore()

    def greet(hh, rr):
        pl.semaphore_signal(barrier, inc=1, device_id=(hh, rr), device_id_type=MESH)

    @pl.loop(1, HOPS)
    def _(d):
        greet(peer(d), r)

    @functools.partial(each, 1, R)
    def _(e):
        greet(h, lax.rem(r + e, R))

    def rows_start(buf, name):
        @functools.partial(each, 1, R)
        def _(e):
            rc(buf.at[r], buf.at[r], name, e, h, lax.rem(r + e, R)).start()

    def rows_wait(buf, name):
        @functools.partial(each, 1, R)
        def _(e):
            src = lax.rem(r + R - e, R)
            done(rc(buf.at[src], buf.at[src], name, e, h, lax.rem(r + e, R)))

    def hops_start(buf, name):
        @pl.loop(1, HOPS)
        def _(d):
            rc(buf.at[h], buf.at[h], name, d, peer(d), r).start()

    def hops_wait(buf, name):
        @pl.loop(1, HOPS)
        def _(d):
            done(rc(buf.at[peer(d)], buf.at[peer(d)], name, d, peer(d), r))

    def total(buf, n, dtype=F32):
        return lax.fori_loop(1, n, lambda i, t: t + buf[i].astype(dtype), buf[0].astype(dtype))

    loc = pltpu.make_async_copy(ft.at[pl.ds(0, MAIN), :], fs.at[pl.ds(0, MAIN), :], ss.at[names["loc"]])
    loc.start()

    def pack4(src, dst):
        n = st4.shape[1]
        for b in range(4):
            st4[pl.ds(4 * b, 4), :] = src[pl.ds(0, 4), pl.ds(b * n, n)].astype(F32)
        dst[...] = st4[pl.ds(0, 16), :].astype(BF16)

    def unpack4(src, dst):
        n = st4.shape[1]
        row = lax.broadcasted_iota(jnp.int32, (32, n), 0)
        st4[pl.ds(0, 16), :] = src[...].astype(F32)
        st4[pl.ds(16, 32), :] = jnp.where(row == ONES - MAIN, 1.0, 0.0)
        for b in range(4):
            st4[pl.ds(16, 4), :] = st4[pl.ds(4 * b, 4), :]
            dst[pl.ds(MAIN, 32), pl.ds(b * n, n)] = st4[pl.ds(16, 32), :].astype(BF16)

    wrow = pl.ds(hid, 128)
    wall[0, pl.ds(hid + 96, 32), :] = jnp.zeros((32, hid), BF16)
    wall[0, pl.ds(hid, 100), :] = wb[...]

    @pl.loop(0, hid // 128)
    def _(i):
        k = lanes_at(i, 128)
        wall[0, pl.ds(0, hid), k] = wm[k, :].astype(F32).T.astype(BF16)

    def feat_copy(d):
        rows = pl.ds(0, MAIN)
        return rc(fs.at[rows, lanes_at(peer(d), sub)], fx.at[d, rows, :], "feat", d, peer(d), r)

    def feat_half(p):
        rows = pl.ds(0, MAIN)
        d = HOPS - 1
        n = sub // 2
        return rc(fs.at[rows, lanes_at(2 * peer(d) + p, n)], fx.at[d, rows, pl.ds(p * n, n)], "feat", d + p, peer(d), r)

    def ft_copy(d):
        return rc(ftail.at[peer(d)], frt.at[d], "ft", d, peer(d), r)

    pl.semaphore_wait(barrier, HOPS - 1 + R - 1)

    S = min(Z, 2)
    part = (hid + 128) // (2 * S)
    zpar = lax.rem(zi, S)
    zmate = zi + (S - 1) - 2 * (S - 1) * zpar

    def part_rows(core, par):
        return pl.ds(pl.multiple_of((core * S + par) * part, 16), part)

    def ws_copy(d):
        rows = part_rows(c, zpar)
        return rc(wall.at[0, rows, :], wall.at[d, rows, :], "ws", d, peer(d), r)

    def zf_copy(d, par):
        ref = wall.at[d, part_rows(c, par), :]
        return rc(ref, ref, "zf", d, h, 2 * zmate + c)

    def dd_copy(d, core):
        ref = wall.at[d, pl.ds(pl.multiple_of(core * S * part, 16), S * part), :]
        return rc(ref, ref, "dd", d, h, sib)

    first, second = 1 + c, 2 - c
    ws_copy(first).start()
    ws_copy(second).start()
    ws_copy(HOPS - 1).start()
    loc.wait()
    feat_copy(first).start()
    feat_copy(second).start()

    @pl.loop(0, HOPS)
    def _(j):
        lanes = lanes_at(j, sub)
        pack4(ft4.at[:, lanes], ftail.at[j])
        unpack4(ftail.at[j], fs.at[:, lanes])


    @pl.loop(1, HOPS)
    def _(d):
        ft_copy(d).start()

    fx0 = pltpu.make_async_copy(fs.at[:, lanes_at(h, sub)], fx.at[0], ss.at[names["loc"]])
    fx0.start()

    def gram(i, g):
        f = fs[:, lanes_at(i, sub)]
        return g + dot_nt(f, f)

    g = lax.fori_loop(0, HOPS, gram, jnp.zeros((128, 128), F32))
    wown = wall[0, wrow, :]
    wown32 = wown.astype(F32)
    g1, g2, g3 = split3(g)
    gw = dot(g1, wown) + dot(g2, wown) + dot(g3, wown)
    s1[r, :, pl.ds(0, hid)] = gw[ONES : ONES + 1, :]
    s1[r, :, pl.ds(hid, hid)] = jnp.sum(gw * wown32, axis=0, keepdims=True)
    rows_start(s1, "s1")
    gown[...] = g

    @pl.loop(0, HOPS * (sub // 128))
    def _(i):
        d = lax.div(i, sub // 128)
        b = lax.rem(i, sub // 128)
        late = peer(d) - 2
        m = jnp.where(late >= 0, msk[jnp.maximum(late, 0), h * (sub // 128) + b], 1)
        keep[d, :, lanes_at(b, 128)] = jnp.full((16, 128), 0.5 * m.astype(F32)).astype(BF16)

    wcs[...] = jnp.zeros(wcs.shape, F32)
    wcs[pl.ds(0, wc.shape[0]), :] = wc[...].astype(F32)
    cbs[...] = jnp.zeros(cbs.shape, F32)
    cbs[pl.ds(0, 1), pl.ds(0, cb.shape[1])] = cb[...]
    ncls = wc.shape[0]

    @pl.loop(0, hid // 16)
    def _(i):
        rows = lanes_at(i, 16)
        mixed[rows, :] = jnp.zeros((16, sub), F32)
        mi[0, rows, pl.ds(0, big)] = jnp.zeros((16, big), BF16)

    fx0.wait()

    rows_wait(s1, "s1")
    st = total(s1, R)
    mean = st[:, :hid] * inv_n
    var = st[:, hid:] * inv_n - mean * mean
    inv = lax.rsqrt(var + EPS)
    scale = inv * bgain[...]
    ab[0, :, pl.ds(0, hid)] = scale
    ab[0, :, pl.ds(hid, hid)] = bbias[...] - mean * scale

    def ab_copy(d):
        return rc(ab.at[0], ab.at[d], "ab", d, peer(d), r)

    @pl.loop(1, HOPS)
    def _(d):
        ab_copy(d).start()

    def prepare(d):
        a = ab[d, :, pl.ds(0, hid)]
        b = ab[d, :, pl.ds(hid, hid)]
        ws = wall[d, wrow, :].astype(F32) * (a * KAPPA)
        aw[d] = ws[:FP].astype(BF16)
        row = lax.broadcasted_iota(jnp.int32, (128, hid), 0)
        wt = jnp.where(row == ONES, b * KAPPA, ws).T
        hi, lo = split2(wt)
        wl[d, :, pl.ds(0, 128)] = hi
        wl[d, :, pl.ds(128, 128)] = lo

    g_pair = rc(gown.at[lanes_at(1 - c, 64), :], gpr, "gp", 0, h, sib)

    def gz_copy(e, which):
        return rc(gz.at[which], gz.at[which], "gz", e, h, lax.rem(zi + e, Z) * 2 + c)

    def gd_copy(core):
        return rc(gfin.at[core], gfin.at[core], "gd", 0, h, sib)

    @pl.loop(0, HOPS * NT)
    def _(it):
        d = lax.div(it, NT)
        t = lax.rem(it, NT)

        @pl.when(t == 0)
        def _():
            @pl.when(d > 0)
            def _():
                @pl.when(d < HOPS - 1)
                def _():
                    done(feat_copy(d))

                @pl.when(d == HOPS - 1)
                def _():
                    done(feat_half(0))

                done(ft_copy(d))
                unpack4(frt.at[d], fx.at[d])
                dd_copy(d, c).wait_send()
                dd_copy(d, 1 - c).wait_recv()
                done(ab_copy(d))

            prepare(d)

        if S > 1:

            @pl.when(it == min(1, NT - 1))
            def _():
                @pl.loop(1, HOPS)
                def _(j):
                    done(ws_copy(j))

                zf_copy(1, zpar).start()

        @pl.when(it == min(2, NT - 1))
        def _():
            feat_half(0).start()
            feat_half(1).start()

        @pl.when(jnp.logical_and(t == NT - 1, d < HOPS - 1))
        def _():
            if S > 1:
                zf_copy(d + 1, zpar).wait_send()
                zf_copy(d + 1, 1 - zpar).wait_recv()

                @pl.when(d < HOPS - 2)
                def _():
                    zf_copy(d + 2, zpar).start()

            else:
                done(ws_copy(d + 1))
            dd_copy(d + 1, c).start()

        @pl.when(it == 2 * NT)
        def _():
            g_pair.start()

        @pl.when(it == 3 * NT)
        def _():
            done(g_pair)
            gz[zi] = gown[lanes_at(c, 64), :] + gpr[...]

            @functools.partial(each, 1, Z)
            def _(e):
                gz_copy(e, zi).start()

        @pl.when(it == 3 * NT + NT // 2)
        def _():
            done(feat_half(1))

        pit = jnp.maximum(it - 1, 0)
        pd = lax.div(pit, NT)
        pt = lax.rem(pit, NT)
        adds = []
        for u in range(UN):
            adds.append(dot(wall[pd, pl.ds(0, hid), :], mi[pd, :, lanes_at(pt * UN + u, TILE)]))
        for u in range(UN):
            n = lanes_at(t * UN + u, TILE)
            f = fx[d, :, n]
            z = dot(wl[d], jnp.concatenate([f, f], axis=0))
            k = keep[d, :, n]
            k = jnp.concatenate([k] * 4, axis=0)
            for i in range(0, hid, 64):
                g1, d1 = scaled_gelu_slope(z[i : i + 64].astype(BF16))
                g2, d2 = scaled_gelu_slope(g1 * k)
                mi[d, pl.ds(i, 64), n] = g2
                gp[d, pl.ds(i, 64), n] = d1 * d2 * k
        for u in range(UN):
            n = lanes_at(pt * UN + u, TILE)
            mixed[:, n] = mixed[:, n] + adds[u]

    acc0[...] = jnp.zeros(acc0.shape, F32)
    acc1[...] = jnp.zeros(acc1.shape, F32)

    @pl.loop(0, UN)
    def _(u):
        n = lanes_at((NT - 1) * UN + u, TILE)
        mixed[:, n] = mixed[:, n] + dot(wall[HOPS - 1, pl.ds(0, hid), :], mi[HOPS - 1, :, n])

    @pl.loop(0, hid // 32)
    def _(i):
        rows = lanes_at(i, 32)
        x = mixed[rows, :]
        acc0[rows, :] = fold(x)
        acc1[rows, :] = fold(x * x)

    def natural(lo, hi):
        @pl.loop(lo * (hid // 128), hi * (hid // 128))
        def _(i):
            d = lax.div(i, hid // 128)
            k = lanes_at(lax.rem(i, hid // 128), 128)
            wmx[d, k, :] = wall[d, pl.ds(0, hid), k].astype(F32).T.astype(BF16)

    s2h[h, :, pl.ds(0, hid)] = row_of(acc0[...])
    s2h[h, :, pl.ds(hid, hid)] = row_of(acc1[...])
    hops_start(s2h, "s2h")
    natural(0, 2)
    hops_wait(s2h, "s2h")
    s2r[r] = total(s2h, HOPS)
    rows_start(s2r, "s2r")
    natural(2, HOPS)
    wc48 = wcs[pl.ds(0, 48), :].astype(BF16)
    wcNs[...] = wcs[...].T.astype(BF16)
    crow = lax.broadcasted_iota(jnp.int32, (128, 128), 0)
    cbc = jnp.where(crow < ncls, jnp.broadcast_to(cbs[pl.ds(0, 1), :], (128, 128)).T, -1e30)[:48]
    rows_wait(s2r, "s2r")
    st2 = total(s2r, R)
    mean2 = st2[:, :hid] * inv_n
    inv2 = lax.rsqrt(st2[:, hid:] * inv_n - mean2 * mean2 + EPS * 4.0 * KAPPA * KAPPA)
    scale2 = inv2 * gain2[...]
    cols[0] = col_of(scale2)
    cols[1] = col_of(bias2[...] - mean2 * scale2)
    acc0[...] = jnp.zeros(acc0.shape, F32)
    acc1[...] = jnp.zeros(acc1.shape, F32)
    accl[...] = jnp.zeros(accl.shape, F32)
    accw[...] = jnp.zeros(accw.shape, F32)

    o_own = lanes_at(h, sub)

    def lp_copy(d):
        return rc(lps, o_lp.at[:, o_own], "lp", d, peer(d), r)

    dlp[...] = jnp.zeros(dlp.shape, BF16)
    HR = 128

    @pl.loop(0, NT)
    def _(t):
        n = lanes_at(t, big)

        @pl.loop(0, hid // HR)
        def _(i):
            rows = lanes_at(i, HR)
            z2 = mixed[rows, n] * spread(cols[0, rows, :], big) + spread(cols[1, rows, :], big)
            gv, dg = gelu_slope(z2)
            hb[rows, :] = gv.astype(BF16)
            dn2[rows, n] = dg

        lg = dot(wc48, hb[...]) + spread(cbc, big)
        lg = lg - jnp.max(lg, axis=0, keepdims=True)
        ex = jnp.exp(lg)
        se = jnp.sum(ex, axis=0, keepdims=True)
        lp = lg - jnp.log(se)
        lps[:, n] = lp.astype(BF16)
        own = lanes_at(h * NT + t, big)
        hit = lax.broadcasted_iota(jnp.int32, (48, big), 0) == lab[:, own]
        accl[pl.ds(48, 48), :] += fold(jnp.where(hit, lp, 0.0))
        dl = ((ex / se - jnp.where(hit, 1.0, 0.0)) * inv_n).astype(BF16)
        accl[pl.ds(0, 48), :] += fold(dl.astype(F32))
        accw[...] += dot_nt(dl, hb[...])
        dlp[pl.ds(0, 48), :] = dl

        @pl.loop(0, hid // HR)
        def _(i):
            rows = lanes_at(i, HR)
            dn = dot(wcNs[rows, :], dlp[...]) * dn2[rows, n]
            dn2[rows, n] = dn
            acc0[rows, :] += fold(dn * mixed[rows, n])
            acc1[rows, :] += fold(dn)

    own_lp = pltpu.make_async_copy(lps, o_lp.at[:, o_own], ss.at[names["lp"]])
    own_lp.start()
    s3h[h, :, pl.ds(0, hid)] = row_of(acc0[...])
    s3h[h, :, pl.ds(hid, hid)] = row_of(acc1[...])
    zpad = jnp.zeros((80, 128), F32)
    s3h[h, :, pl.ds(2 * hid, 128)] = row_of(jnp.concatenate([accl[pl.ds(0, 48), :], zpad], axis=0))
    s3h[h, :, pl.ds(2 * hid + 128, 128)] = row_of(jnp.concatenate([accl[pl.ds(48, 48), :], zpad], axis=0))
    hops_start(s3h, "s3h")

    def cwh_copy(d):
        return rc(cwp.at[d], cwh.at[d], "cwh", d, peer(d), r)

    q = hid // HOPS

    @pl.loop(0, HOPS)
    def _(d):
        cwp[d] = accw[:, lanes_at(peer(d), q)].astype(BF16)

    hops_wait(s3h, "s3h")
    s3r[r] = total(s3h, HOPS)
    rows_start(s3r, "s3r")

    @pl.loop(1, HOPS)
    def _(d):
        cwh_copy(d).start()

    lp_copy(first).start()
    lp_copy(second).start()
    lp_copy(HOPS - 1).start()
    rows_wait(s3r, "s3r")
    st3 = total(s3r, R)
    db2 = st3[:, hid : 2 * hid]
    dg2t = inv2 * (st3[:, :hid] - mean2 * db2)
    o_small[pl.ds(0, 1), :] = dg2t
    o_small[pl.ds(1, 1), :] = db2
    o_small[pl.ds(4, 1), pl.ds(0, 256)] = st3[:, 2 * hid : 2 * hid + 256]
    o_small[pl.ds(4, 1), pl.ds(256, hid - 256)] = jnp.zeros((1, hid - 256), F32)
    t2 = scale2 * inv2 * dg2t * inv_n
    cols[1] = col_of(-t2)
    cols[2] = col_of(t2 * mean2 - scale2 * db2 * inv_n)

    @pl.loop(0, hid // 16)
    def _(i):
        rows = lanes_at(i, 16)
        v = dn2[rows, :] * spread(cols[0, rows, :], sub)
        v = v + mixed[rows, :] * spread(cols[1, rows, :], sub) + spread(cols[2, rows, :], sub)
        dmx[rows, :] = v.astype(BF16)

    @functools.partial(each, 1, Z)
    def _(e):
        gz_copy(e, zi).wait_send()
        gz_copy(e, lax.rem(zi + Z - e, Z)).wait_recv()

    gfin[c] = total(gz, Z)
    gd_copy(c).start()

    mine = lanes_at(c, half)
    theirs = lanes_at(1 - c, half)

    def pair_copy(d):
        return rc(dmp.at[d, theirs, :], pr.at[d], "pair", d, h, sib)

    qrows = half // S
    zown = pl.ds(pl.multiple_of(c * half + zpar * qrows, 16), qrows)
    zother = pl.ds(pl.multiple_of(c * half + (1 - zpar) * qrows, 16), qrows)

    def z1_copy(d):
        return rc(dmp.at[d, zother, :], z1r.at[d], "z1", d, h, 2 * zmate + c)

    def z1_start(d):
        if S > 1:
            z1_copy(d).start()

    def z1_sum(d):
        if S > 1:
            done(z1_copy(d))

            @pl.loop(0, qrows // 32)
            def _(i):
                rows = pl.ds(pl.multiple_of(c * half + zpar * qrows + i * 32, 32), 32)
                dmp[d, rows, :] = (dmp[d, rows, :].astype(F32) + z1r[d, lanes_at(i, 32), :].astype(F32)).astype(BF16)

    def hop_copy(d):
        return rc(dmp.at[d, zown, :], hr.at[d], "hop", d, peer(d), r)

    def pair_sum(d):
        done(pair_copy(d))

        @pl.loop(0, half // 32)
        def _(i):
            rows = pl.ds(pl.multiple_of(c * half + i * 32, 32), 32)
            dmp[d, rows, :] = (dmp[d, rows, :].astype(F32) + pr[d, lanes_at(i, 32), :].astype(F32)).astype(BF16)

    def mix_grad(d):
        dmp[d] = dot_nt(mi[d], dmx[...]).astype(BF16)
        pair_copy(d).start()

    def mix_grads(lo):
        @pl.loop(0, 2)
        def _(i):
            mix_grad(lo + 1 - i)

        pair_sum(lo + 1)
        z1_start(lo + 1)

    def mix_hop(d):
        z1_sum(d)
        hop_copy(d).start()

    mix_grads(2)

    G2 = Z // S
    zq = lax.div(zi, S)

    def zr_copy(e, which):
        rows, lanes = chunk(0, which, qrows, G2, hid)
        return rc(hr.at[0, rows, lanes], zr.at[e], "zr", e, h, (lax.rem(zq + e, G2) * S + zpar) * 2 + c)

    def final_chunk(z):
        return chunk(c * half + lax.rem(z, S) * qrows, lax.div(z, S), qrows, G2, hid)

    def zg_copy(e, which):
        rows, lanes = final_chunk(which)
        ref = fin.at[rows, lanes]
        return rc(ref, ref, "zg", e, h, lax.rem(zi + e, Z) * 2 + c)

    def ddm_copy(core):
        ref = fin.at[lanes_at(core, half), :]
        return rc(ref, ref, "ddm", 0, h, sib)

    def d_copy(d):
        return rc(dsend.at[d], o_d.at[h], "d", d, peer(d), r)

    def dt_copy(d):
        return rc(dtail.at[d], o_dt.at[h], "dt", d, peer(d), r)

    def pp_copy(d):
        return rc(ps.at[d, :, theirs], ph.at[d], "pp", d, h, sib)

    def p_copy(d):
        return rc(phalf.at[d], prv.at[d], "p", d, peer(d), r)

    def p_half(d):
        done(pp_copy(d))
        phalf[d] = (ps[d, :, mine].astype(F32) + ph[d].astype(F32)).astype(BF16)

    def q_copy(d):
        return rc(qs.at[d], qv.at[d], "q", d, peer(d), r)

    @pl.loop(0, HOPS * NT)
    def _(it):
        dd = lax.div(it, NT)
        t = lax.rem(it, NT)
        d = HOPS - 1 - dd

        @pl.when(t == 0)
        def _():
            pT[...] = jnp.zeros(pT.shape, F32)

        @pl.when(jnp.logical_and(t == NT // 2, dd > 0))
        def _():
            p_half(d + 1)
            p_copy(d + 1).start()

            @pl.when(dd > 1)
            def _():
                dt_copy(d + 1).start()
                d_copy(d + 1).start()


        @pl.when(it == NT // 2)
        def _():
            pair_sum(2)
            z1_start(2)

        @pl.when(it == NT + NT // 2)
        def _():
            @pl.loop(1, HOPS)
            def _(j):
                done(cwh_copy(j))

            cw = cwp[0].astype(F32)
            for j in range(1, HOPS):
                cw = cw + cwh[j].astype(F32)
            cwr[r] = cw.astype(BF16)
            rows_start(cwr, "cwr")
            pair_sum(0)
            z1_start(0)
            mix_hop(2)

        @pl.when(it == 2 * NT + NT // 2)
        def _():
            mix_hop(1)
            rows_wait(cwr, "cwr")
            cwg[h] = total(cwr, R, F32).astype(BF16)
            hops_start(cwg, "cwg")

        @pl.when(it == 3 * NT + NT // 2)
        def _():
            z1_sum(0)

            @pl.loop(1, HOPS)
            def _(j):
                done(hop_copy(j))

            @pl.loop(0, qrows // 32)
            def _(i):
                rows = lanes_at(i, 32)
                own = pl.ds(pl.multiple_of(c * half + zpar * qrows + i * 32, 32), 32)
                hsum = dmp[0, own, :].astype(F32)
                for j in range(1, HOPS):
                    hsum = hsum + hr[j, rows, :].astype(F32)
                hr[0, rows, :] = hsum.astype(BF16)

            @functools.partial(each, 1, G2)
            def _(e):
                zr_copy(e, lax.rem(zq + e, G2)).start()

            hops_wait(cwg, "cwg")
            for j in range(HOPS):
                o_cw[:, pl.ds(j * q, q)] = cwg[j].astype(F32)

        @pl.when(it == HOPS * NT - 1)
        def _():
            @functools.partial(each, 1, G2)
            def _(e):
                done(zr_copy(e, lax.rem(zq + e, G2)))

            rows, lanes = chunk(0, zq, qrows, G2, hid)
            zt = lax.fori_loop(1, G2, lambda e, v: v + zr[e].astype(F32), hr[0, rows, lanes].astype(F32))
            frows, flanes = final_chunk(zi)
            fin[frows, flanes] = zt.astype(BF16)

            @functools.partial(each, 1, Z)
            def _(e):
                zg_copy(e, zi).start()

        n = lanes_at(t, big)
        dn = dot(wmx[d], dmx[:, n]).astype(BF16) * gp[d, :, n]
        pT[...] += dot_nt(dn, fx[d, :, n])
        grad = dot(aw[d], dn)
        dsend[d, :, n] = grad[:MAIN].astype(BF16)
        d4[:, n] = grad[MAIN : MAIN + 8]

        @pl.when(t == NT - 1)
        def _():
            pw = pT[...].T * KAPPA
            qs[d, :, pl.ds(0, hid)] = jnp.sum(pw * wall[d, wrow, :].astype(F32), axis=0, keepdims=True)
            qs[d, :, pl.ds(hid, hid)] = pw[ONES : ONES + 1, :]
            ps[d] = pw[:FP].astype(BF16)
            pp_copy(d).start()
            pack4(d4, dtail.at[d])

            @pl.when(dd < HOPS - 1)
            def _():
                q_copy(d).start()

            @pl.when(dd == 0)
            def _():
                dt_copy(d).start()
                d_copy(d).start()
                mix_hop(d)
                mix_grads(0)

    @pl.loop(1, HOPS)
    def _(d):
        done(q_copy(d))

    qr[r] = qs[0] + (qv[1] + qv[2] + qv[3])
    rows_start(qr, "qr")
    own_d = pltpu.make_async_copy(dsend.at[0], o_d.at[h], ss.at[names["d"]])
    own_d.start()
    own_dt = pltpu.make_async_copy(dtail.at[0], o_dt.at[h], ss.at[names["dt"]])
    own_dt.start()

    p_half(0)

    @pl.loop(1, HOPS)
    def _(d):
        done(p_copy(d))

    psum = phalf[0].astype(F32) + (prv[1].astype(F32) + prv[2].astype(F32) + prv[3].astype(F32))
    pz[zi] = psum.astype(BF16)

    def pz_copy(e, which):
        return rc(pz.at[which], pz.at[which], "pz", e, h, lax.rem(zi + e, Z) * 2 + c)

    @functools.partial(each, 1, Z)
    def _(e):
        pz_copy(e, zi).start()

    @functools.partial(each, 1, Z)
    def _(e):
        zg_copy(e, zi).wait_send()
        zg_copy(e, lax.rem(zi + Z - e, Z)).wait_recv()

    ddm_copy(c).start()

    rows_wait(qr, "qr")
    qt = total(qr, R)
    db = qt[:, hid:]
    dgn = inv * (qt[:, :hid] - mean * db)
    o_small[pl.ds(2, 1), :] = dgn
    o_small[pl.ds(3, 1), :] = db
    c1 = scale * db * inv_n
    c2 = inv * scale * dgn * inv_n
    shift = c1 - mean * c2
    row = lax.broadcasted_iota(jnp.int32, (128, hid), 0)
    q1, q2 = split2(jnp.where(row == ONES, shift, wown32 * c2))
    o_m[...] = (dot_nt(wown, q1) + dot_nt(wown, q2))[:FP]
    gd_copy(c).wait_send()
    gd_copy(1 - c).wait_recv()
    g1, g2, g3 = split3(jnp.concatenate([gfin[0], gfin[1]], axis=0))
    gq = dot(g1, q1) + dot(g2, q1) + dot(g3, q1) + dot(g1, q2) + dot(g2, q2)

    @functools.partial(each, 1, Z)
    def _(e):
        pz_copy(e, zi).wait_send()
        pz_copy(e, lax.rem(zi + Z - e, Z)).wait_recv()

    pfin[c] = total(pz, Z).astype(BF16)

    def pd_copy(core):
        return rc(pfin.at[core], pfin.at[core], "pd", 0, h, sib)

    pd_copy(c).start()
    ddm_copy(c).wait_send()
    ddm_copy(1 - c).wait_recv()
    o_mix[...] = fin[...]

    pd_copy(c).wait_send()
    pd_copy(1 - c).wait_recv()
    ptot = jnp.concatenate([pfin[0], pfin[1]], axis=1).astype(F32)
    o_gw[...] = ptot * scale - gq[:FP]
    own_d.wait()
    own_dt.wait()
    own_lp.wait()

    @pl.loop(1, HOPS)
    def _(d):
        done(d_copy(d))
        done(dt_copy(d))
        done(lp_copy(d))


def last_kernel(
    nodes,
    ft, d, dt, lp, m, mix, gw, small, cw,
    o_lp, o_gf, o_mix, o_gw, o_gg, o_gb, o_hg, o_hb, o_cw, o_cb, o_loss, low,
):
    feat, n = ft.shape
    ncls = o_lp.shape[0]
    o_lp[...] = lp[...].astype(F32)[:ncls]
    mm = m[...]
    f = ft[...]
    fix = dot(mm[:, :feat].astype(BF16), f) + mm[:, ONES : ONES + 1]
    tail = dt[0].astype(F32)
    for b in range(4):
        low[pl.ds(0, 4), pl.ds(b * (n // 4), n // 4)] = tail[4 * b : 4 * b + 4]
    gf = jnp.concatenate([d[0].astype(F32), low[...]], axis=0)[:feat] - fix[:feat]
    if STRIDED:
        flat = o_gf.reshape(feat * (n // 128), 128)
        for i in range(n // 128):
            flat[pl.ds(i, feat, stride=n // 128), :] = gf[:, i * 128 : (i + 1) * 128]
    else:
        for i in range(n // 128):
            o_gf[:, i, :] = gf[:, i * 128 : (i + 1) * 128]

    @pl.when(pl.program_id(0) == 0)
    def _():
        hid = mix.shape[1]
        o_mix[...] = mix[...].astype(F32)
        for i in range(hid // 128):
            o_gw[:, i, :] = gw[pl.ds(0, feat), pl.ds(i * 128, 128)]
        o_hg[...] = small[pl.ds(0, 1), :]
        o_hb[...] = small[pl.ds(1, 1), :]
        o_gg[...] = small[pl.ds(2, 1), :]
        o_gb[...] = small[pl.ds(3, 1), :]
        o_cw[...] = cw[pl.ds(0, ncls), :]
        o_cb[...] = small[pl.ds(4, 1), pl.ds(0, ncls)]
        o_loss[...] = jnp.sum(small[pl.ds(4, 1), pl.ds(128, 128)], axis=1, keepdims=True) * (-1.0 / nodes)


def shards(
    R, features, branch_weight, branch_gain, branch_bias, mix_weight, mixing_norm_gain, mixing_norm_bias,
    class_weight, class_bias, labels, hop_mask,
):
    local, feat = features.shape[1:]
    hid = mix_weight.shape[0]
    ncls = class_weight.shape[1]
    nodes = local * R
    sub = local // HOPS
    Z = R // 2
    half = hid // 2
    S = min(Z, 2)
    G2, qrows = Z // S, half // S
    zrows, zcols = chunk(0, 0, qrows, G2, hid)
    assert feat == ONES and ncls == 47 and local // hop_mask.shape[0] == 128
    ft = features[0].T
    sd = jax.ShapeDtypeStruct
    vm = pl.BlockSpec(memory_space=pltpu.VMEM)
    hbm = pl.BlockSpec(memory_space=pl.ANY)
    _, nsem = sem_plan(R)
    V = pltpu.VMEM
    outs = pl.pallas_call(
        functools.partial(main_kernel, R, nodes),
        grid=(1,),
        out_shape=(
            sd((48, local), BF16),
            sd((HOPS, MAIN, sub), BF16),
            sd((HOPS, 16, sub // 4), BF16),
            sd((FP, 128), F32),
            sd((hid, hid), BF16),
            sd((FP, hid), F32),
            sd((8, hid), F32),
            sd((48, hid), F32),
        ),
        in_specs=[hbm, pl.BlockSpec((16, local), lambda i: (MAIN // 16, 0))]
        + [vm] * 9
        + [pl.BlockSpec(memory_space=pltpu.SMEM)],
        out_specs=(hbm, hbm, hbm, vm, vm, vm, vm, vm),
        scratch_shapes=[
            V((128, local), BF16),
            V((HOPS, 128, sub), BF16),
            V((HOPS, 16, sub // 4), BF16),
            V((HOPS, 16, sub // 4), BF16),
            V((48, sub // 4), F32),
            V((HOPS, hid + 128, hid), BF16),
            V((HOPS, hid, 256), BF16),
            V((HOPS, FP, hid), BF16),
            V((HOPS, hid, hid), BF16),
            V((HOPS, 16, sub), BF16),
            V((HOPS, hid, sub), BF16),
            V((HOPS, hid, sub), BF16),
            V((hid, sub), F32),
            V((hid, sub), F32),
            V((hid, sub), BF16),
            V((128, 128), F32),
            V((64, 128), F32),
            V((Z, 64, 128), F32),
            V((2, 64, 128), F32),
            V((R, 1, 2 * hid), F32),
            V((HOPS, 1, 2 * hid), F32),
            V((HOPS, 1, 2 * hid), F32),
            V((R, 1, 2 * hid), F32),
            V((HOPS, 1, 2 * hid + 256), F32),
            V((R, 1, 2 * hid + 256), F32),
            V((HOPS, 48, hid // HOPS), BF16),
            V((HOPS, 48, hid // HOPS), BF16),
            V((R, 48, hid // HOPS), BF16),
            V((HOPS, 48, hid // HOPS), BF16),
            V((48, sub), BF16),
            V((128, hid), F32),
            V((hid, 128), BF16),
            V((8, 128), F32),
            V((hid, min(2 * TILE, sub)), BF16),
            V((128, min(2 * TILE, sub)), BF16),
            V((hid, 128), F32),
            V((hid, 128), F32),
            V((96, 128), F32),
            V((48, hid), F32),
            V((3, hid, 128), F32),
            V((HOPS, hid, hid), BF16),
            V((HOPS, half, hid), BF16),
            V((HOPS, qrows, hid), BF16),
            V((HOPS, qrows, hid), BF16),
            V((max(G2, 2), zrows.size, zcols.size), BF16),
            V((hid, hid), BF16),
            V((HOPS, MAIN, sub), BF16),
            V((8, sub), F32),
            V((HOPS, 16, sub // 4), BF16),
            V((hid, 128), F32),
            V((HOPS, FP, hid), BF16),
            V((HOPS, FP, half), BF16),
            V((HOPS, FP, half), BF16),
            V((HOPS, FP, half), BF16),
            V((HOPS, 1, 2 * hid), F32),
            V((HOPS, 1, 2 * hid), F32),
            V((R, 1, 2 * hid), F32),
            V((Z, FP, half), BF16),
            V((2, FP, half), BF16),
            pltpu.SemaphoreType.DMA((nsem,)),
            pltpu.SemaphoreType.DMA((nsem,)),
        ],
        compiler_params=pltpu.CompilerParams(
            collective_id=0, has_side_effects=True, vmem_limit_bytes=63 * 1024 * 1024
        ),
        cost_estimate=pl.CostEstimate(flops=2 * 8 * 10**9, bytes_accessed=10**7, transcendentals=10**7),
        name="main",
    )(
        ft, ft, branch_weight[0], branch_gain, branch_bias, mix_weight, mixing_norm_gain[None], mixing_norm_bias[None],
        class_weight.T, class_bias[None], labels[None], hop_mask.T,
    )
    lp, dd, dt, m, mix, gw, small, cw = outs
    nb = sub
    whole = lambda shape: pl.BlockSpec(shape, lambda i: (0,) * len(shape))
    lp, gf, mix, gw, gg, gb, hg, hb, cw, cb, loss = pl.pallas_call(
        functools.partial(last_kernel, nodes),
        grid=(local // nb,),
        out_shape=(
            sd((ncls, local), F32),
            sd((feat, local // 128, 128), F32),
            sd((hid, hid), F32),
            sd((feat, hid // 128, 128), F32),
            sd((1, hid), F32),
            sd((1, hid), F32),
            sd((1, hid), F32),
            sd((1, hid), F32),
            sd((ncls, hid), F32),
            sd((1, ncls), F32),
            sd((1, 1), F32),
        ),
        in_specs=[
            pl.BlockSpec((feat, nb), lambda i: (0, i)),
            pl.BlockSpec((1, MAIN, nb), lambda i: (i, 0, 0)),
            pl.BlockSpec((1, 16, nb // 4), lambda i: (i, 0, 0)),
            pl.BlockSpec((48, nb), lambda i: (0, i)),
            whole((FP, 128)),
            whole((hid, hid)),
            whole((FP, hid)),
            whole((8, hid)),
            whole((48, hid)),
        ],
        out_specs=(
            pl.BlockSpec((ncls, nb), lambda i: (0, i)),
            pl.BlockSpec((feat, nb // 128, 128), lambda i: (0, i, 0)),
            whole((hid, hid)),
            whole((feat, hid // 128, 128)),
            whole((1, hid)),
            whole((1, hid)),
            whole((1, hid)),
            whole((1, hid)),
            whole((ncls, hid)),
            whole((1, ncls)),
            whole((1, 1)),
        ),
        scratch_shapes=[V((8, nb), F32)],
        compiler_params=pltpu.CompilerParams(vmem_limit_bytes=60 * 1024 * 1024),
        name="last",
    )(ft, dd, dt, lp, m, mix, gw, small, cw)
    return (
        lp.T,
        loss[0, 0],
        with_layout_constraint(gf.reshape(feat, 1, local), Layout((0, 1, 2))).transpose(1, 2, 0),
        gw.reshape(1, feat, hid),
        gg,
        gb,
        mix,
        hg[0],
        hb[0],
        cw.T,
        cb[0],
    )


def solution(mesh):
    placed = (
        P("hop", "rows", None), P("hop", None, None), P("hop", None), P("hop", None), P("hop", None),
        P(), P(), P(), P(), P("rows"), P("rows", None),
    )
    assert mesh.shape["hop"] == HOPS
    return jax.shard_map(
        functools.partial(shards, mesh.shape["rows"]),
        mesh=mesh,
        in_specs=placed,
        out_specs=(
            P("rows", None), P(), P("hop", "rows", None), P("hop", None, None), P("hop", None), P("hop", None),
            P("hop", None), P(), P(), P(), P(),
        ),
        check_vma=False,
    )
```

```python
import functools
import math

import jax
import jax.numpy as jnp
from jax import lax
from jax.experimental import pallas as pl
from jax.experimental.layout import Layout, with_layout_constraint
from jax.experimental.pallas import tpu as pltpu
from jax.sharding import PartitionSpec as P

MESH = pl.DeviceIdType.MESH
EPS = 1e-05
HOPS = 4
ONES = 100
FP = 112
PROWS = 128
MAIN = 96
TILE = 256
STRIDED = True
C0 = math.sqrt(2.0 / math.pi)
C1 = C0 * 0.044715
KAPPA = C1 ** (1.0 / 3.0)
ALPHA = C0 / KAPPA
F32 = jnp.float32
BF16 = jnp.bfloat16


def dot(a, b):
    return lax.dot_general(a, b, (((1,), (0,)), ((), ())), preferred_element_type=F32)


def dot_nt(a, b):
    return lax.dot_general(a, b, (((1,), (1,)), ((), ())), preferred_element_type=F32)


def split2(x):
    hi = x.astype(BF16)
    return hi, (x - hi.astype(F32)).astype(BF16)


def split3(x):
    hi = x.astype(BF16)
    rest = x - hi.astype(F32)
    mid = rest.astype(BF16)
    return hi, mid, (rest - mid.astype(F32)).astype(BF16)


def gelu_slope(z):
    u = z * z
    t = jnp.tanh(z * (C0 + C1 * u))
    s = 0.5 * t + 0.5
    g = z * s
    return g, s + (g - g * s) * (2.0 * C0 + 6.0 * C1 * u)


def scaled_gelu_slope(y):
    u = y * y
    t = jnp.tanh(y * (u + ALPHA))
    up = t + 1.0
    g = y * up
    return g, up + (g * (1.0 - t)) * (3.0 * u + ALPHA)


def fold(x):
    total = x[:, :128]
    for i in range(1, x.shape[1] // 128):
        total = total + x[:, i * 128 : (i + 1) * 128]
    return total


def spread(c, n):
    return jnp.concatenate([c] * (n // 128), axis=1)


def row_of(acc):
    return jnp.sum(acc.T, axis=0, keepdims=True)


def col_of(row):
    return jnp.broadcast_to(row, (128, row.shape[1])).T


def each(lo, hi, body):
    if hi - lo == 1:
        body(lo)
    elif hi > lo:
        pl.loop(lo, hi)(body)


class Alloc:
    def __init__(self):
        self.n = 0

    def __call__(self, count):
        base = self.n
        self.n += count
        return base


def sem_plan(R):
    Z = R // 2
    a = Alloc()
    names = {}
    for name, count in (
        ("feat", 5), ("ft", 4), ("loc", 1), ("ws", 4), ("zf", 4), ("dd", 4), ("s1", R), ("ab", 4), ("gp", 1), ("gz", Z), ("gd", 1),
        ("s2h", 4), ("s2r", R), ("s3h", 4), ("s3r", R), ("lp", 4), ("cwh", 4), ("cwr", R), ("cwg", 4),
        ("pair", 4), ("z1", 4), ("hop", 4), ("zr", Z), ("zg", Z), ("ddm", 1), ("d", 4), ("dt", 4), ("p", 4), ("q", 4),
        ("qr", R), ("pp", 4), ("pz", Z), ("pd", 1), ("pg", R),
    ):
        names[name] = a(count)
    return names, a.n


def chunk(base, i, rows, pieces, cols):
    if rows // pieces >= 16:
        take = rows // pieces
        return pl.ds(pl.multiple_of(base + i * take, 16), take), pl.ds(0, cols)
    m = 16 * pieces // rows
    wide = cols // m
    return (
        pl.ds(pl.multiple_of(base + (i // m) * 16, 16), 16),
        pl.ds(pl.multiple_of((i % m) * wide, 128), wide),
    )


def main_kernel(
    R,
    nodes,
    ft, ft4, wb, bgain, bbias, wm, gain2, bias2, wc, cb, lab, msk,
    o_lp, o_d, o_dt, o_m, o_mix, o_gw, o_small, o_cw,
    fs, fx, ftail, frt, st4, wall, wl, aw, wmx, keep, mi, gp, mixed, dn2, dmx,
    gown, gpr, gz, gfin, s1, ab, s2h, s2r, s3h, s3r, cwp, cwh, cwr, cwg, lps,
    wcs, wcNs, cbs, hb, dlp, acc0, acc1, accl, accw, cols,
    dmp, pr, z1r, hr, zr, fin, dsend, d4, dtail, pT, ps, ph, phalf, prv, qs, qv, qr, pall, pz, pfin,
    ss, rs,
):
    names, _ = sem_plan(R)
    Z = R // 2
    h = lax.axis_index("hop")
    r = lax.axis_index("rows")
    c = lax.rem(r, 2)
    zi = lax.div(r, 2)
    sib = r + 1 - 2 * c
    local = ft.shape[1]
    sub = local // HOPS
    hid = wm.shape[0]
    half = hid // 2
    big = min(2 * TILE, sub)
    UN = big // TILE
    NT = sub // big
    inv_n = 1.0 / nodes

    def peer(d):
        x = lax.rem(h + d, 2)
        y = lax.rem(lax.div(h, 2) + lax.div(d, 2), 2)
        return 2 * y + x

    def rc(src, dst, name, i, hh, rr):
        return pltpu.make_async_remote_copy(
            src_ref=src, dst_ref=dst, send_sem=ss.at[names[name] + i], recv_sem=rs.at[names[name] + i],
            device_id=(hh, rr), device_id_type=MESH,
        )

    def done(cp):
        cp.wait_send()
        cp.wait_recv()

    def lanes_at(i, n):
        return pl.ds(pl.multiple_of(i * n, n), n)

    barrier = pltpu.get_barrier_semaphore()

    def greet(hh, rr):
        pl.semaphore_signal(barrier, inc=1, device_id=(hh, rr), device_id_type=MESH)

    @pl.loop(1, HOPS)
    def _(d):
        greet(peer(d), r)

    @functools.partial(each, 1, R)
    def _(e):
        greet(h, lax.rem(r + e, R))

    def rows_start(buf, name):
        @functools.partial(each, 1, R)
        def _(e):
            rc(buf.at[r], buf.at[r], name, e, h, lax.rem(r + e, R)).start()

    def rows_wait(buf, name):
        @functools.partial(each, 1, R)
        def _(e):
            src = lax.rem(r + R - e, R)
            done(rc(buf.at[src], buf.at[src], name, e, h, lax.rem(r + e, R)))

    def hops_start(buf, name):
        @pl.loop(1, HOPS)
        def _(d):
            rc(buf.at[h], buf.at[h], name, d, peer(d), r).start()

    def hops_wait(buf, name):
        @pl.loop(1, HOPS)
        def _(d):
            done(rc(buf.at[peer(d)], buf.at[peer(d)], name, d, peer(d), r))

    def total(buf, n, dtype=F32):
        return lax.fori_loop(1, n, lambda i, t: t + buf[i].astype(dtype), buf[0].astype(dtype))

    loc = pltpu.make_async_copy(ft.at[pl.ds(0, MAIN), :], fs.at[pl.ds(0, MAIN), :], ss.at[names["loc"]])
    loc.start()

    def pack4(src, dst):
        n = st4.shape[1]
        for b in range(4):
            st4[pl.ds(4 * b, 4), :] = src[pl.ds(0, 4), pl.ds(b * n, n)].astype(F32)
        dst[...] = st4[pl.ds(0, 16), :].astype(BF16)

    def unpack4(src, dst):
        n = st4.shape[1]
        row = lax.broadcasted_iota(jnp.int32, (32, n), 0)
        st4[pl.ds(0, 16), :] = src[...].astype(F32)
        st4[pl.ds(16, 32), :] = jnp.where(row == ONES - MAIN, 1.0, 0.0)
        for b in range(4):
            st4[pl.ds(16, 4), :] = st4[pl.ds(4 * b, 4), :]
            dst[pl.ds(MAIN, 32), pl.ds(b * n, n)] = st4[pl.ds(16, 32), :].astype(BF16)

    wrow = pl.ds(hid, 128)
    wall[0, pl.ds(hid + 96, 32), :] = jnp.zeros((32, hid), BF16)
    wall[0, pl.ds(hid, 100), :] = wb[...]

    @pl.loop(0, hid // 128)
    def _(i):
        k = lanes_at(i, 128)
        wall[0, pl.ds(0, hid), k] = wm[k, :].astype(F32).T.astype(BF16)

    def feat_copy(d):
        rows = pl.ds(0, MAIN)
        return rc(fs.at[rows, lanes_at(peer(d), sub)], fx.at[d, rows, :], "feat", d, peer(d), r)

    def feat_half(p):
        rows = pl.ds(0, MAIN)
        d = HOPS - 1
        n = sub // 2
        return rc(fs.at[rows, lanes_at(2 * peer(d) + p, n)], fx.at[d, rows, pl.ds(p * n, n)], "feat", d + p, peer(d), r)

    def ft_copy(d):
        return rc(ftail.at[peer(d)], frt.at[d], "ft", d, peer(d), r)

    pl.semaphore_wait(barrier, HOPS - 1 + R - 1)

    S = min(Z, 2)
    part = (hid + 128) // (2 * S)
    zpar = lax.rem(zi, S)
    zmate = zi + (S - 1) - 2 * (S - 1) * zpar

    def part_rows(core, par):
        return pl.ds(pl.multiple_of((core * S + par) * part, 16), part)

    def ws_copy(d):
        rows = part_rows(c, zpar)
        return rc(wall.at[0, rows, :], wall.at[d, rows, :], "ws", d, peer(d), r)

    def zf_copy(d, par):
        ref = wall.at[d, part_rows(c, par), :]
        return rc(ref, ref, "zf", d, h, 2 * zmate + c)

    def dd_copy(d, core):
        ref = wall.at[d, pl.ds(pl.multiple_of(core * S * part, 16), S * part), :]
        return rc(ref, ref, "dd", d, h, sib)

    first, second = 1 + c, 2 - c
    ws_copy(first).start()
    ws_copy(second).start()
    ws_copy(HOPS - 1).start()
    loc.wait()
    feat_copy(first).start()
    feat_copy(second).start()

    @pl.loop(0, HOPS)
    def _(j):
        lanes = lanes_at(j, sub)
        pack4(ft4.at[:, lanes], ftail.at[j])
        unpack4(ftail.at[j], fs.at[:, lanes])


    @pl.loop(1, HOPS)
    def _(d):
        ft_copy(d).start()

    fx0 = pltpu.make_async_copy(fs.at[:, lanes_at(h, sub)], fx.at[0], ss.at[names["loc"]])
    fx0.start()

    def gram(i, g):
        f = fs[:, lanes_at(i, sub)]
        return g + dot_nt(f, f)

    g = lax.fori_loop(0, HOPS, gram, jnp.zeros((128, 128), F32))
    wown = wall[0, wrow, :]
    wown32 = wown.astype(F32)
    g1, g2, g3 = split3(g)
    gw = dot(g1, wown) + dot(g2, wown) + dot(g3, wown)
    s1[r, :, pl.ds(0, hid)] = gw[ONES : ONES + 1, :]
    s1[r, :, pl.ds(hid, hid)] = jnp.sum(gw * wown32, axis=0, keepdims=True)
    rows_start(s1, "s1")
    gown[...] = g

    @pl.loop(0, HOPS * (sub // 128))
    def _(i):
        d = lax.div(i, sub // 128)
        b = lax.rem(i, sub // 128)
        late = peer(d) - 2
        m = jnp.where(late >= 0, msk[jnp.maximum(late, 0), h * (sub // 128) + b], 1)
        keep[d, :, lanes_at(b, 128)] = jnp.full((16, 128), 0.5 * m.astype(F32)).astype(BF16)

    wcs[...] = jnp.zeros(wcs.shape, F32)
    wcs[pl.ds(0, wc.shape[0]), :] = wc[...].astype(F32)
    cbs[...] = jnp.zeros(cbs.shape, F32)
    cbs[pl.ds(0, 1), pl.ds(0, cb.shape[1])] = cb[...]
    ncls = wc.shape[0]

    @pl.loop(0, hid // 16)
    def _(i):
        rows = lanes_at(i, 16)
        mixed[rows, :] = jnp.zeros((16, sub), F32)
        mi[0, rows, pl.ds(0, big)] = jnp.zeros((16, big), BF16)

    fx0.wait()

    rows_wait(s1, "s1")
    st = total(s1, R)
    mean = st[:, :hid] * inv_n
    var = st[:, hid:] * inv_n - mean * mean
    inv = lax.rsqrt(var + EPS)
    scale = inv * bgain[...]
    ab[0, :, pl.ds(0, hid)] = scale
    ab[0, :, pl.ds(hid, hid)] = bbias[...] - mean * scale

    def ab_copy(d):
        return rc(ab.at[0], ab.at[d], "ab", d, peer(d), r)

    @pl.loop(1, HOPS)
    def _(d):
        ab_copy(d).start()

    def prepare(d):
        a = ab[d, :, pl.ds(0, hid)]
        b = ab[d, :, pl.ds(hid, hid)]
        ws = wall[d, wrow, :].astype(F32) * (a * KAPPA)
        aw[d] = ws[:FP].astype(BF16)
        row = lax.broadcasted_iota(jnp.int32, (128, hid), 0)
        wt = jnp.where(row == ONES, b * KAPPA, ws).T
        hi, lo = split2(wt)
        wl[d, :, pl.ds(0, 128)] = hi
        wl[d, :, pl.ds(128, 128)] = lo

    g_pair = rc(gown.at[lanes_at(1 - c, 64), :], gpr, "gp", 0, h, sib)

    def gz_copy(e, which):
        return rc(gz.at[which], gz.at[which], "gz", e, h, lax.rem(zi + e, Z) * 2 + c)

    def gd_copy(core):
        return rc(gfin.at[core], gfin.at[core], "gd", 0, h, sib)

    @pl.loop(0, HOPS * NT)
    def _(it):
        d = lax.div(it, NT)
        t = lax.rem(it, NT)

        @pl.when(t == 0)
        def _():
            @pl.when(d > 0)
            def _():
                @pl.when(d < HOPS - 1)
                def _():
                    done(feat_copy(d))

                @pl.when(d == HOPS - 1)
                def _():
                    done(feat_half(0))

                done(ft_copy(d))
                unpack4(frt.at[d], fx.at[d])
                dd_copy(d, c).wait_send()
                dd_copy(d, 1 - c).wait_recv()
                done(ab_copy(d))

            prepare(d)

        if S > 1:

            @pl.when(it == min(1, NT - 1))
            def _():
                @pl.loop(1, HOPS)
                def _(j):
                    done(ws_copy(j))

                zf_copy(1, zpar).start()

        @pl.when(it == min(2, NT - 1))
        def _():
            feat_half(0).start()
            feat_half(1).start()

        @pl.when(jnp.logical_and(t == NT - 1, d < HOPS - 1))
        def _():
            if S > 1:
                zf_copy(d + 1, zpar).wait_send()
                zf_copy(d + 1, 1 - zpar).wait_recv()

                @pl.when(d < HOPS - 2)
                def _():
                    zf_copy(d + 2, zpar).start()

            else:
                done(ws_copy(d + 1))
            dd_copy(d + 1, c).start()

        @pl.when(it == 2 * NT)
        def _():
            g_pair.start()

        @pl.when(it == 3 * NT)
        def _():
            done(g_pair)
            gz[zi] = gown[lanes_at(c, 64), :] + gpr[...]

            @functools.partial(each, 1, Z)
            def _(e):
                gz_copy(e, zi).start()

        @pl.when(it == 3 * NT + NT // 2)
        def _():
            done(feat_half(1))

        pit = jnp.maximum(it - 1, 0)
        pd = lax.div(pit, NT)
        pt = lax.rem(pit, NT)
        adds = []
        for u in range(UN):
            adds.append(dot(wall[pd, pl.ds(0, hid), :], mi[pd, :, lanes_at(pt * UN + u, TILE)]))
        for u in range(UN):
            n = lanes_at(t * UN + u, TILE)
            f = fx[d, :, n]
            z = dot(wl[d], jnp.concatenate([f, f], axis=0))
            k = keep[d, :, n]
            k = jnp.concatenate([k] * 4, axis=0)
            for i in range(0, hid, 64):
                g1, d1 = scaled_gelu_slope(z[i : i + 64].astype(BF16))
                g2, d2 = scaled_gelu_slope(g1 * k)
                mi[d, pl.ds(i, 64), n] = g2
                gp[d, pl.ds(i, 64), n] = d1 * d2 * k
        for u in range(UN):
            n = lanes_at(pt * UN + u, TILE)
            mixed[:, n] = mixed[:, n] + adds[u]

    acc0[...] = jnp.zeros(acc0.shape, F32)
    acc1[...] = jnp.zeros(acc1.shape, F32)

    @pl.loop(0, UN)
    def _(u):
        n = lanes_at((NT - 1) * UN + u, TILE)
        mixed[:, n] = mixed[:, n] + dot(wall[HOPS - 1, pl.ds(0, hid), :], mi[HOPS - 1, :, n])

    @pl.loop(0, hid // 32)
    def _(i):
        rows = lanes_at(i, 32)
        x = mixed[rows, :]
        acc0[rows, :] = fold(x)
        acc1[rows, :] = fold(x * x)

    def natural(lo, hi):
        @pl.loop(lo * (hid // 128), hi * (hid // 128))
        def _(i):
            d = lax.div(i, hid // 128)
            k = lanes_at(lax.rem(i, hid // 128), 128)
            wmx[d, k, :] = wall[d, pl.ds(0, hid), k].astype(F32).T.astype(BF16)

    s2h[h, :, pl.ds(0, hid)] = row_of(acc0[...])
    s2h[h, :, pl.ds(hid, hid)] = row_of(acc1[...])
    hops_start(s2h, "s2h")
    natural(0, 2)
    hops_wait(s2h, "s2h")
    s2r[r] = total(s2h, HOPS)
    rows_start(s2r, "s2r")
    natural(2, HOPS)
    wc48 = wcs[pl.ds(0, 48), :].astype(BF16)
    wcNs[...] = wcs[...].T.astype(BF16)
    crow = lax.broadcasted_iota(jnp.int32, (128, 128), 0)
    cbc = jnp.where(crow < ncls, jnp.broadcast_to(cbs[pl.ds(0, 1), :], (128, 128)).T, -1e30)[:48]
    rows_wait(s2r, "s2r")
    st2 = total(s2r, R)
    mean2 = st2[:, :hid] * inv_n
    inv2 = lax.rsqrt(st2[:, hid:] * inv_n - mean2 * mean2 + EPS * 4.0 * KAPPA * KAPPA)
    scale2 = inv2 * gain2[...]
    cols[0] = col_of(scale2)
    cols[1] = col_of(bias2[...] - mean2 * scale2)
    acc0[...] = jnp.zeros(acc0.shape, F32)
    acc1[...] = jnp.zeros(acc1.shape, F32)
    accl[...] = jnp.zeros(accl.shape, F32)
    accw[...] = jnp.zeros(accw.shape, F32)

    o_own = lanes_at(h, sub)

    def lp_copy(d):
        return rc(lps, o_lp.at[:, o_own], "lp", d, peer(d), r)

    dlp[...] = jnp.zeros(dlp.shape, BF16)
    HR = 128

    @pl.loop(0, NT)
    def _(t):
        n = lanes_at(t, big)

        @pl.loop(0, hid // HR)
        def _(i):
            rows = lanes_at(i, HR)
            z2 = mixed[rows, n] * spread(cols[0, rows, :], big) + spread(cols[1, rows, :], big)
            gv, dg = gelu_slope(z2)
            hb[rows, :] = gv.astype(BF16)
            dn2[rows, n] = dg

        lg = dot(wc48, hb[...]) + spread(cbc, big)
        lg = lg - jnp.max(lg, axis=0, keepdims=True)
        ex = jnp.exp(lg)
        se = jnp.sum(ex, axis=0, keepdims=True)
        lp = lg - jnp.log(se)
        lps[:, n] = lp.astype(BF16)
        own = lanes_at(h * NT + t, big)
        hit = lax.broadcasted_iota(jnp.int32, (48, big), 0) == lab[:, own]
        accl[pl.ds(48, 48), :] += fold(jnp.where(hit, lp, 0.0))
        dl = ((ex / se - jnp.where(hit, 1.0, 0.0)) * inv_n).astype(BF16)
        accl[pl.ds(0, 48), :] += fold(dl.astype(F32))
        accw[...] += dot_nt(dl, hb[...])
        dlp[pl.ds(0, 48), :] = dl

        @pl.loop(0, hid // HR)
        def _(i):
            rows = lanes_at(i, HR)
            dn = dot(wcNs[rows, :], dlp[...]) * dn2[rows, n]
            dn2[rows, n] = dn
            acc0[rows, :] += fold(dn * mixed[rows, n])
            acc1[rows, :] += fold(dn)

    own_lp = pltpu.make_async_copy(lps, o_lp.at[:, o_own], ss.at[names["lp"]])
    own_lp.start()
    s3h[h, :, pl.ds(0, hid)] = row_of(acc0[...])
    s3h[h, :, pl.ds(hid, hid)] = row_of(acc1[...])
    zpad = jnp.zeros((80, 128), F32)
    s3h[h, :, pl.ds(2 * hid, 128)] = row_of(jnp.concatenate([accl[pl.ds(0, 48), :], zpad], axis=0))
    s3h[h, :, pl.ds(2 * hid + 128, 128)] = row_of(jnp.concatenate([accl[pl.ds(48, 48), :], zpad], axis=0))
    hops_start(s3h, "s3h")

    def cwh_copy(d):
        return rc(cwp.at[d], cwh.at[d], "cwh", d, peer(d), r)

    q = hid // HOPS

    @pl.loop(0, HOPS)
    def _(d):
        cwp[d] = accw[:, lanes_at(peer(d), q)].astype(BF16)

    hops_wait(s3h, "s3h")
    s3r[r] = total(s3h, HOPS)
    rows_start(s3r, "s3r")

    @pl.loop(1, HOPS)
    def _(d):
        cwh_copy(d).start()

    lp_copy(first).start()
    lp_copy(second).start()
    lp_copy(HOPS - 1).start()
    rows_wait(s3r, "s3r")
    st3 = total(s3r, R)
    db2 = st3[:, hid : 2 * hid]
    dg2t = inv2 * (st3[:, :hid] - mean2 * db2)
    o_small[pl.ds(0, 1), :] = dg2t
    o_small[pl.ds(1, 1), :] = db2
    o_small[pl.ds(4, 1), pl.ds(0, 256)] = st3[:, 2 * hid : 2 * hid + 256]
    o_small[pl.ds(4, 1), pl.ds(256, hid - 256)] = jnp.zeros((1, hid - 256), F32)
    t2 = scale2 * inv2 * dg2t * inv_n
    cols[1] = col_of(-t2)
    cols[2] = col_of(t2 * mean2 - scale2 * db2 * inv_n)

    @pl.loop(0, hid // 16)
    def _(i):
        rows = lanes_at(i, 16)
        v = dn2[rows, :] * spread(cols[0, rows, :], sub)
        v = v + mixed[rows, :] * spread(cols[1, rows, :], sub) + spread(cols[2, rows, :], sub)
        dmx[rows, :] = v.astype(BF16)

    @functools.partial(each, 1, Z)
    def _(e):
        gz_copy(e, zi).wait_send()
        gz_copy(e, lax.rem(zi + Z - e, Z)).wait_recv()

    gfin[c] = total(gz, Z)
    gd_copy(c).start()

    mine = lanes_at(c, half)
    theirs = lanes_at(1 - c, half)

    def pair_copy(d):
        return rc(dmp.at[d, theirs, :], pr.at[d], "pair", d, h, sib)

    qrows = half // S
    zown = pl.ds(pl.multiple_of(c * half + zpar * qrows, 16), qrows)
    zother = pl.ds(pl.multiple_of(c * half + (1 - zpar) * qrows, 16), qrows)

    def z1_copy(d):
        return rc(dmp.at[d, zother, :], z1r.at[d], "z1", d, h, 2 * zmate + c)

    def z1_start(d):
        if S > 1:
            z1_copy(d).start()

    def z1_sum(d):
        if S > 1:
            done(z1_copy(d))

            @pl.loop(0, qrows // 32)
            def _(i):
                rows = pl.ds(pl.multiple_of(c * half + zpar * qrows + i * 32, 32), 32)
                dmp[d, rows, :] = (dmp[d, rows, :].astype(F32) + z1r[d, lanes_at(i, 32), :].astype(F32)).astype(BF16)

    def hop_copy(d):
        return rc(dmp.at[d, zown, :], hr.at[d], "hop", d, peer(d), r)

    def pair_sum(d):
        done(pair_copy(d))

        @pl.loop(0, half // 32)
        def _(i):
            rows = pl.ds(pl.multiple_of(c * half + i * 32, 32), 32)
            dmp[d, rows, :] = (dmp[d, rows, :].astype(F32) + pr[d, lanes_at(i, 32), :].astype(F32)).astype(BF16)

    def mix_grad(d):
        dmp[d] = dot_nt(mi[d], dmx[...]).astype(BF16)
        pair_copy(d).start()

    def mix_grads(lo):
        @pl.loop(0, 2)
        def _(i):
            mix_grad(lo + 1 - i)

        pair_sum(lo + 1)
        z1_start(lo + 1)

    def mix_hop(d):
        z1_sum(d)
        hop_copy(d).start()

    mix_grads(2)

    G2 = Z // S
    zq = lax.div(zi, S)

    def zr_copy(e, which):
        rows, lanes = chunk(0, which, qrows, G2, hid)
        return rc(hr.at[0, rows, lanes], zr.at[e], "zr", e, h, (lax.rem(zq + e, G2) * S + zpar) * 2 + c)

    def final_chunk(z):
        return chunk(c * half + lax.rem(z, S) * qrows, lax.div(z, S), qrows, G2, hid)

    def zg_copy(e, which):
        rows, lanes = final_chunk(which)
        ref = fin.at[rows, lanes]
        return rc(ref, ref, "zg", e, h, lax.rem(zi + e, Z) * 2 + c)

    def ddm_copy(core):
        ref = fin.at[lanes_at(core, half), :]
        return rc(ref, ref, "ddm", 0, h, sib)

    def d_copy(d):
        return rc(dsend.at[d], o_d.at[h], "d", d, peer(d), r)

    def dt_copy(d):
        return rc(dtail.at[d], o_dt.at[h], "dt", d, peer(d), r)

    def pp_copy(d):
        return rc(ps.at[d, :, theirs], ph.at[d], "pp", d, h, sib)

    def p_copy(d):
        return rc(phalf.at[d], prv.at[d], "p", d, peer(d), r)

    def p_half(d):
        done(pp_copy(d))
        phalf[d] = (ps[d, :, mine].astype(F32) + ph[d].astype(F32)).astype(BF16)

    def q_copy(d):
        return rc(qs.at[d], qv.at[d], "q", d, peer(d), r)

    @pl.loop(0, HOPS * NT)
    def _(it):
        dd = lax.div(it, NT)
        t = lax.rem(it, NT)
        d = HOPS - 1 - dd

        @pl.when(t == 0)
        def _():
            pT[...] = jnp.zeros(pT.shape, F32)

        @pl.when(jnp.logical_and(t == NT // 2, dd > 0))
        def _():
            p_half(d + 1)
            p_copy(d + 1).start()

            @pl.when(dd > 1)
            def _():
                dt_copy(d + 1).start()
                d_copy(d + 1).start()


        @pl.when(it == NT // 2)
        def _():
            pair_sum(2)
            z1_start(2)

        @pl.when(it == NT + NT // 2)
        def _():
            @pl.loop(1, HOPS)
            def _(j):
                done(cwh_copy(j))

            cw = cwp[0].astype(F32)
            for j in range(1, HOPS):
                cw = cw + cwh[j].astype(F32)
            cwr[r] = cw.astype(BF16)
            rows_start(cwr, "cwr")
            pair_sum(0)
            z1_start(0)
            mix_hop(2)

        @pl.when(it == 2 * NT + NT // 2)
        def _():
            mix_hop(1)
            rows_wait(cwr, "cwr")
            cwg[h] = total(cwr, R, F32).astype(BF16)
            hops_start(cwg, "cwg")

        @pl.when(it == 3 * NT + NT // 2)
        def _():
            z1_sum(0)

            @pl.loop(1, HOPS)
            def _(j):
                done(hop_copy(j))

            @pl.loop(0, qrows // 32)
            def _(i):
                rows = lanes_at(i, 32)
                own = pl.ds(pl.multiple_of(c * half + zpar * qrows + i * 32, 32), 32)
                hsum = dmp[0, own, :].astype(F32)
                for j in range(1, HOPS):
                    hsum = hsum + hr[j, rows, :].astype(F32)
                hr[0, rows, :] = hsum.astype(BF16)

            @functools.partial(each, 1, G2)
            def _(e):
                zr_copy(e, lax.rem(zq + e, G2)).start()

            hops_wait(cwg, "cwg")
            for j in range(HOPS):
                o_cw[:, pl.ds(j * q, q)] = cwg[j].astype(F32)

        n = lanes_at(t, big)
        dn = dot(wmx[d], dmx[:, n]).astype(BF16) * gp[d, :, n]
        pT[...] += dot_nt(dn, fx[d, :, n])
        grad = dot(aw[d], dn)
        dsend[d, :, n] = grad[:MAIN].astype(BF16)
        d4[:, n] = grad[MAIN : MAIN + 8]

        @pl.when(t == NT - 1)
        def _():
            pw = pT[...].T * KAPPA
            qs[d, :, pl.ds(0, hid)] = jnp.sum(pw * wall[d, wrow, :].astype(F32), axis=0, keepdims=True)
            qs[d, :, pl.ds(hid, hid)] = pw[ONES : ONES + 1, :]
            ps[d] = pw[:FP].astype(BF16)
            pp_copy(d).start()
            pack4(d4, dtail.at[d])

            @pl.when(dd < HOPS - 1)
            def _():
                q_copy(d).start()

            @pl.when(dd == 0)
            def _():
                dt_copy(d).start()
                d_copy(d).start()
                mix_hop(d)
                mix_grads(0)

    @pl.loop(1, HOPS)
    def _(d):
        done(q_copy(d))

    qr[r] = qs[0] + (qv[1] + qv[2] + qv[3])
    rows_start(qr, "qr")
    own_d = pltpu.make_async_copy(dsend.at[0], o_d.at[h], ss.at[names["d"]])
    own_d.start()
    own_dt = pltpu.make_async_copy(dtail.at[0], o_dt.at[h], ss.at[names["dt"]])
    own_dt.start()

    @functools.partial(each, 1, G2)
    def _(e):
        done(zr_copy(e, lax.rem(zq + e, G2)))

    rows, lanes = chunk(0, zq, qrows, G2, hid)
    zt = lax.fori_loop(1, G2, lambda e, v: v + zr[e].astype(F32), hr[0, rows, lanes].astype(F32))
    frows, flanes = final_chunk(zi)
    fin[frows, flanes] = zt.astype(BF16)

    @functools.partial(each, 1, Z)
    def _(e):
        zg_copy(e, zi).start()

    p_half(0)

    @pl.loop(1, HOPS)
    def _(d):
        done(p_copy(d))

    psum = phalf[0].astype(F32) + (prv[1].astype(F32) + prv[2].astype(F32) + prv[3].astype(F32))
    parts = Z if PROWS // Z >= 16 else 1
    cz = PROWS // parts
    pall[...] = jnp.concatenate([psum, jnp.zeros((PROWS - FP, half), F32)], axis=0).astype(BF16)

    def pz_copy(e, to, slot):
        rows = pl.ds(pl.multiple_of(to * cz, 16), cz) if parts > 1 else pl.ds(0, cz)
        return rc(pall.at[rows, :], pz.at[slot], "pz", e, h, lax.rem(zi + e, Z) * 2 + c)

    def pd_copy(core):
        return rc(pfin.at[core], pfin.at[core], "pd", 0, h, sib)

    def pg_copy(e, who):
        core, z = lax.rem(who, 2), lax.div(who, 2)
        rows = pl.ds(pl.multiple_of(z * cz, 16), cz) if parts > 1 else pl.ds(0, cz)
        return rc(pfin.at[core, rows, :], pfin.at[core, rows, :], "pg", e, h, lax.rem(r + e, R))

    @functools.partial(each, 1, Z)
    def _(e):
        pz_copy(e, lax.rem(zi + e, Z), zi).start()

    @functools.partial(each, 1, Z)
    def _(e):
        zg_copy(e, zi).wait_send()
        zg_copy(e, lax.rem(zi + Z - e, Z)).wait_recv()

    ddm_copy(c).start()

    rows_wait(qr, "qr")
    qt = total(qr, R)
    db = qt[:, hid:]
    dgn = inv * (qt[:, :hid] - mean * db)
    o_small[pl.ds(2, 1), :] = dgn
    o_small[pl.ds(3, 1), :] = db
    c1 = scale * db * inv_n
    c2 = inv * scale * dgn * inv_n
    shift = c1 - mean * c2
    row = lax.broadcasted_iota(jnp.int32, (128, hid), 0)
    q1, q2 = split2(jnp.where(row == ONES, shift, wown32 * c2))
    o_m[...] = (dot_nt(wown, q1) + dot_nt(wown, q2))[:FP]
    gd_copy(c).wait_send()
    gd_copy(1 - c).wait_recv()
    g1, g2, g3 = split3(jnp.concatenate([gfin[0], gfin[1]], axis=0))
    gq = dot(g1, q1) + dot(g2, q1) + dot(g3, q1) + dot(g1, q2) + dot(g2, q2)

    @functools.partial(each, 1, Z)
    def _(e):
        pz_copy(e, lax.rem(zi + e, Z), zi).wait_send()
        pz_copy(e, zi, lax.rem(zi + Z - e, Z)).wait_recv()

    mine_z = pl.ds(pl.multiple_of(zi * cz, 16), cz) if parts > 1 else pl.ds(0, cz)
    pz[zi] = pall[mine_z, :]
    pfin[c, mine_z, :] = total(pz, Z).astype(BF16)
    if parts > 1:

        @functools.partial(each, 1, R)
        def _(e):
            pg_copy(e, r).start()

    else:

        pd_copy(c).start()

    ddm_copy(c).wait_send()
    ddm_copy(1 - c).wait_recv()
    o_mix[...] = fin[...]

    if parts > 1:

        @functools.partial(each, 1, R)
        def _(e):
            pg_copy(e, r).wait_send()
            pg_copy(e, lax.rem(r + R - e, R)).wait_recv()

    else:
        pd_copy(c).wait_send()
        pd_copy(1 - c).wait_recv()

    ptot = jnp.concatenate([pfin[0], pfin[1]], axis=1)[:FP].astype(F32)
    o_gw[...] = ptot * scale - gq[:FP]
    own_d.wait()
    own_dt.wait()
    own_lp.wait()

    @pl.loop(1, HOPS)
    def _(d):
        done(d_copy(d))
        done(dt_copy(d))
        done(lp_copy(d))


def last_kernel(
    nodes,
    ft, d, dt, lp, m, mix, gw, small, cw,
    o_lp, o_gf, o_mix, o_gw, o_gg, o_gb, o_hg, o_hb, o_cw, o_cb, o_loss, low,
):
    feat, n = ft.shape
    ncls = o_lp.shape[0]
    o_lp[...] = lp[...].astype(F32)[:ncls]
    mm = m[...]
    f = ft[...]
    fix = dot(mm[:, :feat].astype(BF16), f) + mm[:, ONES : ONES + 1]
    tail = dt[0].astype(F32)
    for b in range(4):
        low[pl.ds(0, 4), pl.ds(b * (n // 4), n // 4)] = tail[4 * b : 4 * b + 4]
    gf = jnp.concatenate([d[0].astype(F32), low[...]], axis=0)[:feat] - fix[:feat]
    if STRIDED:
        flat = o_gf.reshape(feat * (n // 128), 128)
        for i in range(n // 128):
            flat[pl.ds(i, feat, stride=n // 128), :] = gf[:, i * 128 : (i + 1) * 128]
    else:
        for i in range(n // 128):
            o_gf[:, i, :] = gf[:, i * 128 : (i + 1) * 128]

    @pl.when(pl.program_id(0) == 0)
    def _():
        hid = mix.shape[1]
        o_mix[...] = mix[...].astype(F32)
        for i in range(hid // 128):
            o_gw[:, i, :] = gw[pl.ds(0, feat), pl.ds(i * 128, 128)]
        o_hg[...] = small[pl.ds(0, 1), :]
        o_hb[...] = small[pl.ds(1, 1), :]
        o_gg[...] = small[pl.ds(2, 1), :]
        o_gb[...] = small[pl.ds(3, 1), :]
        o_cw[...] = cw[pl.ds(0, ncls), :]
        o_cb[...] = small[pl.ds(4, 1), pl.ds(0, ncls)]
        o_loss[...] = jnp.sum(small[pl.ds(4, 1), pl.ds(128, 128)], axis=1, keepdims=True) * (-1.0 / nodes)


def shards(
    R, features, branch_weight, branch_gain, branch_bias, mix_weight, mixing_norm_gain, mixing_norm_bias,
    class_weight, class_bias, labels, hop_mask,
):
    local, feat = features.shape[1:]
    hid = mix_weight.shape[0]
    ncls = class_weight.shape[1]
    nodes = local * R
    sub = local // HOPS
    Z = R // 2
    half = hid // 2
    S = min(Z, 2)
    G2, qrows = Z // S, half // S
    zrows, zcols = chunk(0, 0, qrows, G2, hid)
    assert feat == ONES and ncls == 47 and local // hop_mask.shape[0] == 128
    ft = features[0].T
    sd = jax.ShapeDtypeStruct
    vm = pl.BlockSpec(memory_space=pltpu.VMEM)
    hbm = pl.BlockSpec(memory_space=pl.ANY)
    _, nsem = sem_plan(R)
    V = pltpu.VMEM
    outs = pl.pallas_call(
        functools.partial(main_kernel, R, nodes),
        grid=(1,),
        out_shape=(
            sd((48, local), BF16),
            sd((HOPS, MAIN, sub), BF16),
            sd((HOPS, 16, sub // 4), BF16),
            sd((FP, 128), F32),
            sd((hid, hid), BF16),
            sd((FP, hid), F32),
            sd((8, hid), F32),
            sd((48, hid), F32),
        ),
        in_specs=[hbm, pl.BlockSpec((16, local), lambda i: (MAIN // 16, 0))]
        + [vm] * 9
        + [pl.BlockSpec(memory_space=pltpu.SMEM)],
        out_specs=(hbm, hbm, hbm, vm, vm, vm, vm, vm),
        scratch_shapes=[
            V((128, local), BF16),
            V((HOPS, 128, sub), BF16),
            V((HOPS, 16, sub // 4), BF16),
            V((HOPS, 16, sub // 4), BF16),
            V((48, sub // 4), F32),
            V((HOPS, hid + 128, hid), BF16),
            V((HOPS, hid, 256), BF16),
            V((HOPS, FP, hid), BF16),
            V((HOPS, hid, hid), BF16),
            V((HOPS, 16, sub), BF16),
            V((HOPS, hid, sub), BF16),
            V((HOPS, hid, sub), BF16),
            V((hid, sub), F32),
            V((hid, sub), F32),
            V((hid, sub), BF16),
            V((128, 128), F32),
            V((64, 128), F32),
            V((Z, 64, 128), F32),
            V((2, 64, 128), F32),
            V((R, 1, 2 * hid), F32),
            V((HOPS, 1, 2 * hid), F32),
            V((HOPS, 1, 2 * hid), F32),
            V((R, 1, 2 * hid), F32),
            V((HOPS, 1, 2 * hid + 256), F32),
            V((R, 1, 2 * hid + 256), F32),
            V((HOPS, 48, hid // HOPS), BF16),
            V((HOPS, 48, hid // HOPS), BF16),
            V((R, 48, hid // HOPS), BF16),
            V((HOPS, 48, hid // HOPS), BF16),
            V((48, sub), BF16),
            V((128, hid), F32),
            V((hid, 128), BF16),
            V((8, 128), F32),
            V((hid, min(2 * TILE, sub)), BF16),
            V((128, min(2 * TILE, sub)), BF16),
            V((hid, 128), F32),
            V((hid, 128), F32),
            V((96, 128), F32),
            V((48, hid), F32),
            V((3, hid, 128), F32),
            V((HOPS, hid, hid), BF16),
            V((HOPS, half, hid), BF16),
            V((HOPS, qrows, hid), BF16),
            V((HOPS, qrows, hid), BF16),
            V((max(G2, 2), zrows.size, zcols.size), BF16),
            V((hid, hid), BF16),
            V((HOPS, MAIN, sub), BF16),
            V((8, sub), F32),
            V((HOPS, 16, sub // 4), BF16),
            V((hid, 128), F32),
            V((HOPS, FP, hid), BF16),
            V((HOPS, FP, half), BF16),
            V((HOPS, FP, half), BF16),
            V((HOPS, FP, half), BF16),
            V((HOPS, 1, 2 * hid), F32),
            V((HOPS, 1, 2 * hid), F32),
            V((R, 1, 2 * hid), F32),
            V((PROWS, half), BF16),
            V((Z, PROWS // Z if PROWS // Z >= 16 else PROWS, half), BF16),
            V((2, PROWS, half), BF16),
            pltpu.SemaphoreType.DMA((nsem,)),
            pltpu.SemaphoreType.DMA((nsem,)),
        ],
        compiler_params=pltpu.CompilerParams(
            collective_id=0, has_side_effects=True, vmem_limit_bytes=63 * 1024 * 1024
        ),
        cost_estimate=pl.CostEstimate(flops=2 * 8 * 10**9, bytes_accessed=10**7, transcendentals=10**7),
        name="main",
    )(
        ft, ft, branch_weight[0], branch_gain, branch_bias, mix_weight, mixing_norm_gain[None], mixing_norm_bias[None],
        class_weight.T, class_bias[None], labels[None], hop_mask.T,
    )
    lp, dd, dt, m, mix, gw, small, cw = outs
    nb = sub
    whole = lambda shape: pl.BlockSpec(shape, lambda i: (0,) * len(shape))
    lp, gf, mix, gw, gg, gb, hg, hb, cw, cb, loss = pl.pallas_call(
        functools.partial(last_kernel, nodes),
        grid=(local // nb,),
        out_shape=(
            sd((ncls, local), F32),
            sd((feat, local // 128, 128), F32),
            sd((hid, hid), F32),
            sd((feat, hid // 128, 128), F32),
            sd((1, hid), F32),
            sd((1, hid), F32),
            sd((1, hid), F32),
            sd((1, hid), F32),
            sd((ncls, hid), F32),
            sd((1, ncls), F32),
            sd((1, 1), F32),
        ),
        in_specs=[
            pl.BlockSpec((feat, nb), lambda i: (0, i)),
            pl.BlockSpec((1, MAIN, nb), lambda i: (i, 0, 0)),
            pl.BlockSpec((1, 16, nb // 4), lambda i: (i, 0, 0)),
            pl.BlockSpec((48, nb), lambda i: (0, i)),
            whole((FP, 128)),
            whole((hid, hid)),
            whole((FP, hid)),
            whole((8, hid)),
            whole((48, hid)),
        ],
        out_specs=(
            pl.BlockSpec((ncls, nb), lambda i: (0, i)),
            pl.BlockSpec((feat, nb // 128, 128), lambda i: (0, i, 0)),
            whole((hid, hid)),
            whole((feat, hid // 128, 128)),
            whole((1, hid)),
            whole((1, hid)),
            whole((1, hid)),
            whole((1, hid)),
            whole((ncls, hid)),
            whole((1, ncls)),
            whole((1, 1)),
        ),
        scratch_shapes=[V((8, nb), F32)],
        compiler_params=pltpu.CompilerParams(vmem_limit_bytes=60 * 1024 * 1024),
        name="last",
    )(ft, dd, dt, lp, m, mix, gw, small, cw)
    return (
        lp.T,
        loss[0, 0],
        with_layout_constraint(gf.reshape(feat, 1, local), Layout((0, 1, 2))).transpose(1, 2, 0),
        gw.reshape(1, feat, hid),
        gg,
        gb,
        mix,
        hg[0],
        hb[0],
        cw.T,
        cb[0],
    )


def solution(mesh):
    placed = (
        P("hop", "rows", None), P("hop", None, None), P("hop", None), P("hop", None), P("hop", None),
        P(), P(), P(), P(), P("rows"), P("rows", None),
    )
    assert mesh.shape["hop"] == HOPS
    return jax.shard_map(
        functools.partial(shards, mesh.shape["rows"]),
        mesh=mesh,
        in_specs=placed,
        out_specs=(
            P("rows", None), P(), P("hop", "rows", None), P("hop", None, None), P("hop", None), P("hop", None),
            P("hop", None), P(), P(), P(), P(),
        ),
        check_vma=False,
    )
```

```python
import functools
import math

import jax
import jax.numpy as jnp
from jax import lax
from jax.experimental import pallas as pl
from jax.experimental.layout import Layout, with_layout_constraint
from jax.experimental.pallas import tpu as pltpu
from jax.sharding import PartitionSpec as P

MESH = pl.DeviceIdType.MESH
EPS = 1e-05
HOPS = 4
ONES = 100
FP = 112
MAIN = 96
TILE = 256
STRIDED = True
C0 = math.sqrt(2.0 / math.pi)
C1 = C0 * 0.044715
KAPPA = C1 ** (1.0 / 3.0)
ALPHA = C0 / KAPPA
F32 = jnp.float32
BF16 = jnp.bfloat16


def dot(a, b):
    return lax.dot_general(a, b, (((1,), (0,)), ((), ())), preferred_element_type=F32)


def dot_nt(a, b):
    return lax.dot_general(a, b, (((1,), (1,)), ((), ())), preferred_element_type=F32)


def split2(x):
    hi = x.astype(BF16)
    return hi, (x - hi.astype(F32)).astype(BF16)


def split3(x):
    hi = x.astype(BF16)
    rest = x - hi.astype(F32)
    mid = rest.astype(BF16)
    return hi, mid, (rest - mid.astype(F32)).astype(BF16)


def scaled_gelu_slope(y):
    u = y * y
    t = jnp.tanh(y * (u + ALPHA))
    up = t + 1.0
    g = y * up
    return g, up + (g * (1.0 - t)) * (3.0 * u + ALPHA)


def fold(x):
    total = x[:, :128]
    for i in range(1, x.shape[1] // 128):
        total = total + x[:, i * 128 : (i + 1) * 128]
    return total


def spread(c, n):
    return jnp.concatenate([c] * (n // 128), axis=1)


def row_of(acc):
    return jnp.sum(acc.T, axis=0, keepdims=True)


def col_of(row):
    return jnp.broadcast_to(row, (128, row.shape[1])).T


def each(lo, hi, body):
    if hi - lo == 1:
        body(lo)
    elif hi > lo:
        pl.loop(lo, hi)(body)


class Alloc:
    def __init__(self):
        self.n = 0

    def __call__(self, count):
        base = self.n
        self.n += count
        return base


def sem_plan(R):
    Z = R // 2
    a = Alloc()
    names = {}
    for name, count in (
        ("feat", 7), ("ft", 4), ("loc", 1), ("ws", 4), ("zf", 4), ("dd", 4), ("s1", R), ("ab", 4), ("gp", 1), ("gz", Z), ("gd", 1),
        ("s2h", 4), ("s2r", R), ("s3h", 4), ("s3r", R), ("lp", 4), ("cwh", 4), ("cwr", R), ("cwg", 4),
        ("pair", 4), ("z1", 4), ("hop", 4), ("zr", Z), ("zg", Z), ("ddm", 1), ("d", 4), ("dt", 4), ("p", 4), ("q", 4),
        ("qr", R), ("pp", 4), ("pz", Z), ("pd", 1),
    ):
        names[name] = a(count)
    return names, a.n


def chunk(base, i, rows, pieces, cols):
    if rows // pieces >= 16:
        take = rows // pieces
        return pl.ds(pl.multiple_of(base + i * take, 16), take), pl.ds(0, cols)
    m = 16 * pieces // rows
    wide = cols // m
    return (
        pl.ds(pl.multiple_of(base + (i // m) * 16, 16), 16),
        pl.ds(pl.multiple_of((i % m) * wide, 128), wide),
    )


def main_kernel(
    R,
    nodes,
    ft, ft4, wb, bgain, bbias, wm, gain2, bias2, wc, cb, lab, msk,
    o_lp, o_d, o_dt, o_m, o_mix, o_gw, o_small, o_cw,
    fs, fx, ftail, frt, st4, wall, wl, aw, wmx, keep, mi, gp, mixed, dn2, dmx,
    gown, gpr, gz, gfin, s1, ab, s2h, s2r, s3h, s3r, cwp, cwh, cwr, cwg, lps,
    wcs, wcNs, cbs, hb, hs, dlp, acc0, acc1, accl, accw, cols,
    dmp, pr, z1r, hr, zr, fin, dsend, d4, dtail, pT, ps, ph, phalf, prv, qs, qv, qr, pz, pfin,
    ss, rs,
):
    names, _ = sem_plan(R)
    Z = R // 2
    h = lax.axis_index("hop")
    r = lax.axis_index("rows")
    c = lax.rem(r, 2)
    zi = lax.div(r, 2)
    sib = r + 1 - 2 * c
    local = ft.shape[1]
    sub = local // HOPS
    hid = wm.shape[0]
    half = hid // 2
    big = min(2 * TILE, sub)
    UN = big // TILE
    NT = sub // big
    inv_n = 1.0 / nodes

    def peer(d):
        x = lax.rem(h + d, 2)
        y = lax.rem(lax.div(h, 2) + lax.div(d, 2), 2)
        return 2 * y + x

    def rc(src, dst, name, i, hh, rr):
        return pltpu.make_async_remote_copy(
            src_ref=src, dst_ref=dst, send_sem=ss.at[names[name] + i], recv_sem=rs.at[names[name] + i],
            device_id=(hh, rr), device_id_type=MESH,
        )

    def done(cp):
        cp.wait_send()
        cp.wait_recv()

    def lanes_at(i, n):
        return pl.ds(pl.multiple_of(i * n, n), n)

    barrier = pltpu.get_barrier_semaphore()

    def greet(hh, rr):
        pl.semaphore_signal(barrier, inc=1, device_id=(hh, rr), device_id_type=MESH)

    @pl.loop(1, HOPS)
    def _(d):
        greet(peer(d), r)

    @functools.partial(each, 1, R)
    def _(e):
        greet(h, lax.rem(r + e, R))

    def rows_start(buf, name):
        @functools.partial(each, 1, R)
        def _(e):
            rc(buf.at[r], buf.at[r], name, e, h, lax.rem(r + e, R)).start()

    def rows_wait(buf, name):
        @functools.partial(each, 1, R)
        def _(e):
            src = lax.rem(r + R - e, R)
            done(rc(buf.at[src], buf.at[src], name, e, h, lax.rem(r + e, R)))

    def hops_start(buf, name):
        @pl.loop(1, HOPS)
        def _(d):
            rc(buf.at[h], buf.at[h], name, d, peer(d), r).start()

    def hops_wait(buf, name):
        @pl.loop(1, HOPS)
        def _(d):
            done(rc(buf.at[peer(d)], buf.at[peer(d)], name, d, peer(d), r))

    def total(buf, n, dtype=F32):
        return lax.fori_loop(1, n, lambda i, t: t + buf[i].astype(dtype), buf[0].astype(dtype))

    loc = pltpu.make_async_copy(ft.at[pl.ds(0, MAIN), :], fs.at[pl.ds(0, MAIN), :], ss.at[names["loc"]])
    loc.start()

    def pack4(src, dst):
        n = st4.shape[1]
        for b in range(4):
            st4[pl.ds(4 * b, 4), :] = src[pl.ds(0, 4), pl.ds(b * n, n)].astype(F32)
        dst[...] = st4[pl.ds(0, 16), :].astype(BF16)

    def unpack4(src, dst):
        n = st4.shape[1]
        row = lax.broadcasted_iota(jnp.int32, (32, n), 0)
        st4[pl.ds(0, 16), :] = src[...].astype(F32)
        st4[pl.ds(16, 32), :] = jnp.where(row == ONES - MAIN, 1.0, 0.0)
        for b in range(4):
            st4[pl.ds(16, 4), :] = st4[pl.ds(4 * b, 4), :]
            dst[pl.ds(MAIN, 32), pl.ds(b * n, n)] = st4[pl.ds(16, 32), :].astype(BF16)

    wrow = pl.ds(hid, 128)
    wall[0, pl.ds(hid + 96, 32), :] = jnp.zeros((32, hid), BF16)
    wall[0, pl.ds(hid, 100), :] = wb[...]

    @pl.loop(0, hid // 128)
    def _(i):
        k = lanes_at(i, 128)
        wall[0, pl.ds(0, hid), k] = wm[k, :].astype(F32).T.astype(BF16)

    def feat_copy(d):
        rows = pl.ds(0, MAIN)
        return rc(fs.at[rows, lanes_at(peer(d), sub)], fx.at[d, rows, :], "feat", d, peer(d), r)

    def feat_part(p):
        rows = pl.ds(0, MAIN)
        d = HOPS - 1
        return rc(
            fs.at[rows, lanes_at(NT * peer(d) + p, big)], fx.at[d, rows, lanes_at(p, big)], "feat", d + p, peer(d), r
        )

    def ft_copy(d):
        return rc(ftail.at[peer(d)], frt.at[d], "ft", d, peer(d), r)

    pl.semaphore_wait(barrier, HOPS - 1 + R - 1)

    S = min(Z, 2)
    part = (hid + 128) // (2 * S)
    zpar = lax.rem(zi, S)
    zmate = zi + (S - 1) - 2 * (S - 1) * zpar

    def part_rows(core, par):
        return pl.ds(pl.multiple_of((core * S + par) * part, 16), part)

    def ws_copy(d):
        rows = part_rows(c, zpar)
        return rc(wall.at[0, rows, :], wall.at[d, rows, :], "ws", d, peer(d), r)

    def zf_copy(d, par):
        ref = wall.at[d, part_rows(c, par), :]
        return rc(ref, ref, "zf", d, h, 2 * zmate + c)

    def dd_copy(d, core):
        ref = wall.at[d, pl.ds(pl.multiple_of(core * S * part, 16), S * part), :]
        return rc(ref, ref, "dd", d, h, sib)

    first, second = 1 + c, 2 - c
    ws_copy(first).start()
    ws_copy(second).start()
    ws_copy(HOPS - 1).start()
    loc.wait()
    feat_copy(first).start()
    feat_copy(second).start()

    @pl.loop(0, HOPS)
    def _(j):
        lanes = lanes_at(j, sub)
        pack4(ft4.at[:, lanes], ftail.at[j])
        unpack4(ftail.at[j], fs.at[:, lanes])


    @pl.loop(1, HOPS)
    def _(d):
        ft_copy(d).start()

    fx0 = pltpu.make_async_copy(fs.at[:, lanes_at(h, sub)], fx.at[0], ss.at[names["loc"]])
    fx0.start()

    def gram(i, g):
        f = fs[:, lanes_at(i, sub)]
        return g + dot_nt(f, f)

    g = lax.fori_loop(0, HOPS, gram, jnp.zeros((128, 128), F32))
    wown = wall[0, wrow, :]
    wown32 = wown.astype(F32)
    g1, g2, g3 = split3(g)
    gw = dot(g1, wown) + dot(g2, wown) + dot(g3, wown)
    s1[r, :, pl.ds(0, hid)] = gw[ONES : ONES + 1, :]
    s1[r, :, pl.ds(hid, hid)] = jnp.sum(gw * wown32, axis=0, keepdims=True)
    rows_start(s1, "s1")
    gown[...] = g

    @pl.loop(0, HOPS * (sub // 128))
    def _(i):
        d = lax.div(i, sub // 128)
        b = lax.rem(i, sub // 128)
        late = peer(d) - 2
        m = jnp.where(late >= 0, msk[jnp.maximum(late, 0), h * (sub // 128) + b], 1)
        keep[d, :, lanes_at(b, 128)] = jnp.full((16, 128), 0.5 * m.astype(F32)).astype(BF16)

    wcs[...] = jnp.zeros(wcs.shape, F32)
    wcs[pl.ds(0, wc.shape[0]), :] = wc[...].astype(F32)
    cbs[...] = jnp.zeros(cbs.shape, F32)
    cbs[pl.ds(0, 1), pl.ds(0, cb.shape[1])] = cb[...]
    ncls = wc.shape[0]

    @pl.loop(0, hid // 16)
    def _(i):
        rows = lanes_at(i, 16)
        mixed[rows, :] = jnp.zeros((16, sub), F32)
        mi[0, rows, pl.ds(0, big)] = jnp.zeros((16, big), BF16)

    fx0.wait()

    rows_wait(s1, "s1")
    st = total(s1, R)
    mean = st[:, :hid] * inv_n
    var = st[:, hid:] * inv_n - mean * mean
    inv = lax.rsqrt(var + EPS)
    scale = inv * bgain[...]
    ab[0, :, pl.ds(0, hid)] = scale
    ab[0, :, pl.ds(hid, hid)] = bbias[...] - mean * scale

    def ab_copy(d):
        return rc(ab.at[0], ab.at[d], "ab", d, peer(d), r)

    @pl.loop(1, HOPS)
    def _(d):
        ab_copy(d).start()

    def prepare(d):
        a = ab[d, :, pl.ds(0, hid)]
        b = ab[d, :, pl.ds(hid, hid)]
        ws = wall[d, wrow, :].astype(F32) * (a * KAPPA)
        aw[d] = ws[:FP].astype(BF16)
        row = lax.broadcasted_iota(jnp.int32, (128, hid), 0)
        wt = jnp.where(row == ONES, b * KAPPA, ws).T
        hi, lo = split2(wt)
        wl[d, :, pl.ds(0, 128)] = hi
        wl[d, :, pl.ds(128, 128)] = lo

    g_pair = rc(gown.at[lanes_at(1 - c, 64), :], gpr, "gp", 0, h, sib)

    def gz_copy(e, which):
        return rc(gz.at[which], gz.at[which], "gz", e, h, lax.rem(zi + e, Z) * 2 + c)

    def gd_copy(core):
        return rc(gfin.at[core], gfin.at[core], "gd", 0, h, sib)

    acc0[...] = jnp.zeros(acc0.shape, F32)
    acc1[...] = jnp.zeros(acc1.shape, F32)

    def block_sums(t):
        @pl.loop(0, hid // 64)
        def _(i):
            rows = lanes_at(i, 64)
            x = mixed[rows, lanes_at(t, big)]
            acc0[rows, :] += fold(x)
            acc1[rows, :] += fold(x * x)

    @pl.loop(0, HOPS * NT)
    def _(it):
        d = lax.div(it, NT)
        t = lax.rem(it, NT)

        @pl.when(t == 0)
        def _():
            @pl.when(d > 0)
            def _():
                @pl.when(d < HOPS - 1)
                def _():
                    done(feat_copy(d))

                done(ft_copy(d))
                unpack4(frt.at[d], fx.at[d])
                dd_copy(d, c).wait_send()
                dd_copy(d, 1 - c).wait_recv()
                done(ab_copy(d))

            prepare(d)

        if S > 1:

            @pl.when(it == min(1, NT - 1))
            def _():
                @pl.loop(1, HOPS)
                def _(j):
                    done(ws_copy(j))

                zf_copy(1, zpar).start()

        @pl.when(it == min(2, NT - 1))
        def _():
            @pl.loop(0, NT)
            def _(p):
                feat_part(p).start()

        @pl.when(jnp.logical_and(t == NT - 1, d < HOPS - 1))
        def _():
            if S > 1:
                zf_copy(d + 1, zpar).wait_send()
                zf_copy(d + 1, 1 - zpar).wait_recv()

                @pl.when(d < HOPS - 2)
                def _():
                    zf_copy(d + 2, zpar).start()

            else:
                done(ws_copy(d + 1))
            dd_copy(d + 1, c).start()

        @pl.when(it == 2 * NT)
        def _():
            g_pair.start()

        @pl.when(it == 3 * NT)
        def _():
            done(g_pair)
            gz[zi] = gown[lanes_at(c, 64), :] + gpr[...]

            @functools.partial(each, 1, Z)
            def _(e):
                gz_copy(e, zi).start()

        @pl.when(d == HOPS - 1)
        def _():
            done(feat_part(t))

        pit = jnp.maximum(it - 1, 0)
        pd = lax.div(pit, NT)
        pt = lax.rem(pit, NT)
        adds = []
        for u in range(UN):
            adds.append(dot(wall[pd, pl.ds(0, hid), :], mi[pd, :, lanes_at(pt * UN + u, TILE)]))
        for u in range(UN):
            n = lanes_at(t * UN + u, TILE)
            f = fx[d, :, n]
            z = dot(wl[d], jnp.concatenate([f, f], axis=0))
            k = keep[d, :, n]
            k = jnp.concatenate([k] * 4, axis=0)
            for i in range(0, hid, 64):
                g1, d1 = scaled_gelu_slope(z[i : i + 64].astype(BF16))
                g2, d2 = scaled_gelu_slope(g1 * k)
                mi[d, pl.ds(i, 64), n] = g2
                gp[d, pl.ds(i, 64), n] = d1 * d2 * k
        for u in range(UN):
            n = lanes_at(pt * UN + u, TILE)
            mixed[:, n] = mixed[:, n] + adds[u]

        @pl.when(jnp.logical_and(pd == HOPS - 1, it > pit))
        def _():
            block_sums(pt)


    @pl.loop(0, UN)
    def _(u):
        n = lanes_at((NT - 1) * UN + u, TILE)
        mixed[:, n] = mixed[:, n] + dot(wall[HOPS - 1, pl.ds(0, hid), :], mi[HOPS - 1, :, n])

    block_sums(NT - 1)

    def natural(lo, hi):
        @pl.loop(lo * (hid // 128), hi * (hid // 128))
        def _(i):
            d = lax.div(i, hid // 128)
            k = lanes_at(lax.rem(i, hid // 128), 128)
            wmx[d, k, :] = wall[d, pl.ds(0, hid), k].astype(F32).T.astype(BF16)

    s2h[h, :, pl.ds(0, hid)] = row_of(acc0[...])
    s2h[h, :, pl.ds(hid, hid)] = row_of(acc1[...])
    hops_start(s2h, "s2h")
    natural(0, 2)
    hops_wait(s2h, "s2h")
    s2r[r] = total(s2h, HOPS)
    rows_start(s2r, "s2r")
    natural(2, HOPS)
    wc48 = wcs[pl.ds(0, 48), :].astype(BF16)
    wcNs[...] = wcs[...].T.astype(BF16)
    crow = lax.broadcasted_iota(jnp.int32, (128, 128), 0)
    cbc = jnp.where(crow < ncls, jnp.broadcast_to(cbs[pl.ds(0, 1), :], (128, 128)).T, -1e30)[:48]
    rows_wait(s2r, "s2r")
    st2 = total(s2r, R)
    mean2 = st2[:, :hid] * inv_n
    inv2 = lax.rsqrt(st2[:, hid:] * inv_n - mean2 * mean2 + EPS * 4.0 * KAPPA * KAPPA)
    scale2 = inv2 * gain2[...]
    cols[0] = col_of(scale2 * KAPPA)
    cols[1] = col_of((bias2[...] - mean2 * scale2) * KAPPA)
    acc0[...] = jnp.zeros(acc0.shape, F32)
    acc1[...] = jnp.zeros(acc1.shape, F32)
    accl[...] = jnp.zeros(accl.shape, F32)
    accw[...] = jnp.zeros(accw.shape, F32)

    o_own = lanes_at(h, sub)

    def lp_copy(d):
        return rc(lps, o_lp.at[:, o_own], "lp", d, peer(d), r)

    dlp[...] = jnp.zeros(dlp.shape, BF16)
    HR = 128

    @pl.loop(0, NT)
    def _(t):
        n = lanes_at(t, big)

        @pl.loop(0, hid // HR)
        def _(i):
            rows = lanes_at(i, HR)
            y2 = mixed[rows, n] * spread(cols[0, rows, :], big) + spread(cols[1, rows, :], big)
            gv, dg = scaled_gelu_slope(y2.astype(BF16))
            hb[rows, :] = (gv.astype(F32) * (0.5 / KAPPA)).astype(BF16)
            hs[rows, :] = dg

        lg = dot(wc48, hb[...]) + spread(cbc, big)
        lg = lg - jnp.max(lg, axis=0, keepdims=True)
        ex = jnp.exp(lg)
        se = jnp.sum(ex, axis=0, keepdims=True)
        lp = lg - jnp.log(se)
        lps[:, n] = lp.astype(BF16)
        own = lanes_at(h * NT + t, big)
        hit = lax.broadcasted_iota(jnp.int32, (48, big), 0) == lab[:, own]
        accl[pl.ds(48, 48), :] += fold(jnp.where(hit, lp, 0.0))
        dl = ((ex / se - jnp.where(hit, 1.0, 0.0)) * inv_n).astype(BF16)
        accl[pl.ds(0, 48), :] += fold(dl.astype(F32))
        accw[...] += dot_nt(dl, hb[...])
        dlp[pl.ds(0, 48), :] = dl * 0.5

        @pl.loop(0, hid // HR)
        def _(i):
            rows = lanes_at(i, HR)
            dn = dot(wcNs[rows, :], dlp[...]) * hs[rows, :].astype(F32)
            dn2[rows, n] = dn
            acc0[rows, :] += fold(dn * mixed[rows, n])
            acc1[rows, :] += fold(dn)

    own_lp = pltpu.make_async_copy(lps, o_lp.at[:, o_own], ss.at[names["lp"]])
    own_lp.start()
    s3h[h, :, pl.ds(0, hid)] = row_of(acc0[...])
    s3h[h, :, pl.ds(hid, hid)] = row_of(acc1[...])
    zpad = jnp.zeros((80, 128), F32)
    s3h[h, :, pl.ds(2 * hid, 128)] = row_of(jnp.concatenate([accl[pl.ds(0, 48), :], zpad], axis=0))
    s3h[h, :, pl.ds(2 * hid + 128, 128)] = row_of(jnp.concatenate([accl[pl.ds(48, 48), :], zpad], axis=0))
    hops_start(s3h, "s3h")

    def cwh_copy(d):
        return rc(cwp.at[d], cwh.at[d], "cwh", d, peer(d), r)

    q = hid // HOPS

    @pl.loop(0, HOPS)
    def _(d):
        cwp[d] = accw[:, lanes_at(peer(d), q)].astype(BF16)

    hops_wait(s3h, "s3h")
    s3r[r] = total(s3h, HOPS)
    rows_start(s3r, "s3r")

    @pl.loop(1, HOPS)
    def _(d):
        cwh_copy(d).start()

    lp_copy(first).start()
    lp_copy(second).start()
    lp_copy(HOPS - 1).start()
    rows_wait(s3r, "s3r")
    st3 = total(s3r, R)
    db2 = st3[:, hid : 2 * hid]
    dg2t = inv2 * (st3[:, :hid] - mean2 * db2)
    o_small[pl.ds(0, 1), :] = dg2t
    o_small[pl.ds(1, 1), :] = db2
    o_small[pl.ds(4, 1), pl.ds(0, 256)] = st3[:, 2 * hid : 2 * hid + 256]
    o_small[pl.ds(4, 1), pl.ds(256, hid - 256)] = jnp.zeros((1, hid - 256), F32)
    t2 = scale2 * inv2 * dg2t * inv_n
    cols[0] = col_of(scale2)
    cols[1] = col_of(-t2)
    cols[2] = col_of(t2 * mean2 - scale2 * db2 * inv_n)

    @pl.loop(0, hid // 16)
    def _(i):
        rows = lanes_at(i, 16)
        v = dn2[rows, :] * spread(cols[0, rows, :], sub)
        v = v + mixed[rows, :] * spread(cols[1, rows, :], sub) + spread(cols[2, rows, :], sub)
        dmx[rows, :] = v.astype(BF16)

    @functools.partial(each, 1, Z)
    def _(e):
        gz_copy(e, zi).wait_send()
        gz_copy(e, lax.rem(zi + Z - e, Z)).wait_recv()

    gfin[c] = total(gz, Z)
    gd_copy(c).start()

    mine = lanes_at(c, half)
    theirs = lanes_at(1 - c, half)

    def pair_copy(d):
        return rc(dmp.at[d, theirs, :], pr.at[d], "pair", d, h, sib)

    qrows = half // S
    zown = pl.ds(pl.multiple_of(c * half + zpar * qrows, 16), qrows)
    zother = pl.ds(pl.multiple_of(c * half + (1 - zpar) * qrows, 16), qrows)

    def z1_copy(d):
        return rc(dmp.at[d, zother, :], z1r.at[d], "z1", d, h, 2 * zmate + c)

    def z1_start(d):
        if S > 1:
            z1_copy(d).start()

    def z1_sum(d):
        if S > 1:
            done(z1_copy(d))

            @pl.loop(0, qrows // 32)
            def _(i):
                rows = pl.ds(pl.multiple_of(c * half + zpar * qrows + i * 32, 32), 32)
                dmp[d, rows, :] = (dmp[d, rows, :].astype(F32) + z1r[d, lanes_at(i, 32), :].astype(F32)).astype(BF16)

    def hop_copy(d):
        return rc(dmp.at[d, zown, :], hr.at[d], "hop", d, peer(d), r)

    def pair_sum(d):
        done(pair_copy(d))

        @pl.loop(0, half // 32)
        def _(i):
            rows = pl.ds(pl.multiple_of(c * half + i * 32, 32), 32)
            dmp[d, rows, :] = (dmp[d, rows, :].astype(F32) + pr[d, lanes_at(i, 32), :].astype(F32)).astype(BF16)

    def mix_grad(d):
        dmp[d] = dot_nt(mi[d], dmx[...]).astype(BF16)
        pair_copy(d).start()

    def mix_grads(lo):
        @pl.loop(0, 2)
        def _(i):
            mix_grad(lo + 1 - i)

        pair_sum(lo + 1)
        z1_start(lo + 1)

    def mix_hop(d):
        z1_sum(d)
        hop_copy(d).start()

    mix_grads(2)

    G2 = Z // S
    zq = lax.div(zi, S)

    def zr_copy(e, which):
        rows, lanes = chunk(0, which, qrows, G2, hid)
        return rc(hr.at[0, rows, lanes], zr.at[e], "zr", e, h, (lax.rem(zq + e, G2) * S + zpar) * 2 + c)

    def final_chunk(z):
        return chunk(c * half + lax.rem(z, S) * qrows, lax.div(z, S), qrows, G2, hid)

    def zg_copy(e, which):
        rows, lanes = final_chunk(which)
        ref = fin.at[rows, lanes]
        return rc(ref, ref, "zg", e, h, lax.rem(zi + e, Z) * 2 + c)

    def ddm_copy(core):
        ref = fin.at[lanes_at(core, half), :]
        return rc(ref, ref, "ddm", 0, h, sib)

    def d_copy(d):
        return rc(dsend.at[d], o_d.at[h], "d", d, peer(d), r)

    def dt_copy(d):
        return rc(dtail.at[d], o_dt.at[h], "dt", d, peer(d), r)

    def pp_copy(d):
        return rc(ps.at[d, :, theirs], ph.at[d], "pp", d, h, sib)

    def p_copy(d):
        return rc(phalf.at[d], prv.at[d], "p", d, peer(d), r)

    def p_half(d):
        done(pp_copy(d))
        phalf[d] = (ps[d, :, mine].astype(F32) + ph[d].astype(F32)).astype(BF16)

    def q_copy(d):
        return rc(qs.at[d], qv.at[d], "q", d, peer(d), r)

    @pl.loop(0, HOPS * NT)
    def _(it):
        dd = lax.div(it, NT)
        t = lax.rem(it, NT)
        d = HOPS - 1 - dd

        @pl.when(t == 0)
        def _():
            pT[...] = jnp.zeros(pT.shape, F32)

        @pl.when(jnp.logical_and(t == NT // 2, dd > 0))
        def _():
            p_half(d + 1)
            p_copy(d + 1).start()

            @pl.when(dd > 1)
            def _():
                dt_copy(d + 1).start()
                d_copy(d + 1).start()


        @pl.when(it == NT // 2)
        def _():
            pair_sum(2)
            z1_start(2)

        @pl.when(it == NT + NT // 2)
        def _():
            @pl.loop(1, HOPS)
            def _(j):
                done(cwh_copy(j))

            cw = cwp[0].astype(F32)
            for j in range(1, HOPS):
                cw = cw + cwh[j].astype(F32)
            cwr[r] = cw.astype(BF16)
            rows_start(cwr, "cwr")
            pair_sum(0)
            z1_start(0)
            mix_hop(2)

        @pl.when(it == 2 * NT + NT // 2)
        def _():
            mix_hop(1)
            rows_wait(cwr, "cwr")
            cwg[h] = total(cwr, R, F32).astype(BF16)
            hops_start(cwg, "cwg")

        @pl.when(it == 3 * NT + NT // 2)
        def _():
            z1_sum(0)

            @pl.loop(1, HOPS)
            def _(j):
                done(hop_copy(j))

            @pl.loop(0, qrows // 32)
            def _(i):
                rows = lanes_at(i, 32)
                own = pl.ds(pl.multiple_of(c * half + zpar * qrows + i * 32, 32), 32)
                hsum = dmp[0, own, :].astype(F32)
                for j in range(1, HOPS):
                    hsum = hsum + hr[j, rows, :].astype(F32)
                hr[0, rows, :] = hsum.astype(BF16)

            @functools.partial(each, 1, G2)
            def _(e):
                zr_copy(e, lax.rem(zq + e, G2)).start()

            hops_wait(cwg, "cwg")
            for j in range(HOPS):
                o_cw[:, pl.ds(j * q, q)] = cwg[j].astype(F32)

        @pl.when(it == HOPS * NT - 1)
        def _():
            @functools.partial(each, 1, G2)
            def _(e):
                done(zr_copy(e, lax.rem(zq + e, G2)))

            rows, lanes = chunk(0, zq, qrows, G2, hid)
            zt = lax.fori_loop(1, G2, lambda e, v: v + zr[e].astype(F32), hr[0, rows, lanes].astype(F32))
            frows, flanes = final_chunk(zi)
            fin[frows, flanes] = zt.astype(BF16)

            @functools.partial(each, 1, Z)
            def _(e):
                zg_copy(e, zi).start()

        n = lanes_at(t, big)
        dn = dot(wmx[d], dmx[:, n]).astype(BF16) * gp[d, :, n]
        pT[...] += dot_nt(dn, fx[d, :, n])
        grad = dot(aw[d], dn)
        dsend[d, :, n] = grad[:MAIN].astype(BF16)
        d4[:, n] = grad[MAIN : MAIN + 8]

        @pl.when(t == NT - 1)
        def _():
            pw = pT[...].T * KAPPA
            qs[d, :, pl.ds(0, hid)] = jnp.sum(pw * wall[d, wrow, :].astype(F32), axis=0, keepdims=True)
            qs[d, :, pl.ds(hid, hid)] = pw[ONES : ONES + 1, :]
            ps[d] = pw[:FP].astype(BF16)
            pp_copy(d).start()
            pack4(d4, dtail.at[d])

            @pl.when(dd < HOPS - 1)
            def _():
                q_copy(d).start()

            @pl.when(dd == 0)
            def _():
                dt_copy(d).start()
                d_copy(d).start()
                mix_hop(d)
                mix_grads(0)

    @pl.loop(1, HOPS)
    def _(d):
        done(q_copy(d))

    qr[r] = qs[0] + (qv[1] + qv[2] + qv[3])
    rows_start(qr, "qr")
    own_d = pltpu.make_async_copy(dsend.at[0], o_d.at[h], ss.at[names["d"]])
    own_d.start()
    own_dt = pltpu.make_async_copy(dtail.at[0], o_dt.at[h], ss.at[names["dt"]])
    own_dt.start()

    p_half(0)

    @pl.loop(1, HOPS)
    def _(d):
        done(p_copy(d))

    psum = phalf[0].astype(F32) + (prv[1].astype(F32) + prv[2].astype(F32) + prv[3].astype(F32))
    pz[zi] = psum.astype(BF16)

    def pz_copy(e, which):
        return rc(pz.at[which], pz.at[which], "pz", e, h, lax.rem(zi + e, Z) * 2 + c)

    @functools.partial(each, 1, Z)
    def _(e):
        pz_copy(e, zi).start()

    @functools.partial(each, 1, Z)
    def _(e):
        zg_copy(e, zi).wait_send()
        zg_copy(e, lax.rem(zi + Z - e, Z)).wait_recv()

    ddm_copy(c).start()

    rows_wait(qr, "qr")
    qt = total(qr, R)
    db = qt[:, hid:]
    dgn = inv * (qt[:, :hid] - mean * db)
    o_small[pl.ds(2, 1), :] = dgn
    o_small[pl.ds(3, 1), :] = db
    c1 = scale * db * inv_n
    c2 = inv * scale * dgn * inv_n
    shift = c1 - mean * c2
    row = lax.broadcasted_iota(jnp.int32, (128, hid), 0)
    q1, q2 = split2(jnp.where(row == ONES, shift, wown32 * c2))
    o_m[...] = (dot_nt(wown, q1) + dot_nt(wown, q2))[:FP]
    gd_copy(c).wait_send()
    gd_copy(1 - c).wait_recv()
    g1, g2, g3 = split3(jnp.concatenate([gfin[0], gfin[1]], axis=0))
    gq = dot(g1, q1) + dot(g2, q1) + dot(g3, q1) + dot(g1, q2) + dot(g2, q2)

    @functools.partial(each, 1, Z)
    def _(e):
        pz_copy(e, zi).wait_send()
        pz_copy(e, lax.rem(zi + Z - e, Z)).wait_recv()

    pfin[c] = total(pz, Z).astype(BF16)

    def pd_copy(core):
        return rc(pfin.at[core], pfin.at[core], "pd", 0, h, sib)

    pd_copy(c).start()
    ddm_copy(c).wait_send()
    ddm_copy(1 - c).wait_recv()
    o_mix[...] = fin[...]

    pd_copy(c).wait_send()
    pd_copy(1 - c).wait_recv()
    ptot = jnp.concatenate([pfin[0], pfin[1]], axis=1).astype(F32)
    o_gw[...] = ptot * scale - gq[:FP]
    own_d.wait()
    own_dt.wait()
    own_lp.wait()

    @pl.loop(1, HOPS)
    def _(d):
        done(d_copy(d))
        done(dt_copy(d))
        done(lp_copy(d))


def last_kernel(
    nodes,
    ft, d, dt, lp, m, mix, gw, small, cw,
    o_lp, o_gf, o_mix, o_gw, o_gg, o_gb, o_hg, o_hb, o_cw, o_cb, o_loss, low,
):
    feat, n = ft.shape
    ncls = o_lp.shape[0]
    o_lp[...] = lp[...].astype(F32)[:ncls]
    mm = m[...]
    f = ft[...]
    fix = dot(mm[:, :feat].astype(BF16), f) + mm[:, ONES : ONES + 1]
    tail = dt[0].astype(F32)
    for b in range(4):
        low[pl.ds(0, 4), pl.ds(b * (n // 4), n // 4)] = tail[4 * b : 4 * b + 4]
    gf = jnp.concatenate([d[0].astype(F32), low[...]], axis=0)[:feat] - fix[:feat]
    if STRIDED:
        flat = o_gf.reshape(feat * (n // 128), 128)
        for i in range(n // 128):
            flat[pl.ds(i, feat, stride=n // 128), :] = gf[:, i * 128 : (i + 1) * 128]
    else:
        for i in range(n // 128):
            o_gf[:, i, :] = gf[:, i * 128 : (i + 1) * 128]

    @pl.when(pl.program_id(0) == 0)
    def _():
        hid = mix.shape[1]
        o_mix[...] = mix[...].astype(F32)
        for i in range(hid // 128):
            o_gw[:, i, :] = gw[pl.ds(0, feat), pl.ds(i * 128, 128)]
        o_hg[...] = small[pl.ds(0, 1), :]
        o_hb[...] = small[pl.ds(1, 1), :]
        o_gg[...] = small[pl.ds(2, 1), :]
        o_gb[...] = small[pl.ds(3, 1), :]
        o_cw[...] = cw[pl.ds(0, ncls), :]
        o_cb[...] = small[pl.ds(4, 1), pl.ds(0, ncls)]
        o_loss[...] = jnp.sum(small[pl.ds(4, 1), pl.ds(128, 128)], axis=1, keepdims=True) * (-1.0 / nodes)


def shards(
    R, features, branch_weight, branch_gain, branch_bias, mix_weight, mixing_norm_gain, mixing_norm_bias,
    class_weight, class_bias, labels, hop_mask,
):
    local, feat = features.shape[1:]
    hid = mix_weight.shape[0]
    ncls = class_weight.shape[1]
    nodes = local * R
    sub = local // HOPS
    Z = R // 2
    half = hid // 2
    S = min(Z, 2)
    G2, qrows = Z // S, half // S
    zrows, zcols = chunk(0, 0, qrows, G2, hid)
    assert feat == ONES and ncls == 47 and local // hop_mask.shape[0] == 128
    ft = features[0].T
    sd = jax.ShapeDtypeStruct
    vm = pl.BlockSpec(memory_space=pltpu.VMEM)
    hbm = pl.BlockSpec(memory_space=pl.ANY)
    _, nsem = sem_plan(R)
    V = pltpu.VMEM
    outs = pl.pallas_call(
        functools.partial(main_kernel, R, nodes),
        grid=(1,),
        out_shape=(
            sd((48, local), BF16),
            sd((HOPS, MAIN, sub), BF16),
            sd((HOPS, 16, sub // 4), BF16),
            sd((FP, 128), F32),
            sd((hid, hid), BF16),
            sd((FP, hid), F32),
            sd((8, hid), F32),
            sd((48, hid), F32),
        ),
        in_specs=[hbm, pl.BlockSpec((16, local), lambda i: (MAIN // 16, 0))]
        + [vm] * 9
        + [pl.BlockSpec(memory_space=pltpu.SMEM)],
        out_specs=(hbm, hbm, hbm, vm, vm, vm, vm, vm),
        scratch_shapes=[
            V((128, local), BF16),
            V((HOPS, 128, sub), BF16),
            V((HOPS, 16, sub // 4), BF16),
            V((HOPS, 16, sub // 4), BF16),
            V((48, sub // 4), F32),
            V((HOPS, hid + 128, hid), BF16),
            V((HOPS, hid, 256), BF16),
            V((HOPS, FP, hid), BF16),
            V((HOPS, hid, hid), BF16),
            V((HOPS, 16, sub), BF16),
            V((HOPS, hid, sub), BF16),
            V((HOPS, hid, sub), BF16),
            V((hid, sub), F32),
            V((hid, sub), F32),
            V((hid, sub), BF16),
            V((128, 128), F32),
            V((64, 128), F32),
            V((Z, 64, 128), F32),
            V((2, 64, 128), F32),
            V((R, 1, 2 * hid), F32),
            V((HOPS, 1, 2 * hid), F32),
            V((HOPS, 1, 2 * hid), F32),
            V((R, 1, 2 * hid), F32),
            V((HOPS, 1, 2 * hid + 256), F32),
            V((R, 1, 2 * hid + 256), F32),
            V((HOPS, 48, hid // HOPS), BF16),
            V((HOPS, 48, hid // HOPS), BF16),
            V((R, 48, hid // HOPS), BF16),
            V((HOPS, 48, hid // HOPS), BF16),
            V((48, sub), BF16),
            V((128, hid), F32),
            V((hid, 128), BF16),
            V((8, 128), F32),
            V((hid, min(2 * TILE, sub)), BF16),
            V((hid, min(2 * TILE, sub)), BF16),
            V((128, min(2 * TILE, sub)), BF16),
            V((hid, 128), F32),
            V((hid, 128), F32),
            V((96, 128), F32),
            V((48, hid), F32),
            V((3, hid, 128), F32),
            V((HOPS, hid, hid), BF16),
            V((HOPS, half, hid), BF16),
            V((HOPS, qrows, hid), BF16),
            V((HOPS, qrows, hid), BF16),
            V((max(G2, 2), zrows.size, zcols.size), BF16),
            V((hid, hid), BF16),
            V((HOPS, MAIN, sub), BF16),
            V((8, sub), F32),
            V((HOPS, 16, sub // 4), BF16),
            V((hid, 128), F32),
            V((HOPS, FP, hid), BF16),
            V((HOPS, FP, half), BF16),
            V((HOPS, FP, half), BF16),
            V((HOPS, FP, half), BF16),
            V((HOPS, 1, 2 * hid), F32),
            V((HOPS, 1, 2 * hid), F32),
            V((R, 1, 2 * hid), F32),
            V((Z, FP, half), BF16),
            V((2, FP, half), BF16),
            pltpu.SemaphoreType.DMA((nsem,)),
            pltpu.SemaphoreType.DMA((nsem,)),
        ],
        compiler_params=pltpu.CompilerParams(
            collective_id=0, has_side_effects=True, vmem_limit_bytes=63 * 1024 * 1024
        ),
        cost_estimate=pl.CostEstimate(flops=2 * 8 * 10**9, bytes_accessed=10**7, transcendentals=10**7),
        name="main",
    )(
        ft, ft, branch_weight[0], branch_gain, branch_bias, mix_weight, mixing_norm_gain[None], mixing_norm_bias[None],
        class_weight.T, class_bias[None], labels[None], hop_mask.T,
    )
    lp, dd, dt, m, mix, gw, small, cw = outs
    nb = sub
    whole = lambda shape: pl.BlockSpec(shape, lambda i: (0,) * len(shape))
    lp, gf, mix, gw, gg, gb, hg, hb, cw, cb, loss = pl.pallas_call(
        functools.partial(last_kernel, nodes),
        grid=(local // nb,),
        out_shape=(
            sd((ncls, local), F32),
            sd((feat, local // 128, 128), F32),
            sd((hid, hid), F32),
            sd((feat, hid // 128, 128), F32),
            sd((1, hid), F32),
            sd((1, hid), F32),
            sd((1, hid), F32),
            sd((1, hid), F32),
            sd((ncls, hid), F32),
            sd((1, ncls), F32),
            sd((1, 1), F32),
        ),
        in_specs=[
            pl.BlockSpec((feat, nb), lambda i: (0, i)),
            pl.BlockSpec((1, MAIN, nb), lambda i: (i, 0, 0)),
            pl.BlockSpec((1, 16, nb // 4), lambda i: (i, 0, 0)),
            pl.BlockSpec((48, nb), lambda i: (0, i)),
            whole((FP, 128)),
            whole((hid, hid)),
            whole((FP, hid)),
            whole((8, hid)),
            whole((48, hid)),
        ],
        out_specs=(
            pl.BlockSpec((ncls, nb), lambda i: (0, i)),
            pl.BlockSpec((feat, nb // 128, 128), lambda i: (0, i, 0)),
            whole((hid, hid)),
            whole((feat, hid // 128, 128)),
            whole((1, hid)),
            whole((1, hid)),
            whole((1, hid)),
            whole((1, hid)),
            whole((ncls, hid)),
            whole((1, ncls)),
            whole((1, 1)),
        ),
        scratch_shapes=[V((8, nb), F32)],
        compiler_params=pltpu.CompilerParams(vmem_limit_bytes=60 * 1024 * 1024),
        name="last",
    )(ft, dd, dt, lp, m, mix, gw, small, cw)
    return (
        lp.T,
        loss[0, 0],
        with_layout_constraint(gf.reshape(feat, 1, local), Layout((0, 1, 2))).transpose(1, 2, 0),
        gw.reshape(1, feat, hid),
        gg,
        gb,
        mix,
        hg[0],
        hb[0],
        cw.T,
        cb[0],
    )


def solution(mesh):
    placed = (
        P("hop", "rows", None), P("hop", None, None), P("hop", None), P("hop", None), P("hop", None),
        P(), P(), P(), P(), P("rows"), P("rows", None),
    )
    assert mesh.shape["hop"] == HOPS
    return jax.shard_map(
        functools.partial(shards, mesh.shape["rows"]),
        mesh=mesh,
        in_specs=placed,
        out_specs=(
            P("rows", None), P(), P("hop", "rows", None), P("hop", None, None), P("hop", None), P("hop", None),
            P("hop", None), P(), P(), P(), P(),
        ),
        check_vma=False,
    )
```

```python
import functools
import math

import jax
import jax.numpy as jnp
from jax import lax
from jax.experimental import pallas as pl
from jax.experimental.layout import Layout, with_layout_constraint
from jax.experimental.pallas import tpu as pltpu
from jax.sharding import PartitionSpec as P

MESH = pl.DeviceIdType.MESH
EPS = 1e-05
HOPS = 4
ONES = 100
FP = 112
MAIN = 96
TILE = 256
STRIDED = True
C0 = math.sqrt(2.0 / math.pi)
C1 = C0 * 0.044715
KAPPA = C1 ** (1.0 / 3.0)
ALPHA = C0 / KAPPA
F32 = jnp.float32
BF16 = jnp.bfloat16


def dot(a, b):
    return lax.dot_general(a, b, (((1,), (0,)), ((), ())), preferred_element_type=F32)


def dot_nt(a, b):
    return lax.dot_general(a, b, (((1,), (1,)), ((), ())), preferred_element_type=F32)


def split2(x):
    hi = x.astype(BF16)
    return hi, (x - hi.astype(F32)).astype(BF16)


def split3(x):
    hi = x.astype(BF16)
    rest = x - hi.astype(F32)
    mid = rest.astype(BF16)
    return hi, mid, (rest - mid.astype(F32)).astype(BF16)


def scaled_gelu_slope(y):
    u = y * y
    t = jnp.tanh(y * (u + ALPHA))
    up = t + 1.0
    g = y * up
    return g, up + (g * (1.0 - t)) * (3.0 * u + ALPHA)


def fold(x):
    total = x[:, :128]
    for i in range(1, x.shape[1] // 128):
        total = total + x[:, i * 128 : (i + 1) * 128]
    return total


def spread(c, n):
    return jnp.concatenate([c] * (n // 128), axis=1)


def row_of(acc):
    return jnp.sum(acc.T, axis=0, keepdims=True)


def col_of(row):
    return jnp.broadcast_to(row, (128, row.shape[1])).T


def each(lo, hi, body):
    if hi - lo == 1:
        body(lo)
    elif hi > lo:
        pl.loop(lo, hi)(body)


class Alloc:
    def __init__(self):
        self.n = 0

    def __call__(self, count):
        base = self.n
        self.n += count
        return base


def sem_plan(R):
    Z = R // 2
    a = Alloc()
    names = {}
    for name, count in (
        ("feat", 7), ("ft", 4), ("loc", 1), ("ws", 4), ("zf", 4), ("dd", 4), ("s1", R), ("ab", 4), ("gp", 1), ("gz", Z), ("gd", 1),
        ("s2h", 4), ("s2r", R), ("s3h", 4), ("s3r", R), ("lp", 4), ("cwh", 4), ("cwr", R), ("cwg", 4),
        ("pair", 4), ("z1", 4), ("hop", 4), ("hopb", 4), ("zr", Z), ("zrb", Z), ("zg", Z), ("zgb", Z), ("ddm", 1), ("d", 4), ("dt", 4), ("p", 4), ("q", 4),
        ("qr", R), ("pp", 4), ("pz", Z), ("pd", 1),
    ):
        names[name] = a(count)
    return names, a.n


def chunk(base, i, rows, pieces, cols):
    if rows // pieces >= 16:
        take = rows // pieces
        return pl.ds(pl.multiple_of(base + i * take, 16), take), pl.ds(0, cols)
    m = 16 * pieces // rows
    wide = cols // m
    return (
        pl.ds(pl.multiple_of(base + (i // m) * 16, 16), 16),
        pl.ds(pl.multiple_of((i % m) * wide, 128), wide),
    )


def main_kernel(
    R,
    nodes,
    ft, ft4, wb, bgain, bbias, wm, gain2, bias2, wc, cb, lab, msk,
    o_lp, o_d, o_dt, o_m, o_mix, o_gw, o_small, o_cw,
    fs, fx, ftail, frt, st4, wall, wl, aw, wmx, keep, mi, gp, mixed, dn2, dmx,
    gown, gpr, gz, gfin, s1, ab, s2h, s2r, s3h, s3r, cwp, cwh, cwr, cwg, lps,
    wcs, wcNs, cbs, hb, hs, dlp, acc0, acc1, accl, accw, cols,
    dmp, pr, z1r, hr, hrb, zr, zrb, fin, dsend, d4, dtail, pT, ps, ph, phalf, prv, qs, qv, qr, pz, pfin,
    ss, rs,
):
    names, _ = sem_plan(R)
    Z = R // 2
    h = lax.axis_index("hop")
    r = lax.axis_index("rows")
    c = lax.rem(r, 2)
    zi = lax.div(r, 2)
    sib = r + 1 - 2 * c
    local = ft.shape[1]
    sub = local // HOPS
    hid = wm.shape[0]
    half = hid // 2
    big = min(2 * TILE, sub)
    UN = big // TILE
    NT = sub // big
    inv_n = 1.0 / nodes

    def peer(d):
        x = lax.rem(h + d, 2)
        y = lax.rem(lax.div(h, 2) + lax.div(d, 2), 2)
        return 2 * y + x

    def rc(src, dst, name, i, hh, rr):
        return pltpu.make_async_remote_copy(
            src_ref=src, dst_ref=dst, send_sem=ss.at[names[name] + i], recv_sem=rs.at[names[name] + i],
            device_id=(hh, rr), device_id_type=MESH,
        )

    def done(cp):
        cp.wait_send()
        cp.wait_recv()

    def lanes_at(i, n):
        return pl.ds(pl.multiple_of(i * n, n), n)

    barrier = pltpu.get_barrier_semaphore()

    def greet(hh, rr):
        pl.semaphore_signal(barrier, inc=1, device_id=(hh, rr), device_id_type=MESH)

    @pl.loop(1, HOPS)
    def _(d):
        greet(peer(d), r)

    @functools.partial(each, 1, R)
    def _(e):
        greet(h, lax.rem(r + e, R))

    def rows_start(buf, name):
        @functools.partial(each, 1, R)
        def _(e):
            rc(buf.at[r], buf.at[r], name, e, h, lax.rem(r + e, R)).start()

    def rows_wait(buf, name):
        @functools.partial(each, 1, R)
        def _(e):
            src = lax.rem(r + R - e, R)
            done(rc(buf.at[src], buf.at[src], name, e, h, lax.rem(r + e, R)))

    def hops_start(buf, name):
        @pl.loop(1, HOPS)
        def _(d):
            rc(buf.at[h], buf.at[h], name, d, peer(d), r).start()

    def hops_wait(buf, name):
        @pl.loop(1, HOPS)
        def _(d):
            done(rc(buf.at[peer(d)], buf.at[peer(d)], name, d, peer(d), r))

    def total(buf, n, dtype=F32):
        return lax.fori_loop(1, n, lambda i, t: t + buf[i].astype(dtype), buf[0].astype(dtype))

    loc = pltpu.make_async_copy(ft.at[pl.ds(0, MAIN), :], fs.at[pl.ds(0, MAIN), :], ss.at[names["loc"]])
    loc.start()

    def pack4(src, dst):
        n = st4.shape[1]
        for b in range(4):
            st4[pl.ds(4 * b, 4), :] = src[pl.ds(0, 4), pl.ds(b * n, n)].astype(F32)
        dst[...] = st4[pl.ds(0, 16), :].astype(BF16)

    def unpack4(src, dst):
        n = st4.shape[1]
        row = lax.broadcasted_iota(jnp.int32, (32, n), 0)
        st4[pl.ds(0, 16), :] = src[...].astype(F32)
        st4[pl.ds(16, 32), :] = jnp.where(row == ONES - MAIN, 1.0, 0.0)
        for b in range(4):
            st4[pl.ds(16, 4), :] = st4[pl.ds(4 * b, 4), :]
            dst[pl.ds(MAIN, 32), pl.ds(b * n, n)] = st4[pl.ds(16, 32), :].astype(BF16)

    wrow = pl.ds(hid, 128)
    wall[0, pl.ds(hid + 96, 32), :] = jnp.zeros((32, hid), BF16)
    wall[0, pl.ds(hid, 100), :] = wb[...]

    @pl.loop(0, hid // 128)
    def _(i):
        k = lanes_at(i, 128)
        wall[0, pl.ds(0, hid), k] = wm[k, :].astype(F32).T.astype(BF16)

    def feat_copy(d):
        rows = pl.ds(0, MAIN)
        return rc(fs.at[rows, lanes_at(peer(d), sub)], fx.at[d, rows, :], "feat", d, peer(d), r)

    def feat_part(p):
        rows = pl.ds(0, MAIN)
        d = HOPS - 1
        return rc(
            fs.at[rows, lanes_at(NT * peer(d) + p, big)], fx.at[d, rows, lanes_at(p, big)], "feat", d + p, peer(d), r
        )

    def ft_copy(d):
        return rc(ftail.at[peer(d)], frt.at[d], "ft", d, peer(d), r)

    pl.semaphore_wait(barrier, HOPS - 1 + R - 1)

    S = min(Z, 2)
    part = (hid + 128) // (2 * S)
    zpar = lax.rem(zi, S)
    zmate = zi + (S - 1) - 2 * (S - 1) * zpar

    def part_rows(core, par):
        return pl.ds(pl.multiple_of((core * S + par) * part, 16), part)

    def ws_copy(d):
        rows = part_rows(c, zpar)
        return rc(wall.at[0, rows, :], wall.at[d, rows, :], "ws", d, peer(d), r)

    def zf_copy(d, par):
        ref = wall.at[d, part_rows(c, par), :]
        return rc(ref, ref, "zf", d, h, 2 * zmate + c)

    def dd_copy(d, core):
        ref = wall.at[d, pl.ds(pl.multiple_of(core * S * part, 16), S * part), :]
        return rc(ref, ref, "dd", d, h, sib)

    first, second = 1 + c, 2 - c
    ws_copy(first).start()
    ws_copy(second).start()
    ws_copy(HOPS - 1).start()
    loc.wait()
    feat_copy(first).start()
    feat_copy(second).start()

    @pl.loop(0, HOPS)
    def _(j):
        lanes = lanes_at(j, sub)
        pack4(ft4.at[:, lanes], ftail.at[j])
        unpack4(ftail.at[j], fs.at[:, lanes])


    @pl.loop(1, HOPS)
    def _(d):
        ft_copy(d).start()

    fx0 = pltpu.make_async_copy(fs.at[:, lanes_at(h, sub)], fx.at[0], ss.at[names["loc"]])
    fx0.start()

    def gram(i, g):
        f = fs[:, lanes_at(i, sub)]
        return g + dot_nt(f, f)

    g = lax.fori_loop(0, HOPS, gram, jnp.zeros((128, 128), F32))
    wown = wall[0, wrow, :]
    wown32 = wown.astype(F32)
    g1, g2, g3 = split3(g)
    gw = dot(g1, wown) + dot(g2, wown) + dot(g3, wown)
    s1[r, :, pl.ds(0, hid)] = gw[ONES : ONES + 1, :]
    s1[r, :, pl.ds(hid, hid)] = jnp.sum(gw * wown32, axis=0, keepdims=True)
    rows_start(s1, "s1")
    gown[...] = g

    @pl.loop(0, HOPS * (sub // 128))
    def _(i):
        d = lax.div(i, sub // 128)
        b = lax.rem(i, sub // 128)
        late = peer(d) - 2
        m = jnp.where(late >= 0, msk[jnp.maximum(late, 0), h * (sub // 128) + b], 1)
        keep[d, :, lanes_at(b, 128)] = jnp.full((16, 128), 0.5 * m.astype(F32)).astype(BF16)

    wcs[...] = jnp.zeros(wcs.shape, F32)
    wcs[pl.ds(0, wc.shape[0]), :] = wc[...].astype(F32)
    cbs[...] = jnp.zeros(cbs.shape, F32)
    cbs[pl.ds(0, 1), pl.ds(0, cb.shape[1])] = cb[...]
    ncls = wc.shape[0]

    @pl.loop(0, hid // 16)
    def _(i):
        rows = lanes_at(i, 16)
        mixed[rows, :] = jnp.zeros((16, sub), F32)
        mi[0, rows, pl.ds(0, big)] = jnp.zeros((16, big), BF16)

    fx0.wait()

    rows_wait(s1, "s1")
    st = total(s1, R)
    mean = st[:, :hid] * inv_n
    var = st[:, hid:] * inv_n - mean * mean
    inv = lax.rsqrt(var + EPS)
    scale = inv * bgain[...]
    ab[0, :, pl.ds(0, hid)] = scale
    ab[0, :, pl.ds(hid, hid)] = bbias[...] - mean * scale

    def ab_copy(d):
        return rc(ab.at[0], ab.at[d], "ab", d, peer(d), r)

    @pl.loop(1, HOPS)
    def _(d):
        ab_copy(d).start()

    def prepare(d):
        a = ab[d, :, pl.ds(0, hid)]
        b = ab[d, :, pl.ds(hid, hid)]
        ws = wall[d, wrow, :].astype(F32) * (a * KAPPA)
        aw[d] = ws[:FP].astype(BF16)
        row = lax.broadcasted_iota(jnp.int32, (128, hid), 0)
        wt = jnp.where(row == ONES, b * KAPPA, ws).T
        hi, lo = split2(wt)
        wl[d, :, pl.ds(0, 128)] = hi
        wl[d, :, pl.ds(128, 128)] = lo

    g_pair = rc(gown.at[lanes_at(1 - c, 64), :], gpr, "gp", 0, h, sib)

    def gz_copy(e, which):
        return rc(gz.at[which], gz.at[which], "gz", e, h, lax.rem(zi + e, Z) * 2 + c)

    def gd_copy(core):
        return rc(gfin.at[core], gfin.at[core], "gd", 0, h, sib)

    acc0[...] = jnp.zeros(acc0.shape, F32)
    acc1[...] = jnp.zeros(acc1.shape, F32)

    def block_sums(t):
        @pl.loop(0, hid // 64)
        def _(i):
            rows = lanes_at(i, 64)
            x = mixed[rows, lanes_at(t, big)]
            acc0[rows, :] += fold(x)
            acc1[rows, :] += fold(x * x)

    @pl.loop(0, HOPS * NT)
    def _(it):
        d = lax.div(it, NT)
        t = lax.rem(it, NT)

        @pl.when(t == 0)
        def _():
            @pl.when(d > 0)
            def _():
                @pl.when(d < HOPS - 1)
                def _():
                    done(feat_copy(d))

                done(ft_copy(d))
                unpack4(frt.at[d], fx.at[d])
                dd_copy(d, c).wait_send()
                dd_copy(d, 1 - c).wait_recv()
                done(ab_copy(d))

            prepare(d)

        if S > 1:

            @pl.when(it == min(1, NT - 1))
            def _():
                @pl.loop(1, HOPS)
                def _(j):
                    done(ws_copy(j))

                zf_copy(1, zpar).start()

        @pl.when(it == min(2, NT - 1))
        def _():
            @pl.loop(0, NT)
            def _(p):
                feat_part(p).start()

        @pl.when(jnp.logical_and(t == NT - 1, d < HOPS - 1))
        def _():
            if S > 1:
                zf_copy(d + 1, zpar).wait_send()
                zf_copy(d + 1, 1 - zpar).wait_recv()

                @pl.when(d < HOPS - 2)
                def _():
                    zf_copy(d + 2, zpar).start()

            else:
                done(ws_copy(d + 1))
            dd_copy(d + 1, c).start()

        @pl.when(it == 2 * NT)
        def _():
            g_pair.start()

        @pl.when(it == 3 * NT)
        def _():
            done(g_pair)
            gz[zi] = gown[lanes_at(c, 64), :] + gpr[...]

            @functools.partial(each, 1, Z)
            def _(e):
                gz_copy(e, zi).start()

        @pl.when(d == HOPS - 1)
        def _():
            done(feat_part(t))

        pit = jnp.maximum(it - 1, 0)
        pd = lax.div(pit, NT)
        pt = lax.rem(pit, NT)
        adds = []
        for u in range(UN):
            adds.append(dot(wall[pd, pl.ds(0, hid), :], mi[pd, :, lanes_at(pt * UN + u, TILE)]))
        for u in range(UN):
            n = lanes_at(t * UN + u, TILE)
            f = fx[d, :, n]
            z = dot(wl[d], jnp.concatenate([f, f], axis=0))
            k = keep[d, :, n]
            k = jnp.concatenate([k] * 4, axis=0)
            for i in range(0, hid, 64):
                g1, d1 = scaled_gelu_slope(z[i : i + 64].astype(BF16))
                g2, d2 = scaled_gelu_slope(g1 * k)
                mi[d, pl.ds(i, 64), n] = g2
                gp[d, pl.ds(i, 64), n] = d1 * d2 * k
        for u in range(UN):
            n = lanes_at(pt * UN + u, TILE)
            mixed[:, n] = mixed[:, n] + adds[u]

        @pl.when(jnp.logical_and(pd == HOPS - 1, it > pit))
        def _():
            block_sums(pt)


    @pl.loop(0, UN)
    def _(u):
        n = lanes_at((NT - 1) * UN + u, TILE)
        mixed[:, n] = mixed[:, n] + dot(wall[HOPS - 1, pl.ds(0, hid), :], mi[HOPS - 1, :, n])

    block_sums(NT - 1)

    def natural(lo, hi):
        @pl.loop(lo * (hid // 128), hi * (hid // 128))
        def _(i):
            d = lax.div(i, hid // 128)
            k = lanes_at(lax.rem(i, hid // 128), 128)
            wmx[d, k, :] = wall[d, pl.ds(0, hid), k].astype(F32).T.astype(BF16)

    s2h[h, :, pl.ds(0, hid)] = row_of(acc0[...])
    s2h[h, :, pl.ds(hid, hid)] = row_of(acc1[...])
    hops_start(s2h, "s2h")
    natural(0, 2)
    hops_wait(s2h, "s2h")
    s2r[r] = total(s2h, HOPS)
    rows_start(s2r, "s2r")
    natural(2, HOPS)
    wc48 = wcs[pl.ds(0, 48), :].astype(BF16)
    wcNs[...] = wcs[...].T.astype(BF16)
    crow = lax.broadcasted_iota(jnp.int32, (128, 128), 0)
    cbc = jnp.where(crow < ncls, jnp.broadcast_to(cbs[pl.ds(0, 1), :], (128, 128)).T, -1e30)[:48]
    rows_wait(s2r, "s2r")
    st2 = total(s2r, R)
    mean2 = st2[:, :hid] * inv_n
    inv2 = lax.rsqrt(st2[:, hid:] * inv_n - mean2 * mean2 + EPS * 4.0 * KAPPA * KAPPA)
    scale2 = inv2 * gain2[...]
    cols[0] = col_of(scale2 * KAPPA)
    cols[1] = col_of((bias2[...] - mean2 * scale2) * KAPPA)
    acc0[...] = jnp.zeros(acc0.shape, F32)
    acc1[...] = jnp.zeros(acc1.shape, F32)
    accl[...] = jnp.zeros(accl.shape, F32)
    accw[...] = jnp.zeros(accw.shape, F32)

    o_own = lanes_at(h, sub)

    def lp_copy(d):
        return rc(lps, o_lp.at[:, o_own], "lp", d, peer(d), r)

    dlp[...] = jnp.zeros(dlp.shape, BF16)
    HR = 128

    @pl.loop(0, NT)
    def _(t):
        n = lanes_at(t, big)

        @pl.loop(0, hid // HR)
        def _(i):
            rows = lanes_at(i, HR)
            y2 = mixed[rows, n] * spread(cols[0, rows, :], big) + spread(cols[1, rows, :], big)
            gv, dg = scaled_gelu_slope(y2.astype(BF16))
            hb[rows, :] = (gv.astype(F32) * (0.5 / KAPPA)).astype(BF16)
            hs[rows, :] = dg

        lg = dot(wc48, hb[...]) + spread(cbc, big)
        lg = lg - jnp.max(lg, axis=0, keepdims=True)
        ex = jnp.exp(lg)
        se = jnp.sum(ex, axis=0, keepdims=True)
        lp = lg - jnp.log(se)
        lps[:, n] = lp.astype(BF16)
        own = lanes_at(h * NT + t, big)
        hit = lax.broadcasted_iota(jnp.int32, (48, big), 0) == lab[:, own]
        accl[pl.ds(48, 48), :] += fold(jnp.where(hit, lp, 0.0))
        dl = ((ex / se - jnp.where(hit, 1.0, 0.0)) * inv_n).astype(BF16)
        accl[pl.ds(0, 48), :] += fold(dl.astype(F32))
        accw[...] += dot_nt(dl, hb[...])
        dlp[pl.ds(0, 48), :] = dl * 0.5

        @pl.loop(0, hid // HR)
        def _(i):
            rows = lanes_at(i, HR)
            dn = dot(wcNs[rows, :], dlp[...]) * hs[rows, :].astype(F32)
            dn2[rows, n] = dn
            acc0[rows, :] += fold(dn * mixed[rows, n])
            acc1[rows, :] += fold(dn)

    own_lp = pltpu.make_async_copy(lps, o_lp.at[:, o_own], ss.at[names["lp"]])
    own_lp.start()
    s3h[h, :, pl.ds(0, hid)] = row_of(acc0[...])
    s3h[h, :, pl.ds(hid, hid)] = row_of(acc1[...])
    zpad = jnp.zeros((80, 128), F32)
    s3h[h, :, pl.ds(2 * hid, 128)] = row_of(jnp.concatenate([accl[pl.ds(0, 48), :], zpad], axis=0))
    s3h[h, :, pl.ds(2 * hid + 128, 128)] = row_of(jnp.concatenate([accl[pl.ds(48, 48), :], zpad], axis=0))
    hops_start(s3h, "s3h")

    def cwh_copy(d):
        return rc(cwp.at[d], cwh.at[d], "cwh", d, peer(d), r)

    q = hid // HOPS

    @pl.loop(0, HOPS)
    def _(d):
        cwp[d] = accw[:, lanes_at(peer(d), q)].astype(BF16)

    hops_wait(s3h, "s3h")
    s3r[r] = total(s3h, HOPS)
    rows_start(s3r, "s3r")

    @pl.loop(1, HOPS)
    def _(d):
        cwh_copy(d).start()

    lp_copy(first).start()
    lp_copy(second).start()
    lp_copy(HOPS - 1).start()
    rows_wait(s3r, "s3r")
    st3 = total(s3r, R)
    db2 = st3[:, hid : 2 * hid]
    dg2t = inv2 * (st3[:, :hid] - mean2 * db2)
    o_small[pl.ds(0, 1), :] = dg2t
    o_small[pl.ds(1, 1), :] = db2
    o_small[pl.ds(4, 1), pl.ds(0, 256)] = st3[:, 2 * hid : 2 * hid + 256]
    o_small[pl.ds(4, 1), pl.ds(256, hid - 256)] = jnp.zeros((1, hid - 256), F32)
    t2 = scale2 * inv2 * dg2t * inv_n
    cols[0] = col_of(scale2)
    cols[1] = col_of(-t2)
    cols[2] = col_of(t2 * mean2 - scale2 * db2 * inv_n)

    @pl.loop(0, hid // 16)
    def _(i):
        rows = lanes_at(i, 16)
        v = dn2[rows, :] * spread(cols[0, rows, :], sub)
        v = v + mixed[rows, :] * spread(cols[1, rows, :], sub) + spread(cols[2, rows, :], sub)
        dmx[rows, :] = v.astype(BF16)

    @functools.partial(each, 1, Z)
    def _(e):
        gz_copy(e, zi).wait_send()
        gz_copy(e, lax.rem(zi + Z - e, Z)).wait_recv()

    gfin[c] = total(gz, Z)
    gd_copy(c).start()

    mine = lanes_at(c, half)
    theirs = lanes_at(1 - c, half)

    def pair_copy(d):
        return rc(dmp.at[d, theirs, :], pr.at[d], "pair", d, h, sib)

    S = min(Z, 2)
    zpar = lax.rem(zi, S)
    zmate = zi + (S - 1) - 2 * (S - 1) * zpar
    ha = half // 2
    qrows = ha // S
    a0 = c * half
    b0 = c * half + ha
    zown = pl.ds(pl.multiple_of(a0 + zpar * qrows, 16), qrows)
    zother = pl.ds(pl.multiple_of(a0 + (1 - zpar) * qrows, 16), qrows)
    brows = pl.ds(pl.multiple_of(b0, 16), ha)

    def z1_copy(d):
        return rc(dmp.at[d, zother, :], z1r.at[d], "z1", d, h, 2 * zmate + c)

    def z1_sum(d):
        if S > 1:
            done(z1_copy(d))

            @pl.loop(0, qrows // 32)
            def _(i):
                rows = pl.ds(pl.multiple_of(a0 + zpar * qrows + i * 32, 32), 32)
                dmp[d, rows, :] = (dmp[d, rows, :].astype(F32) + z1r[d, lanes_at(i, 32), :].astype(F32)).astype(BF16)

    def hop_copy(d):
        return rc(dmp.at[d, zown, :], hr.at[d], "hop", d, peer(d), r)

    def hopb_copy(d):
        return rc(dmp.at[d, brows, :], hrb.at[d], "hopb", d, peer(d), r)

    def z1_start(d):
        if S > 1:
            z1_copy(d).start()
        if not isinstance(d, int) or d > 0:
            hopb_copy(d).start()

    def hop_sum(base, rows_of, buf, copy):
        @pl.loop(1, HOPS)
        def _(j):
            done(copy(j))

        @pl.loop(0, rows_of // 32)
        def _(i):
            rows = lanes_at(i, 32)
            hsum = dmp[0, pl.ds(pl.multiple_of(base + i * 32, 32), 32), :].astype(F32)
            for j in range(1, HOPS):
                hsum = hsum + buf[j, rows, :].astype(F32)
            buf[0, rows, :] = hsum.astype(BF16)

    def pair_sum(d):
        done(pair_copy(d))

        @pl.loop(0, half // 32)
        def _(i):
            rows = pl.ds(pl.multiple_of(c * half + i * 32, 32), 32)
            dmp[d, rows, :] = (dmp[d, rows, :].astype(F32) + pr[d, lanes_at(i, 32), :].astype(F32)).astype(BF16)

    def mix_grad(d):
        dmp[d] = dot_nt(mi[d], dmx[...]).astype(BF16)
        pair_copy(d).start()

    def mix_grads(lo):
        @pl.loop(0, 2)
        def _(i):
            mix_grad(lo + 1 - i)

        pair_sum(lo + 1)
        z1_start(lo + 1)

    def mix_hop(d):
        z1_sum(d)
        hop_copy(d).start()

    mix_grads(2)

    G2 = Z // S
    zq = lax.div(zi, S)

    def zrb_copy(e, which):
        rows, lanes = chunk(0, which, ha, Z, hid)
        return rc(hrb.at[0, rows, lanes], zrb.at[e], "zrb", e, h, lax.rem(zi + e, Z) * 2 + c)

    def zr_copy(e, which):
        rows, lanes = chunk(0, which, qrows, G2, hid)
        return rc(hr.at[0, rows, lanes], zr.at[e], "zr", e, h, (lax.rem(zq + e, G2) * S + zpar) * 2 + c)

    def final_chunk(z):
        return chunk(a0 + lax.rem(z, S) * qrows, lax.div(z, S), qrows, G2, hid)

    def zgb_copy(e, which):
        rows, lanes = chunk(b0, which, ha, Z, hid)
        ref = fin.at[rows, lanes]
        return rc(ref, ref, "zgb", e, h, lax.rem(zi + e, Z) * 2 + c)

    def zg_copy(e, which):
        rows, lanes = final_chunk(which)
        ref = fin.at[rows, lanes]
        return rc(ref, ref, "zg", e, h, lax.rem(zi + e, Z) * 2 + c)

    def ddm_copy(core):
        ref = fin.at[lanes_at(core, half), :]
        return rc(ref, ref, "ddm", 0, h, sib)

    def d_copy(d):
        return rc(dsend.at[d], o_d.at[h], "d", d, peer(d), r)

    def dt_copy(d):
        return rc(dtail.at[d], o_dt.at[h], "dt", d, peer(d), r)

    def pp_copy(d):
        return rc(ps.at[d, :, theirs], ph.at[d], "pp", d, h, sib)

    def p_copy(d):
        return rc(phalf.at[d], prv.at[d], "p", d, peer(d), r)

    def p_half(d):
        done(pp_copy(d))
        phalf[d] = (ps[d, :, mine].astype(F32) + ph[d].astype(F32)).astype(BF16)

    def q_copy(d):
        return rc(qs.at[d], qv.at[d], "q", d, peer(d), r)

    @pl.loop(0, HOPS * NT)
    def _(it):
        dd = lax.div(it, NT)
        t = lax.rem(it, NT)
        d = HOPS - 1 - dd

        @pl.when(t == 0)
        def _():
            pT[...] = jnp.zeros(pT.shape, F32)

        @pl.when(jnp.logical_and(t == NT // 2, dd > 0))
        def _():
            p_half(d + 1)
            p_copy(d + 1).start()

            @pl.when(dd > 1)
            def _():
                dt_copy(d + 1).start()
                d_copy(d + 1).start()


        @pl.when(it == NT // 2)
        def _():
            pair_sum(2)
            z1_start(2)

        @pl.when(it == NT + NT // 2)
        def _():
            @pl.loop(1, HOPS)
            def _(j):
                done(cwh_copy(j))

            cw = cwp[0].astype(F32)
            for j in range(1, HOPS):
                cw = cw + cwh[j].astype(F32)
            cwr[r] = cw.astype(BF16)
            rows_start(cwr, "cwr")
            pair_sum(0)
            z1_start(0)
            mix_hop(2)

        @pl.when(it == 2 * NT + NT // 2)
        def _():
            mix_hop(1)
            rows_wait(cwr, "cwr")
            cwg[h] = total(cwr, R, F32).astype(BF16)
            hops_start(cwg, "cwg")

        @pl.when(it == 3 * NT + NT // 2)
        def _():
            hop_sum(b0, ha, hrb, hopb_copy)

            @functools.partial(each, 1, Z)
            def _(e):
                zrb_copy(e, lax.rem(zi + e, Z)).start()

            z1_sum(0)
            hop_sum(a0 + zpar * qrows, qrows, hr, hop_copy)

            @functools.partial(each, 1, G2)
            def _(e):
                zr_copy(e, lax.rem(zq + e, G2)).start()

            hops_wait(cwg, "cwg")
            for j in range(HOPS):
                o_cw[:, pl.ds(j * q, q)] = cwg[j].astype(F32)

        n = lanes_at(t, big)
        dn = dot(wmx[d], dmx[:, n]).astype(BF16) * gp[d, :, n]
        pT[...] += dot_nt(dn, fx[d, :, n])
        grad = dot(aw[d], dn)
        dsend[d, :, n] = grad[:MAIN].astype(BF16)
        d4[:, n] = grad[MAIN : MAIN + 8]

        @pl.when(t == NT - 1)
        def _():
            pw = pT[...].T * KAPPA
            qs[d, :, pl.ds(0, hid)] = jnp.sum(pw * wall[d, wrow, :].astype(F32), axis=0, keepdims=True)
            qs[d, :, pl.ds(hid, hid)] = pw[ONES : ONES + 1, :]
            ps[d] = pw[:FP].astype(BF16)
            pp_copy(d).start()
            pack4(d4, dtail.at[d])

            @pl.when(dd < HOPS - 1)
            def _():
                q_copy(d).start()

            @pl.when(dd == 0)
            def _():
                mix_hop(d)
                mix_grads(0)
                dt_copy(d).start()
                d_copy(d).start()

    @pl.loop(1, HOPS)
    def _(d):
        done(q_copy(d))

    qr[r] = qs[0] + (qv[1] + qv[2] + qv[3])
    rows_start(qr, "qr")
    own_d = pltpu.make_async_copy(dsend.at[0], o_d.at[h], ss.at[names["d"]])
    own_d.start()
    own_dt = pltpu.make_async_copy(dtail.at[0], o_dt.at[h], ss.at[names["dt"]])
    own_dt.start()

    @functools.partial(each, 1, Z)
    def _(e):
        done(zrb_copy(e, lax.rem(zi + e, Z)))

    rows, lanes = chunk(0, zi, ha, Z, hid)
    zt = lax.fori_loop(1, Z, lambda e, v: v + zrb[e].astype(F32), hrb[0, rows, lanes].astype(F32))
    frows, flanes = chunk(b0, zi, ha, Z, hid)
    fin[frows, flanes] = zt.astype(BF16)

    @functools.partial(each, 1, Z)
    def _(e):
        zgb_copy(e, zi).start()

    @functools.partial(each, 1, G2)
    def _(e):
        done(zr_copy(e, lax.rem(zq + e, G2)))

    rows, lanes = chunk(0, zq, qrows, G2, hid)
    zt = lax.fori_loop(1, G2, lambda e, v: v + zr[e].astype(F32), hr[0, rows, lanes].astype(F32))
    frows, flanes = final_chunk(zi)
    fin[frows, flanes] = zt.astype(BF16)

    @functools.partial(each, 1, Z)
    def _(e):
        zg_copy(e, zi).start()

    p_half(0)

    @pl.loop(1, HOPS)
    def _(d):
        done(p_copy(d))

    psum = phalf[0].astype(F32) + (prv[1].astype(F32) + prv[2].astype(F32) + prv[3].astype(F32))
    pz[zi] = psum.astype(BF16)

    def pz_copy(e, which):
        return rc(pz.at[which], pz.at[which], "pz", e, h, lax.rem(zi + e, Z) * 2 + c)

    @functools.partial(each, 1, Z)
    def _(e):
        pz_copy(e, zi).start()

    @functools.partial(each, 1, Z)
    def _(e):
        zg_copy(e, zi).wait_send()
        zg_copy(e, lax.rem(zi + Z - e, Z)).wait_recv()
        zgb_copy(e, zi).wait_send()
        zgb_copy(e, lax.rem(zi + Z - e, Z)).wait_recv()

    ddm_copy(c).start()

    rows_wait(qr, "qr")
    qt = total(qr, R)
    db = qt[:, hid:]
    dgn = inv * (qt[:, :hid] - mean * db)
    o_small[pl.ds(2, 1), :] = dgn
    o_small[pl.ds(3, 1), :] = db
    c1 = scale * db * inv_n
    c2 = inv * scale * dgn * inv_n
    shift = c1 - mean * c2
    row = lax.broadcasted_iota(jnp.int32, (128, hid), 0)
    q1, q2 = split2(jnp.where(row == ONES, shift, wown32 * c2))
    o_m[...] = (dot_nt(wown, q1) + dot_nt(wown, q2))[:FP]
    gd_copy(c).wait_send()
    gd_copy(1 - c).wait_recv()
    g1, g2, g3 = split3(jnp.concatenate([gfin[0], gfin[1]], axis=0))
    gq = dot(g1, q1) + dot(g2, q1) + dot(g3, q1) + dot(g1, q2) + dot(g2, q2)

    @functools.partial(each, 1, Z)
    def _(e):
        pz_copy(e, zi).wait_send()
        pz_copy(e, lax.rem(zi + Z - e, Z)).wait_recv()

    pfin[c] = total(pz, Z).astype(BF16)

    def pd_copy(core):
        return rc(pfin.at[core], pfin.at[core], "pd", 0, h, sib)

    pd_copy(c).start()
    ddm_copy(c).wait_send()
    ddm_copy(1 - c).wait_recv()
    o_mix[...] = fin[...]

    pd_copy(c).wait_send()
    pd_copy(1 - c).wait_recv()
    ptot = jnp.concatenate([pfin[0], pfin[1]], axis=1).astype(F32)
    o_gw[...] = ptot * scale - gq[:FP]
    own_d.wait()
    own_dt.wait()
    own_lp.wait()

    @pl.loop(1, HOPS)
    def _(d):
        done(d_copy(d))
        done(dt_copy(d))
        done(lp_copy(d))


def last_kernel(
    nodes,
    ft, d, dt, lp, m, mix, gw, small, cw,
    o_lp, o_gf, o_mix, o_gw, o_gg, o_gb, o_hg, o_hb, o_cw, o_cb, o_loss, low,
):
    feat, n = ft.shape
    ncls = o_lp.shape[0]
    o_lp[...] = lp[...].astype(F32)[:ncls]
    mm = m[...]
    f = ft[...]
    fix = dot(mm[:, :feat].astype(BF16), f) + mm[:, ONES : ONES + 1]
    tail = dt[0].astype(F32)
    for b in range(4):
        low[pl.ds(0, 4), pl.ds(b * (n // 4), n // 4)] = tail[4 * b : 4 * b + 4]
    gf = jnp.concatenate([d[0].astype(F32), low[...]], axis=0)[:feat] - fix[:feat]
    if STRIDED:
        flat = o_gf.reshape(feat * (n // 128), 128)
        for i in range(n // 128):
            flat[pl.ds(i, feat, stride=n // 128), :] = gf[:, i * 128 : (i + 1) * 128]
    else:
        for i in range(n // 128):
            o_gf[:, i, :] = gf[:, i * 128 : (i + 1) * 128]

    @pl.when(pl.program_id(0) == 0)
    def _():
        hid = mix.shape[1]
        o_mix[...] = mix[...].astype(F32)
        for i in range(hid // 128):
            o_gw[:, i, :] = gw[pl.ds(0, feat), pl.ds(i * 128, 128)]
        o_hg[...] = small[pl.ds(0, 1), :]
        o_hb[...] = small[pl.ds(1, 1), :]
        o_gg[...] = small[pl.ds(2, 1), :]
        o_gb[...] = small[pl.ds(3, 1), :]
        o_cw[...] = cw[pl.ds(0, ncls), :]
        o_cb[...] = small[pl.ds(4, 1), pl.ds(0, ncls)]
        o_loss[...] = jnp.sum(small[pl.ds(4, 1), pl.ds(128, 128)], axis=1, keepdims=True) * (-1.0 / nodes)


def shards(
    R, features, branch_weight, branch_gain, branch_bias, mix_weight, mixing_norm_gain, mixing_norm_bias,
    class_weight, class_bias, labels, hop_mask,
):
    local, feat = features.shape[1:]
    hid = mix_weight.shape[0]
    ncls = class_weight.shape[1]
    nodes = local * R
    sub = local // HOPS
    Z = R // 2
    half = hid // 2
    S = min(Z, 2)
    G2, qrows = Z // S, half // 2 // S
    zrows, zcols = chunk(0, 0, qrows, G2, hid)
    brows, bcols = chunk(0, 0, half // 2, Z, hid)
    assert feat == ONES and ncls == 47 and local // hop_mask.shape[0] == 128
    ft = features[0].T
    sd = jax.ShapeDtypeStruct
    vm = pl.BlockSpec(memory_space=pltpu.VMEM)
    hbm = pl.BlockSpec(memory_space=pl.ANY)
    _, nsem = sem_plan(R)
    V = pltpu.VMEM
    outs = pl.pallas_call(
        functools.partial(main_kernel, R, nodes),
        grid=(1,),
        out_shape=(
            sd((48, local), BF16),
            sd((HOPS, MAIN, sub), BF16),
            sd((HOPS, 16, sub // 4), BF16),
            sd((FP, 128), F32),
            sd((hid, hid), BF16),
            sd((FP, hid), F32),
            sd((8, hid), F32),
            sd((48, hid), F32),
        ),
        in_specs=[hbm, pl.BlockSpec((16, local), lambda i: (MAIN // 16, 0))]
        + [vm] * 9
        + [pl.BlockSpec(memory_space=pltpu.SMEM)],
        out_specs=(hbm, hbm, hbm, vm, vm, vm, vm, vm),
        scratch_shapes=[
            V((128, local), BF16),
            V((HOPS, 128, sub), BF16),
            V((HOPS, 16, sub // 4), BF16),
            V((HOPS, 16, sub // 4), BF16),
            V((48, sub // 4), F32),
            V((HOPS, hid + 128, hid), BF16),
            V((HOPS, hid, 256), BF16),
            V((HOPS, FP, hid), BF16),
            V((HOPS, hid, hid), BF16),
            V((HOPS, 16, sub), BF16),
            V((HOPS, hid, sub), BF16),
            V((HOPS, hid, sub), BF16),
            V((hid, sub), F32),
            V((hid, sub), F32),
            V((hid, sub), BF16),
            V((128, 128), F32),
            V((64, 128), F32),
            V((Z, 64, 128), F32),
            V((2, 64, 128), F32),
            V((R, 1, 2 * hid), F32),
            V((HOPS, 1, 2 * hid), F32),
            V((HOPS, 1, 2 * hid), F32),
            V((R, 1, 2 * hid), F32),
            V((HOPS, 1, 2 * hid + 256), F32),
            V((R, 1, 2 * hid + 256), F32),
            V((HOPS, 48, hid // HOPS), BF16),
            V((HOPS, 48, hid // HOPS), BF16),
            V((R, 48, hid // HOPS), BF16),
            V((HOPS, 48, hid // HOPS), BF16),
            V((48, sub), BF16),
            V((128, hid), F32),
            V((hid, 128), BF16),
            V((8, 128), F32),
            V((hid, min(2 * TILE, sub)), BF16),
            V((hid, min(2 * TILE, sub)), BF16),
            V((128, min(2 * TILE, sub)), BF16),
            V((hid, 128), F32),
            V((hid, 128), F32),
            V((96, 128), F32),
            V((48, hid), F32),
            V((3, hid, 128), F32),
            V((HOPS, hid, hid), BF16),
            V((HOPS, half, hid), BF16),
            V((HOPS, qrows, hid), BF16),
            V((HOPS, qrows, hid), BF16),
            V((HOPS, half // 2, hid), BF16),
            V((max(G2, 2), zrows.size, zcols.size), BF16),
            V((max(Z, 2), brows.size, bcols.size), BF16),
            V((hid, hid), BF16),
            V((HOPS, MAIN, sub), BF16),
            V((8, sub), F32),
            V((HOPS, 16, sub // 4), BF16),
            V((hid, 128), F32),
            V((HOPS, FP, hid), BF16),
            V((HOPS, FP, half), BF16),
            V((HOPS, FP, half), BF16),
            V((HOPS, FP, half), BF16),
            V((HOPS, 1, 2 * hid), F32),
            V((HOPS, 1, 2 * hid), F32),
            V((R, 1, 2 * hid), F32),
            V((Z, FP, half), BF16),
            V((2, FP, half), BF16),
            pltpu.SemaphoreType.DMA((nsem,)),
            pltpu.SemaphoreType.DMA((nsem,)),
        ],
        compiler_params=pltpu.CompilerParams(
            collective_id=0, has_side_effects=True, vmem_limit_bytes=63 * 1024 * 1024
        ),
        cost_estimate=pl.CostEstimate(flops=2 * 8 * 10**9, bytes_accessed=10**7, transcendentals=10**7),
        name="main",
    )(
        ft, ft, branch_weight[0], branch_gain, branch_bias, mix_weight, mixing_norm_gain[None], mixing_norm_bias[None],
        class_weight.T, class_bias[None], labels[None], hop_mask.T,
    )
    lp, dd, dt, m, mix, gw, small, cw = outs
    nb = sub
    whole = lambda shape: pl.BlockSpec(shape, lambda i: (0,) * len(shape))
    lp, gf, mix, gw, gg, gb, hg, hb, cw, cb, loss = pl.pallas_call(
        functools.partial(last_kernel, nodes),
        grid=(local // nb,),
        out_shape=(
            sd((ncls, local), F32),
            sd((feat, local // 128, 128), F32),
            sd((hid, hid), F32),
            sd((feat, hid // 128, 128), F32),
            sd((1, hid), F32),
            sd((1, hid), F32),
            sd((1, hid), F32),
            sd((1, hid), F32),
            sd((ncls, hid), F32),
            sd((1, ncls), F32),
            sd((1, 1), F32),
        ),
        in_specs=[
            pl.BlockSpec((feat, nb), lambda i: (0, i)),
            pl.BlockSpec((1, MAIN, nb), lambda i: (i, 0, 0)),
            pl.BlockSpec((1, 16, nb // 4), lambda i: (i, 0, 0)),
            pl.BlockSpec((48, nb), lambda i: (0, i)),
            whole((FP, 128)),
            whole((hid, hid)),
            whole((FP, hid)),
            whole((8, hid)),
            whole((48, hid)),
        ],
        out_specs=(
            pl.BlockSpec((ncls, nb), lambda i: (0, i)),
            pl.BlockSpec((feat, nb // 128, 128), lambda i: (0, i, 0)),
            whole((hid, hid)),
            whole((feat, hid // 128, 128)),
            whole((1, hid)),
            whole((1, hid)),
            whole((1, hid)),
            whole((1, hid)),
            whole((ncls, hid)),
            whole((1, ncls)),
            whole((1, 1)),
        ),
        scratch_shapes=[V((8, nb), F32)],
        compiler_params=pltpu.CompilerParams(vmem_limit_bytes=60 * 1024 * 1024),
        name="last",
    )(ft, dd, dt, lp, m, mix, gw, small, cw)
    return (
        lp.T,
        loss[0, 0],
        with_layout_constraint(gf.reshape(feat, 1, local), Layout((0, 1, 2))).transpose(1, 2, 0),
        gw.reshape(1, feat, hid),
        gg,
        gb,
        mix,
        hg[0],
        hb[0],
        cw.T,
        cb[0],
    )


def solution(mesh):
    placed = (
        P("hop", "rows", None), P("hop", None, None), P("hop", None), P("hop", None), P("hop", None),
        P(), P(), P(), P(), P("rows"), P("rows", None),
    )
    assert mesh.shape["hop"] == HOPS
    return jax.shard_map(
        functools.partial(shards, mesh.shape["rows"]),
        mesh=mesh,
        in_specs=placed,
        out_specs=(
            P("rows", None), P(), P("hop", "rows", None), P("hop", None, None), P("hop", None), P("hop", None),
            P("hop", None), P(), P(), P(), P(),
        ),
        check_vma=False,
    )
```

```python
import functools
import math

import jax
import jax.numpy as jnp
from jax import lax
from jax.experimental import pallas as pl
from jax.experimental.layout import Layout, with_layout_constraint
from jax.experimental.pallas import tpu as pltpu
from jax.sharding import PartitionSpec as P

MESH = pl.DeviceIdType.MESH
EPS = 1e-05
HOPS = 4
ONES = 100
FP = 112
MAIN = 96
TILE = 256
STRIDED = True
C0 = math.sqrt(2.0 / math.pi)
C1 = C0 * 0.044715
KAPPA = C1 ** (1.0 / 3.0)
ALPHA = C0 / KAPPA
F32 = jnp.float32
BF16 = jnp.bfloat16


def dot(a, b):
    return lax.dot_general(a, b, (((1,), (0,)), ((), ())), preferred_element_type=F32)


def dot_nt(a, b):
    return lax.dot_general(a, b, (((1,), (1,)), ((), ())), preferred_element_type=F32)


def split2(x):
    hi = x.astype(BF16)
    return hi, (x - hi.astype(F32)).astype(BF16)


def split3(x):
    hi = x.astype(BF16)
    rest = x - hi.astype(F32)
    mid = rest.astype(BF16)
    return hi, mid, (rest - mid.astype(F32)).astype(BF16)


def scaled_gelu_slope(y):
    u = y * y
    t = jnp.tanh(y * (u + ALPHA))
    up = t + 1.0
    g = y * up
    return g, up + (g * (1.0 - t)) * (3.0 * u + ALPHA)


def fold(x):
    total = x[:, :128]
    for i in range(1, x.shape[1] // 128):
        total = total + x[:, i * 128 : (i + 1) * 128]
    return total


def spread(c, n):
    return jnp.concatenate([c] * (n // 128), axis=1)


def row_of(acc):
    return jnp.sum(acc.T, axis=0, keepdims=True)


def col_of(row):
    return jnp.broadcast_to(row, (128, row.shape[1])).T


def each(lo, hi, body):
    if hi - lo == 1:
        body(lo)
    elif hi > lo:
        pl.loop(lo, hi)(body)


class Alloc:
    def __init__(self):
        self.n = 0

    def __call__(self, count):
        base = self.n
        self.n += count
        return base


def sem_plan(R):
    Z = R // 2
    a = Alloc()
    names = {}
    for name, count in (
        ("feat", 7), ("ft", 4), ("loc", 1), ("ws", 4), ("zf", 4), ("dd", 4), ("s1", R), ("ab", 4), ("gp", 1), ("gz", Z), ("gd", 1),
        ("s2h", 4), ("s2r", R), ("s3h", 4), ("s3r", R), ("lp", 4), ("cwh", 4), ("cwr", R), ("cwg", 4),
        ("pair", 4), ("z1", 4), ("hop", 4), ("zr", Z), ("zg", Z), ("ddm", 1), ("d", 4), ("dt", 4), ("p", 4), ("q", 4),
        ("qr", R), ("pp", 4), ("pz", Z), ("pd", 1),
    ):
        names[name] = a(count)
    return names, a.n


def chunk(base, i, rows, pieces, cols):
    if rows // pieces >= 16:
        take = rows // pieces
        return pl.ds(pl.multiple_of(base + i * take, 16), take), pl.ds(0, cols)
    m = 16 * pieces // rows
    wide = cols // m
    return (
        pl.ds(pl.multiple_of(base + (i // m) * 16, 16), 16),
        pl.ds(pl.multiple_of((i % m) * wide, 128), wide),
    )


def main_kernel(
    R,
    nodes,
    ft, ft4, wb, bgain, bbias, wm, gain2, bias2, wc, cb, lab, msk,
    o_lp, o_d, o_dt, o_m, o_mix, o_gw, o_small, o_cw,
    fs, fx, ftail, frt, st4, wall, wl, aw, wmx, keep, mi, gp, mixed, dn2, dmx,
    gown, gpr, gz, gfin, s1, ab, s2h, s2r, s3h, s3r, cwp, cwh, cwr, cwg, lps,
    wcs, wcNs, cbs, hb, hs, dlp, acc0, acc1, accl, accw, cols,
    dmp, pr, z1r, hr, zr, fin, dsend, d4, dtail, pT, ps, ph, phalf, prv, qs, qv, qr, pz, pfin,
    ss, rs,
):
    names, _ = sem_plan(R)
    Z = R // 2
    h = lax.axis_index("hop")
    r = lax.axis_index("rows")
    c = lax.rem(r, 2)
    zi = lax.div(r, 2)
    sib = r + 1 - 2 * c
    local = ft.shape[1]
    sub = local // HOPS
    hid = wm.shape[0]
    half = hid // 2
    big = min(4 * TILE, sub)
    UN = big // TILE
    NT = sub // big
    inv_n = 1.0 / nodes

    def peer(d):
        x = lax.rem(h + d, 2)
        y = lax.rem(lax.div(h, 2) + lax.div(d, 2), 2)
        return 2 * y + x

    def rc(src, dst, name, i, hh, rr):
        return pltpu.make_async_remote_copy(
            src_ref=src, dst_ref=dst, send_sem=ss.at[names[name] + i], recv_sem=rs.at[names[name] + i],
            device_id=(hh, rr), device_id_type=MESH,
        )

    def done(cp):
        cp.wait_send()
        cp.wait_recv()

    def lanes_at(i, n):
        return pl.ds(pl.multiple_of(i * n, n), n)

    barrier = pltpu.get_barrier_semaphore()

    def greet(hh, rr):
        pl.semaphore_signal(barrier, inc=1, device_id=(hh, rr), device_id_type=MESH)

    @pl.loop(1, HOPS)
    def _(d):
        greet(peer(d), r)

    @functools.partial(each, 1, R)
    def _(e):
        greet(h, lax.rem(r + e, R))

    def rows_start(buf, name):
        @functools.partial(each, 1, R)
        def _(e):
            rc(buf.at[r], buf.at[r], name, e, h, lax.rem(r + e, R)).start()

    def rows_wait(buf, name):
        @functools.partial(each, 1, R)
        def _(e):
            src = lax.rem(r + R - e, R)
            done(rc(buf.at[src], buf.at[src], name, e, h, lax.rem(r + e, R)))

    def hops_start(buf, name):
        @pl.loop(1, HOPS)
        def _(d):
            rc(buf.at[h], buf.at[h], name, d, peer(d), r).start()

    def hops_wait(buf, name):
        @pl.loop(1, HOPS)
        def _(d):
            done(rc(buf.at[peer(d)], buf.at[peer(d)], name, d, peer(d), r))

    def total(buf, n, dtype=F32):
        return lax.fori_loop(1, n, lambda i, t: t + buf[i].astype(dtype), buf[0].astype(dtype))

    loc = pltpu.make_async_copy(ft.at[pl.ds(0, MAIN), :], fs.at[pl.ds(0, MAIN), :], ss.at[names["loc"]])
    loc.start()

    def pack4(src, dst):
        n = st4.shape[1]
        for b in range(4):
            st4[pl.ds(4 * b, 4), :] = src[pl.ds(0, 4), pl.ds(b * n, n)].astype(F32)
        dst[...] = st4[pl.ds(0, 16), :].astype(BF16)

    def unpack4(src, dst):
        n = st4.shape[1]
        row = lax.broadcasted_iota(jnp.int32, (32, n), 0)
        st4[pl.ds(0, 16), :] = src[...].astype(F32)
        st4[pl.ds(16, 32), :] = jnp.where(row == ONES - MAIN, 1.0, 0.0)
        for b in range(4):
            st4[pl.ds(16, 4), :] = st4[pl.ds(4 * b, 4), :]
            dst[pl.ds(MAIN, 32), pl.ds(b * n, n)] = st4[pl.ds(16, 32), :].astype(BF16)

    wrow = pl.ds(hid, 128)
    wall[0, pl.ds(hid + 96, 32), :] = jnp.zeros((32, hid), BF16)
    wall[0, pl.ds(hid, 100), :] = wb[...]

    @pl.loop(0, hid // 128)
    def _(i):
        k = lanes_at(i, 128)
        wall[0, pl.ds(0, hid), k] = wm[k, :].astype(F32).T.astype(BF16)

    def feat_copy(d):
        rows = pl.ds(0, MAIN)
        return rc(fs.at[rows, lanes_at(peer(d), sub)], fx.at[d, rows, :], "feat", d, peer(d), r)

    def feat_part(p):
        rows = pl.ds(0, MAIN)
        d = HOPS - 1
        return rc(
            fs.at[rows, lanes_at(NT * peer(d) + p, big)], fx.at[d, rows, lanes_at(p, big)], "feat", d + p, peer(d), r
        )

    def ft_copy(d):
        return rc(ftail.at[peer(d)], frt.at[d], "ft", d, peer(d), r)

    pl.semaphore_wait(barrier, HOPS - 1 + R - 1)

    S = min(Z, 2)
    part = (hid + 128) // (2 * S)
    zpar = lax.rem(zi, S)
    zmate = zi + (S - 1) - 2 * (S - 1) * zpar

    def part_rows(core, par):
        return pl.ds(pl.multiple_of((core * S + par) * part, 16), part)

    def ws_copy(d):
        rows = part_rows(c, zpar)
        return rc(wall.at[0, rows, :], wall.at[d, rows, :], "ws", d, peer(d), r)

    def zf_copy(d, par):
        ref = wall.at[d, part_rows(c, par), :]
        return rc(ref, ref, "zf", d, h, 2 * zmate + c)

    def dd_copy(d, core):
        ref = wall.at[d, pl.ds(pl.multiple_of(core * S * part, 16), S * part), :]
        return rc(ref, ref, "dd", d, h, sib)

    first, second = 1 + c, 2 - c
    ws_copy(first).start()
    ws_copy(second).start()
    ws_copy(HOPS - 1).start()
    loc.wait()
    feat_copy(first).start()
    feat_copy(second).start()

    @pl.loop(0, HOPS)
    def _(j):
        lanes = lanes_at(j, sub)
        pack4(ft4.at[:, lanes], ftail.at[j])
        unpack4(ftail.at[j], fs.at[:, lanes])


    @pl.loop(1, HOPS)
    def _(d):
        ft_copy(d).start()

    fx0 = pltpu.make_async_copy(fs.at[:, lanes_at(h, sub)], fx.at[0], ss.at[names["loc"]])
    fx0.start()

    def gram(i, g):
        f = fs[:, lanes_at(i, sub)]
        return g + dot_nt(f, f)

    g = lax.fori_loop(0, HOPS, gram, jnp.zeros((128, 128), F32))
    wown = wall[0, wrow, :]
    wown32 = wown.astype(F32)
    g1, g2, g3 = split3(g)
    gw = dot(g1, wown) + dot(g2, wown) + dot(g3, wown)
    s1[r, :, pl.ds(0, hid)] = gw[ONES : ONES + 1, :]
    s1[r, :, pl.ds(hid, hid)] = jnp.sum(gw * wown32, axis=0, keepdims=True)
    rows_start(s1, "s1")
    gown[...] = g

    @pl.loop(0, HOPS * (sub // 128))
    def _(i):
        d = lax.div(i, sub // 128)
        b = lax.rem(i, sub // 128)
        late = peer(d) - 2
        m = jnp.where(late >= 0, msk[jnp.maximum(late, 0), h * (sub // 128) + b], 1)
        keep[d, :, lanes_at(b, 128)] = jnp.full((16, 128), 0.5 * m.astype(F32)).astype(BF16)

    wcs[...] = jnp.zeros(wcs.shape, F32)
    wcs[pl.ds(0, wc.shape[0]), :] = wc[...].astype(F32)
    cbs[...] = jnp.zeros(cbs.shape, F32)
    cbs[pl.ds(0, 1), pl.ds(0, cb.shape[1])] = cb[...]
    ncls = wc.shape[0]

    @pl.loop(0, hid // 16)
    def _(i):
        rows = lanes_at(i, 16)
        mixed[rows, :] = jnp.zeros((16, sub), F32)
        mi[0, rows, pl.ds(0, big)] = jnp.zeros((16, big), BF16)

    fx0.wait()

    rows_wait(s1, "s1")
    st = total(s1, R)
    mean = st[:, :hid] * inv_n
    var = st[:, hid:] * inv_n - mean * mean
    inv = lax.rsqrt(var + EPS)
    scale = inv * bgain[...]
    ab[0, :, pl.ds(0, hid)] = scale
    ab[0, :, pl.ds(hid, hid)] = bbias[...] - mean * scale

    def ab_copy(d):
        return rc(ab.at[0], ab.at[d], "ab", d, peer(d), r)

    @pl.loop(1, HOPS)
    def _(d):
        ab_copy(d).start()

    def prepare(d):
        a = ab[d, :, pl.ds(0, hid)]
        b = ab[d, :, pl.ds(hid, hid)]
        ws = wall[d, wrow, :].astype(F32) * (a * KAPPA)
        aw[d] = ws[:FP].astype(BF16)
        row = lax.broadcasted_iota(jnp.int32, (128, hid), 0)
        wt = jnp.where(row == ONES, b * KAPPA, ws).T
        hi, lo = split2(wt)
        wl[d, :, pl.ds(0, 128)] = hi
        wl[d, :, pl.ds(128, 128)] = lo

    g_pair = rc(gown.at[lanes_at(1 - c, 64), :], gpr, "gp", 0, h, sib)

    def gz_copy(e, which):
        return rc(gz.at[which], gz.at[which], "gz", e, h, lax.rem(zi + e, Z) * 2 + c)

    def gd_copy(core):
        return rc(gfin.at[core], gfin.at[core], "gd", 0, h, sib)

    acc0[...] = jnp.zeros(acc0.shape, F32)
    acc1[...] = jnp.zeros(acc1.shape, F32)

    def block_sums(t):
        @pl.loop(0, hid // 64)
        def _(i):
            rows = lanes_at(i, 64)
            x = mixed[rows, lanes_at(t, big)]
            acc0[rows, :] += fold(x)
            acc1[rows, :] += fold(x * x)

    @pl.loop(0, HOPS * NT)
    def _(it):
        d = lax.div(it, NT)
        t = lax.rem(it, NT)

        @pl.when(t == 0)
        def _():
            @pl.when(d > 0)
            def _():
                @pl.when(d < HOPS - 1)
                def _():
                    done(feat_copy(d))

                done(ft_copy(d))
                unpack4(frt.at[d], fx.at[d])
                dd_copy(d, c).wait_send()
                dd_copy(d, 1 - c).wait_recv()
                done(ab_copy(d))

            prepare(d)

        if S > 1:

            @pl.when(it == min(1, NT - 1))
            def _():
                @pl.loop(1, HOPS)
                def _(j):
                    done(ws_copy(j))

                zf_copy(1, zpar).start()

        @pl.when(it == min(2, NT - 1))
        def _():
            @pl.loop(0, NT)
            def _(p):
                feat_part(p).start()

        @pl.when(jnp.logical_and(t == NT - 1, d < HOPS - 1))
        def _():
            if S > 1:
                zf_copy(d + 1, zpar).wait_send()
                zf_copy(d + 1, 1 - zpar).wait_recv()

                @pl.when(d < HOPS - 2)
                def _():
                    zf_copy(d + 2, zpar).start()

            else:
                done(ws_copy(d + 1))
            dd_copy(d + 1, c).start()

        @pl.when(it == 2 * NT)
        def _():
            g_pair.start()

        @pl.when(it == 3 * NT)
        def _():
            done(g_pair)
            gz[zi] = gown[lanes_at(c, 64), :] + gpr[...]

            @functools.partial(each, 1, Z)
            def _(e):
                gz_copy(e, zi).start()

        @pl.when(d == HOPS - 1)
        def _():
            done(feat_part(t))

        pit = jnp.maximum(it - 1, 0)
        pd = lax.div(pit, NT)
        pt = lax.rem(pit, NT)
        adds = []
        for u in range(UN):
            adds.append(dot(wall[pd, pl.ds(0, hid), :], mi[pd, :, lanes_at(pt * UN + u, TILE)]))
        for u in range(UN):
            n = lanes_at(t * UN + u, TILE)
            f = fx[d, :, n]
            z = dot(wl[d], jnp.concatenate([f, f], axis=0))
            k = keep[d, :, n]
            k = jnp.concatenate([k] * 4, axis=0)
            for i in range(0, hid, 64):
                g1, d1 = scaled_gelu_slope(z[i : i + 64].astype(BF16))
                g2, d2 = scaled_gelu_slope(g1 * k)
                mi[d, pl.ds(i, 64), n] = g2
                gp[d, pl.ds(i, 64), n] = d1 * d2 * k
        for u in range(UN):
            n = lanes_at(pt * UN + u, TILE)
            mixed[:, n] = mixed[:, n] + adds[u]

        @pl.when(jnp.logical_and(pd == HOPS - 1, it > pit))
        def _():
            block_sums(pt)


    @pl.loop(0, UN)
    def _(u):
        n = lanes_at((NT - 1) * UN + u, TILE)
        mixed[:, n] = mixed[:, n] + dot(wall[HOPS - 1, pl.ds(0, hid), :], mi[HOPS - 1, :, n])

    block_sums(NT - 1)

    def natural(lo, hi):
        @pl.loop(lo * (hid // 128), hi * (hid // 128))
        def _(i):
            d = lax.div(i, hid // 128)
            k = lanes_at(lax.rem(i, hid // 128), 128)
            wmx[d, k, :] = wall[d, pl.ds(0, hid), k].astype(F32).T.astype(BF16)

    s2h[h, :, pl.ds(0, hid)] = row_of(acc0[...])
    s2h[h, :, pl.ds(hid, hid)] = row_of(acc1[...])
    hops_start(s2h, "s2h")
    natural(0, 2)
    hops_wait(s2h, "s2h")
    s2r[r] = total(s2h, HOPS)
    rows_start(s2r, "s2r")
    natural(2, HOPS)
    wc48 = wcs[pl.ds(0, 48), :].astype(BF16)
    wcNs[...] = wcs[...].T.astype(BF16)
    crow = lax.broadcasted_iota(jnp.int32, (128, 128), 0)
    cbc = jnp.where(crow < ncls, jnp.broadcast_to(cbs[pl.ds(0, 1), :], (128, 128)).T, -1e30)[:48]
    rows_wait(s2r, "s2r")
    st2 = total(s2r, R)
    mean2 = st2[:, :hid] * inv_n
    inv2 = lax.rsqrt(st2[:, hid:] * inv_n - mean2 * mean2 + EPS * 4.0 * KAPPA * KAPPA)
    scale2 = inv2 * gain2[...]
    cols[0] = col_of(scale2 * KAPPA)
    cols[1] = col_of((bias2[...] - mean2 * scale2) * KAPPA)
    acc0[...] = jnp.zeros(acc0.shape, F32)
    acc1[...] = jnp.zeros(acc1.shape, F32)
    accl[...] = jnp.zeros(accl.shape, F32)
    accw[...] = jnp.zeros(accw.shape, F32)

    o_own = lanes_at(h, sub)

    def lp_copy(d):
        return rc(lps, o_lp.at[:, o_own], "lp", d, peer(d), r)

    dlp[...] = jnp.zeros(dlp.shape, BF16)
    HR = 128

    @pl.loop(0, NT)
    def _(t):
        n = lanes_at(t, big)

        @pl.loop(0, hid // HR)
        def _(i):
            rows = lanes_at(i, HR)
            y2 = mixed[rows, n] * spread(cols[0, rows, :], big) + spread(cols[1, rows, :], big)
            gv, dg = scaled_gelu_slope(y2.astype(BF16))
            hb[rows, :] = (gv.astype(F32) * (0.5 / KAPPA)).astype(BF16)
            hs[rows, :] = dg

        lg = dot(wc48, hb[...]) + spread(cbc, big)
        lg = lg - jnp.max(lg, axis=0, keepdims=True)
        ex = jnp.exp(lg)
        se = jnp.sum(ex, axis=0, keepdims=True)
        lp = lg - jnp.log(se)
        lps[:, n] = lp.astype(BF16)
        own = lanes_at(h * NT + t, big)
        hit = lax.broadcasted_iota(jnp.int32, (48, big), 0) == lab[:, own]
        accl[pl.ds(48, 48), :] += fold(jnp.where(hit, lp, 0.0))
        dl = ((ex / se - jnp.where(hit, 1.0, 0.0)) * inv_n).astype(BF16)
        accl[pl.ds(0, 48), :] += fold(dl.astype(F32))
        accw[...] += dot_nt(dl, hb[...])
        dlp[pl.ds(0, 48), :] = dl * 0.5

        @pl.loop(0, hid // HR)
        def _(i):
            rows = lanes_at(i, HR)
            dn = dot(wcNs[rows, :], dlp[...]) * hs[rows, :].astype(F32)
            dn2[rows, n] = dn
            acc0[rows, :] += fold(dn * mixed[rows, n])
            acc1[rows, :] += fold(dn)

    own_lp = pltpu.make_async_copy(lps, o_lp.at[:, o_own], ss.at[names["lp"]])
    own_lp.start()
    s3h[h, :, pl.ds(0, hid)] = row_of(acc0[...])
    s3h[h, :, pl.ds(hid, hid)] = row_of(acc1[...])
    zpad = jnp.zeros((80, 128), F32)
    s3h[h, :, pl.ds(2 * hid, 128)] = row_of(jnp.concatenate([accl[pl.ds(0, 48), :], zpad], axis=0))
    s3h[h, :, pl.ds(2 * hid + 128, 128)] = row_of(jnp.concatenate([accl[pl.ds(48, 48), :], zpad], axis=0))
    hops_start(s3h, "s3h")

    def cwh_copy(d):
        return rc(cwp.at[d], cwh.at[d], "cwh", d, peer(d), r)

    q = hid // HOPS

    @pl.loop(0, HOPS)
    def _(d):
        cwp[d] = accw[:, lanes_at(peer(d), q)].astype(BF16)

    hops_wait(s3h, "s3h")
    s3r[r] = total(s3h, HOPS)
    rows_start(s3r, "s3r")

    @pl.loop(1, HOPS)
    def _(d):
        cwh_copy(d).start()

    lp_copy(first).start()
    lp_copy(second).start()
    lp_copy(HOPS - 1).start()
    rows_wait(s3r, "s3r")
    st3 = total(s3r, R)
    db2 = st3[:, hid : 2 * hid]
    dg2t = inv2 * (st3[:, :hid] - mean2 * db2)
    o_small[pl.ds(0, 1), :] = dg2t
    o_small[pl.ds(1, 1), :] = db2
    o_small[pl.ds(4, 1), pl.ds(0, 256)] = st3[:, 2 * hid : 2 * hid + 256]
    o_small[pl.ds(4, 1), pl.ds(256, hid - 256)] = jnp.zeros((1, hid - 256), F32)
    t2 = scale2 * inv2 * dg2t * inv_n
    cols[0] = col_of(scale2)
    cols[1] = col_of(-t2)
    cols[2] = col_of(t2 * mean2 - scale2 * db2 * inv_n)

    @pl.loop(0, hid // 16)
    def _(i):
        rows = lanes_at(i, 16)
        v = dn2[rows, :] * spread(cols[0, rows, :], sub)
        v = v + mixed[rows, :] * spread(cols[1, rows, :], sub) + spread(cols[2, rows, :], sub)
        dmx[rows, :] = v.astype(BF16)

    @functools.partial(each, 1, Z)
    def _(e):
        gz_copy(e, zi).wait_send()
        gz_copy(e, lax.rem(zi + Z - e, Z)).wait_recv()

    gfin[c] = total(gz, Z)
    gd_copy(c).start()

    mine = lanes_at(c, half)
    theirs = lanes_at(1 - c, half)

    def pair_copy(d):
        return rc(dmp.at[d, theirs, :], pr.at[d], "pair", d, h, sib)

    qrows = half // S
    zown = pl.ds(pl.multiple_of(c * half + zpar * qrows, 16), qrows)
    zother = pl.ds(pl.multiple_of(c * half + (1 - zpar) * qrows, 16), qrows)

    def z1_copy(d):
        return rc(dmp.at[d, zother, :], z1r.at[d], "z1", d, h, 2 * zmate + c)

    def z1_start(d):
        if S > 1:
            z1_copy(d).start()

    def z1_sum(d):
        if S > 1:
            done(z1_copy(d))

            @pl.loop(0, qrows // 32)
            def _(i):
                rows = pl.ds(pl.multiple_of(c * half + zpar * qrows + i * 32, 32), 32)
                dmp[d, rows, :] = (dmp[d, rows, :].astype(F32) + z1r[d, lanes_at(i, 32), :].astype(F32)).astype(BF16)

    def hop_copy(d):
        return rc(dmp.at[d, zown, :], hr.at[d], "hop", d, peer(d), r)

    def pair_sum(d):
        done(pair_copy(d))

        @pl.loop(0, half // 32)
        def _(i):
            rows = pl.ds(pl.multiple_of(c * half + i * 32, 32), 32)
            dmp[d, rows, :] = (dmp[d, rows, :].astype(F32) + pr[d, lanes_at(i, 32), :].astype(F32)).astype(BF16)

    def mix_grad(d):
        dmp[d] = dot_nt(mi[d], dmx[...]).astype(BF16)
        pair_copy(d).start()

    def mix_grads(lo):
        @pl.loop(0, 2)
        def _(i):
            mix_grad(lo + 1 - i)

        pair_sum(lo + 1)
        z1_start(lo + 1)

    def mix_hop(d):
        z1_sum(d)
        hop_copy(d).start()

    mix_grads(2)

    G2 = Z // S
    zq = lax.div(zi, S)

    def zr_copy(e, which):
        rows, lanes = chunk(0, which, qrows, G2, hid)
        return rc(hr.at[0, rows, lanes], zr.at[e], "zr", e, h, (lax.rem(zq + e, G2) * S + zpar) * 2 + c)

    def final_chunk(z):
        return chunk(c * half + lax.rem(z, S) * qrows, lax.div(z, S), qrows, G2, hid)

    def zg_copy(e, which):
        rows, lanes = final_chunk(which)
        ref = fin.at[rows, lanes]
        return rc(ref, ref, "zg", e, h, lax.rem(zi + e, Z) * 2 + c)

    def ddm_copy(core):
        ref = fin.at[lanes_at(core, half), :]
        return rc(ref, ref, "ddm", 0, h, sib)

    def d_copy(d):
        return rc(dsend.at[d], o_d.at[h], "d", d, peer(d), r)

    def dt_copy(d):
        return rc(dtail.at[d], o_dt.at[h], "dt", d, peer(d), r)

    def pp_copy(d):
        return rc(ps.at[d, :, theirs], ph.at[d], "pp", d, h, sib)

    def p_copy(d):
        return rc(phalf.at[d], prv.at[d], "p", d, peer(d), r)

    def p_half(d):
        done(pp_copy(d))
        phalf[d] = (ps[d, :, mine].astype(F32) + ph[d].astype(F32)).astype(BF16)

    def q_copy(d):
        return rc(qs.at[d], qv.at[d], "q", d, peer(d), r)

    @pl.loop(0, HOPS * NT)
    def _(it):
        dd = lax.div(it, NT)
        t = lax.rem(it, NT)
        d = HOPS - 1 - dd

        @pl.when(t == 0)
        def _():
            pT[...] = jnp.zeros(pT.shape, F32)

        @pl.when(jnp.logical_and(t == NT // 2, dd > 0))
        def _():
            p_half(d + 1)
            p_copy(d + 1).start()

            @pl.when(dd > 1)
            def _():
                dt_copy(d + 1).start()
                d_copy(d + 1).start()


        @pl.when(it == NT // 2)
        def _():
            pair_sum(2)
            z1_start(2)

        @pl.when(it == NT + NT // 2)
        def _():
            @pl.loop(1, HOPS)
            def _(j):
                done(cwh_copy(j))

            cw = cwp[0].astype(F32)
            for j in range(1, HOPS):
                cw = cw + cwh[j].astype(F32)
            cwr[r] = cw.astype(BF16)
            rows_start(cwr, "cwr")
            pair_sum(0)
            z1_start(0)
            mix_hop(2)

        @pl.when(it == 2 * NT + NT // 2)
        def _():
            mix_hop(1)
            rows_wait(cwr, "cwr")
            cwg[h] = total(cwr, R, F32).astype(BF16)
            hops_start(cwg, "cwg")

        @pl.when(it == 3 * NT + NT // 2)
        def _():
            z1_sum(0)

            @pl.loop(1, HOPS)
            def _(j):
                done(hop_copy(j))

            @pl.loop(0, qrows // 32)
            def _(i):
                rows = lanes_at(i, 32)
                own = pl.ds(pl.multiple_of(c * half + zpar * qrows + i * 32, 32), 32)
                hsum = dmp[0, own, :].astype(F32)
                for j in range(1, HOPS):
                    hsum = hsum + hr[j, rows, :].astype(F32)
                hr[0, rows, :] = hsum.astype(BF16)

            @functools.partial(each, 1, G2)
            def _(e):
                zr_copy(e, lax.rem(zq + e, G2)).start()

            hops_wait(cwg, "cwg")
            for j in range(HOPS):
                o_cw[:, pl.ds(j * q, q)] = cwg[j].astype(F32)

        @pl.when(it == HOPS * NT - 1)
        def _():
            @functools.partial(each, 1, G2)
            def _(e):
                done(zr_copy(e, lax.rem(zq + e, G2)))

            rows, lanes = chunk(0, zq, qrows, G2, hid)
            zt = lax.fori_loop(1, G2, lambda e, v: v + zr[e].astype(F32), hr[0, rows, lanes].astype(F32))
            frows, flanes = final_chunk(zi)
            fin[frows, flanes] = zt.astype(BF16)

            @functools.partial(each, 1, Z)
            def _(e):
                zg_copy(e, zi).start()

        n = lanes_at(t, big)
        dn = dot(wmx[d], dmx[:, n]).astype(BF16) * gp[d, :, n]
        pT[...] += dot_nt(dn, fx[d, :, n])
        grad = dot(aw[d], dn)
        dsend[d, :, n] = grad[:MAIN].astype(BF16)
        d4[:, n] = grad[MAIN : MAIN + 8]

        @pl.when(t == NT - 1)
        def _():
            pw = pT[...].T * KAPPA
            qs[d, :, pl.ds(0, hid)] = jnp.sum(pw * wall[d, wrow, :].astype(F32), axis=0, keepdims=True)
            qs[d, :, pl.ds(hid, hid)] = pw[ONES : ONES + 1, :]
            ps[d] = pw[:FP].astype(BF16)
            pp_copy(d).start()
            pack4(d4, dtail.at[d])

            @pl.when(dd < HOPS - 1)
            def _():
                q_copy(d).start()

            @pl.when(dd == 0)
            def _():
                dt_copy(d).start()
                d_copy(d).start()
                mix_hop(d)
                mix_grads(0)

    @pl.loop(1, HOPS)
    def _(d):
        done(q_copy(d))

    qr[r] = qs[0] + (qv[1] + qv[2] + qv[3])
    rows_start(qr, "qr")
    own_d = pltpu.make_async_copy(dsend.at[0], o_d.at[h], ss.at[names["d"]])
    own_d.start()
    own_dt = pltpu.make_async_copy(dtail.at[0], o_dt.at[h], ss.at[names["dt"]])
    own_dt.start()

    p_half(0)

    @pl.loop(1, HOPS)
    def _(d):
        done(p_copy(d))

    psum = phalf[0].astype(F32) + (prv[1].astype(F32) + prv[2].astype(F32) + prv[3].astype(F32))
    pz[zi] = psum.astype(BF16)

    def pz_copy(e, which):
        return rc(pz.at[which], pz.at[which], "pz", e, h, lax.rem(zi + e, Z) * 2 + c)

    @functools.partial(each, 1, Z)
    def _(e):
        pz_copy(e, zi).start()

    @functools.partial(each, 1, Z)
    def _(e):
        zg_copy(e, zi).wait_send()
        zg_copy(e, lax.rem(zi + Z - e, Z)).wait_recv()

    ddm_copy(c).start()

    rows_wait(qr, "qr")
    qt = total(qr, R)
    db = qt[:, hid:]
    dgn = inv * (qt[:, :hid] - mean * db)
    o_small[pl.ds(2, 1), :] = dgn
    o_small[pl.ds(3, 1), :] = db
    c1 = scale * db * inv_n
    c2 = inv * scale * dgn * inv_n
    shift = c1 - mean * c2
    row = lax.broadcasted_iota(jnp.int32, (128, hid), 0)
    q1, q2 = split2(jnp.where(row == ONES, shift, wown32 * c2))
    o_m[...] = (dot_nt(wown, q1) + dot_nt(wown, q2))[:FP]
    gd_copy(c).wait_send()
    gd_copy(1 - c).wait_recv()
    g1, g2, g3 = split3(jnp.concatenate([gfin[0], gfin[1]], axis=0))
    gq = dot(g1, q1) + dot(g2, q1) + dot(g3, q1) + dot(g1, q2) + dot(g2, q2)

    @functools.partial(each, 1, Z)
    def _(e):
        pz_copy(e, zi).wait_send()
        pz_copy(e, lax.rem(zi + Z - e, Z)).wait_recv()

    pfin[c] = total(pz, Z).astype(BF16)

    def pd_copy(core):
        return rc(pfin.at[core], pfin.at[core], "pd", 0, h, sib)

    pd_copy(c).start()
    ddm_copy(c).wait_send()
    ddm_copy(1 - c).wait_recv()
    o_mix[...] = fin[...]

    pd_copy(c).wait_send()
    pd_copy(1 - c).wait_recv()
    ptot = jnp.concatenate([pfin[0], pfin[1]], axis=1).astype(F32)
    o_gw[...] = ptot * scale - gq[:FP]
    own_d.wait()
    own_dt.wait()
    own_lp.wait()

    @pl.loop(1, HOPS)
    def _(d):
        done(d_copy(d))
        done(dt_copy(d))
        done(lp_copy(d))


def last_kernel(
    nodes,
    ft, d, dt, lp, m, mix, gw, small, cw,
    o_lp, o_gf, o_mix, o_gw, o_gg, o_gb, o_hg, o_hb, o_cw, o_cb, o_loss, low,
):
    feat, n = ft.shape
    ncls = o_lp.shape[0]
    o_lp[...] = lp[...].astype(F32)[:ncls]
    mm = m[...]
    f = ft[...]
    fix = dot(mm[:, :feat].astype(BF16), f) + mm[:, ONES : ONES + 1]
    tail = dt[0].astype(F32)
    for b in range(4):
        low[pl.ds(0, 4), pl.ds(b * (n // 4), n // 4)] = tail[4 * b : 4 * b + 4]
    gf = jnp.concatenate([d[0].astype(F32), low[...]], axis=0)[:feat] - fix[:feat]
    if STRIDED:
        flat = o_gf.reshape(feat * (n // 128), 128)
        for i in range(n // 128):
            flat[pl.ds(i, feat, stride=n // 128), :] = gf[:, i * 128 : (i + 1) * 128]
    else:
        for i in range(n // 128):
            o_gf[:, i, :] = gf[:, i * 128 : (i + 1) * 128]

    @pl.when(pl.program_id(0) == 0)
    def _():
        hid = mix.shape[1]
        o_mix[...] = mix[...].astype(F32)
        for i in range(hid // 128):
            o_gw[:, i, :] = gw[pl.ds(0, feat), pl.ds(i * 128, 128)]
        o_hg[...] = small[pl.ds(0, 1), :]
        o_hb[...] = small[pl.ds(1, 1), :]
        o_gg[...] = small[pl.ds(2, 1), :]
        o_gb[...] = small[pl.ds(3, 1), :]
        o_cw[...] = cw[pl.ds(0, ncls), :]
        o_cb[...] = small[pl.ds(4, 1), pl.ds(0, ncls)]
        o_loss[...] = jnp.sum(small[pl.ds(4, 1), pl.ds(128, 128)], axis=1, keepdims=True) * (-1.0 / nodes)


def shards(
    R, features, branch_weight, branch_gain, branch_bias, mix_weight, mixing_norm_gain, mixing_norm_bias,
    class_weight, class_bias, labels, hop_mask,
):
    local, feat = features.shape[1:]
    hid = mix_weight.shape[0]
    ncls = class_weight.shape[1]
    nodes = local * R
    sub = local // HOPS
    Z = R // 2
    half = hid // 2
    S = min(Z, 2)
    G2, qrows = Z // S, half // S
    zrows, zcols = chunk(0, 0, qrows, G2, hid)
    assert feat == ONES and ncls == 47 and local // hop_mask.shape[0] == 128
    ft = features[0].T
    sd = jax.ShapeDtypeStruct
    vm = pl.BlockSpec(memory_space=pltpu.VMEM)
    hbm = pl.BlockSpec(memory_space=pl.ANY)
    _, nsem = sem_plan(R)
    V = pltpu.VMEM
    outs = pl.pallas_call(
        functools.partial(main_kernel, R, nodes),
        grid=(1,),
        out_shape=(
            sd((48, local), BF16),
            sd((HOPS, MAIN, sub), BF16),
            sd((HOPS, 16, sub // 4), BF16),
            sd((FP, 128), F32),
            sd((hid, hid), BF16),
            sd((FP, hid), F32),
            sd((8, hid), F32),
            sd((48, hid), F32),
        ),
        in_specs=[hbm, pl.BlockSpec((16, local), lambda i: (MAIN // 16, 0))]
        + [vm] * 9
        + [pl.BlockSpec(memory_space=pltpu.SMEM)],
        out_specs=(hbm, hbm, hbm, vm, vm, vm, vm, vm),
        scratch_shapes=[
            V((128, local), BF16),
            V((HOPS, 128, sub), BF16),
            V((HOPS, 16, sub // 4), BF16),
            V((HOPS, 16, sub // 4), BF16),
            V((48, sub // 4), F32),
            V((HOPS, hid + 128, hid), BF16),
            V((HOPS, hid, 256), BF16),
            V((HOPS, FP, hid), BF16),
            V((HOPS, hid, hid), BF16),
            V((HOPS, 16, sub), BF16),
            V((HOPS, hid, sub), BF16),
            V((HOPS, hid, sub), BF16),
            V((hid, sub), F32),
            V((hid, sub), F32),
            V((hid, sub), BF16),
            V((128, 128), F32),
            V((64, 128), F32),
            V((Z, 64, 128), F32),
            V((2, 64, 128), F32),
            V((R, 1, 2 * hid), F32),
            V((HOPS, 1, 2 * hid), F32),
            V((HOPS, 1, 2 * hid), F32),
            V((R, 1, 2 * hid), F32),
            V((HOPS, 1, 2 * hid + 256), F32),
            V((R, 1, 2 * hid + 256), F32),
            V((HOPS, 48, hid // HOPS), BF16),
            V((HOPS, 48, hid // HOPS), BF16),
            V((R, 48, hid // HOPS), BF16),
            V((HOPS, 48, hid // HOPS), BF16),
            V((48, sub), BF16),
            V((128, hid), F32),
            V((hid, 128), BF16),
            V((8, 128), F32),
            V((hid, min(4 * TILE, sub)), BF16),
            V((hid, min(4 * TILE, sub)), BF16),
            V((128, min(4 * TILE, sub)), BF16),
            V((hid, 128), F32),
            V((hid, 128), F32),
            V((96, 128), F32),
            V((48, hid), F32),
            V((3, hid, 128), F32),
            V((HOPS, hid, hid), BF16),
            V((HOPS, half, hid), BF16),
            V((HOPS, qrows, hid), BF16),
            V((HOPS, qrows, hid), BF16),
            V((max(G2, 2), zrows.size, zcols.size), BF16),
            V((hid, hid), BF16),
            V((HOPS, MAIN, sub), BF16),
            V((8, sub), F32),
            V((HOPS, 16, sub // 4), BF16),
            V((hid, 128), F32),
            V((HOPS, FP, hid), BF16),
            V((HOPS, FP, half), BF16),
            V((HOPS, FP, half), BF16),
            V((HOPS, FP, half), BF16),
            V((HOPS, 1, 2 * hid), F32),
            V((HOPS, 1, 2 * hid), F32),
            V((R, 1, 2 * hid), F32),
            V((Z, FP, half), BF16),
            V((2, FP, half), BF16),
            pltpu.SemaphoreType.DMA((nsem,)),
            pltpu.SemaphoreType.DMA((nsem,)),
        ],
        compiler_params=pltpu.CompilerParams(
            collective_id=0, has_side_effects=True, vmem_limit_bytes=63 * 1024 * 1024
        ),
        cost_estimate=pl.CostEstimate(flops=2 * 8 * 10**9, bytes_accessed=10**7, transcendentals=10**7),
        name="main",
    )(
        ft, ft, branch_weight[0], branch_gain, branch_bias, mix_weight, mixing_norm_gain[None], mixing_norm_bias[None],
        class_weight.T, class_bias[None], labels[None], hop_mask.T,
    )
    lp, dd, dt, m, mix, gw, small, cw = outs
    nb = sub
    whole = lambda shape: pl.BlockSpec(shape, lambda i: (0,) * len(shape))
    lp, gf, mix, gw, gg, gb, hg, hb, cw, cb, loss = pl.pallas_call(
        functools.partial(last_kernel, nodes),
        grid=(local // nb,),
        out_shape=(
            sd((ncls, local), F32),
            sd((feat, local // 128, 128), F32),
            sd((hid, hid), F32),
            sd((feat, hid // 128, 128), F32),
            sd((1, hid), F32),
            sd((1, hid), F32),
            sd((1, hid), F32),
            sd((1, hid), F32),
            sd((ncls, hid), F32),
            sd((1, ncls), F32),
            sd((1, 1), F32),
        ),
        in_specs=[
            pl.BlockSpec((feat, nb), lambda i: (0, i)),
            pl.BlockSpec((1, MAIN, nb), lambda i: (i, 0, 0)),
            pl.BlockSpec((1, 16, nb // 4), lambda i: (i, 0, 0)),
            pl.BlockSpec((48, nb), lambda i: (0, i)),
            whole((FP, 128)),
            whole((hid, hid)),
            whole((FP, hid)),
            whole((8, hid)),
            whole((48, hid)),
        ],
        out_specs=(
            pl.BlockSpec((ncls, nb), lambda i: (0, i)),
            pl.BlockSpec((feat, nb // 128, 128), lambda i: (0, i, 0)),
            whole((hid, hid)),
            whole((feat, hid // 128, 128)),
            whole((1, hid)),
            whole((1, hid)),
            whole((1, hid)),
            whole((1, hid)),
            whole((ncls, hid)),
            whole((1, ncls)),
            whole((1, 1)),
        ),
        scratch_shapes=[V((8, nb), F32)],
        compiler_params=pltpu.CompilerParams(vmem_limit_bytes=60 * 1024 * 1024),
        name="last",
    )(ft, dd, dt, lp, m, mix, gw, small, cw)
    return (
        lp.T,
        loss[0, 0],
        with_layout_constraint(gf.reshape(feat, 1, local), Layout((0, 1, 2))).transpose(1, 2, 0),
        gw.reshape(1, feat, hid),
        gg,
        gb,
        mix,
        hg[0],
        hb[0],
        cw.T,
        cb[0],
    )


def solution(mesh):
    placed = (
        P("hop", "rows", None), P("hop", None, None), P("hop", None), P("hop", None), P("hop", None),
        P(), P(), P(), P(), P("rows"), P("rows", None),
    )
    assert mesh.shape["hop"] == HOPS
    return jax.shard_map(
        functools.partial(shards, mesh.shape["rows"]),
        mesh=mesh,
        in_specs=placed,
        out_specs=(
            P("rows", None), P(), P("hop", "rows", None), P("hop", None, None), P("hop", None), P("hop", None),
            P("hop", None), P(), P(), P(), P(),
        ),
        check_vma=False,
    )
```

```python
import functools
import math

import jax
import jax.numpy as jnp
from jax import lax
from jax.experimental import pallas as pl
from jax.experimental.layout import Layout, with_layout_constraint
from jax.experimental.pallas import tpu as pltpu
from jax.sharding import PartitionSpec as P

MESH = pl.DeviceIdType.MESH
EPS = 1e-05
HOPS = 4
ONES = 100
FP = 112
MAIN = 96
TILE = 256
STRIDED = True
C0 = math.sqrt(2.0 / math.pi)
C1 = C0 * 0.044715
KAPPA = C1 ** (1.0 / 3.0)
ALPHA = C0 / KAPPA
F32 = jnp.float32
BF16 = jnp.bfloat16


def dot(a, b):
    return lax.dot_general(a, b, (((1,), (0,)), ((), ())), preferred_element_type=F32)


def dot_nt(a, b):
    return lax.dot_general(a, b, (((1,), (1,)), ((), ())), preferred_element_type=F32)


def split2(x):
    hi = x.astype(BF16)
    return hi, (x - hi.astype(F32)).astype(BF16)


def split3(x):
    hi = x.astype(BF16)
    rest = x - hi.astype(F32)
    mid = rest.astype(BF16)
    return hi, mid, (rest - mid.astype(F32)).astype(BF16)


def scaled_gelu_slope(y):
    u = y * y
    t = jnp.tanh(y * (u + ALPHA))
    up = t + 1.0
    g = y * up
    return g, up + (g * (1.0 - t)) * (3.0 * u + ALPHA)


def fold(x):
    total = x[:, :128]
    for i in range(1, x.shape[1] // 128):
        total = total + x[:, i * 128 : (i + 1) * 128]
    return total


def spread(c, n):
    return jnp.concatenate([c] * (n // 128), axis=1)


def row_of(acc):
    return jnp.sum(acc.T, axis=0, keepdims=True)


def col_of(row):
    return jnp.broadcast_to(row, (128, row.shape[1])).T


def each(lo, hi, body):
    if hi - lo == 1:
        body(lo)
    elif hi > lo:
        pl.loop(lo, hi)(body)


class Alloc:
    def __init__(self):
        self.n = 0

    def __call__(self, count):
        base = self.n
        self.n += count
        return base


def sem_plan(R):
    Z = R // 2
    a = Alloc()
    names = {}
    for name, count in (
        ("feat", 7), ("ft", 4), ("loc", 1), ("ws", 4), ("zf", 4), ("dd", 4), ("s1", R), ("ab", 4), ("gp", 1), ("gz", Z), ("gd", 1),
        ("s2h", 4), ("s2r", R), ("s3h", 4), ("s3r", R), ("lp", 4), ("cwh", 4), ("cwr", R), ("cwg", 4),
        ("pair", 4), ("z1", 4), ("hop", 4), ("zr", Z), ("zg", Z), ("ddm", 1), ("d", 4), ("dt", 4), ("p", 4), ("q", 4),
        ("qr", R), ("pp", 4), ("pz", Z), ("pd", 1),
    ):
        names[name] = a(count)
    return names, a.n


def chunk(base, i, rows, pieces, cols):
    if rows // pieces >= 16:
        take = rows // pieces
        return pl.ds(pl.multiple_of(base + i * take, 16), take), pl.ds(0, cols)
    m = 16 * pieces // rows
    wide = cols // m
    return (
        pl.ds(pl.multiple_of(base + (i // m) * 16, 16), 16),
        pl.ds(pl.multiple_of((i % m) * wide, 128), wide),
    )


def main_kernel(
    R,
    nodes,
    ft, ft4, wb, bgain, bbias, wm, gain2, bias2, wc, cb, lab, msk,
    o_lp, o_d, o_dt, o_m, o_mix, o_gw, o_small, o_cw,
    fs, fx, ftail, frt, st4, wall, wl, aw, wmx, keep, mi, gp, mixed, dn2, dmx,
    gown, gpr, gz, gfin, s1, ab, s2h, s2r, s3h, s3r, cwp, cwh, cwr, cwg, lps,
    wcs, wcNs, cbs, hb, hs, dlp, acc0, acc1, accl, accw, cols,
    dmp, pr, z1r, hr, zr, fin, dsend, d4, dtail, pT, ps, ph, phalf, prv, qs, qv, qr, pz, pfin,
    ss, rs,
):
    names, _ = sem_plan(R)
    Z = R // 2
    h = lax.axis_index("hop")
    r = lax.axis_index("rows")
    c = lax.rem(r, 2)
    zi = lax.div(r, 2)
    sib = r + 1 - 2 * c
    local = ft.shape[1]
    sub = local // HOPS
    hid = wm.shape[0]
    half = hid // 2
    big = min(4 * TILE, sub)
    UN = big // TILE
    NT = sub // big
    inv_n = 1.0 / nodes

    def peer(d):
        x = lax.rem(h + d, 2)
        y = lax.rem(lax.div(h, 2) + lax.div(d, 2), 2)
        return 2 * y + x

    def rc(src, dst, name, i, hh, rr):
        return pltpu.make_async_remote_copy(
            src_ref=src, dst_ref=dst, send_sem=ss.at[names[name] + i], recv_sem=rs.at[names[name] + i],
            device_id=(hh, rr), device_id_type=MESH,
        )

    def done(cp):
        cp.wait_send()
        cp.wait_recv()

    def lanes_at(i, n):
        return pl.ds(pl.multiple_of(i * n, n), n)

    barrier = pltpu.get_barrier_semaphore()

    def greet(hh, rr):
        pl.semaphore_signal(barrier, inc=1, device_id=(hh, rr), device_id_type=MESH)

    @pl.loop(1, HOPS)
    def _(d):
        greet(peer(d), r)

    @functools.partial(each, 1, R)
    def _(e):
        greet(h, lax.rem(r + e, R))

    def rows_start(buf, name):
        @functools.partial(each, 1, R)
        def _(e):
            rc(buf.at[r], buf.at[r], name, e, h, lax.rem(r + e, R)).start()

    def rows_wait(buf, name):
        @functools.partial(each, 1, R)
        def _(e):
            src = lax.rem(r + R - e, R)
            done(rc(buf.at[src], buf.at[src], name, e, h, lax.rem(r + e, R)))

    def hops_start(buf, name):
        @pl.loop(1, HOPS)
        def _(d):
            rc(buf.at[h], buf.at[h], name, d, peer(d), r).start()

    def hops_wait(buf, name):
        @pl.loop(1, HOPS)
        def _(d):
            done(rc(buf.at[peer(d)], buf.at[peer(d)], name, d, peer(d), r))

    def total(buf, n, dtype=F32):
        return lax.fori_loop(1, n, lambda i, t: t + buf[i].astype(dtype), buf[0].astype(dtype))

    loc = pltpu.make_async_copy(ft.at[pl.ds(0, MAIN), :], fs.at[pl.ds(0, MAIN), :], ss.at[names["loc"]])
    loc.start()

    def pack4(src, dst):
        n = st4.shape[1]
        for b in range(4):
            st4[pl.ds(4 * b, 4), :] = src[pl.ds(0, 4), pl.ds(b * n, n)].astype(F32)
        dst[...] = st4[pl.ds(0, 16), :].astype(BF16)

    def unpack4(src, dst):
        n = st4.shape[1]
        row = lax.broadcasted_iota(jnp.int32, (32, n), 0)
        st4[pl.ds(0, 16), :] = src[...].astype(F32)
        st4[pl.ds(16, 32), :] = jnp.where(row == ONES - MAIN, 1.0, 0.0)
        for b in range(4):
            st4[pl.ds(16, 4), :] = st4[pl.ds(4 * b, 4), :]
            dst[pl.ds(MAIN, 32), pl.ds(b * n, n)] = st4[pl.ds(16, 32), :].astype(BF16)

    wrow = pl.ds(hid, 128)
    wall[0, pl.ds(hid + 96, 32), :] = jnp.zeros((32, hid), BF16)
    wall[0, pl.ds(hid, 100), :] = wb[...]

    @pl.loop(0, hid // 128)
    def _(i):
        k = lanes_at(i, 128)
        wall[0, pl.ds(0, hid), k] = wm[k, :].astype(F32).T.astype(BF16)

    def feat_copy(d):
        rows = pl.ds(0, MAIN)
        return rc(fs.at[rows, lanes_at(peer(d), sub)], fx.at[d, rows, :], "feat", d, peer(d), r)

    def feat_part(p):
        rows = pl.ds(0, MAIN)
        d = HOPS - 1
        return rc(
            fs.at[rows, lanes_at(NT * peer(d) + p, big)], fx.at[d, rows, lanes_at(p, big)], "feat", d + p, peer(d), r
        )

    def ft_copy(d):
        return rc(ftail.at[peer(d)], frt.at[d], "ft", d, peer(d), r)

    pl.semaphore_wait(barrier, HOPS - 1 + R - 1)

    S = min(Z, 2)
    part = (hid + 128) // (2 * S)
    zpar = lax.rem(zi, S)
    zmate = zi + (S - 1) - 2 * (S - 1) * zpar

    def part_rows(core, par):
        return pl.ds(pl.multiple_of((core * S + par) * part, 16), part)

    def ws_copy(d):
        rows = part_rows(c, zpar)
        return rc(wall.at[0, rows, :], wall.at[d, rows, :], "ws", d, peer(d), r)

    def zf_copy(d, par):
        ref = wall.at[d, part_rows(c, par), :]
        return rc(ref, ref, "zf", d, h, 2 * zmate + c)

    def dd_copy(d, core):
        ref = wall.at[d, pl.ds(pl.multiple_of(core * S * part, 16), S * part), :]
        return rc(ref, ref, "dd", d, h, sib)

    first, second = 1 + c, 2 - c
    ws_copy(first).start()
    ws_copy(second).start()
    ws_copy(HOPS - 1).start()
    loc.wait()
    feat_copy(first).start()
    feat_copy(second).start()

    @pl.loop(0, HOPS)
    def _(j):
        lanes = lanes_at(j, sub)
        pack4(ft4.at[:, lanes], ftail.at[j])
        unpack4(ftail.at[j], fs.at[:, lanes])


    @pl.loop(1, HOPS)
    def _(d):
        ft_copy(d).start()

    fx0 = pltpu.make_async_copy(fs.at[:, lanes_at(h, sub)], fx.at[0], ss.at[names["loc"]])
    fx0.start()

    def gram(i, g):
        f = fs[:, lanes_at(i, sub)]
        return g + dot_nt(f, f)

    g = lax.fori_loop(0, HOPS, gram, jnp.zeros((128, 128), F32))
    wown = wall[0, wrow, :]
    wown32 = wown.astype(F32)
    g1, g2, g3 = split3(g)
    gw = dot(g1, wown) + dot(g2, wown) + dot(g3, wown)
    s1[r, :, pl.ds(0, hid)] = gw[ONES : ONES + 1, :]
    s1[r, :, pl.ds(hid, hid)] = jnp.sum(gw * wown32, axis=0, keepdims=True)
    rows_start(s1, "s1")
    gown[...] = g

    @pl.loop(0, HOPS * (sub // 128))
    def _(i):
        d = lax.div(i, sub // 128)
        b = lax.rem(i, sub // 128)
        late = peer(d) - 2
        m = jnp.where(late >= 0, msk[jnp.maximum(late, 0), h * (sub // 128) + b], 1)
        keep[d, :, lanes_at(b, 128)] = jnp.full((16, 128), 0.5 * m.astype(F32)).astype(BF16)

    wcs[...] = jnp.zeros(wcs.shape, F32)
    wcs[pl.ds(0, wc.shape[0]), :] = wc[...].astype(F32)
    cbs[...] = jnp.zeros(cbs.shape, F32)
    cbs[pl.ds(0, 1), pl.ds(0, cb.shape[1])] = cb[...]
    ncls = wc.shape[0]

    @pl.loop(0, hid // 16)
    def _(i):
        rows = lanes_at(i, 16)
        mixed[rows, :] = jnp.zeros((16, sub), F32)
        mi[0, rows, pl.ds(0, big)] = jnp.zeros((16, big), BF16)

    fx0.wait()

    rows_wait(s1, "s1")
    st = total(s1, R)
    mean = st[:, :hid] * inv_n
    var = st[:, hid:] * inv_n - mean * mean
    inv = lax.rsqrt(var + EPS)
    scale = inv * bgain[...]
    ab[0, :, pl.ds(0, hid)] = scale
    ab[0, :, pl.ds(hid, hid)] = bbias[...] - mean * scale

    def ab_copy(d):
        return rc(ab.at[0], ab.at[d], "ab", d, peer(d), r)

    @pl.loop(1, HOPS)
    def _(d):
        ab_copy(d).start()

    def prepare(d):
        a = ab[d, :, pl.ds(0, hid)]
        b = ab[d, :, pl.ds(hid, hid)]
        ws = wall[d, wrow, :].astype(F32) * (a * KAPPA)
        aw[d] = ws[:FP].astype(BF16)
        row = lax.broadcasted_iota(jnp.int32, (128, hid), 0)
        wt = jnp.where(row == ONES, b * KAPPA, ws).T
        hi, lo = split2(wt)
        wl[d, :, pl.ds(0, 128)] = hi
        wl[d, :, pl.ds(128, 128)] = lo

    g_pair = rc(gown.at[lanes_at(1 - c, 64), :], gpr, "gp", 0, h, sib)

    def gz_copy(e, which):
        return rc(gz.at[which], gz.at[which], "gz", e, h, lax.rem(zi + e, Z) * 2 + c)

    def gd_copy(core):
        return rc(gfin.at[core], gfin.at[core], "gd", 0, h, sib)

    acc0[...] = jnp.zeros(acc0.shape, F32)
    acc1[...] = jnp.zeros(acc1.shape, F32)

    def block_sums(t):
        @pl.loop(0, hid // 64)
        def _(i):
            rows = lanes_at(i, 64)
            x = mixed[rows, lanes_at(t, big)]
            acc0[rows, :] += fold(x)
            acc1[rows, :] += fold(x * x)

    @pl.loop(0, HOPS * NT)
    def _(it):
        d = lax.div(it, NT)
        t = lax.rem(it, NT)

        @pl.when(t == 0)
        def _():
            @pl.when(d > 0)
            def _():
                @pl.when(d < HOPS - 1)
                def _():
                    done(feat_copy(d))

                done(ft_copy(d))
                unpack4(frt.at[d], fx.at[d])
                dd_copy(d, c).wait_send()
                dd_copy(d, 1 - c).wait_recv()
                done(ab_copy(d))

            prepare(d)

        if S > 1:

            @pl.when(it == 0)
            def _():
                @pl.loop(1, HOPS)
                def _(j):
                    done(ws_copy(j))

                zf_copy(1, zpar).start()

        @pl.when(it == min(2, NT - 1))
        def _():
            @pl.loop(0, NT)
            def _(p):
                feat_part(p).start()

        @pl.when(jnp.logical_and(t == NT - 1, d < HOPS - 1))
        def _():
            if S > 1:
                zf_copy(d + 1, zpar).wait_send()
                zf_copy(d + 1, 1 - zpar).wait_recv()

                @pl.when(d < HOPS - 2)
                def _():
                    zf_copy(d + 2, zpar).start()

            else:
                done(ws_copy(d + 1))
            dd_copy(d + 1, c).start()

        @pl.when(it == 2 * NT)
        def _():
            g_pair.start()

        @pl.when(it == 3 * NT)
        def _():
            done(g_pair)
            gz[zi] = gown[lanes_at(c, 64), :] + gpr[...]

            @functools.partial(each, 1, Z)
            def _(e):
                gz_copy(e, zi).start()

        @pl.when(d == HOPS - 1)
        def _():
            done(feat_part(t))

        pit = jnp.maximum(it - 1, 0)
        pd = lax.div(pit, NT)
        pt = lax.rem(pit, NT)
        adds = []
        for u in range(UN):
            adds.append(dot(wall[pd, pl.ds(0, hid), :], mi[pd, :, lanes_at(pt * UN + u, TILE)]))
        for u in range(UN):
            n = lanes_at(t * UN + u, TILE)
            f = fx[d, :, n]
            z = dot(wl[d], jnp.concatenate([f, f], axis=0))
            k = keep[d, :, n]
            k = jnp.concatenate([k] * 4, axis=0)
            for i in range(0, hid, 64):
                g1, d1 = scaled_gelu_slope(z[i : i + 64].astype(BF16))
                g2, d2 = scaled_gelu_slope(g1 * k)
                mi[d, pl.ds(i, 64), n] = g2
                gp[d, pl.ds(i, 64), n] = d1 * d2 * k
        for u in range(UN):
            n = lanes_at(pt * UN + u, TILE)
            mixed[:, n] = mixed[:, n] + adds[u]

        @pl.when(jnp.logical_and(pd == HOPS - 1, it > pit))
        def _():
            block_sums(pt)


    @pl.loop(0, UN)
    def _(u):
        n = lanes_at((NT - 1) * UN + u, TILE)
        mixed[:, n] = mixed[:, n] + dot(wall[HOPS - 1, pl.ds(0, hid), :], mi[HOPS - 1, :, n])

    block_sums(NT - 1)

    def natural(lo, hi):
        @pl.loop(lo * (hid // 128), hi * (hid // 128))
        def _(i):
            d = lax.div(i, hid // 128)
            k = lanes_at(lax.rem(i, hid // 128), 128)
            wmx[d, k, :] = wall[d, pl.ds(0, hid), k].astype(F32).T.astype(BF16)

    s2h[h, :, pl.ds(0, hid)] = row_of(acc0[...])
    s2h[h, :, pl.ds(hid, hid)] = row_of(acc1[...])
    hops_start(s2h, "s2h")
    natural(0, 2)
    hops_wait(s2h, "s2h")
    s2r[r] = total(s2h, HOPS)
    rows_start(s2r, "s2r")
    natural(2, HOPS)
    wc48 = wcs[pl.ds(0, 48), :].astype(BF16)
    wcNs[...] = wcs[...].T.astype(BF16)
    crow = lax.broadcasted_iota(jnp.int32, (128, 128), 0)
    cbc = jnp.where(crow < ncls, jnp.broadcast_to(cbs[pl.ds(0, 1), :], (128, 128)).T, -1e30)[:48]
    rows_wait(s2r, "s2r")
    st2 = total(s2r, R)
    mean2 = st2[:, :hid] * inv_n
    inv2 = lax.rsqrt(st2[:, hid:] * inv_n - mean2 * mean2 + EPS * 4.0 * KAPPA * KAPPA)
    scale2 = inv2 * gain2[...]
    cols[0] = col_of(scale2 * KAPPA)
    cols[1] = col_of((bias2[...] - mean2 * scale2) * KAPPA)
    acc0[...] = jnp.zeros(acc0.shape, F32)
    acc1[...] = jnp.zeros(acc1.shape, F32)
    accl[...] = jnp.zeros(accl.shape, F32)
    accw[...] = jnp.zeros(accw.shape, F32)

    o_own = lanes_at(h, sub)

    def lp_copy(d):
        return rc(lps, o_lp.at[:, o_own], "lp", d, peer(d), r)

    dlp[...] = jnp.zeros(dlp.shape, BF16)
    HR = 128

    @pl.loop(0, NT)
    def _(t):
        n = lanes_at(t, big)

        @pl.loop(0, hid // HR)
        def _(i):
            rows = lanes_at(i, HR)
            y2 = mixed[rows, n] * spread(cols[0, rows, :], big) + spread(cols[1, rows, :], big)
            gv, dg = scaled_gelu_slope(y2.astype(BF16))
            hb[rows, :] = (gv.astype(F32) * (0.5 / KAPPA)).astype(BF16)
            hs[rows, :] = dg

        lg = dot(wc48, hb[...]) + spread(cbc, big)
        lg = lg - jnp.max(lg, axis=0, keepdims=True)
        ex = jnp.exp(lg)
        se = jnp.sum(ex, axis=0, keepdims=True)
        lp = lg - jnp.log(se)
        lps[:, n] = lp.astype(BF16)
        own = lanes_at(h * NT + t, big)
        hit = lax.broadcasted_iota(jnp.int32, (48, big), 0) == lab[:, own]
        accl[pl.ds(48, 48), :] += fold(jnp.where(hit, lp, 0.0))
        dl = ((ex / se - jnp.where(hit, 1.0, 0.0)) * inv_n).astype(BF16)
        accl[pl.ds(0, 48), :] += fold(dl.astype(F32))
        accw[...] += dot_nt(dl, hb[...])
        dlp[pl.ds(0, 48), :] = dl * 0.5

        @pl.loop(0, hid // HR)
        def _(i):
            rows = lanes_at(i, HR)
            dn = dot(wcNs[rows, :], dlp[...]) * hs[rows, :].astype(F32)
            dn2[rows, n] = dn
            acc0[rows, :] += fold(dn * mixed[rows, n])
            acc1[rows, :] += fold(dn)

    own_lp = pltpu.make_async_copy(lps, o_lp.at[:, o_own], ss.at[names["lp"]])
    own_lp.start()
    s3h[h, :, pl.ds(0, hid)] = row_of(acc0[...])
    s3h[h, :, pl.ds(hid, hid)] = row_of(acc1[...])
    zpad = jnp.zeros((80, 128), F32)
    s3h[h, :, pl.ds(2 * hid, 128)] = row_of(jnp.concatenate([accl[pl.ds(0, 48), :], zpad], axis=0))
    s3h[h, :, pl.ds(2 * hid + 128, 128)] = row_of(jnp.concatenate([accl[pl.ds(48, 48), :], zpad], axis=0))
    hops_start(s3h, "s3h")

    def cwh_copy(d):
        return rc(cwp.at[d], cwh.at[d], "cwh", d, peer(d), r)

    q = hid // HOPS

    @pl.loop(0, HOPS)
    def _(d):
        cwp[d] = accw[:, lanes_at(peer(d), q)].astype(BF16)

    hops_wait(s3h, "s3h")
    s3r[r] = total(s3h, HOPS)
    rows_start(s3r, "s3r")

    @pl.loop(1, HOPS)
    def _(d):
        cwh_copy(d).start()

    lp_copy(first).start()
    lp_copy(second).start()
    lp_copy(HOPS - 1).start()
    rows_wait(s3r, "s3r")
    st3 = total(s3r, R)
    db2 = st3[:, hid : 2 * hid]
    dg2t = inv2 * (st3[:, :hid] - mean2 * db2)
    o_small[pl.ds(0, 1), :] = dg2t
    o_small[pl.ds(1, 1), :] = db2
    o_small[pl.ds(4, 1), pl.ds(0, 256)] = st3[:, 2 * hid : 2 * hid + 256]
    o_small[pl.ds(4, 1), pl.ds(256, hid - 256)] = jnp.zeros((1, hid - 256), F32)
    t2 = scale2 * inv2 * dg2t * inv_n
    cols[0] = col_of(scale2)
    cols[1] = col_of(-t2)
    cols[2] = col_of(t2 * mean2 - scale2 * db2 * inv_n)

    @pl.loop(0, hid // 16)
    def _(i):
        rows = lanes_at(i, 16)
        v = dn2[rows, :] * spread(cols[0, rows, :], sub)
        v = v + mixed[rows, :] * spread(cols[1, rows, :], sub) + spread(cols[2, rows, :], sub)
        dmx[rows, :] = v.astype(BF16)

    @functools.partial(each, 1, Z)
    def _(e):
        gz_copy(e, zi).wait_send()
        gz_copy(e, lax.rem(zi + Z - e, Z)).wait_recv()

    gfin[c] = total(gz, Z)
    gd_copy(c).start()

    mine = lanes_at(c, half)
    theirs = lanes_at(1 - c, half)

    def pair_copy(d):
        return rc(dmp.at[d, theirs, :], pr.at[d], "pair", d, h, sib)

    qrows = half // S
    zown = pl.ds(pl.multiple_of(c * half + zpar * qrows, 16), qrows)
    zother = pl.ds(pl.multiple_of(c * half + (1 - zpar) * qrows, 16), qrows)

    def z1_copy(d):
        return rc(dmp.at[d, zother, :], z1r.at[d], "z1", d, h, 2 * zmate + c)

    def z1_start(d):
        if S > 1:
            z1_copy(d).start()

    def z1_sum(d):
        if S > 1:
            done(z1_copy(d))

            @pl.loop(0, qrows // 32)
            def _(i):
                rows = pl.ds(pl.multiple_of(c * half + zpar * qrows + i * 32, 32), 32)
                dmp[d, rows, :] = (dmp[d, rows, :].astype(F32) + z1r[d, lanes_at(i, 32), :].astype(F32)).astype(BF16)

    def hop_copy(d):
        return rc(dmp.at[d, zown, :], hr.at[d], "hop", d, peer(d), r)

    def pair_sum(d):
        done(pair_copy(d))

        @pl.loop(0, half // 32)
        def _(i):
            rows = pl.ds(pl.multiple_of(c * half + i * 32, 32), 32)
            dmp[d, rows, :] = (dmp[d, rows, :].astype(F32) + pr[d, lanes_at(i, 32), :].astype(F32)).astype(BF16)

    def mix_grad(d):
        dmp[d] = dot_nt(mi[d], dmx[...]).astype(BF16)
        pair_copy(d).start()

    def mix_grads(lo):
        @pl.loop(0, 2)
        def _(i):
            mix_grad(lo + 1 - i)

        pair_sum(lo + 1)
        z1_start(lo + 1)

    def mix_hop(d):
        z1_sum(d)
        hop_copy(d).start()

    mix_grads(2)

    G2 = Z // S
    zq = lax.div(zi, S)

    def zr_copy(e, which):
        rows, lanes = chunk(0, which, qrows, G2, hid)
        return rc(hr.at[0, rows, lanes], zr.at[e], "zr", e, h, (lax.rem(zq + e, G2) * S + zpar) * 2 + c)

    def final_chunk(z):
        return chunk(c * half + lax.rem(z, S) * qrows, lax.div(z, S), qrows, G2, hid)

    def zg_copy(e, which):
        rows, lanes = final_chunk(which)
        ref = fin.at[rows, lanes]
        return rc(ref, ref, "zg", e, h, lax.rem(zi + e, Z) * 2 + c)

    def ddm_copy(core):
        ref = fin.at[lanes_at(core, half), :]
        return rc(ref, ref, "ddm", 0, h, sib)

    def d_copy(d):
        return rc(dsend.at[d], o_d.at[h], "d", d, peer(d), r)

    def dt_copy(d):
        return rc(dtail.at[d], o_dt.at[h], "dt", d, peer(d), r)

    def pp_copy(d):
        return rc(ps.at[d, :, theirs], ph.at[d], "pp", d, h, sib)

    def p_copy(d):
        return rc(phalf.at[d], prv.at[d], "p", d, peer(d), r)

    def p_half(d):
        done(pp_copy(d))
        phalf[d] = (ps[d, :, mine].astype(F32) + ph[d].astype(F32)).astype(BF16)

    def q_copy(d):
        return rc(qs.at[d], qv.at[d], "q", d, peer(d), r)

    @pl.loop(0, HOPS * NT)
    def _(it):
        dd = lax.div(it, NT)
        t = lax.rem(it, NT)
        d = HOPS - 1 - dd

        @pl.when(t == 0)
        def _():
            pT[...] = jnp.zeros(pT.shape, F32)

        @pl.when(jnp.logical_and(t == NT // 2, dd > 0))
        def _():
            p_half(d + 1)
            p_copy(d + 1).start()

            @pl.when(dd > 1)
            def _():
                dt_copy(d + 1).start()
                d_copy(d + 1).start()


        @pl.when(it == NT // 2)
        def _():
            pair_sum(2)
            z1_start(2)

        @pl.when(it == NT + NT // 2)
        def _():
            @pl.loop(1, HOPS)
            def _(j):
                done(cwh_copy(j))

            cw = cwp[0].astype(F32)
            for j in range(1, HOPS):
                cw = cw + cwh[j].astype(F32)
            cwr[r] = cw.astype(BF16)
            rows_start(cwr, "cwr")
            pair_sum(0)
            z1_start(0)
            mix_hop(2)

        @pl.when(it == 2 * NT + NT // 2)
        def _():
            mix_hop(1)
            rows_wait(cwr, "cwr")
            cwg[h] = total(cwr, R, F32).astype(BF16)
            hops_start(cwg, "cwg")

        @pl.when(it == 3 * NT + NT // 2)
        def _():
            z1_sum(0)

            @pl.loop(1, HOPS)
            def _(j):
                done(hop_copy(j))

            @pl.loop(0, qrows // 32)
            def _(i):
                rows = lanes_at(i, 32)
                own = pl.ds(pl.multiple_of(c * half + zpar * qrows + i * 32, 32), 32)
                hsum = dmp[0, own, :].astype(F32)
                for j in range(1, HOPS):
                    hsum = hsum + hr[j, rows, :].astype(F32)
                hr[0, rows, :] = hsum.astype(BF16)

            @functools.partial(each, 1, G2)
            def _(e):
                zr_copy(e, lax.rem(zq + e, G2)).start()

            hops_wait(cwg, "cwg")
            for j in range(HOPS):
                o_cw[:, pl.ds(j * q, q)] = cwg[j].astype(F32)

        @pl.when(it == HOPS * NT - 1)
        def _():
            @functools.partial(each, 1, G2)
            def _(e):
                done(zr_copy(e, lax.rem(zq + e, G2)))

            rows, lanes = chunk(0, zq, qrows, G2, hid)
            zt = lax.fori_loop(1, G2, lambda e, v: v + zr[e].astype(F32), hr[0, rows, lanes].astype(F32))
            frows, flanes = final_chunk(zi)
            fin[frows, flanes] = zt.astype(BF16)

            @functools.partial(each, 1, Z)
            def _(e):
                zg_copy(e, zi).start()

        n = lanes_at(t, big)
        dn = dot(wmx[d], dmx[:, n]).astype(BF16) * gp[d, :, n]
        pT[...] += dot_nt(dn, fx[d, :, n])
        grad = dot(aw[d], dn)
        dsend[d, :, n] = grad[:MAIN].astype(BF16)
        d4[:, n] = grad[MAIN : MAIN + 8]

        @pl.when(t == NT - 1)
        def _():
            pw = pT[...].T * KAPPA
            qs[d, :, pl.ds(0, hid)] = jnp.sum(pw * wall[d, wrow, :].astype(F32), axis=0, keepdims=True)
            qs[d, :, pl.ds(hid, hid)] = pw[ONES : ONES + 1, :]
            ps[d] = pw[:FP].astype(BF16)
            pp_copy(d).start()
            pack4(d4, dtail.at[d])

            @pl.when(dd < HOPS - 1)
            def _():
                q_copy(d).start()

            @pl.when(dd == 0)
            def _():
                dt_copy(d).start()
                d_copy(d).start()
                mix_hop(d)
                mix_grads(0)

    @pl.loop(1, HOPS)
    def _(d):
        done(q_copy(d))

    qr[r] = qs[0] + (qv[1] + qv[2] + qv[3])
    rows_start(qr, "qr")
    own_d = pltpu.make_async_copy(dsend.at[0], o_d.at[h], ss.at[names["d"]])
    own_d.start()
    own_dt = pltpu.make_async_copy(dtail.at[0], o_dt.at[h], ss.at[names["dt"]])
    own_dt.start()

    p_half(0)

    @pl.loop(1, HOPS)
    def _(d):
        done(p_copy(d))

    psum = phalf[0].astype(F32) + (prv[1].astype(F32) + prv[2].astype(F32) + prv[3].astype(F32))
    pz[zi] = psum.astype(BF16)

    def pz_copy(e, which):
        return rc(pz.at[which], pz.at[which], "pz", e, h, lax.rem(zi + e, Z) * 2 + c)

    @functools.partial(each, 1, Z)
    def _(e):
        pz_copy(e, zi).start()

    @functools.partial(each, 1, Z)
    def _(e):
        zg_copy(e, zi).wait_send()
        zg_copy(e, lax.rem(zi + Z - e, Z)).wait_recv()

    ddm_copy(c).start()

    rows_wait(qr, "qr")
    qt = total(qr, R)
    db = qt[:, hid:]
    dgn = inv * (qt[:, :hid] - mean * db)
    o_small[pl.ds(2, 1), :] = dgn
    o_small[pl.ds(3, 1), :] = db
    c1 = scale * db * inv_n
    c2 = inv * scale * dgn * inv_n
    shift = c1 - mean * c2
    row = lax.broadcasted_iota(jnp.int32, (128, hid), 0)
    q1, q2 = split2(jnp.where(row == ONES, shift, wown32 * c2))
    o_m[...] = (dot_nt(wown, q1) + dot_nt(wown, q2))[:FP]
    gd_copy(c).wait_send()
    gd_copy(1 - c).wait_recv()
    g1, g2, g3 = split3(jnp.concatenate([gfin[0], gfin[1]], axis=0))
    gq = dot(g1, q1) + dot(g2, q1) + dot(g3, q1) + dot(g1, q2) + dot(g2, q2)

    @functools.partial(each, 1, Z)
    def _(e):
        pz_copy(e, zi).wait_send()
        pz_copy(e, lax.rem(zi + Z - e, Z)).wait_recv()

    pfin[c] = total(pz, Z).astype(BF16)

    def pd_copy(core):
        return rc(pfin.at[core], pfin.at[core], "pd", 0, h, sib)

    pd_copy(c).start()
    ddm_copy(c).wait_send()
    ddm_copy(1 - c).wait_recv()
    o_mix[...] = fin[...]

    pd_copy(c).wait_send()
    pd_copy(1 - c).wait_recv()
    ptot = jnp.concatenate([pfin[0], pfin[1]], axis=1).astype(F32)
    o_gw[...] = ptot * scale - gq[:FP]
    own_d.wait()
    own_dt.wait()
    own_lp.wait()

    @pl.loop(1, HOPS)
    def _(d):
        done(d_copy(d))
        done(dt_copy(d))
        done(lp_copy(d))


def last_kernel(
    nodes,
    ft, d, dt, lp, m, mix, gw, small, cw,
    o_lp, o_gf, o_mix, o_gw, o_gg, o_gb, o_hg, o_hb, o_cw, o_cb, o_loss, low,
):
    feat, n = ft.shape
    ncls = o_lp.shape[0]
    o_lp[...] = lp[...].astype(F32)[:ncls]
    mm = m[...]
    f = ft[...]
    fix = dot(mm[:, :feat].astype(BF16), f) + mm[:, ONES : ONES + 1]
    tail = dt[0].astype(F32)
    for b in range(4):
        low[pl.ds(0, 4), pl.ds(b * (n // 4), n // 4)] = tail[4 * b : 4 * b + 4]
    gf = jnp.concatenate([d[0].astype(F32), low[...]], axis=0)[:feat] - fix[:feat]
    if STRIDED:
        flat = o_gf.reshape(feat * (n // 128), 128)
        for i in range(n // 128):
            flat[pl.ds(i, feat, stride=n // 128), :] = gf[:, i * 128 : (i + 1) * 128]
    else:
        for i in range(n // 128):
            o_gf[:, i, :] = gf[:, i * 128 : (i + 1) * 128]

    @pl.when(pl.program_id(0) == 0)
    def _():
        hid = mix.shape[1]
        o_mix[...] = mix[...].astype(F32)
        for i in range(hid // 128):
            o_gw[:, i, :] = gw[pl.ds(0, feat), pl.ds(i * 128, 128)]
        o_hg[...] = small[pl.ds(0, 1), :]
        o_hb[...] = small[pl.ds(1, 1), :]
        o_gg[...] = small[pl.ds(2, 1), :]
        o_gb[...] = small[pl.ds(3, 1), :]
        o_cw[...] = cw[pl.ds(0, ncls), :]
        o_cb[...] = small[pl.ds(4, 1), pl.ds(0, ncls)]
        o_loss[...] = jnp.sum(small[pl.ds(4, 1), pl.ds(128, 128)], axis=1, keepdims=True) * (-1.0 / nodes)


def shards(
    R, features, branch_weight, branch_gain, branch_bias, mix_weight, mixing_norm_gain, mixing_norm_bias,
    class_weight, class_bias, labels, hop_mask,
):
    local, feat = features.shape[1:]
    hid = mix_weight.shape[0]
    ncls = class_weight.shape[1]
    nodes = local * R
    sub = local // HOPS
    Z = R // 2
    half = hid // 2
    S = min(Z, 2)
    G2, qrows = Z // S, half // S
    zrows, zcols = chunk(0, 0, qrows, G2, hid)
    assert feat == ONES and ncls == 47 and local // hop_mask.shape[0] == 128
    ft = features[0].T
    sd = jax.ShapeDtypeStruct
    vm = pl.BlockSpec(memory_space=pltpu.VMEM)
    hbm = pl.BlockSpec(memory_space=pl.ANY)
    _, nsem = sem_plan(R)
    V = pltpu.VMEM
    outs = pl.pallas_call(
        functools.partial(main_kernel, R, nodes),
        grid=(1,),
        out_shape=(
            sd((48, local), BF16),
            sd((HOPS, MAIN, sub), BF16),
            sd((HOPS, 16, sub // 4), BF16),
            sd((FP, 128), F32),
            sd((hid, hid), BF16),
            sd((FP, hid), F32),
            sd((8, hid), F32),
            sd((48, hid), F32),
        ),
        in_specs=[hbm, pl.BlockSpec((16, local), lambda i: (MAIN // 16, 0))]
        + [vm] * 9
        + [pl.BlockSpec(memory_space=pltpu.SMEM)],
        out_specs=(hbm, hbm, hbm, vm, vm, vm, vm, vm),
        scratch_shapes=[
            V((128, local), BF16),
            V((HOPS, 128, sub), BF16),
            V((HOPS, 16, sub // 4), BF16),
            V((HOPS, 16, sub // 4), BF16),
            V((48, sub // 4), F32),
            V((HOPS, hid + 128, hid), BF16),
            V((HOPS, hid, 256), BF16),
            V((HOPS, FP, hid), BF16),
            V((HOPS, hid, hid), BF16),
            V((HOPS, 16, sub), BF16),
            V((HOPS, hid, sub), BF16),
            V((HOPS, hid, sub), BF16),
            V((hid, sub), F32),
            V((hid, sub), F32),
            V((hid, sub), BF16),
            V((128, 128), F32),
            V((64, 128), F32),
            V((Z, 64, 128), F32),
            V((2, 64, 128), F32),
            V((R, 1, 2 * hid), F32),
            V((HOPS, 1, 2 * hid), F32),
            V((HOPS, 1, 2 * hid), F32),
            V((R, 1, 2 * hid), F32),
            V((HOPS, 1, 2 * hid + 256), F32),
            V((R, 1, 2 * hid + 256), F32),
            V((HOPS, 48, hid // HOPS), BF16),
            V((HOPS, 48, hid // HOPS), BF16),
            V((R, 48, hid // HOPS), BF16),
            V((HOPS, 48, hid // HOPS), BF16),
            V((48, sub), BF16),
            V((128, hid), F32),
            V((hid, 128), BF16),
            V((8, 128), F32),
            V((hid, min(4 * TILE, sub)), BF16),
            V((hid, min(4 * TILE, sub)), BF16),
            V((128, min(4 * TILE, sub)), BF16),
            V((hid, 128), F32),
            V((hid, 128), F32),
            V((96, 128), F32),
            V((48, hid), F32),
            V((3, hid, 128), F32),
            V((HOPS, hid, hid), BF16),
            V((HOPS, half, hid), BF16),
            V((HOPS, qrows, hid), BF16),
            V((HOPS, qrows, hid), BF16),
            V((max(G2, 2), zrows.size, zcols.size), BF16),
            V((hid, hid), BF16),
            V((HOPS, MAIN, sub), BF16),
            V((8, sub), F32),
            V((HOPS, 16, sub // 4), BF16),
            V((hid, 128), F32),
            V((HOPS, FP, hid), BF16),
            V((HOPS, FP, half), BF16),
            V((HOPS, FP, half), BF16),
            V((HOPS, FP, half), BF16),
            V((HOPS, 1, 2 * hid), F32),
            V((HOPS, 1, 2 * hid), F32),
            V((R, 1, 2 * hid), F32),
            V((Z, FP, half), BF16),
            V((2, FP, half), BF16),
            pltpu.SemaphoreType.DMA((nsem,)),
            pltpu.SemaphoreType.DMA((nsem,)),
        ],
        compiler_params=pltpu.CompilerParams(
            collective_id=0, has_side_effects=True, vmem_limit_bytes=63 * 1024 * 1024
        ),
        cost_estimate=pl.CostEstimate(flops=2 * 8 * 10**9, bytes_accessed=10**7, transcendentals=10**7),
        name="main",
    )(
        ft, ft, branch_weight[0], branch_gain, branch_bias, mix_weight, mixing_norm_gain[None], mixing_norm_bias[None],
        class_weight.T, class_bias[None], labels[None], hop_mask.T,
    )
    lp, dd, dt, m, mix, gw, small, cw = outs
    nb = sub
    whole = lambda shape: pl.BlockSpec(shape, lambda i: (0,) * len(shape))
    lp, gf, mix, gw, gg, gb, hg, hb, cw, cb, loss = pl.pallas_call(
        functools.partial(last_kernel, nodes),
        grid=(local // nb,),
        out_shape=(
            sd((ncls, local), F32),
            sd((feat, local // 128, 128), F32),
            sd((hid, hid), F32),
            sd((feat, hid // 128, 128), F32),
            sd((1, hid), F32),
            sd((1, hid), F32),
            sd((1, hid), F32),
            sd((1, hid), F32),
            sd((ncls, hid), F32),
            sd((1, ncls), F32),
            sd((1, 1), F32),
        ),
        in_specs=[
            pl.BlockSpec((feat, nb), lambda i: (0, i)),
            pl.BlockSpec((1, MAIN, nb), lambda i: (i, 0, 0)),
            pl.BlockSpec((1, 16, nb // 4), lambda i: (i, 0, 0)),
            pl.BlockSpec((48, nb), lambda i: (0, i)),
            whole((FP, 128)),
            whole((hid, hid)),
            whole((FP, hid)),
            whole((8, hid)),
            whole((48, hid)),
        ],
        out_specs=(
            pl.BlockSpec((ncls, nb), lambda i: (0, i)),
            pl.BlockSpec((feat, nb // 128, 128), lambda i: (0, i, 0)),
            whole((hid, hid)),
            whole((feat, hid // 128, 128)),
            whole((1, hid)),
            whole((1, hid)),
            whole((1, hid)),
            whole((1, hid)),
            whole((ncls, hid)),
            whole((1, ncls)),
            whole((1, 1)),
        ),
        scratch_shapes=[V((8, nb), F32)],
        compiler_params=pltpu.CompilerParams(vmem_limit_bytes=60 * 1024 * 1024),
        name="last",
    )(ft, dd, dt, lp, m, mix, gw, small, cw)
    return (
        lp.T,
        loss[0, 0],
        with_layout_constraint(gf.reshape(feat, 1, local), Layout((0, 1, 2))).transpose(1, 2, 0),
        gw.reshape(1, feat, hid),
        gg,
        gb,
        mix,
        hg[0],
        hb[0],
        cw.T,
        cb[0],
    )


def solution(mesh):
    placed = (
        P("hop", "rows", None), P("hop", None, None), P("hop", None), P("hop", None), P("hop", None),
        P(), P(), P(), P(), P("rows"), P("rows", None),
    )
    assert mesh.shape["hop"] == HOPS
    return jax.shard_map(
        functools.partial(shards, mesh.shape["rows"]),
        mesh=mesh,
        in_specs=placed,
        out_specs=(
            P("rows", None), P(), P("hop", "rows", None), P("hop", None, None), P("hop", None), P("hop", None),
            P("hop", None), P(), P(), P(), P(),
        ),
        check_vma=False,
    )
```

```python
import functools
import math

import jax
import jax.numpy as jnp
from jax import lax
from jax.experimental import pallas as pl
from jax.experimental.layout import Layout, with_layout_constraint
from jax.experimental.pallas import tpu as pltpu
from jax.sharding import PartitionSpec as P

MESH = pl.DeviceIdType.MESH
EPS = 1e-05
HOPS = 4
ONES = 100
FP = 112
MAIN = 96
TILE = 256
STRIDED = True
C0 = math.sqrt(2.0 / math.pi)
C1 = C0 * 0.044715
KAPPA = C1 ** (1.0 / 3.0)
ALPHA = C0 / KAPPA
F32 = jnp.float32
BF16 = jnp.bfloat16


def dot(a, b):
    return lax.dot_general(a, b, (((1,), (0,)), ((), ())), preferred_element_type=F32)


def dot_nt(a, b):
    return lax.dot_general(a, b, (((1,), (1,)), ((), ())), preferred_element_type=F32)


def split2(x):
    hi = x.astype(BF16)
    return hi, (x - hi.astype(F32)).astype(BF16)


def split3(x):
    hi = x.astype(BF16)
    rest = x - hi.astype(F32)
    mid = rest.astype(BF16)
    return hi, mid, (rest - mid.astype(F32)).astype(BF16)


def scaled_gelu_slope(y):
    u = y * y
    t = jnp.tanh(y * (u + ALPHA))
    up = t + 1.0
    g = y * up
    return g, up + (g * (1.0 - t)) * (3.0 * u + ALPHA)


def fold(x):
    total = x[:, :128]
    for i in range(1, x.shape[1] // 128):
        total = total + x[:, i * 128 : (i + 1) * 128]
    return total


def spread(c, n):
    return jnp.concatenate([c] * (n // 128), axis=1)


def row_of(acc):
    return jnp.sum(acc.T, axis=0, keepdims=True)


def col_of(row):
    return jnp.broadcast_to(row, (128, row.shape[1])).T


def each(lo, hi, body):
    if hi - lo == 1:
        body(lo)
    elif hi > lo:
        pl.loop(lo, hi)(body)


class Alloc:
    def __init__(self):
        self.n = 0

    def __call__(self, count):
        base = self.n
        self.n += count
        return base


def sem_plan(R):
    Z = R // 2
    a = Alloc()
    names = {}
    for name, count in (
        ("feat", 7), ("ft", 4), ("loc", 1), ("ws", 4), ("zf", 4), ("dd", 4), ("s1", R), ("ab", 4), ("gp", 1), ("gz", Z), ("gd", 1),
        ("s2h", 4), ("s2r", R), ("s3h", 4), ("s3r", R), ("lp", 4), ("cwh", 4), ("cwr", R), ("cwg", 4),
        ("pair", 4), ("z1", 4), ("hop", 4), ("zr", Z), ("zg", Z), ("ddm", 1), ("d", 4), ("dt", 4), ("p", 4), ("q", 4),
        ("qr", R), ("pp", 4), ("pz", Z), ("pd", 1),
    ):
        names[name] = a(count)
    return names, a.n


def chunk(base, i, rows, pieces, cols):
    if rows // pieces >= 16:
        take = rows // pieces
        return pl.ds(pl.multiple_of(base + i * take, 16), take), pl.ds(0, cols)
    m = 16 * pieces // rows
    wide = cols // m
    return (
        pl.ds(pl.multiple_of(base + (i // m) * 16, 16), 16),
        pl.ds(pl.multiple_of((i % m) * wide, 128), wide),
    )


def main_kernel(
    R,
    nodes,
    ft, ft4, wb, bgain, bbias, wm, gain2, bias2, wc, cb, lab, msk,
    o_lp, o_d, o_dt, o_m, o_mix, o_gw, o_small, o_cw,
    fs, fx, ftail, frt, st4, wall, wl, aw, wmx, keep, mi, gp, mixed, dn2, dmx,
    gown, gpr, gz, gfin, s1, ab, s2h, s2r, s3h, s3r, cwp, cwh, cwr, cwg, lps,
    wcs, wcNs, cbs, hb, hs, dlp, acc0, acc1, accl, accw, cols,
    dmp, pr, z1r, hr, zr, fin, dsend, d4, dtail, pT, ps, ph, phalf, prv, qs, qv, qr, pz, pfin,
    ss, rs,
):
    names, _ = sem_plan(R)
    Z = R // 2
    h = lax.axis_index("hop")
    r = lax.axis_index("rows")
    c = lax.rem(r, 2)
    zi = lax.div(r, 2)
    sib = r + 1 - 2 * c
    local = ft.shape[1]
    sub = local // HOPS
    hid = wm.shape[0]
    half = hid // 2
    big = min(4 * TILE, sub)
    UN = big // TILE
    NT = sub // big
    wide = min(8 * TILE, sub)
    NB = sub // wide
    inv_n = 1.0 / nodes

    def peer(d):
        x = lax.rem(h + d, 2)
        y = lax.rem(lax.div(h, 2) + lax.div(d, 2), 2)
        return 2 * y + x

    def rc(src, dst, name, i, hh, rr):
        return pltpu.make_async_remote_copy(
            src_ref=src, dst_ref=dst, send_sem=ss.at[names[name] + i], recv_sem=rs.at[names[name] + i],
            device_id=(hh, rr), device_id_type=MESH,
        )

    def done(cp):
        cp.wait_send()
        cp.wait_recv()

    def lanes_at(i, n):
        return pl.ds(pl.multiple_of(i * n, n), n)

    barrier = pltpu.get_barrier_semaphore()

    def greet(hh, rr):
        pl.semaphore_signal(barrier, inc=1, device_id=(hh, rr), device_id_type=MESH)

    @pl.loop(1, HOPS)
    def _(d):
        greet(peer(d), r)

    @functools.partial(each, 1, R)
    def _(e):
        greet(h, lax.rem(r + e, R))

    def rows_start(buf, name):
        @functools.partial(each, 1, R)
        def _(e):
            rc(buf.at[r], buf.at[r], name, e, h, lax.rem(r + e, R)).start()

    def rows_wait(buf, name):
        @functools.partial(each, 1, R)
        def _(e):
            src = lax.rem(r + R - e, R)
            done(rc(buf.at[src], buf.at[src], name, e, h, lax.rem(r + e, R)))

    def hops_start(buf, name):
        @pl.loop(1, HOPS)
        def _(d):
            rc(buf.at[h], buf.at[h], name, d, peer(d), r).start()

    def hops_wait(buf, name):
        @pl.loop(1, HOPS)
        def _(d):
            done(rc(buf.at[peer(d)], buf.at[peer(d)], name, d, peer(d), r))

    def total(buf, n, dtype=F32):
        return lax.fori_loop(1, n, lambda i, t: t + buf[i].astype(dtype), buf[0].astype(dtype))

    loc = pltpu.make_async_copy(ft.at[pl.ds(0, MAIN), :], fs.at[pl.ds(0, MAIN), :], ss.at[names["loc"]])
    loc.start()

    def pack4(src, dst):
        n = st4.shape[1]
        for b in range(4):
            st4[pl.ds(4 * b, 4), :] = src[pl.ds(0, 4), pl.ds(b * n, n)].astype(F32)
        dst[...] = st4[pl.ds(0, 16), :].astype(BF16)

    def unpack4(src, dst):
        n = st4.shape[1]
        row = lax.broadcasted_iota(jnp.int32, (32, n), 0)
        st4[pl.ds(0, 16), :] = src[...].astype(F32)
        st4[pl.ds(16, 32), :] = jnp.where(row == ONES - MAIN, 1.0, 0.0)
        for b in range(4):
            st4[pl.ds(16, 4), :] = st4[pl.ds(4 * b, 4), :]
            dst[pl.ds(MAIN, 32), pl.ds(b * n, n)] = st4[pl.ds(16, 32), :].astype(BF16)

    wrow = pl.ds(hid, 128)
    wall[0, pl.ds(hid + 96, 32), :] = jnp.zeros((32, hid), BF16)
    wall[0, pl.ds(hid, 100), :] = wb[...]

    @pl.loop(0, hid // 128)
    def _(i):
        k = lanes_at(i, 128)
        wall[0, pl.ds(0, hid), k] = wm[k, :].astype(F32).T.astype(BF16)

    def feat_copy(d):
        rows = pl.ds(0, MAIN)
        return rc(fs.at[rows, lanes_at(peer(d), sub)], fx.at[d, rows, :], "feat", d, peer(d), r)

    def feat_part(p):
        rows = pl.ds(0, MAIN)
        d = HOPS - 1
        return rc(
            fs.at[rows, lanes_at(NT * peer(d) + p, big)], fx.at[d, rows, lanes_at(p, big)], "feat", d + p, peer(d), r
        )

    def ft_copy(d):
        return rc(ftail.at[peer(d)], frt.at[d], "ft", d, peer(d), r)

    pl.semaphore_wait(barrier, HOPS - 1 + R - 1)

    S = min(Z, 2)
    part = (hid + 128) // (2 * S)
    zpar = lax.rem(zi, S)
    zmate = zi + (S - 1) - 2 * (S - 1) * zpar

    def part_rows(core, par):
        return pl.ds(pl.multiple_of((core * S + par) * part, 16), part)

    def ws_copy(d):
        rows = part_rows(c, zpar)
        return rc(wall.at[0, rows, :], wall.at[d, rows, :], "ws", d, peer(d), r)

    def zf_copy(d, par):
        ref = wall.at[d, part_rows(c, par), :]
        return rc(ref, ref, "zf", d, h, 2 * zmate + c)

    def dd_copy(d, core):
        ref = wall.at[d, pl.ds(pl.multiple_of(core * S * part, 16), S * part), :]
        return rc(ref, ref, "dd", d, h, sib)

    first, second = 1 + c, 2 - c
    ws_copy(first).start()
    ws_copy(second).start()
    ws_copy(HOPS - 1).start()
    loc.wait()
    feat_copy(first).start()
    feat_copy(second).start()

    @pl.loop(0, HOPS)
    def _(j):
        lanes = lanes_at(j, sub)
        pack4(ft4.at[:, lanes], ftail.at[j])
        unpack4(ftail.at[j], fs.at[:, lanes])


    @pl.loop(1, HOPS)
    def _(d):
        ft_copy(d).start()

    fx0 = pltpu.make_async_copy(fs.at[:, lanes_at(h, sub)], fx.at[0], ss.at[names["loc"]])
    fx0.start()

    def gram(i, g):
        f = fs[:, lanes_at(i, sub)]
        return g + dot_nt(f, f)

    g = lax.fori_loop(0, HOPS, gram, jnp.zeros((128, 128), F32))
    wown = wall[0, wrow, :]
    wown32 = wown.astype(F32)
    g1, g2, g3 = split3(g)
    gw = dot(g1, wown) + dot(g2, wown) + dot(g3, wown)
    s1[r, :, pl.ds(0, hid)] = gw[ONES : ONES + 1, :]
    s1[r, :, pl.ds(hid, hid)] = jnp.sum(gw * wown32, axis=0, keepdims=True)
    rows_start(s1, "s1")
    gown[...] = g

    @pl.loop(0, HOPS * (sub // 128))
    def _(i):
        d = lax.div(i, sub // 128)
        b = lax.rem(i, sub // 128)
        late = peer(d) - 2
        m = jnp.where(late >= 0, msk[jnp.maximum(late, 0), h * (sub // 128) + b], 1)
        keep[d, :, lanes_at(b, 128)] = jnp.full((16, 128), 0.5 * m.astype(F32)).astype(BF16)

    wcs[...] = jnp.zeros(wcs.shape, F32)
    wcs[pl.ds(0, wc.shape[0]), :] = wc[...].astype(F32)
    cbs[...] = jnp.zeros(cbs.shape, F32)
    cbs[pl.ds(0, 1), pl.ds(0, cb.shape[1])] = cb[...]
    ncls = wc.shape[0]

    @pl.loop(0, hid // 16)
    def _(i):
        rows = lanes_at(i, 16)
        mixed[rows, :] = jnp.zeros((16, sub), F32)
        mi[0, rows, pl.ds(0, big)] = jnp.zeros((16, big), BF16)

    fx0.wait()

    rows_wait(s1, "s1")
    st = total(s1, R)
    mean = st[:, :hid] * inv_n
    var = st[:, hid:] * inv_n - mean * mean
    inv = lax.rsqrt(var + EPS)
    scale = inv * bgain[...]
    ab[0, :, pl.ds(0, hid)] = scale
    ab[0, :, pl.ds(hid, hid)] = bbias[...] - mean * scale

    def ab_copy(d):
        return rc(ab.at[0], ab.at[d], "ab", d, peer(d), r)

    @pl.loop(1, HOPS)
    def _(d):
        ab_copy(d).start()

    def prepare(d):
        a = ab[d, :, pl.ds(0, hid)]
        b = ab[d, :, pl.ds(hid, hid)]
        ws = wall[d, wrow, :].astype(F32) * (a * KAPPA)
        aw[d] = ws[:FP].astype(BF16)
        row = lax.broadcasted_iota(jnp.int32, (128, hid), 0)
        wt = jnp.where(row == ONES, b * KAPPA, ws).T
        hi, lo = split2(wt)
        wl[d, :, pl.ds(0, 128)] = hi
        wl[d, :, pl.ds(128, 128)] = lo

    g_pair = rc(gown.at[lanes_at(1 - c, 64), :], gpr, "gp", 0, h, sib)

    def gz_copy(e, which):
        return rc(gz.at[which], gz.at[which], "gz", e, h, lax.rem(zi + e, Z) * 2 + c)

    def gd_copy(core):
        return rc(gfin.at[core], gfin.at[core], "gd", 0, h, sib)

    acc0[...] = jnp.zeros(acc0.shape, F32)
    acc1[...] = jnp.zeros(acc1.shape, F32)

    def block_sums(t):
        @pl.loop(0, hid // 64)
        def _(i):
            rows = lanes_at(i, 64)
            x = mixed[rows, lanes_at(t, big)]
            acc0[rows, :] += fold(x)
            acc1[rows, :] += fold(x * x)

    @pl.loop(0, HOPS * NT)
    def _(it):
        d = lax.div(it, NT)
        t = lax.rem(it, NT)

        @pl.when(t == 0)
        def _():
            @pl.when(d > 0)
            def _():
                @pl.when(d < HOPS - 1)
                def _():
                    done(feat_copy(d))

                done(ft_copy(d))
                unpack4(frt.at[d], fx.at[d])
                dd_copy(d, c).wait_send()
                dd_copy(d, 1 - c).wait_recv()
                done(ab_copy(d))

            prepare(d)

        if S > 1:

            @pl.when(it == 0)
            def _():
                @pl.loop(1, HOPS)
                def _(j):
                    done(ws_copy(j))

                zf_copy(1, zpar).start()

        @pl.when(it == min(2, NT - 1))
        def _():
            @pl.loop(0, NT)
            def _(p):
                feat_part(p).start()

        @pl.when(jnp.logical_and(t == NT - 1, d < HOPS - 1))
        def _():
            if S > 1:
                zf_copy(d + 1, zpar).wait_send()
                zf_copy(d + 1, 1 - zpar).wait_recv()

                @pl.when(d < HOPS - 2)
                def _():
                    zf_copy(d + 2, zpar).start()

            else:
                done(ws_copy(d + 1))
            dd_copy(d + 1, c).start()

        @pl.when(it == 2 * NT)
        def _():
            g_pair.start()

        @pl.when(it == 3 * NT)
        def _():
            done(g_pair)
            gz[zi] = gown[lanes_at(c, 64), :] + gpr[...]

            @functools.partial(each, 1, Z)
            def _(e):
                gz_copy(e, zi).start()

        @pl.when(d == HOPS - 1)
        def _():
            done(feat_part(t))

        pit = jnp.maximum(it - 1, 0)
        pd = lax.div(pit, NT)
        pt = lax.rem(pit, NT)
        adds = []
        for u in range(UN):
            adds.append(dot(wall[pd, pl.ds(0, hid), :], mi[pd, :, lanes_at(pt * UN + u, TILE)]))
        for u in range(UN):
            n = lanes_at(t * UN + u, TILE)
            f = fx[d, :, n]
            z = dot(wl[d], jnp.concatenate([f, f], axis=0))
            k = keep[d, :, n]
            k = jnp.concatenate([k] * 4, axis=0)
            for i in range(0, hid, 64):
                g1, d1 = scaled_gelu_slope(z[i : i + 64].astype(BF16))
                g2, d2 = scaled_gelu_slope(g1 * k)
                mi[d, pl.ds(i, 64), n] = g2
                gp[d, pl.ds(i, 64), n] = d1 * d2 * k
        for u in range(UN):
            n = lanes_at(pt * UN + u, TILE)
            mixed[:, n] = mixed[:, n] + adds[u]

        @pl.when(jnp.logical_and(pd == HOPS - 1, it > pit))
        def _():
            block_sums(pt)


    @pl.loop(0, UN)
    def _(u):
        n = lanes_at((NT - 1) * UN + u, TILE)
        mixed[:, n] = mixed[:, n] + dot(wall[HOPS - 1, pl.ds(0, hid), :], mi[HOPS - 1, :, n])

    block_sums(NT - 1)

    def natural(lo, hi):
        @pl.loop(lo * (hid // 128), hi * (hid // 128))
        def _(i):
            d = lax.div(i, hid // 128)
            k = lanes_at(lax.rem(i, hid // 128), 128)
            wmx[d, k, :] = wall[d, pl.ds(0, hid), k].astype(F32).T.astype(BF16)

    s2h[h, :, pl.ds(0, hid)] = row_of(acc0[...])
    s2h[h, :, pl.ds(hid, hid)] = row_of(acc1[...])
    hops_start(s2h, "s2h")
    natural(0, 2)
    hops_wait(s2h, "s2h")
    s2r[r] = total(s2h, HOPS)
    rows_start(s2r, "s2r")
    natural(2, HOPS)
    wc48 = wcs[pl.ds(0, 48), :].astype(BF16)
    wcNs[...] = wcs[...].T.astype(BF16)
    crow = lax.broadcasted_iota(jnp.int32, (128, 128), 0)
    cbc = jnp.where(crow < ncls, jnp.broadcast_to(cbs[pl.ds(0, 1), :], (128, 128)).T, -1e30)[:48]
    rows_wait(s2r, "s2r")
    st2 = total(s2r, R)
    mean2 = st2[:, :hid] * inv_n
    inv2 = lax.rsqrt(st2[:, hid:] * inv_n - mean2 * mean2 + EPS * 4.0 * KAPPA * KAPPA)
    scale2 = inv2 * gain2[...]
    cols[0] = col_of(scale2 * KAPPA)
    cols[1] = col_of((bias2[...] - mean2 * scale2) * KAPPA)
    acc0[...] = jnp.zeros(acc0.shape, F32)
    acc1[...] = jnp.zeros(acc1.shape, F32)
    accl[...] = jnp.zeros(accl.shape, F32)
    accw[...] = jnp.zeros(accw.shape, F32)

    o_own = lanes_at(h, sub)

    def lp_copy(d):
        return rc(lps, o_lp.at[:, o_own], "lp", d, peer(d), r)

    dlp[...] = jnp.zeros(dlp.shape, BF16)
    HR = 128

    @pl.loop(0, NB)
    def _(t):
        n = lanes_at(t, wide)

        @pl.loop(0, hid // HR)
        def _(i):
            rows = lanes_at(i, HR)
            y2 = mixed[rows, n] * spread(cols[0, rows, :], wide) + spread(cols[1, rows, :], wide)
            gv, dg = scaled_gelu_slope(y2.astype(BF16))
            hb[rows, :] = (gv.astype(F32) * (0.5 / KAPPA)).astype(BF16)
            hs[rows, :] = dg

        lg = dot(wc48, hb[...]) + spread(cbc, wide)
        lg = lg - jnp.max(lg, axis=0, keepdims=True)
        ex = jnp.exp(lg)
        se = jnp.sum(ex, axis=0, keepdims=True)
        lp = lg - jnp.log(se)
        lps[:, n] = lp.astype(BF16)
        own = lanes_at(h * NB + t, wide)
        hit = lax.broadcasted_iota(jnp.int32, (48, wide), 0) == lab[:, own]
        accl[pl.ds(48, 48), :] += fold(jnp.where(hit, lp, 0.0))
        dl = ((ex / se - jnp.where(hit, 1.0, 0.0)) * inv_n).astype(BF16)
        accl[pl.ds(0, 48), :] += fold(dl.astype(F32))
        accw[...] += dot_nt(dl, hb[...])
        dlp[pl.ds(0, 48), :] = dl * 0.5

        @pl.loop(0, hid // HR)
        def _(i):
            rows = lanes_at(i, HR)
            dn = dot(wcNs[rows, :], dlp[...]) * hs[rows, :].astype(F32)
            dn2[rows, n] = dn
            acc0[rows, :] += fold(dn * mixed[rows, n])
            acc1[rows, :] += fold(dn)

    own_lp = pltpu.make_async_copy(lps, o_lp.at[:, o_own], ss.at[names["lp"]])
    own_lp.start()
    s3h[h, :, pl.ds(0, hid)] = row_of(acc0[...])
    s3h[h, :, pl.ds(hid, hid)] = row_of(acc1[...])
    zpad = jnp.zeros((80, 128), F32)
    s3h[h, :, pl.ds(2 * hid, 128)] = row_of(jnp.concatenate([accl[pl.ds(0, 48), :], zpad], axis=0))
    s3h[h, :, pl.ds(2 * hid + 128, 128)] = row_of(jnp.concatenate([accl[pl.ds(48, 48), :], zpad], axis=0))
    hops_start(s3h, "s3h")

    def cwh_copy(d):
        return rc(cwp.at[d], cwh.at[d], "cwh", d, peer(d), r)

    q = hid // HOPS

    @pl.loop(0, HOPS)
    def _(d):
        cwp[d] = accw[:, lanes_at(peer(d), q)].astype(BF16)

    hops_wait(s3h, "s3h")
    s3r[r] = total(s3h, HOPS)
    rows_start(s3r, "s3r")

    @pl.loop(1, HOPS)
    def _(d):
        cwh_copy(d).start()

    lp_copy(first).start()
    lp_copy(second).start()
    lp_copy(HOPS - 1).start()
    rows_wait(s3r, "s3r")
    st3 = total(s3r, R)
    db2 = st3[:, hid : 2 * hid]
    dg2t = inv2 * (st3[:, :hid] - mean2 * db2)
    o_small[pl.ds(0, 1), :] = dg2t
    o_small[pl.ds(1, 1), :] = db2
    o_small[pl.ds(4, 1), pl.ds(0, 256)] = st3[:, 2 * hid : 2 * hid + 256]
    o_small[pl.ds(4, 1), pl.ds(256, hid - 256)] = jnp.zeros((1, hid - 256), F32)
    t2 = scale2 * inv2 * dg2t * inv_n
    cols[0] = col_of(scale2)
    cols[1] = col_of(-t2)
    cols[2] = col_of(t2 * mean2 - scale2 * db2 * inv_n)

    @pl.loop(0, hid // 16)
    def _(i):
        rows = lanes_at(i, 16)
        v = dn2[rows, :] * spread(cols[0, rows, :], sub)
        v = v + mixed[rows, :] * spread(cols[1, rows, :], sub) + spread(cols[2, rows, :], sub)
        dmx[rows, :] = v.astype(BF16)

    @functools.partial(each, 1, Z)
    def _(e):
        gz_copy(e, zi).wait_send()
        gz_copy(e, lax.rem(zi + Z - e, Z)).wait_recv()

    gfin[c] = total(gz, Z)
    gd_copy(c).start()

    mine = lanes_at(c, half)
    theirs = lanes_at(1 - c, half)

    def pair_copy(d):
        return rc(dmp.at[d, theirs, :], pr.at[d], "pair", d, h, sib)

    qrows = half // S
    zown = pl.ds(pl.multiple_of(c * half + zpar * qrows, 16), qrows)
    zother = pl.ds(pl.multiple_of(c * half + (1 - zpar) * qrows, 16), qrows)

    def z1_copy(d):
        return rc(dmp.at[d, zother, :], z1r.at[d], "z1", d, h, 2 * zmate + c)

    def z1_start(d):
        if S > 1:
            z1_copy(d).start()

    def z1_sum(d):
        if S > 1:
            done(z1_copy(d))

            @pl.loop(0, qrows // 32)
            def _(i):
                rows = pl.ds(pl.multiple_of(c * half + zpar * qrows + i * 32, 32), 32)
                dmp[d, rows, :] = (dmp[d, rows, :].astype(F32) + z1r[d, lanes_at(i, 32), :].astype(F32)).astype(BF16)

    def hop_copy(d):
        return rc(dmp.at[d, zown, :], hr.at[d], "hop", d, peer(d), r)

    def pair_sum(d):
        done(pair_copy(d))

        @pl.loop(0, half // 32)
        def _(i):
            rows = pl.ds(pl.multiple_of(c * half + i * 32, 32), 32)
            dmp[d, rows, :] = (dmp[d, rows, :].astype(F32) + pr[d, lanes_at(i, 32), :].astype(F32)).astype(BF16)

    def mix_grad(d):
        dmp[d] = dot_nt(mi[d], dmx[...]).astype(BF16)
        pair_copy(d).start()

    def mix_grads(lo):
        @pl.loop(0, 2)
        def _(i):
            mix_grad(lo + 1 - i)

        pair_sum(lo + 1)
        z1_start(lo + 1)

    def mix_hop(d):
        z1_sum(d)
        hop_copy(d).start()

    mix_grads(2)

    G2 = Z // S
    zq = lax.div(zi, S)

    def zr_copy(e, which):
        rows, lanes = chunk(0, which, qrows, G2, hid)
        return rc(hr.at[0, rows, lanes], zr.at[e], "zr", e, h, (lax.rem(zq + e, G2) * S + zpar) * 2 + c)

    def final_chunk(z):
        return chunk(c * half + lax.rem(z, S) * qrows, lax.div(z, S), qrows, G2, hid)

    def zg_copy(e, which):
        rows, lanes = final_chunk(which)
        ref = fin.at[rows, lanes]
        return rc(ref, ref, "zg", e, h, lax.rem(zi + e, Z) * 2 + c)

    def ddm_copy(core):
        ref = fin.at[lanes_at(core, half), :]
        return rc(ref, ref, "ddm", 0, h, sib)

    def d_copy(d):
        return rc(dsend.at[d], o_d.at[h], "d", d, peer(d), r)

    def dt_copy(d):
        return rc(dtail.at[d], o_dt.at[h], "dt", d, peer(d), r)

    def pp_copy(d):
        return rc(ps.at[d, :, theirs], ph.at[d], "pp", d, h, sib)

    def p_copy(d):
        return rc(phalf.at[d], prv.at[d], "p", d, peer(d), r)

    def p_half(d):
        done(pp_copy(d))
        phalf[d] = (ps[d, :, mine].astype(F32) + ph[d].astype(F32)).astype(BF16)

    def q_copy(d):
        return rc(qs.at[d], qv.at[d], "q", d, peer(d), r)

    @pl.loop(0, HOPS * NB)
    def _(it):
        dd = lax.div(it, NB)
        t = lax.rem(it, NB)
        d = HOPS - 1 - dd

        @pl.when(t == 0)
        def _():
            pT[...] = jnp.zeros(pT.shape, F32)

        n = lanes_at(t, wide)
        dn = dot(wmx[d], dmx[:, n]).astype(BF16) * gp[d, :, n]

        @pl.when(jnp.logical_and(t == NB // 2, dd > 0))
        def _():
            p_half(d + 1)
            p_copy(d + 1).start()

            @pl.when(dd > 1)
            def _():
                dt_copy(d + 1).start()
                d_copy(d + 1).start()


        @pl.when(it == NB // 2)
        def _():
            pair_sum(2)
            z1_start(2)

        @pl.when(it == NB + NB // 2)
        def _():
            @pl.loop(1, HOPS)
            def _(j):
                done(cwh_copy(j))

            cw = cwp[0].astype(F32)
            for j in range(1, HOPS):
                cw = cw + cwh[j].astype(F32)
            cwr[r] = cw.astype(BF16)
            rows_start(cwr, "cwr")
            pair_sum(0)
            z1_start(0)
            mix_hop(2)

        @pl.when(it == 2 * NB + NB // 2)
        def _():
            mix_hop(1)
            rows_wait(cwr, "cwr")
            cwg[h] = total(cwr, R, F32).astype(BF16)
            hops_start(cwg, "cwg")

        @pl.when(it == 3 * NB + NB // 2)
        def _():
            z1_sum(0)

            @pl.loop(1, HOPS)
            def _(j):
                done(hop_copy(j))

            @pl.loop(0, qrows // 32)
            def _(i):
                rows = lanes_at(i, 32)
                own = pl.ds(pl.multiple_of(c * half + zpar * qrows + i * 32, 32), 32)
                hsum = dmp[0, own, :].astype(F32)
                for j in range(1, HOPS):
                    hsum = hsum + hr[j, rows, :].astype(F32)
                hr[0, rows, :] = hsum.astype(BF16)

            @functools.partial(each, 1, G2)
            def _(e):
                zr_copy(e, lax.rem(zq + e, G2)).start()

            hops_wait(cwg, "cwg")
            for j in range(HOPS):
                o_cw[:, pl.ds(j * q, q)] = cwg[j].astype(F32)

        pT[...] += dot_nt(dn, fx[d, :, n])
        grad = dot(aw[d], dn)
        dsend[d, :, n] = grad[:MAIN].astype(BF16)
        d4[:, n] = grad[MAIN : MAIN + 8]

        @pl.when(it == HOPS * NB - 1)
        def _():
            @functools.partial(each, 1, G2)
            def _(e):
                done(zr_copy(e, lax.rem(zq + e, G2)))

            rows, lanes = chunk(0, zq, qrows, G2, hid)
            zt = lax.fori_loop(1, G2, lambda e, v: v + zr[e].astype(F32), hr[0, rows, lanes].astype(F32))
            frows, flanes = final_chunk(zi)
            fin[frows, flanes] = zt.astype(BF16)

            @functools.partial(each, 1, Z)
            def _(e):
                zg_copy(e, zi).start()

        @pl.when(t == NB - 1)
        def _():
            pw = pT[...].T * KAPPA
            qs[d, :, pl.ds(0, hid)] = jnp.sum(pw * wall[d, wrow, :].astype(F32), axis=0, keepdims=True)
            qs[d, :, pl.ds(hid, hid)] = pw[ONES : ONES + 1, :]
            ps[d] = pw[:FP].astype(BF16)
            pp_copy(d).start()
            pack4(d4, dtail.at[d])

            @pl.when(dd < HOPS - 1)
            def _():
                q_copy(d).start()

            @pl.when(dd == 0)
            def _():
                dt_copy(d).start()
                d_copy(d).start()
                mix_hop(d)
                mix_grads(0)

    @pl.loop(1, HOPS)
    def _(d):
        done(q_copy(d))

    qr[r] = qs[0] + (qv[1] + qv[2] + qv[3])
    rows_start(qr, "qr")
    own_d = pltpu.make_async_copy(dsend.at[0], o_d.at[h], ss.at[names["d"]])
    own_d.start()
    own_dt = pltpu.make_async_copy(dtail.at[0], o_dt.at[h], ss.at[names["dt"]])
    own_dt.start()

    p_half(0)

    @pl.loop(1, HOPS)
    def _(d):
        done(p_copy(d))

    psum = phalf[0].astype(F32) + (prv[1].astype(F32) + prv[2].astype(F32) + prv[3].astype(F32))
    pz[zi] = psum.astype(BF16)

    def pz_copy(e, which):
        return rc(pz.at[which], pz.at[which], "pz", e, h, lax.rem(zi + e, Z) * 2 + c)

    @functools.partial(each, 1, Z)
    def _(e):
        pz_copy(e, zi).start()

    @functools.partial(each, 1, Z)
    def _(e):
        zg_copy(e, zi).wait_send()
        zg_copy(e, lax.rem(zi + Z - e, Z)).wait_recv()

    ddm_copy(c).start()

    rows_wait(qr, "qr")
    qt = total(qr, R)
    db = qt[:, hid:]
    dgn = inv * (qt[:, :hid] - mean * db)
    o_small[pl.ds(2, 1), :] = dgn
    o_small[pl.ds(3, 1), :] = db
    c1 = scale * db * inv_n
    c2 = inv * scale * dgn * inv_n
    shift = c1 - mean * c2
    row = lax.broadcasted_iota(jnp.int32, (128, hid), 0)
    q1, q2 = split2(jnp.where(row == ONES, shift, wown32 * c2))
    o_m[...] = (dot_nt(wown, q1) + dot_nt(wown, q2))[:FP]
    gd_copy(c).wait_send()
    gd_copy(1 - c).wait_recv()
    g1, g2, g3 = split3(jnp.concatenate([gfin[0], gfin[1]], axis=0))
    gq = dot(g1, q1) + dot(g2, q1) + dot(g3, q1) + dot(g1, q2) + dot(g2, q2)

    @functools.partial(each, 1, Z)
    def _(e):
        pz_copy(e, zi).wait_send()
        pz_copy(e, lax.rem(zi + Z - e, Z)).wait_recv()

    pfin[c] = total(pz, Z).astype(BF16)

    def pd_copy(core):
        return rc(pfin.at[core], pfin.at[core], "pd", 0, h, sib)

    pd_copy(c).start()
    ddm_copy(c).wait_send()
    ddm_copy(1 - c).wait_recv()
    o_mix[...] = fin[...]

    pd_copy(c).wait_send()
    pd_copy(1 - c).wait_recv()
    ptot = jnp.concatenate([pfin[0], pfin[1]], axis=1).astype(F32)
    o_gw[...] = ptot * scale - gq[:FP]
    own_d.wait()
    own_dt.wait()
    own_lp.wait()

    @pl.loop(1, HOPS)
    def _(d):
        done(d_copy(d))
        done(dt_copy(d))
        done(lp_copy(d))


def last_kernel(
    nodes,
    ft, d, dt, lp, m, mix, gw, small, cw,
    o_lp, o_gf, o_mix, o_gw, o_gg, o_gb, o_hg, o_hb, o_cw, o_cb, o_loss, low,
):
    feat, n = ft.shape
    ncls = o_lp.shape[0]
    o_lp[...] = lp[...].astype(F32)[:ncls]
    mm = m[...]
    f = ft[...]
    fix = dot(mm[:, :feat].astype(BF16), f) + mm[:, ONES : ONES + 1]
    tail = dt[0].astype(F32)
    for b in range(4):
        low[pl.ds(0, 4), pl.ds(b * (n // 4), n // 4)] = tail[4 * b : 4 * b + 4]
    gf = jnp.concatenate([d[0].astype(F32), low[...]], axis=0)[:feat] - fix[:feat]
    if STRIDED:
        flat = o_gf.reshape(feat * (n // 128), 128)
        for i in range(n // 128):
            flat[pl.ds(i, feat, stride=n // 128), :] = gf[:, i * 128 : (i + 1) * 128]
    else:
        for i in range(n // 128):
            o_gf[:, i, :] = gf[:, i * 128 : (i + 1) * 128]

    @pl.when(pl.program_id(0) == 0)
    def _():
        hid = mix.shape[1]
        o_mix[...] = mix[...].astype(F32)
        for i in range(hid // 128):
            o_gw[:, i, :] = gw[pl.ds(0, feat), pl.ds(i * 128, 128)]
        o_hg[...] = small[pl.ds(0, 1), :]
        o_hb[...] = small[pl.ds(1, 1), :]
        o_gg[...] = small[pl.ds(2, 1), :]
        o_gb[...] = small[pl.ds(3, 1), :]
        o_cw[...] = cw[pl.ds(0, ncls), :]
        o_cb[...] = small[pl.ds(4, 1), pl.ds(0, ncls)]
        o_loss[...] = jnp.sum(small[pl.ds(4, 1), pl.ds(128, 128)], axis=1, keepdims=True) * (-1.0 / nodes)


def shards(
    R, features, branch_weight, branch_gain, branch_bias, mix_weight, mixing_norm_gain, mixing_norm_bias,
    class_weight, class_bias, labels, hop_mask,
):
    local, feat = features.shape[1:]
    hid = mix_weight.shape[0]
    ncls = class_weight.shape[1]
    nodes = local * R
    sub = local // HOPS
    Z = R // 2
    half = hid // 2
    S = min(Z, 2)
    G2, qrows = Z // S, half // S
    zrows, zcols = chunk(0, 0, qrows, G2, hid)
    assert feat == ONES and ncls == 47 and local // hop_mask.shape[0] == 128
    ft = features[0].T
    sd = jax.ShapeDtypeStruct
    vm = pl.BlockSpec(memory_space=pltpu.VMEM)
    hbm = pl.BlockSpec(memory_space=pl.ANY)
    _, nsem = sem_plan(R)
    V = pltpu.VMEM
    outs = pl.pallas_call(
        functools.partial(main_kernel, R, nodes),
        grid=(1,),
        out_shape=(
            sd((48, local), BF16),
            sd((HOPS, MAIN, sub), BF16),
            sd((HOPS, 16, sub // 4), BF16),
            sd((FP, 128), F32),
            sd((hid, hid), BF16),
            sd((FP, hid), F32),
            sd((8, hid), F32),
            sd((48, hid), F32),
        ),
        in_specs=[hbm, pl.BlockSpec((16, local), lambda i: (MAIN // 16, 0))]
        + [vm] * 9
        + [pl.BlockSpec(memory_space=pltpu.SMEM)],
        out_specs=(hbm, hbm, hbm, vm, vm, vm, vm, vm),
        scratch_shapes=[
            V((128, local), BF16),
            V((HOPS, 128, sub), BF16),
            V((HOPS, 16, sub // 4), BF16),
            V((HOPS, 16, sub // 4), BF16),
            V((48, sub // 4), F32),
            V((HOPS, hid + 128, hid), BF16),
            V((HOPS, hid, 256), BF16),
            V((HOPS, FP, hid), BF16),
            V((HOPS, hid, hid), BF16),
            V((HOPS, 16, sub), BF16),
            V((HOPS, hid, sub), BF16),
            V((HOPS, hid, sub), BF16),
            V((hid, sub), F32),
            V((hid, sub), F32),
            V((hid, sub), BF16),
            V((128, 128), F32),
            V((64, 128), F32),
            V((Z, 64, 128), F32),
            V((2, 64, 128), F32),
            V((R, 1, 2 * hid), F32),
            V((HOPS, 1, 2 * hid), F32),
            V((HOPS, 1, 2 * hid), F32),
            V((R, 1, 2 * hid), F32),
            V((HOPS, 1, 2 * hid + 256), F32),
            V((R, 1, 2 * hid + 256), F32),
            V((HOPS, 48, hid // HOPS), BF16),
            V((HOPS, 48, hid // HOPS), BF16),
            V((R, 48, hid // HOPS), BF16),
            V((HOPS, 48, hid // HOPS), BF16),
            V((48, sub), BF16),
            V((128, hid), F32),
            V((hid, 128), BF16),
            V((8, 128), F32),
            V((hid, min(8 * TILE, sub)), BF16),
            V((hid, min(8 * TILE, sub)), BF16),
            V((128, min(8 * TILE, sub)), BF16),
            V((hid, 128), F32),
            V((hid, 128), F32),
            V((96, 128), F32),
            V((48, hid), F32),
            V((3, hid, 128), F32),
            V((HOPS, hid, hid), BF16),
            V((HOPS, half, hid), BF16),
            V((HOPS, qrows, hid), BF16),
            V((HOPS, qrows, hid), BF16),
            V((max(G2, 2), zrows.size, zcols.size), BF16),
            V((hid, hid), BF16),
            V((HOPS, MAIN, sub), BF16),
            V((8, sub), F32),
            V((HOPS, 16, sub // 4), BF16),
            V((hid, 128), F32),
            V((HOPS, FP, hid), BF16),
            V((HOPS, FP, half), BF16),
            V((HOPS, FP, half), BF16),
            V((HOPS, FP, half), BF16),
            V((HOPS, 1, 2 * hid), F32),
            V((HOPS, 1, 2 * hid), F32),
            V((R, 1, 2 * hid), F32),
            V((Z, FP, half), BF16),
            V((2, FP, half), BF16),
            pltpu.SemaphoreType.DMA((nsem,)),
            pltpu.SemaphoreType.DMA((nsem,)),
        ],
        compiler_params=pltpu.CompilerParams(
            collective_id=0, has_side_effects=True, vmem_limit_bytes=63 * 1024 * 1024
        ),
        cost_estimate=pl.CostEstimate(flops=2 * 8 * 10**9, bytes_accessed=10**7, transcendentals=10**7),
        name="main",
    )(
        ft, ft, branch_weight[0], branch_gain, branch_bias, mix_weight, mixing_norm_gain[None], mixing_norm_bias[None],
        class_weight.T, class_bias[None], labels[None], hop_mask.T,
    )
    lp, dd, dt, m, mix, gw, small, cw = outs
    nb = sub
    whole = lambda shape: pl.BlockSpec(shape, lambda i: (0,) * len(shape))
    lp, gf, mix, gw, gg, gb, hg, hb, cw, cb, loss = pl.pallas_call(
        functools.partial(last_kernel, nodes),
        grid=(local // nb,),
        out_shape=(
            sd((ncls, local), F32),
            sd((feat, local // 128, 128), F32),
            sd((hid, hid), F32),
            sd((feat, hid // 128, 128), F32),
            sd((1, hid), F32),
            sd((1, hid), F32),
            sd((1, hid), F32),
            sd((1, hid), F32),
            sd((ncls, hid), F32),
            sd((1, ncls), F32),
            sd((1, 1), F32),
        ),
        in_specs=[
            pl.BlockSpec((feat, nb), lambda i: (0, i)),
            pl.BlockSpec((1, MAIN, nb), lambda i: (i, 0, 0)),
            pl.BlockSpec((1, 16, nb // 4), lambda i: (i, 0, 0)),
            pl.BlockSpec((48, nb), lambda i: (0, i)),
            whole((FP, 128)),
            whole((hid, hid)),
            whole((FP, hid)),
            whole((8, hid)),
            whole((48, hid)),
        ],
        out_specs=(
            pl.BlockSpec((ncls, nb), lambda i: (0, i)),
            pl.BlockSpec((feat, nb // 128, 128), lambda i: (0, i, 0)),
            whole((hid, hid)),
            whole((feat, hid // 128, 128)),
            whole((1, hid)),
            whole((1, hid)),
            whole((1, hid)),
            whole((1, hid)),
            whole((ncls, hid)),
            whole((1, ncls)),
            whole((1, 1)),
        ),
        scratch_shapes=[V((8, nb), F32)],
        compiler_params=pltpu.CompilerParams(vmem_limit_bytes=60 * 1024 * 1024),
        name="last",
    )(ft, dd, dt, lp, m, mix, gw, small, cw)
    return (
        lp.T,
        loss[0, 0],
        with_layout_constraint(gf.reshape(feat, 1, local), Layout((0, 1, 2))).transpose(1, 2, 0),
        gw.reshape(1, feat, hid),
        gg,
        gb,
        mix,
        hg[0],
        hb[0],
        cw.T,
        cb[0],
    )


def solution(mesh):
    placed = (
        P("hop", "rows", None), P("hop", None, None), P("hop", None), P("hop", None), P("hop", None),
        P(), P(), P(), P(), P("rows"), P("rows", None),
    )
    assert mesh.shape["hop"] == HOPS
    return jax.shard_map(
        functools.partial(shards, mesh.shape["rows"]),
        mesh=mesh,
        in_specs=placed,
        out_specs=(
            P("rows", None), P(), P("hop", "rows", None), P("hop", None, None), P("hop", None), P("hop", None),
            P("hop", None), P(), P(), P(), P(),
        ),
        check_vma=False,
    )
```

```python
import functools
import math

import jax
import jax.numpy as jnp
from jax import lax
from jax.experimental import pallas as pl
from jax.experimental.layout import Layout, with_layout_constraint
from jax.experimental.pallas import tpu as pltpu
from jax.sharding import PartitionSpec as P

MESH = pl.DeviceIdType.MESH
EPS = 1e-05
HOPS = 4
ONES = 100
FP = 112
MAIN = 96
TILE = 512
STRIDED = True
C0 = math.sqrt(2.0 / math.pi)
C1 = C0 * 0.044715
KAPPA = C1 ** (1.0 / 3.0)
ALPHA = C0 / KAPPA
F32 = jnp.float32
BF16 = jnp.bfloat16


def dot(a, b):
    return lax.dot_general(a, b, (((1,), (0,)), ((), ())), preferred_element_type=F32)


def dot_nt(a, b):
    return lax.dot_general(a, b, (((1,), (1,)), ((), ())), preferred_element_type=F32)


def split2(x):
    hi = x.astype(BF16)
    return hi, (x - hi.astype(F32)).astype(BF16)


def split3(x):
    hi = x.astype(BF16)
    rest = x - hi.astype(F32)
    mid = rest.astype(BF16)
    return hi, mid, (rest - mid.astype(F32)).astype(BF16)


def scaled_gelu_slope(y):
    u = y * y
    t = jnp.tanh(y * (u + ALPHA))
    up = t + 1.0
    g = y * up
    return g, up + (g * (1.0 - t)) * (3.0 * u + ALPHA)


def fold(x):
    total = x[:, :128]
    for i in range(1, x.shape[1] // 128):
        total = total + x[:, i * 128 : (i + 1) * 128]
    return total


def spread(c, n):
    return jnp.concatenate([c] * (n // 128), axis=1)


def row_of(acc):
    return jnp.sum(acc.T, axis=0, keepdims=True)


def col_of(row):
    return jnp.broadcast_to(row, (128, row.shape[1])).T


def each(lo, hi, body):
    if hi - lo == 1:
        body(lo)
    elif hi > lo:
        pl.loop(lo, hi)(body)


class Alloc:
    def __init__(self):
        self.n = 0

    def __call__(self, count):
        base = self.n
        self.n += count
        return base


def sem_plan(R):
    Z = R // 2
    a = Alloc()
    names = {}
    for name, count in (
        ("feat", 7), ("ft", 4), ("loc", 1), ("ws", 4), ("zf", 4), ("dd", 4), ("s1", R), ("ab", 4), ("gp", 1), ("gz", Z), ("gd", 1),
        ("s2h", 4), ("s2r", R), ("s3h", 4), ("s3r", R), ("lp", 4), ("cwh", 4), ("cwr", R), ("cwg", 4),
        ("pair", 4), ("z1", 4), ("hop", 4), ("zr", Z), ("zg", Z), ("ddm", 1), ("d", 4), ("dt", 4), ("p", 4), ("q", 4),
        ("qr", R), ("pp", 4), ("pz", Z), ("pd", 1),
    ):
        names[name] = a(count)
    return names, a.n


def chunk(base, i, rows, pieces, cols):
    if rows // pieces >= 16:
        take = rows // pieces
        return pl.ds(pl.multiple_of(base + i * take, 16), take), pl.ds(0, cols)
    m = 16 * pieces // rows
    wide = cols // m
    return (
        pl.ds(pl.multiple_of(base + (i // m) * 16, 16), 16),
        pl.ds(pl.multiple_of((i % m) * wide, 128), wide),
    )


def main_kernel(
    R,
    nodes,
    ft, ft4, wb, bgain, bbias, wm, gain2, bias2, wc, cb, lab, msk,
    o_lp, o_d, o_dt, o_m, o_mix, o_gw, o_small, o_cw,
    fs, fx, ftail, frt, st4, wall, wl, aw, wmx, keep, mi, gp, mixed, dn2, dmx,
    gown, gpr, gz, gfin, s1, ab, s2h, s2r, s3h, s3r, cwp, cwh, cwr, cwg, lps,
    wcs, wcNs, cbs, hb, hs, dlp, acc0, acc1, accl, accw, cols,
    dmp, pr, z1r, hr, zr, fin, dsend, d4, dtail, pT, ps, ph, phalf, prv, qs, qv, qr, pz, pfin,
    ss, rs,
):
    names, _ = sem_plan(R)
    Z = R // 2
    h = lax.axis_index("hop")
    r = lax.axis_index("rows")
    c = lax.rem(r, 2)
    zi = lax.div(r, 2)
    sib = r + 1 - 2 * c
    local = ft.shape[1]
    sub = local // HOPS
    hid = wm.shape[0]
    half = hid // 2
    big = min(2 * TILE, sub)
    UN = big // TILE
    NT = sub // big
    inv_n = 1.0 / nodes

    def peer(d):
        x = lax.rem(h + d, 2)
        y = lax.rem(lax.div(h, 2) + lax.div(d, 2), 2)
        return 2 * y + x

    def rc(src, dst, name, i, hh, rr):
        return pltpu.make_async_remote_copy(
            src_ref=src, dst_ref=dst, send_sem=ss.at[names[name] + i], recv_sem=rs.at[names[name] + i],
            device_id=(hh, rr), device_id_type=MESH,
        )

    def done(cp):
        cp.wait_send()
        cp.wait_recv()

    def lanes_at(i, n):
        return pl.ds(pl.multiple_of(i * n, n), n)

    barrier = pltpu.get_barrier_semaphore()

    def greet(hh, rr):
        pl.semaphore_signal(barrier, inc=1, device_id=(hh, rr), device_id_type=MESH)

    @pl.loop(1, HOPS)
    def _(d):
        greet(peer(d), r)

    @functools.partial(each, 1, R)
    def _(e):
        greet(h, lax.rem(r + e, R))

    def rows_start(buf, name):
        @functools.partial(each, 1, R)
        def _(e):
            rc(buf.at[r], buf.at[r], name, e, h, lax.rem(r + e, R)).start()

    def rows_wait(buf, name):
        @functools.partial(each, 1, R)
        def _(e):
            src = lax.rem(r + R - e, R)
            done(rc(buf.at[src], buf.at[src], name, e, h, lax.rem(r + e, R)))

    def hops_start(buf, name):
        @pl.loop(1, HOPS)
        def _(d):
            rc(buf.at[h], buf.at[h], name, d, peer(d), r).start()

    def hops_wait(buf, name):
        @pl.loop(1, HOPS)
        def _(d):
            done(rc(buf.at[peer(d)], buf.at[peer(d)], name, d, peer(d), r))

    def total(buf, n, dtype=F32):
        return lax.fori_loop(1, n, lambda i, t: t + buf[i].astype(dtype), buf[0].astype(dtype))

    loc = pltpu.make_async_copy(ft.at[pl.ds(0, MAIN), :], fs.at[pl.ds(0, MAIN), :], ss.at[names["loc"]])
    loc.start()

    def pack4(src, dst):
        n = st4.shape[1]
        for b in range(4):
            st4[pl.ds(4 * b, 4), :] = src[pl.ds(0, 4), pl.ds(b * n, n)].astype(F32)
        dst[...] = st4[pl.ds(0, 16), :].astype(BF16)

    def unpack4(src, dst):
        n = st4.shape[1]
        row = lax.broadcasted_iota(jnp.int32, (32, n), 0)
        st4[pl.ds(0, 16), :] = src[...].astype(F32)
        st4[pl.ds(16, 32), :] = jnp.where(row == ONES - MAIN, 1.0, 0.0)
        for b in range(4):
            st4[pl.ds(16, 4), :] = st4[pl.ds(4 * b, 4), :]
            dst[pl.ds(MAIN, 32), pl.ds(b * n, n)] = st4[pl.ds(16, 32), :].astype(BF16)

    wrow = pl.ds(hid, 128)
    wall[0, pl.ds(hid + 96, 32), :] = jnp.zeros((32, hid), BF16)
    wall[0, pl.ds(hid, 100), :] = wb[...]

    @pl.loop(0, hid // 128)
    def _(i):
        k = lanes_at(i, 128)
        wall[0, pl.ds(0, hid), k] = wm[k, :].astype(F32).T.astype(BF16)

    def feat_copy(d):
        rows = pl.ds(0, MAIN)
        return rc(fs.at[rows, lanes_at(peer(d), sub)], fx.at[d, rows, :], "feat", d, peer(d), r)

    def feat_part(p):
        rows = pl.ds(0, MAIN)
        d = HOPS - 1
        return rc(
            fs.at[rows, lanes_at(NT * peer(d) + p, big)], fx.at[d, rows, lanes_at(p, big)], "feat", d + p, peer(d), r
        )

    def ft_copy(d):
        return rc(ftail.at[peer(d)], frt.at[d], "ft", d, peer(d), r)

    pl.semaphore_wait(barrier, HOPS - 1 + R - 1)

    S = min(Z, 2)
    part = (hid + 128) // (2 * S)
    zpar = lax.rem(zi, S)
    zmate = zi + (S - 1) - 2 * (S - 1) * zpar

    def part_rows(core, par):
        return pl.ds(pl.multiple_of((core * S + par) * part, 16), part)

    def ws_copy(d):
        rows = part_rows(c, zpar)
        return rc(wall.at[0, rows, :], wall.at[d, rows, :], "ws", d, peer(d), r)

    def zf_copy(d, par):
        ref = wall.at[d, part_rows(c, par), :]
        return rc(ref, ref, "zf", d, h, 2 * zmate + c)

    def dd_copy(d, core):
        ref = wall.at[d, pl.ds(pl.multiple_of(core * S * part, 16), S * part), :]
        return rc(ref, ref, "dd", d, h, sib)

    first, second = 1 + c, 2 - c
    ws_copy(first).start()
    ws_copy(second).start()
    ws_copy(HOPS - 1).start()
    loc.wait()
    feat_copy(first).start()
    feat_copy(second).start()

    @pl.loop(0, HOPS)
    def _(j):
        lanes = lanes_at(j, sub)
        pack4(ft4.at[:, lanes], ftail.at[j])
        unpack4(ftail.at[j], fs.at[:, lanes])


    @pl.loop(1, HOPS)
    def _(d):
        ft_copy(d).start()

    fx0 = pltpu.make_async_copy(fs.at[:, lanes_at(h, sub)], fx.at[0], ss.at[names["loc"]])
    fx0.start()

    def gram(i, g):
        f = fs[:, lanes_at(i, sub)]
        return g + dot_nt(f, f)

    g = lax.fori_loop(0, HOPS, gram, jnp.zeros((128, 128), F32))
    wown = wall[0, wrow, :]
    wown32 = wown.astype(F32)
    g1, g2, g3 = split3(g)
    gw = dot(g1, wown) + dot(g2, wown) + dot(g3, wown)
    s1[r, :, pl.ds(0, hid)] = gw[ONES : ONES + 1, :]
    s1[r, :, pl.ds(hid, hid)] = jnp.sum(gw * wown32, axis=0, keepdims=True)
    rows_start(s1, "s1")
    gown[...] = g

    @pl.loop(0, HOPS * (sub // 128))
    def _(i):
        d = lax.div(i, sub // 128)
        b = lax.rem(i, sub // 128)
        late = peer(d) - 2
        m = jnp.where(late >= 0, msk[jnp.maximum(late, 0), h * (sub // 128) + b], 1)
        keep[d, :, lanes_at(b, 128)] = jnp.full((16, 128), 0.5 * m.astype(F32)).astype(BF16)

    wcs[...] = jnp.zeros(wcs.shape, F32)
    wcs[pl.ds(0, wc.shape[0]), :] = wc[...].astype(F32)
    cbs[...] = jnp.zeros(cbs.shape, F32)
    cbs[pl.ds(0, 1), pl.ds(0, cb.shape[1])] = cb[...]
    ncls = wc.shape[0]

    @pl.loop(0, hid // 16)
    def _(i):
        rows = lanes_at(i, 16)
        mixed[rows, :] = jnp.zeros((16, sub), F32)
        mi[0, rows, pl.ds(0, big)] = jnp.zeros((16, big), BF16)

    fx0.wait()

    rows_wait(s1, "s1")
    st = total(s1, R)
    mean = st[:, :hid] * inv_n
    var = st[:, hid:] * inv_n - mean * mean
    inv = lax.rsqrt(var + EPS)
    scale = inv * bgain[...]
    ab[0, :, pl.ds(0, hid)] = scale
    ab[0, :, pl.ds(hid, hid)] = bbias[...] - mean * scale

    def ab_copy(d):
        return rc(ab.at[0], ab.at[d], "ab", d, peer(d), r)

    @pl.loop(1, HOPS)
    def _(d):
        ab_copy(d).start()

    def prepare(d):
        a = ab[d, :, pl.ds(0, hid)]
        b = ab[d, :, pl.ds(hid, hid)]
        ws = wall[d, wrow, :].astype(F32) * (a * KAPPA)
        aw[d] = ws[:FP].astype(BF16)
        row = lax.broadcasted_iota(jnp.int32, (128, hid), 0)
        wt = jnp.where(row == ONES, b * KAPPA, ws).T
        hi, lo = split2(wt)
        wl[d, :, pl.ds(0, 128)] = hi
        wl[d, :, pl.ds(128, 128)] = lo

    g_pair = rc(gown.at[lanes_at(1 - c, 64), :], gpr, "gp", 0, h, sib)

    def gz_copy(e, which):
        return rc(gz.at[which], gz.at[which], "gz", e, h, lax.rem(zi + e, Z) * 2 + c)

    def gd_copy(core):
        return rc(gfin.at[core], gfin.at[core], "gd", 0, h, sib)

    acc0[...] = jnp.zeros(acc0.shape, F32)
    acc1[...] = jnp.zeros(acc1.shape, F32)

    def block_sums(t):
        @pl.loop(0, hid // 64)
        def _(i):
            rows = lanes_at(i, 64)
            x = mixed[rows, lanes_at(t, big)]
            acc0[rows, :] += fold(x)
            acc1[rows, :] += fold(x * x)

    @pl.loop(0, HOPS * NT)
    def _(it):
        d = lax.div(it, NT)
        t = lax.rem(it, NT)

        @pl.when(t == 0)
        def _():
            @pl.when(d > 0)
            def _():
                @pl.when(d < HOPS - 1)
                def _():
                    done(feat_copy(d))

                done(ft_copy(d))
                unpack4(frt.at[d], fx.at[d])
                dd_copy(d, c).wait_send()
                dd_copy(d, 1 - c).wait_recv()
                done(ab_copy(d))

            prepare(d)

        if S > 1:

            @pl.when(it == 0)
            def _():
                @pl.loop(1, HOPS)
                def _(j):
                    done(ws_copy(j))

                zf_copy(1, zpar).start()

        @pl.when(it == min(2, NT - 1))
        def _():
            @pl.loop(0, NT)
            def _(p):
                feat_part(p).start()

        @pl.when(jnp.logical_and(t == NT - 1, d < HOPS - 1))
        def _():
            if S > 1:
                zf_copy(d + 1, zpar).wait_send()
                zf_copy(d + 1, 1 - zpar).wait_recv()

                @pl.when(d < HOPS - 2)
                def _():
                    zf_copy(d + 2, zpar).start()

            else:
                done(ws_copy(d + 1))
            dd_copy(d + 1, c).start()

        @pl.when(it == 2 * NT)
        def _():
            g_pair.start()

        @pl.when(it == 3 * NT)
        def _():
            done(g_pair)
            gz[zi] = gown[lanes_at(c, 64), :] + gpr[...]

            @functools.partial(each, 1, Z)
            def _(e):
                gz_copy(e, zi).start()

        @pl.when(d == HOPS - 1)
        def _():
            done(feat_part(t))

        pit = jnp.maximum(it - 1, 0)
        pd = lax.div(pit, NT)
        pt = lax.rem(pit, NT)
        adds = []
        for u in range(UN):
            adds.append(dot(wall[pd, pl.ds(0, hid), :], mi[pd, :, lanes_at(pt * UN + u, TILE)]))
        for u in range(UN):
            n = lanes_at(t * UN + u, TILE)
            f = fx[d, :, n]
            z = dot(wl[d], jnp.concatenate([f, f], axis=0))
            k = keep[d, :, n]
            k = jnp.concatenate([k] * 4, axis=0)
            for i in range(0, hid, 64):
                g1, d1 = scaled_gelu_slope(z[i : i + 64].astype(BF16))
                g2, d2 = scaled_gelu_slope(g1 * k)
                mi[d, pl.ds(i, 64), n] = g2
                gp[d, pl.ds(i, 64), n] = d1 * d2 * k
        for u in range(UN):
            n = lanes_at(pt * UN + u, TILE)
            mixed[:, n] = mixed[:, n] + adds[u]

        @pl.when(jnp.logical_and(pd == HOPS - 1, it > pit))
        def _():
            block_sums(pt)


    @pl.loop(0, UN)
    def _(u):
        n = lanes_at((NT - 1) * UN + u, TILE)
        mixed[:, n] = mixed[:, n] + dot(wall[HOPS - 1, pl.ds(0, hid), :], mi[HOPS - 1, :, n])

    block_sums(NT - 1)

    def natural(lo, hi):
        @pl.loop(lo * (hid // 128), hi * (hid // 128))
        def _(i):
            d = lax.div(i, hid // 128)
            k = lanes_at(lax.rem(i, hid // 128), 128)
            wmx[d, k, :] = wall[d, pl.ds(0, hid), k].astype(F32).T.astype(BF16)

    s2h[h, :, pl.ds(0, hid)] = row_of(acc0[...])
    s2h[h, :, pl.ds(hid, hid)] = row_of(acc1[...])
    hops_start(s2h, "s2h")
    natural(0, 2)
    hops_wait(s2h, "s2h")
    s2r[r] = total(s2h, HOPS)
    rows_start(s2r, "s2r")
    natural(2, HOPS)
    wc48 = wcs[pl.ds(0, 48), :].astype(BF16)
    wcNs[...] = wcs[...].T.astype(BF16)
    crow = lax.broadcasted_iota(jnp.int32, (128, 128), 0)
    cbc = jnp.where(crow < ncls, jnp.broadcast_to(cbs[pl.ds(0, 1), :], (128, 128)).T, -1e30)[:48]
    rows_wait(s2r, "s2r")
    st2 = total(s2r, R)
    mean2 = st2[:, :hid] * inv_n
    inv2 = lax.rsqrt(st2[:, hid:] * inv_n - mean2 * mean2 + EPS * 4.0 * KAPPA * KAPPA)
    scale2 = inv2 * gain2[...]
    cols[0] = col_of(scale2 * KAPPA)
    cols[1] = col_of((bias2[...] - mean2 * scale2) * KAPPA)
    acc0[...] = jnp.zeros(acc0.shape, F32)
    acc1[...] = jnp.zeros(acc1.shape, F32)
    accl[...] = jnp.zeros(accl.shape, F32)
    accw[...] = jnp.zeros(accw.shape, F32)

    o_own = lanes_at(h, sub)

    def lp_copy(d):
        return rc(lps, o_lp.at[:, o_own], "lp", d, peer(d), r)

    dlp[...] = jnp.zeros(dlp.shape, BF16)
    HR = 128

    @pl.loop(0, NT)
    def _(t):
        n = lanes_at(t, big)

        @pl.loop(0, hid // HR)
        def _(i):
            rows = lanes_at(i, HR)
            y2 = mixed[rows, n] * spread(cols[0, rows, :], big) + spread(cols[1, rows, :], big)
            gv, dg = scaled_gelu_slope(y2.astype(BF16))
            hb[rows, :] = (gv.astype(F32) * (0.5 / KAPPA)).astype(BF16)
            hs[rows, :] = dg

        lg = dot(wc48, hb[...]) + spread(cbc, big)
        lg = lg - jnp.max(lg, axis=0, keepdims=True)
        ex = jnp.exp(lg)
        se = jnp.sum(ex, axis=0, keepdims=True)
        lp = lg - jnp.log(se)
        lps[:, n] = lp.astype(BF16)
        own = lanes_at(h * NT + t, big)
        hit = lax.broadcasted_iota(jnp.int32, (48, big), 0) == lab[:, own]
        accl[pl.ds(48, 48), :] += fold(jnp.where(hit, lp, 0.0))
        dl = ((ex / se - jnp.where(hit, 1.0, 0.0)) * inv_n).astype(BF16)
        accl[pl.ds(0, 48), :] += fold(dl.astype(F32))
        accw[...] += dot_nt(dl, hb[...])
        dlp[pl.ds(0, 48), :] = dl * 0.5

        @pl.loop(0, hid // HR)
        def _(i):
            rows = lanes_at(i, HR)
            dn = dot(wcNs[rows, :], dlp[...]) * hs[rows, :].astype(F32)
            dn2[rows, n] = dn
            acc0[rows, :] += fold(dn * mixed[rows, n])
            acc1[rows, :] += fold(dn)

    own_lp = pltpu.make_async_copy(lps, o_lp.at[:, o_own], ss.at[names["lp"]])
    own_lp.start()
    s3h[h, :, pl.ds(0, hid)] = row_of(acc0[...])
    s3h[h, :, pl.ds(hid, hid)] = row_of(acc1[...])
    zpad = jnp.zeros((80, 128), F32)
    s3h[h, :, pl.ds(2 * hid, 128)] = row_of(jnp.concatenate([accl[pl.ds(0, 48), :], zpad], axis=0))
    s3h[h, :, pl.ds(2 * hid + 128, 128)] = row_of(jnp.concatenate([accl[pl.ds(48, 48), :], zpad], axis=0))
    hops_start(s3h, "s3h")

    def cwh_copy(d):
        return rc(cwp.at[d], cwh.at[d], "cwh", d, peer(d), r)

    q = hid // HOPS

    @pl.loop(0, HOPS)
    def _(d):
        cwp[d] = accw[:, lanes_at(peer(d), q)].astype(BF16)

    hops_wait(s3h, "s3h")
    s3r[r] = total(s3h, HOPS)
    rows_start(s3r, "s3r")

    @pl.loop(1, HOPS)
    def _(d):
        cwh_copy(d).start()

    lp_copy(first).start()
    lp_copy(second).start()
    lp_copy(HOPS - 1).start()
    rows_wait(s3r, "s3r")
    st3 = total(s3r, R)
    db2 = st3[:, hid : 2 * hid]
    dg2t = inv2 * (st3[:, :hid] - mean2 * db2)
    o_small[pl.ds(0, 1), :] = dg2t
    o_small[pl.ds(1, 1), :] = db2
    o_small[pl.ds(4, 1), pl.ds(0, 256)] = st3[:, 2 * hid : 2 * hid + 256]
    o_small[pl.ds(4, 1), pl.ds(256, hid - 256)] = jnp.zeros((1, hid - 256), F32)
    t2 = scale2 * inv2 * dg2t * inv_n
    cols[0] = col_of(scale2)
    cols[1] = col_of(-t2)
    cols[2] = col_of(t2 * mean2 - scale2 * db2 * inv_n)

    @pl.loop(0, hid // 16)
    def _(i):
        rows = lanes_at(i, 16)
        v = dn2[rows, :] * spread(cols[0, rows, :], sub)
        v = v + mixed[rows, :] * spread(cols[1, rows, :], sub) + spread(cols[2, rows, :], sub)
        dmx[rows, :] = v.astype(BF16)

    @functools.partial(each, 1, Z)
    def _(e):
        gz_copy(e, zi).wait_send()
        gz_copy(e, lax.rem(zi + Z - e, Z)).wait_recv()

    gfin[c] = total(gz, Z)
    gd_copy(c).start()

    mine = lanes_at(c, half)
    theirs = lanes_at(1 - c, half)

    def pair_copy(d):
        return rc(dmp.at[d, theirs, :], pr.at[d], "pair", d, h, sib)

    qrows = half // S
    zown = pl.ds(pl.multiple_of(c * half + zpar * qrows, 16), qrows)
    zother = pl.ds(pl.multiple_of(c * half + (1 - zpar) * qrows, 16), qrows)

    def z1_copy(d):
        return rc(dmp.at[d, zother, :], z1r.at[d], "z1", d, h, 2 * zmate + c)

    def z1_start(d):
        if S > 1:
            z1_copy(d).start()

    def z1_sum(d):
        if S > 1:
            done(z1_copy(d))

            @pl.loop(0, qrows // 32)
            def _(i):
                rows = pl.ds(pl.multiple_of(c * half + zpar * qrows + i * 32, 32), 32)
                dmp[d, rows, :] = (dmp[d, rows, :].astype(F32) + z1r[d, lanes_at(i, 32), :].astype(F32)).astype(BF16)

    def hop_copy(d):
        return rc(dmp.at[d, zown, :], hr.at[d], "hop", d, peer(d), r)

    def pair_sum(d):
        done(pair_copy(d))

        @pl.loop(0, half // 32)
        def _(i):
            rows = pl.ds(pl.multiple_of(c * half + i * 32, 32), 32)
            dmp[d, rows, :] = (dmp[d, rows, :].astype(F32) + pr[d, lanes_at(i, 32), :].astype(F32)).astype(BF16)

    def mix_grad(d):
        dmp[d] = dot_nt(mi[d], dmx[...]).astype(BF16)
        pair_copy(d).start()

    def mix_grads(lo):
        @pl.loop(0, 2)
        def _(i):
            mix_grad(lo + 1 - i)

        pair_sum(lo + 1)
        z1_start(lo + 1)

    def mix_hop(d):
        z1_sum(d)
        hop_copy(d).start()

    mix_grads(2)

    G2 = Z // S
    zq = lax.div(zi, S)

    def zr_copy(e, which):
        rows, lanes = chunk(0, which, qrows, G2, hid)
        return rc(hr.at[0, rows, lanes], zr.at[e], "zr", e, h, (lax.rem(zq + e, G2) * S + zpar) * 2 + c)

    def final_chunk(z):
        return chunk(c * half + lax.rem(z, S) * qrows, lax.div(z, S), qrows, G2, hid)

    def zg_copy(e, which):
        rows, lanes = final_chunk(which)
        ref = fin.at[rows, lanes]
        return rc(ref, ref, "zg", e, h, lax.rem(zi + e, Z) * 2 + c)

    def ddm_copy(core):
        ref = fin.at[lanes_at(core, half), :]
        return rc(ref, ref, "ddm", 0, h, sib)

    def d_copy(d):
        return rc(dsend.at[d], o_d.at[h], "d", d, peer(d), r)

    def dt_copy(d):
        return rc(dtail.at[d], o_dt.at[h], "dt", d, peer(d), r)

    def pp_copy(d):
        return rc(ps.at[d, :, theirs], ph.at[d], "pp", d, h, sib)

    def p_copy(d):
        return rc(phalf.at[d], prv.at[d], "p", d, peer(d), r)

    def p_half(d):
        done(pp_copy(d))
        phalf[d] = (ps[d, :, mine].astype(F32) + ph[d].astype(F32)).astype(BF16)

    def q_copy(d):
        return rc(qs.at[d], qv.at[d], "q", d, peer(d), r)

    @pl.loop(0, HOPS * NT)
    def _(it):
        dd = lax.div(it, NT)
        t = lax.rem(it, NT)
        d = HOPS - 1 - dd

        @pl.when(t == 0)
        def _():
            pT[...] = jnp.zeros(pT.shape, F32)

        @pl.when(jnp.logical_and(t == NT // 2, dd > 0))
        def _():
            p_half(d + 1)
            p_copy(d + 1).start()

            @pl.when(dd > 1)
            def _():
                dt_copy(d + 1).start()
                d_copy(d + 1).start()


        @pl.when(it == NT // 2)
        def _():
            pair_sum(2)
            z1_start(2)

        @pl.when(it == NT + NT // 2)
        def _():
            @pl.loop(1, HOPS)
            def _(j):
                done(cwh_copy(j))

            cw = cwp[0].astype(F32)
            for j in range(1, HOPS):
                cw = cw + cwh[j].astype(F32)
            cwr[r] = cw.astype(BF16)
            rows_start(cwr, "cwr")
            pair_sum(0)
            z1_start(0)
            mix_hop(2)

        @pl.when(it == 2 * NT + NT // 2)
        def _():
            mix_hop(1)
            rows_wait(cwr, "cwr")
            cwg[h] = total(cwr, R, F32).astype(BF16)
            hops_start(cwg, "cwg")

        @pl.when(it == 3 * NT + NT // 2)
        def _():
            z1_sum(0)

            @pl.loop(1, HOPS)
            def _(j):
                done(hop_copy(j))

            @pl.loop(0, qrows // 32)
            def _(i):
                rows = lanes_at(i, 32)
                own = pl.ds(pl.multiple_of(c * half + zpar * qrows + i * 32, 32), 32)
                hsum = dmp[0, own, :].astype(F32)
                for j in range(1, HOPS):
                    hsum = hsum + hr[j, rows, :].astype(F32)
                hr[0, rows, :] = hsum.astype(BF16)

            @functools.partial(each, 1, G2)
            def _(e):
                zr_copy(e, lax.rem(zq + e, G2)).start()

            hops_wait(cwg, "cwg")
            for j in range(HOPS):
                o_cw[:, pl.ds(j * q, q)] = cwg[j].astype(F32)

        @pl.when(it == HOPS * NT - 1)
        def _():
            @functools.partial(each, 1, G2)
            def _(e):
                done(zr_copy(e, lax.rem(zq + e, G2)))

            rows, lanes = chunk(0, zq, qrows, G2, hid)
            zt = lax.fori_loop(1, G2, lambda e, v: v + zr[e].astype(F32), hr[0, rows, lanes].astype(F32))
            frows, flanes = final_chunk(zi)
            fin[frows, flanes] = zt.astype(BF16)

            @functools.partial(each, 1, Z)
            def _(e):
                zg_copy(e, zi).start()

        n = lanes_at(t, big)
        dn = dot(wmx[d], dmx[:, n]).astype(BF16) * gp[d, :, n]
        pT[...] += dot_nt(dn, fx[d, :, n])
        grad = dot(aw[d], dn)
        dsend[d, :, n] = grad[:MAIN].astype(BF16)
        d4[:, n] = grad[MAIN : MAIN + 8]

        @pl.when(t == NT - 1)
        def _():
            pw = pT[...].T * KAPPA
            qs[d, :, pl.ds(0, hid)] = jnp.sum(pw * wall[d, wrow, :].astype(F32), axis=0, keepdims=True)
            qs[d, :, pl.ds(hid, hid)] = pw[ONES : ONES + 1, :]
            ps[d] = pw[:FP].astype(BF16)
            pp_copy(d).start()
            pack4(d4, dtail.at[d])

            @pl.when(dd < HOPS - 1)
            def _():
                q_copy(d).start()

            @pl.when(dd == 0)
            def _():
                dt_copy(d).start()
                d_copy(d).start()
                mix_hop(d)
                mix_grads(0)

    @pl.loop(1, HOPS)
    def _(d):
        done(q_copy(d))

    qr[r] = qs[0] + (qv[1] + qv[2] + qv[3])
    rows_start(qr, "qr")
    own_d = pltpu.make_async_copy(dsend.at[0], o_d.at[h], ss.at[names["d"]])
    own_d.start()
    own_dt = pltpu.make_async_copy(dtail.at[0], o_dt.at[h], ss.at[names["dt"]])
    own_dt.start()

    p_half(0)

    @pl.loop(1, HOPS)
    def _(d):
        done(p_copy(d))

    psum = phalf[0].astype(F32) + (prv[1].astype(F32) + prv[2].astype(F32) + prv[3].astype(F32))
    pz[zi] = psum.astype(BF16)

    def pz_copy(e, which):
        return rc(pz.at[which], pz.at[which], "pz", e, h, lax.rem(zi + e, Z) * 2 + c)

    @functools.partial(each, 1, Z)
    def _(e):
        pz_copy(e, zi).start()

    @functools.partial(each, 1, Z)
    def _(e):
        zg_copy(e, zi).wait_send()
        zg_copy(e, lax.rem(zi + Z - e, Z)).wait_recv()

    ddm_copy(c).start()

    rows_wait(qr, "qr")
    qt = total(qr, R)
    db = qt[:, hid:]
    dgn = inv * (qt[:, :hid] - mean * db)
    o_small[pl.ds(2, 1), :] = dgn
    o_small[pl.ds(3, 1), :] = db
    c1 = scale * db * inv_n
    c2 = inv * scale * dgn * inv_n
    shift = c1 - mean * c2
    row = lax.broadcasted_iota(jnp.int32, (128, hid), 0)
    q1, q2 = split2(jnp.where(row == ONES, shift, wown32 * c2))
    o_m[...] = (dot_nt(wown, q1) + dot_nt(wown, q2))[:FP]
    gd_copy(c).wait_send()
    gd_copy(1 - c).wait_recv()
    g1, g2, g3 = split3(jnp.concatenate([gfin[0], gfin[1]], axis=0))
    gq = dot(g1, q1) + dot(g2, q1) + dot(g3, q1) + dot(g1, q2) + dot(g2, q2)

    @functools.partial(each, 1, Z)
    def _(e):
        pz_copy(e, zi).wait_send()
        pz_copy(e, lax.rem(zi + Z - e, Z)).wait_recv()

    pfin[c] = total(pz, Z).astype(BF16)

    def pd_copy(core):
        return rc(pfin.at[core], pfin.at[core], "pd", 0, h, sib)

    pd_copy(c).start()
    ddm_copy(c).wait_send()
    ddm_copy(1 - c).wait_recv()
    o_mix[...] = fin[...]

    pd_copy(c).wait_send()
    pd_copy(1 - c).wait_recv()
    ptot = jnp.concatenate([pfin[0], pfin[1]], axis=1).astype(F32)
    o_gw[...] = ptot * scale - gq[:FP]
    own_d.wait()
    own_dt.wait()
    own_lp.wait()

    @pl.loop(1, HOPS)
    def _(d):
        done(d_copy(d))
        done(dt_copy(d))
        done(lp_copy(d))


def last_kernel(
    nodes,
    ft, d, dt, lp, m, mix, gw, small, cw,
    o_lp, o_gf, o_mix, o_gw, o_gg, o_gb, o_hg, o_hb, o_cw, o_cb, o_loss, low,
):
    feat, n = ft.shape
    ncls = o_lp.shape[0]
    o_lp[...] = lp[...].astype(F32)[:ncls]
    mm = m[...]
    f = ft[...]
    fix = dot(mm[:, :feat].astype(BF16), f) + mm[:, ONES : ONES + 1]
    tail = dt[0].astype(F32)
    for b in range(4):
        low[pl.ds(0, 4), pl.ds(b * (n // 4), n // 4)] = tail[4 * b : 4 * b + 4]
    gf = jnp.concatenate([d[0].astype(F32), low[...]], axis=0)[:feat] - fix[:feat]
    if STRIDED:
        flat = o_gf.reshape(feat * (n // 128), 128)
        for i in range(n // 128):
            flat[pl.ds(i, feat, stride=n // 128), :] = gf[:, i * 128 : (i + 1) * 128]
    else:
        for i in range(n // 128):
            o_gf[:, i, :] = gf[:, i * 128 : (i + 1) * 128]

    @pl.when(pl.program_id(0) == 0)
    def _():
        hid = mix.shape[1]
        o_mix[...] = mix[...].astype(F32)
        for i in range(hid // 128):
            o_gw[:, i, :] = gw[pl.ds(0, feat), pl.ds(i * 128, 128)]
        o_hg[...] = small[pl.ds(0, 1), :]
        o_hb[...] = small[pl.ds(1, 1), :]
        o_gg[...] = small[pl.ds(2, 1), :]
        o_gb[...] = small[pl.ds(3, 1), :]
        o_cw[...] = cw[pl.ds(0, ncls), :]
        o_cb[...] = small[pl.ds(4, 1), pl.ds(0, ncls)]
        o_loss[...] = jnp.sum(small[pl.ds(4, 1), pl.ds(128, 128)], axis=1, keepdims=True) * (-1.0 / nodes)


def shards(
    R, features, branch_weight, branch_gain, branch_bias, mix_weight, mixing_norm_gain, mixing_norm_bias,
    class_weight, class_bias, labels, hop_mask,
):
    local, feat = features.shape[1:]
    hid = mix_weight.shape[0]
    ncls = class_weight.shape[1]
    nodes = local * R
    sub = local // HOPS
    Z = R // 2
    half = hid // 2
    S = min(Z, 2)
    G2, qrows = Z // S, half // S
    zrows, zcols = chunk(0, 0, qrows, G2, hid)
    assert feat == ONES and ncls == 47 and local // hop_mask.shape[0] == 128
    ft = features[0].T
    sd = jax.ShapeDtypeStruct
    vm = pl.BlockSpec(memory_space=pltpu.VMEM)
    hbm = pl.BlockSpec(memory_space=pl.ANY)
    _, nsem = sem_plan(R)
    V = pltpu.VMEM
    outs = pl.pallas_call(
        functools.partial(main_kernel, R, nodes),
        grid=(1,),
        out_shape=(
            sd((48, local), BF16),
            sd((HOPS, MAIN, sub), BF16),
            sd((HOPS, 16, sub // 4), BF16),
            sd((FP, 128), F32),
            sd((hid, hid), BF16),
            sd((FP, hid), F32),
            sd((8, hid), F32),
            sd((48, hid), F32),
        ),
        in_specs=[hbm, pl.BlockSpec((16, local), lambda i: (MAIN // 16, 0))]
        + [vm] * 9
        + [pl.BlockSpec(memory_space=pltpu.SMEM)],
        out_specs=(hbm, hbm, hbm, vm, vm, vm, vm, vm),
        scratch_shapes=[
            V((128, local), BF16),
            V((HOPS, 128, sub), BF16),
            V((HOPS, 16, sub // 4), BF16),
            V((HOPS, 16, sub // 4), BF16),
            V((48, sub // 4), F32),
            V((HOPS, hid + 128, hid), BF16),
            V((HOPS, hid, 256), BF16),
            V((HOPS, FP, hid), BF16),
            V((HOPS, hid, hid), BF16),
            V((HOPS, 16, sub), BF16),
            V((HOPS, hid, sub), BF16),
            V((HOPS, hid, sub), BF16),
            V((hid, sub), F32),
            V((hid, sub), F32),
            V((hid, sub), BF16),
            V((128, 128), F32),
            V((64, 128), F32),
            V((Z, 64, 128), F32),
            V((2, 64, 128), F32),
            V((R, 1, 2 * hid), F32),
            V((HOPS, 1, 2 * hid), F32),
            V((HOPS, 1, 2 * hid), F32),
            V((R, 1, 2 * hid), F32),
            V((HOPS, 1, 2 * hid + 256), F32),
            V((R, 1, 2 * hid + 256), F32),
            V((HOPS, 48, hid // HOPS), BF16),
            V((HOPS, 48, hid // HOPS), BF16),
            V((R, 48, hid // HOPS), BF16),
            V((HOPS, 48, hid // HOPS), BF16),
            V((48, sub), BF16),
            V((128, hid), F32),
            V((hid, 128), BF16),
            V((8, 128), F32),
            V((hid, min(2 * TILE, sub)), BF16),
            V((hid, min(2 * TILE, sub)), BF16),
            V((128, min(2 * TILE, sub)), BF16),
            V((hid, 128), F32),
            V((hid, 128), F32),
            V((96, 128), F32),
            V((48, hid), F32),
            V((3, hid, 128), F32),
            V((HOPS, hid, hid), BF16),
            V((HOPS, half, hid), BF16),
            V((HOPS, qrows, hid), BF16),
            V((HOPS, qrows, hid), BF16),
            V((max(G2, 2), zrows.size, zcols.size), BF16),
            V((hid, hid), BF16),
            V((HOPS, MAIN, sub), BF16),
            V((8, sub), F32),
            V((HOPS, 16, sub // 4), BF16),
            V((hid, 128), F32),
            V((HOPS, FP, hid), BF16),
            V((HOPS, FP, half), BF16),
            V((HOPS, FP, half), BF16),
            V((HOPS, FP, half), BF16),
            V((HOPS, 1, 2 * hid), F32),
            V((HOPS, 1, 2 * hid), F32),
            V((R, 1, 2 * hid), F32),
            V((Z, FP, half), BF16),
            V((2, FP, half), BF16),
            pltpu.SemaphoreType.DMA((nsem,)),
            pltpu.SemaphoreType.DMA((nsem,)),
        ],
        compiler_params=pltpu.CompilerParams(
            collective_id=0, has_side_effects=True, vmem_limit_bytes=63 * 1024 * 1024
        ),
        cost_estimate=pl.CostEstimate(flops=2 * 8 * 10**9, bytes_accessed=10**7, transcendentals=10**7),
        name="main",
    )(
        ft, ft, branch_weight[0], branch_gain, branch_bias, mix_weight, mixing_norm_gain[None], mixing_norm_bias[None],
        class_weight.T, class_bias[None], labels[None], hop_mask.T,
    )
    lp, dd, dt, m, mix, gw, small, cw = outs
    nb = sub
    whole = lambda shape: pl.BlockSpec(shape, lambda i: (0,) * len(shape))
    lp, gf, mix, gw, gg, gb, hg, hb, cw, cb, loss = pl.pallas_call(
        functools.partial(last_kernel, nodes),
        grid=(local // nb,),
        out_shape=(
            sd((ncls, local), F32),
            sd((feat, local // 128, 128), F32),
            sd((hid, hid), F32),
            sd((feat, hid // 128, 128), F32),
            sd((1, hid), F32),
            sd((1, hid), F32),
            sd((1, hid), F32),
            sd((1, hid), F32),
            sd((ncls, hid), F32),
            sd((1, ncls), F32),
            sd((1, 1), F32),
        ),
        in_specs=[
            pl.BlockSpec((feat, nb), lambda i: (0, i)),
            pl.BlockSpec((1, MAIN, nb), lambda i: (i, 0, 0)),
            pl.BlockSpec((1, 16, nb // 4), lambda i: (i, 0, 0)),
            pl.BlockSpec((48, nb), lambda i: (0, i)),
            whole((FP, 128)),
            whole((hid, hid)),
            whole((FP, hid)),
            whole((8, hid)),
            whole((48, hid)),
        ],
        out_specs=(
            pl.BlockSpec((ncls, nb), lambda i: (0, i)),
            pl.BlockSpec((feat, nb // 128, 128), lambda i: (0, i, 0)),
            whole((hid, hid)),
            whole((feat, hid // 128, 128)),
            whole((1, hid)),
            whole((1, hid)),
            whole((1, hid)),
            whole((1, hid)),
            whole((ncls, hid)),
            whole((1, ncls)),
            whole((1, 1)),
        ),
        scratch_shapes=[V((8, nb), F32)],
        compiler_params=pltpu.CompilerParams(vmem_limit_bytes=60 * 1024 * 1024),
        name="last",
    )(ft, dd, dt, lp, m, mix, gw, small, cw)
    return (
        lp.T,
        loss[0, 0],
        with_layout_constraint(gf.reshape(feat, 1, local), Layout((0, 1, 2))).transpose(1, 2, 0),
        gw.reshape(1, feat, hid),
        gg,
        gb,
        mix,
        hg[0],
        hb[0],
        cw.T,
        cb[0],
    )


def solution(mesh):
    placed = (
        P("hop", "rows", None), P("hop", None, None), P("hop", None), P("hop", None), P("hop", None),
        P(), P(), P(), P(), P("rows"), P("rows", None),
    )
    assert mesh.shape["hop"] == HOPS
    return jax.shard_map(
        functools.partial(shards, mesh.shape["rows"]),
        mesh=mesh,
        in_specs=placed,
        out_specs=(
            P("rows", None), P(), P("hop", "rows", None), P("hop", None, None), P("hop", None), P("hop", None),
            P("hop", None), P(), P(), P(), P(),
        ),
        check_vma=False,
    )
```
